32 devices in a mesh: ulysses: 4 (over y, x), blk: 8 (over z, core).
Axes of the slice: x: 2, y: 2, z: 4, core: 2. Of those that a mesh axis runs over, the one named last changes fastest.
Arguments:
- inputs: bfloat16 [4096, 2048], P(('ulysses', 'blk')), may hold values from -6 to 6
- cotangent: bfloat16 [4096, 2048], P(('ulysses', 'blk')), may hold values from -6 to 6
- segments: int32 [4096], replicated, may hold values from 0 to 7, as said below
- expert_ids: int32 [4096, 8], P(('ulysses', 'blk')), may hold values from 0 to 15, all different within a row; in each aligned block of 128 rows (0 to 127, 128 to 255, ...) at most 128 rows name the same one
- gate_weights: float32 [4096, 8], P(('ulysses', 'blk')), as said below
- fill_order: int32 [4096], P(('ulysses', 'blk')), may hold values from 0 to 127, as said below
- norm1_gain: bfloat16 [2048], P(('ulysses', 'blk')), may hold values from 0.099609375 to 1.8984375
- w_query: bfloat16 [2048, 2048], P(('ulysses', 'blk')), may hold values from -0.125 to 0.125
- w_key: bfloat16 [2048, 2048], P(('ulysses', 'blk')), may hold values from -0.125 to 0.125
- w_value: bfloat16 [2048, 2048], P(('ulysses', 'blk')), may hold values from -0.125 to 0.125
- w_output: bfloat16 [2048, 2048], P(('ulysses', 'blk')), may hold values from -0.5 to 0.5
- query_gain: bfloat16 [2048], P(('ulysses', 'blk')), may hold values from 0.099609375 to 1.8984375
- key_gain: bfloat16 [2048], P(('ulysses', 'blk')), may hold values from 0.099609375 to 1.8984375
- norm2_gain: bfloat16 [2048], P(('ulysses', 'blk')), may hold values from 0.099609375 to 1.8984375
- expert_gate: bfloat16 [32768, 1024], P(('ulysses', 'blk')), may hold values from -0.125 to 0.125
- expert_up: bfloat16 [32768, 1024], P(('ulysses', 'blk')), may hold values from -0.125 to 0.125
- expert_down: bfloat16 [16384, 2048], P(('ulysses', 'blk')), may hold values from -0.5 to 0.5
Outputs:
- output: float32 [4096, 2048], P(('ulysses', 'blk'))
- d_inputs: float32 [4096, 2048], P(('ulysses', 'blk'))
- d_norm1_gain: float32 [2048], P(('ulysses', 'blk'))
- d_w_query: float32 [2048, 2048], P(('ulysses', 'blk'))
- d_w_key: float32 [2048, 2048], P(('ulysses', 'blk'))
- d_w_value: float32 [2048, 2048], P(('ulysses', 'blk'))
- d_w_output: float32 [2048, 2048], P(('ulysses', 'blk'))
- d_query_gain: float32 [2048], P(('ulysses', 'blk'))
- d_key_gain: float32 [2048], P(('ulysses', 'blk'))
- d_norm2_gain: float32 [2048], P(('ulysses', 'blk'))
- d_expert_gate: float32 [32768, 1024], P(('ulysses', 'blk'))
- d_expert_up: float32 [32768, 1024], P(('ulysses', 'blk'))
- d_expert_down: float32 [16384, 2048], P(('ulysses', 'blk'))
The draws below stay inside these ranges and needn't reach their ends.
Inputs may be any that keep to these rules, and one draw needn't show every extreme that they name: `segments`: document ids along the positions: they start at 0, never fall and rise by one where a new document begins; each document has 1 to 1024 positions, and one document has exactly 1024. `expert_ids`: each row names 8 different experts; in each aligned block of 128 rows (the rows of one device) no expert is named by more than 128 rows, a bound that some block reaches. `gate_weights`: Positive; each row sums to one. `fill_order`: within each aligned block of 128 positions, a permutation of 0 to 127.
All inputs are finite; a program needn't handle non-finite values.
Results may differ from the reference program's by a relative error of at most 0.025.
Values may be sent and summed in bfloat16 or wider, within the bound.
A program may use at most 256 MiB of HBM per device.

```python
import math
import jax
import jax.numpy as jnp
import numpy as np
from jax import lax

D = 2048
HEADS = 16
HEAD_DIM = 128
FF = 1024
TOPK = 8
TOK_DEV = 128
DOC_LEAST = 200
EXPERTS = 16
LEN = 4096
C_SRC = 128
CAP = 2304
DOC_MOST = 1024
N_ULYSSES = 4


def draw_segments(key, part):
    key = jax.random.fold_in(key, 11)
    key_start, key_offset = jax.random.split(key, 2)
    unit_len = DOC_MOST // 2
    unit_count = LEN // unit_len
    doc_start = (jax.random.randint(key_start, (), 0, N_ULYSSES - 1) * DOC_MOST).astype(jnp.int32)
    doc_end = doc_start + DOC_MOST
    unit_ids = jnp.arange(unit_count, dtype=jnp.int32)
    unit_first = unit_ids * unit_len
    offsets = jax.random.randint(key_offset, (unit_count,), DOC_LEAST // 2, unit_len - DOC_LEAST // 2).astype(jnp.int32)
    outside = ((unit_first < doc_start) | (unit_first >= doc_end)) & (unit_ids > 0)
    marks = jnp.where(outside, unit_first + offsets, LEN).astype(jnp.int32)
    starts_at = jnp.zeros((LEN,), jnp.int32)
    starts_at = starts_at.at[marks].set(1, mode='drop')
    starts_at = starts_at.at[jnp.stack([doc_start, doc_end])].set(1, mode='drop')
    starts_at = starts_at.at[0].set(0)
    return jnp.cumsum(starts_at).astype(jnp.int32)


def draw_fill_order(key, part):
    key = jax.random.fold_in(key, 12)
    block_keys = jax.random.split(key, LEN // TOK_DEV)
    orders = jax.vmap(lambda sub_key: jax.random.permutation(sub_key, TOK_DEV))(block_keys)
    return orders.reshape(LEN).astype(jnp.int32)


def draw_gate_weights(key, part):
    key = jax.random.fold_in(key, 13)
    logits = 0.5 * jax.random.normal(key, (LEN, TOPK), jnp.float32)
    return jax.nn.softmax(logits, axis=-1)


def steps_of(rng, shape, cuts, low, largest):
    def one(axis_at, blocks):
        steps = jax.random.uniform(jax.random.fold_in(jax.random.fold_in(rng, 6), axis_at), (blocks,), jnp.float32, low / len(cuts), largest / len(cuts))
        return jnp.repeat(jnp.exp(steps), shape[axis_at] // blocks).reshape((-1,) + (1,) * (len(shape) - axis_at - 1))

    level = one(*cuts[0])
    for cut in cuts[1:]:
        level = level * one(*cut)
    return level


def routed_block(own_key, own, number, rows, number_of, top, bound, slope):
    order = jax.random.permutation(own_key, number_of)
    heavy_load, ordinary = load_shares(number_of, rows * top, bound, slope, True), load_shares(number_of, rows * top, bound, slope, False)
    places = jnp.arange(number_of)

    def named(lengths, rotation):
        used = int((lengths > 0).sum())
        fixed = max(1, used // 4)
        moved = fixed + (places - fixed + rotation * (used - fixed)) % max(1, number_of - fixed)
        return jnp.zeros((number_of,), jnp.int32).at[order[jnp.where(places < fixed, places, moved)]].set(jnp.asarray(lengths, jnp.int32))

    lengths = jnp.where(number % 4 == 0, named(heavy_load, number // 4), named(ordinary, number - number // 4 - 1))
    mixed = jax.random.permutation(jax.random.fold_in(own, 3), number_of)
    donor, taker = mixed[0:number_of // 2 * 2:2], mixed[1:number_of // 2 * 2:2]
    margin = jnp.minimum(lengths[donor] - 1, bound - lengths[taker]) // 2
    margin = jnp.where((donor == order[0]) | (taker == order[0]) | (lengths[taker] == 0), 0, jnp.maximum(margin, 0))
    moved = jax.random.randint(jax.random.fold_in(own, 4), (number_of // 2,), 0, 1 << 20) % (margin + 1)
    lengths = lengths.at[donor].add(-moved).at[taker].add(moved)
    members = jnp.searchsorted(jnp.cumsum(lengths), jnp.arange(rows * top), side="right").astype(jnp.int32)
    listing = members.reshape(top, rows).T
    listing = listing[jax.random.permutation(jax.random.fold_in(own, 1), rows)]
    rotation = jax.random.randint(jax.random.fold_in(own, 2), (rows, 1), 0, top)
    return jnp.take_along_axis(listing, (jnp.arange(top)[None, :] + rotation) % top, axis=1)


def load_shares(number_of, total, reach, slope, full):
    loads = [(1 << 20) // math.isqrt(grade ** slope) + 1 for grade in range(1, number_of + 1)]
    largest = reach if full else min(reach, max(-(-total // number_of), total * loads[0] // sum(loads)))
    least = 1 if total - largest >= number_of - 1 else 0
    holding, surplus = [largest] + [least] * (number_of - 1), total - largest - least * (number_of - 1)
    while surplus > 0:
        movable = [i for i in range(1, number_of) if holding[i] < largest] or [i for i in range(1, number_of) if holding[i] < reach]
        pool, remaining = sum([loads[i] for i in movable]), surplus
        for i in movable:
            extra = min(reach - holding[i], max(1, remaining * loads[i] // pool), surplus)
            holding[i] = holding[i] + extra
            surplus = surplus - extra
    return np.array(holding)


def centred(own_key, shape, width, most, cuts=(), kind=jnp.bfloat16):
    values = width * jax.random.normal(own_key, shape, jnp.float32)
    if cuts:
        values = values * steps_of(own_key, shape, cuts, -0.22, 0.18)
    return jnp.clip(values, -most, most).astype(kind)


def setup_inputs(seed: int = 0) -> dict:
    key_list = jax.random.split(jax.random.key(seed), 18)
    inputs = centred(key_list[0], (LEN, D), 1.0, 6.0, ((0, 32),))
    cotangent = centred(key_list[1], (LEN, D), 1.0, 6.0, ((0, 32),))
    segments = draw_segments(jax.random.fold_in(key_list[17], 71), 0)
    expert_ids_keys = jax.random.split(jax.random.fold_in(key_list[3], 1), LEN // TOK_DEV)
    expert_ids_turns = jax.random.permutation(jax.random.fold_in(key_list[3], 3), LEN // TOK_DEV)
    expert_ids = jax.vmap(lambda own, number: routed_block(jax.random.fold_in(key_list[3], 2), own, number, TOK_DEV, EXPERTS, TOPK, C_SRC, 2))(expert_ids_keys, expert_ids_turns).reshape((LEN, TOPK))
    gate_weights = draw_gate_weights(jax.random.fold_in(key_list[17], 71), 0)
    fill_order = draw_fill_order(jax.random.fold_in(key_list[17], 71), 0)
    norm1_gain = jnp.clip(1.0 + 0.18 * jax.random.normal(key_list[6], (D,), jnp.float32), 0.099609375, 1.8984375).astype(jnp.bfloat16)
    w_query = centred(key_list[7], (D, D), D ** -0.5, 0.125, ((0, 32),))
    w_key = centred(key_list[8], (D, D), D ** -0.5, 0.125, ((0, 32),))
    w_value = centred(key_list[9], (D, D), D ** -0.5, 0.125, ((0, 32),))
    w_output = centred(key_list[10], (D, D), (D // 16) ** -0.5, 0.5, ((0, 32),))
    query_gain = jnp.clip(1.0 + 0.18 * jax.random.normal(key_list[11], (D,), jnp.float32), 0.099609375, 1.8984375).astype(jnp.bfloat16)
    key_gain = jnp.clip(1.0 + 0.18 * jax.random.normal(key_list[12], (D,), jnp.float32), 0.099609375, 1.8984375).astype(jnp.bfloat16)
    norm2_gain = jnp.clip(1.0 + 0.18 * jax.random.normal(key_list[13], (D,), jnp.float32), 0.099609375, 1.8984375).astype(jnp.bfloat16)
    expert_gate = centred(key_list[14], (EXPERTS * D, FF), D ** -0.5, 0.125, ((0, 32),))
    expert_up = centred(key_list[15], (EXPERTS * D, FF), D ** -0.5, 0.125, ((0, 32),))
    expert_down = centred(key_list[16], (EXPERTS * FF, D), (FF // 8) ** -0.5, 0.5, ((0, 32),))
    return {"inputs": inputs, "cotangent": cotangent, "segments": segments, "expert_ids": expert_ids, "gate_weights": gate_weights, "fill_order": fill_order, "norm1_gain": norm1_gain, "w_query": w_query, "w_key": w_key, "w_value": w_value, "w_output": w_output, "query_gain": query_gain, "key_gain": key_gain, "norm2_gain": norm2_gain, "expert_gate": expert_gate, "expert_up": expert_up, "expert_down": expert_down}


EPS = 1e-05
ROPE_BASE = 10000.0
NEG = -1e+30
HIGH = lax.Precision.HIGHEST

@jax.custom_vjp
def low(v):
    return lax.optimization_barrier(v.astype(jnp.bfloat16)).astype(jnp.float32)

@jax.custom_vjp
def low_back(v):
    return v

def low_keep(v):
    return (low(v), None)

def low_pass(kept, grad):
    return (grad,)

def back_keep(v):
    return (v, None)

def back_low(kept, grad):
    return (low(grad),)
low.defvjp(low_keep, low_pass)
low_back.defvjp(back_keep, back_low)

def norm_rows(values, gain_vec):
    return values * lax.rsqrt(lax.optimization_barrier(jnp.mean(values * values, axis=-1, keepdims=True)) + EPS) * gain_vec

def rotate(values, positions):
    half_dim = HEAD_DIM // 2
    inv_freq = jnp.exp(jnp.arange(half_dim, dtype=jnp.float32) * (-2.0 * math.log(ROPE_BASE) / HEAD_DIM))
    angles = positions.astype(jnp.float32)[:, None] * inv_freq[None, :]
    cosine = jnp.cos(angles)[:, None, :]
    sin_t = jnp.sin(angles)[:, None, :]
    shaped = values.reshape(values.shape[0], HEADS, HEAD_DIM)
    lower_half = shaped[..., :half_dim]
    upper_half = shaped[..., half_dim:]
    turned = jnp.concatenate([lower_half * cosine - upper_half * sin_t, upper_half * cosine + lower_half * sin_t], axis=-1)
    return turned.reshape(values.shape)

def attention(q_rot, k_rot, v_all, segments):
    q_heads = q_rot.reshape(LEN, HEADS, HEAD_DIM)
    k_padded = jnp.concatenate([jnp.zeros((DOC_MOST, HEADS, HEAD_DIM), k_rot.dtype), k_rot.reshape(LEN, HEADS, HEAD_DIM)], axis=0)
    v_padded = jnp.concatenate([jnp.zeros((DOC_MOST, HEADS, HEAD_DIM), v_all.dtype), v_all.reshape(LEN, HEADS, HEAD_DIM)], axis=0)
    seg_padded = jnp.concatenate([jnp.full((DOC_MOST,), -1, jnp.int32), segments.astype(jnp.int32)], axis=0)
    block_rows = min(512, LEN)
    key_span = block_rows + DOC_MOST
    score_scale = 1.0 / math.sqrt(HEAD_DIM)

    def attend_block(block_index):
        row_start = (block_index * block_rows).astype(jnp.int32)
        q_block = lax.dynamic_slice_in_dim(q_heads, row_start, block_rows, 0)
        k_block = lax.dynamic_slice_in_dim(k_padded, row_start, key_span, 0)
        v_block = lax.dynamic_slice_in_dim(v_padded, row_start, key_span, 0)
        q_seg = lax.dynamic_slice_in_dim(segments.astype(jnp.int32), row_start, block_rows, 0)
        k_seg = lax.dynamic_slice_in_dim(seg_padded, row_start, key_span, 0)
        q_pos = row_start + jnp.arange(block_rows, dtype=jnp.int32)
        k_pos = row_start - DOC_MOST + jnp.arange(key_span, dtype=jnp.int32)
        scores = low_back(jnp.einsum('qhd,khd->hqk', q_block, k_block, precision=HIGH) * score_scale)
        allowed = (k_seg[None, :] == q_seg[:, None]) & (k_pos[None, :] <= q_pos[:, None])
        scores = jnp.where(allowed[None], scores, NEG)
        row_max = lax.optimization_barrier(jnp.max(scores, axis=-1, keepdims=True))
        weights = jnp.exp(scores - row_max)
        prob_rows = weights / lax.optimization_barrier(jnp.sum(weights, axis=-1, keepdims=True))
        return jnp.einsum('hqk,khd->qhd', low(prob_rows), v_block, precision=HIGH)
    outputs = lax.map(jax.checkpoint(attend_block), jnp.arange(LEN // block_rows, dtype=jnp.int32))
    return outputs.reshape(LEN, D)

def slot_tables(expert_ids, fill_order):
    tokens = jnp.arange(LEN, dtype=jnp.int32)
    order_key = (tokens // TOK_DEV * TOK_DEV + fill_order).astype(jnp.int32)
    by_key = jnp.zeros((LEN,), jnp.int32).at[order_key].set(tokens)
    chosen = lax.optimization_barrier(jnp.sum((expert_ids[:, :, None] == jnp.arange(EXPERTS, dtype=jnp.int32)[None, None, :]).astype(jnp.int32), axis=1))
    sorted_rows = chosen[by_key]
    before = jnp.cumsum(sorted_rows, axis=0).astype(jnp.int32) - sorted_rows
    rank_all = before[order_key]
    pair_rank = jnp.take_along_axis(rank_all, expert_ids, axis=1)
    kept_pair = pair_rank < CAP
    flat_slot = jnp.where(kept_pair, expert_ids * CAP + pair_rank, EXPERTS * CAP).astype(jnp.int32)
    owners = jnp.broadcast_to(tokens[:, None], expert_ids.shape)
    slot_token = jnp.zeros((EXPERTS * CAP,), jnp.int32).at[flat_slot.reshape(-1)].set(owners.reshape(-1), mode='drop')
    return (kept_pair, flat_slot, slot_token)

def mixture(normed_two, w_gate, w_up, w_down, slot_token, flat_slot, pair_share):

    def expert_block(expert_index):
        picked = lax.dynamic_slice_in_dim(slot_token, (expert_index * CAP).astype(jnp.int32), CAP, 0)
        x_rows = low_back(normed_two[picked])
        gate_rows = lax.dynamic_slice_in_dim(w_gate, (expert_index * D).astype(jnp.int32), D, 0)
        up_rows = lax.dynamic_slice_in_dim(w_up, (expert_index * D).astype(jnp.int32), D, 0)
        down_rows = lax.dynamic_slice_in_dim(w_down, (expert_index * FF).astype(jnp.int32), FF, 0)
        gate_pre = low_back(jnp.dot(x_rows, gate_rows, precision=HIGH))
        up_pre = low_back(jnp.dot(x_rows, up_rows, precision=HIGH))
        hidden = low(jax.nn.silu(gate_pre) * up_pre)
        return low_back(low(jnp.dot(hidden, down_rows, precision=HIGH)))
    produced = lax.map(jax.checkpoint(expert_block), jnp.arange(EXPERTS, dtype=jnp.int32)).reshape(EXPERTS * CAP, D)
    produced = jnp.concatenate([produced, jnp.zeros((1, D), produced.dtype)], axis=0)
    combined = jnp.zeros_like(normed_two)
    for pick_index in range(TOPK):
        combined = combined + pair_share[:, pick_index][:, None] * produced[flat_slot[:, pick_index]]
    return combined

def reference(inputs, cotangent, segments, expert_ids, gate_weights, fill_order, norm1_gain, w_query, w_key, w_value, w_output, query_gain, key_gain, norm2_gain, expert_gate, expert_up, expert_down):
    kept_pair, flat_slot, slot_token = slot_tables(expert_ids, fill_order)
    pair_share = jnp.where(kept_pair, gate_weights.astype(jnp.float32), 0.0)
    positions = jnp.arange(LEN, dtype=jnp.int32)

    def layer(layer_in, gain_one, w_q, w_k, w_v, w_o, gain_q, gain_k, gain_two, w_gate, w_up, w_down):
        normed_one = low(norm_rows(layer_in, gain_one))
        q_lin = low_back(jnp.dot(normed_one, w_q, precision=HIGH))
        k_lin = low_back(jnp.dot(normed_one, w_k, precision=HIGH))
        v_lin = jnp.dot(normed_one, w_v, precision=HIGH)
        q_rot = low_back(low(rotate(norm_rows(q_lin, gain_q), positions)))
        k_rot = low_back(low(rotate(norm_rows(k_lin, gain_k), positions)))
        v_all = low_back(low(v_lin))
        attended = low_back(low(attention(q_rot, k_rot, v_all, segments)))
        residual = layer_in + low_back(jnp.dot(attended, w_o, precision=HIGH))
        normed_two = low(norm_rows(residual, gain_two))
        return residual + mixture(normed_two, w_gate, w_up, w_down, slot_token, flat_slot, pair_share)
    output, backward = jax.vjp(layer, inputs.astype(jnp.float32), norm1_gain.astype(jnp.float32), w_query.astype(jnp.float32), w_key.astype(jnp.float32), w_value.astype(jnp.float32), w_output.astype(jnp.float32), query_gain.astype(jnp.float32), key_gain.astype(jnp.float32), norm2_gain.astype(jnp.float32), expert_gate.astype(jnp.float32), expert_up.astype(jnp.float32), expert_down.astype(jnp.float32))
    grads = backward(cotangent.astype(jnp.float32))
    return (output, grads[0], grads[1], grads[2], grads[3], grads[4], grads[5], grads[6], grads[7], grads[8], grads[9], grads[10], grads[11])
```

```python
import functools
import math

import jax
import jax.numpy as jnp
from jax import lax
from jax.experimental import pallas as pl
from jax.experimental.pallas import tpu as pltpu
from jax.sharding import Mesh
from jax.sharding import PartitionSpec as P

HEAD_DIM = 128


EPS = 1e-05
ROPE_BASE = 10000.0
NEG = -1e30


def as_sent(value):

    def short(part):
        return part.astype(jnp.bfloat16) if part.dtype == jnp.float32 else part

    return jax.tree.map(short, value)


def passed_along(block, axis, distance):
    devices = range(lax.axis_size(axis))
    route = [((i - distance) % len(devices), i) for i in devices]
    return lax.ppermute(block, axis, route)


def prefix(value, axis, join, neutral):
    count, mine = (lax.axis_size(axis), lax.axis_index(axis))
    pieces = lax.all_gather(value, axis)
    subtotal = jnp.full_like(value, 0) + jnp.asarray(neutral, value.dtype)

    def hop(position, subtotal):
        longer = join(subtotal, pieces[position])
        return jnp.where(position < mine, longer, subtotal)

    return lax.fori_loop(0, count - 1, hop, subtotal)


def partner_2(block, axis, bit):
    count = lax.axis_size(axis)
    route = []
    for low in range(count):
        high = low | 1 << bit
        if high != low and high < count:
            route += [(low, high), (high, low)]
    return lax.ppermute(block, axis, route)


def norm_rows(values, gain_vec):
    return values * lax.rsqrt(jnp.mean(values * values, axis=-1, keepdims=True) + EPS) * gain_vec


def rotate(values, positions):
    half_dim = HEAD_DIM // 2
    heads_here = values.shape[1] // HEAD_DIM
    inv_freq = jnp.exp(
        jnp.arange(half_dim, dtype=jnp.float32) * (-2.0 * math.log(ROPE_BASE) / HEAD_DIM)
    )
    angles = positions.astype(jnp.float32)[:, None] * inv_freq[None, :]
    cosine = jnp.cos(angles)[:, None, :]
    sin_t = jnp.sin(angles)[:, None, :]
    shaped = values.reshape(values.shape[0], heads_here, HEAD_DIM)
    lower_half = shaped[..., :half_dim]
    upper_half = shaped[..., half_dim:]
    turned = jnp.concatenate(
        [lower_half * cosine - upper_half * sin_t, upper_half * cosine + lower_half * sin_t],
        axis=-1,
    )
    return turned.reshape(values.shape)


def attn_inputs(q_lin, k_lin, gain_q, gain_k, positions):
    return (
        rotate(norm_rows(q_lin, gain_q), positions),
        rotate(norm_rows(k_lin, gain_k), positions),
    )


def banded(shaped, fill_value):
    earlier = jnp.concatenate([jnp.full_like(shaped[:1], fill_value), shaped[:-1]], axis=0)
    return jnp.concatenate([earlier, shaped], axis=1)


def unbanded(band, local_rows):
    earlier = band[:, :local_rows]
    own_part = band[:, local_rows:]
    moved_up = jnp.concatenate([earlier[1:], jnp.zeros_like(earlier[:1])], axis=0)
    return own_part + moved_up


def add_counts(earlier, later):
    return earlier + later


def expert_move(buffer):
    return lax.all_to_all(buffer, ("ulysses", "blk"), split_axis=0, concat_axis=0, tiled=True)


def to_head_layout(values):
    return jax.tree.map(
        lambda part, own: part.astype(own.dtype),
        lax.all_to_all(as_sent(values), "ulysses", split_axis=1, concat_axis=0, tiled=True),
        values,
    )


def to_token_layout(values):
    return jax.tree.map(
        lambda part, own: part.astype(own.dtype),
        lax.all_to_all(as_sent(values), "ulysses", split_axis=0, concat_axis=1, tiled=True),
        values,
    )


def local(
    inputs,
    cotangent,
    segments,
    expert_ids,
    gate_weights,
    fill_order,
    norm1_gain,
    w_query,
    w_key,
    w_value,
    w_output,
    query_gain,
    key_gain,
    norm2_gain,
    expert_gate,
    expert_up,
    expert_down,
):
    blk_size = lax.axis_size("blk")
    groups = lax.axis_size("ulysses")
    devices = blk_size * groups
    local_rows = inputs.shape[0]
    model_width = inputs.shape[1]
    blk_index = lax.axis_index("blk")
    group_index = lax.axis_index("ulysses")
    device_index = group_index * blk_size + blk_index
    positions = device_index * local_rows + jnp.arange(local_rows, dtype=jnp.int32)
    heads_dev = model_width // groups // HEAD_DIM
    score_scale = 1.0 / math.sqrt(HEAD_DIM)
    layer_in = inputs.astype(jnp.float32)
    dense = (w_query, w_key, w_value, w_output, norm1_gain, query_gain, key_gain, norm2_gain)
    gathered = (
        lax.all_gather(dense[0], ("ulysses", "blk"), axis=0, tiled=True),
        lax.all_gather(dense[1], ("ulysses", "blk"), axis=0, tiled=True),
        lax.all_gather(dense[2], ("ulysses", "blk"), axis=0, tiled=True),
        lax.all_gather(dense[3], ("ulysses", "blk"), axis=0, tiled=True),
        lax.all_gather(dense[4], ("ulysses", "blk"), axis=0, tiled=True),
        lax.all_gather(dense[5], ("ulysses", "blk"), axis=0, tiled=True),
        lax.all_gather(dense[6], ("ulysses", "blk"), axis=0, tiled=True),
        lax.all_gather(dense[7], ("ulysses", "blk"), axis=0, tiled=True),
    )
    w_q, w_k, w_v, w_o = (gathered[0], gathered[1], gathered[2], gathered[3])
    gain_one = gathered[4].astype(jnp.float32)
    gain_q = gathered[5].astype(jnp.float32)
    gain_k = gathered[6].astype(jnp.float32)
    gain_two = gathered[7].astype(jnp.float32)
    normed_one = norm_rows(layer_in, gain_one).astype(jnp.bfloat16)
    q_lin = jnp.dot(normed_one, w_q, preferred_element_type=jnp.float32)
    k_lin = jnp.dot(normed_one, w_k, preferred_element_type=jnp.float32)
    v_lin = jnp.dot(normed_one, w_v, preferred_element_type=jnp.float32)
    (q_rot, k_rot), pre_back = jax.vjp(
        lambda q_in, k_in, gq_in, gk_in: attn_inputs(q_in, k_in, gq_in, gk_in, positions),
        q_lin,
        k_lin,
        gain_q,
        gain_k,
    )
    q_heads, k_heads, v_heads = to_head_layout(
        (q_rot.astype(jnp.bfloat16), k_rot.astype(jnp.bfloat16), v_lin.astype(jnp.bfloat16))
    )
    group_ids = jnp.arange(groups, dtype=jnp.int32)[:, None]
    row_ids = jnp.arange(local_rows, dtype=jnp.int32)[None, :]
    q_pos = (group_ids * blk_size + blk_index) * local_rows + row_ids
    q_seg = segments[q_pos]
    four_shape = (groups, local_rows, heads_dev, HEAD_DIM)
    q_four = q_heads.reshape(four_shape)

    def score_block(k_now, source):
        k_pos = (group_ids * blk_size + source) * local_rows + row_ids
        k_seg = banded(segments[k_pos], -1)
        k_pos = banded(k_pos, 0)
        k_band = banded(k_now.reshape(four_shape), 0)
        raw_scores = (
            jnp.einsum("gqhd,gkhd->gqhk", q_four, k_band, preferred_element_type=jnp.float32)
            * score_scale
        )
        allowed = (k_seg[:, None, :] == q_seg[:, :, None]) & (
            k_pos[:, None, :] <= q_pos[:, :, None]
        )
        return (raw_scores, allowed[:, :, None, :], k_band)

    def forward_step(flash_state, kv_stack, step_id):
        run_max, run_sum, run_out = flash_state
        source = jnp.mod(blk_index - step_id, blk_size)
        raw_scores, allowed, k_band = score_block(kv_stack[0], source)
        raw_scores = jnp.where(allowed, raw_scores, NEG)
        new_max = jnp.maximum(run_max, jnp.max(raw_scores, axis=-1))
        shrink = jnp.exp(run_max - new_max)
        weights = jnp.where(allowed, jnp.exp(raw_scores - new_max[..., None]), 0.0)
        run_sum = run_sum * shrink + jnp.sum(weights, axis=-1)
        v_band = banded(kv_stack[1].reshape(four_shape), 0)
        run_out = run_out * shrink[..., None] + jnp.einsum(
            "gqhk,gkhd->gqhd",
            weights.astype(jnp.bfloat16),
            v_band,
            preferred_element_type=jnp.float32,
        )
        return (new_max, run_sum, run_out)

    start_state = (
        jnp.full((groups, local_rows, heads_dev), NEG, jnp.float32),
        jnp.zeros((groups, local_rows, heads_dev), jnp.float32),
        jnp.zeros(four_shape, jnp.float32),
    )
    kv_home = jnp.stack([k_heads, v_heads])
    first_state = forward_step(start_state, kv_home, 0)

    def forward_turn(step_id, loop_state):
        flash_state, kv_stack = loop_state
        moved = passed_along(kv_stack, "blk", 1)
        return (forward_step(flash_state, moved, step_id), moved)

    final_state, unused_kv = lax.fori_loop(1, blk_size, forward_turn, (first_state, kv_home))
    run_max, run_sum, run_out = final_state
    o_four = (run_out / run_sum[..., None]).astype(jnp.bfloat16)
    log_total = run_max + jnp.log(run_sum)
    o_heads = o_four.reshape(groups * local_rows, heads_dev * HEAD_DIM)
    attended = to_token_layout(o_heads)
    residual = layer_in + jnp.dot(attended, w_o, preferred_element_type=jnp.float32)
    normed_two_f, norm_two_back = jax.vjp(norm_rows, residual, gain_two)
    normed_two = normed_two_f.astype(jnp.bfloat16)
    experts_n = devices // 2
    topk = expert_ids.shape[1]
    per_source = 2 * local_rows * topk // experts_n
    half_slots = per_source // 2
    capacity = 9 * local_rows * devices * topk // (8 * experts_n)
    slots_all = experts_n * per_source
    tokens_local = jnp.arange(local_rows, dtype=jnp.int32)
    chosen = jnp.sum(
        (expert_ids[:, :, None] == jnp.arange(experts_n, dtype=jnp.int32)[None, None, :]).astype(
            jnp.int32
        ),
        axis=1,
    )
    by_fill = jnp.zeros((local_rows,), jnp.int32).at[fill_order].set(tokens_local)
    sorted_rows = chosen[by_fill]
    before = jnp.cumsum(sorted_rows, axis=0) - sorted_rows
    rank_all = before[fill_order]
    pair_rank = jnp.take_along_axis(rank_all, expert_ids, axis=1)
    counts = jnp.sum(chosen, axis=0)
    offsets = prefix(counts, ("ulysses", "blk"), add_counts, jnp.zeros_like(counts))
    kept_pair = offsets[expert_ids] + pair_rank < capacity
    pair_slot = expert_ids * per_source + pair_rank
    pair_index = tokens_local[:, None] * topk + jnp.arange(topk, dtype=jnp.int32)[None, :]
    slot_pair = (
        jnp.zeros((slots_all,), jnp.int32).at[pair_slot.reshape(-1)].set(pair_index.reshape(-1))
    )
    slot_live = (
        jnp.zeros((slots_all,), jnp.bool_).at[pair_slot.reshape(-1)].set(kept_pair.reshape(-1))
    )
    slot_token = slot_pair // topk
    send_rows = jnp.where(slot_live[:, None], normed_two[slot_token], jnp.zeros((), jnp.bfloat16))
    received = expert_move(send_rows.reshape(devices, half_slots, model_width)).reshape(
        devices * half_slots, model_width
    )
    parity = jnp.mod(blk_index, 2)
    partner = partner_2((expert_gate, expert_up, expert_down), "blk", 0)

    def joined(own_half, other_half):
        lower_part = jnp.where(parity == 0, own_half, other_half)
        upper_part = jnp.where(parity == 0, other_half, own_half)
        return jnp.concatenate([lower_part, upper_part], axis=0)

    gate_full = joined(expert_gate, partner[0])
    up_full = joined(expert_up, partner[1])
    down_full = joined(expert_down, partner[2])
    gate_pre = jnp.dot(received, gate_full, preferred_element_type=jnp.float32)
    up_pre = jnp.dot(received, up_full, preferred_element_type=jnp.float32)
    hidden = (jax.nn.silu(gate_pre) * up_pre).astype(jnp.bfloat16)
    produced = jnp.dot(hidden, down_full, preferred_element_type=jnp.float32).astype(jnp.bfloat16)
    returned = expert_move(produced.reshape(devices, half_slots, model_width)).reshape(
        slots_all, model_width
    )
    pair_share = jnp.where(kept_pair, gate_weights, 0.0)
    mixed = jnp.einsum("tk,tkd->td", pair_share, returned[pair_slot].astype(jnp.float32))
    output = residual + mixed
    grad_out = cotangent.astype(jnp.float32)
    slot_share = jnp.where(slot_live, gate_weights.reshape(-1)[slot_pair], 0.0)
    grad_send = (slot_share[:, None] * grad_out[slot_token]).astype(jnp.bfloat16)
    grad_rows = expert_move(grad_send.reshape(devices, half_slots, model_width)).reshape(
        devices * half_slots, model_width
    )
    d_down_full = jnp.einsum("rf,rd->fd", hidden, grad_rows, preferred_element_type=jnp.float32)
    d_hidden = jnp.einsum("rd,fd->rf", grad_rows, down_full, preferred_element_type=jnp.float32)
    sigma = jax.nn.sigmoid(gate_pre)
    d_gate_pre = (d_hidden * up_pre * sigma * (1.0 + gate_pre * (1.0 - sigma))).astype(jnp.bfloat16)
    d_up_pre = (d_hidden * gate_pre * sigma).astype(jnp.bfloat16)
    d_gate_full = jnp.einsum("rd,rf->df", received, d_gate_pre, preferred_element_type=jnp.float32)
    d_up_full = jnp.einsum("rd,rf->df", received, d_up_pre, preferred_element_type=jnp.float32)
    d_pair_rows = (
        jnp.einsum("rf,df->rd", d_gate_pre, gate_full, preferred_element_type=jnp.float32)
        + jnp.einsum("rf,df->rd", d_up_pre, up_full, preferred_element_type=jnp.float32)
    ).astype(jnp.bfloat16)
    back_rows = expert_move(d_pair_rows.reshape(devices, half_slots, model_width)).reshape(
        slots_all, model_width
    )
    d_normed_two = jnp.sum(
        jnp.where(kept_pair[:, :, None], back_rows[pair_slot].astype(jnp.float32), 0.0), axis=1
    )
    half_rows = expert_gate.shape[0]
    half_hidden = expert_down.shape[0]

    def halves(full_grad, size):
        own_half = lax.dynamic_slice_in_dim(full_grad, parity * size, size, 0)
        other_half = lax.dynamic_slice_in_dim(full_grad, (1 - parity) * size, size, 0)
        return (own_half, other_half)

    gate_own, gate_other = halves(d_gate_full, half_rows)
    up_own, up_other = halves(d_up_full, half_rows)
    down_own, down_other = halves(d_down_full, half_hidden)
    partner_grads = (
        partner_2(gate_other.astype(jnp.bfloat16), "blk", 0).astype(gate_other.dtype),
        partner_2(up_other.astype(jnp.bfloat16), "blk", 0).astype(up_other.dtype),
        partner_2(down_other.astype(jnp.bfloat16), "blk", 0).astype(down_other.dtype),
    )
    d_expert_gate = gate_own + partner_grads[0]
    d_expert_up = up_own + partner_grads[1]
    d_expert_down = down_own + partner_grads[2]
    d_resid_norm, d_gain_two = norm_two_back(d_normed_two)
    d_residual = grad_out + d_resid_norm
    d_res_low = d_residual.astype(jnp.bfloat16)
    d_attended = jnp.einsum("te,de->td", d_res_low, w_o, preferred_element_type=jnp.float32).astype(
        jnp.bfloat16
    )
    d_o_heads = to_head_layout(d_attended)
    d_o_four = d_o_heads.reshape(four_shape)
    row_delta = jnp.sum(d_o_four.astype(jnp.float32) * o_four.astype(jnp.float32), axis=-1)

    def back_turn(step_id, loop_state):
        moving, dq_acc = loop_state
        source = jnp.mod(blk_index - step_id, blk_size)
        k_now = moving[0].astype(jnp.bfloat16)
        v_now = moving[1].astype(jnp.bfloat16)
        raw_scores, allowed, k_band = score_block(k_now, source)
        prob_rows = jnp.where(allowed, jnp.exp(raw_scores - log_total[..., None]), 0.0)
        v_band = banded(v_now.reshape(four_shape), 0)
        d_probs = jnp.einsum(
            "gqhd,gkhd->gqhk", d_o_four, v_band, preferred_element_type=jnp.float32
        )
        d_scores = (prob_rows * (d_probs - row_delta[..., None])).astype(jnp.bfloat16)
        dv_band = jnp.einsum(
            "gqhk,gqhd->gkhd",
            prob_rows.astype(jnp.bfloat16),
            d_o_four,
            preferred_element_type=jnp.float32,
        )
        dk_band = (
            jnp.einsum("gqhk,gqhd->gkhd", d_scores, q_four, preferred_element_type=jnp.float32)
            * score_scale
        )
        dq_acc = (
            dq_acc
            + jnp.einsum("gqhk,gkhd->gqhd", d_scores, k_band, preferred_element_type=jnp.float32)
            * score_scale
        )
        flat_shape = moving[2].shape
        dk_new = moving[2] + unbanded(dk_band, local_rows).reshape(flat_shape)
        dv_new = moving[3] + unbanded(dv_band, local_rows).reshape(flat_shape)
        moving = passed_along(
            jnp.stack([moving[0], moving[1], dk_new, dv_new]).astype(jnp.bfloat16), "blk", 1
        ).astype(jnp.float32)
        return (moving, dq_acc)

    zero_rows = jnp.zeros(k_heads.shape, jnp.float32)
    start_moving = jnp.stack(
        [k_heads.astype(jnp.float32), v_heads.astype(jnp.float32), zero_rows, zero_rows]
    )
    moving, dq_acc = lax.fori_loop(
        0, blk_size, back_turn, (start_moving, jnp.zeros(four_shape, jnp.float32))
    )
    d_q_send = dq_acc.astype(jnp.bfloat16).reshape(k_heads.shape)
    d_k_send = moving[2].astype(jnp.bfloat16)
    d_v_send = moving[3].astype(jnp.bfloat16)
    d_q_rot, d_k_rot, d_v_lin = to_token_layout((d_q_send, d_k_send, d_v_send))
    d_q_lin, d_k_lin, d_gain_q, d_gain_k = pre_back(
        (d_q_rot.astype(jnp.float32), d_k_rot.astype(jnp.float32))
    )
    d_q_low = d_q_lin.astype(jnp.bfloat16)
    d_k_low = d_k_lin.astype(jnp.bfloat16)
    d_normed_one = jnp.einsum("te,de->td", d_q_low, w_q, preferred_element_type=jnp.float32)
    d_normed_one = d_normed_one + jnp.einsum(
        "te,de->td", d_k_low, w_k, preferred_element_type=jnp.float32
    )
    d_normed_one = d_normed_one + jnp.einsum(
        "te,de->td", d_v_lin, w_v, preferred_element_type=jnp.float32
    )
    unused_norm, norm_one_back = jax.vjp(norm_rows, layer_in, gain_one)
    d_layer_in, d_gain_one = norm_one_back(d_normed_one)
    d_inputs = d_residual + d_layer_in
    d_qk_heads = to_head_layout((d_q_low, d_k_low))
    rows_all = (
        lax.all_gather(normed_one, "ulysses", axis=0, tiled=True),
        lax.all_gather(d_res_low, "ulysses", axis=0, tiled=True),
    )
    head_cols = model_width // groups
    piece_rows = model_width // devices

    def by_owner(part):
        rest = part.shape[1:]
        shaped = part.reshape((groups, blk_size, piece_rows) + rest)
        return jnp.swapaxes(shaped, 0, 1).reshape((model_width,) + rest)

    part_q = jnp.einsum("td,te->de", rows_all[0], d_qk_heads[0], preferred_element_type=jnp.float32)
    part_k = jnp.einsum("td,te->de", rows_all[0], d_qk_heads[1], preferred_element_type=jnp.float32)
    part_v = jnp.einsum("td,te->de", rows_all[0], d_v_send, preferred_element_type=jnp.float32)
    part_o = jnp.einsum("te,td->ed", o_heads, rows_all[1], preferred_element_type=jnp.float32)
    blk_sums = (
        lax.psum_scatter(
            by_owner(part_q).astype(jnp.bfloat16), "blk", scatter_dimension=0, tiled=True
        ).astype(jnp.float32),
        lax.psum_scatter(
            by_owner(part_k).astype(jnp.bfloat16), "blk", scatter_dimension=0, tiled=True
        ).astype(jnp.float32),
        lax.psum_scatter(
            by_owner(part_v).astype(jnp.bfloat16), "blk", scatter_dimension=0, tiled=True
        ).astype(jnp.float32),
        lax.psum_scatter(
            part_o.astype(jnp.bfloat16), "blk", scatter_dimension=0, tiled=True
        ).astype(jnp.float32),
        lax.psum_scatter(
            by_owner(d_gain_one).astype(jnp.bfloat16), "blk", scatter_dimension=0, tiled=True
        ).astype(jnp.float32),
        lax.psum_scatter(
            by_owner(d_gain_q).astype(jnp.bfloat16), "blk", scatter_dimension=0, tiled=True
        ).astype(jnp.float32),
        lax.psum_scatter(
            by_owner(d_gain_k).astype(jnp.bfloat16), "blk", scatter_dimension=0, tiled=True
        ).astype(jnp.float32),
        lax.psum_scatter(
            by_owner(d_gain_two).astype(jnp.bfloat16), "blk", scatter_dimension=0, tiled=True
        ).astype(jnp.float32),
    )

    def widened(part):
        return lax.dynamic_update_slice_in_dim(
            jnp.zeros((part.shape[0], model_width), jnp.float32), part, group_index * head_cols, 1
        )

    col_sums = (
        lax.psum_scatter(
            widened(blk_sums[0]).astype(jnp.bfloat16), "ulysses", scatter_dimension=0, tiled=True
        ).astype(jnp.float32),
        lax.psum_scatter(
            widened(blk_sums[1]).astype(jnp.bfloat16), "ulysses", scatter_dimension=0, tiled=True
        ).astype(jnp.float32),
        lax.psum_scatter(
            widened(blk_sums[2]).astype(jnp.bfloat16), "ulysses", scatter_dimension=0, tiled=True
        ).astype(jnp.float32),
        lax.psum_scatter(
            blk_sums[4].astype(jnp.bfloat16), "ulysses", scatter_dimension=0, tiled=True
        ).astype(jnp.float32),
        lax.psum_scatter(
            blk_sums[5].astype(jnp.bfloat16), "ulysses", scatter_dimension=0, tiled=True
        ).astype(jnp.float32),
        lax.psum_scatter(
            blk_sums[6].astype(jnp.bfloat16), "ulysses", scatter_dimension=0, tiled=True
        ).astype(jnp.float32),
        lax.psum_scatter(
            blk_sums[7].astype(jnp.bfloat16), "ulysses", scatter_dimension=0, tiled=True
        ).astype(jnp.float32),
    )
    result_grads = (
        col_sums[0],
        col_sums[1],
        col_sums[2],
        blk_sums[3],
        col_sums[3],
        col_sums[4],
        col_sums[5],
        col_sums[6],
    )
    return (
        output,
        d_inputs,
        result_grads[4],
        result_grads[0],
        result_grads[1],
        result_grads[2],
        result_grads[3],
        result_grads[5],
        result_grads[6],
        result_grads[7],
        d_expert_gate,
        d_expert_up,
        d_expert_down,
    )


MESH = pl.DeviceIdType.MESH
P1 = 96

def place():
    u = lax.axis_index("ulysses"); z = lax.axis_index("z"); c = lax.axis_index("core")
    return u, z, c

def ag_kernel(cut, x_ref, o_ref, local_sem, s_sem, zr, xr, yr, d1r, d2r, bs, br, bzr):
    u, z, c = place()
    Z = 4
    R = x_ref.shape[0]
    ux, uy = u ^ 1, u ^ 2
    xn, yn, up, dn = (ux, z, c), (uy, z, c), (u, z + 1, c), (u, z - 1, c)
    has_up, has_dn = z < Z - 1, z > 0
    bar = pltpu.get_barrier_semaphore()
    for n in (xn, yn):
        pl.semaphore_signal(bar, inc=1, device_id=n, device_id_type=MESH)
    @pl.when(has_up)
    def _():
        pl.semaphore_signal(bar, inc=1, device_id=up, device_id_type=MESH)
    @pl.when(has_dn)
    def _():
        pl.semaphore_signal(bar, inc=1, device_id=dn, device_id_type=MESH)
    pl.semaphore_wait(bar, 2 + has_up.astype(jnp.int32) + has_dn.astype(jnp.int32))
    sends = []
    def copy(src, dst, ss, rs, dev):
        return pltpu.make_async_remote_copy(src_ref=src, dst_ref=dst, send_sem=ss, recv_sem=rs, device_id=dev, device_id_type=MESH)
    def go(cond, make):
        idx = len(sends)
        def mk():
            return make(s_sem.at[idx])
        sends.append((cond, mk))
        if cond is None:
            mk().start()
        else:
            pl.when(cond)(lambda: mk().start())
    def both(a, b):
        if a is None: return b
        if b is None: return a
        return jnp.logical_and(a, b)
    def wait(cond, ref, sem):
        def w():
            pltpu.make_async_copy(ref, ref, sem).wait()
        if cond is None: w()
        else: pl.when(cond)(w)
    own = pltpu.make_async_copy(x_ref, o_ref.at[u, z], local_sem)
    own.start()
    A = slice(0, cut)
    h = cut // 2
    def oa(uu, zz, lo=0, n=cut):
        return o_ref.at[uu, zz, pl.ds(lo, n), :]
    def spread(s, zz, cond):
        src = (lambda: x_ref.at[pl.ds(0, cut), :]) if s == 0 else (lambda: oa(u, zz))
        go(cond, lambda sm: copy(src(), oa(u, zz), sm, xr.at[zz], xn))
        go(cond, lambda sm: copy(src(), oa(u, zz), sm, yr.at[zz], yn))
    def cross(zz, cond):
        wait(cond, oa(ux, zz), xr.at[zz])
        go(cond, lambda sm: copy(oa(ux, zz, 0, h), oa(ux, zz, 0, h), sm, d1r.at[zz], yn))
        wait(cond, oa(uy, zz), yr.at[zz])
        go(cond, lambda sm: copy(oa(uy, zz, h, h), oa(uy, zz, h, h), sm, d2r.at[zz], xn))
    rb = R - cut
    hb = rb // 2
    def ob(uu, zz, lo=0, n=None):
        return o_ref.at[uu, zz, pl.ds(cut + lo, rb if n is None else n), :]
    go(has_up, lambda sm: copy(x_ref.at[pl.ds(0, cut), :], oa(u, z), sm, zr.at[z], up))
    go(has_dn, lambda sm: copy(x_ref.at[pl.ds(0, cut), :], oa(u, z), sm, zr.at[z], dn))
    if rb:
        go(None, lambda sm: copy(x_ref.at[pl.ds(cut, rb), :], ob(u, z), sm, br.at[0], xn))
        go(None, lambda sm: copy(x_ref.at[pl.ds(cut, rb), :], ob(u, z), sm, br.at[1], yn))
    spread(0, z, None)
    if rb:
        wait(None, ob(ux, z), br.at[0])
        go(None, lambda sm: copy(ob(ux, z, 0, hb), ob(ux, z, 0, hb), sm, br.at[2], yn))
        wait(None, ob(uy, z), br.at[1])
        go(None, lambda sm: copy(ob(uy, z, hb, hb), ob(uy, z, hb, hb), sm, br.at[3], xn))
    own.wait()
    def quad(zz):
        return o_ref.at[:, zz, pl.ds(cut, rb), :]
    def zs(s):
        zl, zh = z - s, z + s
        cl, ch = zl >= 0, zh < Z
        zlc, zhc = jnp.maximum(zl, 0), jnp.minimum(zh, Z - 1)
        return (zlc, cl, has_up, up), (zhc, ch, has_dn, dn)
    prev = [(z, None)]
    for s in range(1, Z):
        cur = []
        for (zz, cond, fwd, dev) in zs(s):
            wait(cond, oa(u, zz), zr.at[zz])
            go(both(cond, fwd), lambda sm, zz=zz, dev=dev: copy(oa(u, zz), oa(u, zz), sm, zr.at[zz], dev))
            spread(s, zz, cond)
            cur.append((zz, cond))
        if rb and s == 1:
            wait(None, ob(u ^ 3, z, 0, hb), br.at[2])
            wait(None, ob(u ^ 3, z, hb, hb), br.at[3])
            go(has_up, lambda sm: copy(quad(z), quad(z), sm, bzr.at[z], up))
            go(has_dn, lambda sm: copy(quad(z), quad(z), sm, bzr.at[z], dn))
        elif rb:
            for (zz, cond, fwd, dev) in zs(s - 1):
                wait(cond, quad(zz), bzr.at[zz])
                go(both(cond, fwd), lambda sm, zz=zz, dev=dev: copy(quad(zz), quad(zz), sm, bzr.at[zz], dev))
        for zz, cond in prev:
            cross(zz, cond)
        prev = cur
    if rb:
        for (zz, cond, fwd, dev) in zs(Z - 1):
            wait(cond, quad(zz), bzr.at[zz])
    for zz, cond in prev:
        cross(zz, cond)
    for zz in range(Z):
        wait(None, oa(u ^ 3, zz, 0, h), d1r.at[zz])
        wait(None, oa(u ^ 3, zz, h, h), d2r.at[zz])
    for cond, mk in sends:
        if cond is None: mk().wait_send()
        else: pl.when(cond)(lambda mk=mk: mk().wait_send())

def ag16(x, cid, cut=P1, space=pl.ANY):
    R, D = x.shape
    DMA = pltpu.SemaphoreType.DMA
    return pl.pallas_call(
        functools.partial(ag_kernel, cut),
        out_shape=jax.ShapeDtypeStruct((4, 4, R, D), x.dtype),
        in_specs=[pl.BlockSpec(memory_space=space)],
        out_specs=pl.BlockSpec(memory_space=space),
        scratch_shapes=[DMA, DMA((64,)), DMA((4,)), DMA((4,)), DMA((4,)), DMA((4,)), DMA((4,)), DMA((4,)), DMA((4,)), DMA((4,))],
        compiler_params=pltpu.CompilerParams(collective_id=cid, has_side_effects=True, vmem_limit_bytes=48 * 2**20),
        name="gather_rows",
    )(x)
F32 = jnp.float32
BF = jnp.bfloat16

class Net:
    def __init__(self, sems):
        self.sems, self.sends = sems, []
        self.u, self.z, self.c = place()
        u, z, c = self.u, self.z, self.c
        self.ux, self.uy, self.ud = u ^ 1, u ^ 2, u ^ 3
        self.xn, self.yn, self.up, self.dn = (u ^ 1, z, c), (u ^ 2, z, c), (u, z + 1, c), (u, z - 1, c)
        self.has_up, self.has_dn = z < 3, z > 0
    def barrier(self):
        bar = pltpu.get_barrier_semaphore()
        for n in (self.xn, self.yn):
            pl.semaphore_signal(bar, inc=1, device_id=n, device_id_type=MESH)
        for cond, n in ((self.has_up, self.up), (self.has_dn, self.dn)):
            pl.when(cond)(lambda n=n: pl.semaphore_signal(bar, inc=1, device_id=n, device_id_type=MESH))
        pl.semaphore_wait(bar, 2 + self.has_up.astype(jnp.int32) + self.has_dn.astype(jnp.int32))
    def go(self, cond, src, dst, rsem, dev):
        idx = len(self.sends)
        def mk():
            return pltpu.make_async_remote_copy(src_ref=src(), dst_ref=dst(), send_sem=self.sems.at[idx], recv_sem=rsem, device_id=dev, device_id_type=MESH)
        self.sends.append((cond, mk))
        if cond is None: mk().start()
        else: pl.when(cond)(lambda: mk().start())
    def wait(self, cond, ref, sem):
        def w(): pltpu.make_async_copy(ref(), ref(), sem).wait()
        if cond is None: w()
        else: pl.when(cond)(w)
    def finish(self):
        for cond, mk in self.sends:
            if cond is None: mk().wait_send()
            else: pl.when(cond)(lambda mk=mk: mk().wait_send())

def strips(rows, body, step=16):
    def it(i, _):
        body(pl.ds(pl.multiple_of(i * step, step), step))
        return 0
    lax.fori_loop(0, rows // step, it, 0)

def rs_body(net, cut, P, out_store, mid1, mid2, fx, fy, be, ab, bbe, bab, bm, m1s, m2s, fxs, fys, bes, abs_, bbes, babs, bms):
    u, z = net.u, net.z
    R = P.shape[2]
    h = cut // 2
    rb = R - cut
    hb = rb // 2
    order = (3, 0, 2, 1)
    f = lambda v: v.astype(F32)
    for zd in order:
        net.go(None, lambda: P.at[net.ud, zd, pl.ds(0, h), :], lambda: mid1.at[zd], m1s.at[zd], net.xn)
        net.go(None, lambda: P.at[net.ud, zd, pl.ds(h, h), :], lambda: mid2.at[zd], m2s.at[zd], net.yn)
    def bsend(zd, first):
        lo, hi = net.z < zd, net.z > zd
        if first:
            net.go(z == 0, lambda: P.at[:, zd, pl.ds(cut, rb), :], lambda: bbe.at[zd], bbes.at[zd], net.up)
            net.go(z == 3, lambda: P.at[:, zd, pl.ds(cut, rb), :], lambda: bab.at[zd], babs.at[zd], net.dn)
    for zd in order:
        if zd > 0:
            net.go(z == 0, lambda: P.at[:, zd, pl.ds(cut, rb), :], lambda: bbe.at[zd], bbes.at[zd], net.up)
        if zd < 3:
            net.go(z == 3, lambda: P.at[:, zd, pl.ds(cut, rb), :], lambda: bab.at[zd], babs.at[zd], net.dn)
    for zd in order:
        net.go(None, lambda: P.at[net.ux, zd, pl.ds(0, h), :], lambda: fx.at[zd, pl.ds(0, h), :], fxs.at[zd, 0], net.xn)
        net.go(None, lambda: P.at[net.uy, zd, pl.ds(h, h), :], lambda: fy.at[zd, pl.ds(h, h), :], fys.at[zd, 1], net.yn)
    def bpass(zd):
        def addto(buf, zd):
            for q in range(4):
                strips(rb, lambda sl: buf.__setitem__((zd, q, sl, slice(None)), (f(buf[zd, q, sl, :]) + f(P[q, zd, pl.ds(cut + sl.start, 16), :])).astype(BF)))
        up_mid = jnp.logical_and(z > 0, z < zd)
        net.wait(up_mid, lambda: bbe.at[zd], bbes.at[zd])
        pl.when(up_mid)(lambda: addto(bbe, zd))
        net.go(up_mid, lambda: bbe.at[zd], lambda: bbe.at[zd], bbes.at[zd], net.up)
        dn_mid = jnp.logical_and(z < 3, z > zd)
        net.wait(dn_mid, lambda: bab.at[zd], babs.at[zd])
        pl.when(dn_mid)(lambda: addto(bab, zd))
        net.go(dn_mid, lambda: bab.at[zd], lambda: bab.at[zd], babs.at[zd], net.dn)
    for zd in order:
        net.wait(None, lambda: mid1.at[zd], m1s.at[zd])
        strips(h, lambda sl: mid1.__setitem__((zd, sl, slice(None)), (f(mid1[zd, sl, :]) + f(P[net.uy, zd, sl, :])).astype(BF)))
        net.go(None, lambda: mid1.at[zd], lambda: fy.at[zd, pl.ds(0, h), :], fys.at[zd, 0], net.yn)
        net.wait(None, lambda: mid2.at[zd], m2s.at[zd])
        strips(h, lambda sl: mid2.__setitem__((zd, sl, slice(None)), (f(mid2[zd, sl, :]) + f(P[net.ux, zd, pl.ds(h + sl.start, 16), :])).astype(BF)))
        net.go(None, lambda: mid2.at[zd], lambda: fx.at[zd, pl.ds(h, h), :], fxs.at[zd, 1], net.xn)
        if rb:
            bpass(zd)
    def line(zd):
        for half in (0, 1):
            net.wait(None, lambda: fx.at[zd, pl.ds(half * h, h), :], fxs.at[zd, half])
            net.wait(None, lambda: fy.at[zd, pl.ds(half * h, h), :], fys.at[zd, half])
        def local(sl):
            return f(P[u, zd, sl, :]) + f(fx[zd, sl, :]) + f(fy[zd, sl, :])
        def start_sum(sl):
            fx[zd, sl, :] = local(sl).astype(BF)
        def plus(buf):
            def g(sl): buf[zd, sl, :] = (local(sl) + f(buf[zd, sl, :])).astype(BF)
            return g
        if zd > 0:
            pl.when(z == 0)(lambda: strips(cut, start_sum))
            net.go(z == 0, lambda: fx.at[zd], lambda: be.at[zd], bes.at[zd], net.up)
            mid = jnp.logical_and(z > 0, z < zd)
            net.wait(mid, lambda: be.at[zd], bes.at[zd])
            pl.when(mid)(lambda: strips(cut, plus(be)))
            net.go(mid, lambda: be.at[zd], lambda: be.at[zd], bes.at[zd], net.up)
        if zd < 3:
            pl.when(z == 3)(lambda: strips(cut, start_sum))
            net.go(z == 3, lambda: fx.at[zd], lambda: ab.at[zd], abs_.at[zd], net.dn)
            mid = jnp.logical_and(z < 3, z > zd)
            net.wait(mid, lambda: ab.at[zd], abs_.at[zd])
            pl.when(mid)(lambda: strips(cut, plus(ab)))
            net.go(mid, lambda: ab.at[zd], lambda: ab.at[zd], abs_.at[zd], net.dn)
    def bquad():
        net.wait(net.has_dn, lambda: bbe.at[z], bbes.at[z])
        net.wait(net.has_up, lambda: bab.at[z], babs.at[z])
        def fold(q, sl):
            s = f(P[q, z, pl.ds(cut + sl.start, 16), :])
            s = s + jnp.where(net.has_dn, f(bbe[z, q, sl, :]), 0.0)
            s = s + jnp.where(net.has_up, f(bab[z, q, sl, :]), 0.0)
            bm[q, sl, :] = s.astype(BF)
        for q in range(4):
            strips(rb, lambda sl: fold(q, sl))
        net.go(None, lambda: bm.at[net.ud, pl.ds(0, hb), :], lambda: bm.at[4, pl.ds(0, hb), :], bms.at[0], net.xn)
        net.go(None, lambda: bm.at[net.ud, pl.ds(hb, hb), :], lambda: bm.at[5, pl.ds(0, hb), :], bms.at[1], net.yn)
        net.go(None, lambda: bm.at[net.ux, pl.ds(0, hb), :], lambda: bm.at[6, pl.ds(0, hb), :], bms.at[2], net.xn)
        net.go(None, lambda: bm.at[net.uy, pl.ds(hb, hb), :], lambda: bm.at[7, pl.ds(hb, hb), :], bms.at[3], net.yn)
    def bquad2():
        net.wait(None, lambda: bm.at[4, pl.ds(0, hb), :], bms.at[0])
        strips(hb, lambda sl: bm.__setitem__((4, sl, slice(None)), (f(bm[4, sl, :]) + f(bm[net.uy, sl, :])).astype(BF)))
        net.go(None, lambda: bm.at[4, pl.ds(0, hb), :], lambda: bm.at[7, pl.ds(0, hb), :], bms.at[4], net.yn)
        net.wait(None, lambda: bm.at[5, pl.ds(0, hb), :], bms.at[1])
        strips(hb, lambda sl: bm.__setitem__((5, sl, slice(None)), (f(bm[5, sl, :]) + f(bm[net.ux, pl.ds(hb + sl.start, 16), :])).astype(BF)))
        net.go(None, lambda: bm.at[5, pl.ds(0, hb), :], lambda: bm.at[6, pl.ds(hb, hb), :], bms.at[5], net.xn)
    line(3)
    line(0)
    if rb:
        bquad()
    line(2)
    if rb:
        bquad2()
    line(1)
    def last(sl):
        s = f(P[u, z, sl, :]) + f(fx[z, sl, :]) + f(fy[z, sl, :])
        s = s + jnp.where(net.has_dn, f(be[z, sl, :]), 0.0)
        s = s + jnp.where(net.has_up, f(ab[z, sl, :]), 0.0)
        out_store(sl, s)
    net.wait(net.has_dn, lambda: be.at[z], bes.at[z])
    net.wait(net.has_up, lambda: ab.at[z], abs_.at[z])
    strips(cut, last)
    if rb:
        net.wait(None, lambda: bm.at[6, pl.ds(0, hb), :], bms.at[2])
        net.wait(None, lambda: bm.at[6, pl.ds(hb, hb), :], bms.at[5])
        net.wait(None, lambda: bm.at[7, pl.ds(0, hb), :], bms.at[4])
        net.wait(None, lambda: bm.at[7, pl.ds(hb, hb), :], bms.at[3])
        strips(rb, lambda sl: out_store(pl.ds(cut + sl.start, 16), f(bm[u, sl, :]) + f(bm[6, sl, :]) + f(bm[7, sl, :])))

def rs_scratch(cut, R, D):
    h, rb = cut // 2, R - cut
    V = lambda *s: pltpu.VMEM(s, BF)
    S = pltpu.SemaphoreType.DMA
    return [V(4, h, D), V(4, h, D), V(4, cut, D), V(4, cut, D), V(4, cut, D), V(4, cut, D),
            V(4, 4, max(rb, 16), D), V(4, 4, max(rb, 16), D), V(8, max(rb, 16), D),
            S((4,)), S((4,)), S((4, 2)), S((4, 2)), S((4,)), S((4,)), S((4,)), S((4,)), S((6,))]

def rs_kernel(cut, P, o_ref, ssem, *scr):
    net = Net(ssem)
    net.barrier()
    def store(sl, v):
        o_ref[sl, :] = v.astype(o_ref.dtype)
    rs_body(net, cut, P, store, *scr)
    net.finish()

def rs16(p, cid, cut=96, dtype=F32):
    _, _, R, D = p.shape
    DMA = pltpu.SemaphoreType.DMA
    return pl.pallas_call(
        functools.partial(rs_kernel, cut),
        out_shape=jax.ShapeDtypeStruct((R, D), dtype),
        in_specs=[pl.BlockSpec(memory_space=pltpu.VMEM)],
        out_specs=pl.BlockSpec(memory_space=pltpu.VMEM),
        scratch_shapes=[DMA((96,))] + rs_scratch(cut, R, D),
        compiler_params=pltpu.CompilerParams(collective_id=cid, has_side_effects=True, vmem_limit_bytes=56 * 2**20),
        name="scatter_rows",
    )(p)
def swap_kernel(src, out, lsem, ssem, rsem):
    u, z, c = place()
    me = u * 8 + z * 2 + c
    count = out.shape[0]
    bar = pltpu.get_barrier_semaphore()

    def at(j):
        t = lax.rem(me + j, count)
        return t // 8, lax.rem(t, 8) // 2, lax.rem(t, 2), t // 2

    def hello(j, _):
        tu, tz, tc, _e = at(j)
        pl.semaphore_signal(bar, inc=1, device_id=(tu, tz, tc), device_id_type=MESH)
        return 0

    lax.fori_loop(1, count, hello, 0)
    pl.semaphore_wait(bar, count - 1)

    def copy(j):
        tu, tz, tc, e = at(j)
        return pltpu.make_async_remote_copy(
            src_ref=src.at[e], dst_ref=out.at[me], send_sem=ssem, recv_sem=rsem,
            device_id=(tu, tz, tc), device_id_type=MESH)

    own = pltpu.make_async_copy(src.at[me // 2], out.at[me], lsem)
    own.start()

    def send(j, _):
        copy(j).start()
        return 0

    lax.fori_loop(1, count, send, 0)
    own.wait()
    part = out.at[pl.ds(0, count - 1)]
    pltpu.make_async_copy(part, part, rsem).wait()
    pltpu.make_async_copy(part, part, ssem).wait()


def swap(block, cid):
    chips, r, lanes = block.shape
    S = pltpu.SemaphoreType.DMA
    return pl.pallas_call(
        swap_kernel,
        out_shape=jax.ShapeDtypeStruct((2 * chips, r, lanes), block.dtype),
        in_specs=[pl.BlockSpec(memory_space=pltpu.VMEM)],
        out_specs=pl.BlockSpec(memory_space=pltpu.VMEM),
        scratch_shapes=[S, S, S],
        compiler_params=pltpu.CompilerParams(collective_id=cid, has_side_effects=True),
        name="swap_rows",
    )(block)


def spread_kernel(src, out, lsem, ssem, rsem):
    u, z, c = place()
    me = u * 4 + z
    count = out.shape[0]
    bar = pltpu.get_barrier_semaphore()

    def at(j):
        t = lax.rem(me + j, count)
        return t // 4, lax.rem(t, 4), c

    def hello(j, _):
        pl.semaphore_signal(bar, inc=1, device_id=at(j), device_id_type=MESH)
        return 0

    lax.fori_loop(1, count, hello, 0)
    pl.semaphore_wait(bar, count - 1)
    own = pltpu.make_async_copy(src, out.at[me], lsem)
    own.start()

    def send(j, _):
        pltpu.make_async_remote_copy(
            src_ref=src, dst_ref=out.at[me], send_sem=ssem, recv_sem=rsem,
            device_id=at(j), device_id_type=MESH).start()
        return 0

    lax.fori_loop(1, count, send, 0)
    own.wait()
    part = out.at[pl.ds(0, count - 1)]
    pltpu.make_async_copy(part, part, rsem).wait()
    pltpu.make_async_copy(part, part, ssem).wait()


def spread(block, cid):
    S = pltpu.SemaphoreType.DMA
    return pl.pallas_call(
        spread_kernel,
        out_shape=jax.ShapeDtypeStruct((16,) + block.shape, block.dtype),
        in_specs=[pl.BlockSpec(memory_space=pltpu.VMEM)],
        out_specs=pl.BlockSpec(memory_space=pltpu.VMEM),
        scratch_shapes=[S, S, S],
        compiler_params=pltpu.CompilerParams(collective_id=cid, has_side_effects=True),
        name="spread_rows",
    )(block)


def band_scores(q, k, q_seg, k_seg, scale, reach):
    scores = dot(q, k, ((1,), (1,))) * scale
    q_at = lax.broadcasted_iota(jnp.int32, scores.shape, 0)
    k_at = lax.broadcasted_iota(jnp.int32, scores.shape, 1)
    return scores, (k_seg == q_seg) & (k_at <= q_at + reach)


def attend_kernel(scale, reach, q_ref, k_ref, v_ref, qs_ref, ks_ref, o_ref, l_ref):
    rows = q_ref.shape[0]
    first = pl.multiple_of((pl.program_id(0) * 2 + lax.axis_index("core")) * rows, rows)
    band = pl.ds(first, rows + reach)
    scores, allowed = band_scores(q_ref[...], k_ref[band, :], qs_ref[...], ks_ref[:, band], scale, reach)
    scores = jnp.where(allowed, scores, NEG)
    top = jnp.max(scores, axis=1, keepdims=True)
    weights = jnp.where(allowed, jnp.exp(scores - top), 0.0)
    total = jnp.sum(weights, axis=1, keepdims=True)
    probs = (weights / total).astype(BF)
    o_ref[...] = dot(probs, v_ref[band, :], ((1,), (0,))).astype(BF)
    l_ref[...] = top + jnp.log(total)


def attend_back_kernel(scale, reach, q_ref, k_ref, v_ref, qs_ref, ks_ref, l_ref, o_ref, do_ref, dq_ref, dk_ref, dv_ref):
    rows = q_ref.shape[0]

    @pl.when(pl.program_id(0) == 0)
    def _():
        dk_ref[...] = jnp.zeros_like(dk_ref)
        dv_ref[...] = jnp.zeros_like(dv_ref)

    first = pl.multiple_of((pl.program_id(0) * 2 + lax.axis_index("core")) * rows, rows)
    band = pl.ds(first, rows + reach)
    q, k, d_out = q_ref[...], k_ref[band, :], do_ref[...]
    scores, allowed = band_scores(q, k, qs_ref[...], ks_ref[:, band], scale, reach)
    probs = jnp.where(allowed, jnp.exp(scores - l_ref[...]), 0.0)
    d_probs = dot(d_out, v_ref[band, :], ((1,), (1,)))
    delta = jnp.sum(d_out.astype(F32) * o_ref[...].astype(F32), axis=1, keepdims=True)
    d_scores = (probs * (d_probs - delta)).astype(BF)
    dq_ref[...] = (dot(d_scores, k, ((1,), (0,))) * scale).astype(BF)
    dk_ref[band, :] += dot(d_scores, q, ((0,), (0,))) * scale
    dv_ref[band, :] += dot(probs.astype(BF), d_out, ((0,), (0,)))


def core_pair(value):
    return lax.ppermute(value, "core", [(0, 1), (1, 0)])


def dot(a, b, dims):
    return lax.dot_general(a, b, (dims, ((), ())), preferred_element_type=jnp.float32)


def local_chip(
    inputs, cotangent, segments, expert_ids, gate_weights, fill_order, norm1_gain, w_query, w_key,
    w_value, w_output, query_gain, key_gain, norm2_gain, expert_gate, expert_up, expert_down,
):
    chips = 16
    devices = 2 * chips
    rows, width = inputs.shape
    u, z, core = place()
    chip = u * 4 + z
    device = chip * 2 + core
    topk = expert_ids.shape[1]
    experts_n = chips
    capacity = 9 * rows * devices * topk // (8 * experts_n)
    one_hot = expert_ids[:, :, None] == jnp.arange(experts_n, dtype=jnp.int32)[None, None, :]
    chosen = jnp.any(one_hot, axis=1)
    weight = jnp.sum(jnp.where(one_hot, gate_weights[:, :, None], 0.0), axis=1)
    earlier = (fill_order[None, :] < fill_order[:, None]).astype(jnp.bfloat16)
    rank = dot(earlier, chosen.astype(jnp.bfloat16), ((1,), (0,)))
    rank = jnp.where(chosen, rank, -1.0)
    gains = jnp.concatenate([norm1_gain, query_gain, key_gain, norm2_gain]).astype(F32)
    gains = jnp.broadcast_to(gains.reshape(1, 2, 128), (chips, 2, 128))
    block = jnp.concatenate(
        [weight.T[:, None, :], rank.T[:, None, :], gains, jnp.zeros((chips, 4, 128), F32)], axis=1)
    swapped = swap(block, 1)
    gains = swapped[:, 2:4, :].reshape(devices, 4, 64).transpose(1, 0, 2).reshape(4, width)
    gain_one, gain_q, gain_k, gain_two = gains[0], gains[1], gains[2], gains[3]
    rank_all = swapped[:, 1, :]
    taken = rank_all >= 0.0
    counts = jnp.sum(taken.astype(F32), axis=1)
    before = jnp.cumsum(counts) - counts
    kept = taken & (before[:, None] + rank_all < float(capacity))
    share = jnp.where(kept, swapped[:, 0, :], 0.0).reshape(chips, 2, rows)
    share = lax.dynamic_index_in_dim(share, core, 1, keepdims=False).reshape(chips * rows, 1)


    layer_in = inputs.astype(F32)
    mine = ("ulysses", "z")

    def in_order(own, other):
        return jnp.where(core == 0, own, other), jnp.where(core == 0, other, own)

    cols = jnp.stack([w_query, w_key, w_value]).reshape(3, 64, chips, HEAD_DIM).transpose(2, 0, 1, 3)
    cols = lax.all_to_all(cols, mine, split_axis=0, concat_axis=0, tiled=True)
    cols = jnp.stack(in_order(cols, core_pair(cols)), axis=1)
    w_qkv = cols.transpose(0, 1, 3, 2, 4).reshape(width, 3 * HEAD_DIM)
    w_o = jnp.concatenate(in_order(w_output, core_pair(w_output)), axis=0)

    def my_head(gain):
        return lax.dynamic_slice_in_dim(gain, chip * HEAD_DIM, HEAD_DIM, 0)

    x_rows = ag16(inputs, 2).reshape(chips * rows, width).astype(F32)
    n1_rows = norm_rows(x_rows, gain_one).astype(BF)
    lin = dot(n1_rows, w_qkv, ((1,), (0,)))
    q_lin, k_lin, v_lin = lin[:, :HEAD_DIM], lin[:, HEAD_DIM : 2 * HEAD_DIM], lin[:, 2 * HEAD_DIM :]

    def over_chips(a, b, cid):
        both = jnp.stack([a, b]).reshape(2 * chips, rows)
        both = jnp.sum(spread(both, cid), axis=0).reshape(2, chips * rows, 1)
        return both[0], both[1]

    square_q, square_k = over_chips(jnp.sum(q_lin * q_lin, axis=1), jnp.sum(k_lin * k_lin, axis=1), 3)
    rq = lax.rsqrt(square_q / width + EPS)
    rk = lax.rsqrt(square_k / width + EPS)
    positions = (jnp.arange(chips, dtype=jnp.int32)[:, None] * 2 + core) * rows + jnp.arange(rows, dtype=jnp.int32)
    half_dim = HEAD_DIM // 2
    inv_freq = jnp.exp(jnp.arange(half_dim, dtype=F32) * (-2.0 * math.log(ROPE_BASE) / HEAD_DIM))
    angles = positions.reshape(-1).astype(F32)[:, None] * inv_freq[None, :]
    cosine, sine = jnp.cos(angles), jnp.sin(angles)
    cosine = jnp.concatenate([cosine, cosine], axis=1)
    sine = jnp.concatenate([-sine, sine], axis=1)

    def halves_swapped(v):
        return jnp.concatenate([v[:, half_dim:], v[:, :half_dim]], axis=1)

    def turn(v):
        return v * cosine + halves_swapped(v) * sine

    def turn_back(v):
        return v * cosine - halves_swapped(v) * sine

    gq, gk = my_head(gain_q), my_head(gain_k)
    q_rot = turn(q_lin * rq * gq).astype(BF)
    k_rot = turn(k_lin * rk * gk).astype(BF)
    kv = jnp.stack([k_rot, v_lin.astype(BF)]).reshape(2, chips, 1, rows, HEAD_DIM)
    kv = jnp.concatenate(in_order(kv, core_pair(kv)), axis=2).reshape(2, devices * rows, HEAD_DIM)
    reach = devices * rows // 4
    kv = jnp.concatenate([jnp.zeros((2, reach, HEAD_DIM), BF), kv], axis=1)
    k_seg = jnp.concatenate([jnp.full((reach,), -1, jnp.int32), segments]).reshape(1, -1)
    q_seg = lax.dynamic_index_in_dim(segments.reshape(chips, 2, rows), core, 1, keepdims=False).reshape(-1, 1)
    scale = 1.0 / math.sqrt(HEAD_DIM)
    row_block = pl.BlockSpec((rows, HEAD_DIM), lambda i: (i, 0))
    one_block = pl.BlockSpec((rows, 1), lambda i: (i, 0))

    def whole_block(value):
        return pl.BlockSpec(value.shape, lambda i: (0,) * value.ndim)

    tokens = chips * rows
    attended, log_total = pl.pallas_call(
        functools.partial(attend_kernel, scale, reach),
        grid=(chips,),
        out_shape=(jax.ShapeDtypeStruct((tokens, HEAD_DIM), BF), jax.ShapeDtypeStruct((tokens, 1), F32)),
        in_specs=[row_block, whole_block(kv[0]), whole_block(kv[1]), one_block, whole_block(k_seg)],
        out_specs=(row_block, one_block),
        compiler_params=pltpu.CompilerParams(vmem_limit_bytes=32 * 2**20),
        name="attend",
    )(q_rot, kv[0], kv[1], q_seg, k_seg)

    def to_blocks(part):
        return part.astype(BF).reshape(4, 4, rows, width)

    residual = layer_in + rs16(to_blocks(dot(attended, w_o, ((1,), (0,)))), 4)
    r2 = lax.rsqrt(jnp.mean(residual * residual, axis=1, keepdims=True) + EPS)
    normed_two = (residual * r2 * gain_two).astype(BF)
    n2_rows = ag16(normed_two, 5).reshape(tokens, width)
    cot_rows = lax.all_gather(cotangent, mine, axis=0, tiled=True)

    joined = [
        jnp.concatenate(in_order(part, core_pair(part)), axis=0)
        for part in (expert_gate, expert_up, expert_down)
    ]
    gate_full, up_full, down_full = joined
    gate_pre = dot(n2_rows, gate_full, ((1,), (0,)))
    up_pre = dot(n2_rows, up_full, ((1,), (0,)))
    sigma = jax.nn.sigmoid(gate_pre)
    hidden = (gate_pre * sigma * up_pre).astype(BF)
    produced = dot(hidden, down_full, ((1,), (0,))).astype(BF)
    mixed = lax.psum_scatter(
        (share * produced.astype(F32)).astype(BF), mine, scatter_dimension=0, tiled=True)
    output = residual + mixed.astype(F32)
    d_produced = (share * cot_rows.astype(F32)).astype(BF)
    d_hidden = dot(d_produced, down_full, ((1,), (1,)))
    d_gate_pre = (d_hidden * up_pre * sigma * (1.0 + gate_pre * (1.0 - sigma))).astype(BF)
    d_up_pre = (d_hidden * gate_pre * sigma).astype(BF)
    d_pair = dot(d_gate_pre, gate_full, ((1,), (1,))) + dot(d_up_pre, up_full, ((1,), (1,)))
    d_normed_two = rs16(to_blocks(d_pair), 6)

    def shared_grad(full):
        size = full.shape[0] // 2
        own = lax.dynamic_slice_in_dim(full, core * size, size, 0)
        other = lax.dynamic_slice_in_dim(full, (1 - core) * size, size, 0)
        return own + core_pair(other.astype(BF)).astype(F32)

    d_expert_gate = shared_grad(dot(n2_rows, d_gate_pre, ((0,), (0,))))
    d_expert_up = shared_grad(dot(n2_rows, d_up_pre, ((0,), (0,))))
    d_expert_down = shared_grad(dot(hidden, d_produced, ((0,), (0,))))

    def norm_back(d_out, values, r, gain):
        d_scaled = d_out * gain
        inner = jnp.mean(d_scaled * values, axis=1, keepdims=True)
        d_gain = jnp.sum(d_out * values * r, axis=0)
        return r * d_scaled - values * (r * r * r * inner), d_gain

    d_resid_norm, d_gain_two = norm_back(d_normed_two, residual, r2, gain_two)
    d_residual = cotangent.astype(F32) + d_resid_norm
    d_res_rows = ag16(d_residual.astype(BF), 7).reshape(tokens, width)
    d_attended = dot(d_res_rows, w_o, ((1,), (1,))).astype(BF)
    d_w_output = shared_grad(dot(attended, d_res_rows, ((0,), (0,))))
    padded = jax.ShapeDtypeStruct((reach + devices * rows, HEAD_DIM), F32)
    d_q, d_k, d_v = pl.pallas_call(
        functools.partial(attend_back_kernel, scale, reach),
        grid=(chips,),
        out_shape=(jax.ShapeDtypeStruct((tokens, HEAD_DIM), BF), padded, padded),
        in_specs=[row_block, whole_block(kv[0]), whole_block(kv[1]), one_block, whole_block(k_seg), one_block, row_block, row_block],
        out_specs=(row_block, whole_block(padded), whole_block(padded)),
        compiler_params=pltpu.CompilerParams(vmem_limit_bytes=48 * 2**20),
        name="attend_back",
    )(q_rot, kv[0], kv[1], q_seg, k_seg, log_total, attended, d_attended)
    d_kv = jnp.stack([d_k[reach:], d_v[reach:]]).reshape(2, chips, 2, rows, HEAD_DIM)
    d_kv_own = lax.dynamic_index_in_dim(d_kv, core, 2, keepdims=False)
    d_kv_other = lax.dynamic_index_in_dim(d_kv, 1 - core, 2, keepdims=False)
    d_kv = (d_kv_own + core_pair(d_kv_other.astype(BF)).astype(F32)).astype(BF).reshape(2, tokens, HEAD_DIM)
    d_q_un = turn_back(d_q.astype(F32))
    d_k_un = turn_back(d_kv[0].astype(F32))
    inner_q, inner_k = over_chips(
        jnp.sum(d_q_un * gq * q_lin, axis=1), jnp.sum(d_k_un * gk * k_lin, axis=1), 8)
    d_q_lin = rq * (d_q_un * gq) - q_lin * (rq * rq * rq * (inner_q / width))
    d_k_lin = rk * (d_k_un * gk) - k_lin * (rk * rk * rk * (inner_k / width))
    d_gain_q = jnp.sum(d_q_un * q_lin * rq, axis=0)
    d_gain_k = jnp.sum(d_k_un * k_lin * rk, axis=0)
    d_lin = jnp.concatenate([d_q_lin.astype(BF), d_k_lin.astype(BF), d_kv[1]], axis=1)
    d_normed_one = rs16(to_blocks(dot(d_lin, w_qkv, ((1,), (1,)))), 9)
    d_cols = dot(n1_rows, d_lin, ((0,), (0,))).reshape(chips, 2, 64, 3 * HEAD_DIM)
    d_cols_own = lax.dynamic_index_in_dim(d_cols, core, 1, keepdims=False)
    d_cols_other = lax.dynamic_index_in_dim(d_cols, 1 - core, 1, keepdims=False)
    d_cols = (d_cols_own + core_pair(d_cols_other.astype(BF)).astype(F32)).astype(BF)
    d_cols = lax.all_to_all(d_cols, mine, split_axis=0, concat_axis=0, tiled=True)
    d_cols = d_cols.reshape(chips, 64, 3, HEAD_DIM).transpose(2, 1, 0, 3).reshape(3, 64, width).astype(F32)
    r1 = lax.rsqrt(jnp.mean(layer_in * layer_in, axis=1, keepdims=True) + EPS)
    d_layer_in, d_gain_one = norm_back(d_normed_one, layer_in, r1, gain_one)
    d_inputs = d_residual + d_layer_in
    block = jnp.concatenate(
        [d_gain_one.reshape(chips, 1, 128), d_gain_two.reshape(chips, 1, 128), jnp.zeros((chips, 6, 128), F32)], axis=1)
    d_gains = jnp.sum(swap(block, 10)[:, :2, :], axis=0)

    def my_half(row):
        return lax.dynamic_slice_in_dim(row, core * 64, 64, 0)

    d_qk_gains = jnp.stack([d_gain_q, d_gain_k])
    d_qk_gains = d_qk_gains + core_pair(d_qk_gains)
    return (
        output,
        d_inputs,
        my_half(d_gains[0]),
        d_cols[0],
        d_cols[1],
        d_cols[2],
        d_w_output,
        my_half(d_qk_gains[0]),
        my_half(d_qk_gains[1]),
        my_half(d_gains[1]),
        d_expert_gate,
        d_expert_up,
        d_expert_down,
    )
def whole(mesh, step, rows):
    return jax.shard_map(
        step,
        mesh=mesh,
        in_specs=(
            P(rows, None),
            P(rows, None),
            P(),
            P(rows, None),
            P(rows, None),
            P(rows),
            P(rows),
            P(rows, None),
            P(rows, None),
            P(rows, None),
            P(rows, None),
            P(rows),
            P(rows),
            P(rows),
            P(rows, None),
            P(rows, None),
            P(rows, None),
        ),
        out_specs=(
            P(rows, None),
            P(rows, None),
            P(rows),
            P(rows, None),
            P(rows, None),
            P(rows, None),
            P(rows, None),
            P(rows),
            P(rows),
            P(rows),
            P(rows, None),
            P(rows, None),
            P(rows, None),
        ),
        check_vma=False,
    )


def solution(mesh):
    groups, blk_size = mesh.shape["ulysses"], mesh.shape["blk"]

    def step(*args):
        if groups != 4 or blk_size != 8 or args[7].shape[1] // HEAD_DIM != groups * blk_size // 2:
            return whole(mesh, local, ("ulysses", "blk"))(*args)
        chips = Mesh(mesh.devices.reshape(groups, blk_size // 2, 2), ("ulysses", "z", "core"))
        return whole(chips, local_chip, ("ulysses", "z", "core"))(*args)

    return step
```

```python
import functools
import math

import jax
import jax.numpy as jnp
from jax import lax
from jax.experimental import pallas as pl
from jax.experimental.pallas import tpu as pltpu
from jax.sharding import Mesh
from jax.sharding import PartitionSpec as P

HEAD_DIM = 128


EPS = 1e-05
ROPE_BASE = 10000.0
NEG = -1e30


def as_sent(value):

    def short(part):
        return part.astype(jnp.bfloat16) if part.dtype == jnp.float32 else part

    return jax.tree.map(short, value)


def passed_along(block, axis, distance):
    devices = range(lax.axis_size(axis))
    route = [((i - distance) % len(devices), i) for i in devices]
    return lax.ppermute(block, axis, route)


def prefix(value, axis, join, neutral):
    count, mine = (lax.axis_size(axis), lax.axis_index(axis))
    pieces = lax.all_gather(value, axis)
    subtotal = jnp.full_like(value, 0) + jnp.asarray(neutral, value.dtype)

    def hop(position, subtotal):
        longer = join(subtotal, pieces[position])
        return jnp.where(position < mine, longer, subtotal)

    return lax.fori_loop(0, count - 1, hop, subtotal)


def partner_2(block, axis, bit):
    count = lax.axis_size(axis)
    route = []
    for low in range(count):
        high = low | 1 << bit
        if high != low and high < count:
            route += [(low, high), (high, low)]
    return lax.ppermute(block, axis, route)


def norm_rows(values, gain_vec):
    return values * lax.rsqrt(jnp.mean(values * values, axis=-1, keepdims=True) + EPS) * gain_vec


def rotate(values, positions):
    half_dim = HEAD_DIM // 2
    heads_here = values.shape[1] // HEAD_DIM
    inv_freq = jnp.exp(
        jnp.arange(half_dim, dtype=jnp.float32) * (-2.0 * math.log(ROPE_BASE) / HEAD_DIM)
    )
    angles = positions.astype(jnp.float32)[:, None] * inv_freq[None, :]
    cosine = jnp.cos(angles)[:, None, :]
    sin_t = jnp.sin(angles)[:, None, :]
    shaped = values.reshape(values.shape[0], heads_here, HEAD_DIM)
    lower_half = shaped[..., :half_dim]
    upper_half = shaped[..., half_dim:]
    turned = jnp.concatenate(
        [lower_half * cosine - upper_half * sin_t, upper_half * cosine + lower_half * sin_t],
        axis=-1,
    )
    return turned.reshape(values.shape)


def attn_inputs(q_lin, k_lin, gain_q, gain_k, positions):
    return (
        rotate(norm_rows(q_lin, gain_q), positions),
        rotate(norm_rows(k_lin, gain_k), positions),
    )


def banded(shaped, fill_value):
    earlier = jnp.concatenate([jnp.full_like(shaped[:1], fill_value), shaped[:-1]], axis=0)
    return jnp.concatenate([earlier, shaped], axis=1)


def unbanded(band, local_rows):
    earlier = band[:, :local_rows]
    own_part = band[:, local_rows:]
    moved_up = jnp.concatenate([earlier[1:], jnp.zeros_like(earlier[:1])], axis=0)
    return own_part + moved_up


def add_counts(earlier, later):
    return earlier + later


def expert_move(buffer):
    return lax.all_to_all(buffer, ("ulysses", "blk"), split_axis=0, concat_axis=0, tiled=True)


def to_head_layout(values):
    return jax.tree.map(
        lambda part, own: part.astype(own.dtype),
        lax.all_to_all(as_sent(values), "ulysses", split_axis=1, concat_axis=0, tiled=True),
        values,
    )


def to_token_layout(values):
    return jax.tree.map(
        lambda part, own: part.astype(own.dtype),
        lax.all_to_all(as_sent(values), "ulysses", split_axis=0, concat_axis=1, tiled=True),
        values,
    )


def local(
    inputs,
    cotangent,
    segments,
    expert_ids,
    gate_weights,
    fill_order,
    norm1_gain,
    w_query,
    w_key,
    w_value,
    w_output,
    query_gain,
    key_gain,
    norm2_gain,
    expert_gate,
    expert_up,
    expert_down,
):
    blk_size = lax.axis_size("blk")
    groups = lax.axis_size("ulysses")
    devices = blk_size * groups
    local_rows = inputs.shape[0]
    model_width = inputs.shape[1]
    blk_index = lax.axis_index("blk")
    group_index = lax.axis_index("ulysses")
    device_index = group_index * blk_size + blk_index
    positions = device_index * local_rows + jnp.arange(local_rows, dtype=jnp.int32)
    heads_dev = model_width // groups // HEAD_DIM
    score_scale = 1.0 / math.sqrt(HEAD_DIM)
    layer_in = inputs.astype(jnp.float32)
    dense = (w_query, w_key, w_value, w_output, norm1_gain, query_gain, key_gain, norm2_gain)
    gathered = (
        lax.all_gather(dense[0], ("ulysses", "blk"), axis=0, tiled=True),
        lax.all_gather(dense[1], ("ulysses", "blk"), axis=0, tiled=True),
        lax.all_gather(dense[2], ("ulysses", "blk"), axis=0, tiled=True),
        lax.all_gather(dense[3], ("ulysses", "blk"), axis=0, tiled=True),
        lax.all_gather(dense[4], ("ulysses", "blk"), axis=0, tiled=True),
        lax.all_gather(dense[5], ("ulysses", "blk"), axis=0, tiled=True),
        lax.all_gather(dense[6], ("ulysses", "blk"), axis=0, tiled=True),
        lax.all_gather(dense[7], ("ulysses", "blk"), axis=0, tiled=True),
    )
    w_q, w_k, w_v, w_o = (gathered[0], gathered[1], gathered[2], gathered[3])
    gain_one = gathered[4].astype(jnp.float32)
    gain_q = gathered[5].astype(jnp.float32)
    gain_k = gathered[6].astype(jnp.float32)
    gain_two = gathered[7].astype(jnp.float32)
    normed_one = norm_rows(layer_in, gain_one).astype(jnp.bfloat16)
    q_lin = jnp.dot(normed_one, w_q, preferred_element_type=jnp.float32)
    k_lin = jnp.dot(normed_one, w_k, preferred_element_type=jnp.float32)
    v_lin = jnp.dot(normed_one, w_v, preferred_element_type=jnp.float32)
    (q_rot, k_rot), pre_back = jax.vjp(
        lambda q_in, k_in, gq_in, gk_in: attn_inputs(q_in, k_in, gq_in, gk_in, positions),
        q_lin,
        k_lin,
        gain_q,
        gain_k,
    )
    q_heads, k_heads, v_heads = to_head_layout(
        (q_rot.astype(jnp.bfloat16), k_rot.astype(jnp.bfloat16), v_lin.astype(jnp.bfloat16))
    )
    group_ids = jnp.arange(groups, dtype=jnp.int32)[:, None]
    row_ids = jnp.arange(local_rows, dtype=jnp.int32)[None, :]
    q_pos = (group_ids * blk_size + blk_index) * local_rows + row_ids
    q_seg = segments[q_pos]
    four_shape = (groups, local_rows, heads_dev, HEAD_DIM)
    q_four = q_heads.reshape(four_shape)

    def score_block(k_now, source):
        k_pos = (group_ids * blk_size + source) * local_rows + row_ids
        k_seg = banded(segments[k_pos], -1)
        k_pos = banded(k_pos, 0)
        k_band = banded(k_now.reshape(four_shape), 0)
        raw_scores = (
            jnp.einsum("gqhd,gkhd->gqhk", q_four, k_band, preferred_element_type=jnp.float32)
            * score_scale
        )
        allowed = (k_seg[:, None, :] == q_seg[:, :, None]) & (
            k_pos[:, None, :] <= q_pos[:, :, None]
        )
        return (raw_scores, allowed[:, :, None, :], k_band)

    def forward_step(flash_state, kv_stack, step_id):
        run_max, run_sum, run_out = flash_state
        source = jnp.mod(blk_index - step_id, blk_size)
        raw_scores, allowed, k_band = score_block(kv_stack[0], source)
        raw_scores = jnp.where(allowed, raw_scores, NEG)
        new_max = jnp.maximum(run_max, jnp.max(raw_scores, axis=-1))
        shrink = jnp.exp(run_max - new_max)
        weights = jnp.where(allowed, jnp.exp(raw_scores - new_max[..., None]), 0.0)
        run_sum = run_sum * shrink + jnp.sum(weights, axis=-1)
        v_band = banded(kv_stack[1].reshape(four_shape), 0)
        run_out = run_out * shrink[..., None] + jnp.einsum(
            "gqhk,gkhd->gqhd",
            weights.astype(jnp.bfloat16),
            v_band,
            preferred_element_type=jnp.float32,
        )
        return (new_max, run_sum, run_out)

    start_state = (
        jnp.full((groups, local_rows, heads_dev), NEG, jnp.float32),
        jnp.zeros((groups, local_rows, heads_dev), jnp.float32),
        jnp.zeros(four_shape, jnp.float32),
    )
    kv_home = jnp.stack([k_heads, v_heads])
    first_state = forward_step(start_state, kv_home, 0)

    def forward_turn(step_id, loop_state):
        flash_state, kv_stack = loop_state
        moved = passed_along(kv_stack, "blk", 1)
        return (forward_step(flash_state, moved, step_id), moved)

    final_state, unused_kv = lax.fori_loop(1, blk_size, forward_turn, (first_state, kv_home))
    run_max, run_sum, run_out = final_state
    o_four = (run_out / run_sum[..., None]).astype(jnp.bfloat16)
    log_total = run_max + jnp.log(run_sum)
    o_heads = o_four.reshape(groups * local_rows, heads_dev * HEAD_DIM)
    attended = to_token_layout(o_heads)
    residual = layer_in + jnp.dot(attended, w_o, preferred_element_type=jnp.float32)
    normed_two_f, norm_two_back = jax.vjp(norm_rows, residual, gain_two)
    normed_two = normed_two_f.astype(jnp.bfloat16)
    experts_n = devices // 2
    topk = expert_ids.shape[1]
    per_source = 2 * local_rows * topk // experts_n
    half_slots = per_source // 2
    capacity = 9 * local_rows * devices * topk // (8 * experts_n)
    slots_all = experts_n * per_source
    tokens_local = jnp.arange(local_rows, dtype=jnp.int32)
    chosen = jnp.sum(
        (expert_ids[:, :, None] == jnp.arange(experts_n, dtype=jnp.int32)[None, None, :]).astype(
            jnp.int32
        ),
        axis=1,
    )
    by_fill = jnp.zeros((local_rows,), jnp.int32).at[fill_order].set(tokens_local)
    sorted_rows = chosen[by_fill]
    before = jnp.cumsum(sorted_rows, axis=0) - sorted_rows
    rank_all = before[fill_order]
    pair_rank = jnp.take_along_axis(rank_all, expert_ids, axis=1)
    counts = jnp.sum(chosen, axis=0)
    offsets = prefix(counts, ("ulysses", "blk"), add_counts, jnp.zeros_like(counts))
    kept_pair = offsets[expert_ids] + pair_rank < capacity
    pair_slot = expert_ids * per_source + pair_rank
    pair_index = tokens_local[:, None] * topk + jnp.arange(topk, dtype=jnp.int32)[None, :]
    slot_pair = (
        jnp.zeros((slots_all,), jnp.int32).at[pair_slot.reshape(-1)].set(pair_index.reshape(-1))
    )
    slot_live = (
        jnp.zeros((slots_all,), jnp.bool_).at[pair_slot.reshape(-1)].set(kept_pair.reshape(-1))
    )
    slot_token = slot_pair // topk
    send_rows = jnp.where(slot_live[:, None], normed_two[slot_token], jnp.zeros((), jnp.bfloat16))
    received = expert_move(send_rows.reshape(devices, half_slots, model_width)).reshape(
        devices * half_slots, model_width
    )
    parity = jnp.mod(blk_index, 2)
    partner = partner_2((expert_gate, expert_up, expert_down), "blk", 0)

    def joined(own_half, other_half):
        lower_part = jnp.where(parity == 0, own_half, other_half)
        upper_part = jnp.where(parity == 0, other_half, own_half)
        return jnp.concatenate([lower_part, upper_part], axis=0)

    gate_full = joined(expert_gate, partner[0])
    up_full = joined(expert_up, partner[1])
    down_full = joined(expert_down, partner[2])
    gate_pre = jnp.dot(received, gate_full, preferred_element_type=jnp.float32)
    up_pre = jnp.dot(received, up_full, preferred_element_type=jnp.float32)
    hidden = (jax.nn.silu(gate_pre) * up_pre).astype(jnp.bfloat16)
    produced = jnp.dot(hidden, down_full, preferred_element_type=jnp.float32).astype(jnp.bfloat16)
    returned = expert_move(produced.reshape(devices, half_slots, model_width)).reshape(
        slots_all, model_width
    )
    pair_share = jnp.where(kept_pair, gate_weights, 0.0)
    mixed = jnp.einsum("tk,tkd->td", pair_share, returned[pair_slot].astype(jnp.float32))
    output = residual + mixed
    grad_out = cotangent.astype(jnp.float32)
    slot_share = jnp.where(slot_live, gate_weights.reshape(-1)[slot_pair], 0.0)
    grad_send = (slot_share[:, None] * grad_out[slot_token]).astype(jnp.bfloat16)
    grad_rows = expert_move(grad_send.reshape(devices, half_slots, model_width)).reshape(
        devices * half_slots, model_width
    )
    d_down_full = jnp.einsum("rf,rd->fd", hidden, grad_rows, preferred_element_type=jnp.float32)
    d_hidden = jnp.einsum("rd,fd->rf", grad_rows, down_full, preferred_element_type=jnp.float32)
    sigma = jax.nn.sigmoid(gate_pre)
    d_gate_pre = (d_hidden * up_pre * sigma * (1.0 + gate_pre * (1.0 - sigma))).astype(jnp.bfloat16)
    d_up_pre = (d_hidden * gate_pre * sigma).astype(jnp.bfloat16)
    d_gate_full = jnp.einsum("rd,rf->df", received, d_gate_pre, preferred_element_type=jnp.float32)
    d_up_full = jnp.einsum("rd,rf->df", received, d_up_pre, preferred_element_type=jnp.float32)
    d_pair_rows = (
        jnp.einsum("rf,df->rd", d_gate_pre, gate_full, preferred_element_type=jnp.float32)
        + jnp.einsum("rf,df->rd", d_up_pre, up_full, preferred_element_type=jnp.float32)
    ).astype(jnp.bfloat16)
    back_rows = expert_move(d_pair_rows.reshape(devices, half_slots, model_width)).reshape(
        slots_all, model_width
    )
    d_normed_two = jnp.sum(
        jnp.where(kept_pair[:, :, None], back_rows[pair_slot].astype(jnp.float32), 0.0), axis=1
    )
    half_rows = expert_gate.shape[0]
    half_hidden = expert_down.shape[0]

    def halves(full_grad, size):
        own_half = lax.dynamic_slice_in_dim(full_grad, parity * size, size, 0)
        other_half = lax.dynamic_slice_in_dim(full_grad, (1 - parity) * size, size, 0)
        return (own_half, other_half)

    gate_own, gate_other = halves(d_gate_full, half_rows)
    up_own, up_other = halves(d_up_full, half_rows)
    down_own, down_other = halves(d_down_full, half_hidden)
    partner_grads = (
        partner_2(gate_other.astype(jnp.bfloat16), "blk", 0).astype(gate_other.dtype),
        partner_2(up_other.astype(jnp.bfloat16), "blk", 0).astype(up_other.dtype),
        partner_2(down_other.astype(jnp.bfloat16), "blk", 0).astype(down_other.dtype),
    )
    d_expert_gate = gate_own + partner_grads[0]
    d_expert_up = up_own + partner_grads[1]
    d_expert_down = down_own + partner_grads[2]
    d_resid_norm, d_gain_two = norm_two_back(d_normed_two)
    d_residual = grad_out + d_resid_norm
    d_res_low = d_residual.astype(jnp.bfloat16)
    d_attended = jnp.einsum("te,de->td", d_res_low, w_o, preferred_element_type=jnp.float32).astype(
        jnp.bfloat16
    )
    d_o_heads = to_head_layout(d_attended)
    d_o_four = d_o_heads.reshape(four_shape)
    row_delta = jnp.sum(d_o_four.astype(jnp.float32) * o_four.astype(jnp.float32), axis=-1)

    def back_turn(step_id, loop_state):
        moving, dq_acc = loop_state
        source = jnp.mod(blk_index - step_id, blk_size)
        k_now = moving[0].astype(jnp.bfloat16)
        v_now = moving[1].astype(jnp.bfloat16)
        raw_scores, allowed, k_band = score_block(k_now, source)
        prob_rows = jnp.where(allowed, jnp.exp(raw_scores - log_total[..., None]), 0.0)
        v_band = banded(v_now.reshape(four_shape), 0)
        d_probs = jnp.einsum(
            "gqhd,gkhd->gqhk", d_o_four, v_band, preferred_element_type=jnp.float32
        )
        d_scores = (prob_rows * (d_probs - row_delta[..., None])).astype(jnp.bfloat16)
        dv_band = jnp.einsum(
            "gqhk,gqhd->gkhd",
            prob_rows.astype(jnp.bfloat16),
            d_o_four,
            preferred_element_type=jnp.float32,
        )
        dk_band = (
            jnp.einsum("gqhk,gqhd->gkhd", d_scores, q_four, preferred_element_type=jnp.float32)
            * score_scale
        )
        dq_acc = (
            dq_acc
            + jnp.einsum("gqhk,gkhd->gqhd", d_scores, k_band, preferred_element_type=jnp.float32)
            * score_scale
        )
        flat_shape = moving[2].shape
        dk_new = moving[2] + unbanded(dk_band, local_rows).reshape(flat_shape)
        dv_new = moving[3] + unbanded(dv_band, local_rows).reshape(flat_shape)
        moving = passed_along(
            jnp.stack([moving[0], moving[1], dk_new, dv_new]).astype(jnp.bfloat16), "blk", 1
        ).astype(jnp.float32)
        return (moving, dq_acc)

    zero_rows = jnp.zeros(k_heads.shape, jnp.float32)
    start_moving = jnp.stack(
        [k_heads.astype(jnp.float32), v_heads.astype(jnp.float32), zero_rows, zero_rows]
    )
    moving, dq_acc = lax.fori_loop(
        0, blk_size, back_turn, (start_moving, jnp.zeros(four_shape, jnp.float32))
    )
    d_q_send = dq_acc.astype(jnp.bfloat16).reshape(k_heads.shape)
    d_k_send = moving[2].astype(jnp.bfloat16)
    d_v_send = moving[3].astype(jnp.bfloat16)
    d_q_rot, d_k_rot, d_v_lin = to_token_layout((d_q_send, d_k_send, d_v_send))
    d_q_lin, d_k_lin, d_gain_q, d_gain_k = pre_back(
        (d_q_rot.astype(jnp.float32), d_k_rot.astype(jnp.float32))
    )
    d_q_low = d_q_lin.astype(jnp.bfloat16)
    d_k_low = d_k_lin.astype(jnp.bfloat16)
    d_normed_one = jnp.einsum("te,de->td", d_q_low, w_q, preferred_element_type=jnp.float32)
    d_normed_one = d_normed_one + jnp.einsum(
        "te,de->td", d_k_low, w_k, preferred_element_type=jnp.float32
    )
    d_normed_one = d_normed_one + jnp.einsum(
        "te,de->td", d_v_lin, w_v, preferred_element_type=jnp.float32
    )
    unused_norm, norm_one_back = jax.vjp(norm_rows, layer_in, gain_one)
    d_layer_in, d_gain_one = norm_one_back(d_normed_one)
    d_inputs = d_residual + d_layer_in
    d_qk_heads = to_head_layout((d_q_low, d_k_low))
    rows_all = (
        lax.all_gather(normed_one, "ulysses", axis=0, tiled=True),
        lax.all_gather(d_res_low, "ulysses", axis=0, tiled=True),
    )
    head_cols = model_width // groups
    piece_rows = model_width // devices

    def by_owner(part):
        rest = part.shape[1:]
        shaped = part.reshape((groups, blk_size, piece_rows) + rest)
        return jnp.swapaxes(shaped, 0, 1).reshape((model_width,) + rest)

    part_q = jnp.einsum("td,te->de", rows_all[0], d_qk_heads[0], preferred_element_type=jnp.float32)
    part_k = jnp.einsum("td,te->de", rows_all[0], d_qk_heads[1], preferred_element_type=jnp.float32)
    part_v = jnp.einsum("td,te->de", rows_all[0], d_v_send, preferred_element_type=jnp.float32)
    part_o = jnp.einsum("te,td->ed", o_heads, rows_all[1], preferred_element_type=jnp.float32)
    blk_sums = (
        lax.psum_scatter(
            by_owner(part_q).astype(jnp.bfloat16), "blk", scatter_dimension=0, tiled=True
        ).astype(jnp.float32),
        lax.psum_scatter(
            by_owner(part_k).astype(jnp.bfloat16), "blk", scatter_dimension=0, tiled=True
        ).astype(jnp.float32),
        lax.psum_scatter(
            by_owner(part_v).astype(jnp.bfloat16), "blk", scatter_dimension=0, tiled=True
        ).astype(jnp.float32),
        lax.psum_scatter(
            part_o.astype(jnp.bfloat16), "blk", scatter_dimension=0, tiled=True
        ).astype(jnp.float32),
        lax.psum_scatter(
            by_owner(d_gain_one).astype(jnp.bfloat16), "blk", scatter_dimension=0, tiled=True
        ).astype(jnp.float32),
        lax.psum_scatter(
            by_owner(d_gain_q).astype(jnp.bfloat16), "blk", scatter_dimension=0, tiled=True
        ).astype(jnp.float32),
        lax.psum_scatter(
            by_owner(d_gain_k).astype(jnp.bfloat16), "blk", scatter_dimension=0, tiled=True
        ).astype(jnp.float32),
        lax.psum_scatter(
            by_owner(d_gain_two).astype(jnp.bfloat16), "blk", scatter_dimension=0, tiled=True
        ).astype(jnp.float32),
    )

    def widened(part):
        return lax.dynamic_update_slice_in_dim(
            jnp.zeros((part.shape[0], model_width), jnp.float32), part, group_index * head_cols, 1
        )

    col_sums = (
        lax.psum_scatter(
            widened(blk_sums[0]).astype(jnp.bfloat16), "ulysses", scatter_dimension=0, tiled=True
        ).astype(jnp.float32),
        lax.psum_scatter(
            widened(blk_sums[1]).astype(jnp.bfloat16), "ulysses", scatter_dimension=0, tiled=True
        ).astype(jnp.float32),
        lax.psum_scatter(
            widened(blk_sums[2]).astype(jnp.bfloat16), "ulysses", scatter_dimension=0, tiled=True
        ).astype(jnp.float32),
        lax.psum_scatter(
            blk_sums[4].astype(jnp.bfloat16), "ulysses", scatter_dimension=0, tiled=True
        ).astype(jnp.float32),
        lax.psum_scatter(
            blk_sums[5].astype(jnp.bfloat16), "ulysses", scatter_dimension=0, tiled=True
        ).astype(jnp.float32),
        lax.psum_scatter(
            blk_sums[6].astype(jnp.bfloat16), "ulysses", scatter_dimension=0, tiled=True
        ).astype(jnp.float32),
        lax.psum_scatter(
            blk_sums[7].astype(jnp.bfloat16), "ulysses", scatter_dimension=0, tiled=True
        ).astype(jnp.float32),
    )
    result_grads = (
        col_sums[0],
        col_sums[1],
        col_sums[2],
        blk_sums[3],
        col_sums[3],
        col_sums[4],
        col_sums[5],
        col_sums[6],
    )
    return (
        output,
        d_inputs,
        result_grads[4],
        result_grads[0],
        result_grads[1],
        result_grads[2],
        result_grads[3],
        result_grads[5],
        result_grads[6],
        result_grads[7],
        d_expert_gate,
        d_expert_up,
        d_expert_down,
    )


MESH = pl.DeviceIdType.MESH
P1 = 96

def place():
    u = lax.axis_index("ulysses"); z = lax.axis_index("z"); c = lax.axis_index("core")
    return u, z, c

def ag_kernel(cut, x_ref, o_ref, local_sem, s_sem, zr, xr, yr, d1r, d2r, bs, br, bzr):
    u, z, c = place()
    Z = 4
    R = x_ref.shape[0]
    ux, uy = u ^ 1, u ^ 2
    xn, yn, up, dn = (ux, z, c), (uy, z, c), (u, z + 1, c), (u, z - 1, c)
    has_up, has_dn = z < Z - 1, z > 0
    bar = pltpu.get_barrier_semaphore()
    for n in (xn, yn):
        pl.semaphore_signal(bar, inc=1, device_id=n, device_id_type=MESH)
    @pl.when(has_up)
    def _():
        pl.semaphore_signal(bar, inc=1, device_id=up, device_id_type=MESH)
    @pl.when(has_dn)
    def _():
        pl.semaphore_signal(bar, inc=1, device_id=dn, device_id_type=MESH)
    pl.semaphore_wait(bar, 2 + has_up.astype(jnp.int32) + has_dn.astype(jnp.int32))
    sends = []
    def copy(src, dst, ss, rs, dev):
        return pltpu.make_async_remote_copy(src_ref=src, dst_ref=dst, send_sem=ss, recv_sem=rs, device_id=dev, device_id_type=MESH)
    def go(cond, make):
        idx = len(sends)
        def mk():
            return make(s_sem.at[idx])
        sends.append((cond, mk))
        if cond is None:
            mk().start()
        else:
            pl.when(cond)(lambda: mk().start())
    def both(a, b):
        if a is None: return b
        if b is None: return a
        return jnp.logical_and(a, b)
    def wait(cond, ref, sem):
        def w():
            pltpu.make_async_copy(ref, ref, sem).wait()
        if cond is None: w()
        else: pl.when(cond)(w)
    own = pltpu.make_async_copy(x_ref, o_ref.at[u, z], local_sem)
    own.start()
    A = slice(0, cut)
    h = cut // 2
    def oa(uu, zz, lo=0, n=cut):
        return o_ref.at[uu, zz, pl.ds(lo, n), :]
    def spread(s, zz, cond):
        src = (lambda: x_ref.at[pl.ds(0, cut), :]) if s == 0 else (lambda: oa(u, zz))
        go(cond, lambda sm: copy(src(), oa(u, zz), sm, xr.at[zz], xn))
        go(cond, lambda sm: copy(src(), oa(u, zz), sm, yr.at[zz], yn))
    def cross(zz, cond):
        wait(cond, oa(ux, zz), xr.at[zz])
        go(cond, lambda sm: copy(oa(ux, zz, 0, h), oa(ux, zz, 0, h), sm, d1r.at[zz], yn))
        wait(cond, oa(uy, zz), yr.at[zz])
        go(cond, lambda sm: copy(oa(uy, zz, h, h), oa(uy, zz, h, h), sm, d2r.at[zz], xn))
    rb = R - cut
    hb = rb // 2
    def ob(uu, zz, lo=0, n=None):
        return o_ref.at[uu, zz, pl.ds(cut + lo, rb if n is None else n), :]
    go(has_up, lambda sm: copy(x_ref.at[pl.ds(0, cut), :], oa(u, z), sm, zr.at[z], up))
    go(has_dn, lambda sm: copy(x_ref.at[pl.ds(0, cut), :], oa(u, z), sm, zr.at[z], dn))
    if rb:
        go(None, lambda sm: copy(x_ref.at[pl.ds(cut, rb), :], ob(u, z), sm, br.at[0], xn))
        go(None, lambda sm: copy(x_ref.at[pl.ds(cut, rb), :], ob(u, z), sm, br.at[1], yn))
    spread(0, z, None)
    if rb:
        wait(None, ob(ux, z), br.at[0])
        go(None, lambda sm: copy(ob(ux, z, 0, hb), ob(ux, z, 0, hb), sm, br.at[2], yn))
        wait(None, ob(uy, z), br.at[1])
        go(None, lambda sm: copy(ob(uy, z, hb, hb), ob(uy, z, hb, hb), sm, br.at[3], xn))
    own.wait()
    def quad(zz):
        return o_ref.at[:, zz, pl.ds(cut, rb), :]
    def zs(s):
        zl, zh = z - s, z + s
        cl, ch = zl >= 0, zh < Z
        zlc, zhc = jnp.maximum(zl, 0), jnp.minimum(zh, Z - 1)
        return (zlc, cl, has_up, up), (zhc, ch, has_dn, dn)
    prev = [(z, None)]
    for s in range(1, Z):
        cur = []
        for (zz, cond, fwd, dev) in zs(s):
            wait(cond, oa(u, zz), zr.at[zz])
            go(both(cond, fwd), lambda sm, zz=zz, dev=dev: copy(oa(u, zz), oa(u, zz), sm, zr.at[zz], dev))
            spread(s, zz, cond)
            cur.append((zz, cond))
        if rb and s == 1:
            wait(None, ob(u ^ 3, z, 0, hb), br.at[2])
            wait(None, ob(u ^ 3, z, hb, hb), br.at[3])
            go(has_up, lambda sm: copy(quad(z), quad(z), sm, bzr.at[z], up))
            go(has_dn, lambda sm: copy(quad(z), quad(z), sm, bzr.at[z], dn))
        elif rb:
            for (zz, cond, fwd, dev) in zs(s - 1):
                wait(cond, quad(zz), bzr.at[zz])
                go(both(cond, fwd), lambda sm, zz=zz, dev=dev: copy(quad(zz), quad(zz), sm, bzr.at[zz], dev))
        for zz, cond in prev:
            cross(zz, cond)
        prev = cur
    if rb:
        for (zz, cond, fwd, dev) in zs(Z - 1):
            wait(cond, quad(zz), bzr.at[zz])
    for zz, cond in prev:
        cross(zz, cond)
    for zz in range(Z):
        wait(None, oa(u ^ 3, zz, 0, h), d1r.at[zz])
        wait(None, oa(u ^ 3, zz, h, h), d2r.at[zz])
    for cond, mk in sends:
        if cond is None: mk().wait_send()
        else: pl.when(cond)(lambda mk=mk: mk().wait_send())

def ag16(x, cid, cut=P1, space=pl.ANY):
    R, D = x.shape
    DMA = pltpu.SemaphoreType.DMA
    return pl.pallas_call(
        functools.partial(ag_kernel, cut),
        out_shape=jax.ShapeDtypeStruct((4, 4, R, D), x.dtype),
        in_specs=[pl.BlockSpec(memory_space=space)],
        out_specs=pl.BlockSpec(memory_space=space),
        scratch_shapes=[DMA, DMA((64,)), DMA((4,)), DMA((4,)), DMA((4,)), DMA((4,)), DMA((4,)), DMA((4,)), DMA((4,)), DMA((4,))],
        compiler_params=pltpu.CompilerParams(collective_id=cid, has_side_effects=True, vmem_limit_bytes=48 * 2**20),
        name="gather_rows",
    )(x)
F32 = jnp.float32
BF = jnp.bfloat16


class Net:
    def __init__(self, sems):
        self.sems, self.sends = sems, []
        self.u, self.z, self.c = place()
        u, z, c = self.u, self.z, self.c
        self.ux, self.uy, self.ud = u ^ 1, u ^ 2, u ^ 3
        self.xn, self.yn, self.up, self.dn = (u ^ 1, z, c), (u ^ 2, z, c), (u, z + 1, c), (u, z - 1, c)
        self.has_up, self.has_dn = z < 3, z > 0
        self.at = [z == i for i in range(4)]

    def barrier(self, more=()):
        bar = pltpu.get_barrier_semaphore()
        for n in (self.xn, self.yn) + tuple(more):
            pl.semaphore_signal(bar, inc=1, device_id=n, device_id_type=MESH)
        for cond, n in ((self.has_up, self.up), (self.has_dn, self.dn)):
            pl.when(cond)(lambda n=n: pl.semaphore_signal(bar, inc=1, device_id=n, device_id_type=MESH))
        pl.semaphore_wait(bar, 2 + len(more) + self.has_up.astype(jnp.int32) + self.has_dn.astype(jnp.int32))

    def go(self, cond, src, dst, rsem, dev):
        idx = len(self.sends)

        def mk():
            return pltpu.make_async_remote_copy(
                src_ref=src(), dst_ref=dst(), send_sem=self.sems.at[idx], recv_sem=rsem(),
                device_id=dev, device_id_type=MESH)

        self.sends.append((cond, mk))
        if cond is None:
            mk().start()
        else:
            pl.when(cond)(lambda: mk().start())

    def wait(self, cond, ref, sem):
        def w():
            pltpu.make_async_copy(ref(), ref(), sem).wait()

        if cond is None:
            w()
        else:
            pl.when(cond)(w)

    def finish(self):
        for cond, mk in self.sends:
            if cond is None:
                mk().wait_send()
            else:
                pl.when(cond)(lambda mk=mk: mk().wait_send())


def strips(rows, body, step=16):
    def it(i, _):
        body(pl.ds(pl.multiple_of(i * step, step), step))
        return 0

    lax.fori_loop(0, rows // step, it, 0)


def wide(v):
    return v.astype(F32)


class Scatter:
    def __init__(self, net, cut, P, bufs):
        self.net, self.cut, self.P = net, cut, P
        (self.mid1, self.mid2, self.fx, self.fy, self.be, self.ab, self.bbe, self.bab, self.bm,
         self.m1s, self.m2s, self.fxs, self.fys, self.bes, self.abs_, self.bbes, self.babs, self.bms) = bufs
        self.R = P.shape[2]
        self.h = cut // 2
        self.rb = self.R - cut
        self.hb = self.rb // 2

    def first(self, zd):
        net, P, h, cut, rb = self.net, self.P, self.h, self.cut, self.rb
        net.go(None, lambda: P.at[net.ud, zd, pl.ds(0, h), :], lambda: self.mid1.at[zd], lambda: self.m1s.at[zd], net.xn)
        net.go(None, lambda: P.at[net.ud, zd, pl.ds(h, h), :], lambda: self.mid2.at[zd], lambda: self.m2s.at[zd], net.yn)
        if rb and zd > 0:
            net.go(net.at[0], lambda: P.at[:, zd, pl.ds(cut, rb), :], lambda: self.bbe.at[zd], lambda: self.bbes.at[zd], net.up)
        if rb and zd < 3:
            net.go(net.at[3], lambda: P.at[:, zd, pl.ds(cut, rb), :], lambda: self.bab.at[zd], lambda: self.babs.at[zd], net.dn)
        net.go(None, lambda: P.at[net.ux, zd, pl.ds(0, h), :], lambda: self.fx.at[zd, pl.ds(0, h), :], lambda: self.fxs.at[zd, 0], net.xn)
        net.go(None, lambda: P.at[net.uy, zd, pl.ds(h, h), :], lambda: self.fy.at[zd, pl.ds(h, h), :], lambda: self.fys.at[zd, 1], net.yn)

    def mids(self, zd):
        net, P, h, mid1, mid2 = self.net, self.P, self.h, self.mid1, self.mid2

        def add1(sl):
            mid1[zd, sl, :] = (wide(mid1[zd, sl, :]) + wide(P[net.uy, zd, sl, :])).astype(BF)

        def add2(sl):
            mid2[zd, sl, :] = (wide(mid2[zd, sl, :]) + wide(P[net.ux, zd, pl.ds(h + sl.start, 16), :])).astype(BF)

        net.wait(None, lambda: mid1.at[zd], self.m1s.at[zd])
        strips(h, add1)
        net.go(None, lambda: mid1.at[zd], lambda: self.fy.at[zd, pl.ds(0, h), :], lambda: self.fys.at[zd, 0], net.yn)
        net.wait(None, lambda: mid2.at[zd], self.m2s.at[zd])
        strips(h, add2)
        net.go(None, lambda: mid2.at[zd], lambda: self.fx.at[zd, pl.ds(h, h), :], lambda: self.fxs.at[zd, 1], net.xn)

    def route(self, zd, zz):
        if zz < zd:
            return True, self.net.up
        return False, self.net.dn

    def bhop(self, zd, zz):
        net, P, cut, rb = self.net, self.P, self.cut, self.rb
        if not rb:
            return
        upward, dev = self.route(zd, zz)
        buf, sems = (self.bbe, self.bbes) if upward else (self.bab, self.babs)
        here = net.at[zz]
        net.wait(here, lambda: buf.at[zd], sems.at[zd])

        def add():
            for q in range(4):
                def one(sl, q=q):
                    buf[zd, q, sl, :] = (wide(buf[zd, q, sl, :]) + wide(P[q, zd, pl.ds(cut + sl.start, 16), :])).astype(BF)
                strips(rb, one)

        pl.when(here)(add)
        net.go(here, lambda: buf.at[zd], lambda: buf.at[zd], lambda: sems.at[zd], dev)

    def square(self, zd, cond):
        net, h = self.net, self.h
        for half in (0, 1):
            net.wait(cond, lambda: self.fx.at[zd, pl.ds(half * h, h), :], self.fxs.at[zd, half])
            net.wait(cond, lambda: self.fy.at[zd, pl.ds(half * h, h), :], self.fys.at[zd, half])

    def local(self, zd, sl):
        return wide(self.P[self.net.u, zd, sl, :]) + wide(self.fx[zd, sl, :]) + wide(self.fy[zd, sl, :])

    def hop(self, zd, zz):
        net = self.net
        upward, dev = self.route(zd, zz)
        buf, sems = (self.be, self.bes) if upward else (self.ab, self.abs_)
        here = net.at[zz]
        self.square(zd, here)
        if zz in (0, 3):
            def begin(sl):
                self.fx[zd, sl, :] = self.local(zd, sl).astype(BF)

            pl.when(here)(lambda: strips(self.cut, begin))
            net.go(here, lambda: self.fx.at[zd], lambda: buf.at[zd], lambda: sems.at[zd], dev)
        else:
            def plus(sl):
                buf[zd, sl, :] = (self.local(zd, sl) + wide(buf[zd, sl, :])).astype(BF)

            net.wait(here, lambda: buf.at[zd], sems.at[zd])
            pl.when(here)(lambda: strips(self.cut, plus))
            net.go(here, lambda: buf.at[zd], lambda: buf.at[zd], lambda: sems.at[zd], dev)

    def bquad(self):
        net, P, cut, rb, hb, bm, bms = self.net, self.P, self.cut, self.rb, self.hb, self.bm, self.bms
        if not rb:
            return
        z = net.z
        net.wait(net.has_dn, lambda: self.bbe.at[z], self.bbes.at[z])
        net.wait(net.has_up, lambda: self.bab.at[z], self.babs.at[z])
        for q in range(4):
            def fold(sl, q=q):
                s = wide(P[q, z, pl.ds(cut + sl.start, 16), :])
                s = s + jnp.where(net.has_dn, wide(self.bbe[z, q, sl, :]), 0.0)
                s = s + jnp.where(net.has_up, wide(self.bab[z, q, sl, :]), 0.0)
                bm[q, sl, :] = s.astype(BF)
            strips(rb, fold)
        net.go(None, lambda: bm.at[net.ud, pl.ds(0, hb), :], lambda: bm.at[4, pl.ds(0, hb), :], lambda: bms.at[0], net.xn)
        net.go(None, lambda: bm.at[net.ud, pl.ds(hb, hb), :], lambda: bm.at[5, pl.ds(0, hb), :], lambda: bms.at[1], net.yn)
        net.go(None, lambda: bm.at[net.ux, pl.ds(0, hb), :], lambda: bm.at[6, pl.ds(0, hb), :], lambda: bms.at[2], net.xn)
        net.go(None, lambda: bm.at[net.uy, pl.ds(hb, hb), :], lambda: bm.at[7, pl.ds(hb, hb), :], lambda: bms.at[3], net.yn)

    def bquad2(self):
        net, rb, hb, bm, bms = self.net, self.rb, self.hb, self.bm, self.bms
        if not rb:
            return

        def add4(sl):
            bm[4, sl, :] = (wide(bm[4, sl, :]) + wide(bm[net.uy, sl, :])).astype(BF)

        def add5(sl):
            bm[5, sl, :] = (wide(bm[5, sl, :]) + wide(bm[net.ux, pl.ds(hb + sl.start, 16), :])).astype(BF)

        net.wait(None, lambda: bm.at[4, pl.ds(0, hb), :], bms.at[0])
        strips(hb, add4)
        net.go(None, lambda: bm.at[4, pl.ds(0, hb), :], lambda: bm.at[7, pl.ds(0, hb), :], lambda: bms.at[4], net.yn)
        net.wait(None, lambda: bm.at[5, pl.ds(0, hb), :], bms.at[1])
        strips(hb, add5)
        net.go(None, lambda: bm.at[5, pl.ds(0, hb), :], lambda: bm.at[6, pl.ds(hb, hb), :], lambda: bms.at[5], net.xn)

    def last(self, store):
        net, cut, rb, hb, bm, bms = self.net, self.cut, self.rb, self.hb, self.bm, self.bms
        z = net.z
        self.square(z, None)

        def own(sl):
            s = self.local(z, sl)
            s = s + jnp.where(net.has_dn, wide(self.be[z, sl, :]), 0.0)
            s = s + jnp.where(net.has_up, wide(self.ab[z, sl, :]), 0.0)
            store(sl, s)

        net.wait(net.has_dn, lambda: self.be.at[z], self.bes.at[z])
        net.wait(net.has_up, lambda: self.ab.at[z], self.abs_.at[z])
        strips(cut, own)
        if rb:
            net.wait(None, lambda: bm.at[6, pl.ds(0, hb), :], bms.at[2])
            net.wait(None, lambda: bm.at[6, pl.ds(hb, hb), :], bms.at[5])
            net.wait(None, lambda: bm.at[7, pl.ds(0, hb), :], bms.at[4])
            net.wait(None, lambda: bm.at[7, pl.ds(hb, hb), :], bms.at[3])
            strips(rb, lambda sl: store(
                pl.ds(cut + sl.start, 16), wide(bm[net.u, sl, :]) + wide(bm[6, sl, :]) + wide(bm[7, sl, :])))


def rs_scratch(cut, R, D):
    h, rb = cut // 2, R - cut
    V = lambda *s: pltpu.VMEM(s, BF)
    S = pltpu.SemaphoreType.DMA
    return [V(4, h, D), V(4, h, D), V(4, cut, D), V(4, cut, D), V(4, cut, D), V(4, cut, D),
            V(4, 4, max(rb, 16), D), V(4, 4, max(rb, 16), D), V(8, max(rb, 16), D),
            S((4,)), S((4,)), S((4, 2)), S((4, 2)), S((4,)), S((4,)), S((4,)), S((4,)), S((6,))]


def rs_kernel(cut, P, o_ref, ssem, *scr):
    net = Net(ssem)
    net.barrier()
    sc = Scatter(net, cut, P, scr)

    def store(sl, v):
        o_ref[sl, :] = v.astype(o_ref.dtype)

    for zd in (3, 0, 2, 1):
        sc.first(zd)
    for zd in (3, 0, 2, 1):
        sc.mids(zd)
    sc.hop(3, 0); sc.hop(0, 3); sc.bhop(3, 1); sc.bhop(0, 2)
    sc.hop(2, 0); sc.hop(1, 3); sc.bhop(2, 1); sc.bhop(1, 2)
    sc.hop(3, 1); sc.hop(0, 2); sc.bhop(3, 2); sc.bhop(0, 1)
    sc.hop(1, 0); sc.hop(2, 3); sc.bquad()
    sc.hop(2, 1); sc.hop(1, 2)
    sc.hop(3, 2); sc.hop(0, 1); sc.bquad2()
    sc.last(store)
    net.finish()


def rs16(p, cid, cut=96, dtype=F32):
    _, _, R, D = p.shape
    DMA = pltpu.SemaphoreType.DMA
    return pl.pallas_call(
        functools.partial(rs_kernel, cut),
        out_shape=jax.ShapeDtypeStruct((R, D), dtype),
        in_specs=[pl.BlockSpec(memory_space=pltpu.VMEM)],
        out_specs=pl.BlockSpec(memory_space=pltpu.VMEM),
        scratch_shapes=[DMA((96,))] + rs_scratch(cut, R, D),
        compiler_params=pltpu.CompilerParams(collective_id=cid, has_side_effects=True, vmem_limit_bytes=56 * 2**20),
        name="scatter_rows",
    )(p)

def group_of(t):
    g = t // 2
    return jnp.where(g == 0, 3, jnp.where(g == 1, 0, jnp.where(g == 2, 2, 1)))


def expert_kernel(cut, n2, cot, share, gate, up, down, d_n2, p_out, hid_o, dg_o, du_o, dp_o,
                  P, G, U, W, hid, dg, du, xb, cb, pb, wsem, xsem, csem, psem, osem, ssem, *scr):
    net = Net(ssem)
    for i, (src, dst) in enumerate(((gate, G), (up, U), (down, W))):
        pltpu.make_async_copy(src, dst, wsem.at[i]).start()

    def load(t, slot, start):
        zd, j = group_of(t), lax.rem(t, 2)
        for src, dst, sem in ((n2, xb, xsem), (cot, cb, csem)):
            copy = pltpu.make_async_copy(src.at[pl.ds(2 * j, 2), zd], dst.at[slot], sem.at[slot])
            if start:
                copy.start()
            else:
                copy.wait()

    load(0, 0, True)
    net.barrier()
    sc = Scatter(net, cut, P, scr)
    for i, (src, dst) in enumerate(((gate, G), (up, U), (down, W))):
        pltpu.make_async_copy(src, dst, wsem.at[i]).wait()
    rows, width = P.shape[2], P.shape[3]
    ff = G.shape[1]
    tile = 256

    def outs(t, slot):
        zd, j = group_of(t), lax.rem(t, 2)
        quads = pl.ds(2 * j, 2)
        return (pltpu.make_async_copy(pb.at[slot], p_out.at[quads, zd], psem.at[slot]),
                pltpu.make_async_copy(cb.at[slot], dp_o.at[quads, zd], osem.at[slot]))

    def compute(t):
        slot = lax.rem(t, 2)
        zd, j = group_of(t), lax.rem(t, 2)
        quads = pl.ds(2 * j, 2)

        @pl.when(t >= 1)
        def _():
            for o in outs(t - 1, 1 - slot):
                o.wait()

        @pl.when(t < 7)
        def _():
            load(t + 1, 1 - slot, True)

        load(t, slot, False)
        weight = share[quads, zd]

        def scale(i, _):
            sl = pl.ds(pl.multiple_of(i * 16, 16), 16)
            cb[slot, :, sl, :] = (share[quads, zd, sl, :] * cb[slot, :, sl, :].astype(F32)).astype(BF)
            return 0

        lax.fori_loop(0, rows // 16, scale, 0)
        x = xb.at[slot]
        d_prod = cb.at[slot]

        def inner(n, _):
            cols = pl.ds(pl.multiple_of(n * tile, tile), tile)
            xv = x[...].reshape(2 * rows, width)
            g = dot(xv, G[:, cols], ((1,), (0,)))
            uu = dot(xv, U[:, cols], ((1,), (0,)))
            dh = dot(d_prod[...].reshape(2 * rows, width), W[cols, :], ((1,), (1,)))
            s = jax.nn.sigmoid(g)
            gs = g * s
            hid[quads, zd, :, cols] = (gs * uu).astype(BF).reshape(2, rows, tile)
            dg[quads, zd, :, cols] = (dh * uu * s * (1.0 + g * (1.0 - s))).astype(BF).reshape(2, rows, tile)
            du[quads, zd, :, cols] = (dh * gs).astype(BF).reshape(2, rows, tile)
            return 0

        lax.fori_loop(0, ff // tile, inner, 0)

        def outer(n, _):
            cols = pl.ds(pl.multiple_of(n * tile, tile), tile)
            dgv = dg[quads, zd].reshape(2 * rows, ff)
            duv = du[quads, zd].reshape(2 * rows, ff)
            back = dot(dgv, G[cols, :], ((1,), (1,))) + dot(duv, U[cols, :], ((1,), (1,)))
            P[quads, zd, :, cols] = back.astype(BF).reshape(2, rows, tile)
            made = dot(hid[quads, zd].reshape(2 * rows, ff), W[:, cols], ((1,), (0,)))
            made = made.astype(BF).astype(F32).reshape(2, rows, tile)
            pb[slot, :, :, cols] = (weight * made).astype(BF)
            return 0

        lax.fori_loop(0, width // tile, outer, 0)
        for o in outs(t, slot):
            o.start()

    steps = {
        1: [lambda: sc.first(3)],
        2: [lambda: sc.mids(3)],
        3: [lambda: sc.first(0), lambda: sc.bhop(3, 1), lambda: sc.hop(3, 0)],
        4: [lambda: sc.mids(0), lambda: sc.bhop(3, 2), lambda: sc.hop(3, 1)],
        5: [lambda: sc.first(2), lambda: sc.bhop(0, 2), lambda: sc.hop(0, 3), lambda: sc.hop(3, 2)],
        6: [lambda: sc.mids(2), lambda: sc.bhop(0, 1), lambda: sc.hop(0, 2)],
        7: [lambda: sc.first(1), lambda: sc.bhop(2, 1), lambda: sc.hop(0, 1), lambda: sc.hop(2, 0), lambda: sc.hop(2, 3)],
    }

    def turn(t, _):
        compute(t)
        for at, todo in steps.items():
            def act(todo=todo):
                for one in todo:
                    one()
            pl.when(t == at)(act)
        return 0

    lax.fori_loop(0, 8, turn, 0)
    for o in outs(7, 1):
        o.wait()
    keep = [pltpu.make_async_copy(a, b, wsem.at[i]) for i, (a, b) in enumerate(((hid, hid_o), (dg, dg_o), (du, du_o)))]
    for k in keep:
        k.start()
    sc.mids(1)
    sc.hop(2, 1); sc.bhop(1, 2)
    sc.hop(1, 0); sc.hop(1, 3)
    sc.bquad()
    sc.hop(1, 2)
    sc.bquad2()

    def store(sl, v):
        d_n2[sl, :] = v

    sc.last(store)
    for k in keep:
        k.wait()
    net.finish()


def run_expert(n2, cot, share, gate, up, down, cid, cut=96):
    _, _, R, D = n2.shape
    ff = gate.shape[1]
    DMA = pltpu.SemaphoreType.DMA
    S = jax.ShapeDtypeStruct
    V = lambda *s: pltpu.VMEM(s, BF)
    A = pl.BlockSpec(memory_space=pl.ANY)
    M = pl.BlockSpec(memory_space=pltpu.VMEM)
    return pl.pallas_call(
        functools.partial(expert_kernel, cut),
        out_shape=(S((R, D), F32), S((4, 4, R, D), BF), S((4, 4, R, ff), BF), S((4, 4, R, ff), BF), S((4, 4, R, ff), BF), S((4, 4, R, D), BF)),
        in_specs=[A, A, M, A, A, A],
        out_specs=(M, A, A, A, A, A),
        scratch_shapes=[V(4, 4, R, D), V(D, ff), V(D, ff), V(ff, D), V(4, 4, R, ff), V(4, 4, R, ff), V(4, 4, R, ff),
                        V(2, 2, R, D), V(2, 2, R, D), V(2, 2, R, D),
                        DMA((3,)), DMA((2,)), DMA((2,)), DMA((2,)), DMA((2,)), DMA((96,))] + rs_scratch(cut, R, D),
        compiler_params=pltpu.CompilerParams(collective_id=cid, has_side_effects=True, vmem_limit_bytes=62 * 2**20),
        name="expert",
    )(n2, cot, share, gate, up, down)
def swap_kernel(src, out, lsem, ssem, rsem):
    u, z, c = place()
    me = u * 8 + z * 2 + c
    count = out.shape[0]
    bar = pltpu.get_barrier_semaphore()

    def at(j):
        t = lax.rem(me + j, count)
        return t // 8, lax.rem(t, 8) // 2, lax.rem(t, 2), t // 2

    def hello(j, _):
        tu, tz, tc, _e = at(j)
        pl.semaphore_signal(bar, inc=1, device_id=(tu, tz, tc), device_id_type=MESH)
        return 0

    lax.fori_loop(1, count, hello, 0)
    pl.semaphore_wait(bar, count - 1)

    def copy(j):
        tu, tz, tc, e = at(j)
        return pltpu.make_async_remote_copy(
            src_ref=src.at[e], dst_ref=out.at[me], send_sem=ssem, recv_sem=rsem,
            device_id=(tu, tz, tc), device_id_type=MESH)

    own = pltpu.make_async_copy(src.at[me // 2], out.at[me], lsem)
    own.start()

    def send(j, _):
        copy(j).start()
        return 0

    lax.fori_loop(1, count, send, 0)
    own.wait()
    part = out.at[pl.ds(0, count - 1)]
    pltpu.make_async_copy(part, part, rsem).wait()
    pltpu.make_async_copy(part, part, ssem).wait()


def swap(block, cid):
    chips, r, lanes = block.shape
    S = pltpu.SemaphoreType.DMA
    return pl.pallas_call(
        swap_kernel,
        out_shape=jax.ShapeDtypeStruct((2 * chips, r, lanes), block.dtype),
        in_specs=[pl.BlockSpec(memory_space=pltpu.VMEM)],
        out_specs=pl.BlockSpec(memory_space=pltpu.VMEM),
        scratch_shapes=[S, S, S],
        compiler_params=pltpu.CompilerParams(collective_id=cid, has_side_effects=True),
        name="swap_rows",
    )(block)


def spread_kernel(src, out, lsem, ssem, rsem):
    u, z, c = place()
    me = u * 4 + z
    count = out.shape[0]
    bar = pltpu.get_barrier_semaphore()

    def at(j):
        t = lax.rem(me + j, count)
        return t // 4, lax.rem(t, 4), c

    def hello(j, _):
        pl.semaphore_signal(bar, inc=1, device_id=at(j), device_id_type=MESH)
        return 0

    lax.fori_loop(1, count, hello, 0)
    pl.semaphore_wait(bar, count - 1)
    own = pltpu.make_async_copy(src, out.at[me], lsem)
    own.start()

    def send(j, _):
        pltpu.make_async_remote_copy(
            src_ref=src, dst_ref=out.at[me], send_sem=ssem, recv_sem=rsem,
            device_id=at(j), device_id_type=MESH).start()
        return 0

    lax.fori_loop(1, count, send, 0)
    own.wait()
    part = out.at[pl.ds(0, count - 1)]
    pltpu.make_async_copy(part, part, rsem).wait()
    pltpu.make_async_copy(part, part, ssem).wait()


def spread(block, cid):
    S = pltpu.SemaphoreType.DMA
    return pl.pallas_call(
        spread_kernel,
        out_shape=jax.ShapeDtypeStruct((16,) + block.shape, block.dtype),
        in_specs=[pl.BlockSpec(memory_space=pltpu.VMEM)],
        out_specs=pl.BlockSpec(memory_space=pltpu.VMEM),
        scratch_shapes=[S, S, S],
        compiler_params=pltpu.CompilerParams(collective_id=cid, has_side_effects=True),
        name="spread_rows",
    )(block)


def band_scores(q, k, q_seg, k_seg, scale, reach):
    scores = dot(q, k, ((1,), (1,))) * scale
    q_at = lax.broadcasted_iota(jnp.int32, scores.shape, 0)
    k_at = lax.broadcasted_iota(jnp.int32, scores.shape, 1)
    return scores, (k_seg == q_seg) & (k_at <= q_at + reach)


def attend_kernel(scale, reach, q_ref, k_ref, v_ref, qs_ref, ks_ref, o_ref, l_ref):
    rows = q_ref.shape[0]
    first = pl.multiple_of((pl.program_id(0) * 2 + lax.axis_index("core")) * rows, rows)
    band = pl.ds(first, rows + reach)
    scores, allowed = band_scores(q_ref[...], k_ref[band, :], qs_ref[...], ks_ref[:, band], scale, reach)
    scores = jnp.where(allowed, scores, NEG)
    top = jnp.max(scores, axis=1, keepdims=True)
    weights = jnp.where(allowed, jnp.exp(scores - top), 0.0)
    total = jnp.sum(weights, axis=1, keepdims=True)
    probs = (weights / total).astype(BF)
    o_ref[...] = dot(probs, v_ref[band, :], ((1,), (0,))).astype(BF)
    l_ref[...] = top + jnp.log(total)


def attend_back_kernel(scale, reach, q_ref, k_ref, v_ref, qs_ref, ks_ref, l_ref, o_ref, do_ref, dq_ref, dk_ref, dv_ref):
    rows = q_ref.shape[0]

    @pl.when(pl.program_id(0) == 0)
    def _():
        dk_ref[...] = jnp.zeros_like(dk_ref)
        dv_ref[...] = jnp.zeros_like(dv_ref)

    first = pl.multiple_of((pl.program_id(0) * 2 + lax.axis_index("core")) * rows, rows)
    band = pl.ds(first, rows + reach)
    q, k, d_out = q_ref[...], k_ref[band, :], do_ref[...]
    scores, allowed = band_scores(q, k, qs_ref[...], ks_ref[:, band], scale, reach)
    probs = jnp.where(allowed, jnp.exp(scores - l_ref[...]), 0.0)
    d_probs = dot(d_out, v_ref[band, :], ((1,), (1,)))
    delta = jnp.sum(d_out.astype(F32) * o_ref[...].astype(F32), axis=1, keepdims=True)
    d_scores = (probs * (d_probs - delta)).astype(BF)
    dq_ref[...] = (dot(d_scores, k, ((1,), (0,))) * scale).astype(BF)
    dk_ref[band, :] += dot(d_scores, q, ((0,), (0,))) * scale
    dv_ref[band, :] += dot(probs.astype(BF), d_out, ((0,), (0,)))


def core_pair(value):
    return lax.ppermute(value, "core", [(0, 1), (1, 0)])


def dot(a, b, dims):
    return lax.dot_general(a, b, (dims, ((), ())), preferred_element_type=jnp.float32)


def local_chip(
    inputs, cotangent, segments, expert_ids, gate_weights, fill_order, norm1_gain, w_query, w_key,
    w_value, w_output, query_gain, key_gain, norm2_gain, expert_gate, expert_up, expert_down,
):
    chips = 16
    devices = 2 * chips
    rows, width = inputs.shape
    u, z, core = place()
    chip = u * 4 + z
    device = chip * 2 + core
    topk = expert_ids.shape[1]
    experts_n = chips
    capacity = 9 * rows * devices * topk // (8 * experts_n)
    one_hot = expert_ids[:, :, None] == jnp.arange(experts_n, dtype=jnp.int32)[None, None, :]
    chosen = jnp.any(one_hot, axis=1)
    weight = jnp.sum(jnp.where(one_hot, gate_weights[:, :, None], 0.0), axis=1)
    earlier = (fill_order[None, :] < fill_order[:, None]).astype(jnp.bfloat16)
    rank = dot(earlier, chosen.astype(jnp.bfloat16), ((1,), (0,)))
    rank = jnp.where(chosen, rank, -1.0)
    gains = jnp.concatenate([norm1_gain, query_gain, key_gain, norm2_gain]).astype(F32)
    gains = jnp.broadcast_to(gains.reshape(1, 2, 128), (chips, 2, 128))
    block = jnp.concatenate(
        [weight.T[:, None, :], rank.T[:, None, :], gains, jnp.zeros((chips, 4, 128), F32)], axis=1)
    swapped = swap(block, 1)
    gains = swapped[:, 2:4, :].reshape(devices, 4, 64).transpose(1, 0, 2).reshape(4, width)
    gain_one, gain_q, gain_k, gain_two = gains[0], gains[1], gains[2], gains[3]
    rank_all = swapped[:, 1, :]
    taken = rank_all >= 0.0
    counts = jnp.sum(taken.astype(F32), axis=1)
    before = jnp.cumsum(counts) - counts
    kept = taken & (before[:, None] + rank_all < float(capacity))
    share = jnp.where(kept, swapped[:, 0, :], 0.0).reshape(chips, 2, rows)
    share = lax.dynamic_index_in_dim(share, core, 1, keepdims=False).reshape(chips * rows, 1)


    layer_in = inputs.astype(F32)
    mine = ("ulysses", "z")

    def in_order(own, other):
        return jnp.where(core == 0, own, other), jnp.where(core == 0, other, own)

    cols = jnp.stack([w_query, w_key, w_value]).reshape(3, 64, chips, HEAD_DIM).transpose(2, 0, 1, 3)
    cols = lax.all_to_all(cols, mine, split_axis=0, concat_axis=0, tiled=True)
    cols = jnp.stack(in_order(cols, core_pair(cols)), axis=1)
    w_qkv = cols.transpose(0, 1, 3, 2, 4).reshape(width, 3 * HEAD_DIM)
    w_o = jnp.concatenate(in_order(w_output, core_pair(w_output)), axis=0)

    def my_head(gain):
        return lax.dynamic_slice_in_dim(gain, chip * HEAD_DIM, HEAD_DIM, 0)

    x_rows = ag16(inputs, 2).reshape(chips * rows, width)
    cotangent_later, x_rows = lax.optimization_barrier((cotangent, x_rows))
    cot_rows = lax.all_gather(cotangent_later, mine, axis=0, tiled=True)
    x_rows = x_rows.astype(F32)
    n1_rows = norm_rows(x_rows, gain_one).astype(BF)
    lin = dot(n1_rows, w_qkv, ((1,), (0,)))
    q_lin, k_lin, v_lin = lin[:, :HEAD_DIM], lin[:, HEAD_DIM : 2 * HEAD_DIM], lin[:, 2 * HEAD_DIM :]

    def over_chips(a, b, cid):
        both = jnp.stack([a, b]).reshape(2 * chips, rows)
        both = jnp.sum(spread(both, cid), axis=0).reshape(2, chips * rows, 1)
        return both[0], both[1]

    square_q, square_k = over_chips(jnp.sum(q_lin * q_lin, axis=1), jnp.sum(k_lin * k_lin, axis=1), 3)
    rq = lax.rsqrt(square_q / width + EPS)
    rk = lax.rsqrt(square_k / width + EPS)
    positions = (jnp.arange(chips, dtype=jnp.int32)[:, None] * 2 + core) * rows + jnp.arange(rows, dtype=jnp.int32)
    half_dim = HEAD_DIM // 2
    inv_freq = jnp.exp(jnp.arange(half_dim, dtype=F32) * (-2.0 * math.log(ROPE_BASE) / HEAD_DIM))
    angles = positions.reshape(-1).astype(F32)[:, None] * inv_freq[None, :]
    cosine, sine = jnp.cos(angles), jnp.sin(angles)
    cosine = jnp.concatenate([cosine, cosine], axis=1)
    sine = jnp.concatenate([-sine, sine], axis=1)

    def halves_swapped(v):
        return jnp.concatenate([v[:, half_dim:], v[:, :half_dim]], axis=1)

    def turn(v):
        return v * cosine + halves_swapped(v) * sine

    def turn_back(v):
        return v * cosine - halves_swapped(v) * sine

    gq, gk = my_head(gain_q), my_head(gain_k)
    q_rot = turn(q_lin * rq * gq).astype(BF)
    k_rot = turn(k_lin * rk * gk).astype(BF)
    kv = jnp.stack([k_rot, v_lin.astype(BF)]).reshape(2, chips, 1, rows, HEAD_DIM)
    kv = jnp.concatenate(in_order(kv, core_pair(kv)), axis=2).reshape(2, devices * rows, HEAD_DIM)
    reach = devices * rows // 4
    kv = jnp.concatenate([jnp.zeros((2, reach, HEAD_DIM), BF), kv], axis=1)
    k_seg = jnp.concatenate([jnp.full((reach,), -1, jnp.int32), segments]).reshape(1, -1)
    q_seg = lax.dynamic_index_in_dim(segments.reshape(chips, 2, rows), core, 1, keepdims=False).reshape(-1, 1)
    scale = 1.0 / math.sqrt(HEAD_DIM)
    row_block = pl.BlockSpec((rows, HEAD_DIM), lambda i: (i, 0))
    one_block = pl.BlockSpec((rows, 1), lambda i: (i, 0))

    def whole_block(value):
        return pl.BlockSpec(value.shape, lambda i: (0,) * value.ndim)

    tokens = chips * rows
    attended, log_total = pl.pallas_call(
        functools.partial(attend_kernel, scale, reach),
        grid=(chips,),
        out_shape=(jax.ShapeDtypeStruct((tokens, HEAD_DIM), BF), jax.ShapeDtypeStruct((tokens, 1), F32)),
        in_specs=[row_block, whole_block(kv[0]), whole_block(kv[1]), one_block, whole_block(k_seg)],
        out_specs=(row_block, one_block),
        compiler_params=pltpu.CompilerParams(vmem_limit_bytes=32 * 2**20),
        name="attend",
    )(q_rot, kv[0], kv[1], q_seg, k_seg)

    def to_blocks(part):
        return part.astype(BF).reshape(4, 4, rows, width)

    residual = layer_in + rs16(to_blocks(dot(attended, w_o, ((1,), (0,)))), 4)
    r2 = lax.rsqrt(jnp.mean(residual * residual, axis=1, keepdims=True) + EPS)
    normed_two = (residual * r2 * gain_two).astype(BF)
    n2_rows = ag16(normed_two, 5).reshape(tokens, width)

    joined = [
        jnp.concatenate(in_order(part, core_pair(part)), axis=0)
        for part in (expert_gate, expert_up, expert_down)
    ]
    gate_full, up_full, down_full = joined
    blocks = (4, 4, rows, width)
    d_normed_two, mixed, hidden, d_gate_pre, d_up_pre, d_produced = run_expert(
        n2_rows.reshape(blocks), cot_rows.reshape(blocks), share.reshape(4, 4, rows, 1),
        gate_full, up_full, down_full, 6)
    mixed = lax.psum_scatter(mixed.reshape(tokens, width), mine, scatter_dimension=0, tiled=True)
    output = residual + mixed.astype(F32)
    hidden, d_gate_pre, d_up_pre, d_produced = (
        v.reshape(tokens, v.shape[-1]) for v in (hidden, d_gate_pre, d_up_pre, d_produced))

    def shared_grad(full):
        size = full.shape[0] // 2
        own = lax.dynamic_slice_in_dim(full, core * size, size, 0)
        other = lax.dynamic_slice_in_dim(full, (1 - core) * size, size, 0)
        return own + core_pair(other.astype(BF)).astype(F32)

    d_expert_gate = shared_grad(dot(n2_rows, d_gate_pre, ((0,), (0,))))
    d_expert_up = shared_grad(dot(n2_rows, d_up_pre, ((0,), (0,))))
    d_expert_down = shared_grad(dot(hidden, d_produced, ((0,), (0,))))

    def norm_back(d_out, values, r, gain):
        d_scaled = d_out * gain
        inner = jnp.mean(d_scaled * values, axis=1, keepdims=True)
        d_gain = jnp.sum(d_out * values * r, axis=0)
        return r * d_scaled - values * (r * r * r * inner), d_gain

    d_resid_norm, d_gain_two = norm_back(d_normed_two, residual, r2, gain_two)
    d_residual = cotangent.astype(F32) + d_resid_norm
    d_res_rows = ag16(d_residual.astype(BF), 7).reshape(tokens, width)
    d_attended = dot(d_res_rows, w_o, ((1,), (1,))).astype(BF)
    d_w_output = shared_grad(dot(attended, d_res_rows, ((0,), (0,))))
    padded = jax.ShapeDtypeStruct((reach + devices * rows, HEAD_DIM), F32)
    d_q, d_k, d_v = pl.pallas_call(
        functools.partial(attend_back_kernel, scale, reach),
        grid=(chips,),
        out_shape=(jax.ShapeDtypeStruct((tokens, HEAD_DIM), BF), padded, padded),
        in_specs=[row_block, whole_block(kv[0]), whole_block(kv[1]), one_block, whole_block(k_seg), one_block, row_block, row_block],
        out_specs=(row_block, whole_block(padded), whole_block(padded)),
        compiler_params=pltpu.CompilerParams(vmem_limit_bytes=48 * 2**20),
        name="attend_back",
    )(q_rot, kv[0], kv[1], q_seg, k_seg, log_total, attended, d_attended)
    d_kv = jnp.stack([d_k[reach:], d_v[reach:]]).reshape(2, chips, 2, rows, HEAD_DIM)
    d_kv_own = lax.dynamic_index_in_dim(d_kv, core, 2, keepdims=False)
    d_kv_other = lax.dynamic_index_in_dim(d_kv, 1 - core, 2, keepdims=False)
    d_kv = (d_kv_own + core_pair(d_kv_other.astype(BF)).astype(F32)).astype(BF).reshape(2, tokens, HEAD_DIM)
    d_q_un = turn_back(d_q.astype(F32))
    d_k_un = turn_back(d_kv[0].astype(F32))
    inner_q, inner_k = over_chips(
        jnp.sum(d_q_un * gq * q_lin, axis=1), jnp.sum(d_k_un * gk * k_lin, axis=1), 8)
    d_q_lin = rq * (d_q_un * gq) - q_lin * (rq * rq * rq * (inner_q / width))
    d_k_lin = rk * (d_k_un * gk) - k_lin * (rk * rk * rk * (inner_k / width))
    d_gain_q = jnp.sum(d_q_un * q_lin * rq, axis=0)
    d_gain_k = jnp.sum(d_k_un * k_lin * rk, axis=0)
    d_lin = jnp.concatenate([d_q_lin.astype(BF), d_k_lin.astype(BF), d_kv[1]], axis=1)
    d_normed_one = rs16(to_blocks(dot(d_lin, w_qkv, ((1,), (1,)))), 9)
    d_cols = dot(n1_rows, d_lin, ((0,), (0,))).reshape(chips, 2, 64, 3 * HEAD_DIM)
    d_cols_own = lax.dynamic_index_in_dim(d_cols, core, 1, keepdims=False)
    d_cols_other = lax.dynamic_index_in_dim(d_cols, 1 - core, 1, keepdims=False)
    d_cols = (d_cols_own + core_pair(d_cols_other.astype(BF)).astype(F32)).astype(BF)
    d_cols = lax.all_to_all(d_cols, mine, split_axis=0, concat_axis=0, tiled=True)
    d_cols = d_cols.reshape(chips, 64, 3, HEAD_DIM).transpose(2, 1, 0, 3).reshape(3, 64, width).astype(F32)
    r1 = lax.rsqrt(jnp.mean(layer_in * layer_in, axis=1, keepdims=True) + EPS)
    d_layer_in, d_gain_one = norm_back(d_normed_one, layer_in, r1, gain_one)
    d_inputs = d_residual + d_layer_in
    block = jnp.concatenate(
        [d_gain_one.reshape(chips, 1, 128), d_gain_two.reshape(chips, 1, 128), jnp.zeros((chips, 6, 128), F32)], axis=1)
    d_gains = jnp.sum(swap(block, 10)[:, :2, :], axis=0)

    def my_half(row):
        return lax.dynamic_slice_in_dim(row, core * 64, 64, 0)

    d_qk_gains = jnp.stack([d_gain_q, d_gain_k])
    d_qk_gains = d_qk_gains + core_pair(d_qk_gains)
    return (
        output,
        d_inputs,
        my_half(d_gains[0]),
        d_cols[0],
        d_cols[1],
        d_cols[2],
        d_w_output,
        my_half(d_qk_gains[0]),
        my_half(d_qk_gains[1]),
        my_half(d_gains[1]),
        d_expert_gate,
        d_expert_up,
        d_expert_down,
    )
def whole(mesh, step, rows):
    return jax.shard_map(
        step,
        mesh=mesh,
        in_specs=(
            P(rows, None),
            P(rows, None),
            P(),
            P(rows, None),
            P(rows, None),
            P(rows),
            P(rows),
            P(rows, None),
            P(rows, None),
            P(rows, None),
            P(rows, None),
            P(rows),
            P(rows),
            P(rows),
            P(rows, None),
            P(rows, None),
            P(rows, None),
        ),
        out_specs=(
            P(rows, None),
            P(rows, None),
            P(rows),
            P(rows, None),
            P(rows, None),
            P(rows, None),
            P(rows, None),
            P(rows),
            P(rows),
            P(rows),
            P(rows, None),
            P(rows, None),
            P(rows, None),
        ),
        check_vma=False,
    )


def solution(mesh):
    groups, blk_size = mesh.shape["ulysses"], mesh.shape["blk"]

    def step(*args):
        if groups != 4 or blk_size != 8 or args[7].shape[1] // HEAD_DIM != groups * blk_size // 2:
            return whole(mesh, local, ("ulysses", "blk"))(*args)
        chips = Mesh(mesh.devices.reshape(groups, blk_size // 2, 2), ("ulysses", "z", "core"))
        return whole(chips, local_chip, ("ulysses", "z", "core"))(*args)

    return step
```

```python
import functools
import math

import jax
import jax.numpy as jnp
from jax import lax
from jax.experimental import pallas as pl
from jax.experimental.pallas import tpu as pltpu
from jax.sharding import Mesh
from jax.sharding import PartitionSpec as P

HEAD_DIM = 128


EPS = 1e-05
ROPE_BASE = 10000.0
NEG = -1e30


def as_sent(value):

    def short(part):
        return part.astype(jnp.bfloat16) if part.dtype == jnp.float32 else part

    return jax.tree.map(short, value)


def passed_along(block, axis, distance):
    devices = range(lax.axis_size(axis))
    route = [((i - distance) % len(devices), i) for i in devices]
    return lax.ppermute(block, axis, route)


def prefix(value, axis, join, neutral):
    count, mine = (lax.axis_size(axis), lax.axis_index(axis))
    pieces = lax.all_gather(value, axis)
    subtotal = jnp.full_like(value, 0) + jnp.asarray(neutral, value.dtype)

    def hop(position, subtotal):
        longer = join(subtotal, pieces[position])
        return jnp.where(position < mine, longer, subtotal)

    return lax.fori_loop(0, count - 1, hop, subtotal)


def partner_2(block, axis, bit):
    count = lax.axis_size(axis)
    route = []
    for low in range(count):
        high = low | 1 << bit
        if high != low and high < count:
            route += [(low, high), (high, low)]
    return lax.ppermute(block, axis, route)


def norm_rows(values, gain_vec):
    return values * lax.rsqrt(jnp.mean(values * values, axis=-1, keepdims=True) + EPS) * gain_vec


def rotate(values, positions):
    half_dim = HEAD_DIM // 2
    heads_here = values.shape[1] // HEAD_DIM
    inv_freq = jnp.exp(
        jnp.arange(half_dim, dtype=jnp.float32) * (-2.0 * math.log(ROPE_BASE) / HEAD_DIM)
    )
    angles = positions.astype(jnp.float32)[:, None] * inv_freq[None, :]
    cosine = jnp.cos(angles)[:, None, :]
    sin_t = jnp.sin(angles)[:, None, :]
    shaped = values.reshape(values.shape[0], heads_here, HEAD_DIM)
    lower_half = shaped[..., :half_dim]
    upper_half = shaped[..., half_dim:]
    turned = jnp.concatenate(
        [lower_half * cosine - upper_half * sin_t, upper_half * cosine + lower_half * sin_t],
        axis=-1,
    )
    return turned.reshape(values.shape)


def attn_inputs(q_lin, k_lin, gain_q, gain_k, positions):
    return (
        rotate(norm_rows(q_lin, gain_q), positions),
        rotate(norm_rows(k_lin, gain_k), positions),
    )


def banded(shaped, fill_value):
    earlier = jnp.concatenate([jnp.full_like(shaped[:1], fill_value), shaped[:-1]], axis=0)
    return jnp.concatenate([earlier, shaped], axis=1)


def unbanded(band, local_rows):
    earlier = band[:, :local_rows]
    own_part = band[:, local_rows:]
    moved_up = jnp.concatenate([earlier[1:], jnp.zeros_like(earlier[:1])], axis=0)
    return own_part + moved_up


def add_counts(earlier, later):
    return earlier + later


def expert_move(buffer):
    return lax.all_to_all(buffer, ("ulysses", "blk"), split_axis=0, concat_axis=0, tiled=True)


def to_head_layout(values):
    return jax.tree.map(
        lambda part, own: part.astype(own.dtype),
        lax.all_to_all(as_sent(values), "ulysses", split_axis=1, concat_axis=0, tiled=True),
        values,
    )


def to_token_layout(values):
    return jax.tree.map(
        lambda part, own: part.astype(own.dtype),
        lax.all_to_all(as_sent(values), "ulysses", split_axis=0, concat_axis=1, tiled=True),
        values,
    )


def local(
    inputs,
    cotangent,
    segments,
    expert_ids,
    gate_weights,
    fill_order,
    norm1_gain,
    w_query,
    w_key,
    w_value,
    w_output,
    query_gain,
    key_gain,
    norm2_gain,
    expert_gate,
    expert_up,
    expert_down,
):
    blk_size = lax.axis_size("blk")
    groups = lax.axis_size("ulysses")
    devices = blk_size * groups
    local_rows = inputs.shape[0]
    model_width = inputs.shape[1]
    blk_index = lax.axis_index("blk")
    group_index = lax.axis_index("ulysses")
    device_index = group_index * blk_size + blk_index
    positions = device_index * local_rows + jnp.arange(local_rows, dtype=jnp.int32)
    heads_dev = model_width // groups // HEAD_DIM
    score_scale = 1.0 / math.sqrt(HEAD_DIM)
    layer_in = inputs.astype(jnp.float32)
    dense = (w_query, w_key, w_value, w_output, norm1_gain, query_gain, key_gain, norm2_gain)
    gathered = (
        lax.all_gather(dense[0], ("ulysses", "blk"), axis=0, tiled=True),
        lax.all_gather(dense[1], ("ulysses", "blk"), axis=0, tiled=True),
        lax.all_gather(dense[2], ("ulysses", "blk"), axis=0, tiled=True),
        lax.all_gather(dense[3], ("ulysses", "blk"), axis=0, tiled=True),
        lax.all_gather(dense[4], ("ulysses", "blk"), axis=0, tiled=True),
        lax.all_gather(dense[5], ("ulysses", "blk"), axis=0, tiled=True),
        lax.all_gather(dense[6], ("ulysses", "blk"), axis=0, tiled=True),
        lax.all_gather(dense[7], ("ulysses", "blk"), axis=0, tiled=True),
    )
    w_q, w_k, w_v, w_o = (gathered[0], gathered[1], gathered[2], gathered[3])
    gain_one = gathered[4].astype(jnp.float32)
    gain_q = gathered[5].astype(jnp.float32)
    gain_k = gathered[6].astype(jnp.float32)
    gain_two = gathered[7].astype(jnp.float32)
    normed_one = norm_rows(layer_in, gain_one).astype(jnp.bfloat16)
    q_lin = jnp.dot(normed_one, w_q, preferred_element_type=jnp.float32)
    k_lin = jnp.dot(normed_one, w_k, preferred_element_type=jnp.float32)
    v_lin = jnp.dot(normed_one, w_v, preferred_element_type=jnp.float32)
    (q_rot, k_rot), pre_back = jax.vjp(
        lambda q_in, k_in, gq_in, gk_in: attn_inputs(q_in, k_in, gq_in, gk_in, positions),
        q_lin,
        k_lin,
        gain_q,
        gain_k,
    )
    q_heads, k_heads, v_heads = to_head_layout(
        (q_rot.astype(jnp.bfloat16), k_rot.astype(jnp.bfloat16), v_lin.astype(jnp.bfloat16))
    )
    group_ids = jnp.arange(groups, dtype=jnp.int32)[:, None]
    row_ids = jnp.arange(local_rows, dtype=jnp.int32)[None, :]
    q_pos = (group_ids * blk_size + blk_index) * local_rows + row_ids
    q_seg = segments[q_pos]
    four_shape = (groups, local_rows, heads_dev, HEAD_DIM)
    q_four = q_heads.reshape(four_shape)

    def score_block(k_now, source):
        k_pos = (group_ids * blk_size + source) * local_rows + row_ids
        k_seg = banded(segments[k_pos], -1)
        k_pos = banded(k_pos, 0)
        k_band = banded(k_now.reshape(four_shape), 0)
        raw_scores = (
            jnp.einsum("gqhd,gkhd->gqhk", q_four, k_band, preferred_element_type=jnp.float32)
            * score_scale
        )
        allowed = (k_seg[:, None, :] == q_seg[:, :, None]) & (
            k_pos[:, None, :] <= q_pos[:, :, None]
        )
        return (raw_scores, allowed[:, :, None, :], k_band)

    def forward_step(flash_state, kv_stack, step_id):
        run_max, run_sum, run_out = flash_state
        source = jnp.mod(blk_index - step_id, blk_size)
        raw_scores, allowed, k_band = score_block(kv_stack[0], source)
        raw_scores = jnp.where(allowed, raw_scores, NEG)
        new_max = jnp.maximum(run_max, jnp.max(raw_scores, axis=-1))
        shrink = jnp.exp(run_max - new_max)
        weights = jnp.where(allowed, jnp.exp(raw_scores - new_max[..., None]), 0.0)
        run_sum = run_sum * shrink + jnp.sum(weights, axis=-1)
        v_band = banded(kv_stack[1].reshape(four_shape), 0)
        run_out = run_out * shrink[..., None] + jnp.einsum(
            "gqhk,gkhd->gqhd",
            weights.astype(jnp.bfloat16),
            v_band,
            preferred_element_type=jnp.float32,
        )
        return (new_max, run_sum, run_out)

    start_state = (
        jnp.full((groups, local_rows, heads_dev), NEG, jnp.float32),
        jnp.zeros((groups, local_rows, heads_dev), jnp.float32),
        jnp.zeros(four_shape, jnp.float32),
    )
    kv_home = jnp.stack([k_heads, v_heads])
    first_state = forward_step(start_state, kv_home, 0)

    def forward_turn(step_id, loop_state):
        flash_state, kv_stack = loop_state
        moved = passed_along(kv_stack, "blk", 1)
        return (forward_step(flash_state, moved, step_id), moved)

    final_state, unused_kv = lax.fori_loop(1, blk_size, forward_turn, (first_state, kv_home))
    run_max, run_sum, run_out = final_state
    o_four = (run_out / run_sum[..., None]).astype(jnp.bfloat16)
    log_total = run_max + jnp.log(run_sum)
    o_heads = o_four.reshape(groups * local_rows, heads_dev * HEAD_DIM)
    attended = to_token_layout(o_heads)
    residual = layer_in + jnp.dot(attended, w_o, preferred_element_type=jnp.float32)
    normed_two_f, norm_two_back = jax.vjp(norm_rows, residual, gain_two)
    normed_two = normed_two_f.astype(jnp.bfloat16)
    experts_n = devices // 2
    topk = expert_ids.shape[1]
    per_source = 2 * local_rows * topk // experts_n
    half_slots = per_source // 2
    capacity = 9 * local_rows * devices * topk // (8 * experts_n)
    slots_all = experts_n * per_source
    tokens_local = jnp.arange(local_rows, dtype=jnp.int32)
    chosen = jnp.sum(
        (expert_ids[:, :, None] == jnp.arange(experts_n, dtype=jnp.int32)[None, None, :]).astype(
            jnp.int32
        ),
        axis=1,
    )
    by_fill = jnp.zeros((local_rows,), jnp.int32).at[fill_order].set(tokens_local)
    sorted_rows = chosen[by_fill]
    before = jnp.cumsum(sorted_rows, axis=0) - sorted_rows
    rank_all = before[fill_order]
    pair_rank = jnp.take_along_axis(rank_all, expert_ids, axis=1)
    counts = jnp.sum(chosen, axis=0)
    offsets = prefix(counts, ("ulysses", "blk"), add_counts, jnp.zeros_like(counts))
    kept_pair = offsets[expert_ids] + pair_rank < capacity
    pair_slot = expert_ids * per_source + pair_rank
    pair_index = tokens_local[:, None] * topk + jnp.arange(topk, dtype=jnp.int32)[None, :]
    slot_pair = (
        jnp.zeros((slots_all,), jnp.int32).at[pair_slot.reshape(-1)].set(pair_index.reshape(-1))
    )
    slot_live = (
        jnp.zeros((slots_all,), jnp.bool_).at[pair_slot.reshape(-1)].set(kept_pair.reshape(-1))
    )
    slot_token = slot_pair // topk
    send_rows = jnp.where(slot_live[:, None], normed_two[slot_token], jnp.zeros((), jnp.bfloat16))
    received = expert_move(send_rows.reshape(devices, half_slots, model_width)).reshape(
        devices * half_slots, model_width
    )
    parity = jnp.mod(blk_index, 2)
    partner = partner_2((expert_gate, expert_up, expert_down), "blk", 0)

    def joined(own_half, other_half):
        lower_part = jnp.where(parity == 0, own_half, other_half)
        upper_part = jnp.where(parity == 0, other_half, own_half)
        return jnp.concatenate([lower_part, upper_part], axis=0)

    gate_full = joined(expert_gate, partner[0])
    up_full = joined(expert_up, partner[1])
    down_full = joined(expert_down, partner[2])
    gate_pre = jnp.dot(received, gate_full, preferred_element_type=jnp.float32)
    up_pre = jnp.dot(received, up_full, preferred_element_type=jnp.float32)
    hidden = (jax.nn.silu(gate_pre) * up_pre).astype(jnp.bfloat16)
    produced = jnp.dot(hidden, down_full, preferred_element_type=jnp.float32).astype(jnp.bfloat16)
    returned = expert_move(produced.reshape(devices, half_slots, model_width)).reshape(
        slots_all, model_width
    )
    pair_share = jnp.where(kept_pair, gate_weights, 0.0)
    mixed = jnp.einsum("tk,tkd->td", pair_share, returned[pair_slot].astype(jnp.float32))
    output = residual + mixed
    grad_out = cotangent.astype(jnp.float32)
    slot_share = jnp.where(slot_live, gate_weights.reshape(-1)[slot_pair], 0.0)
    grad_send = (slot_share[:, None] * grad_out[slot_token]).astype(jnp.bfloat16)
    grad_rows = expert_move(grad_send.reshape(devices, half_slots, model_width)).reshape(
        devices * half_slots, model_width
    )
    d_down_full = jnp.einsum("rf,rd->fd", hidden, grad_rows, preferred_element_type=jnp.float32)
    d_hidden = jnp.einsum("rd,fd->rf", grad_rows, down_full, preferred_element_type=jnp.float32)
    sigma = jax.nn.sigmoid(gate_pre)
    d_gate_pre = (d_hidden * up_pre * sigma * (1.0 + gate_pre * (1.0 - sigma))).astype(jnp.bfloat16)
    d_up_pre = (d_hidden * gate_pre * sigma).astype(jnp.bfloat16)
    d_gate_full = jnp.einsum("rd,rf->df", received, d_gate_pre, preferred_element_type=jnp.float32)
    d_up_full = jnp.einsum("rd,rf->df", received, d_up_pre, preferred_element_type=jnp.float32)
    d_pair_rows = (
        jnp.einsum("rf,df->rd", d_gate_pre, gate_full, preferred_element_type=jnp.float32)
        + jnp.einsum("rf,df->rd", d_up_pre, up_full, preferred_element_type=jnp.float32)
    ).astype(jnp.bfloat16)
    back_rows = expert_move(d_pair_rows.reshape(devices, half_slots, model_width)).reshape(
        slots_all, model_width
    )
    d_normed_two = jnp.sum(
        jnp.where(kept_pair[:, :, None], back_rows[pair_slot].astype(jnp.float32), 0.0), axis=1
    )
    half_rows = expert_gate.shape[0]
    half_hidden = expert_down.shape[0]

    def halves(full_grad, size):
        own_half = lax.dynamic_slice_in_dim(full_grad, parity * size, size, 0)
        other_half = lax.dynamic_slice_in_dim(full_grad, (1 - parity) * size, size, 0)
        return (own_half, other_half)

    gate_own, gate_other = halves(d_gate_full, half_rows)
    up_own, up_other = halves(d_up_full, half_rows)
    down_own, down_other = halves(d_down_full, half_hidden)
    partner_grads = (
        partner_2(gate_other.astype(jnp.bfloat16), "blk", 0).astype(gate_other.dtype),
        partner_2(up_other.astype(jnp.bfloat16), "blk", 0).astype(up_other.dtype),
        partner_2(down_other.astype(jnp.bfloat16), "blk", 0).astype(down_other.dtype),
    )
    d_expert_gate = gate_own + partner_grads[0]
    d_expert_up = up_own + partner_grads[1]
    d_expert_down = down_own + partner_grads[2]
    d_resid_norm, d_gain_two = norm_two_back(d_normed_two)
    d_residual = grad_out + d_resid_norm
    d_res_low = d_residual.astype(jnp.bfloat16)
    d_attended = jnp.einsum("te,de->td", d_res_low, w_o, preferred_element_type=jnp.float32).astype(
        jnp.bfloat16
    )
    d_o_heads = to_head_layout(d_attended)
    d_o_four = d_o_heads.reshape(four_shape)
    row_delta = jnp.sum(d_o_four.astype(jnp.float32) * o_four.astype(jnp.float32), axis=-1)

    def back_turn(step_id, loop_state):
        moving, dq_acc = loop_state
        source = jnp.mod(blk_index - step_id, blk_size)
        k_now = moving[0].astype(jnp.bfloat16)
        v_now = moving[1].astype(jnp.bfloat16)
        raw_scores, allowed, k_band = score_block(k_now, source)
        prob_rows = jnp.where(allowed, jnp.exp(raw_scores - log_total[..., None]), 0.0)
        v_band = banded(v_now.reshape(four_shape), 0)
        d_probs = jnp.einsum(
            "gqhd,gkhd->gqhk", d_o_four, v_band, preferred_element_type=jnp.float32
        )
        d_scores = (prob_rows * (d_probs - row_delta[..., None])).astype(jnp.bfloat16)
        dv_band = jnp.einsum(
            "gqhk,gqhd->gkhd",
            prob_rows.astype(jnp.bfloat16),
            d_o_four,
            preferred_element_type=jnp.float32,
        )
        dk_band = (
            jnp.einsum("gqhk,gqhd->gkhd", d_scores, q_four, preferred_element_type=jnp.float32)
            * score_scale
        )
        dq_acc = (
            dq_acc
            + jnp.einsum("gqhk,gkhd->gqhd", d_scores, k_band, preferred_element_type=jnp.float32)
            * score_scale
        )
        flat_shape = moving[2].shape
        dk_new = moving[2] + unbanded(dk_band, local_rows).reshape(flat_shape)
        dv_new = moving[3] + unbanded(dv_band, local_rows).reshape(flat_shape)
        moving = passed_along(
            jnp.stack([moving[0], moving[1], dk_new, dv_new]).astype(jnp.bfloat16), "blk", 1
        ).astype(jnp.float32)
        return (moving, dq_acc)

    zero_rows = jnp.zeros(k_heads.shape, jnp.float32)
    start_moving = jnp.stack(
        [k_heads.astype(jnp.float32), v_heads.astype(jnp.float32), zero_rows, zero_rows]
    )
    moving, dq_acc = lax.fori_loop(
        0, blk_size, back_turn, (start_moving, jnp.zeros(four_shape, jnp.float32))
    )
    d_q_send = dq_acc.astype(jnp.bfloat16).reshape(k_heads.shape)
    d_k_send = moving[2].astype(jnp.bfloat16)
    d_v_send = moving[3].astype(jnp.bfloat16)
    d_q_rot, d_k_rot, d_v_lin = to_token_layout((d_q_send, d_k_send, d_v_send))
    d_q_lin, d_k_lin, d_gain_q, d_gain_k = pre_back(
        (d_q_rot.astype(jnp.float32), d_k_rot.astype(jnp.float32))
    )
    d_q_low = d_q_lin.astype(jnp.bfloat16)
    d_k_low = d_k_lin.astype(jnp.bfloat16)
    d_normed_one = jnp.einsum("te,de->td", d_q_low, w_q, preferred_element_type=jnp.float32)
    d_normed_one = d_normed_one + jnp.einsum(
        "te,de->td", d_k_low, w_k, preferred_element_type=jnp.float32
    )
    d_normed_one = d_normed_one + jnp.einsum(
        "te,de->td", d_v_lin, w_v, preferred_element_type=jnp.float32
    )
    unused_norm, norm_one_back = jax.vjp(norm_rows, layer_in, gain_one)
    d_layer_in, d_gain_one = norm_one_back(d_normed_one)
    d_inputs = d_residual + d_layer_in
    d_qk_heads = to_head_layout((d_q_low, d_k_low))
    rows_all = (
        lax.all_gather(normed_one, "ulysses", axis=0, tiled=True),
        lax.all_gather(d_res_low, "ulysses", axis=0, tiled=True),
    )
    head_cols = model_width // groups
    piece_rows = model_width // devices

    def by_owner(part):
        rest = part.shape[1:]
        shaped = part.reshape((groups, blk_size, piece_rows) + rest)
        return jnp.swapaxes(shaped, 0, 1).reshape((model_width,) + rest)

    part_q = jnp.einsum("td,te->de", rows_all[0], d_qk_heads[0], preferred_element_type=jnp.float32)
    part_k = jnp.einsum("td,te->de", rows_all[0], d_qk_heads[1], preferred_element_type=jnp.float32)
    part_v = jnp.einsum("td,te->de", rows_all[0], d_v_send, preferred_element_type=jnp.float32)
    part_o = jnp.einsum("te,td->ed", o_heads, rows_all[1], preferred_element_type=jnp.float32)
    blk_sums = (
        lax.psum_scatter(
            by_owner(part_q).astype(jnp.bfloat16), "blk", scatter_dimension=0, tiled=True
        ).astype(jnp.float32),
        lax.psum_scatter(
            by_owner(part_k).astype(jnp.bfloat16), "blk", scatter_dimension=0, tiled=True
        ).astype(jnp.float32),
        lax.psum_scatter(
            by_owner(part_v).astype(jnp.bfloat16), "blk", scatter_dimension=0, tiled=True
        ).astype(jnp.float32),
        lax.psum_scatter(
            part_o.astype(jnp.bfloat16), "blk", scatter_dimension=0, tiled=True
        ).astype(jnp.float32),
        lax.psum_scatter(
            by_owner(d_gain_one).astype(jnp.bfloat16), "blk", scatter_dimension=0, tiled=True
        ).astype(jnp.float32),
        lax.psum_scatter(
            by_owner(d_gain_q).astype(jnp.bfloat16), "blk", scatter_dimension=0, tiled=True
        ).astype(jnp.float32),
        lax.psum_scatter(
            by_owner(d_gain_k).astype(jnp.bfloat16), "blk", scatter_dimension=0, tiled=True
        ).astype(jnp.float32),
        lax.psum_scatter(
            by_owner(d_gain_two).astype(jnp.bfloat16), "blk", scatter_dimension=0, tiled=True
        ).astype(jnp.float32),
    )

    def widened(part):
        return lax.dynamic_update_slice_in_dim(
            jnp.zeros((part.shape[0], model_width), jnp.float32), part, group_index * head_cols, 1
        )

    col_sums = (
        lax.psum_scatter(
            widened(blk_sums[0]).astype(jnp.bfloat16), "ulysses", scatter_dimension=0, tiled=True
        ).astype(jnp.float32),
        lax.psum_scatter(
            widened(blk_sums[1]).astype(jnp.bfloat16), "ulysses", scatter_dimension=0, tiled=True
        ).astype(jnp.float32),
        lax.psum_scatter(
            widened(blk_sums[2]).astype(jnp.bfloat16), "ulysses", scatter_dimension=0, tiled=True
        ).astype(jnp.float32),
        lax.psum_scatter(
            blk_sums[4].astype(jnp.bfloat16), "ulysses", scatter_dimension=0, tiled=True
        ).astype(jnp.float32),
        lax.psum_scatter(
            blk_sums[5].astype(jnp.bfloat16), "ulysses", scatter_dimension=0, tiled=True
        ).astype(jnp.float32),
        lax.psum_scatter(
            blk_sums[6].astype(jnp.bfloat16), "ulysses", scatter_dimension=0, tiled=True
        ).astype(jnp.float32),
        lax.psum_scatter(
            blk_sums[7].astype(jnp.bfloat16), "ulysses", scatter_dimension=0, tiled=True
        ).astype(jnp.float32),
    )
    result_grads = (
        col_sums[0],
        col_sums[1],
        col_sums[2],
        blk_sums[3],
        col_sums[3],
        col_sums[4],
        col_sums[5],
        col_sums[6],
    )
    return (
        output,
        d_inputs,
        result_grads[4],
        result_grads[0],
        result_grads[1],
        result_grads[2],
        result_grads[3],
        result_grads[5],
        result_grads[6],
        result_grads[7],
        d_expert_gate,
        d_expert_up,
        d_expert_down,
    )


MESH = pl.DeviceIdType.MESH
P1 = 96

def place():
    u = lax.axis_index("ulysses"); z = lax.axis_index("z"); c = lax.axis_index("core")
    return u, z, c

def ag_kernel(cut, x_ref, o_ref, local_sem, s_sem, zr, xr, yr, d1r, d2r, bs, br, bzr):
    u, z, c = place()
    Z = 4
    R = x_ref.shape[0]
    ux, uy = u ^ 1, u ^ 2
    xn, yn, up, dn = (ux, z, c), (uy, z, c), (u, z + 1, c), (u, z - 1, c)
    has_up, has_dn = z < Z - 1, z > 0
    bar = pltpu.get_barrier_semaphore()
    for n in (xn, yn):
        pl.semaphore_signal(bar, inc=1, device_id=n, device_id_type=MESH)
    @pl.when(has_up)
    def _():
        pl.semaphore_signal(bar, inc=1, device_id=up, device_id_type=MESH)
    @pl.when(has_dn)
    def _():
        pl.semaphore_signal(bar, inc=1, device_id=dn, device_id_type=MESH)
    pl.semaphore_wait(bar, 2 + has_up.astype(jnp.int32) + has_dn.astype(jnp.int32))
    sends = []
    def copy(src, dst, ss, rs, dev):
        return pltpu.make_async_remote_copy(src_ref=src, dst_ref=dst, send_sem=ss, recv_sem=rs, device_id=dev, device_id_type=MESH)
    def go(cond, make):
        idx = len(sends)
        def mk():
            return make(s_sem.at[idx])
        sends.append((cond, mk))
        if cond is None:
            mk().start()
        else:
            pl.when(cond)(lambda: mk().start())
    def both(a, b):
        if a is None: return b
        if b is None: return a
        return jnp.logical_and(a, b)
    def wait(cond, ref, sem):
        def w():
            pltpu.make_async_copy(ref, ref, sem).wait()
        if cond is None: w()
        else: pl.when(cond)(w)
    own = pltpu.make_async_copy(x_ref, o_ref.at[u, z], local_sem)
    own.start()
    A = slice(0, cut)
    h = cut // 2
    def oa(uu, zz, lo=0, n=cut):
        return o_ref.at[uu, zz, pl.ds(lo, n), :]
    def spread(s, zz, cond):
        src = (lambda: x_ref.at[pl.ds(0, cut), :]) if s == 0 else (lambda: oa(u, zz))
        go(cond, lambda sm: copy(src(), oa(u, zz), sm, xr.at[zz], xn))
        go(cond, lambda sm: copy(src(), oa(u, zz), sm, yr.at[zz], yn))
    def cross(zz, cond):
        wait(cond, oa(ux, zz), xr.at[zz])
        go(cond, lambda sm: copy(oa(ux, zz, 0, h), oa(ux, zz, 0, h), sm, d1r.at[zz], yn))
        wait(cond, oa(uy, zz), yr.at[zz])
        go(cond, lambda sm: copy(oa(uy, zz, h, h), oa(uy, zz, h, h), sm, d2r.at[zz], xn))
    rb = R - cut
    hb = rb // 2
    def ob(uu, zz, lo=0, n=None):
        return o_ref.at[uu, zz, pl.ds(cut + lo, rb if n is None else n), :]
    go(has_up, lambda sm: copy(x_ref.at[pl.ds(0, cut), :], oa(u, z), sm, zr.at[z], up))
    go(has_dn, lambda sm: copy(x_ref.at[pl.ds(0, cut), :], oa(u, z), sm, zr.at[z], dn))
    if rb:
        go(None, lambda sm: copy(x_ref.at[pl.ds(cut, rb), :], ob(u, z), sm, br.at[0], xn))
        go(None, lambda sm: copy(x_ref.at[pl.ds(cut, rb), :], ob(u, z), sm, br.at[1], yn))
    spread(0, z, None)
    if rb:
        wait(None, ob(ux, z), br.at[0])
        go(None, lambda sm: copy(ob(ux, z, 0, hb), ob(ux, z, 0, hb), sm, br.at[2], yn))
        wait(None, ob(uy, z), br.at[1])
        go(None, lambda sm: copy(ob(uy, z, hb, hb), ob(uy, z, hb, hb), sm, br.at[3], xn))
    own.wait()
    def quad(zz):
        return o_ref.at[:, zz, pl.ds(cut, rb), :]
    def zs(s):
        zl, zh = z - s, z + s
        cl, ch = zl >= 0, zh < Z
        zlc, zhc = jnp.maximum(zl, 0), jnp.minimum(zh, Z - 1)
        return (zlc, cl, has_up, up), (zhc, ch, has_dn, dn)
    prev = [(z, None)]
    for s in range(1, Z):
        cur = []
        for (zz, cond, fwd, dev) in zs(s):
            wait(cond, oa(u, zz), zr.at[zz])
            go(both(cond, fwd), lambda sm, zz=zz, dev=dev: copy(oa(u, zz), oa(u, zz), sm, zr.at[zz], dev))
            spread(s, zz, cond)
            cur.append((zz, cond))
        if rb and s == 1:
            wait(None, ob(u ^ 3, z, 0, hb), br.at[2])
            wait(None, ob(u ^ 3, z, hb, hb), br.at[3])
            go(has_up, lambda sm: copy(quad(z), quad(z), sm, bzr.at[z], up))
            go(has_dn, lambda sm: copy(quad(z), quad(z), sm, bzr.at[z], dn))
        elif rb:
            for (zz, cond, fwd, dev) in zs(s - 1):
                wait(cond, quad(zz), bzr.at[zz])
                go(both(cond, fwd), lambda sm, zz=zz, dev=dev: copy(quad(zz), quad(zz), sm, bzr.at[zz], dev))
        for zz, cond in prev:
            cross(zz, cond)
        prev = cur
    if rb:
        for (zz, cond, fwd, dev) in zs(Z - 1):
            wait(cond, quad(zz), bzr.at[zz])
    for zz, cond in prev:
        cross(zz, cond)
    for zz in range(Z):
        wait(None, oa(u ^ 3, zz, 0, h), d1r.at[zz])
        wait(None, oa(u ^ 3, zz, h, h), d2r.at[zz])
    for cond, mk in sends:
        if cond is None: mk().wait_send()
        else: pl.when(cond)(lambda mk=mk: mk().wait_send())

def ag16(x, cid, cut=P1, space=pl.ANY):
    R, D = x.shape
    DMA = pltpu.SemaphoreType.DMA
    return pl.pallas_call(
        functools.partial(ag_kernel, cut),
        out_shape=jax.ShapeDtypeStruct((4, 4, R, D), x.dtype),
        in_specs=[pl.BlockSpec(memory_space=space)],
        out_specs=pl.BlockSpec(memory_space=space),
        scratch_shapes=[DMA, DMA((64,)), DMA((4,)), DMA((4,)), DMA((4,)), DMA((4,)), DMA((4,)), DMA((4,)), DMA((4,)), DMA((4,))],
        compiler_params=pltpu.CompilerParams(collective_id=cid, has_side_effects=True, vmem_limit_bytes=48 * 2**20),
        name="gather_rows",
    )(x)
F32 = jnp.float32
BF = jnp.bfloat16


class Net:
    def __init__(self, sems):
        self.sems, self.sends = sems, []
        self.u, self.z, self.c = place()
        u, z, c = self.u, self.z, self.c
        self.ux, self.uy, self.ud = u ^ 1, u ^ 2, u ^ 3
        self.xn, self.yn, self.up, self.dn = (u ^ 1, z, c), (u ^ 2, z, c), (u, z + 1, c), (u, z - 1, c)
        self.has_up, self.has_dn = z < 3, z > 0
        self.at = [z == i for i in range(4)]

    def barrier(self, more=()):
        bar = pltpu.get_barrier_semaphore()
        for n in (self.xn, self.yn) + tuple(more):
            pl.semaphore_signal(bar, inc=1, device_id=n, device_id_type=MESH)
        for cond, n in ((self.has_up, self.up), (self.has_dn, self.dn)):
            pl.when(cond)(lambda n=n: pl.semaphore_signal(bar, inc=1, device_id=n, device_id_type=MESH))
        pl.semaphore_wait(bar, 2 + len(more) + self.has_up.astype(jnp.int32) + self.has_dn.astype(jnp.int32))

    def go(self, cond, src, dst, rsem, dev):
        idx = len(self.sends)

        def mk():
            return pltpu.make_async_remote_copy(
                src_ref=src(), dst_ref=dst(), send_sem=self.sems.at[idx], recv_sem=rsem(),
                device_id=dev, device_id_type=MESH)

        self.sends.append((cond, mk))
        if cond is None:
            mk().start()
        else:
            pl.when(cond)(lambda: mk().start())

    def wait(self, cond, ref, sem):
        def w():
            pltpu.make_async_copy(ref(), ref(), sem).wait()

        if cond is None:
            w()
        else:
            pl.when(cond)(w)

    def finish(self):
        for cond, mk in self.sends:
            if cond is None:
                mk().wait_send()
            else:
                pl.when(cond)(lambda mk=mk: mk().wait_send())


def strips(rows, body, step=16):
    def it(i, _):
        body(pl.ds(pl.multiple_of(i * step, step), step))
        return 0

    lax.fori_loop(0, rows // step, it, 0)


def wide(v):
    return v.astype(F32)


class Scatter:
    def __init__(self, net, cut, P, bufs):
        self.net, self.cut, self.P = net, cut, P
        (self.mid1, self.mid2, self.fx, self.fy, self.be, self.ab, self.bbe, self.bab, self.bm,
         self.m1s, self.m2s, self.fxs, self.fys, self.bes, self.abs_, self.bbes, self.babs, self.bms) = bufs
        self.R = P.shape[2]
        self.h = cut // 2
        self.rb = self.R - cut
        self.hb = self.rb // 2

    def first(self, zd):
        net, P, h, cut, rb = self.net, self.P, self.h, self.cut, self.rb
        net.go(None, lambda: P.at[net.ud, zd, pl.ds(0, h), :], lambda: self.mid1.at[zd], lambda: self.m1s.at[zd], net.xn)
        net.go(None, lambda: P.at[net.ud, zd, pl.ds(h, h), :], lambda: self.mid2.at[zd], lambda: self.m2s.at[zd], net.yn)
        if rb and zd > 0:
            net.go(net.at[0], lambda: P.at[:, zd, pl.ds(cut, rb), :], lambda: self.bbe.at[zd], lambda: self.bbes.at[zd], net.up)
        if rb and zd < 3:
            net.go(net.at[3], lambda: P.at[:, zd, pl.ds(cut, rb), :], lambda: self.bab.at[zd], lambda: self.babs.at[zd], net.dn)
        net.go(None, lambda: P.at[net.ux, zd, pl.ds(0, h), :], lambda: self.fx.at[zd, pl.ds(0, h), :], lambda: self.fxs.at[zd, 0], net.xn)
        net.go(None, lambda: P.at[net.uy, zd, pl.ds(h, h), :], lambda: self.fy.at[zd, pl.ds(h, h), :], lambda: self.fys.at[zd, 1], net.yn)

    def mids(self, zd):
        net, P, h, mid1, mid2 = self.net, self.P, self.h, self.mid1, self.mid2

        def add1(sl):
            mid1[zd, sl, :] = (wide(mid1[zd, sl, :]) + wide(P[net.uy, zd, sl, :])).astype(BF)

        def add2(sl):
            mid2[zd, sl, :] = (wide(mid2[zd, sl, :]) + wide(P[net.ux, zd, pl.ds(h + sl.start, 16), :])).astype(BF)

        net.wait(None, lambda: mid1.at[zd], self.m1s.at[zd])
        strips(h, add1)
        net.go(None, lambda: mid1.at[zd], lambda: self.fy.at[zd, pl.ds(0, h), :], lambda: self.fys.at[zd, 0], net.yn)
        net.wait(None, lambda: mid2.at[zd], self.m2s.at[zd])
        strips(h, add2)
        net.go(None, lambda: mid2.at[zd], lambda: self.fx.at[zd, pl.ds(h, h), :], lambda: self.fxs.at[zd, 1], net.xn)

    def route(self, zd, zz):
        if zz < zd:
            return True, self.net.up
        return False, self.net.dn

    def bhop(self, zd, zz):
        net, P, cut, rb = self.net, self.P, self.cut, self.rb
        if not rb:
            return
        upward, dev = self.route(zd, zz)
        buf, sems = (self.bbe, self.bbes) if upward else (self.bab, self.babs)
        here = net.at[zz]
        net.wait(here, lambda: buf.at[zd], sems.at[zd])

        def add():
            for q in range(4):
                def one(sl, q=q):
                    buf[zd, q, sl, :] = (wide(buf[zd, q, sl, :]) + wide(P[q, zd, pl.ds(cut + sl.start, 16), :])).astype(BF)
                strips(rb, one)

        pl.when(here)(add)
        net.go(here, lambda: buf.at[zd], lambda: buf.at[zd], lambda: sems.at[zd], dev)

    def square(self, zd, cond):
        net, h = self.net, self.h
        for half in (0, 1):
            net.wait(cond, lambda: self.fx.at[zd, pl.ds(half * h, h), :], self.fxs.at[zd, half])
            net.wait(cond, lambda: self.fy.at[zd, pl.ds(half * h, h), :], self.fys.at[zd, half])

    def local(self, zd, sl):
        return wide(self.P[self.net.u, zd, sl, :]) + wide(self.fx[zd, sl, :]) + wide(self.fy[zd, sl, :])

    def hop(self, zd, zz):
        net = self.net
        upward, dev = self.route(zd, zz)
        buf, sems = (self.be, self.bes) if upward else (self.ab, self.abs_)
        here = net.at[zz]
        self.square(zd, here)
        if zz in (0, 3):
            def begin(sl):
                self.fx[zd, sl, :] = self.local(zd, sl).astype(BF)

            pl.when(here)(lambda: strips(self.cut, begin))
            net.go(here, lambda: self.fx.at[zd], lambda: buf.at[zd], lambda: sems.at[zd], dev)
        else:
            def plus(sl):
                buf[zd, sl, :] = (self.local(zd, sl) + wide(buf[zd, sl, :])).astype(BF)

            net.wait(here, lambda: buf.at[zd], sems.at[zd])
            pl.when(here)(lambda: strips(self.cut, plus))
            net.go(here, lambda: buf.at[zd], lambda: buf.at[zd], lambda: sems.at[zd], dev)

    def bquad(self):
        net, P, cut, rb, hb, bm, bms = self.net, self.P, self.cut, self.rb, self.hb, self.bm, self.bms
        if not rb:
            return
        z = net.z
        net.wait(net.has_dn, lambda: self.bbe.at[z], self.bbes.at[z])
        net.wait(net.has_up, lambda: self.bab.at[z], self.babs.at[z])
        for q in range(4):
            def fold(sl, q=q):
                s = wide(P[q, z, pl.ds(cut + sl.start, 16), :])
                s = s + jnp.where(net.has_dn, wide(self.bbe[z, q, sl, :]), 0.0)
                s = s + jnp.where(net.has_up, wide(self.bab[z, q, sl, :]), 0.0)
                bm[q, sl, :] = s.astype(BF)
            strips(rb, fold)
        net.go(None, lambda: bm.at[net.ud, pl.ds(0, hb), :], lambda: bm.at[4, pl.ds(0, hb), :], lambda: bms.at[0], net.xn)
        net.go(None, lambda: bm.at[net.ud, pl.ds(hb, hb), :], lambda: bm.at[5, pl.ds(0, hb), :], lambda: bms.at[1], net.yn)
        net.go(None, lambda: bm.at[net.ux, pl.ds(0, hb), :], lambda: bm.at[6, pl.ds(0, hb), :], lambda: bms.at[2], net.xn)
        net.go(None, lambda: bm.at[net.uy, pl.ds(hb, hb), :], lambda: bm.at[7, pl.ds(hb, hb), :], lambda: bms.at[3], net.yn)

    def bquad2(self):
        net, rb, hb, bm, bms = self.net, self.rb, self.hb, self.bm, self.bms
        if not rb:
            return

        def add4(sl):
            bm[4, sl, :] = (wide(bm[4, sl, :]) + wide(bm[net.uy, sl, :])).astype(BF)

        def add5(sl):
            bm[5, sl, :] = (wide(bm[5, sl, :]) + wide(bm[net.ux, pl.ds(hb + sl.start, 16), :])).astype(BF)

        net.wait(None, lambda: bm.at[4, pl.ds(0, hb), :], bms.at[0])
        strips(hb, add4)
        net.go(None, lambda: bm.at[4, pl.ds(0, hb), :], lambda: bm.at[7, pl.ds(0, hb), :], lambda: bms.at[4], net.yn)
        net.wait(None, lambda: bm.at[5, pl.ds(0, hb), :], bms.at[1])
        strips(hb, add5)
        net.go(None, lambda: bm.at[5, pl.ds(0, hb), :], lambda: bm.at[6, pl.ds(hb, hb), :], lambda: bms.at[5], net.xn)

    def last(self, store):
        net, cut, rb, hb, bm, bms = self.net, self.cut, self.rb, self.hb, self.bm, self.bms
        z = net.z
        self.square(z, None)

        def own(sl):
            s = self.local(z, sl)
            s = s + jnp.where(net.has_dn, wide(self.be[z, sl, :]), 0.0)
            s = s + jnp.where(net.has_up, wide(self.ab[z, sl, :]), 0.0)
            store(sl, s)

        net.wait(net.has_dn, lambda: self.be.at[z], self.bes.at[z])
        net.wait(net.has_up, lambda: self.ab.at[z], self.abs_.at[z])
        strips(cut, own)
        if rb:
            net.wait(None, lambda: bm.at[6, pl.ds(0, hb), :], bms.at[2])
            net.wait(None, lambda: bm.at[6, pl.ds(hb, hb), :], bms.at[5])
            net.wait(None, lambda: bm.at[7, pl.ds(0, hb), :], bms.at[4])
            net.wait(None, lambda: bm.at[7, pl.ds(hb, hb), :], bms.at[3])
            strips(rb, lambda sl: store(
                pl.ds(cut + sl.start, 16), wide(bm[net.u, sl, :]) + wide(bm[6, sl, :]) + wide(bm[7, sl, :])))


def rs_scratch(cut, R, D):
    h, rb = cut // 2, R - cut
    V = lambda *s: pltpu.VMEM(s, BF)
    S = pltpu.SemaphoreType.DMA
    return [V(4, h, D), V(4, h, D), V(4, cut, D), V(4, cut, D), V(4, cut, D), V(4, cut, D),
            V(4, 4, max(rb, 16), D), V(4, 4, max(rb, 16), D), V(8, max(rb, 16), D),
            S((4,)), S((4,)), S((4, 2)), S((4, 2)), S((4,)), S((4,)), S((4,)), S((4,)), S((6,))]


def rs_kernel(cut, P, o_ref, ssem, *scr):
    net = Net(ssem)
    net.barrier()
    sc = Scatter(net, cut, P, scr)

    def store(sl, v):
        o_ref[sl, :] = v.astype(o_ref.dtype)

    for zd in (3, 0, 2, 1):
        sc.first(zd)
    for zd in (3, 0, 2, 1):
        sc.mids(zd)
    sc.hop(3, 0); sc.hop(0, 3); sc.bhop(3, 1); sc.bhop(0, 2)
    sc.hop(2, 0); sc.hop(1, 3); sc.bhop(2, 1); sc.bhop(1, 2)
    sc.hop(3, 1); sc.hop(0, 2); sc.bhop(3, 2); sc.bhop(0, 1)
    sc.hop(1, 0); sc.hop(2, 3); sc.bquad()
    sc.hop(2, 1); sc.hop(1, 2)
    sc.hop(3, 2); sc.hop(0, 1); sc.bquad2()
    sc.last(store)
    net.finish()


def rs16(p, cid, cut=96, dtype=F32):
    _, _, R, D = p.shape
    DMA = pltpu.SemaphoreType.DMA
    return pl.pallas_call(
        functools.partial(rs_kernel, cut),
        out_shape=jax.ShapeDtypeStruct((R, D), dtype),
        in_specs=[pl.BlockSpec(memory_space=pltpu.VMEM)],
        out_specs=pl.BlockSpec(memory_space=pltpu.VMEM),
        scratch_shapes=[DMA((96,))] + rs_scratch(cut, R, D),
        compiler_params=pltpu.CompilerParams(collective_id=cid, has_side_effects=True, vmem_limit_bytes=56 * 2**20),
        name="scatter_rows",
    )(p)


class Gather:
    def __init__(self, net, rows, cut, at, plane, sems):
        self.net, self.rows, self.cut, self.ref, self.plane = net, rows, cut, at, plane
        self.zr, self.xr, self.yr, self.d1, self.d2, self.br, self.bz = sems
        self.h, self.rb = cut // 2, rows - cut
        self.hb = self.rb // 2
        z = net.z
        self.near = []
        for s in range(4):
            zl, zh = z - s, z + s
            self.near.append((
                (jnp.maximum(zl, 0), zl >= 0, jnp.logical_and(zl >= 0, net.has_up), net.up),
                (jnp.minimum(zh, 3), zh < 4, jnp.logical_and(zh < 4, net.has_dn), net.dn)))

    def same(self, cond, uu, zz, lo, n, sem, dev):
        ref = lambda: self.ref(uu, zz, lo, n)
        self.net.go(cond, ref, ref, sem, dev)

    def outward(self, zz, cond):
        net, cut = self.net, self.cut
        self.same(cond, net.u, zz, 0, cut, lambda: self.xr.at[zz], net.xn)
        self.same(cond, net.u, zz, 0, cut, lambda: self.yr.at[zz], net.yn)

    def begin(self):
        net, cut, rb, z = self.net, self.cut, self.rb, self.net.z
        self.same(net.has_up, net.u, z, 0, cut, lambda: self.zr.at[z], net.up)
        self.same(net.has_dn, net.u, z, 0, cut, lambda: self.zr.at[z], net.dn)
        if rb:
            self.same(None, net.u, z, cut, rb, lambda: self.br.at[0], net.xn)
            self.same(None, net.u, z, cut, rb, lambda: self.br.at[1], net.yn)
        self.outward(z, None)

    def begin2(self):
        net, cut, rb, hb, z = self.net, self.cut, self.rb, self.hb, self.net.z
        if rb:
            net.wait(None, lambda: self.ref(net.ux, z, cut, rb), self.br.at[0])
            self.same(None, net.ux, z, cut, hb, lambda: self.br.at[2], net.yn)
            net.wait(None, lambda: self.ref(net.uy, z, cut, rb), self.br.at[1])
            self.same(None, net.uy, z, cut + hb, hb, lambda: self.br.at[3], net.xn)

    def along(self, s):
        net = self.net
        for zz, cond, fwd, dev in self.near[s]:
            net.wait(cond, lambda zz=zz: self.ref(net.u, zz, 0, self.cut), self.zr.at[zz])
            self.same(fwd, net.u, zz, 0, self.cut, lambda zz=zz: self.zr.at[zz], dev)
            self.outward(zz, cond)

    def quads(self, s):
        net, cut, rb, hb, z = self.net, self.cut, self.rb, self.hb, self.net.z
        if not rb:
            return
        if s == 0:
            net.wait(None, lambda: self.ref(net.ud, z, cut, hb), self.br.at[2])
            net.wait(None, lambda: self.ref(net.ud, z, cut + hb, hb), self.br.at[3])
            whole = lambda: self.plane(z, cut, rb)
            net.go(net.has_up, whole, whole, lambda: self.bz.at[z], net.up)
            net.go(net.has_dn, whole, whole, lambda: self.bz.at[z], net.dn)
            return
        for zz, cond, fwd, dev in self.near[s]:
            whole = lambda zz=zz: self.plane(zz, cut, rb)
            net.wait(cond, whole, self.bz.at[zz])
            net.go(fwd, whole, whole, lambda zz=zz: self.bz.at[zz], dev)

    def planes(self, s):
        if s == 0:
            return ((self.net.z, None),)
        return tuple((zz, cond) for zz, cond, _f, _d in self.near[s])

    def cross(self, s):
        net, h, cut = self.net, self.h, self.cut
        for zz, cond in self.planes(s):
            net.wait(cond, lambda zz=zz: self.ref(net.ux, zz, 0, cut), self.xr.at[zz])
            self.same(cond, net.ux, zz, 0, h, lambda zz=zz: self.d1.at[zz], net.yn)
            net.wait(cond, lambda zz=zz: self.ref(net.uy, zz, 0, cut), self.yr.at[zz])
            self.same(cond, net.uy, zz, h, h, lambda zz=zz: self.d2.at[zz], net.xn)

    def settle(self, s):
        net, h = self.net, self.h
        for zz, cond in self.planes(s):
            net.wait(cond, lambda zz=zz: self.ref(net.ud, zz, 0, h), self.d1.at[zz])
            net.wait(cond, lambda zz=zz: self.ref(net.ud, zz, h, h), self.d2.at[zz])


def ag_sems():
    S = pltpu.SemaphoreType.DMA
    return [S((4,)) for _ in range(7)]


def greet(net, chips=16):
    bar = pltpu.get_barrier_semaphore()

    def hello(j, _):
        t = lax.rem(net.u * 4 + net.z + j, chips)
        pl.semaphore_signal(bar, inc=1, device_id=(t // 4, lax.rem(t, 4), net.c), device_id_type=MESH)
        return 0

    lax.fori_loop(1, chips, hello, 0)
    pl.semaphore_signal(bar, inc=1, device_id=(net.u, net.z, 1 - net.c), device_id_type=MESH)
    pl.semaphore_wait(bar, chips)


def each_chip(net, body, chips=16):
    def one(j, _):
        t = lax.rem(net.u * 4 + net.z + j, chips)
        body(t, (t // 4, lax.rem(t, 4), net.c))
        return 0

    lax.fori_loop(1, chips, one, 0)


def remote(src, dst, ssem, rsem, dev):
    return pltpu.make_async_remote_copy(
        src_ref=src, dst_ref=dst, send_sem=ssem, recv_sem=rsem, device_id=dev, device_id_type=MESH)


def landed(ref, sem):
    pltpu.make_async_copy(ref, ref, sem).wait()


def row_sums(v):
    return jnp.sum(v.T, axis=0, keepdims=True)


def column(row):
    return jnp.broadcast_to(row, (row.shape[1], row.shape[1])).T


def share_sums(net, sums, sums_all, out, lsem, ssem, rsem):
    me = net.u * 4 + net.z
    own = pltpu.make_async_copy(sums, sums_all.at[me], lsem)
    own.start()
    each_chip(net, lambda t, dev: remote(sums, sums_all.at[me], ssem, rsem, dev).start())
    own.wait()
    part = sums_all.at[pl.ds(0, 15)]
    landed(part, rsem)
    total = sums_all[0]
    for i in range(1, 16):
        total = total + sums_all[i]
    out[...] = total
    landed(part, ssem)


def qkv_kernel(cut, x_ref, cols, gain, n1_o, lin, wf, tot, X, nb, sums, sums_all, lsem, nsem, msem, ssem, *gs):
    net = Net(ssem)
    u, z, c = net.u, net.z, net.c
    me = u * 4 + z
    rows, width = X.shape[2], X.shape[3]
    partner = (u, z, 1 - c)
    own = pltpu.make_async_copy(x_ref, X.at[u, z], lsem.at[0])
    own.start()
    own_w = pltpu.make_async_copy(cols.at[me], wf.at[me, c], lsem.at[1])
    own_w.start()
    greet(net)
    own.wait()
    ga = Gather(net, rows, cut, lambda uu, zz, lo, n: X.at[uu, zz, pl.ds(lo, n), :],
                lambda zz, lo, n: X.at[:, zz, pl.ds(lo, n), :], gs)
    ga.begin()
    each_chip(net, lambda t, dev: remote(cols.at[t], wf.at[me, c], msem.at[0], msem.at[1], dev).start())

    def plane(zz):
        def chunk(uu, _):
            slot = lax.rem(uu, 2)
            k = uu * 4 + zz

            def norm(i, _):
                sl = pl.ds(pl.multiple_of(i * 16, 16), 16)
                v = X[uu, zz, sl, :].astype(F32)
                r = lax.rsqrt(jnp.mean(v * v, axis=1, keepdims=True) + EPS)
                nb[slot, sl, :] = (v * r * gain[...]).astype(BF)
                return 0

            def stored(s):
                return pltpu.make_async_copy(nb.at[s], n1_o.at[k], nsem.at[s])

            pl.when(uu >= 2)(lambda: stored(slot).wait())
            lax.fori_loop(0, rows // 16, norm, 0)
            stored(slot).start()
            got = dot(nb[slot], wf[...].reshape(width, wf.shape[-1]), ((1,), (0,)))
            lin[k] = got
            q, kk = got[:, :128], got[:, 128:256]
            sums[pl.ds(k, 1), :] = row_sums(q * q)
            sums[pl.ds(16 + k, 1), :] = row_sums(kk * kk)
            return 0

        lax.fori_loop(0, 4, chunk, 0)
        for s in (0, 1):
            pltpu.make_async_copy(nb.at[s], n1_o.at[0], nsem.at[s]).wait()

    def compute(s):
        for zz, cond in ga.planes(s):
            if cond is None:
                plane(zz)
            else:
                pl.when(cond)(lambda zz=zz: plane(zz))

    ga.begin2()
    ga.along(1)
    ga.quads(0)
    ga.cross(0)
    own_w.wait()
    landed(wf.at[pl.ds(0, 15), 0], msem.at[1])
    to_partner = remote(wf.at[:, c], wf.at[:, c], msem.at[2], msem.at[3], partner)
    to_partner.start()
    ga.along(2)
    ga.quads(1)
    ga.cross(1)
    ga.settle(0)
    landed(wf.at[:, 1 - c], msem.at[3])
    compute(0)
    ga.along(3)
    ga.quads(2)
    ga.cross(2)
    ga.settle(1)
    compute(1)
    ga.quads(3)
    ga.cross(3)
    ga.settle(2)
    compute(2)
    ga.settle(3)
    compute(3)
    landed(wf.at[pl.ds(0, 15), 0], msem.at[0])
    landed(wf.at[:, c], msem.at[2])
    share_sums(net, sums, sums_all, tot, lsem.at[2], msem.at[4], msem.at[5])
    net.finish()


def run_qkv(x, cols, gain, cid, cut=96):
    R, D = x.shape
    N = cols.shape[2]
    DMA = pltpu.SemaphoreType.DMA
    S = jax.ShapeDtypeStruct
    V = lambda *s: pltpu.VMEM(s, BF)
    A = pl.BlockSpec(memory_space=pl.ANY)
    M = pl.BlockSpec(memory_space=pltpu.VMEM)
    return pl.pallas_call(
        functools.partial(qkv_kernel, cut),
        out_shape=(S((16, R, D), BF), S((16, R, N), F32), S((16, 2, R // 2, N), BF), S((32, 128), F32)),
        in_specs=[A, A, M],
        out_specs=(A, M, M, M),
        scratch_shapes=[V(4, 4, R, D), V(2, R, D), pltpu.VMEM((32, 128), F32), pltpu.VMEM((16, 32, 128), F32),
                        DMA((3,)), DMA((2,)), DMA((6,)), DMA((64,))] + ag_sems(),
        compiler_params=pltpu.CompilerParams(collective_id=cid, has_side_effects=True, vmem_limit_bytes=40 * 2**20),
        name="project",
    )(x, cols, gain)


def group_of(t):
    g = t // 2
    return jnp.where(g == 0, 3, jnp.where(g == 1, 0, jnp.where(g == 2, 2, 1)))


def expert_kernel(cut, n2, cot, share, gate, up, down, d_n2, p_out, n2_o, other, dg_o, du_o, dd_o,
                  X, C, GU, W, A, hid, pb, fs, lsem, wsem, wrs, psem, tsem, osem, ors, fsem, sa, sc_, sr, *scr):
    ga_sems, gc_sems, rs_bufs = scr[:7], scr[7:14], scr[14:]
    na, nc, nr = Net(sa), Net(sc_), Net(sr)
    u, z, c = na.u, na.z, na.c
    partner = (u, z, 1 - c)
    rows, width = X.shape[2], X.shape[3]
    ff = W.shape[0]
    half, half_ff = gate.shape[0], down.shape[0]
    tokens = 16 * rows
    tile = 256
    first = [pltpu.make_async_copy(n2, X.at[u, z], lsem.at[0]), pltpu.make_async_copy(cot, C.at[u, z], lsem.at[1])]

    def weights():
        mine = pl.ds(pl.multiple_of(c * half, half), half)
        mine_ff = pl.ds(pl.multiple_of(c * half_ff, half_ff), half_ff)
        return ((gate, GU.at[mine, pl.ds(0, ff)]), (up, GU.at[mine, pl.ds(ff, ff)]), (down, W.at[mine_ff, :]))

    own_w = [pltpu.make_async_copy(a, b, lsem.at[2 + i]) for i, (a, b) in enumerate(weights())]
    for one in first + own_w:
        one.start()
    na.barrier((partner,))
    first[0].wait()

    def gather(net, buf, sems):
        return Gather(net, rows, cut, lambda uu, zz, lo, n: buf.at[uu, zz, pl.ds(lo, n), :],
                      lambda zz, lo, n: buf.at[:, zz, pl.ds(lo, n), :], sems)

    ga, gc = gather(na, X, ga_sems), gather(nc, C, gc_sems)
    ga.begin()
    sent_w = [remote(a, b, wsem.at[i], wrs.at[i], partner) for i, (a, b) in enumerate(weights())]
    for one in sent_w:
        one.start()

    def forward(zz):
        pltpu.make_async_copy(X.at[:, zz], n2_o.at[:, zz], psem.at[1]).start()

        def part(j, _):
            quads = pl.ds(2 * j, 2)

            def inner(n, _):
                gcols = pl.ds(pl.multiple_of(n * tile, tile), tile)
                ucols = pl.ds(pl.multiple_of(ff + n * tile, tile), tile)
                xv = X[quads, zz].reshape(2 * rows, width)
                g = dot(xv, GU[:, gcols], ((1,), (0,)))
                uu = dot(xv, GU[:, ucols], ((1,), (0,)))
                hid[quads, zz, :, gcols] = (g * jax.nn.sigmoid(g) * uu).astype(BF).reshape(2, rows, tile)
                A[quads, zz, :, gcols] = g.astype(BF).reshape(2, rows, tile)
                A[quads, zz, :, ucols] = uu.astype(BF).reshape(2, rows, tile)
                return 0

            lax.fori_loop(0, ff // tile, inner, 0)
            weight = share[quads, zz]

            def outer(n, _):
                cols = pl.ds(pl.multiple_of(n * tile, tile), tile)
                made = dot(hid[quads, zz].reshape(2 * rows, ff), W[:, cols], ((1,), (0,)))
                made = made.astype(BF).astype(F32).reshape(2, rows, tile)
                pb[:, :, cols] = (weight * made).astype(BF)
                return 0

            lax.fori_loop(0, width // tile, outer, 0)
            out = pltpu.make_async_copy(pb, p_out.at[quads, zz], psem.at[0])
            out.start()
            out.wait()
            return 0

        lax.fori_loop(0, 2, part, 0)

    def planes(s):
        if s == 0:
            forward(z)
            return

        def one(d, _):
            zz = jnp.where(d == 0, z - s, z + s)
            pl.when(jnp.logical_and(zz >= 0, zz < 4))(lambda: forward(zz))
            return 0

        lax.fori_loop(0, 2, one, 0)

    ga.begin2()
    ga.along(1)
    ga.quads(0)
    ga.cross(0)
    ga.along(2)
    ga.quads(1)
    ga.cross(1)
    first[1].wait()
    gc.begin()
    ga.settle(0)
    for one in own_w:
        one.wait()
    for one in sent_w:
        one.wait_recv()
    planes(0)
    gc.begin2()
    ga.along(3)
    ga.quads(2)
    ga.cross(2)
    ga.settle(1)
    gc.along(1)
    gc.quads(0)
    gc.cross(0)
    planes(1)
    ga.quads(3)
    ga.cross(3)
    ga.settle(2)
    gc.along(2)
    gc.quads(1)
    gc.cross(1)
    planes(2)
    ga.settle(3)
    gc.along(3)
    gc.quads(2)
    gc.cross(2)
    planes(3)
    gc.quads(3)
    gc.cross(3)
    for s in range(4):
        gc.settle(s)
    na.finish()
    nc.finish()
    for one in sent_w:
        one.wait_send()
    landed(X, psem.at[1])
    sc = Scatter(nr, cut, X, rs_bufs)

    def backward(t):
        zd, j = group_of(t), lax.rem(t, 2)
        quads = pl.ds(2 * j, 2)

        def scale(i, _):
            sl = pl.ds(pl.multiple_of(i * 16, 16), 16)
            C[quads, zd, sl, :] = (share[quads, zd, sl, :] * C[quads, zd, sl, :].astype(F32)).astype(BF)
            return 0

        lax.fori_loop(0, rows // 16, scale, 0)

        def inner(n, _):
            gcols = pl.ds(pl.multiple_of(n * tile, tile), tile)
            ucols = pl.ds(pl.multiple_of(ff + n * tile, tile), tile)
            dh = dot(C[quads, zd].reshape(2 * rows, width), W[gcols, :], ((1,), (1,)))
            g = wide(A[quads, zd, :, gcols]).reshape(2 * rows, tile)
            uu = wide(A[quads, zd, :, ucols]).reshape(2 * rows, tile)
            s = jax.nn.sigmoid(g)
            A[quads, zd, :, gcols] = (dh * uu * s * (1.0 + g * (1.0 - s))).astype(BF).reshape(2, rows, tile)
            A[quads, zd, :, ucols] = (dh * g * s).astype(BF).reshape(2, rows, tile)
            return 0

        lax.fori_loop(0, ff // tile, inner, 0)

        def outer(n, _):
            cols = pl.ds(pl.multiple_of(n * tile, tile), tile)
            back = dot(A[quads, zd].reshape(2 * rows, 2 * ff), GU[cols, :], ((1,), (1,)))
            X[quads, zd, :, cols] = back.astype(BF).reshape(2, rows, tile)
            return 0

        lax.fori_loop(0, width // tile, outer, 0)

    def acts(steps, t):
        for at, todo in steps.items():
            def act(todo=todo):
                for one in todo:
                    one()
            pl.when(t == at)(act)

    steps = {
        1: [lambda: sc.first(3)],
        2: [lambda: sc.mids(3)],
        3: [lambda: sc.first(0), lambda: sc.bhop(3, 1), lambda: sc.hop(3, 0)],
        4: [lambda: sc.mids(0), lambda: sc.bhop(3, 2), lambda: sc.hop(3, 1)],
        5: [lambda: sc.first(2), lambda: sc.bhop(0, 2), lambda: sc.hop(0, 3), lambda: sc.hop(3, 2)],
        6: [lambda: sc.mids(2), lambda: sc.bhop(0, 1), lambda: sc.hop(0, 2)],
        7: [lambda: sc.first(1), lambda: sc.bhop(2, 1), lambda: sc.hop(0, 1), lambda: sc.hop(2, 0), lambda: sc.hop(2, 3)],
    }

    def turn(t, _):
        backward(t)
        acts(steps, t)
        return 0

    lax.fori_loop(0, 8, turn, 0)

    GU4 = GU.reshape(4, 4, rows, width)
    left = W.at[pl.ds(0, tile), :]

    def tile_load(k, which):
        slot = lax.rem(k, 2)
        cols = pl.ds(pl.multiple_of((which * 4 + k) * tile, tile), tile)
        return pltpu.make_async_copy(
            n2_o.at[:, :, :, cols], GU4.at[:, :, :, pl.ds(pl.multiple_of(slot * tile, tile), tile)], tsem.at[slot])

    def left_tokens(k):
        cols = pl.ds(pl.multiple_of(lax.rem(k, 2) * tile, tile), tile)

        def one(b, _):
            sl = pl.ds(pl.multiple_of(b * tile, tile), tile)
            left[:, sl] = GU[sl, cols].T
            return 0

        lax.fori_loop(0, tokens // tile, one, 0)

    def left_hidden(k, which):
        cols = pl.ds(pl.multiple_of((which * 2 + k) * tile, tile), tile)
        flat = hid.reshape(tokens, ff)

        def one(b, _):
            sl = pl.ds(pl.multiple_of(b * tile, tile), tile)
            left[:, sl] = flat[sl, cols].T
            return 0

        lax.fori_loop(0, tokens // tile, one, 0)

    def products(right, store):
        flat = right.reshape(tokens, width)

        def one(n, _):
            cols = pl.ds(pl.multiple_of(n * 512, 512), 512)
            store(cols, n, dot(left[...], flat[:, cols], ((1,), (0,))))
            return 0

        lax.fori_loop(0, width // 512, one, 0)

    def sent(k):
        slot = W.at[pl.ds(pl.multiple_of(tile + lax.rem(k, 2) * tile, tile), tile), :]
        return slot, remote(slot, other.at[k], osem.at[k], ors.at[k], partner)

    tile_load(0, 1 - c).start()

    def other_tile(k, _):
        slot, copy = sent(k)

        @pl.when(k >= 2)
        def _():
            sent(k - 2)[1].wait_send()

        def store(cols, n, v):
            slot[:, cols] = v.astype(BF)

        @pl.when(k < 4)
        def _():
            pl.when(k < 3)(lambda: tile_load(k + 1, 1 - c).start())
            tile_load(k, 1 - c).wait()
            left_tokens(k)
            products(A, store)

        @pl.when(k >= 4)
        def _():
            left_hidden(k - 4, 1 - c)
            products(C, store)

        copy.start()
        acts({0: [lambda: sc.mids(1)],
              1: [lambda: sc.hop(2, 1), lambda: sc.bhop(1, 2)],
              2: [lambda: sc.hop(1, 0), lambda: sc.hop(1, 3)],
              3: [sc.bquad],
              4: [lambda: sc.hop(1, 2)],
              5: [sc.bquad2]}, k)
        return 0

    lax.fori_loop(0, 6, other_tile, 0)

    def store_out(sl, v):
        d_n2[sl, :] = v

    tile_load(0, c).start()
    got = W.at[pl.ds(3 * tile, tile), :]

    def flush(k, h):
        i = pl.ds(pl.multiple_of(lax.rem(k, 4) * tile, tile), tile)

        def go(dst):
            pltpu.make_async_copy(fs.at[h], dst, fsem.at[h]).start()

        pl.when(k < 4)(lambda: go((dg_o, du_o)[h].at[i, :]))
        pl.when(k >= 4)(lambda: go(dd_o.at[i, pl.ds(h * 1024, 1024)]))

    def own_tile(k, _):
        fetch = pltpu.make_async_copy(other.at[k], got, lsem.at[0])
        landed(other.at[k], ors.at[k])
        fetch.start()

        def finish(right):
            flat = right.reshape(tokens, width)
            fetch.wait()
            for h in (0, 1):
                pl.when(k > 0)(lambda: landed(fs.at[h], fsem.at[h]))
                for n in (0, 1):
                    cols = pl.ds(h * 1024 + n * 512, 512)
                    fs[h, :, n * 512 : (n + 1) * 512] = dot(left[...], flat[:, cols], ((1,), (0,))) + wide(got[:, cols])
                flush(k, h)

        @pl.when(k < 4)
        def _():
            pl.when(k < 3)(lambda: tile_load(k + 1, c).start())
            tile_load(k, c).wait()
            left_tokens(k)
            finish(A)

        @pl.when(k >= 4)
        def _():
            left_hidden(k - 4, c)
            finish(C)

        acts({0: [lambda: sc.last(store_out)]}, k)
        return 0

    lax.fori_loop(0, 6, own_tile, 0)
    for h in (0, 1):
        landed(fs.at[h], fsem.at[h])
    for k in (4, 5):
        sent(k)[1].wait_send()
    nr.finish()


def run_expert(n2, cot, share, gate, up, down, cid, cut=96):
    R, D = n2.shape
    half, ff = gate.shape
    DMA = pltpu.SemaphoreType.DMA
    S = jax.ShapeDtypeStruct
    V = lambda *s: pltpu.VMEM(s, BF)
    A = pl.BlockSpec(memory_space=pl.ANY)
    M = pl.BlockSpec(memory_space=pltpu.VMEM)
    return pl.pallas_call(
        functools.partial(expert_kernel, cut),
        out_shape=(S((R, D), F32), S((4, 4, R, D), BF), S((4, 4, R, D), BF), S((6, 256, D), BF),
                   S((half, ff), F32), S((half, ff), F32), S(down.shape, F32)),
        in_specs=[A, A, M, A, A, A],
        out_specs=(M,) + (A,) * 6,
        scratch_shapes=[V(4, 4, R, D), V(4, 4, R, D), V(D, 2 * ff), V(ff, D), V(4, 4, R, 2 * ff), V(4, 4, R, ff),
                        V(2, R, D), pltpu.VMEM((2, 256, 1024), F32),
                        DMA((5,)), DMA((3,)), DMA((3,)), DMA((2,)), DMA((2,)), DMA((6,)), DMA((6,)), DMA((2,)),
                        DMA((64,)), DMA((64,)), DMA((96,))] + ag_sems() + ag_sems() + rs_scratch(cut, R, D),
        compiler_params=pltpu.CompilerParams(collective_id=cid, has_side_effects=True, vmem_limit_bytes=63 * 2**20),
        name="expert",
    )(n2, cot, share, gate, up, down)

def band_scores(q, k, q_seg, k_seg, scale, reach):
    scores = dot(q, k, ((1,), (1,))) * scale
    q_at = lax.broadcasted_iota(jnp.int32, scores.shape, 0)
    k_at = lax.broadcasted_iota(jnp.int32, scores.shape, 1)
    return scores, (k_seg == q_seg) & (k_at <= q_at + reach)


def turned(v, cosine, sine):
    return v * cosine + pltpu.roll(v, 64, axis=1) * sine


def turned_back(v, cosine, sine):
    return v * cosine - pltpu.roll(v, 64, axis=1) * sine


def attend_kernel(scale, pads, lin, tot, cosine, sine, gq, gk, q_seg, k_seg, w_own, x_in, gain, wo_o, q_rot, kv, o_ref, lse,
                  att, residual, n2, wo, lsem, msem, ssem, *gs):
    net = Net(ssem)
    u, z, c = net.u, net.z, net.c
    me = u * 4 + z
    rows = x_in.shape[0]
    width = x_in.shape[1]
    reach = pads * 2 * rows
    partner = (u, z, 1 - c)
    own = pltpu.make_async_copy(w_own, wo.at[u, z, c], lsem.at[0])
    own.start()
    greet(net)
    own.wait()
    ga = Gather(net, rows // 2, rows // 2, lambda uu, zz, lo, n: wo.at[uu, zz, c, pl.ds(lo, n), :], None, gs)
    ga.begin()
    for i in range(pads):
        kv[:, i] = jnp.zeros(kv.shape[:1] + kv.shape[2:], BF)

    def ready(i, _):
        both = lin[i]
        rq = lax.rsqrt(column(tot[pl.ds(i, 1), :]) / width + EPS)
        rk = lax.rsqrt(column(tot[pl.ds(16 + i, 1), :]) / width + EPS)
        cs, sn = cosine[i], sine[i]
        q_rot[i] = turned(both[:, :128] * rq * gq[...], cs, sn).astype(BF)
        kv[0, pads + i, c] = turned(both[:, 128:256] * rk * gk[...], cs, sn).astype(BF)
        kv[1, pads + i, c] = both[:, 256:].astype(BF)
        return 0

    lax.fori_loop(0, 16, ready, 0)
    mine = kv.at[:, pl.ds(pads, 16), c]
    to_partner = remote(mine, mine, msem.at[0], msem.at[1], partner)
    to_partner.start()
    ga.along(1)
    ga.cross(0)
    landed(kv.at[:, pl.ds(pads, 16), 1 - c], msem.at[1])

    def block(j, _):
        i = lax.rem(me + 1 + j, 16)
        first = 2 * i + c
        band = pl.ds(pl.multiple_of(first * rows, rows), rows + reach)
        kf, vf = kv.at[0].reshape((pads + 16) * 2 * rows, 128), kv.at[1].reshape((pads + 16) * 2 * rows, 128)
        scores, allowed = band_scores(q_rot[i], kf[band, :], q_seg[i], k_seg[:, band], scale, reach)
        scores = jnp.where(allowed, scores, NEG)
        top = jnp.max(scores, axis=1, keepdims=True)
        weights = jnp.where(allowed, jnp.exp(scores - top), 0.0)
        total = jnp.sum(weights, axis=1, keepdims=True)
        probs = (weights / total).astype(BF)
        o_ref[i] = dot(probs, vf[band, :], ((1,), (0,))).astype(BF)
        lse[i] = top + jnp.log(total)

        @pl.when(j < 15)
        def _():
            remote(o_ref.at[i], att.at[me], msem.at[2], msem.at[3], (i // 4, lax.rem(i, 4), c)).start()

        return 0

    lax.fori_loop(0, 5, block, 0)
    ga.along(2)
    ga.cross(1)
    lax.fori_loop(5, 10, block, 0)
    ga.along(3)
    ga.cross(2)
    lax.fori_loop(10, 16, block, 0)
    ga.cross(3)
    for s in range(4):
        ga.settle(s)
    rest = remote(wo.at[:, :, c], wo.at[:, :, c], msem.at[4], msem.at[5], partner)
    rest.start()
    att[me] = o_ref[me]
    part = att.at[pl.ds(0, 15)]
    landed(part, msem.at[3])
    landed(wo.at[:, :, 1 - c], msem.at[5])
    keep = pltpu.make_async_copy(wo, wo_o, lsem.at[1])
    keep.start()
    tile = 256

    def out(n, _):
        cols = pl.ds(pl.multiple_of(n * tile, tile), tile)
        acc = x_in[:, cols].astype(F32)
        for e in range(0, 16, 2):
            pair = jnp.concatenate([att[e], att[e + 1]], axis=1)
            acc = acc + dot(pair, wo[e // 4, pl.ds(e % 4, 2), :, :, cols].reshape(256, tile), ((1,), (0,)))
        residual[:, cols] = acc
        return 0

    lax.fori_loop(0, width // tile, out, 0)

    def norm(i, _):
        sl = pl.ds(pl.multiple_of(i * 16, 16), 16)
        v = residual[sl, :]
        r = lax.rsqrt(jnp.mean(v * v, axis=1, keepdims=True) + EPS)
        n2[sl, :] = (v * r * gain[...]).astype(BF)
        return 0

    lax.fori_loop(0, rows // 16, norm, 0)
    landed(mine, msem.at[0])
    landed(part, msem.at[2])
    landed(wo.at[:, :, c], msem.at[4])
    keep.wait()
    net.finish()


def run_attend(scale, pads, lin, tot, cosine, sine, gq, gk, q_seg, k_seg, w_own, x_in, gain, cid):
    R, D = x_in.shape
    DMA = pltpu.SemaphoreType.DMA
    S = jax.ShapeDtypeStruct
    A = pl.BlockSpec(memory_space=pl.ANY)
    M = pl.BlockSpec(memory_space=pltpu.VMEM)
    wo = (4, 4, 2, R // 2, D)
    return pl.pallas_call(
        functools.partial(attend_kernel, scale, pads),
        out_shape=(S(wo, BF), S((16, R, 128), BF), S((2, pads + 16, 2, R, 128), BF), S((16, R, 128), BF),
                   S((16, R, 1), F32), S((16, R, 128), BF), S((R, D), F32), S((R, D), BF)),
        in_specs=[M] * 8 + [A, M, M],
        out_specs=(A,) + (M,) * 7,
        scratch_shapes=[pltpu.VMEM(wo, BF), DMA((2,)), DMA((6,)), DMA((64,))] + ag_sems(),
        compiler_params=pltpu.CompilerParams(collective_id=cid, has_side_effects=True, vmem_limit_bytes=48 * 2**20),
        name="attend",
    )(lin, tot, cosine, sine, gq, gk, q_seg, k_seg, w_own, x_in, gain)


def attend_back_kernel(scale, pads, d_res, wo_h, q_rot, kv, q_seg, k_seg, lse, o_ref, lin, tot, cosine, sine, gq, gk,
                       d_lin, d_gains, wo, d_mine, d_out, d_q, d_k, d_v, other, got, d_un, sums, sums_all, inner,
                       lsem, msem, ssem):
    net = Net(ssem)
    u, z, c = net.u, net.z, net.c
    me = u * 4 + z
    rows, width = d_res.shape
    reach = pads * 2 * rows
    partner = (u, z, 1 - c)
    load = pltpu.make_async_copy(wo_h, wo, lsem.at[0])
    load.start()
    greet(net)
    load.wait()

    def send(j, _):
        e = lax.rem(me + 1 + j, 16)
        piece = dot(d_res[...], wo[e // 4, lax.rem(e, 4)].reshape(128, width), ((1,), (1,))).astype(BF)

        @pl.when(j < 15)
        def _():
            d_mine[e] = piece
            remote(d_mine.at[e], d_out.at[me], msem.at[0], msem.at[1], (e // 4, lax.rem(e, 4), c)).start()

        @pl.when(j == 15)
        def _():
            d_out[me] = piece

        return 0

    lax.fori_loop(0, 16, send, 0)
    d_k[...] = jnp.zeros_like(d_k)
    d_v[...] = jnp.zeros_like(d_v)
    landed(d_out.at[pl.ds(0, 15)], msem.at[1])
    count = (pads + 16) * 2 * rows

    def block(i, _):
        band = pl.ds(pl.multiple_of((2 * i + c) * rows, rows), rows + reach)
        kf, vf = kv.at[0].reshape(count, 128), kv.at[1].reshape(count, 128)
        q, k, dd = q_rot[i], kf[band, :], d_out[i]
        scores, allowed = band_scores(q, k, q_seg[i], k_seg[:, band], scale, reach)
        probs = jnp.where(allowed, jnp.exp(scores - lse[i]), 0.0)
        d_probs = dot(dd, vf[band, :], ((1,), (1,)))
        delta = jnp.sum(dd.astype(F32) * o_ref[i].astype(F32), axis=1, keepdims=True)
        d_scores = (probs * (d_probs - delta)).astype(BF)
        d_q[i] = (dot(d_scores, k, ((1,), (0,))) * scale).astype(BF)
        d_k[band, :] += dot(d_scores, q, ((0,), (0,))) * scale
        d_v[band, :] += dot(probs.astype(BF), dd, ((0,), (0,)))
        return 0

    lax.fori_loop(0, 16, block, 0)

    def pack(i, _):
        at = pl.ds(pl.multiple_of(((pads + i) * 2 + 1 - c) * rows, rows), rows)
        other[0, i] = d_k[at, :].astype(BF)
        other[1, i] = d_v[at, :].astype(BF)
        return 0

    lax.fori_loop(0, 16, pack, 0)
    remote(other, got, msem.at[2], msem.at[3], partner).start()
    landed(got, msem.at[3])
    d_gains[...] = jnp.zeros_like(d_gains)

    def undo(i, _):
        at = pl.ds(pl.multiple_of(((pads + i) * 2 + c) * rows, rows), rows)
        cs, sn = cosine[i], sine[i]
        both = lin[i]
        rq = lax.rsqrt(column(tot[pl.ds(i, 1), :]) / width + EPS)
        rk = lax.rsqrt(column(tot[pl.ds(16 + i, 1), :]) / width + EPS)
        dk = (d_k[at, :] + wide(got[0, i])).astype(BF).astype(F32)
        d_lin[i, :, 256:] = (d_v[at, :] + wide(got[1, i])).astype(BF)
        uq = turned_back(wide(d_q[i]), cs, sn)
        uk = turned_back(dk, cs, sn)
        q, k = both[:, :128], both[:, 128:256]
        d_gains[0:1, :] += jnp.sum(uq * q * rq, axis=0, keepdims=True)
        d_gains[1:2, :] += jnp.sum(uk * k * rk, axis=0, keepdims=True)
        uq, uk = uq * gq[...], uk * gk[...]
        d_un[0, i] = uq
        d_un[1, i] = uk
        sums[pl.ds(i, 1), :] = row_sums(uq * q)
        sums[pl.ds(16 + i, 1), :] = row_sums(uk * k)
        return 0

    lax.fori_loop(0, 16, undo, 0)
    share_sums(net, sums, sums_all, inner, lsem.at[1], msem.at[4], msem.at[5])

    def finish(i, _):
        both = lin[i]
        for s in (0, 1):
            r = lax.rsqrt(column(tot[pl.ds(16 * s + i, 1), :]) / width + EPS)
            mean = column(inner[pl.ds(16 * s + i, 1), :]) / width
            own = both[:, 128 * s : 128 * (s + 1)]
            d_lin[i, :, 128 * s : 128 * (s + 1)] = (r * d_un[s, i] - own * (r * r * r * mean)).astype(BF)
        return 0

    lax.fori_loop(0, 16, finish, 0)
    landed(d_out.at[pl.ds(0, 15)], msem.at[0])
    landed(other, msem.at[2])


def run_attend_back(scale, pads, d_res, wo, q_rot, kv, q_seg, k_seg, lse, o, lin, tot, cosine, sine, gq, gk, cid):
    R, D = d_res.shape
    DMA = pltpu.SemaphoreType.DMA
    S = jax.ShapeDtypeStruct
    A = pl.BlockSpec(memory_space=pl.ANY)
    M = pl.BlockSpec(memory_space=pltpu.VMEM)
    V = pltpu.VMEM
    span = (pads + 16) * 2 * R
    return pl.pallas_call(
        functools.partial(attend_back_kernel, scale, pads),
        out_shape=(S((16, R, 384), BF), S((8, 128), F32)),
        in_specs=[M, A] + [M] * 12,
        out_specs=(M, M),
        scratch_shapes=[V(wo.shape, BF), V((16, R, 128), BF), V((16, R, 128), BF), V((16, R, 128), BF),
                        V((span, 128), F32), V((span, 128), F32), V((2, 16, R, 128), BF), V((2, 16, R, 128), BF),
                        V((2, 16, R, 128), F32), V((32, 128), F32), V((16, 32, 128), F32), V((32, 128), F32),
                        DMA((2,)), DMA((6,)), DMA((4,))],
        compiler_params=pltpu.CompilerParams(collective_id=cid, has_side_effects=True, vmem_limit_bytes=48 * 2**20),
        name="attend_back",
    )(d_res, wo, q_rot, kv, q_seg, k_seg, lse, o, lin, tot, cosine, sine, gq, gk)
def swap_kernel(src, out, lsem, ssem, rsem):
    u, z, c = place()
    me = u * 8 + z * 2 + c
    count = out.shape[0]
    bar = pltpu.get_barrier_semaphore()

    def at(j):
        t = lax.rem(me + j, count)
        return t // 8, lax.rem(t, 8) // 2, lax.rem(t, 2), t // 2

    def hello(j, _):
        tu, tz, tc, _e = at(j)
        pl.semaphore_signal(bar, inc=1, device_id=(tu, tz, tc), device_id_type=MESH)
        return 0

    lax.fori_loop(1, count, hello, 0)
    pl.semaphore_wait(bar, count - 1)

    def copy(j):
        tu, tz, tc, e = at(j)
        return pltpu.make_async_remote_copy(
            src_ref=src.at[e], dst_ref=out.at[me], send_sem=ssem, recv_sem=rsem,
            device_id=(tu, tz, tc), device_id_type=MESH)

    own = pltpu.make_async_copy(src.at[me // 2], out.at[me], lsem)
    own.start()

    def send(j, _):
        copy(j).start()
        return 0

    lax.fori_loop(1, count, send, 0)
    own.wait()
    part = out.at[pl.ds(0, count - 1)]
    pltpu.make_async_copy(part, part, rsem).wait()
    pltpu.make_async_copy(part, part, ssem).wait()


def swap(block, cid):
    chips, r, lanes = block.shape
    S = pltpu.SemaphoreType.DMA
    return pl.pallas_call(
        swap_kernel,
        out_shape=jax.ShapeDtypeStruct((2 * chips, r, lanes), block.dtype),
        in_specs=[pl.BlockSpec(memory_space=pltpu.VMEM)],
        out_specs=pl.BlockSpec(memory_space=pltpu.VMEM),
        scratch_shapes=[S, S, S],
        compiler_params=pltpu.CompilerParams(collective_id=cid, has_side_effects=True),
        name="swap_rows",
    )(block)


def spread_kernel(src, out, lsem, ssem, rsem):
    u, z, c = place()
    me = u * 4 + z
    count = out.shape[0]
    bar = pltpu.get_barrier_semaphore()

    def at(j):
        t = lax.rem(me + j, count)
        return t // 4, lax.rem(t, 4), c

    def hello(j, _):
        pl.semaphore_signal(bar, inc=1, device_id=at(j), device_id_type=MESH)
        return 0

    lax.fori_loop(1, count, hello, 0)
    pl.semaphore_wait(bar, count - 1)
    own = pltpu.make_async_copy(src, out.at[me], lsem)
    own.start()

    def send(j, _):
        pltpu.make_async_remote_copy(
            src_ref=src, dst_ref=out.at[me], send_sem=ssem, recv_sem=rsem,
            device_id=at(j), device_id_type=MESH).start()
        return 0

    lax.fori_loop(1, count, send, 0)
    own.wait()
    part = out.at[pl.ds(0, count - 1)]
    pltpu.make_async_copy(part, part, rsem).wait()
    pltpu.make_async_copy(part, part, ssem).wait()


def spread(block, cid):
    S = pltpu.SemaphoreType.DMA
    return pl.pallas_call(
        spread_kernel,
        out_shape=jax.ShapeDtypeStruct((16,) + block.shape, block.dtype),
        in_specs=[pl.BlockSpec(memory_space=pltpu.VMEM)],
        out_specs=pl.BlockSpec(memory_space=pltpu.VMEM),
        scratch_shapes=[S, S, S],
        compiler_params=pltpu.CompilerParams(collective_id=cid, has_side_effects=True),
        name="spread_rows",
    )(block)


def core_pair(value):
    return lax.ppermute(value, "core", [(0, 1), (1, 0)])


def dot(a, b, dims):
    return lax.dot_general(a, b, (dims, ((), ())), preferred_element_type=jnp.float32)


def local_chip(
    inputs, cotangent, segments, expert_ids, gate_weights, fill_order, norm1_gain, w_query, w_key,
    w_value, w_output, query_gain, key_gain, norm2_gain, expert_gate, expert_up, expert_down,
):
    chips = 16
    devices = 2 * chips
    rows, width = inputs.shape
    u, z, core = place()
    chip = u * 4 + z
    device = chip * 2 + core
    topk = expert_ids.shape[1]
    experts_n = chips
    capacity = 9 * rows * devices * topk // (8 * experts_n)
    one_hot = expert_ids[:, :, None] == jnp.arange(experts_n, dtype=jnp.int32)[None, None, :]
    chosen = jnp.any(one_hot, axis=1)
    weight = jnp.sum(jnp.where(one_hot, gate_weights[:, :, None], 0.0), axis=1)
    earlier = (fill_order[None, :] < fill_order[:, None]).astype(jnp.bfloat16)
    rank = dot(earlier, chosen.astype(jnp.bfloat16), ((1,), (0,)))
    rank = jnp.where(chosen, rank, -1.0)
    gains = jnp.concatenate([norm1_gain, query_gain, key_gain, norm2_gain]).astype(F32)
    gains = jnp.broadcast_to(gains.reshape(1, 2, 128), (chips, 2, 128))
    block = jnp.concatenate(
        [weight.T[:, None, :], rank.T[:, None, :], gains, jnp.zeros((chips, 4, 128), F32)], axis=1)
    swapped = swap(block, 1)
    gains = swapped[:, 2:4, :].reshape(devices, 4, 64).transpose(1, 0, 2).reshape(4, width)
    gain_one, gain_q, gain_k, gain_two = gains[0], gains[1], gains[2], gains[3]
    rank_all = swapped[:, 1, :]
    taken = rank_all >= 0.0
    counts = jnp.sum(taken.astype(F32), axis=1)
    before = jnp.cumsum(counts) - counts
    kept = taken & (before[:, None] + rank_all < float(capacity))
    share = jnp.where(kept, swapped[:, 0, :], 0.0).reshape(chips, 2, rows)
    share = lax.dynamic_index_in_dim(share, core, 1, keepdims=False).reshape(chips * rows, 1)


    layer_in = inputs.astype(F32)
    mine = ("ulysses", "z")

    def in_order(own, other):
        return jnp.where(core == 0, own, other), jnp.where(core == 0, other, own)

    cols = jnp.stack([w_query, w_key, w_value]).reshape(3, 64, chips, HEAD_DIM)
    cols = cols.transpose(2, 1, 0, 3).reshape(chips, 64, 3 * HEAD_DIM)
    def my_head(gain):
        return lax.dynamic_slice_in_dim(gain, chip * HEAD_DIM, HEAD_DIM, 0)

    n1_rows, lin, w_qkv, squares = run_qkv(inputs, cols, gain_one.reshape(1, width), 2)
    n1_rows, w_qkv = n1_rows.reshape(chips * rows, width), w_qkv.reshape(width, 3 * HEAD_DIM)
    positions = (jnp.arange(chips, dtype=jnp.int32)[:, None] * 2 + core) * rows + jnp.arange(rows, dtype=jnp.int32)
    half_dim = HEAD_DIM // 2
    inv_freq = jnp.exp(jnp.arange(half_dim, dtype=F32) * (-2.0 * math.log(ROPE_BASE) / HEAD_DIM))
    angles = positions.reshape(-1).astype(F32)[:, None] * inv_freq[None, :]
    cosine, sine = jnp.cos(angles), jnp.sin(angles)
    cosine = jnp.concatenate([cosine, cosine], axis=1).reshape(chips, rows, HEAD_DIM)
    sine = jnp.concatenate([-sine, sine], axis=1).reshape(chips, rows, HEAD_DIM)
    gq, gk = my_head(gain_q).reshape(1, HEAD_DIM), my_head(gain_k).reshape(1, HEAD_DIM)
    pads = chips // 4
    k_seg = jnp.concatenate([jnp.full((pads * 2 * rows,), -1, jnp.int32), segments]).reshape(1, -1)
    q_seg = lax.dynamic_index_in_dim(segments.reshape(chips, 2, rows, 1), core, 1, keepdims=False)
    scale = 1.0 / math.sqrt(HEAD_DIM)
    tokens = chips * rows
    w_o, q_rot, kv, head_out, log_total, attended, residual, normed_two = run_attend(
        scale, pads, lin, squares, cosine, sine, gq, gk, q_seg, k_seg, w_output, inputs, gain_two.reshape(1, width), 4)
    r2 = lax.rsqrt(jnp.mean(residual * residual, axis=1, keepdims=True) + EPS)

    def to_blocks(part):
        return part.astype(BF).reshape(4, 4, rows, part.shape[-1])

    d_normed_two, mixed, _n2, _other, d_expert_gate, d_expert_up, d_expert_down = run_expert(
        normed_two, cotangent, share.reshape(4, 4, rows, 1), expert_gate, expert_up, expert_down, 6)
    output = residual + rs16(mixed, 5)

    def norm_back(d_out, values, r, gain):
        d_scaled = d_out * gain
        inner = jnp.mean(d_scaled * values, axis=1, keepdims=True)
        d_gain = jnp.sum(d_out * values * r, axis=0)
        return r * d_scaled - values * (r * r * r * inner), d_gain

    d_resid_norm, d_gain_two = norm_back(d_normed_two, residual, r2, gain_two)
    d_residual = cotangent.astype(F32) + d_resid_norm
    d_res_low = d_residual.astype(BF)
    d_lin, d_qk_gains = run_attend_back(
        scale, pads, d_res_low, w_o, q_rot, kv, q_seg, k_seg, log_total, head_out, lin, squares, cosine, sine, gq, gk, 7)
    d_lin = d_lin.reshape(tokens, 3 * HEAD_DIM)
    d_qk_gains = d_qk_gains[:2] + core_pair(d_qk_gains[:2])
    d_wo = dot(attended.transpose(0, 2, 1).reshape(width, rows), d_res_low, ((1,), (0,)))
    d_wo = d_wo.reshape(4, 4, HEAD_DIM, 2, width // 2)
    d_wo_own = lax.dynamic_index_in_dim(d_wo, core, 3, keepdims=False)
    d_wo_other = lax.dynamic_index_in_dim(d_wo, 1 - core, 3, keepdims=False)
    d_wo = rs16((d_wo_own + core_pair(d_wo_other.astype(BF)).astype(F32)).astype(BF), 8, dtype=BF)
    d_wo = d_wo.reshape(2, 64, width // 2)
    d_wo_mine = lax.dynamic_index_in_dim(d_wo, core, 0, keepdims=False)
    d_wo_other = core_pair(lax.dynamic_index_in_dim(d_wo, 1 - core, 0, keepdims=False))
    d_w_output = jnp.concatenate(in_order(d_wo_mine, d_wo_other), axis=1).astype(F32)
    d_normed_one = rs16(to_blocks(dot(d_lin, w_qkv, ((1,), (1,)))), 9)
    d_cols = dot(n1_rows, d_lin, ((0,), (0,))).reshape(chips, 2, 64, 3 * HEAD_DIM)
    d_cols_own = lax.dynamic_index_in_dim(d_cols, core, 1, keepdims=False)
    d_cols_other = lax.dynamic_index_in_dim(d_cols, 1 - core, 1, keepdims=False)
    d_cols = (d_cols_own + core_pair(d_cols_other.astype(BF)).astype(F32)).astype(BF)
    d_cols = lax.all_to_all(d_cols, mine, split_axis=0, concat_axis=0, tiled=True)
    d_cols = d_cols.reshape(chips, 64, 3, HEAD_DIM).transpose(2, 1, 0, 3).reshape(3, 64, width).astype(F32)
    r1 = lax.rsqrt(jnp.mean(layer_in * layer_in, axis=1, keepdims=True) + EPS)
    d_layer_in, d_gain_one = norm_back(d_normed_one, layer_in, r1, gain_one)
    d_inputs = d_residual + d_layer_in
    block = jnp.concatenate(
        [d_gain_one.reshape(chips, 1, 128), d_gain_two.reshape(chips, 1, 128), jnp.zeros((chips, 6, 128), F32)], axis=1)
    d_gains = jnp.sum(swap(block, 10)[:, :2, :], axis=0)

    def my_half(row):
        return lax.dynamic_slice_in_dim(row, core * 64, 64, 0)

    return (
        output,
        d_inputs,
        my_half(d_gains[0]),
        d_cols[0],
        d_cols[1],
        d_cols[2],
        d_w_output,
        my_half(d_qk_gains[0]),
        my_half(d_qk_gains[1]),
        my_half(d_gains[1]),
        d_expert_gate,
        d_expert_up,
        d_expert_down,
    )
def whole(mesh, step, rows):
    return jax.shard_map(
        step,
        mesh=mesh,
        in_specs=(
            P(rows, None),
            P(rows, None),
            P(),
            P(rows, None),
            P(rows, None),
            P(rows),
            P(rows),
            P(rows, None),
            P(rows, None),
            P(rows, None),
            P(rows, None),
            P(rows),
            P(rows),
            P(rows),
            P(rows, None),
            P(rows, None),
            P(rows, None),
        ),
        out_specs=(
            P(rows, None),
            P(rows, None),
            P(rows),
            P(rows, None),
            P(rows, None),
            P(rows, None),
            P(rows, None),
            P(rows),
            P(rows),
            P(rows),
            P(rows, None),
            P(rows, None),
            P(rows, None),
        ),
        check_vma=False,
    )


def solution(mesh):
    groups, blk_size = mesh.shape["ulysses"], mesh.shape["blk"]

    def step(*args):
        if groups != 4 or blk_size != 8 or args[7].shape[1] // HEAD_DIM != groups * blk_size // 2:
            return whole(mesh, local, ("ulysses", "blk"))(*args)
        chips = Mesh(mesh.devices.reshape(groups, blk_size // 2, 2), ("ulysses", "z", "core"))
        return whole(chips, local_chip, ("ulysses", "z", "core"))(*args)

    return step
```

```python
import functools
import math

import jax
import jax.numpy as jnp
from jax import lax
from jax.experimental import pallas as pl
from jax.experimental.pallas import tpu as pltpu
from jax.sharding import Mesh
from jax.sharding import PartitionSpec as P

HEAD_DIM = 128


EPS = 1e-05
ROPE_BASE = 10000.0
NEG = -1e30


def as_sent(value):

    def short(part):
        return part.astype(jnp.bfloat16) if part.dtype == jnp.float32 else part

    return jax.tree.map(short, value)


def passed_along(block, axis, distance):
    devices = range(lax.axis_size(axis))
    route = [((i - distance) % len(devices), i) for i in devices]
    return lax.ppermute(block, axis, route)


def prefix(value, axis, join, neutral):
    count, mine = (lax.axis_size(axis), lax.axis_index(axis))
    pieces = lax.all_gather(value, axis)
    subtotal = jnp.full_like(value, 0) + jnp.asarray(neutral, value.dtype)

    def hop(position, subtotal):
        longer = join(subtotal, pieces[position])
        return jnp.where(position < mine, longer, subtotal)

    return lax.fori_loop(0, count - 1, hop, subtotal)


def partner_2(block, axis, bit):
    count = lax.axis_size(axis)
    route = []
    for low in range(count):
        high = low | 1 << bit
        if high != low and high < count:
            route += [(low, high), (high, low)]
    return lax.ppermute(block, axis, route)


def norm_rows(values, gain_vec):
    return values * lax.rsqrt(jnp.mean(values * values, axis=-1, keepdims=True) + EPS) * gain_vec


def rotate(values, positions):
    half_dim = HEAD_DIM // 2
    heads_here = values.shape[1] // HEAD_DIM
    inv_freq = jnp.exp(
        jnp.arange(half_dim, dtype=jnp.float32) * (-2.0 * math.log(ROPE_BASE) / HEAD_DIM)
    )
    angles = positions.astype(jnp.float32)[:, None] * inv_freq[None, :]
    cosine = jnp.cos(angles)[:, None, :]
    sin_t = jnp.sin(angles)[:, None, :]
    shaped = values.reshape(values.shape[0], heads_here, HEAD_DIM)
    lower_half = shaped[..., :half_dim]
    upper_half = shaped[..., half_dim:]
    turned = jnp.concatenate(
        [lower_half * cosine - upper_half * sin_t, upper_half * cosine + lower_half * sin_t],
        axis=-1,
    )
    return turned.reshape(values.shape)


def attn_inputs(q_lin, k_lin, gain_q, gain_k, positions):
    return (
        rotate(norm_rows(q_lin, gain_q), positions),
        rotate(norm_rows(k_lin, gain_k), positions),
    )


def banded(shaped, fill_value):
    earlier = jnp.concatenate([jnp.full_like(shaped[:1], fill_value), shaped[:-1]], axis=0)
    return jnp.concatenate([earlier, shaped], axis=1)


def unbanded(band, local_rows):
    earlier = band[:, :local_rows]
    own_part = band[:, local_rows:]
    moved_up = jnp.concatenate([earlier[1:], jnp.zeros_like(earlier[:1])], axis=0)
    return own_part + moved_up


def add_counts(earlier, later):
    return earlier + later


def expert_move(buffer):
    return lax.all_to_all(buffer, ("ulysses", "blk"), split_axis=0, concat_axis=0, tiled=True)


def to_head_layout(values):
    return jax.tree.map(
        lambda part, own: part.astype(own.dtype),
        lax.all_to_all(as_sent(values), "ulysses", split_axis=1, concat_axis=0, tiled=True),
        values,
    )


def to_token_layout(values):
    return jax.tree.map(
        lambda part, own: part.astype(own.dtype),
        lax.all_to_all(as_sent(values), "ulysses", split_axis=0, concat_axis=1, tiled=True),
        values,
    )


def local(
    inputs,
    cotangent,
    segments,
    expert_ids,
    gate_weights,
    fill_order,
    norm1_gain,
    w_query,
    w_key,
    w_value,
    w_output,
    query_gain,
    key_gain,
    norm2_gain,
    expert_gate,
    expert_up,
    expert_down,
):
    blk_size = lax.axis_size("blk")
    groups = lax.axis_size("ulysses")
    devices = blk_size * groups
    local_rows = inputs.shape[0]
    model_width = inputs.shape[1]
    blk_index = lax.axis_index("blk")
    group_index = lax.axis_index("ulysses")
    device_index = group_index * blk_size + blk_index
    positions = device_index * local_rows + jnp.arange(local_rows, dtype=jnp.int32)
    heads_dev = model_width // groups // HEAD_DIM
    score_scale = 1.0 / math.sqrt(HEAD_DIM)
    layer_in = inputs.astype(jnp.float32)
    dense = (w_query, w_key, w_value, w_output, norm1_gain, query_gain, key_gain, norm2_gain)
    gathered = (
        lax.all_gather(dense[0], ("ulysses", "blk"), axis=0, tiled=True),
        lax.all_gather(dense[1], ("ulysses", "blk"), axis=0, tiled=True),
        lax.all_gather(dense[2], ("ulysses", "blk"), axis=0, tiled=True),
        lax.all_gather(dense[3], ("ulysses", "blk"), axis=0, tiled=True),
        lax.all_gather(dense[4], ("ulysses", "blk"), axis=0, tiled=True),
        lax.all_gather(dense[5], ("ulysses", "blk"), axis=0, tiled=True),
        lax.all_gather(dense[6], ("ulysses", "blk"), axis=0, tiled=True),
        lax.all_gather(dense[7], ("ulysses", "blk"), axis=0, tiled=True),
    )
    w_q, w_k, w_v, w_o = (gathered[0], gathered[1], gathered[2], gathered[3])
    gain_one = gathered[4].astype(jnp.float32)
    gain_q = gathered[5].astype(jnp.float32)
    gain_k = gathered[6].astype(jnp.float32)
    gain_two = gathered[7].astype(jnp.float32)
    normed_one = norm_rows(layer_in, gain_one).astype(jnp.bfloat16)
    q_lin = jnp.dot(normed_one, w_q, preferred_element_type=jnp.float32)
    k_lin = jnp.dot(normed_one, w_k, preferred_element_type=jnp.float32)
    v_lin = jnp.dot(normed_one, w_v, preferred_element_type=jnp.float32)
    (q_rot, k_rot), pre_back = jax.vjp(
        lambda q_in, k_in, gq_in, gk_in: attn_inputs(q_in, k_in, gq_in, gk_in, positions),
        q_lin,
        k_lin,
        gain_q,
        gain_k,
    )
    q_heads, k_heads, v_heads = to_head_layout(
        (q_rot.astype(jnp.bfloat16), k_rot.astype(jnp.bfloat16), v_lin.astype(jnp.bfloat16))
    )
    group_ids = jnp.arange(groups, dtype=jnp.int32)[:, None]
    row_ids = jnp.arange(local_rows, dtype=jnp.int32)[None, :]
    q_pos = (group_ids * blk_size + blk_index) * local_rows + row_ids
    q_seg = segments[q_pos]
    four_shape = (groups, local_rows, heads_dev, HEAD_DIM)
    q_four = q_heads.reshape(four_shape)

    def score_block(k_now, source):
        k_pos = (group_ids * blk_size + source) * local_rows + row_ids
        k_seg = banded(segments[k_pos], -1)
        k_pos = banded(k_pos, 0)
        k_band = banded(k_now.reshape(four_shape), 0)
        raw_scores = (
            jnp.einsum("gqhd,gkhd->gqhk", q_four, k_band, preferred_element_type=jnp.float32)
            * score_scale
        )
        allowed = (k_seg[:, None, :] == q_seg[:, :, None]) & (
            k_pos[:, None, :] <= q_pos[:, :, None]
        )
        return (raw_scores, allowed[:, :, None, :], k_band)

    def forward_step(flash_state, kv_stack, step_id):
        run_max, run_sum, run_out = flash_state
        source = jnp.mod(blk_index - step_id, blk_size)
        raw_scores, allowed, k_band = score_block(kv_stack[0], source)
        raw_scores = jnp.where(allowed, raw_scores, NEG)
        new_max = jnp.maximum(run_max, jnp.max(raw_scores, axis=-1))
        shrink = jnp.exp(run_max - new_max)
        weights = jnp.where(allowed, jnp.exp(raw_scores - new_max[..., None]), 0.0)
        run_sum = run_sum * shrink + jnp.sum(weights, axis=-1)
        v_band = banded(kv_stack[1].reshape(four_shape), 0)
        run_out = run_out * shrink[..., None] + jnp.einsum(
            "gqhk,gkhd->gqhd",
            weights.astype(jnp.bfloat16),
            v_band,
            preferred_element_type=jnp.float32,
        )
        return (new_max, run_sum, run_out)

    start_state = (
        jnp.full((groups, local_rows, heads_dev), NEG, jnp.float32),
        jnp.zeros((groups, local_rows, heads_dev), jnp.float32),
        jnp.zeros(four_shape, jnp.float32),
    )
    kv_home = jnp.stack([k_heads, v_heads])
    first_state = forward_step(start_state, kv_home, 0)

    def forward_turn(step_id, loop_state):
        flash_state, kv_stack = loop_state
        moved = passed_along(kv_stack, "blk", 1)
        return (forward_step(flash_state, moved, step_id), moved)

    final_state, unused_kv = lax.fori_loop(1, blk_size, forward_turn, (first_state, kv_home))
    run_max, run_sum, run_out = final_state
    o_four = (run_out / run_sum[..., None]).astype(jnp.bfloat16)
    log_total = run_max + jnp.log(run_sum)
    o_heads = o_four.reshape(groups * local_rows, heads_dev * HEAD_DIM)
    attended = to_token_layout(o_heads)
    residual = layer_in + jnp.dot(attended, w_o, preferred_element_type=jnp.float32)
    normed_two_f, norm_two_back = jax.vjp(norm_rows, residual, gain_two)
    normed_two = normed_two_f.astype(jnp.bfloat16)
    experts_n = devices // 2
    topk = expert_ids.shape[1]
    per_source = 2 * local_rows * topk // experts_n
    half_slots = per_source // 2
    capacity = 9 * local_rows * devices * topk // (8 * experts_n)
    slots_all = experts_n * per_source
    tokens_local = jnp.arange(local_rows, dtype=jnp.int32)
    chosen = jnp.sum(
        (expert_ids[:, :, None] == jnp.arange(experts_n, dtype=jnp.int32)[None, None, :]).astype(
            jnp.int32
        ),
        axis=1,
    )
    by_fill = jnp.zeros((local_rows,), jnp.int32).at[fill_order].set(tokens_local)
    sorted_rows = chosen[by_fill]
    before = jnp.cumsum(sorted_rows, axis=0) - sorted_rows
    rank_all = before[fill_order]
    pair_rank = jnp.take_along_axis(rank_all, expert_ids, axis=1)
    counts = jnp.sum(chosen, axis=0)
    offsets = prefix(counts, ("ulysses", "blk"), add_counts, jnp.zeros_like(counts))
    kept_pair = offsets[expert_ids] + pair_rank < capacity
    pair_slot = expert_ids * per_source + pair_rank
    pair_index = tokens_local[:, None] * topk + jnp.arange(topk, dtype=jnp.int32)[None, :]
    slot_pair = (
        jnp.zeros((slots_all,), jnp.int32).at[pair_slot.reshape(-1)].set(pair_index.reshape(-1))
    )
    slot_live = (
        jnp.zeros((slots_all,), jnp.bool_).at[pair_slot.reshape(-1)].set(kept_pair.reshape(-1))
    )
    slot_token = slot_pair // topk
    send_rows = jnp.where(slot_live[:, None], normed_two[slot_token], jnp.zeros((), jnp.bfloat16))
    received = expert_move(send_rows.reshape(devices, half_slots, model_width)).reshape(
        devices * half_slots, model_width
    )
    parity = jnp.mod(blk_index, 2)
    partner = partner_2((expert_gate, expert_up, expert_down), "blk", 0)

    def joined(own_half, other_half):
        lower_part = jnp.where(parity == 0, own_half, other_half)
        upper_part = jnp.where(parity == 0, other_half, own_half)
        return jnp.concatenate([lower_part, upper_part], axis=0)

    gate_full = joined(expert_gate, partner[0])
    up_full = joined(expert_up, partner[1])
    down_full = joined(expert_down, partner[2])
    gate_pre = jnp.dot(received, gate_full, preferred_element_type=jnp.float32)
    up_pre = jnp.dot(received, up_full, preferred_element_type=jnp.float32)
    hidden = (jax.nn.silu(gate_pre) * up_pre).astype(jnp.bfloat16)
    produced = jnp.dot(hidden, down_full, preferred_element_type=jnp.float32).astype(jnp.bfloat16)
    returned = expert_move(produced.reshape(devices, half_slots, model_width)).reshape(
        slots_all, model_width
    )
    pair_share = jnp.where(kept_pair, gate_weights, 0.0)
    mixed = jnp.einsum("tk,tkd->td", pair_share, returned[pair_slot].astype(jnp.float32))
    output = residual + mixed
    grad_out = cotangent.astype(jnp.float32)
    slot_share = jnp.where(slot_live, gate_weights.reshape(-1)[slot_pair], 0.0)
    grad_send = (slot_share[:, None] * grad_out[slot_token]).astype(jnp.bfloat16)
    grad_rows = expert_move(grad_send.reshape(devices, half_slots, model_width)).reshape(
        devices * half_slots, model_width
    )
    d_down_full = jnp.einsum("rf,rd->fd", hidden, grad_rows, preferred_element_type=jnp.float32)
    d_hidden = jnp.einsum("rd,fd->rf", grad_rows, down_full, preferred_element_type=jnp.float32)
    sigma = jax.nn.sigmoid(gate_pre)
    d_gate_pre = (d_hidden * up_pre * sigma * (1.0 + gate_pre * (1.0 - sigma))).astype(jnp.bfloat16)
    d_up_pre = (d_hidden * gate_pre * sigma).astype(jnp.bfloat16)
    d_gate_full = jnp.einsum("rd,rf->df", received, d_gate_pre, preferred_element_type=jnp.float32)
    d_up_full = jnp.einsum("rd,rf->df", received, d_up_pre, preferred_element_type=jnp.float32)
    d_pair_rows = (
        jnp.einsum("rf,df->rd", d_gate_pre, gate_full, preferred_element_type=jnp.float32)
        + jnp.einsum("rf,df->rd", d_up_pre, up_full, preferred_element_type=jnp.float32)
    ).astype(jnp.bfloat16)
    back_rows = expert_move(d_pair_rows.reshape(devices, half_slots, model_width)).reshape(
        slots_all, model_width
    )
    d_normed_two = jnp.sum(
        jnp.where(kept_pair[:, :, None], back_rows[pair_slot].astype(jnp.float32), 0.0), axis=1
    )
    half_rows = expert_gate.shape[0]
    half_hidden = expert_down.shape[0]

    def halves(full_grad, size):
        own_half = lax.dynamic_slice_in_dim(full_grad, parity * size, size, 0)
        other_half = lax.dynamic_slice_in_dim(full_grad, (1 - parity) * size, size, 0)
        return (own_half, other_half)

    gate_own, gate_other = halves(d_gate_full, half_rows)
    up_own, up_other = halves(d_up_full, half_rows)
    down_own, down_other = halves(d_down_full, half_hidden)
    partner_grads = (
        partner_2(gate_other.astype(jnp.bfloat16), "blk", 0).astype(gate_other.dtype),
        partner_2(up_other.astype(jnp.bfloat16), "blk", 0).astype(up_other.dtype),
        partner_2(down_other.astype(jnp.bfloat16), "blk", 0).astype(down_other.dtype),
    )
    d_expert_gate = gate_own + partner_grads[0]
    d_expert_up = up_own + partner_grads[1]
    d_expert_down = down_own + partner_grads[2]
    d_resid_norm, d_gain_two = norm_two_back(d_normed_two)
    d_residual = grad_out + d_resid_norm
    d_res_low = d_residual.astype(jnp.bfloat16)
    d_attended = jnp.einsum("te,de->td", d_res_low, w_o, preferred_element_type=jnp.float32).astype(
        jnp.bfloat16
    )
    d_o_heads = to_head_layout(d_attended)
    d_o_four = d_o_heads.reshape(four_shape)
    row_delta = jnp.sum(d_o_four.astype(jnp.float32) * o_four.astype(jnp.float32), axis=-1)

    def back_turn(step_id, loop_state):
        moving, dq_acc = loop_state
        source = jnp.mod(blk_index - step_id, blk_size)
        k_now = moving[0].astype(jnp.bfloat16)
        v_now = moving[1].astype(jnp.bfloat16)
        raw_scores, allowed, k_band = score_block(k_now, source)
        prob_rows = jnp.where(allowed, jnp.exp(raw_scores - log_total[..., None]), 0.0)
        v_band = banded(v_now.reshape(four_shape), 0)
        d_probs = jnp.einsum(
            "gqhd,gkhd->gqhk", d_o_four, v_band, preferred_element_type=jnp.float32
        )
        d_scores = (prob_rows * (d_probs - row_delta[..., None])).astype(jnp.bfloat16)
        dv_band = jnp.einsum(
            "gqhk,gqhd->gkhd",
            prob_rows.astype(jnp.bfloat16),
            d_o_four,
            preferred_element_type=jnp.float32,
        )
        dk_band = (
            jnp.einsum("gqhk,gqhd->gkhd", d_scores, q_four, preferred_element_type=jnp.float32)
            * score_scale
        )
        dq_acc = (
            dq_acc
            + jnp.einsum("gqhk,gkhd->gqhd", d_scores, k_band, preferred_element_type=jnp.float32)
            * score_scale
        )
        flat_shape = moving[2].shape
        dk_new = moving[2] + unbanded(dk_band, local_rows).reshape(flat_shape)
        dv_new = moving[3] + unbanded(dv_band, local_rows).reshape(flat_shape)
        moving = passed_along(
            jnp.stack([moving[0], moving[1], dk_new, dv_new]).astype(jnp.bfloat16), "blk", 1
        ).astype(jnp.float32)
        return (moving, dq_acc)

    zero_rows = jnp.zeros(k_heads.shape, jnp.float32)
    start_moving = jnp.stack(
        [k_heads.astype(jnp.float32), v_heads.astype(jnp.float32), zero_rows, zero_rows]
    )
    moving, dq_acc = lax.fori_loop(
        0, blk_size, back_turn, (start_moving, jnp.zeros(four_shape, jnp.float32))
    )
    d_q_send = dq_acc.astype(jnp.bfloat16).reshape(k_heads.shape)
    d_k_send = moving[2].astype(jnp.bfloat16)
    d_v_send = moving[3].astype(jnp.bfloat16)
    d_q_rot, d_k_rot, d_v_lin = to_token_layout((d_q_send, d_k_send, d_v_send))
    d_q_lin, d_k_lin, d_gain_q, d_gain_k = pre_back(
        (d_q_rot.astype(jnp.float32), d_k_rot.astype(jnp.float32))
    )
    d_q_low = d_q_lin.astype(jnp.bfloat16)
    d_k_low = d_k_lin.astype(jnp.bfloat16)
    d_normed_one = jnp.einsum("te,de->td", d_q_low, w_q, preferred_element_type=jnp.float32)
    d_normed_one = d_normed_one + jnp.einsum(
        "te,de->td", d_k_low, w_k, preferred_element_type=jnp.float32
    )
    d_normed_one = d_normed_one + jnp.einsum(
        "te,de->td", d_v_lin, w_v, preferred_element_type=jnp.float32
    )
    unused_norm, norm_one_back = jax.vjp(norm_rows, layer_in, gain_one)
    d_layer_in, d_gain_one = norm_one_back(d_normed_one)
    d_inputs = d_residual + d_layer_in
    d_qk_heads = to_head_layout((d_q_low, d_k_low))
    rows_all = (
        lax.all_gather(normed_one, "ulysses", axis=0, tiled=True),
        lax.all_gather(d_res_low, "ulysses", axis=0, tiled=True),
    )
    head_cols = model_width // groups
    piece_rows = model_width // devices

    def by_owner(part):
        rest = part.shape[1:]
        shaped = part.reshape((groups, blk_size, piece_rows) + rest)
        return jnp.swapaxes(shaped, 0, 1).reshape((model_width,) + rest)

    part_q = jnp.einsum("td,te->de", rows_all[0], d_qk_heads[0], preferred_element_type=jnp.float32)
    part_k = jnp.einsum("td,te->de", rows_all[0], d_qk_heads[1], preferred_element_type=jnp.float32)
    part_v = jnp.einsum("td,te->de", rows_all[0], d_v_send, preferred_element_type=jnp.float32)
    part_o = jnp.einsum("te,td->ed", o_heads, rows_all[1], preferred_element_type=jnp.float32)
    blk_sums = (
        lax.psum_scatter(
            by_owner(part_q).astype(jnp.bfloat16), "blk", scatter_dimension=0, tiled=True
        ).astype(jnp.float32),
        lax.psum_scatter(
            by_owner(part_k).astype(jnp.bfloat16), "blk", scatter_dimension=0, tiled=True
        ).astype(jnp.float32),
        lax.psum_scatter(
            by_owner(part_v).astype(jnp.bfloat16), "blk", scatter_dimension=0, tiled=True
        ).astype(jnp.float32),
        lax.psum_scatter(
            part_o.astype(jnp.bfloat16), "blk", scatter_dimension=0, tiled=True
        ).astype(jnp.float32),
        lax.psum_scatter(
            by_owner(d_gain_one).astype(jnp.bfloat16), "blk", scatter_dimension=0, tiled=True
        ).astype(jnp.float32),
        lax.psum_scatter(
            by_owner(d_gain_q).astype(jnp.bfloat16), "blk", scatter_dimension=0, tiled=True
        ).astype(jnp.float32),
        lax.psum_scatter(
            by_owner(d_gain_k).astype(jnp.bfloat16), "blk", scatter_dimension=0, tiled=True
        ).astype(jnp.float32),
        lax.psum_scatter(
            by_owner(d_gain_two).astype(jnp.bfloat16), "blk", scatter_dimension=0, tiled=True
        ).astype(jnp.float32),
    )

    def widened(part):
        return lax.dynamic_update_slice_in_dim(
            jnp.zeros((part.shape[0], model_width), jnp.float32), part, group_index * head_cols, 1
        )

    col_sums = (
        lax.psum_scatter(
            widened(blk_sums[0]).astype(jnp.bfloat16), "ulysses", scatter_dimension=0, tiled=True
        ).astype(jnp.float32),
        lax.psum_scatter(
            widened(blk_sums[1]).astype(jnp.bfloat16), "ulysses", scatter_dimension=0, tiled=True
        ).astype(jnp.float32),
        lax.psum_scatter(
            widened(blk_sums[2]).astype(jnp.bfloat16), "ulysses", scatter_dimension=0, tiled=True
        ).astype(jnp.float32),
        lax.psum_scatter(
            blk_sums[4].astype(jnp.bfloat16), "ulysses", scatter_dimension=0, tiled=True
        ).astype(jnp.float32),
        lax.psum_scatter(
            blk_sums[5].astype(jnp.bfloat16), "ulysses", scatter_dimension=0, tiled=True
        ).astype(jnp.float32),
        lax.psum_scatter(
            blk_sums[6].astype(jnp.bfloat16), "ulysses", scatter_dimension=0, tiled=True
        ).astype(jnp.float32),
        lax.psum_scatter(
            blk_sums[7].astype(jnp.bfloat16), "ulysses", scatter_dimension=0, tiled=True
        ).astype(jnp.float32),
    )
    result_grads = (
        col_sums[0],
        col_sums[1],
        col_sums[2],
        blk_sums[3],
        col_sums[3],
        col_sums[4],
        col_sums[5],
        col_sums[6],
    )
    return (
        output,
        d_inputs,
        result_grads[4],
        result_grads[0],
        result_grads[1],
        result_grads[2],
        result_grads[3],
        result_grads[5],
        result_grads[6],
        result_grads[7],
        d_expert_gate,
        d_expert_up,
        d_expert_down,
    )


MESH = pl.DeviceIdType.MESH
P1 = 96

def place():
    u = lax.axis_index("ulysses"); z = lax.axis_index("z"); c = lax.axis_index("core")
    return u, z, c

def ag_kernel(cut, x_ref, o_ref, local_sem, s_sem, zr, xr, yr, d1r, d2r, bs, br, bzr):
    u, z, c = place()
    Z = 4
    R = x_ref.shape[0]
    ux, uy = u ^ 1, u ^ 2
    xn, yn, up, dn = (ux, z, c), (uy, z, c), (u, z + 1, c), (u, z - 1, c)
    has_up, has_dn = z < Z - 1, z > 0
    bar = pltpu.get_barrier_semaphore()
    for n in (xn, yn):
        pl.semaphore_signal(bar, inc=1, device_id=n, device_id_type=MESH)
    @pl.when(has_up)
    def _():
        pl.semaphore_signal(bar, inc=1, device_id=up, device_id_type=MESH)
    @pl.when(has_dn)
    def _():
        pl.semaphore_signal(bar, inc=1, device_id=dn, device_id_type=MESH)
    pl.semaphore_wait(bar, 2 + has_up.astype(jnp.int32) + has_dn.astype(jnp.int32))
    sends = []
    def copy(src, dst, ss, rs, dev):
        return pltpu.make_async_remote_copy(src_ref=src, dst_ref=dst, send_sem=ss, recv_sem=rs, device_id=dev, device_id_type=MESH)
    def go(cond, make):
        idx = len(sends)
        def mk():
            return make(s_sem.at[idx])
        sends.append((cond, mk))
        if cond is None:
            mk().start()
        else:
            pl.when(cond)(lambda: mk().start())
    def both(a, b):
        if a is None: return b
        if b is None: return a
        return jnp.logical_and(a, b)
    def wait(cond, ref, sem):
        def w():
            pltpu.make_async_copy(ref, ref, sem).wait()
        if cond is None: w()
        else: pl.when(cond)(w)
    own = pltpu.make_async_copy(x_ref, o_ref.at[u, z], local_sem)
    own.start()
    A = slice(0, cut)
    h = cut // 2
    def oa(uu, zz, lo=0, n=cut):
        return o_ref.at[uu, zz, pl.ds(lo, n), :]
    def spread(s, zz, cond):
        src = (lambda: x_ref.at[pl.ds(0, cut), :]) if s == 0 else (lambda: oa(u, zz))
        go(cond, lambda sm: copy(src(), oa(u, zz), sm, xr.at[zz], xn))
        go(cond, lambda sm: copy(src(), oa(u, zz), sm, yr.at[zz], yn))
    def cross(zz, cond):
        wait(cond, oa(ux, zz), xr.at[zz])
        go(cond, lambda sm: copy(oa(ux, zz, 0, h), oa(ux, zz, 0, h), sm, d1r.at[zz], yn))
        wait(cond, oa(uy, zz), yr.at[zz])
        go(cond, lambda sm: copy(oa(uy, zz, h, h), oa(uy, zz, h, h), sm, d2r.at[zz], xn))
    rb = R - cut
    hb = rb // 2
    def ob(uu, zz, lo=0, n=None):
        return o_ref.at[uu, zz, pl.ds(cut + lo, rb if n is None else n), :]
    go(has_up, lambda sm: copy(x_ref.at[pl.ds(0, cut), :], oa(u, z), sm, zr.at[z], up))
    go(has_dn, lambda sm: copy(x_ref.at[pl.ds(0, cut), :], oa(u, z), sm, zr.at[z], dn))
    if rb:
        go(None, lambda sm: copy(x_ref.at[pl.ds(cut, rb), :], ob(u, z), sm, br.at[0], xn))
        go(None, lambda sm: copy(x_ref.at[pl.ds(cut, rb), :], ob(u, z), sm, br.at[1], yn))
    spread(0, z, None)
    if rb:
        wait(None, ob(ux, z), br.at[0])
        go(None, lambda sm: copy(ob(ux, z, 0, hb), ob(ux, z, 0, hb), sm, br.at[2], yn))
        wait(None, ob(uy, z), br.at[1])
        go(None, lambda sm: copy(ob(uy, z, hb, hb), ob(uy, z, hb, hb), sm, br.at[3], xn))
    own.wait()
    def quad(zz):
        return o_ref.at[:, zz, pl.ds(cut, rb), :]
    def zs(s):
        zl, zh = z - s, z + s
        cl, ch = zl >= 0, zh < Z
        zlc, zhc = jnp.maximum(zl, 0), jnp.minimum(zh, Z - 1)
        return (zlc, cl, has_up, up), (zhc, ch, has_dn, dn)
    prev = [(z, None)]
    for s in range(1, Z):
        cur = []
        for (zz, cond, fwd, dev) in zs(s):
            wait(cond, oa(u, zz), zr.at[zz])
            go(both(cond, fwd), lambda sm, zz=zz, dev=dev: copy(oa(u, zz), oa(u, zz), sm, zr.at[zz], dev))
            spread(s, zz, cond)
            cur.append((zz, cond))
        if rb and s == 1:
            wait(None, ob(u ^ 3, z, 0, hb), br.at[2])
            wait(None, ob(u ^ 3, z, hb, hb), br.at[3])
            go(has_up, lambda sm: copy(quad(z), quad(z), sm, bzr.at[z], up))
            go(has_dn, lambda sm: copy(quad(z), quad(z), sm, bzr.at[z], dn))
        elif rb:
            for (zz, cond, fwd, dev) in zs(s - 1):
                wait(cond, quad(zz), bzr.at[zz])
                go(both(cond, fwd), lambda sm, zz=zz, dev=dev: copy(quad(zz), quad(zz), sm, bzr.at[zz], dev))
        for zz, cond in prev:
            cross(zz, cond)
        prev = cur
    if rb:
        for (zz, cond, fwd, dev) in zs(Z - 1):
            wait(cond, quad(zz), bzr.at[zz])
    for zz, cond in prev:
        cross(zz, cond)
    for zz in range(Z):
        wait(None, oa(u ^ 3, zz, 0, h), d1r.at[zz])
        wait(None, oa(u ^ 3, zz, h, h), d2r.at[zz])
    for cond, mk in sends:
        if cond is None: mk().wait_send()
        else: pl.when(cond)(lambda mk=mk: mk().wait_send())

def ag16(x, cid, cut=P1, space=pl.ANY):
    R, D = x.shape
    DMA = pltpu.SemaphoreType.DMA
    return pl.pallas_call(
        functools.partial(ag_kernel, cut),
        out_shape=jax.ShapeDtypeStruct((4, 4, R, D), x.dtype),
        in_specs=[pl.BlockSpec(memory_space=space)],
        out_specs=pl.BlockSpec(memory_space=space),
        scratch_shapes=[DMA, DMA((64,)), DMA((4,)), DMA((4,)), DMA((4,)), DMA((4,)), DMA((4,)), DMA((4,)), DMA((4,)), DMA((4,))],
        compiler_params=pltpu.CompilerParams(collective_id=cid, has_side_effects=True, vmem_limit_bytes=48 * 2**20),
        name="gather_rows",
    )(x)
F32 = jnp.float32
BF = jnp.bfloat16


class Net:
    def __init__(self, sems):
        self.sems, self.sends = sems, []
        self.u, self.z, self.c = place()
        u, z, c = self.u, self.z, self.c
        self.ux, self.uy, self.ud = u ^ 1, u ^ 2, u ^ 3
        self.xn, self.yn, self.up, self.dn = (u ^ 1, z, c), (u ^ 2, z, c), (u, z + 1, c), (u, z - 1, c)
        self.has_up, self.has_dn = z < 3, z > 0
        self.at = [z == i for i in range(4)]

    def barrier(self, more=()):
        bar = pltpu.get_barrier_semaphore()
        for n in (self.xn, self.yn) + tuple(more):
            pl.semaphore_signal(bar, inc=1, device_id=n, device_id_type=MESH)
        for cond, n in ((self.has_up, self.up), (self.has_dn, self.dn)):
            pl.when(cond)(lambda n=n: pl.semaphore_signal(bar, inc=1, device_id=n, device_id_type=MESH))
        pl.semaphore_wait(bar, 2 + len(more) + self.has_up.astype(jnp.int32) + self.has_dn.astype(jnp.int32))

    def go(self, cond, src, dst, rsem, dev):
        idx = len(self.sends)

        def mk():
            return pltpu.make_async_remote_copy(
                src_ref=src(), dst_ref=dst(), send_sem=self.sems.at[idx], recv_sem=rsem(),
                device_id=dev, device_id_type=MESH)

        self.sends.append((cond, mk))
        if cond is None:
            mk().start()
        else:
            pl.when(cond)(lambda: mk().start())

    def wait(self, cond, ref, sem):
        def w():
            pltpu.make_async_copy(ref(), ref(), sem).wait()

        if cond is None:
            w()
        else:
            pl.when(cond)(w)

    def finish(self):
        for cond, mk in self.sends:
            if cond is None:
                mk().wait_send()
            else:
                pl.when(cond)(lambda mk=mk: mk().wait_send())


def strips(rows, body, step=16):
    def it(i, _):
        body(pl.ds(pl.multiple_of(i * step, step), step))
        return 0

    lax.fori_loop(0, rows // step, it, 0)


def wide(v):
    return v.astype(F32)


class Scatter:
    def __init__(self, net, cut, P, bufs):
        self.net, self.cut, self.P = net, cut, P
        (self.mid1, self.mid2, self.fx, self.fy, self.be, self.ab, self.bbe, self.bab, self.bm,
         self.m1s, self.m2s, self.fxs, self.fys, self.bes, self.abs_, self.bbes, self.babs, self.bms) = bufs
        self.R = P.shape[2]
        self.h = cut // 2
        self.rb = self.R - cut
        self.hb = self.rb // 2

    def first(self, zd):
        net, P, h, cut, rb = self.net, self.P, self.h, self.cut, self.rb
        net.go(None, lambda: P.at[net.ud, zd, pl.ds(0, h), :], lambda: self.mid1.at[zd], lambda: self.m1s.at[zd], net.xn)
        net.go(None, lambda: P.at[net.ud, zd, pl.ds(h, h), :], lambda: self.mid2.at[zd], lambda: self.m2s.at[zd], net.yn)
        if rb and zd > 0:
            net.go(net.at[0], lambda: P.at[:, zd, pl.ds(cut, rb), :], lambda: self.bbe.at[zd], lambda: self.bbes.at[zd], net.up)
        if rb and zd < 3:
            net.go(net.at[3], lambda: P.at[:, zd, pl.ds(cut, rb), :], lambda: self.bab.at[zd], lambda: self.babs.at[zd], net.dn)
        net.go(None, lambda: P.at[net.ux, zd, pl.ds(0, h), :], lambda: self.fx.at[zd, pl.ds(0, h), :], lambda: self.fxs.at[zd, 0], net.xn)
        net.go(None, lambda: P.at[net.uy, zd, pl.ds(h, h), :], lambda: self.fy.at[zd, pl.ds(h, h), :], lambda: self.fys.at[zd, 1], net.yn)

    def mids(self, zd):
        net, P, h, mid1, mid2 = self.net, self.P, self.h, self.mid1, self.mid2

        def add1(sl):
            mid1[zd, sl, :] = (wide(mid1[zd, sl, :]) + wide(P[net.uy, zd, sl, :])).astype(BF)

        def add2(sl):
            mid2[zd, sl, :] = (wide(mid2[zd, sl, :]) + wide(P[net.ux, zd, pl.ds(h + sl.start, 16), :])).astype(BF)

        net.wait(None, lambda: mid1.at[zd], self.m1s.at[zd])
        strips(h, add1)
        net.go(None, lambda: mid1.at[zd], lambda: self.fy.at[zd, pl.ds(0, h), :], lambda: self.fys.at[zd, 0], net.yn)
        net.wait(None, lambda: mid2.at[zd], self.m2s.at[zd])
        strips(h, add2)
        net.go(None, lambda: mid2.at[zd], lambda: self.fx.at[zd, pl.ds(h, h), :], lambda: self.fxs.at[zd, 1], net.xn)

    def route(self, zd, zz):
        if zz < zd:
            return True, self.net.up
        return False, self.net.dn

    def bhop(self, zd, zz):
        net, P, cut, rb = self.net, self.P, self.cut, self.rb
        if not rb:
            return
        upward, dev = self.route(zd, zz)
        buf, sems = (self.bbe, self.bbes) if upward else (self.bab, self.babs)
        here = net.at[zz]
        net.wait(here, lambda: buf.at[zd], sems.at[zd])

        def add():
            for q in range(4):
                def one(sl, q=q):
                    buf[zd, q, sl, :] = (wide(buf[zd, q, sl, :]) + wide(P[q, zd, pl.ds(cut + sl.start, 16), :])).astype(BF)
                strips(rb, one)

        pl.when(here)(add)
        net.go(here, lambda: buf.at[zd], lambda: buf.at[zd], lambda: sems.at[zd], dev)

    def square(self, zd, cond):
        net, h = self.net, self.h
        for half in (0, 1):
            net.wait(cond, lambda: self.fx.at[zd, pl.ds(half * h, h), :], self.fxs.at[zd, half])
            net.wait(cond, lambda: self.fy.at[zd, pl.ds(half * h, h), :], self.fys.at[zd, half])

    def local(self, zd, sl):
        return wide(self.P[self.net.u, zd, sl, :]) + wide(self.fx[zd, sl, :]) + wide(self.fy[zd, sl, :])

    def hop(self, zd, zz):
        net = self.net
        upward, dev = self.route(zd, zz)
        buf, sems = (self.be, self.bes) if upward else (self.ab, self.abs_)
        here = net.at[zz]
        self.square(zd, here)
        if zz in (0, 3):
            def begin(sl):
                self.fx[zd, sl, :] = self.local(zd, sl).astype(BF)

            pl.when(here)(lambda: strips(self.cut, begin))
            net.go(here, lambda: self.fx.at[zd], lambda: buf.at[zd], lambda: sems.at[zd], dev)
        else:
            def plus(sl):
                buf[zd, sl, :] = (self.local(zd, sl) + wide(buf[zd, sl, :])).astype(BF)

            net.wait(here, lambda: buf.at[zd], sems.at[zd])
            pl.when(here)(lambda: strips(self.cut, plus))
            net.go(here, lambda: buf.at[zd], lambda: buf.at[zd], lambda: sems.at[zd], dev)

    def bquad(self):
        net, P, cut, rb, hb, bm, bms = self.net, self.P, self.cut, self.rb, self.hb, self.bm, self.bms
        if not rb:
            return
        z = net.z
        net.wait(net.has_dn, lambda: self.bbe.at[z], self.bbes.at[z])
        net.wait(net.has_up, lambda: self.bab.at[z], self.babs.at[z])
        for q in range(4):
            def fold(sl, q=q):
                s = wide(P[q, z, pl.ds(cut + sl.start, 16), :])
                s = s + jnp.where(net.has_dn, wide(self.bbe[z, q, sl, :]), 0.0)
                s = s + jnp.where(net.has_up, wide(self.bab[z, q, sl, :]), 0.0)
                bm[q, sl, :] = s.astype(BF)
            strips(rb, fold)
        net.go(None, lambda: bm.at[net.ud, pl.ds(0, hb), :], lambda: bm.at[4, pl.ds(0, hb), :], lambda: bms.at[0], net.xn)
        net.go(None, lambda: bm.at[net.ud, pl.ds(hb, hb), :], lambda: bm.at[5, pl.ds(0, hb), :], lambda: bms.at[1], net.yn)
        net.go(None, lambda: bm.at[net.ux, pl.ds(0, hb), :], lambda: bm.at[6, pl.ds(0, hb), :], lambda: bms.at[2], net.xn)
        net.go(None, lambda: bm.at[net.uy, pl.ds(hb, hb), :], lambda: bm.at[7, pl.ds(hb, hb), :], lambda: bms.at[3], net.yn)

    def bquad2(self):
        net, rb, hb, bm, bms = self.net, self.rb, self.hb, self.bm, self.bms
        if not rb:
            return

        def add4(sl):
            bm[4, sl, :] = (wide(bm[4, sl, :]) + wide(bm[net.uy, sl, :])).astype(BF)

        def add5(sl):
            bm[5, sl, :] = (wide(bm[5, sl, :]) + wide(bm[net.ux, pl.ds(hb + sl.start, 16), :])).astype(BF)

        net.wait(None, lambda: bm.at[4, pl.ds(0, hb), :], bms.at[0])
        strips(hb, add4)
        net.go(None, lambda: bm.at[4, pl.ds(0, hb), :], lambda: bm.at[7, pl.ds(0, hb), :], lambda: bms.at[4], net.yn)
        net.wait(None, lambda: bm.at[5, pl.ds(0, hb), :], bms.at[1])
        strips(hb, add5)
        net.go(None, lambda: bm.at[5, pl.ds(0, hb), :], lambda: bm.at[6, pl.ds(hb, hb), :], lambda: bms.at[5], net.xn)

    def last(self, store):
        net, cut, rb, hb, bm, bms = self.net, self.cut, self.rb, self.hb, self.bm, self.bms
        z = net.z
        self.square(z, None)

        def own(sl):
            s = self.local(z, sl)
            s = s + jnp.where(net.has_dn, wide(self.be[z, sl, :]), 0.0)
            s = s + jnp.where(net.has_up, wide(self.ab[z, sl, :]), 0.0)
            store(sl, s)

        net.wait(net.has_dn, lambda: self.be.at[z], self.bes.at[z])
        net.wait(net.has_up, lambda: self.ab.at[z], self.abs_.at[z])
        strips(cut, own)
        if rb:
            net.wait(None, lambda: bm.at[6, pl.ds(0, hb), :], bms.at[2])
            net.wait(None, lambda: bm.at[6, pl.ds(hb, hb), :], bms.at[5])
            net.wait(None, lambda: bm.at[7, pl.ds(0, hb), :], bms.at[4])
            net.wait(None, lambda: bm.at[7, pl.ds(hb, hb), :], bms.at[3])
            strips(rb, lambda sl: store(
                pl.ds(cut + sl.start, 16), wide(bm[net.u, sl, :]) + wide(bm[6, sl, :]) + wide(bm[7, sl, :])))


def rs_scratch(cut, R, D):
    h, rb = cut // 2, R - cut
    V = lambda *s: pltpu.VMEM(s, BF)
    S = pltpu.SemaphoreType.DMA
    return [V(4, h, D), V(4, h, D), V(4, cut, D), V(4, cut, D), V(4, cut, D), V(4, cut, D),
            V(4, 4, max(rb, 16), D), V(4, 4, max(rb, 16), D), V(8, max(rb, 16), D),
            S((4,)), S((4,)), S((4, 2)), S((4, 2)), S((4,)), S((4,)), S((4,)), S((4,)), S((6,))]


def rs_kernel(cut, P, o_ref, ssem, *scr):
    net = Net(ssem)
    net.barrier()
    sc = Scatter(net, cut, P, scr)

    def store(sl, v):
        o_ref[sl, :] = v.astype(o_ref.dtype)

    for zd in (3, 0, 2, 1):
        sc.first(zd)
    for zd in (3, 0, 2, 1):
        sc.mids(zd)
    sc.hop(3, 0); sc.hop(0, 3); sc.bhop(3, 1); sc.bhop(0, 2)
    sc.hop(2, 0); sc.hop(1, 3); sc.bhop(2, 1); sc.bhop(1, 2)
    sc.hop(3, 1); sc.hop(0, 2); sc.bhop(3, 2); sc.bhop(0, 1)
    sc.hop(1, 0); sc.hop(2, 3); sc.bquad()
    sc.hop(2, 1); sc.hop(1, 2)
    sc.hop(3, 2); sc.hop(0, 1); sc.bquad2()
    sc.last(store)
    net.finish()


def rs16(p, cid, cut=96, dtype=F32):
    _, _, R, D = p.shape
    DMA = pltpu.SemaphoreType.DMA
    return pl.pallas_call(
        functools.partial(rs_kernel, cut),
        out_shape=jax.ShapeDtypeStruct((R, D), dtype),
        in_specs=[pl.BlockSpec(memory_space=pltpu.VMEM)],
        out_specs=pl.BlockSpec(memory_space=pltpu.VMEM),
        scratch_shapes=[DMA((96,))] + rs_scratch(cut, R, D),
        compiler_params=pltpu.CompilerParams(collective_id=cid, has_side_effects=True, vmem_limit_bytes=56 * 2**20),
        name="scatter_rows",
    )(p)


class Gather:
    def __init__(self, net, rows, cut, at, plane, sems):
        self.net, self.rows, self.cut, self.ref, self.plane = net, rows, cut, at, plane
        self.zr, self.xr, self.yr, self.d1, self.d2, self.br, self.bz = sems
        self.h, self.rb = cut // 2, rows - cut
        self.hb = self.rb // 2
        z = net.z
        self.near = []
        for s in range(4):
            zl, zh = z - s, z + s
            self.near.append((
                (jnp.maximum(zl, 0), zl >= 0, jnp.logical_and(zl >= 0, net.has_up), net.up),
                (jnp.minimum(zh, 3), zh < 4, jnp.logical_and(zh < 4, net.has_dn), net.dn)))

    def same(self, cond, uu, zz, lo, n, sem, dev):
        ref = lambda: self.ref(uu, zz, lo, n)
        self.net.go(cond, ref, ref, sem, dev)

    def outward(self, zz, cond):
        net, cut = self.net, self.cut
        self.same(cond, net.u, zz, 0, cut, lambda: self.xr.at[zz], net.xn)
        self.same(cond, net.u, zz, 0, cut, lambda: self.yr.at[zz], net.yn)

    def begin(self):
        net, cut, rb, z = self.net, self.cut, self.rb, self.net.z
        self.same(net.has_up, net.u, z, 0, cut, lambda: self.zr.at[z], net.up)
        self.same(net.has_dn, net.u, z, 0, cut, lambda: self.zr.at[z], net.dn)
        if rb:
            self.same(None, net.u, z, cut, rb, lambda: self.br.at[0], net.xn)
            self.same(None, net.u, z, cut, rb, lambda: self.br.at[1], net.yn)
        self.outward(z, None)

    def begin2(self):
        net, cut, rb, hb, z = self.net, self.cut, self.rb, self.hb, self.net.z
        if rb:
            net.wait(None, lambda: self.ref(net.ux, z, cut, rb), self.br.at[0])
            self.same(None, net.ux, z, cut, hb, lambda: self.br.at[2], net.yn)
            net.wait(None, lambda: self.ref(net.uy, z, cut, rb), self.br.at[1])
            self.same(None, net.uy, z, cut + hb, hb, lambda: self.br.at[3], net.xn)

    def along(self, s):
        net = self.net
        for zz, cond, fwd, dev in self.near[s]:
            net.wait(cond, lambda zz=zz: self.ref(net.u, zz, 0, self.cut), self.zr.at[zz])
            self.same(fwd, net.u, zz, 0, self.cut, lambda zz=zz: self.zr.at[zz], dev)
            self.outward(zz, cond)

    def quads(self, s):
        net, cut, rb, hb, z = self.net, self.cut, self.rb, self.hb, self.net.z
        if not rb:
            return
        if s == 0:
            net.wait(None, lambda: self.ref(net.ud, z, cut, hb), self.br.at[2])
            net.wait(None, lambda: self.ref(net.ud, z, cut + hb, hb), self.br.at[3])
            whole = lambda: self.plane(z, cut, rb)
            net.go(net.has_up, whole, whole, lambda: self.bz.at[z], net.up)
            net.go(net.has_dn, whole, whole, lambda: self.bz.at[z], net.dn)
            return
        for zz, cond, fwd, dev in self.near[s]:
            whole = lambda zz=zz: self.plane(zz, cut, rb)
            net.wait(cond, whole, self.bz.at[zz])
            net.go(fwd, whole, whole, lambda zz=zz: self.bz.at[zz], dev)

    def planes(self, s):
        if s == 0:
            return ((self.net.z, None),)
        return tuple((zz, cond) for zz, cond, _f, _d in self.near[s])

    def cross(self, s):
        net, h, cut = self.net, self.h, self.cut
        for zz, cond in self.planes(s):
            net.wait(cond, lambda zz=zz: self.ref(net.ux, zz, 0, cut), self.xr.at[zz])
            self.same(cond, net.ux, zz, 0, h, lambda zz=zz: self.d1.at[zz], net.yn)
            net.wait(cond, lambda zz=zz: self.ref(net.uy, zz, 0, cut), self.yr.at[zz])
            self.same(cond, net.uy, zz, h, h, lambda zz=zz: self.d2.at[zz], net.xn)

    def settle(self, s):
        net, h = self.net, self.h
        for zz, cond in self.planes(s):
            net.wait(cond, lambda zz=zz: self.ref(net.ud, zz, 0, h), self.d1.at[zz])
            net.wait(cond, lambda zz=zz: self.ref(net.ud, zz, h, h), self.d2.at[zz])


def ag_sems():
    S = pltpu.SemaphoreType.DMA
    return [S((4,)) for _ in range(7)]


def greet(net, chips=16):
    bar = pltpu.get_barrier_semaphore()

    def hello(j, _):
        t = lax.rem(net.u * 4 + net.z + j, chips)
        pl.semaphore_signal(bar, inc=1, device_id=(t // 4, lax.rem(t, 4), net.c), device_id_type=MESH)
        return 0

    lax.fori_loop(1, chips, hello, 0)
    pl.semaphore_signal(bar, inc=1, device_id=(net.u, net.z, 1 - net.c), device_id_type=MESH)
    pl.semaphore_wait(bar, chips)


def each_chip(net, body, chips=16):
    def one(j, _):
        t = lax.rem(net.u * 4 + net.z + j, chips)
        body(t, (t // 4, lax.rem(t, 4), net.c))
        return 0

    lax.fori_loop(1, chips, one, 0)


def remote(src, dst, ssem, rsem, dev):
    return pltpu.make_async_remote_copy(
        src_ref=src, dst_ref=dst, send_sem=ssem, recv_sem=rsem, device_id=dev, device_id_type=MESH)


def landed(ref, sem):
    pltpu.make_async_copy(ref, ref, sem).wait()


def row_sums(v):
    return jnp.sum(v.T, axis=0, keepdims=True)


def column(row):
    return jnp.broadcast_to(row, (row.shape[1], row.shape[1])).T


def share_sums(net, sums, sums_all, out, lsem, ssem, rsem):
    me = net.u * 4 + net.z
    own = pltpu.make_async_copy(sums, sums_all.at[me], lsem)
    own.start()
    each_chip(net, lambda t, dev: remote(sums, sums_all.at[me], ssem, rsem, dev).start())
    own.wait()
    part = sums_all.at[pl.ds(0, 15)]
    landed(part, rsem)
    total = sums_all[0]
    for i in range(1, 16):
        total = total + sums_all[i]
    out[...] = total
    landed(part, ssem)


def qkv_kernel(cut, x_ref, cols, gain, n1_o, lin, wf, tot, X, nb, sums, sums_all, lsem, nsem, msem, ssem, *gs):
    net = Net(ssem)
    u, z, c = net.u, net.z, net.c
    me = u * 4 + z
    rows, width = X.shape[2], X.shape[3]
    partner = (u, z, 1 - c)
    own = pltpu.make_async_copy(x_ref, X.at[u, z], lsem.at[0])
    own.start()
    own_w = pltpu.make_async_copy(cols.at[me], wf.at[me, c], lsem.at[1])
    own_w.start()
    greet(net)
    own.wait()
    ga = Gather(net, rows, cut, lambda uu, zz, lo, n: X.at[uu, zz, pl.ds(lo, n), :],
                lambda zz, lo, n: X.at[:, zz, pl.ds(lo, n), :], gs)
    ga.begin()
    each_chip(net, lambda t, dev: remote(cols.at[t], wf.at[me, c], msem.at[0], msem.at[1], dev).start())

    def plane(zz):
        def chunk(uu, _):
            slot = lax.rem(uu, 2)
            k = uu * 4 + zz

            def norm(i, _):
                sl = pl.ds(pl.multiple_of(i * 16, 16), 16)
                v = X[uu, zz, sl, :].astype(F32)
                r = lax.rsqrt(jnp.mean(v * v, axis=1, keepdims=True) + EPS)
                nb[slot, sl, :] = (v * r * gain[...]).astype(BF)
                return 0

            def stored(s):
                return pltpu.make_async_copy(nb.at[s], n1_o.at[k], nsem.at[s])

            pl.when(uu >= 2)(lambda: stored(slot).wait())
            lax.fori_loop(0, rows // 16, norm, 0)
            stored(slot).start()
            got = dot(nb[slot], wf[...].reshape(width, wf.shape[-1]), ((1,), (0,)))
            lin[k] = got
            q, kk = got[:, :128], got[:, 128:256]
            sums[pl.ds(k, 1), :] = row_sums(q * q)
            sums[pl.ds(16 + k, 1), :] = row_sums(kk * kk)
            return 0

        lax.fori_loop(0, 4, chunk, 0)
        for s in (0, 1):
            pltpu.make_async_copy(nb.at[s], n1_o.at[0], nsem.at[s]).wait()

    def compute(s):
        for zz, cond in ga.planes(s):
            if cond is None:
                plane(zz)
            else:
                pl.when(cond)(lambda zz=zz: plane(zz))

    ga.begin2()
    ga.along(1)
    ga.quads(0)
    ga.cross(0)
    own_w.wait()
    landed(wf.at[pl.ds(0, 15), 0], msem.at[1])
    to_partner = remote(wf.at[:, c], wf.at[:, c], msem.at[2], msem.at[3], partner)
    to_partner.start()
    ga.along(2)
    ga.quads(1)
    ga.cross(1)
    ga.settle(0)
    landed(wf.at[:, 1 - c], msem.at[3])
    compute(0)
    ga.along(3)
    ga.quads(2)
    ga.cross(2)
    ga.settle(1)
    compute(1)
    ga.quads(3)
    ga.cross(3)
    ga.settle(2)
    compute(2)
    ga.settle(3)
    compute(3)
    landed(wf.at[pl.ds(0, 15), 0], msem.at[0])
    landed(wf.at[:, c], msem.at[2])
    share_sums(net, sums, sums_all, tot, lsem.at[2], msem.at[4], msem.at[5])
    net.finish()


def run_qkv(x, cols, gain, cid, cut=96):
    R, D = x.shape
    N = cols.shape[2]
    DMA = pltpu.SemaphoreType.DMA
    S = jax.ShapeDtypeStruct
    V = lambda *s: pltpu.VMEM(s, BF)
    A = pl.BlockSpec(memory_space=pl.ANY)
    M = pl.BlockSpec(memory_space=pltpu.VMEM)
    return pl.pallas_call(
        functools.partial(qkv_kernel, cut),
        out_shape=(S((16, R, D), BF), S((16, R, N), F32), S((16, 2, R // 2, N), BF), S((32, 128), F32)),
        in_specs=[A, A, M],
        out_specs=(A, M, M, M),
        scratch_shapes=[V(4, 4, R, D), V(2, R, D), pltpu.VMEM((32, 128), F32), pltpu.VMEM((16, 32, 128), F32),
                        DMA((3,)), DMA((2,)), DMA((6,)), DMA((64,))] + ag_sems(),
        compiler_params=pltpu.CompilerParams(collective_id=cid, has_side_effects=True, vmem_limit_bytes=40 * 2**20),
        name="project",
    )(x, cols, gain)


def group_of(t):
    g = t // 2
    return jnp.where(g == 0, 3, jnp.where(g == 1, 0, jnp.where(g == 2, 2, 1)))


def expert_kernel(cut, n2, cot, share, gate, up, down, d_n2, p_out, n2_o, other, dg_o, du_o, dd_o,
                  X, C, GU, W, A, hid, pb, fs, lsem, wsem, wrs, psem, tsem, osem, ors, fsem, sa, sc_, sr, *scr):
    ga_sems, gc_sems, rs_bufs = scr[:7], scr[7:14], scr[14:]
    na, nc, nr = Net(sa), Net(sc_), Net(sr)
    u, z, c = na.u, na.z, na.c
    partner = (u, z, 1 - c)
    rows, width = X.shape[2], X.shape[3]
    ff = W.shape[0]
    half, half_ff = gate.shape[0], down.shape[0]
    tokens = 16 * rows
    tile = 256
    first = [pltpu.make_async_copy(n2, X.at[u, z], lsem.at[0]), pltpu.make_async_copy(cot, C.at[u, z], lsem.at[1])]

    def weights():
        mine = pl.ds(pl.multiple_of(c * half, half), half)
        mine_ff = pl.ds(pl.multiple_of(c * half_ff, half_ff), half_ff)
        return ((gate, GU.at[mine, pl.ds(0, ff)]), (up, GU.at[mine, pl.ds(ff, ff)]), (down, W.at[mine_ff, :]))

    own_w = [pltpu.make_async_copy(a, b, lsem.at[2 + i]) for i, (a, b) in enumerate(weights())]
    for one in first + own_w:
        one.start()
    na.barrier((partner,))
    first[0].wait()

    def gather(net, buf, sems):
        return Gather(net, rows, cut, lambda uu, zz, lo, n: buf.at[uu, zz, pl.ds(lo, n), :],
                      lambda zz, lo, n: buf.at[:, zz, pl.ds(lo, n), :], sems)

    ga, gc = gather(na, X, ga_sems), gather(nc, C, gc_sems)
    ga.begin()
    sent_w = [remote(a, b, wsem.at[i], wrs.at[i], partner) for i, (a, b) in enumerate(weights())]
    for one in sent_w:
        one.start()

    def forward(zz):
        pltpu.make_async_copy(X.at[:, zz], n2_o.at[:, zz], psem.at[1]).start()

        def part(j, _):
            quads = pl.ds(2 * j, 2)

            def inner(n, _):
                gcols = pl.ds(pl.multiple_of(n * tile, tile), tile)
                ucols = pl.ds(pl.multiple_of(ff + n * tile, tile), tile)
                xv = X[quads, zz].reshape(2 * rows, width)
                g = dot(xv, GU[:, gcols], ((1,), (0,)))
                uu = dot(xv, GU[:, ucols], ((1,), (0,)))
                hid[quads, zz, :, gcols] = (g * jax.nn.sigmoid(g) * uu).astype(BF).reshape(2, rows, tile)
                A[quads, zz, :, gcols] = g.astype(BF).reshape(2, rows, tile)
                A[quads, zz, :, ucols] = uu.astype(BF).reshape(2, rows, tile)
                return 0

            lax.fori_loop(0, ff // tile, inner, 0)
            weight = share[quads, zz]

            def outer(n, _):
                cols = pl.ds(pl.multiple_of(n * tile, tile), tile)
                made = dot(hid[quads, zz].reshape(2 * rows, ff), W[:, cols], ((1,), (0,)))
                made = made.astype(BF).astype(F32).reshape(2, rows, tile)
                pb[:, :, cols] = (weight * made).astype(BF)
                return 0

            lax.fori_loop(0, width // tile, outer, 0)
            out = pltpu.make_async_copy(pb, p_out.at[quads, zz], psem.at[0])
            out.start()
            out.wait()
            return 0

        lax.fori_loop(0, 2, part, 0)

    def planes(s):
        if s == 0:
            forward(z)
            return

        def one(d, _):
            zz = jnp.where(d == 0, z - s, z + s)
            pl.when(jnp.logical_and(zz >= 0, zz < 4))(lambda: forward(zz))
            return 0

        lax.fori_loop(0, 2, one, 0)

    ga.begin2()
    ga.along(1)
    ga.quads(0)
    ga.cross(0)
    ga.along(2)
    ga.quads(1)
    ga.cross(1)
    first[1].wait()
    gc.begin()
    ga.settle(0)
    for one in own_w:
        one.wait()
    for one in sent_w:
        one.wait_recv()
    planes(0)
    gc.begin2()
    ga.along(3)
    ga.quads(2)
    ga.cross(2)
    ga.settle(1)
    gc.along(1)
    gc.quads(0)
    gc.cross(0)
    planes(1)
    ga.quads(3)
    ga.cross(3)
    ga.settle(2)
    gc.along(2)
    gc.quads(1)
    gc.cross(1)
    planes(2)
    ga.settle(3)
    gc.along(3)
    gc.quads(2)
    gc.cross(2)
    planes(3)
    gc.quads(3)
    gc.cross(3)
    for s in range(4):
        gc.settle(s)
    na.finish()
    nc.finish()
    for one in sent_w:
        one.wait_send()
    landed(X, psem.at[1])
    sc = Scatter(nr, cut, X, rs_bufs)

    def backward(t):
        zd, j = group_of(t), lax.rem(t, 2)
        quads = pl.ds(2 * j, 2)

        def scale(i, _):
            sl = pl.ds(pl.multiple_of(i * 16, 16), 16)
            C[quads, zd, sl, :] = (share[quads, zd, sl, :] * C[quads, zd, sl, :].astype(F32)).astype(BF)
            return 0

        lax.fori_loop(0, rows // 16, scale, 0)

        def inner(n, _):
            gcols = pl.ds(pl.multiple_of(n * tile, tile), tile)
            ucols = pl.ds(pl.multiple_of(ff + n * tile, tile), tile)
            dh = dot(C[quads, zd].reshape(2 * rows, width), W[gcols, :], ((1,), (1,)))
            g = wide(A[quads, zd, :, gcols]).reshape(2 * rows, tile)
            uu = wide(A[quads, zd, :, ucols]).reshape(2 * rows, tile)
            s = jax.nn.sigmoid(g)
            A[quads, zd, :, gcols] = (dh * uu * s * (1.0 + g * (1.0 - s))).astype(BF).reshape(2, rows, tile)
            A[quads, zd, :, ucols] = (dh * g * s).astype(BF).reshape(2, rows, tile)
            return 0

        lax.fori_loop(0, ff // tile, inner, 0)

        def outer(n, _):
            cols = pl.ds(pl.multiple_of(n * tile, tile), tile)
            back = dot(A[quads, zd].reshape(2 * rows, 2 * ff), GU[cols, :], ((1,), (1,)))
            X[quads, zd, :, cols] = back.astype(BF).reshape(2, rows, tile)
            return 0

        lax.fori_loop(0, width // tile, outer, 0)

    def acts(steps, t):
        for at, todo in steps.items():
            def act(todo=todo):
                for one in todo:
                    one()
            pl.when(t == at)(act)

    steps = {
        1: [lambda: sc.first(3)],
        2: [lambda: sc.mids(3)],
        3: [lambda: sc.first(0), lambda: sc.bhop(3, 1), lambda: sc.hop(3, 0)],
        4: [lambda: sc.mids(0), lambda: sc.bhop(3, 2), lambda: sc.hop(3, 1)],
        5: [lambda: sc.first(2), lambda: sc.bhop(0, 2), lambda: sc.hop(0, 3), lambda: sc.hop(3, 2)],
        6: [lambda: sc.mids(2), lambda: sc.bhop(0, 1), lambda: sc.hop(0, 2)],
        7: [lambda: sc.first(1), lambda: sc.bhop(2, 1), lambda: sc.hop(0, 1), lambda: sc.hop(2, 0), lambda: sc.hop(2, 3)],
    }

    def turn(t, _):
        backward(t)
        acts(steps, t)
        return 0

    lax.fori_loop(0, 8, turn, 0)

    GU4 = GU.reshape(4, 4, rows, width)
    left = W.at[pl.ds(0, tile), :]

    def tile_load(k, which):
        slot = lax.rem(k, 2)
        cols = pl.ds(pl.multiple_of((which * 4 + k) * tile, tile), tile)
        return pltpu.make_async_copy(
            n2_o.at[:, :, :, cols], GU4.at[:, :, :, pl.ds(pl.multiple_of(slot * tile, tile), tile)], tsem.at[slot])

    def left_tokens(k):
        cols = pl.ds(pl.multiple_of(lax.rem(k, 2) * tile, tile), tile)

        def one(b, _):
            sl = pl.ds(pl.multiple_of(b * tile, tile), tile)
            left[:, sl] = GU[sl, cols].T
            return 0

        lax.fori_loop(0, tokens // tile, one, 0)

    def left_hidden(k, which):
        cols = pl.ds(pl.multiple_of((which * 2 + k) * tile, tile), tile)
        flat = hid.reshape(tokens, ff)

        def one(b, _):
            sl = pl.ds(pl.multiple_of(b * tile, tile), tile)
            left[:, sl] = flat[sl, cols].T
            return 0

        lax.fori_loop(0, tokens // tile, one, 0)

    def products(right, store):
        flat = right.reshape(tokens, width)

        def one(n, _):
            cols = pl.ds(pl.multiple_of(n * 512, 512), 512)
            store(cols, n, dot(left[...], flat[:, cols], ((1,), (0,))))
            return 0

        lax.fori_loop(0, width // 512, one, 0)

    def sent(k):
        slot = W.at[pl.ds(pl.multiple_of(tile + lax.rem(k, 2) * tile, tile), tile), :]
        return slot, remote(slot, other.at[k], osem.at[k], ors.at[k], partner)

    tile_load(0, 1 - c).start()

    def other_tile(k, _):
        slot, copy = sent(k)

        @pl.when(k >= 2)
        def _():
            sent(k - 2)[1].wait_send()

        def store(cols, n, v):
            slot[:, cols] = v.astype(BF)

        @pl.when(k < 4)
        def _():
            pl.when(k < 3)(lambda: tile_load(k + 1, 1 - c).start())
            tile_load(k, 1 - c).wait()
            left_tokens(k)
            products(A, store)

        @pl.when(k >= 4)
        def _():
            left_hidden(k - 4, 1 - c)
            products(C, store)

        copy.start()
        acts({0: [lambda: sc.mids(1)],
              1: [lambda: sc.hop(2, 1), lambda: sc.bhop(1, 2)],
              2: [lambda: sc.hop(1, 0), lambda: sc.hop(1, 3)],
              3: [sc.bquad],
              4: [lambda: sc.hop(1, 2)],
              5: [sc.bquad2]}, k)
        return 0

    lax.fori_loop(0, 6, other_tile, 0)

    def store_out(sl, v):
        d_n2[sl, :] = v

    tile_load(0, c).start()
    got = W.at[pl.ds(3 * tile, tile), :]

    def flush(k, h):
        i = pl.ds(pl.multiple_of(lax.rem(k, 4) * tile, tile), tile)

        def go(dst):
            pltpu.make_async_copy(fs.at[h], dst, fsem.at[h]).start()

        pl.when(k < 4)(lambda: go((dg_o, du_o)[h].at[i, :]))
        pl.when(k >= 4)(lambda: go(dd_o.at[i, pl.ds(h * 1024, 1024)]))

    def own_tile(k, _):
        fetch = pltpu.make_async_copy(other.at[k], got, lsem.at[0])
        landed(other.at[k], ors.at[k])
        fetch.start()

        def finish(right):
            flat = right.reshape(tokens, width)
            fetch.wait()
            for h in (0, 1):
                pl.when(k > 0)(lambda: landed(fs.at[h], fsem.at[h]))
                for n in (0, 1):
                    cols = pl.ds(h * 1024 + n * 512, 512)
                    fs[h, :, n * 512 : (n + 1) * 512] = dot(left[...], flat[:, cols], ((1,), (0,))) + wide(got[:, cols])
                flush(k, h)

        @pl.when(k < 4)
        def _():
            pl.when(k < 3)(lambda: tile_load(k + 1, c).start())
            tile_load(k, c).wait()
            left_tokens(k)
            finish(A)

        @pl.when(k >= 4)
        def _():
            left_hidden(k - 4, c)
            finish(C)

        acts({0: [lambda: sc.last(store_out)]}, k)
        return 0

    lax.fori_loop(0, 6, own_tile, 0)
    for h in (0, 1):
        landed(fs.at[h], fsem.at[h])
    for k in (4, 5):
        sent(k)[1].wait_send()
    nr.finish()


def run_expert(n2, cot, share, gate, up, down, cid, cut=96):
    R, D = n2.shape
    half, ff = gate.shape
    DMA = pltpu.SemaphoreType.DMA
    S = jax.ShapeDtypeStruct
    V = lambda *s: pltpu.VMEM(s, BF)
    A = pl.BlockSpec(memory_space=pl.ANY)
    M = pl.BlockSpec(memory_space=pltpu.VMEM)
    return pl.pallas_call(
        functools.partial(expert_kernel, cut),
        out_shape=(S((R, D), F32), S((4, 4, R, D), BF), S((4, 4, R, D), BF), S((6, 256, D), BF),
                   S((half, ff), F32), S((half, ff), F32), S(down.shape, F32)),
        in_specs=[A, A, M, A, A, A],
        out_specs=(M,) + (A,) * 6,
        scratch_shapes=[V(4, 4, R, D), V(4, 4, R, D), V(D, 2 * ff), V(ff, D), V(4, 4, R, 2 * ff), V(4, 4, R, ff),
                        V(2, R, D), pltpu.VMEM((2, 256, 1024), F32),
                        DMA((5,)), DMA((3,)), DMA((3,)), DMA((2,)), DMA((2,)), DMA((6,)), DMA((6,)), DMA((2,)),
                        DMA((64,)), DMA((64,)), DMA((96,))] + ag_sems() + ag_sems() + rs_scratch(cut, R, D),
        compiler_params=pltpu.CompilerParams(collective_id=cid, has_side_effects=True, vmem_limit_bytes=63 * 2**20),
        name="expert",
    )(n2, cot, share, gate, up, down)


def stages(sc, store):
    def each(f, *pairs):
        return [functools.partial(f, *p) for p in pairs]

    return [
        each(sc.first, (3,), (0,), (2,), (1,)),
        each(sc.mids, (3,), (0,), (2,), (1,)),
        each(sc.hop, (3, 0), (0, 3)) + each(sc.bhop, (3, 1), (0, 2)),
        each(sc.hop, (2, 0), (1, 3)) + each(sc.bhop, (2, 1), (1, 2)),
        each(sc.hop, (3, 1), (0, 2)) + each(sc.bhop, (3, 2), (0, 1)),
        each(sc.hop, (1, 0), (2, 3)) + [sc.bquad],
        each(sc.hop, (2, 1), (1, 2)),
        each(sc.hop, (3, 2), (0, 1)) + [sc.bquad2],
        [functools.partial(sc.last, store)],
    ]


def run_steps(steps):
    for one in steps:
        one()


def greet_all(net, count=32):
    bar = pltpu.get_barrier_semaphore()
    me = net.u * 8 + net.z * 2 + net.c

    def hello(j, _):
        t = lax.rem(me + j, count)
        pl.semaphore_signal(bar, inc=1, device_id=(t // 8, lax.rem(t, 8) // 2, lax.rem(t, 2)), device_id_type=MESH)
        return 0

    lax.fori_loop(1, count, hello, 0)
    pl.semaphore_wait(bar, count - 1)


def finish_kernel(cut, d_lin, wf, n1, p_out, x_in, residual, d_res, gain, d_gain_two,
                  output, d_inputs, d_wq, d_wk, d_wv, gains_o,
                  P, PO, nt, left, keep, give, got, send, recv, d_n1, d_gain, gb, gr,
                  lsem, tsem, msem, s1, s2, *bufs):
    net, net2 = Net(s1), Net(s2)
    u, z, c = net.u, net.z, net.c
    me = u * 4 + z
    rows, width = P.shape[2], P.shape[3]
    lanes = d_lin.shape[2]
    tokens = 16 * rows
    tile = 256
    partner = (u, z, 1 - c)
    half = len(bufs) // 2
    sc1, sc2 = Scatter(net, cut, P, bufs[:half]), Scatter(net2, cut, PO, bufs[half:])
    load = pltpu.make_async_copy(p_out, PO, lsem.at[0])
    load.start()

    def tile_load(k):
        slot = lax.rem(k, 2)
        return pltpu.make_async_copy(n1.at[:, :, pl.ds(pl.multiple_of(k * tile, tile), tile)], nt.at[slot], tsem.at[slot])

    tile_load(0).start()
    greet_all(net)

    def group(zd):
        def one(n, _):
            cols = pl.ds(pl.multiple_of(n * 512, 512), 512)
            w = wf.reshape(width, lanes)
            for q in range(4):
                P[q, zd, :, cols] = dot(d_lin[q * 4 + zd], w[cols, :], ((1,), (1,))).astype(BF)
            return 0

        lax.fori_loop(0, width // 512, one, 0)

    for zd in (3, 0, 2, 1):
        group(zd)
        sc1.first(zd)
    load.wait()

    def store1(sl, v):
        d_n1[sl, :] = v

    def store2(sl, v):
        output[sl, :] = residual[sl, :] + v

    one, two = stages(sc1, store1), stages(sc2, store2)

    def grads(k):
        if k < 7:
            tile_load(k + 1).start()
        tile_load(k).wait()
        slot = k % 2
        flat = nt.at[slot].reshape(tokens, tile)

        def turn(b, _):
            sl = pl.ds(pl.multiple_of(b * tile, tile), tile)
            left[:, sl] = flat[sl, :].T
            return 0

        lax.fori_loop(0, tokens // tile, turn, 0)
        made = dot(left[...], d_lin[...].reshape(tokens, lanes), ((1,), (0,)))
        for i in range(2):
            first, second = made[i * 128 : i * 128 + 64], made[i * 128 + 64 : (i + 1) * 128]
            keep[2 * k + i] = jnp.where(c == 0, first, second)
            give[2 * k + i] = jnp.where(c == 0, second, first).astype(BF)

    run_steps(two[0])
    grads(0)
    run_steps(one[1])
    grads(1)
    run_steps(one[2])
    grads(2)
    run_steps(two[1])
    run_steps(one[3])
    grads(3)
    run_steps(two[2])
    run_steps(one[4])
    grads(4)
    run_steps(two[3])
    run_steps(one[5])
    grads(5)
    run_steps(one[6])
    grads(6)
    run_steps(two[4])
    run_steps(one[7])
    grads(7)
    across = remote(give, got, msem.at[0], msem.at[1], partner)
    across.start()
    run_steps(two[5])
    landed(got, msem.at[1])

    def total(e, _):
        send[e] = (keep[e] + wide(got[e])).astype(BF)
        return 0

    lax.fori_loop(0, 16, total, 0)
    each_chip(net, lambda t, dev: remote(send.at[t], recv.at[me], msem.at[2], msem.at[3], dev).start())
    recv[me] = send[me]
    run_steps(one[8])
    d_gain[...] = jnp.zeros_like(d_gain)

    def norm_back(i, _):
        sl = pl.ds(pl.multiple_of(i * 16, 16), 16)
        v, d = wide(x_in[sl, :]), d_n1[sl, :]
        r = lax.rsqrt(jnp.mean(v * v, axis=1, keepdims=True) + EPS)
        scaled = d * gain[...]
        inner = jnp.mean(scaled * v, axis=1, keepdims=True)
        d_inputs[sl, :] = d_res[sl, :] + r * scaled - v * (r * r * r * inner)
        d_gain[...] += jnp.sum(d * v * r, axis=0, keepdims=True)
        return 0

    lax.fori_loop(0, rows // 16, norm_back, 0)
    for e in range(16):
        gb[e, 0:1, :] = d_gain[:, e * 128 : (e + 1) * 128]
        gb[e, 1:2, :] = d_gain_two[:, e * 128 : (e + 1) * 128]
    dev_me = me * 2 + c

    def tell(j, _):
        t = lax.rem(dev_me + j, 32)
        remote(gb.at[t // 2], gr.at[dev_me], msem.at[4], msem.at[5], (t // 8, lax.rem(t, 8) // 2, lax.rem(t, 2))).start()
        return 0

    lax.fori_loop(1, 32, tell, 0)
    gr[dev_me] = gb[me]
    run_steps(two[6])
    run_steps(two[7])
    landed(recv.at[pl.ds(0, 15)], msem.at[3])
    for e in range(16):
        piece = wide(recv[e])
        for i, out in enumerate((d_wq, d_wk, d_wv)):
            out[:, e * 128 : (e + 1) * 128] = piece[:, i * 128 : (i + 1) * 128]
    landed(gr.at[pl.ds(0, 31)], msem.at[5])
    sums = gr[0]
    for i in range(1, 32):
        sums = sums + gr[i]
    gains_o[...] = sums
    run_steps(two[8])
    landed(give, msem.at[0])
    landed(recv.at[pl.ds(0, 15)], msem.at[2])
    landed(gr.at[pl.ds(0, 31)], msem.at[4])
    net.finish()
    net2.finish()


def run_finish(d_lin, wf, n1, p_out, x_in, residual, d_res, gain, d_gain_two, cid, cut=96):
    R, D = x_in.shape
    N = d_lin.shape[2]
    DMA = pltpu.SemaphoreType.DMA
    S = jax.ShapeDtypeStruct
    V = lambda *s: pltpu.VMEM(s, BF)
    VF = lambda *s: pltpu.VMEM(s, F32)
    A = pl.BlockSpec(memory_space=pl.ANY)
    M = pl.BlockSpec(memory_space=pltpu.VMEM)
    own = S((R // 2, D), F32)
    return pl.pallas_call(
        functools.partial(finish_kernel, cut),
        out_shape=(S((R, D), F32), S((R, D), F32), own, own, own, S((8, 128), F32)),
        in_specs=[M, M, A, A] + [M] * 5,
        out_specs=(M,) * 6,
        scratch_shapes=[V(4, 4, R, D), V(4, 4, R, D), V(2, 16, R, 256), V(256, 16 * R), VF(16, 64, N), V(16, 64, N),
                        V(16, 64, N), V(16, 64, N), V(16, 64, N), VF(R, D), VF(1, D), VF(16, 8, 128), VF(32, 8, 128),
                        DMA((1,)), DMA((2,)), DMA((6,)), DMA((64,)), DMA((64,))] + rs_scratch(cut, R, D) + rs_scratch(cut, R, D),
        compiler_params=pltpu.CompilerParams(collective_id=cid, has_side_effects=True, vmem_limit_bytes=63 * 2**20),
        name="finish",
    )(d_lin, wf, n1, p_out, x_in, residual, d_res, gain, d_gain_two)

def band_scores(q, k, q_seg, k_seg, scale, reach):
    scores = dot(q, k, ((1,), (1,))) * scale
    q_at = lax.broadcasted_iota(jnp.int32, scores.shape, 0)
    k_at = lax.broadcasted_iota(jnp.int32, scores.shape, 1)
    return scores, (k_seg == q_seg) & (k_at <= q_at + reach)


def turned(v, cosine, sine):
    return v * cosine + pltpu.roll(v, 64, axis=1) * sine


def turned_back(v, cosine, sine):
    return v * cosine - pltpu.roll(v, 64, axis=1) * sine


def attend_kernel(scale, pads, lin, tot, cosine, sine, gq, gk, q_seg, k_seg, w_own, x_in, gain, wo_o, q_rot, kv, o_ref, lse,
                  att, residual, n2, wo, lsem, msem, ssem, *gs):
    net = Net(ssem)
    u, z, c = net.u, net.z, net.c
    me = u * 4 + z
    rows = x_in.shape[0]
    width = x_in.shape[1]
    reach = pads * 2 * rows
    partner = (u, z, 1 - c)
    own = pltpu.make_async_copy(w_own, wo.at[u, z, c], lsem.at[0])
    own.start()
    greet(net)
    own.wait()
    ga = Gather(net, rows // 2, rows // 2, lambda uu, zz, lo, n: wo.at[uu, zz, c, pl.ds(lo, n), :], None, gs)
    ga.begin()
    for i in range(pads):
        kv[:, i] = jnp.zeros(kv.shape[:1] + kv.shape[2:], BF)

    def ready(i, _):
        both = lin[i]
        rq = lax.rsqrt(column(tot[pl.ds(i, 1), :]) / width + EPS)
        rk = lax.rsqrt(column(tot[pl.ds(16 + i, 1), :]) / width + EPS)
        cs, sn = cosine[i], sine[i]
        q_rot[i] = turned(both[:, :128] * rq * gq[...], cs, sn).astype(BF)
        kv[0, pads + i, c] = turned(both[:, 128:256] * rk * gk[...], cs, sn).astype(BF)
        kv[1, pads + i, c] = both[:, 256:].astype(BF)
        return 0

    lax.fori_loop(0, 16, ready, 0)
    mine = kv.at[:, pl.ds(pads, 16), c]
    to_partner = remote(mine, mine, msem.at[0], msem.at[1], partner)
    to_partner.start()
    ga.along(1)
    ga.cross(0)
    landed(kv.at[:, pl.ds(pads, 16), 1 - c], msem.at[1])

    def block(j, _):
        i = lax.rem(me + 1 + j, 16)
        first = 2 * i + c
        band = pl.ds(pl.multiple_of(first * rows, rows), rows + reach)
        kf, vf = kv.at[0].reshape((pads + 16) * 2 * rows, 128), kv.at[1].reshape((pads + 16) * 2 * rows, 128)
        scores, allowed = band_scores(q_rot[i], kf[band, :], q_seg[i], k_seg[:, band], scale, reach)
        scores = jnp.where(allowed, scores, NEG)
        top = jnp.max(scores, axis=1, keepdims=True)
        weights = jnp.where(allowed, jnp.exp(scores - top), 0.0)
        total = jnp.sum(weights, axis=1, keepdims=True)
        probs = (weights / total).astype(BF)
        o_ref[i] = dot(probs, vf[band, :], ((1,), (0,))).astype(BF)
        lse[i] = top + jnp.log(total)

        @pl.when(j < 15)
        def _():
            remote(o_ref.at[i], att.at[me], msem.at[2], msem.at[3], (i // 4, lax.rem(i, 4), c)).start()

        return 0

    lax.fori_loop(0, 5, block, 0)
    ga.along(2)
    ga.cross(1)
    lax.fori_loop(5, 10, block, 0)
    ga.along(3)
    ga.cross(2)
    lax.fori_loop(10, 16, block, 0)
    ga.cross(3)
    for s in range(4):
        ga.settle(s)
    rest = remote(wo.at[:, :, c], wo.at[:, :, c], msem.at[4], msem.at[5], partner)
    rest.start()
    att[me] = o_ref[me]
    part = att.at[pl.ds(0, 15)]
    landed(part, msem.at[3])
    landed(wo.at[:, :, 1 - c], msem.at[5])
    keep = pltpu.make_async_copy(wo, wo_o, lsem.at[1])
    keep.start()
    tile = 256

    def out(n, _):
        cols = pl.ds(pl.multiple_of(n * tile, tile), tile)
        acc = x_in[:, cols].astype(F32)
        for e in range(0, 16, 2):
            pair = jnp.concatenate([att[e], att[e + 1]], axis=1)
            acc = acc + dot(pair, wo[e // 4, pl.ds(e % 4, 2), :, :, cols].reshape(256, tile), ((1,), (0,)))
        residual[:, cols] = acc
        return 0

    lax.fori_loop(0, width // tile, out, 0)

    def norm(i, _):
        sl = pl.ds(pl.multiple_of(i * 16, 16), 16)
        v = residual[sl, :]
        r = lax.rsqrt(jnp.mean(v * v, axis=1, keepdims=True) + EPS)
        n2[sl, :] = (v * r * gain[...]).astype(BF)
        return 0

    lax.fori_loop(0, rows // 16, norm, 0)
    landed(mine, msem.at[0])
    landed(part, msem.at[2])
    landed(wo.at[:, :, c], msem.at[4])
    keep.wait()
    net.finish()


def run_attend(scale, pads, lin, tot, cosine, sine, gq, gk, q_seg, k_seg, w_own, x_in, gain, cid):
    R, D = x_in.shape
    DMA = pltpu.SemaphoreType.DMA
    S = jax.ShapeDtypeStruct
    A = pl.BlockSpec(memory_space=pl.ANY)
    M = pl.BlockSpec(memory_space=pltpu.VMEM)
    wo = (4, 4, 2, R // 2, D)
    return pl.pallas_call(
        functools.partial(attend_kernel, scale, pads),
        out_shape=(S(wo, BF), S((16, R, 128), BF), S((2, pads + 16, 2, R, 128), BF), S((16, R, 128), BF),
                   S((16, R, 1), F32), S((16, R, 128), BF), S((R, D), F32), S((R, D), BF)),
        in_specs=[M] * 8 + [A, M, M],
        out_specs=(A,) + (M,) * 7,
        scratch_shapes=[pltpu.VMEM(wo, BF), DMA((2,)), DMA((6,)), DMA((64,))] + ag_sems(),
        compiler_params=pltpu.CompilerParams(collective_id=cid, has_side_effects=True, vmem_limit_bytes=48 * 2**20),
        name="attend",
    )(lin, tot, cosine, sine, gq, gk, q_seg, k_seg, w_own, x_in, gain)


def attend_back_kernel(scale, pads, cut, d_res, wo_h, att, q_rot, kv, q_seg, k_seg, lse, o_ref, lin, tot, cosine, sine, gq, gk,
                       d_lin, d_gains, d_wo, P, PG, PT, wsum, wo, d_mine, d_out, d_q, d_k, d_v, other, got, d_un, sums, sums_all, inner,
                       lsem, msem, ssem, *bufs):
    net = Net(ssem)
    sc = Scatter(net, cut, P, bufs)
    u, z, c = net.u, net.z, net.c
    me = u * 4 + z
    rows, width = d_res.shape
    reach = pads * 2 * rows
    partner = (u, z, 1 - c)
    load = pltpu.make_async_copy(wo_h, wo, lsem.at[0])
    load.start()
    greet(net)
    load.wait()

    def send(j, _):
        e = lax.rem(me + 1 + j, 16)
        piece = dot(d_res[...], wo[e // 4, lax.rem(e, 4)].reshape(128, width), ((1,), (1,))).astype(BF)

        @pl.when(j < 15)
        def _():
            d_mine[e] = piece
            remote(d_mine.at[e], d_out.at[me], msem.at[0], msem.at[1], (e // 4, lax.rem(e, 4), c)).start()

        @pl.when(j == 15)
        def _():
            d_out[me] = piece

        return 0

    lax.fori_loop(0, 16, send, 0)
    side = width // 2
    own_cols = pl.ds(pl.multiple_of(c * side, side), side)
    give_cols = pl.ds(pl.multiple_of((1 - c) * side, side), side)

    def outer(e, _):
        left = att[e].T
        P[e // 4, lax.rem(e, 4)] = dot(left, d_res[:, own_cols], ((1,), (0,))).astype(BF)
        PG[e // 4, lax.rem(e, 4)] = dot(left, d_res[:, give_cols], ((1,), (0,))).astype(BF)
        return 0

    lax.fori_loop(0, 16, outer, 0)
    across = remote(PG, PT, msem.at[6], msem.at[7], partner)
    across.start()
    d_k[...] = jnp.zeros_like(d_k)
    d_v[...] = jnp.zeros_like(d_v)
    landed(d_out.at[pl.ds(0, 15)], msem.at[1])
    count = (pads + 16) * 2 * rows

    def block(i, _):
        band = pl.ds(pl.multiple_of((2 * i + c) * rows, rows), rows + reach)
        kf, vf = kv.at[0].reshape(count, 128), kv.at[1].reshape(count, 128)
        q, k, dd = q_rot[i], kf[band, :], d_out[i]
        scores, allowed = band_scores(q, k, q_seg[i], k_seg[:, band], scale, reach)
        probs = jnp.where(allowed, jnp.exp(scores - lse[i]), 0.0)
        d_probs = dot(dd, vf[band, :], ((1,), (1,)))
        delta = jnp.sum(dd.astype(F32) * o_ref[i].astype(F32), axis=1, keepdims=True)
        d_scores = (probs * (d_probs - delta)).astype(BF)
        d_q[i] = (dot(d_scores, k, ((1,), (0,))) * scale).astype(BF)
        d_k[band, :] += dot(d_scores, q, ((0,), (0,))) * scale
        d_v[band, :] += dot(probs.astype(BF), dd, ((0,), (0,)))
        return 0

    def store(sl, v):
        wsum[sl, :] = v

    steps = stages(sc, store)
    lax.fori_loop(0, 3, block, 0)
    landed(PT, msem.at[7])

    def join(e, _):
        def strip(sl):
            at = (e // 4, lax.rem(e, 4), sl, slice(None))
            P[at] = (wide(P[at]) + wide(PT[at])).astype(BF)

        strips(rows, strip)
        return 0

    lax.fori_loop(0, 16, join, 0)
    run_steps(steps[0])
    lax.fori_loop(3, 6, block, 0)
    run_steps(steps[1])
    lax.fori_loop(6, 8, block, 0)
    run_steps(steps[2])
    lax.fori_loop(8, 10, block, 0)
    run_steps(steps[3])
    lax.fori_loop(10, 13, block, 0)
    run_steps(steps[4])
    lax.fori_loop(13, 16, block, 0)

    def pack(i, _):
        at = pl.ds(pl.multiple_of(((pads + i) * 2 + 1 - c) * rows, rows), rows)
        other[0, i] = d_k[at, :].astype(BF)
        other[1, i] = d_v[at, :].astype(BF)
        return 0

    lax.fori_loop(0, 16, pack, 0)
    remote(other, got, msem.at[2], msem.at[3], partner).start()
    run_steps(steps[5])
    landed(got, msem.at[3])
    d_gains[...] = jnp.zeros_like(d_gains)

    def undo(i, _):
        at = pl.ds(pl.multiple_of(((pads + i) * 2 + c) * rows, rows), rows)
        cs, sn = cosine[i], sine[i]
        both = lin[i]
        rq = lax.rsqrt(column(tot[pl.ds(i, 1), :]) / width + EPS)
        rk = lax.rsqrt(column(tot[pl.ds(16 + i, 1), :]) / width + EPS)
        dk = (d_k[at, :] + wide(got[0, i])).astype(BF).astype(F32)
        d_lin[i, :, 256:] = (d_v[at, :] + wide(got[1, i])).astype(BF)
        uq = turned_back(wide(d_q[i]), cs, sn)
        uk = turned_back(dk, cs, sn)
        q, k = both[:, :128], both[:, 128:256]
        d_gains[0:1, :] += jnp.sum(uq * q * rq, axis=0, keepdims=True)
        d_gains[1:2, :] += jnp.sum(uk * k * rk, axis=0, keepdims=True)
        uq, uk = uq * gq[...], uk * gk[...]
        d_un[0, i] = uq
        d_un[1, i] = uk
        sums[pl.ds(i, 1), :] = row_sums(uq * q)
        sums[pl.ds(16 + i, 1), :] = row_sums(uk * k)
        return 0

    lax.fori_loop(0, 16, undo, 0)
    run_steps(steps[6])
    share_sums(net, sums, sums_all, inner, lsem.at[1], msem.at[4], msem.at[5])

    def finish(i, _):
        both = lin[i]
        for s in (0, 1):
            r = lax.rsqrt(column(tot[pl.ds(16 * s + i, 1), :]) / width + EPS)
            mean = column(inner[pl.ds(16 * s + i, 1), :]) / width
            own = both[:, 128 * s : 128 * (s + 1)]
            d_lin[i, :, 128 * s : 128 * (s + 1)] = (r * d_un[s, i] - own * (r * r * r * mean)).astype(BF)
        return 0

    lax.fori_loop(0, 16, finish, 0)
    run_steps(steps[7])
    run_steps(steps[8])
    d_wo[:, own_cols] = wsum[pl.ds(pl.multiple_of(c * 64, 64), 64), :]
    theirs = remote(wsum.at[pl.ds(pl.multiple_of((1 - c) * 64, 64), 64), :], d_wo.at[:, own_cols], msem.at[8], msem.at[9], partner)
    theirs.start()
    landed(d_out.at[pl.ds(0, 15)], msem.at[0])
    landed(other, msem.at[2])
    landed(PG, msem.at[6])
    theirs.wait_send()
    landed(d_wo.at[:, give_cols], msem.at[9])
    net.finish()


def run_attend_back(scale, pads, d_res, wo, att, q_rot, kv, q_seg, k_seg, lse, o, lin, tot, cosine, sine, gq, gk, cid, cut=96):
    R, D = d_res.shape
    DMA = pltpu.SemaphoreType.DMA
    S = jax.ShapeDtypeStruct
    A = pl.BlockSpec(memory_space=pl.ANY)
    M = pl.BlockSpec(memory_space=pltpu.VMEM)
    V = pltpu.VMEM
    span = (pads + 16) * 2 * R
    return pl.pallas_call(
        functools.partial(attend_back_kernel, scale, pads, cut),
        out_shape=(S((16, R, 384), BF), S((8, 128), F32), S((R // 2, D), F32)),
        in_specs=[M, A] + [M] * 13,
        out_specs=(M, M, M),
        scratch_shapes=[V((4, 4, R, D // 2), BF), V((4, 4, R, D // 2), BF), V((4, 4, R, D // 2), BF), V((R, D // 2), F32), V(wo.shape, BF), V((16, R, 128), BF), V((16, R, 128), BF), V((16, R, 128), BF),
                        V((span, 128), F32), V((span, 128), F32), V((2, 16, R, 128), BF), V((2, 16, R, 128), BF),
                        V((2, 16, R, 128), F32), V((32, 128), F32), V((16, 32, 128), F32), V((32, 128), F32),
                        DMA((2,)), DMA((10,)), DMA((64,))] + rs_scratch(cut, R, D // 2),
        compiler_params=pltpu.CompilerParams(collective_id=cid, has_side_effects=True, vmem_limit_bytes=62 * 2**20),
        name="attend_back",
    )(d_res, wo, att, q_rot, kv, q_seg, k_seg, lse, o, lin, tot, cosine, sine, gq, gk)
def swap_kernel(src, out, lsem, ssem, rsem):
    u, z, c = place()
    me = u * 8 + z * 2 + c
    count = out.shape[0]
    bar = pltpu.get_barrier_semaphore()

    def at(j):
        t = lax.rem(me + j, count)
        return t // 8, lax.rem(t, 8) // 2, lax.rem(t, 2), t // 2

    def hello(j, _):
        tu, tz, tc, _e = at(j)
        pl.semaphore_signal(bar, inc=1, device_id=(tu, tz, tc), device_id_type=MESH)
        return 0

    lax.fori_loop(1, count, hello, 0)
    pl.semaphore_wait(bar, count - 1)

    def copy(j):
        tu, tz, tc, e = at(j)
        return pltpu.make_async_remote_copy(
            src_ref=src.at[e], dst_ref=out.at[me], send_sem=ssem, recv_sem=rsem,
            device_id=(tu, tz, tc), device_id_type=MESH)

    own = pltpu.make_async_copy(src.at[me // 2], out.at[me], lsem)
    own.start()

    def send(j, _):
        copy(j).start()
        return 0

    lax.fori_loop(1, count, send, 0)
    own.wait()
    part = out.at[pl.ds(0, count - 1)]
    pltpu.make_async_copy(part, part, rsem).wait()
    pltpu.make_async_copy(part, part, ssem).wait()


def swap(block, cid):
    chips, r, lanes = block.shape
    S = pltpu.SemaphoreType.DMA
    return pl.pallas_call(
        swap_kernel,
        out_shape=jax.ShapeDtypeStruct((2 * chips, r, lanes), block.dtype),
        in_specs=[pl.BlockSpec(memory_space=pltpu.VMEM)],
        out_specs=pl.BlockSpec(memory_space=pltpu.VMEM),
        scratch_shapes=[S, S, S],
        compiler_params=pltpu.CompilerParams(collective_id=cid, has_side_effects=True),
        name="swap_rows",
    )(block)


def spread_kernel(src, out, lsem, ssem, rsem):
    u, z, c = place()
    me = u * 4 + z
    count = out.shape[0]
    bar = pltpu.get_barrier_semaphore()

    def at(j):
        t = lax.rem(me + j, count)
        return t // 4, lax.rem(t, 4), c

    def hello(j, _):
        pl.semaphore_signal(bar, inc=1, device_id=at(j), device_id_type=MESH)
        return 0

    lax.fori_loop(1, count, hello, 0)
    pl.semaphore_wait(bar, count - 1)
    own = pltpu.make_async_copy(src, out.at[me], lsem)
    own.start()

    def send(j, _):
        pltpu.make_async_remote_copy(
            src_ref=src, dst_ref=out.at[me], send_sem=ssem, recv_sem=rsem,
            device_id=at(j), device_id_type=MESH).start()
        return 0

    lax.fori_loop(1, count, send, 0)
    own.wait()
    part = out.at[pl.ds(0, count - 1)]
    pltpu.make_async_copy(part, part, rsem).wait()
    pltpu.make_async_copy(part, part, ssem).wait()


def spread(block, cid):
    S = pltpu.SemaphoreType.DMA
    return pl.pallas_call(
        spread_kernel,
        out_shape=jax.ShapeDtypeStruct((16,) + block.shape, block.dtype),
        in_specs=[pl.BlockSpec(memory_space=pltpu.VMEM)],
        out_specs=pl.BlockSpec(memory_space=pltpu.VMEM),
        scratch_shapes=[S, S, S],
        compiler_params=pltpu.CompilerParams(collective_id=cid, has_side_effects=True),
        name="spread_rows",
    )(block)


def core_pair(value):
    return lax.ppermute(value, "core", [(0, 1), (1, 0)])


def dot(a, b, dims):
    return lax.dot_general(a, b, (dims, ((), ())), preferred_element_type=jnp.float32)


def local_chip(
    inputs, cotangent, segments, expert_ids, gate_weights, fill_order, norm1_gain, w_query, w_key,
    w_value, w_output, query_gain, key_gain, norm2_gain, expert_gate, expert_up, expert_down,
):
    chips = 16
    devices = 2 * chips
    rows, width = inputs.shape
    u, z, core = place()
    chip = u * 4 + z
    device = chip * 2 + core
    topk = expert_ids.shape[1]
    experts_n = chips
    capacity = 9 * rows * devices * topk // (8 * experts_n)
    one_hot = expert_ids[:, :, None] == jnp.arange(experts_n, dtype=jnp.int32)[None, None, :]
    chosen = jnp.any(one_hot, axis=1)
    weight = jnp.sum(jnp.where(one_hot, gate_weights[:, :, None], 0.0), axis=1)
    earlier = (fill_order[None, :] < fill_order[:, None]).astype(jnp.bfloat16)
    rank = dot(earlier, chosen.astype(jnp.bfloat16), ((1,), (0,)))
    rank = jnp.where(chosen, rank, -1.0)
    gains = jnp.concatenate([norm1_gain, query_gain, key_gain, norm2_gain]).astype(F32)
    gains = jnp.broadcast_to(gains.reshape(1, 2, 128), (chips, 2, 128))
    block = jnp.concatenate(
        [weight.T[:, None, :], rank.T[:, None, :], gains, jnp.zeros((chips, 4, 128), F32)], axis=1)
    swapped = swap(block, 1)
    gains = swapped[:, 2:4, :].reshape(devices, 4, 64).transpose(1, 0, 2).reshape(4, width)
    gain_one, gain_q, gain_k, gain_two = gains[0], gains[1], gains[2], gains[3]
    rank_all = swapped[:, 1, :]
    taken = rank_all >= 0.0
    counts = jnp.sum(taken.astype(F32), axis=1)
    before = jnp.cumsum(counts) - counts
    kept = taken & (before[:, None] + rank_all < float(capacity))
    share = jnp.where(kept, swapped[:, 0, :], 0.0).reshape(chips, 2, rows)
    share = lax.dynamic_index_in_dim(share, core, 1, keepdims=False).reshape(chips * rows, 1)


    layer_in = inputs.astype(F32)
    mine = ("ulysses", "z")

    def in_order(own, other):
        return jnp.where(core == 0, own, other), jnp.where(core == 0, other, own)

    cols = jnp.stack([w_query, w_key, w_value]).reshape(3, 64, chips, HEAD_DIM)
    cols = cols.transpose(2, 1, 0, 3).reshape(chips, 64, 3 * HEAD_DIM)
    def my_head(gain):
        return lax.dynamic_slice_in_dim(gain, chip * HEAD_DIM, HEAD_DIM, 0)

    n1_rows, lin, w_qkv, squares = run_qkv(inputs, cols, gain_one.reshape(1, width), 2)
    positions = (jnp.arange(chips, dtype=jnp.int32)[:, None] * 2 + core) * rows + jnp.arange(rows, dtype=jnp.int32)
    half_dim = HEAD_DIM // 2
    inv_freq = jnp.exp(jnp.arange(half_dim, dtype=F32) * (-2.0 * math.log(ROPE_BASE) / HEAD_DIM))
    angles = positions.reshape(-1).astype(F32)[:, None] * inv_freq[None, :]
    cosine, sine = jnp.cos(angles), jnp.sin(angles)
    cosine = jnp.concatenate([cosine, cosine], axis=1).reshape(chips, rows, HEAD_DIM)
    sine = jnp.concatenate([-sine, sine], axis=1).reshape(chips, rows, HEAD_DIM)
    gq, gk = my_head(gain_q).reshape(1, HEAD_DIM), my_head(gain_k).reshape(1, HEAD_DIM)
    pads = chips // 4
    k_seg = jnp.concatenate([jnp.full((pads * 2 * rows,), -1, jnp.int32), segments]).reshape(1, -1)
    q_seg = lax.dynamic_index_in_dim(segments.reshape(chips, 2, rows, 1), core, 1, keepdims=False)
    scale = 1.0 / math.sqrt(HEAD_DIM)
    tokens = chips * rows
    w_o, q_rot, kv, head_out, log_total, attended, residual, normed_two = run_attend(
        scale, pads, lin, squares, cosine, sine, gq, gk, q_seg, k_seg, w_output, inputs, gain_two.reshape(1, width), 4)
    r2 = lax.rsqrt(jnp.mean(residual * residual, axis=1, keepdims=True) + EPS)

    def to_blocks(part):
        return part.astype(BF).reshape(4, 4, rows, part.shape[-1])

    d_normed_two, mixed, _n2, _other, d_expert_gate, d_expert_up, d_expert_down = run_expert(
        normed_two, cotangent, share.reshape(4, 4, rows, 1), expert_gate, expert_up, expert_down, 6)
    def norm_back(d_out, values, r, gain):
        d_scaled = d_out * gain
        inner = jnp.mean(d_scaled * values, axis=1, keepdims=True)
        d_gain = jnp.sum(d_out * values * r, axis=0)
        return r * d_scaled - values * (r * r * r * inner), d_gain

    d_resid_norm, d_gain_two = norm_back(d_normed_two, residual, r2, gain_two)
    d_residual = cotangent.astype(F32) + d_resid_norm
    d_res_low = d_residual.astype(BF)
    d_lin, d_qk_gains, d_w_output = run_attend_back(
        scale, pads, d_res_low, w_o, attended, q_rot, kv, q_seg, k_seg, log_total, head_out, lin, squares, cosine, sine, gq, gk, 7)
    d_qk_gains = d_qk_gains[:2] + core_pair(d_qk_gains[:2])
    output, d_inputs, d_w_query, d_w_key, d_w_value, d_gains = run_finish(
        d_lin, w_qkv, n1_rows, mixed, inputs, residual, d_residual, gain_one.reshape(1, width), d_gain_two.reshape(1, width), 8)

    def my_half(row):
        return lax.dynamic_slice_in_dim(row, core * 64, 64, 0)

    return (
        output,
        d_inputs,
        my_half(d_gains[0]),
        d_w_query,
        d_w_key,
        d_w_value,
        d_w_output,
        my_half(d_qk_gains[0]),
        my_half(d_qk_gains[1]),
        my_half(d_gains[1]),
        d_expert_gate,
        d_expert_up,
        d_expert_down,
    )
def whole(mesh, step, rows):
    return jax.shard_map(
        step,
        mesh=mesh,
        in_specs=(
            P(rows, None),
            P(rows, None),
            P(),
            P(rows, None),
            P(rows, None),
            P(rows),
            P(rows),
            P(rows, None),
            P(rows, None),
            P(rows, None),
            P(rows, None),
            P(rows),
            P(rows),
            P(rows),
            P(rows, None),
            P(rows, None),
            P(rows, None),
        ),
        out_specs=(
            P(rows, None),
            P(rows, None),
            P(rows),
            P(rows, None),
            P(rows, None),
            P(rows, None),
            P(rows, None),
            P(rows),
            P(rows),
            P(rows),
            P(rows, None),
            P(rows, None),
            P(rows, None),
        ),
        check_vma=False,
    )


def solution(mesh):
    groups, blk_size = mesh.shape["ulysses"], mesh.shape["blk"]

    def step(*args):
        if groups != 4 or blk_size != 8 or args[7].shape[1] // HEAD_DIM != groups * blk_size // 2:
            return whole(mesh, local, ("ulysses", "blk"))(*args)
        chips = Mesh(mesh.devices.reshape(groups, blk_size // 2, 2), ("ulysses", "z", "core"))
        return whole(chips, local_chip, ("ulysses", "z", "core"))(*args)

    return step
```

```python
import functools
import math

import jax
import jax.numpy as jnp
from jax import lax
from jax.experimental import pallas as pl
from jax.experimental.pallas import tpu as pltpu
from jax.sharding import Mesh
from jax.sharding import PartitionSpec as P

HEAD_DIM = 128


EPS = 1e-05
ROPE_BASE = 10000.0
NEG = -1e30


def as_sent(value):

    def short(part):
        return part.astype(jnp.bfloat16) if part.dtype == jnp.float32 else part

    return jax.tree.map(short, value)


def passed_along(block, axis, distance):
    devices = range(lax.axis_size(axis))
    route = [((i - distance) % len(devices), i) for i in devices]
    return lax.ppermute(block, axis, route)


def prefix(value, axis, join, neutral):
    count, mine = (lax.axis_size(axis), lax.axis_index(axis))
    pieces = lax.all_gather(value, axis)
    subtotal = jnp.full_like(value, 0) + jnp.asarray(neutral, value.dtype)

    def hop(position, subtotal):
        longer = join(subtotal, pieces[position])
        return jnp.where(position < mine, longer, subtotal)

    return lax.fori_loop(0, count - 1, hop, subtotal)


def partner_2(block, axis, bit):
    count = lax.axis_size(axis)
    route = []
    for low in range(count):
        high = low | 1 << bit
        if high != low and high < count:
            route += [(low, high), (high, low)]
    return lax.ppermute(block, axis, route)


def norm_rows(values, gain_vec):
    return values * lax.rsqrt(jnp.mean(values * values, axis=-1, keepdims=True) + EPS) * gain_vec


def rotate(values, positions):
    half_dim = HEAD_DIM // 2
    heads_here = values.shape[1] // HEAD_DIM
    inv_freq = jnp.exp(
        jnp.arange(half_dim, dtype=jnp.float32) * (-2.0 * math.log(ROPE_BASE) / HEAD_DIM)
    )
    angles = positions.astype(jnp.float32)[:, None] * inv_freq[None, :]
    cosine = jnp.cos(angles)[:, None, :]
    sin_t = jnp.sin(angles)[:, None, :]
    shaped = values.reshape(values.shape[0], heads_here, HEAD_DIM)
    lower_half = shaped[..., :half_dim]
    upper_half = shaped[..., half_dim:]
    turned = jnp.concatenate(
        [lower_half * cosine - upper_half * sin_t, upper_half * cosine + lower_half * sin_t],
        axis=-1,
    )
    return turned.reshape(values.shape)


def attn_inputs(q_lin, k_lin, gain_q, gain_k, positions):
    return (
        rotate(norm_rows(q_lin, gain_q), positions),
        rotate(norm_rows(k_lin, gain_k), positions),
    )


def banded(shaped, fill_value):
    earlier = jnp.concatenate([jnp.full_like(shaped[:1], fill_value), shaped[:-1]], axis=0)
    return jnp.concatenate([earlier, shaped], axis=1)


def unbanded(band, local_rows):
    earlier = band[:, :local_rows]
    own_part = band[:, local_rows:]
    moved_up = jnp.concatenate([earlier[1:], jnp.zeros_like(earlier[:1])], axis=0)
    return own_part + moved_up


def add_counts(earlier, later):
    return earlier + later


def expert_move(buffer):
    return lax.all_to_all(buffer, ("ulysses", "blk"), split_axis=0, concat_axis=0, tiled=True)


def to_head_layout(values):
    return jax.tree.map(
        lambda part, own: part.astype(own.dtype),
        lax.all_to_all(as_sent(values), "ulysses", split_axis=1, concat_axis=0, tiled=True),
        values,
    )


def to_token_layout(values):
    return jax.tree.map(
        lambda part, own: part.astype(own.dtype),
        lax.all_to_all(as_sent(values), "ulysses", split_axis=0, concat_axis=1, tiled=True),
        values,
    )


def local(
    inputs,
    cotangent,
    segments,
    expert_ids,
    gate_weights,
    fill_order,
    norm1_gain,
    w_query,
    w_key,
    w_value,
    w_output,
    query_gain,
    key_gain,
    norm2_gain,
    expert_gate,
    expert_up,
    expert_down,
):
    blk_size = lax.axis_size("blk")
    groups = lax.axis_size("ulysses")
    devices = blk_size * groups
    local_rows = inputs.shape[0]
    model_width = inputs.shape[1]
    blk_index = lax.axis_index("blk")
    group_index = lax.axis_index("ulysses")
    device_index = group_index * blk_size + blk_index
    positions = device_index * local_rows + jnp.arange(local_rows, dtype=jnp.int32)
    heads_dev = model_width // groups // HEAD_DIM
    score_scale = 1.0 / math.sqrt(HEAD_DIM)
    layer_in = inputs.astype(jnp.float32)
    dense = (w_query, w_key, w_value, w_output, norm1_gain, query_gain, key_gain, norm2_gain)
    gathered = (
        lax.all_gather(dense[0], ("ulysses", "blk"), axis=0, tiled=True),
        lax.all_gather(dense[1], ("ulysses", "blk"), axis=0, tiled=True),
        lax.all_gather(dense[2], ("ulysses", "blk"), axis=0, tiled=True),
        lax.all_gather(dense[3], ("ulysses", "blk"), axis=0, tiled=True),
        lax.all_gather(dense[4], ("ulysses", "blk"), axis=0, tiled=True),
        lax.all_gather(dense[5], ("ulysses", "blk"), axis=0, tiled=True),
        lax.all_gather(dense[6], ("ulysses", "blk"), axis=0, tiled=True),
        lax.all_gather(dense[7], ("ulysses", "blk"), axis=0, tiled=True),
    )
    w_q, w_k, w_v, w_o = (gathered[0], gathered[1], gathered[2], gathered[3])
    gain_one = gathered[4].astype(jnp.float32)
    gain_q = gathered[5].astype(jnp.float32)
    gain_k = gathered[6].astype(jnp.float32)
    gain_two = gathered[7].astype(jnp.float32)
    normed_one = norm_rows(layer_in, gain_one).astype(jnp.bfloat16)
    q_lin = jnp.dot(normed_one, w_q, preferred_element_type=jnp.float32)
    k_lin = jnp.dot(normed_one, w_k, preferred_element_type=jnp.float32)
    v_lin = jnp.dot(normed_one, w_v, preferred_element_type=jnp.float32)
    (q_rot, k_rot), pre_back = jax.vjp(
        lambda q_in, k_in, gq_in, gk_in: attn_inputs(q_in, k_in, gq_in, gk_in, positions),
        q_lin,
        k_lin,
        gain_q,
        gain_k,
    )
    q_heads, k_heads, v_heads = to_head_layout(
        (q_rot.astype(jnp.bfloat16), k_rot.astype(jnp.bfloat16), v_lin.astype(jnp.bfloat16))
    )
    group_ids = jnp.arange(groups, dtype=jnp.int32)[:, None]
    row_ids = jnp.arange(local_rows, dtype=jnp.int32)[None, :]
    q_pos = (group_ids * blk_size + blk_index) * local_rows + row_ids
    q_seg = segments[q_pos]
    four_shape = (groups, local_rows, heads_dev, HEAD_DIM)
    q_four = q_heads.reshape(four_shape)

    def score_block(k_now, source):
        k_pos = (group_ids * blk_size + source) * local_rows + row_ids
        k_seg = banded(segments[k_pos], -1)
        k_pos = banded(k_pos, 0)
        k_band = banded(k_now.reshape(four_shape), 0)
        raw_scores = (
            jnp.einsum("gqhd,gkhd->gqhk", q_four, k_band, preferred_element_type=jnp.float32)
            * score_scale
        )
        allowed = (k_seg[:, None, :] == q_seg[:, :, None]) & (
            k_pos[:, None, :] <= q_pos[:, :, None]
        )
        return (raw_scores, allowed[:, :, None, :], k_band)

    def forward_step(flash_state, kv_stack, step_id):
        run_max, run_sum, run_out = flash_state
        source = jnp.mod(blk_index - step_id, blk_size)
        raw_scores, allowed, k_band = score_block(kv_stack[0], source)
        raw_scores = jnp.where(allowed, raw_scores, NEG)
        new_max = jnp.maximum(run_max, jnp.max(raw_scores, axis=-1))
        shrink = jnp.exp(run_max - new_max)
        weights = jnp.where(allowed, jnp.exp(raw_scores - new_max[..., None]), 0.0)
        run_sum = run_sum * shrink + jnp.sum(weights, axis=-1)
        v_band = banded(kv_stack[1].reshape(four_shape), 0)
        run_out = run_out * shrink[..., None] + jnp.einsum(
            "gqhk,gkhd->gqhd",
            weights.astype(jnp.bfloat16),
            v_band,
            preferred_element_type=jnp.float32,
        )
        return (new_max, run_sum, run_out)

    start_state = (
        jnp.full((groups, local_rows, heads_dev), NEG, jnp.float32),
        jnp.zeros((groups, local_rows, heads_dev), jnp.float32),
        jnp.zeros(four_shape, jnp.float32),
    )
    kv_home = jnp.stack([k_heads, v_heads])
    first_state = forward_step(start_state, kv_home, 0)

    def forward_turn(step_id, loop_state):
        flash_state, kv_stack = loop_state
        moved = passed_along(kv_stack, "blk", 1)
        return (forward_step(flash_state, moved, step_id), moved)

    final_state, unused_kv = lax.fori_loop(1, blk_size, forward_turn, (first_state, kv_home))
    run_max, run_sum, run_out = final_state
    o_four = (run_out / run_sum[..., None]).astype(jnp.bfloat16)
    log_total = run_max + jnp.log(run_sum)
    o_heads = o_four.reshape(groups * local_rows, heads_dev * HEAD_DIM)
    attended = to_token_layout(o_heads)
    residual = layer_in + jnp.dot(attended, w_o, preferred_element_type=jnp.float32)
    normed_two_f, norm_two_back = jax.vjp(norm_rows, residual, gain_two)
    normed_two = normed_two_f.astype(jnp.bfloat16)
    experts_n = devices // 2
    topk = expert_ids.shape[1]
    per_source = 2 * local_rows * topk // experts_n
    half_slots = per_source // 2
    capacity = 9 * local_rows * devices * topk // (8 * experts_n)
    slots_all = experts_n * per_source
    tokens_local = jnp.arange(local_rows, dtype=jnp.int32)
    chosen = jnp.sum(
        (expert_ids[:, :, None] == jnp.arange(experts_n, dtype=jnp.int32)[None, None, :]).astype(
            jnp.int32
        ),
        axis=1,
    )
    by_fill = jnp.zeros((local_rows,), jnp.int32).at[fill_order].set(tokens_local)
    sorted_rows = chosen[by_fill]
    before = jnp.cumsum(sorted_rows, axis=0) - sorted_rows
    rank_all = before[fill_order]
    pair_rank = jnp.take_along_axis(rank_all, expert_ids, axis=1)
    counts = jnp.sum(chosen, axis=0)
    offsets = prefix(counts, ("ulysses", "blk"), add_counts, jnp.zeros_like(counts))
    kept_pair = offsets[expert_ids] + pair_rank < capacity
    pair_slot = expert_ids * per_source + pair_rank
    pair_index = tokens_local[:, None] * topk + jnp.arange(topk, dtype=jnp.int32)[None, :]
    slot_pair = (
        jnp.zeros((slots_all,), jnp.int32).at[pair_slot.reshape(-1)].set(pair_index.reshape(-1))
    )
    slot_live = (
        jnp.zeros((slots_all,), jnp.bool_).at[pair_slot.reshape(-1)].set(kept_pair.reshape(-1))
    )
    slot_token = slot_pair // topk
    send_rows = jnp.where(slot_live[:, None], normed_two[slot_token], jnp.zeros((), jnp.bfloat16))
    received = expert_move(send_rows.reshape(devices, half_slots, model_width)).reshape(
        devices * half_slots, model_width
    )
    parity = jnp.mod(blk_index, 2)
    partner = partner_2((expert_gate, expert_up, expert_down), "blk", 0)

    def joined(own_half, other_half):
        lower_part = jnp.where(parity == 0, own_half, other_half)
        upper_part = jnp.where(parity == 0, other_half, own_half)
        return jnp.concatenate([lower_part, upper_part], axis=0)

    gate_full = joined(expert_gate, partner[0])
    up_full = joined(expert_up, partner[1])
    down_full = joined(expert_down, partner[2])
    gate_pre = jnp.dot(received, gate_full, preferred_element_type=jnp.float32)
    up_pre = jnp.dot(received, up_full, preferred_element_type=jnp.float32)
    hidden = (jax.nn.silu(gate_pre) * up_pre).astype(jnp.bfloat16)
    produced = jnp.dot(hidden, down_full, preferred_element_type=jnp.float32).astype(jnp.bfloat16)
    returned = expert_move(produced.reshape(devices, half_slots, model_width)).reshape(
        slots_all, model_width
    )
    pair_share = jnp.where(kept_pair, gate_weights, 0.0)
    mixed = jnp.einsum("tk,tkd->td", pair_share, returned[pair_slot].astype(jnp.float32))
    output = residual + mixed
    grad_out = cotangent.astype(jnp.float32)
    slot_share = jnp.where(slot_live, gate_weights.reshape(-1)[slot_pair], 0.0)
    grad_send = (slot_share[:, None] * grad_out[slot_token]).astype(jnp.bfloat16)
    grad_rows = expert_move(grad_send.reshape(devices, half_slots, model_width)).reshape(
        devices * half_slots, model_width
    )
    d_down_full = jnp.einsum("rf,rd->fd", hidden, grad_rows, preferred_element_type=jnp.float32)
    d_hidden = jnp.einsum("rd,fd->rf", grad_rows, down_full, preferred_element_type=jnp.float32)
    sigma = jax.nn.sigmoid(gate_pre)
    d_gate_pre = (d_hidden * up_pre * sigma * (1.0 + gate_pre * (1.0 - sigma))).astype(jnp.bfloat16)
    d_up_pre = (d_hidden * gate_pre * sigma).astype(jnp.bfloat16)
    d_gate_full = jnp.einsum("rd,rf->df", received, d_gate_pre, preferred_element_type=jnp.float32)
    d_up_full = jnp.einsum("rd,rf->df", received, d_up_pre, preferred_element_type=jnp.float32)
    d_pair_rows = (
        jnp.einsum("rf,df->rd", d_gate_pre, gate_full, preferred_element_type=jnp.float32)
        + jnp.einsum("rf,df->rd", d_up_pre, up_full, preferred_element_type=jnp.float32)
    ).astype(jnp.bfloat16)
    back_rows = expert_move(d_pair_rows.reshape(devices, half_slots, model_width)).reshape(
        slots_all, model_width
    )
    d_normed_two = jnp.sum(
        jnp.where(kept_pair[:, :, None], back_rows[pair_slot].astype(jnp.float32), 0.0), axis=1
    )
    half_rows = expert_gate.shape[0]
    half_hidden = expert_down.shape[0]

    def halves(full_grad, size):
        own_half = lax.dynamic_slice_in_dim(full_grad, parity * size, size, 0)
        other_half = lax.dynamic_slice_in_dim(full_grad, (1 - parity) * size, size, 0)
        return (own_half, other_half)

    gate_own, gate_other = halves(d_gate_full, half_rows)
    up_own, up_other = halves(d_up_full, half_rows)
    down_own, down_other = halves(d_down_full, half_hidden)
    partner_grads = (
        partner_2(gate_other.astype(jnp.bfloat16), "blk", 0).astype(gate_other.dtype),
        partner_2(up_other.astype(jnp.bfloat16), "blk", 0).astype(up_other.dtype),
        partner_2(down_other.astype(jnp.bfloat16), "blk", 0).astype(down_other.dtype),
    )
    d_expert_gate = gate_own + partner_grads[0]
    d_expert_up = up_own + partner_grads[1]
    d_expert_down = down_own + partner_grads[2]
    d_resid_norm, d_gain_two = norm_two_back(d_normed_two)
    d_residual = grad_out + d_resid_norm
    d_res_low = d_residual.astype(jnp.bfloat16)
    d_attended = jnp.einsum("te,de->td", d_res_low, w_o, preferred_element_type=jnp.float32).astype(
        jnp.bfloat16
    )
    d_o_heads = to_head_layout(d_attended)
    d_o_four = d_o_heads.reshape(four_shape)
    row_delta = jnp.sum(d_o_four.astype(jnp.float32) * o_four.astype(jnp.float32), axis=-1)

    def back_turn(step_id, loop_state):
        moving, dq_acc = loop_state
        source = jnp.mod(blk_index - step_id, blk_size)
        k_now = moving[0].astype(jnp.bfloat16)
        v_now = moving[1].astype(jnp.bfloat16)
        raw_scores, allowed, k_band = score_block(k_now, source)
        prob_rows = jnp.where(allowed, jnp.exp(raw_scores - log_total[..., None]), 0.0)
        v_band = banded(v_now.reshape(four_shape), 0)
        d_probs = jnp.einsum(
            "gqhd,gkhd->gqhk", d_o_four, v_band, preferred_element_type=jnp.float32
        )
        d_scores = (prob_rows * (d_probs - row_delta[..., None])).astype(jnp.bfloat16)
        dv_band = jnp.einsum(
            "gqhk,gqhd->gkhd",
            prob_rows.astype(jnp.bfloat16),
            d_o_four,
            preferred_element_type=jnp.float32,
        )
        dk_band = (
            jnp.einsum("gqhk,gqhd->gkhd", d_scores, q_four, preferred_element_type=jnp.float32)
            * score_scale
        )
        dq_acc = (
            dq_acc
            + jnp.einsum("gqhk,gkhd->gqhd", d_scores, k_band, preferred_element_type=jnp.float32)
            * score_scale
        )
        flat_shape = moving[2].shape
        dk_new = moving[2] + unbanded(dk_band, local_rows).reshape(flat_shape)
        dv_new = moving[3] + unbanded(dv_band, local_rows).reshape(flat_shape)
        moving = passed_along(
            jnp.stack([moving[0], moving[1], dk_new, dv_new]).astype(jnp.bfloat16), "blk", 1
        ).astype(jnp.float32)
        return (moving, dq_acc)

    zero_rows = jnp.zeros(k_heads.shape, jnp.float32)
    start_moving = jnp.stack(
        [k_heads.astype(jnp.float32), v_heads.astype(jnp.float32), zero_rows, zero_rows]
    )
    moving, dq_acc = lax.fori_loop(
        0, blk_size, back_turn, (start_moving, jnp.zeros(four_shape, jnp.float32))
    )
    d_q_send = dq_acc.astype(jnp.bfloat16).reshape(k_heads.shape)
    d_k_send = moving[2].astype(jnp.bfloat16)
    d_v_send = moving[3].astype(jnp.bfloat16)
    d_q_rot, d_k_rot, d_v_lin = to_token_layout((d_q_send, d_k_send, d_v_send))
    d_q_lin, d_k_lin, d_gain_q, d_gain_k = pre_back(
        (d_q_rot.astype(jnp.float32), d_k_rot.astype(jnp.float32))
    )
    d_q_low = d_q_lin.astype(jnp.bfloat16)
    d_k_low = d_k_lin.astype(jnp.bfloat16)
    d_normed_one = jnp.einsum("te,de->td", d_q_low, w_q, preferred_element_type=jnp.float32)
    d_normed_one = d_normed_one + jnp.einsum(
        "te,de->td", d_k_low, w_k, preferred_element_type=jnp.float32
    )
    d_normed_one = d_normed_one + jnp.einsum(
        "te,de->td", d_v_lin, w_v, preferred_element_type=jnp.float32
    )
    unused_norm, norm_one_back = jax.vjp(norm_rows, layer_in, gain_one)
    d_layer_in, d_gain_one = norm_one_back(d_normed_one)
    d_inputs = d_residual + d_layer_in
    d_qk_heads = to_head_layout((d_q_low, d_k_low))
    rows_all = (
        lax.all_gather(normed_one, "ulysses", axis=0, tiled=True),
        lax.all_gather(d_res_low, "ulysses", axis=0, tiled=True),
    )
    head_cols = model_width // groups
    piece_rows = model_width // devices

    def by_owner(part):
        rest = part.shape[1:]
        shaped = part.reshape((groups, blk_size, piece_rows) + rest)
        return jnp.swapaxes(shaped, 0, 1).reshape((model_width,) + rest)

    part_q = jnp.einsum("td,te->de", rows_all[0], d_qk_heads[0], preferred_element_type=jnp.float32)
    part_k = jnp.einsum("td,te->de", rows_all[0], d_qk_heads[1], preferred_element_type=jnp.float32)
    part_v = jnp.einsum("td,te->de", rows_all[0], d_v_send, preferred_element_type=jnp.float32)
    part_o = jnp.einsum("te,td->ed", o_heads, rows_all[1], preferred_element_type=jnp.float32)
    blk_sums = (
        lax.psum_scatter(
            by_owner(part_q).astype(jnp.bfloat16), "blk", scatter_dimension=0, tiled=True
        ).astype(jnp.float32),
        lax.psum_scatter(
            by_owner(part_k).astype(jnp.bfloat16), "blk", scatter_dimension=0, tiled=True
        ).astype(jnp.float32),
        lax.psum_scatter(
            by_owner(part_v).astype(jnp.bfloat16), "blk", scatter_dimension=0, tiled=True
        ).astype(jnp.float32),
        lax.psum_scatter(
            part_o.astype(jnp.bfloat16), "blk", scatter_dimension=0, tiled=True
        ).astype(jnp.float32),
        lax.psum_scatter(
            by_owner(d_gain_one).astype(jnp.bfloat16), "blk", scatter_dimension=0, tiled=True
        ).astype(jnp.float32),
        lax.psum_scatter(
            by_owner(d_gain_q).astype(jnp.bfloat16), "blk", scatter_dimension=0, tiled=True
        ).astype(jnp.float32),
        lax.psum_scatter(
            by_owner(d_gain_k).astype(jnp.bfloat16), "blk", scatter_dimension=0, tiled=True
        ).astype(jnp.float32),
        lax.psum_scatter(
            by_owner(d_gain_two).astype(jnp.bfloat16), "blk", scatter_dimension=0, tiled=True
        ).astype(jnp.float32),
    )

    def widened(part):
        return lax.dynamic_update_slice_in_dim(
            jnp.zeros((part.shape[0], model_width), jnp.float32), part, group_index * head_cols, 1
        )

    col_sums = (
        lax.psum_scatter(
            widened(blk_sums[0]).astype(jnp.bfloat16), "ulysses", scatter_dimension=0, tiled=True
        ).astype(jnp.float32),
        lax.psum_scatter(
            widened(blk_sums[1]).astype(jnp.bfloat16), "ulysses", scatter_dimension=0, tiled=True
        ).astype(jnp.float32),
        lax.psum_scatter(
            widened(blk_sums[2]).astype(jnp.bfloat16), "ulysses", scatter_dimension=0, tiled=True
        ).astype(jnp.float32),
        lax.psum_scatter(
            blk_sums[4].astype(jnp.bfloat16), "ulysses", scatter_dimension=0, tiled=True
        ).astype(jnp.float32),
        lax.psum_scatter(
            blk_sums[5].astype(jnp.bfloat16), "ulysses", scatter_dimension=0, tiled=True
        ).astype(jnp.float32),
        lax.psum_scatter(
            blk_sums[6].astype(jnp.bfloat16), "ulysses", scatter_dimension=0, tiled=True
        ).astype(jnp.float32),
        lax.psum_scatter(
            blk_sums[7].astype(jnp.bfloat16), "ulysses", scatter_dimension=0, tiled=True
        ).astype(jnp.float32),
    )
    result_grads = (
        col_sums[0],
        col_sums[1],
        col_sums[2],
        blk_sums[3],
        col_sums[3],
        col_sums[4],
        col_sums[5],
        col_sums[6],
    )
    return (
        output,
        d_inputs,
        result_grads[4],
        result_grads[0],
        result_grads[1],
        result_grads[2],
        result_grads[3],
        result_grads[5],
        result_grads[6],
        result_grads[7],
        d_expert_gate,
        d_expert_up,
        d_expert_down,
    )


MESH = pl.DeviceIdType.MESH
P1 = 96

def place():
    u = lax.axis_index("ulysses"); z = lax.axis_index("z"); c = lax.axis_index("core")
    return u, z, c

def ag_kernel(cut, x_ref, o_ref, local_sem, s_sem, zr, xr, yr, d1r, d2r, bs, br, bzr):
    u, z, c = place()
    Z = 4
    R = x_ref.shape[0]
    ux, uy = u ^ 1, u ^ 2
    xn, yn, up, dn = (ux, z, c), (uy, z, c), (u, z + 1, c), (u, z - 1, c)
    has_up, has_dn = z < Z - 1, z > 0
    bar = pltpu.get_barrier_semaphore()
    for n in (xn, yn):
        pl.semaphore_signal(bar, inc=1, device_id=n, device_id_type=MESH)
    @pl.when(has_up)
    def _():
        pl.semaphore_signal(bar, inc=1, device_id=up, device_id_type=MESH)
    @pl.when(has_dn)
    def _():
        pl.semaphore_signal(bar, inc=1, device_id=dn, device_id_type=MESH)
    pl.semaphore_wait(bar, 2 + has_up.astype(jnp.int32) + has_dn.astype(jnp.int32))
    sends = []
    def copy(src, dst, ss, rs, dev):
        return pltpu.make_async_remote_copy(src_ref=src, dst_ref=dst, send_sem=ss, recv_sem=rs, device_id=dev, device_id_type=MESH)
    def go(cond, make):
        idx = len(sends)
        def mk():
            return make(s_sem.at[idx])
        sends.append((cond, mk))
        if cond is None:
            mk().start()
        else:
            pl.when(cond)(lambda: mk().start())
    def both(a, b):
        if a is None: return b
        if b is None: return a
        return jnp.logical_and(a, b)
    def wait(cond, ref, sem):
        def w():
            pltpu.make_async_copy(ref, ref, sem).wait()
        if cond is None: w()
        else: pl.when(cond)(w)
    own = pltpu.make_async_copy(x_ref, o_ref.at[u, z], local_sem)
    own.start()
    A = slice(0, cut)
    h = cut // 2
    def oa(uu, zz, lo=0, n=cut):
        return o_ref.at[uu, zz, pl.ds(lo, n), :]
    def spread(s, zz, cond):
        src = (lambda: x_ref.at[pl.ds(0, cut), :]) if s == 0 else (lambda: oa(u, zz))
        go(cond, lambda sm: copy(src(), oa(u, zz), sm, xr.at[zz], xn))
        go(cond, lambda sm: copy(src(), oa(u, zz), sm, yr.at[zz], yn))
    def cross(zz, cond):
        wait(cond, oa(ux, zz), xr.at[zz])
        go(cond, lambda sm: copy(oa(ux, zz, 0, h), oa(ux, zz, 0, h), sm, d1r.at[zz], yn))
        wait(cond, oa(uy, zz), yr.at[zz])
        go(cond, lambda sm: copy(oa(uy, zz, h, h), oa(uy, zz, h, h), sm, d2r.at[zz], xn))
    rb = R - cut
    hb = rb // 2
    def ob(uu, zz, lo=0, n=None):
        return o_ref.at[uu, zz, pl.ds(cut + lo, rb if n is None else n), :]
    go(has_up, lambda sm: copy(x_ref.at[pl.ds(0, cut), :], oa(u, z), sm, zr.at[z], up))
    go(has_dn, lambda sm: copy(x_ref.at[pl.ds(0, cut), :], oa(u, z), sm, zr.at[z], dn))
    if rb:
        go(None, lambda sm: copy(x_ref.at[pl.ds(cut, rb), :], ob(u, z), sm, br.at[0], xn))
        go(None, lambda sm: copy(x_ref.at[pl.ds(cut, rb), :], ob(u, z), sm, br.at[1], yn))
    spread(0, z, None)
    if rb:
        wait(None, ob(ux, z), br.at[0])
        go(None, lambda sm: copy(ob(ux, z, 0, hb), ob(ux, z, 0, hb), sm, br.at[2], yn))
        wait(None, ob(uy, z), br.at[1])
        go(None, lambda sm: copy(ob(uy, z, hb, hb), ob(uy, z, hb, hb), sm, br.at[3], xn))
    own.wait()
    def quad(zz):
        return o_ref.at[:, zz, pl.ds(cut, rb), :]
    def zs(s):
        zl, zh = z - s, z + s
        cl, ch = zl >= 0, zh < Z
        zlc, zhc = jnp.maximum(zl, 0), jnp.minimum(zh, Z - 1)
        return (zlc, cl, has_up, up), (zhc, ch, has_dn, dn)
    prev = [(z, None)]
    for s in range(1, Z):
        cur = []
        for (zz, cond, fwd, dev) in zs(s):
            wait(cond, oa(u, zz), zr.at[zz])
            go(both(cond, fwd), lambda sm, zz=zz, dev=dev: copy(oa(u, zz), oa(u, zz), sm, zr.at[zz], dev))
            spread(s, zz, cond)
            cur.append((zz, cond))
        if rb and s == 1:
            wait(None, ob(u ^ 3, z, 0, hb), br.at[2])
            wait(None, ob(u ^ 3, z, hb, hb), br.at[3])
            go(has_up, lambda sm: copy(quad(z), quad(z), sm, bzr.at[z], up))
            go(has_dn, lambda sm: copy(quad(z), quad(z), sm, bzr.at[z], dn))
        elif rb:
            for (zz, cond, fwd, dev) in zs(s - 1):
                wait(cond, quad(zz), bzr.at[zz])
                go(both(cond, fwd), lambda sm, zz=zz, dev=dev: copy(quad(zz), quad(zz), sm, bzr.at[zz], dev))
        for zz, cond in prev:
            cross(zz, cond)
        prev = cur
    if rb:
        for (zz, cond, fwd, dev) in zs(Z - 1):
            wait(cond, quad(zz), bzr.at[zz])
    for zz, cond in prev:
        cross(zz, cond)
    for zz in range(Z):
        wait(None, oa(u ^ 3, zz, 0, h), d1r.at[zz])
        wait(None, oa(u ^ 3, zz, h, h), d2r.at[zz])
    for cond, mk in sends:
        if cond is None: mk().wait_send()
        else: pl.when(cond)(lambda mk=mk: mk().wait_send())

def ag16(x, cid, cut=P1, space=pl.ANY):
    R, D = x.shape
    DMA = pltpu.SemaphoreType.DMA
    return pl.pallas_call(
        functools.partial(ag_kernel, cut),
        out_shape=jax.ShapeDtypeStruct((4, 4, R, D), x.dtype),
        in_specs=[pl.BlockSpec(memory_space=space)],
        out_specs=pl.BlockSpec(memory_space=space),
        scratch_shapes=[DMA, DMA((64,)), DMA((4,)), DMA((4,)), DMA((4,)), DMA((4,)), DMA((4,)), DMA((4,)), DMA((4,)), DMA((4,))],
        compiler_params=pltpu.CompilerParams(collective_id=cid, has_side_effects=True, vmem_limit_bytes=48 * 2**20),
        name="gather_rows",
    )(x)
F32 = jnp.float32
BF = jnp.bfloat16


class Net:
    def __init__(self, sems):
        self.sems, self.sends = sems, []
        self.u, self.z, self.c = place()
        u, z, c = self.u, self.z, self.c
        self.ux, self.uy, self.ud = u ^ 1, u ^ 2, u ^ 3
        self.xn, self.yn, self.up, self.dn = (u ^ 1, z, c), (u ^ 2, z, c), (u, z + 1, c), (u, z - 1, c)
        self.has_up, self.has_dn = z < 3, z > 0
        self.at = [z == i for i in range(4)]

    def barrier(self, more=()):
        bar = pltpu.get_barrier_semaphore()
        for n in (self.xn, self.yn) + tuple(more):
            pl.semaphore_signal(bar, inc=1, device_id=n, device_id_type=MESH)
        for cond, n in ((self.has_up, self.up), (self.has_dn, self.dn)):
            pl.when(cond)(lambda n=n: pl.semaphore_signal(bar, inc=1, device_id=n, device_id_type=MESH))
        pl.semaphore_wait(bar, 2 + len(more) + self.has_up.astype(jnp.int32) + self.has_dn.astype(jnp.int32))

    def go(self, cond, src, dst, rsem, dev):
        idx = len(self.sends)

        def mk():
            return pltpu.make_async_remote_copy(
                src_ref=src(), dst_ref=dst(), send_sem=self.sems.at[idx], recv_sem=rsem(),
                device_id=dev, device_id_type=MESH)

        self.sends.append((cond, mk))
        if cond is None:
            mk().start()
        else:
            pl.when(cond)(lambda: mk().start())

    def wait(self, cond, ref, sem):
        def w():
            pltpu.make_async_copy(ref(), ref(), sem).wait()

        if cond is None:
            w()
        else:
            pl.when(cond)(w)

    def finish(self):
        for cond, mk in self.sends:
            if cond is None:
                mk().wait_send()
            else:
                pl.when(cond)(lambda mk=mk: mk().wait_send())


def strips(rows, body, step=16):
    def it(i, _):
        body(pl.ds(pl.multiple_of(i * step, step), step))
        return 0

    lax.fori_loop(0, rows // step, it, 0)


def wide(v):
    return v.astype(F32)


class Scatter:
    def __init__(self, net, cut, P, bufs):
        self.net, self.cut, self.P = net, cut, P
        (self.mid1, self.mid2, self.fx, self.fy, self.be, self.ab, self.bbe, self.bab, self.bm,
         self.m1s, self.m2s, self.fxs, self.fys, self.bes, self.abs_, self.bbes, self.babs, self.bms) = bufs
        self.R = P.shape[2]
        self.h = cut // 2
        self.rb = self.R - cut
        self.hb = self.rb // 2

    def mid_send(self, zd):
        net, P, h = self.net, self.P, self.h
        net.go(None, lambda: P.at[net.ud, zd, pl.ds(0, h), :], lambda: self.mid1.at[zd], lambda: self.m1s.at[zd], net.xn)
        net.go(None, lambda: P.at[net.ud, zd, pl.ds(h, h), :], lambda: self.mid2.at[zd], lambda: self.m2s.at[zd], net.yn)

    def bfirst(self, zd):
        net, P, cut, rb = self.net, self.P, self.cut, self.rb
        if rb and zd > 0:
            net.go(net.at[0], lambda: P.at[:, zd, pl.ds(cut, rb), :], lambda: self.bbe.at[zd], lambda: self.bbes.at[zd], net.up)
        if rb and zd < 3:
            net.go(net.at[3], lambda: P.at[:, zd, pl.ds(cut, rb), :], lambda: self.bab.at[zd], lambda: self.babs.at[zd], net.dn)

    def direct(self, zd):
        net, P, h = self.net, self.P, self.h
        net.go(None, lambda: P.at[net.ux, zd, pl.ds(0, h), :], lambda: self.fx.at[zd, pl.ds(0, h), :], lambda: self.fxs.at[zd, 0], net.xn)
        net.go(None, lambda: P.at[net.uy, zd, pl.ds(h, h), :], lambda: self.fy.at[zd, pl.ds(h, h), :], lambda: self.fys.at[zd, 1], net.yn)

    def first(self, zd):
        self.mid_send(zd)
        self.bfirst(zd)
        self.direct(zd)

    def mids(self, zd):
        net, P, h, mid1, mid2 = self.net, self.P, self.h, self.mid1, self.mid2

        def add1(sl):
            mid1[zd, sl, :] = (wide(mid1[zd, sl, :]) + wide(P[net.uy, zd, sl, :])).astype(BF)

        def add2(sl):
            mid2[zd, sl, :] = (wide(mid2[zd, sl, :]) + wide(P[net.ux, zd, pl.ds(h + sl.start, 16), :])).astype(BF)

        net.wait(None, lambda: mid1.at[zd], self.m1s.at[zd])
        strips(h, add1)
        net.go(None, lambda: mid1.at[zd], lambda: self.fy.at[zd, pl.ds(0, h), :], lambda: self.fys.at[zd, 0], net.yn)
        net.wait(None, lambda: mid2.at[zd], self.m2s.at[zd])
        strips(h, add2)
        net.go(None, lambda: mid2.at[zd], lambda: self.fx.at[zd, pl.ds(h, h), :], lambda: self.fxs.at[zd, 1], net.xn)

    def route(self, zd, zz):
        if zz < zd:
            return True, self.net.up
        return False, self.net.dn

    def bhop(self, zd, zz):
        net, P, cut, rb = self.net, self.P, self.cut, self.rb
        if not rb:
            return
        upward, dev = self.route(zd, zz)
        buf, sems = (self.bbe, self.bbes) if upward else (self.bab, self.babs)
        here = net.at[zz]
        net.wait(here, lambda: buf.at[zd], sems.at[zd])

        def add():
            for q in range(4):
                def one(sl, q=q):
                    buf[zd, q, sl, :] = (wide(buf[zd, q, sl, :]) + wide(P[q, zd, pl.ds(cut + sl.start, 16), :])).astype(BF)
                strips(rb, one)

        pl.when(here)(add)
        net.go(here, lambda: buf.at[zd], lambda: buf.at[zd], lambda: sems.at[zd], dev)

    def square(self, zd, cond):
        net, h = self.net, self.h
        for half in (0, 1):
            net.wait(cond, lambda: self.fx.at[zd, pl.ds(half * h, h), :], self.fxs.at[zd, half])
            net.wait(cond, lambda: self.fy.at[zd, pl.ds(half * h, h), :], self.fys.at[zd, half])

    def local(self, zd, sl):
        return wide(self.P[self.net.u, zd, sl, :]) + wide(self.fx[zd, sl, :]) + wide(self.fy[zd, sl, :])

    def hop(self, zd, zz):
        net = self.net
        upward, dev = self.route(zd, zz)
        buf, sems = (self.be, self.bes) if upward else (self.ab, self.abs_)
        here = net.at[zz]
        self.square(zd, here)
        if zz in (0, 3):
            def begin(sl):
                self.fx[zd, sl, :] = self.local(zd, sl).astype(BF)

            pl.when(here)(lambda: strips(self.cut, begin))
            net.go(here, lambda: self.fx.at[zd], lambda: buf.at[zd], lambda: sems.at[zd], dev)
        else:
            def plus(sl):
                buf[zd, sl, :] = (self.local(zd, sl) + wide(buf[zd, sl, :])).astype(BF)

            net.wait(here, lambda: buf.at[zd], sems.at[zd])
            pl.when(here)(lambda: strips(self.cut, plus))
            net.go(here, lambda: buf.at[zd], lambda: buf.at[zd], lambda: sems.at[zd], dev)

    def bquad(self):
        net, P, cut, rb, hb, bm, bms = self.net, self.P, self.cut, self.rb, self.hb, self.bm, self.bms
        if not rb:
            return
        z = net.z
        net.wait(net.has_dn, lambda: self.bbe.at[z], self.bbes.at[z])
        net.wait(net.has_up, lambda: self.bab.at[z], self.babs.at[z])
        for q in range(4):
            def fold(sl, q=q):
                s = wide(P[q, z, pl.ds(cut + sl.start, 16), :])
                s = s + jnp.where(net.has_dn, wide(self.bbe[z, q, sl, :]), 0.0)
                s = s + jnp.where(net.has_up, wide(self.bab[z, q, sl, :]), 0.0)
                bm[q, sl, :] = s.astype(BF)
            strips(rb, fold)
        net.go(None, lambda: bm.at[net.ud, pl.ds(0, hb), :], lambda: bm.at[4, pl.ds(0, hb), :], lambda: bms.at[0], net.xn)
        net.go(None, lambda: bm.at[net.ud, pl.ds(hb, hb), :], lambda: bm.at[5, pl.ds(0, hb), :], lambda: bms.at[1], net.yn)
        net.go(None, lambda: bm.at[net.ux, pl.ds(0, hb), :], lambda: bm.at[6, pl.ds(0, hb), :], lambda: bms.at[2], net.xn)
        net.go(None, lambda: bm.at[net.uy, pl.ds(hb, hb), :], lambda: bm.at[7, pl.ds(hb, hb), :], lambda: bms.at[3], net.yn)

    def bquad2(self):
        net, rb, hb, bm, bms = self.net, self.rb, self.hb, self.bm, self.bms
        if not rb:
            return

        def add4(sl):
            bm[4, sl, :] = (wide(bm[4, sl, :]) + wide(bm[net.uy, sl, :])).astype(BF)

        def add5(sl):
            bm[5, sl, :] = (wide(bm[5, sl, :]) + wide(bm[net.ux, pl.ds(hb + sl.start, 16), :])).astype(BF)

        net.wait(None, lambda: bm.at[4, pl.ds(0, hb), :], bms.at[0])
        strips(hb, add4)
        net.go(None, lambda: bm.at[4, pl.ds(0, hb), :], lambda: bm.at[7, pl.ds(0, hb), :], lambda: bms.at[4], net.yn)
        net.wait(None, lambda: bm.at[5, pl.ds(0, hb), :], bms.at[1])
        strips(hb, add5)
        net.go(None, lambda: bm.at[5, pl.ds(0, hb), :], lambda: bm.at[6, pl.ds(hb, hb), :], lambda: bms.at[5], net.xn)

    def last(self, store):
        net, cut, rb, hb, bm, bms = self.net, self.cut, self.rb, self.hb, self.bm, self.bms
        z = net.z
        self.square(z, None)

        def own(sl):
            s = self.local(z, sl)
            s = s + jnp.where(net.has_dn, wide(self.be[z, sl, :]), 0.0)
            s = s + jnp.where(net.has_up, wide(self.ab[z, sl, :]), 0.0)
            store(sl, s)

        net.wait(net.has_dn, lambda: self.be.at[z], self.bes.at[z])
        net.wait(net.has_up, lambda: self.ab.at[z], self.abs_.at[z])
        strips(cut, own)
        if rb:
            net.wait(None, lambda: bm.at[6, pl.ds(0, hb), :], bms.at[2])
            net.wait(None, lambda: bm.at[6, pl.ds(hb, hb), :], bms.at[5])
            net.wait(None, lambda: bm.at[7, pl.ds(0, hb), :], bms.at[4])
            net.wait(None, lambda: bm.at[7, pl.ds(hb, hb), :], bms.at[3])
            strips(rb, lambda sl: store(
                pl.ds(cut + sl.start, 16), wide(bm[net.u, sl, :]) + wide(bm[6, sl, :]) + wide(bm[7, sl, :])))


def steps_of(sc, text):
    names = {"m": sc.mid_send, "f": sc.bfirst, "d": sc.direct, "M": sc.mids, "h": sc.hop, "b": sc.bhop, "Q": sc.bquad, "q": sc.bquad2}
    return [functools.partial(names[word[0]], *[int(digit) for digit in word[1:]]) for word in text.split()]


def run_steps(steps):
    for one in steps:
        one()


def rs_scratch(cut, R, D):
    h, rb = cut // 2, R - cut
    V = lambda *s: pltpu.VMEM(s, BF)
    S = pltpu.SemaphoreType.DMA
    return [V(4, h, D), V(4, h, D), V(4, cut, D), V(4, cut, D), V(4, cut, D), V(4, cut, D),
            V(4, 4, max(rb, 16), D), V(4, 4, max(rb, 16), D), V(8, max(rb, 16), D),
            S((4,)), S((4,)), S((4, 2)), S((4, 2)), S((4,)), S((4,)), S((4,)), S((4,)), S((6,))]


def rs_kernel(cut, P, o_ref, ssem, *scr):
    net = Net(ssem)
    net.barrier()
    sc = Scatter(net, cut, P, scr)

    def store(sl, v):
        o_ref[sl, :] = v.astype(o_ref.dtype)

    for zd in (3, 0, 2, 1):
        sc.first(zd)
    for zd in (3, 0, 2, 1):
        sc.mids(zd)
    sc.hop(3, 0); sc.hop(0, 3); sc.bhop(3, 1); sc.bhop(0, 2)
    sc.hop(2, 0); sc.hop(1, 3); sc.bhop(2, 1); sc.bhop(1, 2)
    sc.hop(3, 1); sc.hop(0, 2); sc.bhop(3, 2); sc.bhop(0, 1)
    sc.hop(1, 0); sc.hop(2, 3); sc.bquad()
    sc.hop(2, 1); sc.hop(1, 2)
    sc.hop(3, 2); sc.hop(0, 1); sc.bquad2()
    sc.last(store)
    net.finish()


def rs16(p, cid, cut=96, dtype=F32):
    _, _, R, D = p.shape
    DMA = pltpu.SemaphoreType.DMA
    return pl.pallas_call(
        functools.partial(rs_kernel, cut),
        out_shape=jax.ShapeDtypeStruct((R, D), dtype),
        in_specs=[pl.BlockSpec(memory_space=pltpu.VMEM)],
        out_specs=pl.BlockSpec(memory_space=pltpu.VMEM),
        scratch_shapes=[DMA((96,))] + rs_scratch(cut, R, D),
        compiler_params=pltpu.CompilerParams(collective_id=cid, has_side_effects=True, vmem_limit_bytes=56 * 2**20),
        name="scatter_rows",
    )(p)


class Gather:
    def __init__(self, net, rows, cut, at, plane, sems):
        self.net, self.rows, self.cut, self.ref, self.plane = net, rows, cut, at, plane
        self.zr, self.xr, self.yr, self.d1, self.d2, self.br, self.bz = sems
        self.h, self.rb = cut // 2, rows - cut
        self.hb = self.rb // 2
        z = net.z
        self.near = []
        for s in range(4):
            zl, zh = z - s, z + s
            self.near.append((
                (jnp.maximum(zl, 0), zl >= 0, jnp.logical_and(zl >= 0, net.has_up), net.up),
                (jnp.minimum(zh, 3), zh < 4, jnp.logical_and(zh < 4, net.has_dn), net.dn)))

    def same(self, cond, uu, zz, lo, n, sem, dev):
        ref = lambda: self.ref(uu, zz, lo, n)
        self.net.go(cond, ref, ref, sem, dev)

    def outward(self, zz, cond):
        net, cut = self.net, self.cut
        self.same(cond, net.u, zz, 0, cut, lambda: self.xr.at[zz], net.xn)
        self.same(cond, net.u, zz, 0, cut, lambda: self.yr.at[zz], net.yn)

    def begin(self):
        net, cut, rb, z = self.net, self.cut, self.rb, self.net.z
        self.same(net.has_up, net.u, z, 0, cut, lambda: self.zr.at[z], net.up)
        self.same(net.has_dn, net.u, z, 0, cut, lambda: self.zr.at[z], net.dn)
        if rb:
            self.same(None, net.u, z, cut, rb, lambda: self.br.at[0], net.xn)
            self.same(None, net.u, z, cut, rb, lambda: self.br.at[1], net.yn)
        self.outward(z, None)

    def begin2(self):
        net, cut, rb, hb, z = self.net, self.cut, self.rb, self.hb, self.net.z
        if rb:
            net.wait(None, lambda: self.ref(net.ux, z, cut, rb), self.br.at[0])
            self.same(None, net.ux, z, cut, hb, lambda: self.br.at[2], net.yn)
            net.wait(None, lambda: self.ref(net.uy, z, cut, rb), self.br.at[1])
            self.same(None, net.uy, z, cut + hb, hb, lambda: self.br.at[3], net.xn)

    def along(self, s):
        net = self.net
        for zz, cond, fwd, dev in self.near[s]:
            net.wait(cond, lambda zz=zz: self.ref(net.u, zz, 0, self.cut), self.zr.at[zz])
            self.same(fwd, net.u, zz, 0, self.cut, lambda zz=zz: self.zr.at[zz], dev)
            self.outward(zz, cond)

    def quads(self, s):
        net, cut, rb, hb, z = self.net, self.cut, self.rb, self.hb, self.net.z
        if not rb:
            return
        if s == 0:
            net.wait(None, lambda: self.ref(net.ud, z, cut, hb), self.br.at[2])
            net.wait(None, lambda: self.ref(net.ud, z, cut + hb, hb), self.br.at[3])
            whole = lambda: self.plane(z, cut, rb)
            net.go(net.has_up, whole, whole, lambda: self.bz.at[z], net.up)
            net.go(net.has_dn, whole, whole, lambda: self.bz.at[z], net.dn)
            return
        for zz, cond, fwd, dev in self.near[s]:
            whole = lambda zz=zz: self.plane(zz, cut, rb)
            net.wait(cond, whole, self.bz.at[zz])
            net.go(fwd, whole, whole, lambda zz=zz: self.bz.at[zz], dev)

    def planes(self, s):
        if s == 0:
            return ((self.net.z, None),)
        return tuple((zz, cond) for zz, cond, _f, _d in self.near[s])

    def cross(self, s):
        net, h, cut = self.net, self.h, self.cut
        for zz, cond in self.planes(s):
            net.wait(cond, lambda zz=zz: self.ref(net.ux, zz, 0, cut), self.xr.at[zz])
            self.same(cond, net.ux, zz, 0, h, lambda zz=zz: self.d1.at[zz], net.yn)
            net.wait(cond, lambda zz=zz: self.ref(net.uy, zz, 0, cut), self.yr.at[zz])
            self.same(cond, net.uy, zz, h, h, lambda zz=zz: self.d2.at[zz], net.xn)

    def settle(self, s):
        net, h = self.net, self.h
        for zz, cond in self.planes(s):
            net.wait(cond, lambda zz=zz: self.ref(net.ud, zz, 0, h), self.d1.at[zz])
            net.wait(cond, lambda zz=zz: self.ref(net.ud, zz, h, h), self.d2.at[zz])


def ag_sems():
    S = pltpu.SemaphoreType.DMA
    return [S((4,)) for _ in range(7)]


def greet(net, chips=16):
    bar = pltpu.get_barrier_semaphore()

    def hello(j, _):
        t = lax.rem(net.u * 4 + net.z + j, chips)
        pl.semaphore_signal(bar, inc=1, device_id=(t // 4, lax.rem(t, 4), net.c), device_id_type=MESH)
        return 0

    lax.fori_loop(1, chips, hello, 0)
    pl.semaphore_signal(bar, inc=1, device_id=(net.u, net.z, 1 - net.c), device_id_type=MESH)
    pl.semaphore_wait(bar, chips)


def each_chip(net, body, chips=16):
    def one(j, _):
        t = lax.rem(net.u * 4 + net.z + j, chips)
        body(t, (t // 4, lax.rem(t, 4), net.c))
        return 0

    lax.fori_loop(1, chips, one, 0)


def remote(src, dst, ssem, rsem, dev):
    return pltpu.make_async_remote_copy(
        src_ref=src, dst_ref=dst, send_sem=ssem, recv_sem=rsem, device_id=dev, device_id_type=MESH)


def landed(ref, sem):
    pltpu.make_async_copy(ref, ref, sem).wait()


def row_sums(v):
    return jnp.sum(v.T, axis=0, keepdims=True)


def column(row):
    return jnp.broadcast_to(row, (row.shape[1], row.shape[1])).T


def share_sums(net, sums, sums_all, out, lsem, ssem, rsem):
    me = net.u * 4 + net.z
    own = pltpu.make_async_copy(sums, sums_all.at[me], lsem)
    own.start()
    each_chip(net, lambda t, dev: remote(sums, sums_all.at[me], ssem, rsem, dev).start())
    own.wait()
    part = sums_all.at[pl.ds(0, 15)]
    landed(part, rsem)
    total = sums_all[0]
    for i in range(1, 16):
        total = total + sums_all[i]
    out[...] = total
    landed(part, ssem)


def greet_all(net, count=32):
    bar = pltpu.get_barrier_semaphore()
    me = net.u * 8 + net.z * 2 + net.c

    def hello(j, _):
        t = lax.rem(me + j, count)
        pl.semaphore_signal(bar, inc=1, device_id=(t // 8, lax.rem(t, 8) // 2, lax.rem(t, 2)), device_id_type=MESH)
        return 0

    lax.fori_loop(1, count, hello, 0)
    pl.semaphore_wait(bar, count - 1)


def qkv_kernel(cut, x_ref, wq, wk, wv, block, cot, n1_o, lin, wf, tot, sw, C, X, nb, gain, sums, sums_all, lsem, nsem, msem, ssem, csem, *gs):
    net = Net(ssem)
    u, z, c = net.u, net.z, net.c
    me = u * 4 + z
    rows, width = X.shape[2], X.shape[3]
    partner = (u, z, 1 - c)
    own = pltpu.make_async_copy(x_ref, X.at[u, z], lsem.at[0])
    own.start()

    def piece(t, i):
        return ((wq, wk, wv)[i].at[:, pl.ds(pl.multiple_of(t * 128, 128), 128)], wf.at[me, c, :, pl.ds(i * 128, 128)])

    own_w = [pltpu.make_async_copy(*piece(me, i), lsem.at[1]) for i in range(3)]
    for one in own_w:
        one.start()
    own_c = pltpu.make_async_copy(cot, C.at[u, z], lsem.at[3])
    own_c.start()
    dev_me = me * 2 + c
    greet_all(net)
    own.wait()
    ga = Gather(net, rows, cut, lambda uu, zz, lo, n: X.at[uu, zz, pl.ds(lo, n), :],
                lambda zz, lo, n: X.at[:, zz, pl.ds(lo, n), :], gs[:7])
    netc = Net(csem)
    gc = Gather(netc, rows, cut, lambda uu, zz, lo, n: C.at[uu, zz, pl.ds(lo, n), :],
                lambda zz, lo, n: C.at[:, zz, pl.ds(lo, n), :], gs[7:])
    ga.begin()

    def tell(j, _):
        t = lax.rem(dev_me + j, 32)
        remote(block.at[t // 2], sw.at[dev_me], msem.at[6], msem.at[7], (t // 8, lax.rem(t, 8) // 2, lax.rem(t, 2))).start()
        return 0

    lax.fori_loop(1, 32, tell, 0)
    sw[dev_me] = block[me]

    def columns(t, dev):
        for i in range(3):
            remote(*piece(t, i), msem.at[0], msem.at[1], dev).start()

    each_chip(net, columns)

    def plane(zz):
        def chunk(uu, _):
            slot = lax.rem(uu, 2)
            k = uu * 4 + zz

            def norm(i, _):
                sl = pl.ds(pl.multiple_of(i * 16, 16), 16)
                v = X[uu, zz, sl, :].astype(F32)
                r = lax.rsqrt(jnp.mean(v * v, axis=1, keepdims=True) + EPS)
                nb[slot, sl, :] = (v * r * gain[...]).astype(BF)
                return 0

            def stored(s):
                return pltpu.make_async_copy(nb.at[s], n1_o.at[k], nsem.at[s])

            pl.when(uu >= 2)(lambda: stored(slot).wait())
            lax.fori_loop(0, rows // 16, norm, 0)
            stored(slot).start()
            got = dot(nb[slot], wf[...].reshape(width, wf.shape[-1]), ((1,), (0,)))
            lin[k] = got
            q, kk = got[:, :128], got[:, 128:256]
            sums[pl.ds(k, 1), :] = row_sums(q * q)
            sums[pl.ds(16 + k, 1), :] = row_sums(kk * kk)
            return 0

        lax.fori_loop(0, 4, chunk, 0)
        for s in (0, 1):
            pltpu.make_async_copy(nb.at[s], n1_o.at[0], nsem.at[s]).wait()

    def compute(s):
        for zz, cond in ga.planes(s):
            if cond is None:
                plane(zz)
            else:
                pl.when(cond)(lambda zz=zz: plane(zz))

    ga.begin2()
    ga.along(1)
    ga.quads(0)
    ga.cross(0)
    landed(wf.at[0, 0], lsem.at[1])
    landed(wf.at[pl.ds(0, 15), 0], msem.at[1])
    to_partner = remote(wf.at[:, c], wf.at[:, c], msem.at[2], msem.at[3], partner)
    to_partner.start()
    own_c.wait()
    ga.along(2)
    ga.quads(1)
    ga.cross(1)
    gc.begin()
    landed(sw.at[pl.ds(0, 31)], msem.at[7])
    for e in range(16):
        gain[:, e * 128 : (e + 1) * 128] = sw[2 * e, 2:3, :] + sw[2 * e + 1, 2:3, :]
    ga.settle(0)
    landed(wf.at[:, 1 - c], msem.at[3])
    compute(0)
    gc.begin2()
    ga.along(3)
    ga.quads(2)
    ga.cross(2)
    ga.settle(1)
    gc.along(1)
    gc.quads(0)
    gc.cross(0)
    compute(1)
    ga.quads(3)
    ga.cross(3)
    ga.settle(2)
    gc.along(2)
    gc.quads(1)
    gc.cross(1)
    compute(2)
    ga.settle(3)
    gc.along(3)
    gc.quads(2)
    gc.cross(2)
    compute(3)
    landed(wf.at[pl.ds(0, 15), 0], msem.at[0])
    landed(wf.at[:, c], msem.at[2])
    share_sums(net, sums, sums_all, tot, lsem.at[2], msem.at[4], msem.at[5])
    gc.quads(3)
    gc.cross(3)
    for s in range(4):
        gc.settle(s)
    landed(sw.at[pl.ds(0, 31)], msem.at[6])
    net.finish()
    netc.finish()


def run_qkv(x, wq, wk, wv, block, cot, cid, cut=96):
    R, D = x.shape
    N = 384
    DMA = pltpu.SemaphoreType.DMA
    S = jax.ShapeDtypeStruct
    V = lambda *s: pltpu.VMEM(s, BF)
    VF = lambda *s: pltpu.VMEM(s, F32)
    A = pl.BlockSpec(memory_space=pl.ANY)
    M = pl.BlockSpec(memory_space=pltpu.VMEM)
    return pl.pallas_call(
        functools.partial(qkv_kernel, cut),
        out_shape=(S((16, R, D), BF), S((16, R, N), F32), S((16, 2, R // 2, N), BF), S((32, 128), F32),
                   S((32, 8, 128), F32), S((4, 4) + cot.shape, BF)),
        in_specs=[A, A, A, A, M, A],
        out_specs=(A, M, M, M, M, A),
        scratch_shapes=[V(4, 4, R, D), V(2, R, D), VF(1, D), VF(32, 128), VF(16, 32, 128),
                        DMA((4,)), DMA((2,)), DMA((8,)), DMA((64,)), DMA((64,))] + ag_sems() + ag_sems(),
        compiler_params=pltpu.CompilerParams(collective_id=cid, has_side_effects=True, vmem_limit_bytes=40 * 2**20),
        name="project",
    )(x, wq, wk, wv, block, cot)


def group_of(t):
    g = t // 2
    return jnp.where(g == 0, 3, jnp.where(g == 1, 0, jnp.where(g == 2, 2, 1)))


def expert_kernel(cut, n2, cot_a, cot_b, share, gate, up, down, d_n2, p_out, n2_o, other, dg_o, du_o, dd_o,
                  X, C, GU, W, A, hid, pb, fs, lsem, wsem, wrs, psem, tsem, osem, ors, fsem, sa, sr, *scr):
    ga_sems, rs_bufs = scr[:7], scr[7:]
    na, nr = Net(sa), Net(sr)
    u, z, c = na.u, na.z, na.c
    partner = (u, z, 1 - c)
    rows, width = X.shape[2], X.shape[3]
    ff = W.shape[0]
    half, half_ff = gate.shape[0], down.shape[0]
    tokens = 16 * rows
    tile = 256
    span = 512
    side = width // 2
    first = [pltpu.make_async_copy(n2, X.at[u, z], lsem.at[0]),
             pltpu.make_async_copy(cot_a, C.at[:, :, :, pl.ds(0, side)], lsem.at[1]),
             pltpu.make_async_copy(cot_b, C.at[:, :, :, pl.ds(side, side)], lsem.at[5])]

    def weights():
        mine = pl.ds(pl.multiple_of(c * half, half), half)
        mine_ff = pl.ds(pl.multiple_of(c * half_ff, half_ff), half_ff)
        return ((gate, GU.at[mine, pl.ds(0, ff)]), (up, GU.at[mine, pl.ds(ff, ff)]), (down, W.at[mine_ff, :]))

    own_w = [pltpu.make_async_copy(a, b, lsem.at[2 + i]) for i, (a, b) in enumerate(weights())]
    for one in first + own_w:
        one.start()
    na.barrier((partner,))
    first[0].wait()

    def gather(net, buf, sems):
        return Gather(net, rows, cut, lambda uu, zz, lo, n: buf.at[uu, zz, pl.ds(lo, n), :],
                      lambda zz, lo, n: buf.at[:, zz, pl.ds(lo, n), :], sems)

    ga = gather(na, X, ga_sems)
    ga.begin()
    sent_w = [remote(a, b, wsem.at[i], wrs.at[i], partner) for i, (a, b) in enumerate(weights())]
    for one in sent_w:
        one.start()

    def forward(zz):
        pltpu.make_async_copy(X.at[:, zz], n2_o.at[:, zz], psem.at[1]).start()

        def inner(n, _):
            gcols = pl.ds(pl.multiple_of(n * span, span), span)
            ucols = pl.ds(pl.multiple_of(ff + n * span, span), span)
            xv = X[:, zz].reshape(4 * rows, width)
            g = dot(xv, GU[:, gcols], ((1,), (0,)))
            uu = dot(xv, GU[:, ucols], ((1,), (0,)))
            hid[:, zz, :, gcols] = (g * jax.nn.sigmoid(g) * uu).astype(BF).reshape(4, rows, span)
            A[:, zz, :, gcols] = g.astype(BF).reshape(4, rows, span)
            A[:, zz, :, ucols] = uu.astype(BF).reshape(4, rows, span)
            return 0

        lax.fori_loop(0, ff // span, inner, 0)
        weight = share[:, zz]

        def flushed(n):
            cols = pl.ds(pl.multiple_of(n * span, span), span)
            slot = lax.rem(n, 2)
            return pltpu.make_async_copy(pb.at[slot], p_out.at[:, zz, :, cols], osem.at[slot])

        def outer(n, _):
            cols = pl.ds(pl.multiple_of(n * span, span), span)
            made = dot(hid[:, zz].reshape(4 * rows, ff), W[:, cols], ((1,), (0,)))
            made = made.astype(BF).astype(F32).reshape(4, rows, span)
            pl.when(n >= 2)(lambda: flushed(n - 2).wait())
            pb[lax.rem(n, 2)] = (weight * made).astype(BF)
            flushed(n).start()
            return 0

        count = width // span
        lax.fori_loop(0, count, outer, 0)
        flushed(count - 2).wait()
        flushed(count - 1).wait()

    def planes(s):
        if s == 0:
            forward(z)
            return

        def one(d, _):
            zz = jnp.where(d == 0, z - s, z + s)
            pl.when(jnp.logical_and(zz >= 0, zz < 4))(lambda: forward(zz))
            return 0

        lax.fori_loop(0, 2, one, 0)

    ga.begin2()
    ga.along(1)
    ga.quads(0)
    ga.cross(0)
    ga.along(2)
    ga.quads(1)
    ga.cross(1)
    ga.settle(0)
    for one in own_w:
        one.wait()
    for one in sent_w:
        one.wait_recv()
    planes(0)
    ga.along(3)
    ga.quads(2)
    ga.cross(2)
    ga.settle(1)
    planes(1)
    ga.quads(3)
    ga.cross(3)
    ga.settle(2)
    planes(2)
    ga.settle(3)
    planes(3)
    na.finish()
    first[1].wait()
    first[2].wait()
    for one in sent_w:
        one.wait_send()
    landed(X, psem.at[1])
    sc = Scatter(nr, cut, X, rs_bufs)

    def backward(t):
        zd = group_of(t)

        def inner(n, _):
            gcols = pl.ds(pl.multiple_of(n * span, span), span)
            ucols = pl.ds(pl.multiple_of(ff + n * span, span), span)
            dh = dot(C[:, zd].reshape(4 * rows, width), W[gcols, :], ((1,), (1,)))
            g = wide(A[:, zd, :, gcols]).reshape(4 * rows, span)
            uu = wide(A[:, zd, :, ucols]).reshape(4 * rows, span)
            s = jax.nn.sigmoid(g)
            A[:, zd, :, gcols] = (dh * uu * s * (1.0 + g * (1.0 - s))).astype(BF).reshape(4, rows, span)
            A[:, zd, :, ucols] = (dh * g * s).astype(BF).reshape(4, rows, span)
            return 0

        def outer(n, _):
            cols = pl.ds(pl.multiple_of(n * span, span), span)
            back = dot(A[:, zd].reshape(4 * rows, 2 * ff), GU[cols, :], ((1,), (1,)))
            X[:, zd, :, cols] = back.astype(BF).reshape(4, rows, span)
            return 0

        def scale(i, _):
            sl = pl.ds(pl.multiple_of(i * 16, 16), 16)
            C[:, zd, sl, :] = (share[:, zd, sl, :] * C[:, zd, sl, :].astype(F32)).astype(BF)
            return 0

        @pl.when(lax.rem(t, 2) == 0)
        def _():
            lax.fori_loop(0, rows // 16, scale, 0)
            lax.fori_loop(0, ff // span, inner, 0)

        @pl.when(lax.rem(t, 2) == 1)
        def _():
            lax.fori_loop(0, width // span, outer, 0)

    def acts(steps, t):
        for at, todo in steps.items():
            def act(todo=todo):
                for one in todo:
                    one()
            pl.when(t == at)(act)

    def at_turns(table):
        return {t: steps_of(sc, words) for t, words in table.items()}

    steps = at_turns({1: "m3 f3 d3", 3: "m0 f0 d0 M3", 4: "b31", 5: "m2 f2 d2 M0", 6: "h30 b02 b32", 7: "m1 f1 d1 M2 h03"})

    def turn(t, _):
        backward(t)
        acts(steps, t)
        return 0

    lax.fori_loop(0, 8, turn, 0)

    GU4 = GU.reshape(4, 4, rows, width)
    left = W.at[pl.ds(0, tile), :]

    def tile_load(k, which):
        slot = lax.rem(k, 2)
        cols = pl.ds(pl.multiple_of((which * 4 + k) * tile, tile), tile)
        return pltpu.make_async_copy(
            n2_o.at[:, :, :, cols], GU4.at[:, :, :, pl.ds(pl.multiple_of(slot * tile, tile), tile)], tsem.at[slot])

    def left_tokens(k):
        cols = pl.ds(pl.multiple_of(lax.rem(k, 2) * tile, tile), tile)

        def one(b, _):
            sl = pl.ds(pl.multiple_of(b * tile, tile), tile)
            left[:, sl] = GU[sl, cols].T
            return 0

        lax.fori_loop(0, tokens // tile, one, 0)

    def left_hidden(k, which):
        cols = pl.ds(pl.multiple_of((which * 2 + k) * tile, tile), tile)
        flat = hid.reshape(tokens, ff)

        def one(b, _):
            sl = pl.ds(pl.multiple_of(b * tile, tile), tile)
            left[:, sl] = flat[sl, cols].T
            return 0

        lax.fori_loop(0, tokens // tile, one, 0)

    def products(right, store):
        flat = right.reshape(tokens, width)

        def one(n, _):
            cols = pl.ds(pl.multiple_of(n * 512, 512), 512)
            store(cols, n, dot(left[...], flat[:, cols], ((1,), (0,))))
            return 0

        lax.fori_loop(0, width // 512, one, 0)

    def sent(k):
        slot = W.at[pl.ds(pl.multiple_of(tile + lax.rem(k, 2) * tile, tile), tile), :]
        return slot, remote(slot, other.at[k], osem.at[k], ors.at[k], partner)

    tile_load(0, 1 - c).start()

    def other_tile(k, _):
        slot, copy = sent(k)

        @pl.when(k >= 2)
        def _():
            sent(k - 2)[1].wait_send()

        def store(cols, n, v):
            slot[:, cols] = v.astype(BF)

        @pl.when(k < 4)
        def _():
            pl.when(k < 3)(lambda: tile_load(k + 1, 1 - c).start())
            tile_load(k, 1 - c).wait()
            left_tokens(k)
            products(A, store)

        @pl.when(k >= 4)
        def _():
            left_hidden(k - 4, 1 - c)
            products(C, store)

        copy.start()
        acts(at_turns({0: "h31 b01 b21", 1: "M1 h02", 2: "h20", 3: "h23 b12 h32", 4: "h01", 5: "h10"}), k)
        return 0

    lax.fori_loop(0, 6, other_tile, 0)

    def store_out(sl, v):
        d_n2[sl, :] = v

    tile_load(0, c).start()
    got = W.at[pl.ds(3 * tile, tile), :]

    def flush(k, h):
        i = pl.ds(pl.multiple_of(lax.rem(k, 4) * tile, tile), tile)

        def go(dst):
            pltpu.make_async_copy(fs.at[h], dst, fsem.at[h]).start()

        pl.when(k < 4)(lambda: go((dg_o, du_o)[h].at[i, :]))
        pl.when(k >= 4)(lambda: go(dd_o.at[i, pl.ds(h * 1024, 1024)]))

    def own_tile(k, _):
        fetch = pltpu.make_async_copy(other.at[k], got, lsem.at[0])
        landed(other.at[k], ors.at[k])
        fetch.start()

        def finish(right):
            flat = right.reshape(tokens, width)
            fetch.wait()
            for h in (0, 1):
                pl.when(k > 0)(lambda: landed(fs.at[h], fsem.at[h]))
                for n in (0, 1):
                    cols = pl.ds(h * 1024 + n * 512, 512)
                    fs[h, :, n * 512 : (n + 1) * 512] = dot(left[...], flat[:, cols], ((1,), (0,))) + wide(got[:, cols])
                flush(k, h)

        @pl.when(k < 4)
        def _():
            pl.when(k < 3)(lambda: tile_load(k + 1, c).start())
            tile_load(k, c).wait()
            left_tokens(k)
            finish(A)

        @pl.when(k >= 4)
        def _():
            left_hidden(k - 4, c)
            finish(C)

        acts(at_turns({0: "h21", 1: "h13 Q", 3: "h12", 4: "q"}), k)
        return 0

    lax.fori_loop(0, 6, own_tile, 0)
    sc.last(store_out)
    for h in (0, 1):
        landed(fs.at[h], fsem.at[h])
    for k in (4, 5):
        sent(k)[1].wait_send()
    nr.finish()


def run_expert(n2, cot_a, cot_b, share, gate, up, down, cid, cut=96):
    R, D = n2.shape
    half, ff = gate.shape
    DMA = pltpu.SemaphoreType.DMA
    S = jax.ShapeDtypeStruct
    V = lambda *s: pltpu.VMEM(s, BF)
    A = pl.BlockSpec(memory_space=pl.ANY)
    M = pl.BlockSpec(memory_space=pltpu.VMEM)
    return pl.pallas_call(
        functools.partial(expert_kernel, cut),
        out_shape=(S((R, D), F32), S((4, 4, R, D), BF), S((4, 4, R, D), BF), S((6, 256, D), BF),
                   S((half, ff), F32), S((half, ff), F32), S(down.shape, F32)),
        in_specs=[A, A, A, M, A, A, A],
        out_specs=(M,) + (A,) * 6,
        scratch_shapes=[V(4, 4, R, D), V(4, 4, R, D), V(D, 2 * ff), V(ff, D), V(4, 4, R, 2 * ff), V(4, 4, R, ff),
                        V(2, 4, R, 512), pltpu.VMEM((2, 256, 1024), F32),
                        DMA((6,)), DMA((3,)), DMA((3,)), DMA((2,)), DMA((2,)), DMA((6,)), DMA((6,)), DMA((2,)),
                        DMA((64,)), DMA((96,))] + ag_sems() + rs_scratch(cut, R, D),
        compiler_params=pltpu.CompilerParams(collective_id=cid, has_side_effects=True, vmem_limit_bytes=63 * 2**20),
        name="expert",
    )(n2, cot_a, cot_b, share, gate, up, down)


def finish_kernel(cut, d_lin, wf, n1, att, x_in, d_res, gain, d_gain_two,
                  d_wo, d_inputs, d_wq, d_wk, d_wv, gains_o,
                  P, PO, PG, PT, wsum, nt, left, keep, give, got, send, recv, d_n1, d_gain, gb, gr,
                  lsem, tsem, msem, s1, s2, *bufs):
    net, net2 = Net(s1), Net(s2)
    u, z, c = net.u, net.z, net.c
    me = u * 4 + z
    rows, width = P.shape[2], P.shape[3]
    lanes = d_lin.shape[2]
    tokens = 16 * rows
    tile = 256
    partner = (u, z, 1 - c)
    half = len(bufs) // 2
    sc1, sc2 = Scatter(net, cut, P, bufs[:half]), Scatter(net2, cut, PO, bufs[half:])

    def tile_load(k):
        slot = lax.rem(k, 2)
        return pltpu.make_async_copy(n1.at[:, :, pl.ds(pl.multiple_of(k * tile, tile), tile)], nt.at[slot], tsem.at[slot])

    tile_load(0).start()
    greet_all(net)

    def group(zd):
        def one(n, _):
            cols = pl.ds(pl.multiple_of(n * 512, 512), 512)
            w = wf.reshape(width, lanes)
            for q in range(4):
                P[q, zd, :, cols] = dot(d_lin[q * 4 + zd], w[cols, :], ((1,), (1,))).astype(BF)
            return 0

        lax.fori_loop(0, width // 512, one, 0)

    for zd in (3, 0, 2, 1):
        group(zd)
        sc1.first(zd)

    side = width // 2
    own_cols = pl.ds(pl.multiple_of(c * side, side), side)
    give_cols = pl.ds(pl.multiple_of((1 - c) * side, side), side)

    def outer(e, _):
        turned_att = att[e].T
        PG[e // 4, lax.rem(e, 4)] = dot(turned_att, d_res[:, give_cols].astype(BF), ((1,), (0,))).astype(BF)
        PO[e // 4, lax.rem(e, 4)] = dot(turned_att, d_res[:, own_cols].astype(BF), ((1,), (0,))).astype(BF)
        return 0

    lax.fori_loop(0, 16, outer, 0)
    halves = remote(PG, PT, msem.at[6], msem.at[7], partner)
    halves.start()

    def join():
        landed(PT, msem.at[7])

        def add(e, _):
            def strip(sl):
                at = (e // 4, lax.rem(e, 4), sl, slice(None))
                PO[at] = (wide(PO[at]) + wide(PT[at])).astype(BF)

            strips(rows, strip)
            return 0

        lax.fori_loop(0, 16, add, 0)

    def store1(sl, v):
        d_n1[sl, :] = v

    def store2(sl, v):
        wsum[sl, :] = v

    def one(words):
        run_steps(steps_of(sc1, words))

    def two(words):
        run_steps(steps_of(sc2, words))

    def grads(k):
        if k < 7:
            tile_load(k + 1).start()
        tile_load(k).wait()
        slot = k % 2
        flat = nt.at[slot].reshape(tokens, tile)

        def turn(b, _):
            sl = pl.ds(pl.multiple_of(b * tile, tile), tile)
            left[:, sl] = flat[sl, :].T
            return 0

        lax.fori_loop(0, tokens // tile, turn, 0)
        made = dot(left[...], d_lin[...].reshape(tokens, lanes), ((1,), (0,)))
        for i in range(2):
            first, second = made[i * 128 : i * 128 + 64], made[i * 128 + 64 : (i + 1) * 128]
            keep[2 * k + i] = jnp.where(c == 0, first, second)
            give[2 * k + i] = jnp.where(c == 0, second, first).astype(BF)

    grads(0)
    grads(1)
    one("M3")
    grads(2)
    one("M0")
    join()
    two("m3 f3 m0 f0 m2 f2 m1 f1 d3 d0 d2 d1")
    grads(3)
    one("M2 b31 b02")
    grads(4)
    one("M1")
    grads(5)
    one("h30 h03")
    grads(6)
    grads(7)
    across = remote(give, got, msem.at[0], msem.at[1], partner)
    across.start()
    one("b21 b12 b32 b01")
    two("M3 M0 M2 M1")
    landed(got, msem.at[1])

    def total(e, _):
        send[e] = (keep[e] + wide(got[e])).astype(BF)
        return 0

    lax.fori_loop(0, 16, total, 0)
    each_chip(net, lambda t, dev: remote(send.at[t], recv.at[me], msem.at[2], msem.at[3], dev).start())
    recv[me] = send[me]
    one("h20 h13 h31 h02")
    two("b31 b02 b21 b12")
    one("Q h10 h23")
    two("h30 h03 b32 b01")
    one("h32 h01")
    two("h20 h13 h31 h02")
    one("h21 h12 q")
    sc1.last(store1)
    d_gain[...] = jnp.zeros_like(d_gain)

    def norm_back(i, _):
        sl = pl.ds(pl.multiple_of(i * 16, 16), 16)
        v, d = wide(x_in[sl, :]), d_n1[sl, :]
        r = lax.rsqrt(jnp.mean(v * v, axis=1, keepdims=True) + EPS)
        scaled = d * gain[...]
        inner = jnp.mean(scaled * v, axis=1, keepdims=True)
        d_inputs[sl, :] = d_res[sl, :] + r * scaled - v * (r * r * r * inner)
        d_gain[...] += jnp.sum(d * v * r, axis=0, keepdims=True)
        return 0

    lax.fori_loop(0, rows // 16, norm_back, 0)
    for e in range(16):
        gb[e, 0:1, :] = d_gain[:, e * 128 : (e + 1) * 128]
        gb[e, 1:2, :] = d_gain_two[:, e * 128 : (e + 1) * 128]
    dev_me = me * 2 + c

    def tell(j, _):
        t = lax.rem(dev_me + j, 32)
        remote(gb.at[t // 2], gr.at[dev_me], msem.at[4], msem.at[5], (t // 8, lax.rem(t, 8) // 2, lax.rem(t, 2))).start()
        return 0

    lax.fori_loop(1, 32, tell, 0)
    gr[dev_me] = gb[me]
    two("Q h10 h23 h32 h01 h21 h12 q")
    landed(recv.at[pl.ds(0, 15)], msem.at[3])
    for e in range(16):
        piece = wide(recv[e])
        for i, out in enumerate((d_wq, d_wk, d_wv)):
            out[:, e * 128 : (e + 1) * 128] = piece[:, i * 128 : (i + 1) * 128]
    landed(gr.at[pl.ds(0, 31)], msem.at[5])
    sums = gr[0]
    for i in range(1, 32):
        sums = sums + gr[i]
    gains_o[...] = sums
    sc2.last(store2)
    d_wo[:, own_cols] = wsum[pl.ds(pl.multiple_of(c * 64, 64), 64), :]
    theirs = remote(wsum.at[pl.ds(pl.multiple_of((1 - c) * 64, 64), 64), :], d_wo.at[:, own_cols], msem.at[8], msem.at[9], partner)
    theirs.start()
    landed(PG, msem.at[6])
    landed(give, msem.at[0])
    landed(recv.at[pl.ds(0, 15)], msem.at[2])
    landed(gr.at[pl.ds(0, 31)], msem.at[4])
    theirs.wait_send()
    landed(d_wo.at[:, give_cols], msem.at[9])
    net.finish()
    net2.finish()


def run_finish(d_lin, wf, n1, att, x_in, d_res, gain, d_gain_two, cid, cut=96):
    R, D = x_in.shape
    N = d_lin.shape[2]
    DMA = pltpu.SemaphoreType.DMA
    S = jax.ShapeDtypeStruct
    V = lambda *s: pltpu.VMEM(s, BF)
    VF = lambda *s: pltpu.VMEM(s, F32)
    A = pl.BlockSpec(memory_space=pl.ANY)
    M = pl.BlockSpec(memory_space=pltpu.VMEM)
    own = S((R // 2, D), F32)
    return pl.pallas_call(
        functools.partial(finish_kernel, cut),
        out_shape=(own, S((R, D), F32), own, own, own, S((8, 128), F32)),
        in_specs=[M, M, A] + [M] * 5,
        out_specs=(M,) * 6,
        scratch_shapes=[V(4, 4, R, D), V(4, 4, R, D // 2), V(4, 4, R, D // 2), V(4, 4, R, D // 2), VF(R, D // 2), V(2, 16, R, 256), V(256, 16 * R), VF(16, 64, N), V(16, 64, N),
                        V(16, 64, N), V(16, 64, N), V(16, 64, N), VF(R, D), VF(1, D), VF(16, 8, 128), VF(32, 8, 128),
                        DMA((1,)), DMA((2,)), DMA((10,)), DMA((64,)), DMA((64,))] + rs_scratch(cut, R, D) + rs_scratch(cut, R, D // 2),
        compiler_params=pltpu.CompilerParams(collective_id=cid, has_side_effects=True, vmem_limit_bytes=63 * 2**20),
        name="finish",
    )(d_lin, wf, n1, att, x_in, d_res, gain, d_gain_two)

def band_scores(q, k, q_seg, k_seg, scale, reach):
    scores = dot(q, k, ((1,), (1,))) * scale
    q_at = lax.broadcasted_iota(jnp.int32, scores.shape, 0)
    k_at = lax.broadcasted_iota(jnp.int32, scores.shape, 1)
    return scores, (k_seg == q_seg) & (k_at <= q_at + reach)


def turned(v, cosine, sine):
    return v * cosine + pltpu.roll(v, 64, axis=1) * sine


def turned_back(v, cosine, sine):
    return v * cosine - pltpu.roll(v, 64, axis=1) * sine


def attend_kernel(scale, pads, cut, lin, tot, cosine, sine, gq, gk, q_seg, k_seg, w_own, x_in, gain, cot, wo_o, q_rot, kv, o_ref, lse,
                  att, residual, n2, C, wo, lsem, msem, psem, ssem, csem, *gs):
    net = Net(ssem)
    u, z, c = net.u, net.z, net.c
    me = u * 4 + z
    rows = x_in.shape[0]
    width = x_in.shape[1]
    reach = pads * 2 * rows
    partner = (u, z, 1 - c)
    own = pltpu.make_async_copy(w_own, wo.at[u, z, c], lsem.at[0])
    own.start()
    own_c = pltpu.make_async_copy(cot, C.at[u, z], lsem.at[2])
    own_c.start()
    greet(net)
    own.wait()
    ga = Gather(net, rows // 2, rows // 2, lambda uu, zz, lo, n: wo.at[uu, zz, c, pl.ds(lo, n), :], None, gs[:7])
    netc = Net(csem)
    gc = Gather(netc, rows, cut, lambda uu, zz, lo, n: C.at[uu, zz, pl.ds(lo, n), :],
                lambda zz, lo, n: C.at[:, zz, pl.ds(lo, n), :], gs[7:])

    def halves(s):
        ga.settle(s)
        for zz, cond in ga.planes(s):
            ref = lambda zz=zz: wo.at[:, zz, c]
            net.go(cond, ref, ref, lambda zz=zz: psem.at[zz], partner)

    ga.begin()
    for i in range(pads):
        kv[:, i] = jnp.zeros(kv.shape[:1] + kv.shape[2:], BF)

    def ready(i, _):
        both = lin[i]
        rq = lax.rsqrt(column(tot[pl.ds(i, 1), :]) / width + EPS)
        rk = lax.rsqrt(column(tot[pl.ds(16 + i, 1), :]) / width + EPS)
        cs, sn = cosine[i], sine[i]
        q_rot[i] = turned(both[:, :128] * rq * gq[...], cs, sn).astype(BF)
        kv[0, pads + i, c] = turned(both[:, 128:256] * rk * gk[...], cs, sn).astype(BF)
        kv[1, pads + i, c] = both[:, 256:].astype(BF)
        return 0

    lax.fori_loop(0, 16, ready, 0)
    mine = kv.at[:, pl.ds(pads, 16), c]
    to_partner = remote(mine, mine, msem.at[0], msem.at[1], partner)
    to_partner.start()
    ga.along(1)
    ga.cross(0)
    own_c.wait()
    gc.begin()
    landed(kv.at[:, pl.ds(pads, 16), 1 - c], msem.at[1])

    def block(j, _):
        i = lax.rem(me + 1 + j, 16)
        first = 2 * i + c
        band = pl.ds(pl.multiple_of(first * rows, rows), rows + reach)
        kf, vf = kv.at[0].reshape((pads + 16) * 2 * rows, 128), kv.at[1].reshape((pads + 16) * 2 * rows, 128)
        scores, allowed = band_scores(q_rot[i], kf[band, :], q_seg[i], k_seg[:, band], scale, reach)
        scores = jnp.where(allowed, scores, NEG)
        top = jnp.max(scores, axis=1, keepdims=True)
        weights = jnp.where(allowed, jnp.exp(scores - top), 0.0)
        total = jnp.sum(weights, axis=1, keepdims=True)
        probs = (weights / total).astype(BF)
        o_ref[i] = dot(probs, vf[band, :], ((1,), (0,))).astype(BF)
        lse[i] = top + jnp.log(total)

        @pl.when(j < 15)
        def _():
            remote(o_ref.at[i], att.at[me], msem.at[2], msem.at[3], (i // 4, lax.rem(i, 4), c)).start()

        return 0

    lax.fori_loop(0, 5, block, 0)
    ga.along(2)
    ga.cross(1)
    halves(0)
    gc.begin2()
    lax.fori_loop(5, 10, block, 0)
    ga.along(3)
    ga.cross(2)
    halves(1)
    gc.along(1)
    gc.quads(0)
    gc.cross(0)
    lax.fori_loop(10, 16, block, 0)
    ga.cross(3)
    halves(2)
    gc.along(2)
    gc.quads(1)
    gc.cross(1)
    halves(3)
    att[me] = o_ref[me]
    part = att.at[pl.ds(0, 15)]
    landed(part, msem.at[3])
    for zz in range(4):
        landed(wo.at[:, zz, 1 - c], psem.at[zz])
    keep = pltpu.make_async_copy(wo, wo_o, lsem.at[1])
    keep.start()
    tile = 256

    def out(n, _):
        cols = pl.ds(pl.multiple_of(n * tile, tile), tile)
        acc = x_in[:, cols].astype(F32)
        for e in range(0, 16, 2):
            pair = jnp.concatenate([att[e], att[e + 1]], axis=1)
            acc = acc + dot(pair, wo[e // 4, pl.ds(e % 4, 2), :, :, cols].reshape(256, tile), ((1,), (0,)))
        residual[:, cols] = acc
        return 0

    lax.fori_loop(0, width // tile, out, 0)
    gc.along(3)
    gc.quads(2)
    gc.cross(2)

    def norm(i, _):
        sl = pl.ds(pl.multiple_of(i * 16, 16), 16)
        v = residual[sl, :]
        r = lax.rsqrt(jnp.mean(v * v, axis=1, keepdims=True) + EPS)
        n2[sl, :] = (v * r * gain[...]).astype(BF)
        return 0

    lax.fori_loop(0, rows // 16, norm, 0)
    landed(mine, msem.at[0])
    landed(part, msem.at[2])
    gc.quads(3)
    gc.cross(3)
    for s in range(4):
        gc.settle(s)
    keep.wait()
    net.finish()
    netc.finish()


def run_attend(scale, pads, lin, tot, cosine, sine, gq, gk, q_seg, k_seg, w_own, x_in, gain, cot, cid, cut=96):
    R, D = x_in.shape
    DMA = pltpu.SemaphoreType.DMA
    S = jax.ShapeDtypeStruct
    A = pl.BlockSpec(memory_space=pl.ANY)
    M = pl.BlockSpec(memory_space=pltpu.VMEM)
    wo = (4, 4, 2, R // 2, D)
    return pl.pallas_call(
        functools.partial(attend_kernel, scale, pads, cut),
        out_shape=(S(wo, BF), S((16, R, 128), BF), S((2, pads + 16, 2, R, 128), BF), S((16, R, 128), BF),
                   S((16, R, 1), F32), S((16, R, 128), BF), S((R, D), F32), S((R, D), BF), S((4, 4) + cot.shape, BF)),
        in_specs=[M] * 8 + [A, M, M, A],
        out_specs=(A,) + (M,) * 7 + (A,),
        scratch_shapes=[pltpu.VMEM(wo, BF), DMA((3,)), DMA((4,)), DMA((4,)), DMA((64,)), DMA((64,))] + ag_sems() + ag_sems(),
        compiler_params=pltpu.CompilerParams(collective_id=cid, has_side_effects=True, vmem_limit_bytes=48 * 2**20),
        name="attend",
    )(lin, tot, cosine, sine, gq, gk, q_seg, k_seg, w_own, x_in, gain, cot)


def attend_back_kernel(scale, pads, cut, d_res, wo_h, p_out, residual, q_rot, kv, q_seg, k_seg, lse, o_ref, lin, tot, cosine, sine, gq, gk,
                       d_lin, d_gains, output, P, wo, d_mine, d_out, d_q, d_k, d_v, other, got, d_un, sums, sums_all, inner,
                       lsem, msem, ssem, *bufs):
    net = Net(ssem)
    sc = Scatter(net, cut, P, bufs)
    u, z, c = net.u, net.z, net.c
    me = u * 4 + z
    rows, width = d_res.shape
    reach = pads * 2 * rows
    partner = (u, z, 1 - c)
    load = pltpu.make_async_copy(wo_h, wo, lsem.at[0])
    load.start()
    load_p = pltpu.make_async_copy(p_out, P, lsem.at[1])
    load_p.start()
    greet(net)

    def go(words):
        run_steps(steps_of(sc, words))

    load.wait()

    def send(j, _):
        e = lax.rem(me + 1 + j, 16)
        piece = dot(d_res[...], wo[e // 4, lax.rem(e, 4)].reshape(128, width), ((1,), (1,))).astype(BF)

        @pl.when(j < 15)
        def _():
            d_mine[e] = piece
            remote(d_mine.at[e], d_out.at[me], msem.at[0], msem.at[1], (e // 4, lax.rem(e, 4), c)).start()

        @pl.when(j == 15)
        def _():
            d_out[me] = piece

        return 0

    lax.fori_loop(0, 16, send, 0)
    load_p.wait()
    go("m3 f3 m0 f0 m2 f2 m1 f1")
    d_k[...] = jnp.zeros_like(d_k)
    d_v[...] = jnp.zeros_like(d_v)
    landed(d_out.at[pl.ds(0, 15)], msem.at[1])
    count = (pads + 16) * 2 * rows

    def block(i, _):
        band = pl.ds(pl.multiple_of((2 * i + c) * rows, rows), rows + reach)
        kf, vf = kv.at[0].reshape(count, 128), kv.at[1].reshape(count, 128)
        q, k, dd = q_rot[i], kf[band, :], d_out[i]
        scores, allowed = band_scores(q, k, q_seg[i], k_seg[:, band], scale, reach)
        probs = jnp.where(allowed, jnp.exp(scores - lse[i]), 0.0)
        d_probs = dot(dd, vf[band, :], ((1,), (1,)))
        delta = jnp.sum(dd.astype(F32) * o_ref[i].astype(F32), axis=1, keepdims=True)
        d_scores = (probs * (d_probs - delta)).astype(BF)
        d_q[i] = (dot(d_scores, k, ((1,), (0,))) * scale).astype(BF)
        d_k[band, :] += dot(d_scores, q, ((0,), (0,))) * scale
        d_v[band, :] += dot(probs.astype(BF), dd, ((0,), (0,)))
        return 0

    def store(sl, v):
        output[sl, :] = residual[sl, :] + v

    go("d3 d0 d2 d1")
    done = 0
    for upto, words in ((3, "M3 M0"), (6, "b31 b02 M2 M1"), (9, "b21 b12 h30 h03"), (12, "b32 b01"), (14, "h31 h02"), (16, "h20 h13")):
        lax.fori_loop(done, upto, block, 0)
        go(words)
        done = upto

    def pack(i, _):
        at = pl.ds(pl.multiple_of(((pads + i) * 2 + 1 - c) * rows, rows), rows)
        other[0, i] = d_k[at, :].astype(BF)
        other[1, i] = d_v[at, :].astype(BF)
        return 0

    lax.fori_loop(0, 16, pack, 0)
    remote(other, got, msem.at[2], msem.at[3], partner).start()
    go("h32 h01")
    landed(got, msem.at[3])
    d_gains[...] = jnp.zeros_like(d_gains)

    def undo(i, _):
        at = pl.ds(pl.multiple_of(((pads + i) * 2 + c) * rows, rows), rows)
        cs, sn = cosine[i], sine[i]
        both = lin[i]
        rq = lax.rsqrt(column(tot[pl.ds(i, 1), :]) / width + EPS)
        rk = lax.rsqrt(column(tot[pl.ds(16 + i, 1), :]) / width + EPS)
        dk = (d_k[at, :] + wide(got[0, i])).astype(BF).astype(F32)
        d_lin[i, :, 256:] = (d_v[at, :] + wide(got[1, i])).astype(BF)
        uq = turned_back(wide(d_q[i]), cs, sn)
        uk = turned_back(dk, cs, sn)
        q, k = both[:, :128], both[:, 128:256]
        d_gains[0:1, :] += jnp.sum(uq * q * rq, axis=0, keepdims=True)
        d_gains[1:2, :] += jnp.sum(uk * k * rk, axis=0, keepdims=True)
        uq, uk = uq * gq[...], uk * gk[...]
        d_un[0, i] = uq
        d_un[1, i] = uk
        sums[pl.ds(i, 1), :] = row_sums(uq * q)
        sums[pl.ds(16 + i, 1), :] = row_sums(uk * k)
        return 0

    lax.fori_loop(0, 16, undo, 0)
    go("h10 h23 Q")
    share_sums(net, sums, sums_all, inner, lsem.at[1], msem.at[4], msem.at[5])

    def finish(i, _):
        both = lin[i]
        for s in (0, 1):
            r = lax.rsqrt(column(tot[pl.ds(16 * s + i, 1), :]) / width + EPS)
            mean = column(inner[pl.ds(16 * s + i, 1), :]) / width
            own = both[:, 128 * s : 128 * (s + 1)]
            d_lin[i, :, 128 * s : 128 * (s + 1)] = (r * d_un[s, i] - own * (r * r * r * mean)).astype(BF)
        return 0

    lax.fori_loop(0, 16, finish, 0)
    go("h21 h12 q")
    sc.last(store)
    landed(d_out.at[pl.ds(0, 15)], msem.at[0])
    landed(other, msem.at[2])
    net.finish()


def run_attend_back(scale, pads, d_res, wo, p_out, residual, q_rot, kv, q_seg, k_seg, lse, o, lin, tot, cosine, sine, gq, gk, cid, cut=96):
    R, D = d_res.shape
    DMA = pltpu.SemaphoreType.DMA
    S = jax.ShapeDtypeStruct
    A = pl.BlockSpec(memory_space=pl.ANY)
    M = pl.BlockSpec(memory_space=pltpu.VMEM)
    V = pltpu.VMEM
    span = (pads + 16) * 2 * R
    return pl.pallas_call(
        functools.partial(attend_back_kernel, scale, pads, cut),
        out_shape=(S((16, R, 384), BF), S((8, 128), F32), S((R, D), F32)),
        in_specs=[M, A, A] + [M] * 13,
        out_specs=(M, M, M),
        scratch_shapes=[V((4, 4, R, D), BF), V(wo.shape, BF), V((16, R, 128), BF), V((16, R, 128), BF), V((16, R, 128), BF),
                        V((span, 128), F32), V((span, 128), F32), V((2, 16, R, 128), BF), V((2, 16, R, 128), BF),
                        V((2, 16, R, 128), F32), V((32, 128), F32), V((16, 32, 128), F32), V((32, 128), F32),
                        DMA((2,)), DMA((10,)), DMA((64,))] + rs_scratch(cut, R, D),
        compiler_params=pltpu.CompilerParams(collective_id=cid, has_side_effects=True, vmem_limit_bytes=62 * 2**20),
        name="attend_back",
    )(d_res, wo, p_out, residual, q_rot, kv, q_seg, k_seg, lse, o, lin, tot, cosine, sine, gq, gk)
def core_pair(value):
    return lax.ppermute(value, "core", [(0, 1), (1, 0)])


def dot(a, b, dims):
    return lax.dot_general(a, b, (dims, ((), ())), preferred_element_type=jnp.float32)


def local_chip(
    inputs, cotangent, segments, expert_ids, gate_weights, fill_order, norm1_gain, w_query, w_key,
    w_value, w_output, query_gain, key_gain, norm2_gain, expert_gate, expert_up, expert_down,
):
    chips = 16
    devices = 2 * chips
    rows, width = inputs.shape
    u, z, core = place()
    chip = u * 4 + z
    device = chip * 2 + core
    topk = expert_ids.shape[1]
    experts_n = chips
    capacity = 9 * rows * devices * topk // (8 * experts_n)
    one_hot = expert_ids[:, :, None] == jnp.arange(experts_n, dtype=jnp.int32)[None, None, :]
    chosen = jnp.any(one_hot, axis=1)
    weight = jnp.sum(jnp.where(one_hot, gate_weights[:, :, None], 0.0), axis=1)
    earlier = (fill_order[None, :] < fill_order[:, None]).astype(jnp.bfloat16)
    rank = dot(earlier, chosen.astype(jnp.bfloat16), ((1,), (0,)))
    rank = jnp.where(chosen, rank, -1.0)
    gains = jnp.stack([norm1_gain, query_gain, key_gain, norm2_gain]).astype(F32)
    blank = jnp.zeros_like(gains)
    gains = jnp.where(core == 0, jnp.concatenate([gains, blank], axis=1), jnp.concatenate([blank, gains], axis=1))
    gains = jnp.broadcast_to(gains[None], (chips, 4, 128))
    block = jnp.concatenate(
        [weight.T[:, None, :], rank.T[:, None, :], gains, jnp.zeros((chips, 2, 128), F32)], axis=1)
    side = width // 2
    n1_rows, lin, w_qkv, squares, swapped, cot_a = run_qkv(
        inputs, w_query, w_key, w_value, block, cotangent[:, :side], 2)
    gains = jnp.sum(swapped.reshape(chips, 2, 8, 128), axis=1)
    gain_one, gain_two = gains[:, 2].reshape(1, width), gains[:, 5].reshape(1, width)
    gq, gk = (lax.dynamic_slice_in_dim(gains[:, i], chip, 1, 0) for i in (3, 4))
    rank_all = swapped[:, 1, :]
    taken = rank_all >= 0.0
    counts = jnp.sum(taken.astype(F32), axis=1)
    before = jnp.cumsum(counts) - counts
    kept = taken & (before[:, None] + rank_all < float(capacity))
    share = jnp.where(kept, swapped[:, 0, :], 0.0).reshape(chips, 2, rows)
    share = lax.dynamic_index_in_dim(share, core, 1, keepdims=False).reshape(chips * rows, 1)


    positions = (jnp.arange(chips, dtype=jnp.int32)[:, None] * 2 + core) * rows + jnp.arange(rows, dtype=jnp.int32)
    half_dim = HEAD_DIM // 2
    inv_freq = jnp.exp(jnp.arange(half_dim, dtype=F32) * (-2.0 * math.log(ROPE_BASE) / HEAD_DIM))
    angles = positions.reshape(-1).astype(F32)[:, None] * inv_freq[None, :]
    cosine, sine = jnp.cos(angles), jnp.sin(angles)
    cosine = jnp.concatenate([cosine, cosine], axis=1).reshape(chips, rows, HEAD_DIM)
    sine = jnp.concatenate([-sine, sine], axis=1).reshape(chips, rows, HEAD_DIM)
    pads = chips // 4
    k_seg = jnp.concatenate([jnp.full((pads * 2 * rows,), -1, jnp.int32), segments]).reshape(1, -1)
    q_seg = lax.dynamic_index_in_dim(segments.reshape(chips, 2, rows, 1), core, 1, keepdims=False)
    scale = 1.0 / math.sqrt(HEAD_DIM)
    tokens = chips * rows
    w_o, q_rot, kv, head_out, log_total, attended, residual, normed_two, cot_b = run_attend(
        scale, pads, lin, squares, cosine, sine, gq, gk, q_seg, k_seg, w_output, inputs, gain_two, cotangent[:, side:], 4)
    r2 = lax.rsqrt(jnp.mean(residual * residual, axis=1, keepdims=True) + EPS)

    d_normed_two, mixed, _n2, _other, d_expert_gate, d_expert_up, d_expert_down = run_expert(
        normed_two, cot_a, cot_b, share.reshape(4, 4, rows, 1), expert_gate, expert_up, expert_down, 6)
    def norm_back(d_out, values, r, gain):
        d_scaled = d_out * gain
        inner = jnp.mean(d_scaled * values, axis=1, keepdims=True)
        d_gain = jnp.sum(d_out * values * r, axis=0)
        return r * d_scaled - values * (r * r * r * inner), d_gain

    d_resid_norm, d_gain_two = norm_back(d_normed_two, residual, r2, gain_two)
    d_residual = cotangent.astype(F32) + d_resid_norm
    d_res_low = d_residual.astype(BF)
    d_lin, d_qk_gains, output = run_attend_back(
        scale, pads, d_res_low, w_o, mixed, residual, q_rot, kv, q_seg, k_seg, log_total, head_out, lin, squares, cosine, sine, gq, gk, 7)
    d_qk_gains = d_qk_gains[:2] + core_pair(d_qk_gains[:2])
    d_w_output, d_inputs, d_w_query, d_w_key, d_w_value, d_gains = run_finish(
        d_lin, w_qkv, n1_rows, attended, inputs, d_residual, gain_one, d_gain_two.reshape(1, width), 8)

    def my_half(row):
        return lax.dynamic_slice_in_dim(row, core * 64, 64, 0)

    return (
        output,
        d_inputs,
        my_half(d_gains[0]),
        d_w_query,
        d_w_key,
        d_w_value,
        d_w_output,
        my_half(d_qk_gains[0]),
        my_half(d_qk_gains[1]),
        my_half(d_gains[1]),
        d_expert_gate,
        d_expert_up,
        d_expert_down,
    )
def whole(mesh, step, rows):
    return jax.shard_map(
        step,
        mesh=mesh,
        in_specs=(
            P(rows, None),
            P(rows, None),
            P(),
            P(rows, None),
            P(rows, None),
            P(rows),
            P(rows),
            P(rows, None),
            P(rows, None),
            P(rows, None),
            P(rows, None),
            P(rows),
            P(rows),
            P(rows),
            P(rows, None),
            P(rows, None),
            P(rows, None),
        ),
        out_specs=(
            P(rows, None),
            P(rows, None),
            P(rows),
            P(rows, None),
            P(rows, None),
            P(rows, None),
            P(rows, None),
            P(rows),
            P(rows),
            P(rows),
            P(rows, None),
            P(rows, None),
            P(rows, None),
        ),
        check_vma=False,
    )


def solution(mesh):
    groups, blk_size = mesh.shape["ulysses"], mesh.shape["blk"]

    def step(*args):
        if groups != 4 or blk_size != 8 or args[7].shape[1] // HEAD_DIM != groups * blk_size // 2:
            return whole(mesh, local, ("ulysses", "blk"))(*args)
        chips = Mesh(mesh.devices.reshape(groups, blk_size // 2, 2), ("ulysses", "z", "core"))
        return whole(chips, local_chip, ("ulysses", "z", "core"))(*args)

    return step
```

```python
import functools
import math

import jax
import jax.numpy as jnp
from jax import lax
from jax.experimental import pallas as pl
from jax.experimental.pallas import tpu as pltpu
from jax.sharding import Mesh
from jax.sharding import PartitionSpec as P

HEAD_DIM = 128


EPS = 1e-05
ROPE_BASE = 10000.0
NEG = -1e30


def as_sent(value):

    def short(part):
        return part.astype(jnp.bfloat16) if part.dtype == jnp.float32 else part

    return jax.tree.map(short, value)


def passed_along(block, axis, distance):
    devices = range(lax.axis_size(axis))
    route = [((i - distance) % len(devices), i) for i in devices]
    return lax.ppermute(block, axis, route)


def prefix(value, axis, join, neutral):
    count, mine = (lax.axis_size(axis), lax.axis_index(axis))
    pieces = lax.all_gather(value, axis)
    subtotal = jnp.full_like(value, 0) + jnp.asarray(neutral, value.dtype)

    def hop(position, subtotal):
        longer = join(subtotal, pieces[position])
        return jnp.where(position < mine, longer, subtotal)

    return lax.fori_loop(0, count - 1, hop, subtotal)


def partner_2(block, axis, bit):
    count = lax.axis_size(axis)
    route = []
    for low in range(count):
        high = low | 1 << bit
        if high != low and high < count:
            route += [(low, high), (high, low)]
    return lax.ppermute(block, axis, route)


def norm_rows(values, gain_vec):
    return values * lax.rsqrt(jnp.mean(values * values, axis=-1, keepdims=True) + EPS) * gain_vec


def rotate(values, positions):
    half_dim = HEAD_DIM // 2
    heads_here = values.shape[1] // HEAD_DIM
    inv_freq = jnp.exp(
        jnp.arange(half_dim, dtype=jnp.float32) * (-2.0 * math.log(ROPE_BASE) / HEAD_DIM)
    )
    angles = positions.astype(jnp.float32)[:, None] * inv_freq[None, :]
    cosine = jnp.cos(angles)[:, None, :]
    sin_t = jnp.sin(angles)[:, None, :]
    shaped = values.reshape(values.shape[0], heads_here, HEAD_DIM)
    lower_half = shaped[..., :half_dim]
    upper_half = shaped[..., half_dim:]
    turned = jnp.concatenate(
        [lower_half * cosine - upper_half * sin_t, upper_half * cosine + lower_half * sin_t],
        axis=-1,
    )
    return turned.reshape(values.shape)


def attn_inputs(q_lin, k_lin, gain_q, gain_k, positions):
    return (
        rotate(norm_rows(q_lin, gain_q), positions),
        rotate(norm_rows(k_lin, gain_k), positions),
    )


def banded(shaped, fill_value):
    earlier = jnp.concatenate([jnp.full_like(shaped[:1], fill_value), shaped[:-1]], axis=0)
    return jnp.concatenate([earlier, shaped], axis=1)


def unbanded(band, local_rows):
    earlier = band[:, :local_rows]
    own_part = band[:, local_rows:]
    moved_up = jnp.concatenate([earlier[1:], jnp.zeros_like(earlier[:1])], axis=0)
    return own_part + moved_up


def add_counts(earlier, later):
    return earlier + later


def expert_move(buffer):
    return lax.all_to_all(buffer, ("ulysses", "blk"), split_axis=0, concat_axis=0, tiled=True)


def to_head_layout(values):
    return jax.tree.map(
        lambda part, own: part.astype(own.dtype),
        lax.all_to_all(as_sent(values), "ulysses", split_axis=1, concat_axis=0, tiled=True),
        values,
    )


def to_token_layout(values):
    return jax.tree.map(
        lambda part, own: part.astype(own.dtype),
        lax.all_to_all(as_sent(values), "ulysses", split_axis=0, concat_axis=1, tiled=True),
        values,
    )


def local(
    inputs,
    cotangent,
    segments,
    expert_ids,
    gate_weights,
    fill_order,
    norm1_gain,
    w_query,
    w_key,
    w_value,
    w_output,
    query_gain,
    key_gain,
    norm2_gain,
    expert_gate,
    expert_up,
    expert_down,
):
    blk_size = lax.axis_size("blk")
    groups = lax.axis_size("ulysses")
    devices = blk_size * groups
    local_rows = inputs.shape[0]
    model_width = inputs.shape[1]
    blk_index = lax.axis_index("blk")
    group_index = lax.axis_index("ulysses")
    device_index = group_index * blk_size + blk_index
    positions = device_index * local_rows + jnp.arange(local_rows, dtype=jnp.int32)
    heads_dev = model_width // groups // HEAD_DIM
    score_scale = 1.0 / math.sqrt(HEAD_DIM)
    layer_in = inputs.astype(jnp.float32)
    dense = (w_query, w_key, w_value, w_output, norm1_gain, query_gain, key_gain, norm2_gain)
    gathered = (
        lax.all_gather(dense[0], ("ulysses", "blk"), axis=0, tiled=True),
        lax.all_gather(dense[1], ("ulysses", "blk"), axis=0, tiled=True),
        lax.all_gather(dense[2], ("ulysses", "blk"), axis=0, tiled=True),
        lax.all_gather(dense[3], ("ulysses", "blk"), axis=0, tiled=True),
        lax.all_gather(dense[4], ("ulysses", "blk"), axis=0, tiled=True),
        lax.all_gather(dense[5], ("ulysses", "blk"), axis=0, tiled=True),
        lax.all_gather(dense[6], ("ulysses", "blk"), axis=0, tiled=True),
        lax.all_gather(dense[7], ("ulysses", "blk"), axis=0, tiled=True),
    )
    w_q, w_k, w_v, w_o = (gathered[0], gathered[1], gathered[2], gathered[3])
    gain_one = gathered[4].astype(jnp.float32)
    gain_q = gathered[5].astype(jnp.float32)
    gain_k = gathered[6].astype(jnp.float32)
    gain_two = gathered[7].astype(jnp.float32)
    normed_one = norm_rows(layer_in, gain_one).astype(jnp.bfloat16)
    q_lin = jnp.dot(normed_one, w_q, preferred_element_type=jnp.float32)
    k_lin = jnp.dot(normed_one, w_k, preferred_element_type=jnp.float32)
    v_lin = jnp.dot(normed_one, w_v, preferred_element_type=jnp.float32)
    (q_rot, k_rot), pre_back = jax.vjp(
        lambda q_in, k_in, gq_in, gk_in: attn_inputs(q_in, k_in, gq_in, gk_in, positions),
        q_lin,
        k_lin,
        gain_q,
        gain_k,
    )
    q_heads, k_heads, v_heads = to_head_layout(
        (q_rot.astype(jnp.bfloat16), k_rot.astype(jnp.bfloat16), v_lin.astype(jnp.bfloat16))
    )
    group_ids = jnp.arange(groups, dtype=jnp.int32)[:, None]
    row_ids = jnp.arange(local_rows, dtype=jnp.int32)[None, :]
    q_pos = (group_ids * blk_size + blk_index) * local_rows + row_ids
    q_seg = segments[q_pos]
    four_shape = (groups, local_rows, heads_dev, HEAD_DIM)
    q_four = q_heads.reshape(four_shape)

    def score_block(k_now, source):
        k_pos = (group_ids * blk_size + source) * local_rows + row_ids
        k_seg = banded(segments[k_pos], -1)
        k_pos = banded(k_pos, 0)
        k_band = banded(k_now.reshape(four_shape), 0)
        raw_scores = (
            jnp.einsum("gqhd,gkhd->gqhk", q_four, k_band, preferred_element_type=jnp.float32)
            * score_scale
        )
        allowed = (k_seg[:, None, :] == q_seg[:, :, None]) & (
            k_pos[:, None, :] <= q_pos[:, :, None]
        )
        return (raw_scores, allowed[:, :, None, :], k_band)

    def forward_step(flash_state, kv_stack, step_id):
        run_max, run_sum, run_out = flash_state
        source = jnp.mod(blk_index - step_id, blk_size)
        raw_scores, allowed, k_band = score_block(kv_stack[0], source)
        raw_scores = jnp.where(allowed, raw_scores, NEG)
        new_max = jnp.maximum(run_max, jnp.max(raw_scores, axis=-1))
        shrink = jnp.exp(run_max - new_max)
        weights = jnp.where(allowed, jnp.exp(raw_scores - new_max[..., None]), 0.0)
        run_sum = run_sum * shrink + jnp.sum(weights, axis=-1)
        v_band = banded(kv_stack[1].reshape(four_shape), 0)
        run_out = run_out * shrink[..., None] + jnp.einsum(
            "gqhk,gkhd->gqhd",
            weights.astype(jnp.bfloat16),
            v_band,
            preferred_element_type=jnp.float32,
        )
        return (new_max, run_sum, run_out)

    start_state = (
        jnp.full((groups, local_rows, heads_dev), NEG, jnp.float32),
        jnp.zeros((groups, local_rows, heads_dev), jnp.float32),
        jnp.zeros(four_shape, jnp.float32),
    )
    kv_home = jnp.stack([k_heads, v_heads])
    first_state = forward_step(start_state, kv_home, 0)

    def forward_turn(step_id, loop_state):
        flash_state, kv_stack = loop_state
        moved = passed_along(kv_stack, "blk", 1)
        return (forward_step(flash_state, moved, step_id), moved)

    final_state, unused_kv = lax.fori_loop(1, blk_size, forward_turn, (first_state, kv_home))
    run_max, run_sum, run_out = final_state
    o_four = (run_out / run_sum[..., None]).astype(jnp.bfloat16)
    log_total = run_max + jnp.log(run_sum)
    o_heads = o_four.reshape(groups * local_rows, heads_dev * HEAD_DIM)
    attended = to_token_layout(o_heads)
    residual = layer_in + jnp.dot(attended, w_o, preferred_element_type=jnp.float32)
    normed_two_f, norm_two_back = jax.vjp(norm_rows, residual, gain_two)
    normed_two = normed_two_f.astype(jnp.bfloat16)
    experts_n = devices // 2
    topk = expert_ids.shape[1]
    per_source = 2 * local_rows * topk // experts_n
    half_slots = per_source // 2
    capacity = 9 * local_rows * devices * topk // (8 * experts_n)
    slots_all = experts_n * per_source
    tokens_local = jnp.arange(local_rows, dtype=jnp.int32)
    chosen = jnp.sum(
        (expert_ids[:, :, None] == jnp.arange(experts_n, dtype=jnp.int32)[None, None, :]).astype(
            jnp.int32
        ),
        axis=1,
    )
    by_fill = jnp.zeros((local_rows,), jnp.int32).at[fill_order].set(tokens_local)
    sorted_rows = chosen[by_fill]
    before = jnp.cumsum(sorted_rows, axis=0) - sorted_rows
    rank_all = before[fill_order]
    pair_rank = jnp.take_along_axis(rank_all, expert_ids, axis=1)
    counts = jnp.sum(chosen, axis=0)
    offsets = prefix(counts, ("ulysses", "blk"), add_counts, jnp.zeros_like(counts))
    kept_pair = offsets[expert_ids] + pair_rank < capacity
    pair_slot = expert_ids * per_source + pair_rank
    pair_index = tokens_local[:, None] * topk + jnp.arange(topk, dtype=jnp.int32)[None, :]
    slot_pair = (
        jnp.zeros((slots_all,), jnp.int32).at[pair_slot.reshape(-1)].set(pair_index.reshape(-1))
    )
    slot_live = (
        jnp.zeros((slots_all,), jnp.bool_).at[pair_slot.reshape(-1)].set(kept_pair.reshape(-1))
    )
    slot_token = slot_pair // topk
    send_rows = jnp.where(slot_live[:, None], normed_two[slot_token], jnp.zeros((), jnp.bfloat16))
    received = expert_move(send_rows.reshape(devices, half_slots, model_width)).reshape(
        devices * half_slots, model_width
    )
    parity = jnp.mod(blk_index, 2)
    partner = partner_2((expert_gate, expert_up, expert_down), "blk", 0)

    def joined(own_half, other_half):
        lower_part = jnp.where(parity == 0, own_half, other_half)
        upper_part = jnp.where(parity == 0, other_half, own_half)
        return jnp.concatenate([lower_part, upper_part], axis=0)

    gate_full = joined(expert_gate, partner[0])
    up_full = joined(expert_up, partner[1])
    down_full = joined(expert_down, partner[2])
    gate_pre = jnp.dot(received, gate_full, preferred_element_type=jnp.float32)
    up_pre = jnp.dot(received, up_full, preferred_element_type=jnp.float32)
    hidden = (jax.nn.silu(gate_pre) * up_pre).astype(jnp.bfloat16)
    produced = jnp.dot(hidden, down_full, preferred_element_type=jnp.float32).astype(jnp.bfloat16)
    returned = expert_move(produced.reshape(devices, half_slots, model_width)).reshape(
        slots_all, model_width
    )
    pair_share = jnp.where(kept_pair, gate_weights, 0.0)
    mixed = jnp.einsum("tk,tkd->td", pair_share, returned[pair_slot].astype(jnp.float32))
    output = residual + mixed
    grad_out = cotangent.astype(jnp.float32)
    slot_share = jnp.where(slot_live, gate_weights.reshape(-1)[slot_pair], 0.0)
    grad_send = (slot_share[:, None] * grad_out[slot_token]).astype(jnp.bfloat16)
    grad_rows = expert_move(grad_send.reshape(devices, half_slots, model_width)).reshape(
        devices * half_slots, model_width
    )
    d_down_full = jnp.einsum("rf,rd->fd", hidden, grad_rows, preferred_element_type=jnp.float32)
    d_hidden = jnp.einsum("rd,fd->rf", grad_rows, down_full, preferred_element_type=jnp.float32)
    sigma = jax.nn.sigmoid(gate_pre)
    d_gate_pre = (d_hidden * up_pre * sigma * (1.0 + gate_pre * (1.0 - sigma))).astype(jnp.bfloat16)
    d_up_pre = (d_hidden * gate_pre * sigma).astype(jnp.bfloat16)
    d_gate_full = jnp.einsum("rd,rf->df", received, d_gate_pre, preferred_element_type=jnp.float32)
    d_up_full = jnp.einsum("rd,rf->df", received, d_up_pre, preferred_element_type=jnp.float32)
    d_pair_rows = (
        jnp.einsum("rf,df->rd", d_gate_pre, gate_full, preferred_element_type=jnp.float32)
        + jnp.einsum("rf,df->rd", d_up_pre, up_full, preferred_element_type=jnp.float32)
    ).astype(jnp.bfloat16)
    back_rows = expert_move(d_pair_rows.reshape(devices, half_slots, model_width)).reshape(
        slots_all, model_width
    )
    d_normed_two = jnp.sum(
        jnp.where(kept_pair[:, :, None], back_rows[pair_slot].astype(jnp.float32), 0.0), axis=1
    )
    half_rows = expert_gate.shape[0]
    half_hidden = expert_down.shape[0]

    def halves(full_grad, size):
        own_half = lax.dynamic_slice_in_dim(full_grad, parity * size, size, 0)
        other_half = lax.dynamic_slice_in_dim(full_grad, (1 - parity) * size, size, 0)
        return (own_half, other_half)

    gate_own, gate_other = halves(d_gate_full, half_rows)
    up_own, up_other = halves(d_up_full, half_rows)
    down_own, down_other = halves(d_down_full, half_hidden)
    partner_grads = (
        partner_2(gate_other.astype(jnp.bfloat16), "blk", 0).astype(gate_other.dtype),
        partner_2(up_other.astype(jnp.bfloat16), "blk", 0).astype(up_other.dtype),
        partner_2(down_other.astype(jnp.bfloat16), "blk", 0).astype(down_other.dtype),
    )
    d_expert_gate = gate_own + partner_grads[0]
    d_expert_up = up_own + partner_grads[1]
    d_expert_down = down_own + partner_grads[2]
    d_resid_norm, d_gain_two = norm_two_back(d_normed_two)
    d_residual = grad_out + d_resid_norm
    d_res_low = d_residual.astype(jnp.bfloat16)
    d_attended = jnp.einsum("te,de->td", d_res_low, w_o, preferred_element_type=jnp.float32).astype(
        jnp.bfloat16
    )
    d_o_heads = to_head_layout(d_attended)
    d_o_four = d_o_heads.reshape(four_shape)
    row_delta = jnp.sum(d_o_four.astype(jnp.float32) * o_four.astype(jnp.float32), axis=-1)

    def back_turn(step_id, loop_state):
        moving, dq_acc = loop_state
        source = jnp.mod(blk_index - step_id, blk_size)
        k_now = moving[0].astype(jnp.bfloat16)
        v_now = moving[1].astype(jnp.bfloat16)
        raw_scores, allowed, k_band = score_block(k_now, source)
        prob_rows = jnp.where(allowed, jnp.exp(raw_scores - log_total[..., None]), 0.0)
        v_band = banded(v_now.reshape(four_shape), 0)
        d_probs = jnp.einsum(
            "gqhd,gkhd->gqhk", d_o_four, v_band, preferred_element_type=jnp.float32
        )
        d_scores = (prob_rows * (d_probs - row_delta[..., None])).astype(jnp.bfloat16)
        dv_band = jnp.einsum(
            "gqhk,gqhd->gkhd",
            prob_rows.astype(jnp.bfloat16),
            d_o_four,
            preferred_element_type=jnp.float32,
        )
        dk_band = (
            jnp.einsum("gqhk,gqhd->gkhd", d_scores, q_four, preferred_element_type=jnp.float32)
            * score_scale
        )
        dq_acc = (
            dq_acc
            + jnp.einsum("gqhk,gkhd->gqhd", d_scores, k_band, preferred_element_type=jnp.float32)
            * score_scale
        )
        flat_shape = moving[2].shape
        dk_new = moving[2] + unbanded(dk_band, local_rows).reshape(flat_shape)
        dv_new = moving[3] + unbanded(dv_band, local_rows).reshape(flat_shape)
        moving = passed_along(
            jnp.stack([moving[0], moving[1], dk_new, dv_new]).astype(jnp.bfloat16), "blk", 1
        ).astype(jnp.float32)
        return (moving, dq_acc)

    zero_rows = jnp.zeros(k_heads.shape, jnp.float32)
    start_moving = jnp.stack(
        [k_heads.astype(jnp.float32), v_heads.astype(jnp.float32), zero_rows, zero_rows]
    )
    moving, dq_acc = lax.fori_loop(
        0, blk_size, back_turn, (start_moving, jnp.zeros(four_shape, jnp.float32))
    )
    d_q_send = dq_acc.astype(jnp.bfloat16).reshape(k_heads.shape)
    d_k_send = moving[2].astype(jnp.bfloat16)
    d_v_send = moving[3].astype(jnp.bfloat16)
    d_q_rot, d_k_rot, d_v_lin = to_token_layout((d_q_send, d_k_send, d_v_send))
    d_q_lin, d_k_lin, d_gain_q, d_gain_k = pre_back(
        (d_q_rot.astype(jnp.float32), d_k_rot.astype(jnp.float32))
    )
    d_q_low = d_q_lin.astype(jnp.bfloat16)
    d_k_low = d_k_lin.astype(jnp.bfloat16)
    d_normed_one = jnp.einsum("te,de->td", d_q_low, w_q, preferred_element_type=jnp.float32)
    d_normed_one = d_normed_one + jnp.einsum(
        "te,de->td", d_k_low, w_k, preferred_element_type=jnp.float32
    )
    d_normed_one = d_normed_one + jnp.einsum(
        "te,de->td", d_v_lin, w_v, preferred_element_type=jnp.float32
    )
    unused_norm, norm_one_back = jax.vjp(norm_rows, layer_in, gain_one)
    d_layer_in, d_gain_one = norm_one_back(d_normed_one)
    d_inputs = d_residual + d_layer_in
    d_qk_heads = to_head_layout((d_q_low, d_k_low))
    rows_all = (
        lax.all_gather(normed_one, "ulysses", axis=0, tiled=True),
        lax.all_gather(d_res_low, "ulysses", axis=0, tiled=True),
    )
    head_cols = model_width // groups
    piece_rows = model_width // devices

    def by_owner(part):
        rest = part.shape[1:]
        shaped = part.reshape((groups, blk_size, piece_rows) + rest)
        return jnp.swapaxes(shaped, 0, 1).reshape((model_width,) + rest)

    part_q = jnp.einsum("td,te->de", rows_all[0], d_qk_heads[0], preferred_element_type=jnp.float32)
    part_k = jnp.einsum("td,te->de", rows_all[0], d_qk_heads[1], preferred_element_type=jnp.float32)
    part_v = jnp.einsum("td,te->de", rows_all[0], d_v_send, preferred_element_type=jnp.float32)
    part_o = jnp.einsum("te,td->ed", o_heads, rows_all[1], preferred_element_type=jnp.float32)
    blk_sums = (
        lax.psum_scatter(
            by_owner(part_q).astype(jnp.bfloat16), "blk", scatter_dimension=0, tiled=True
        ).astype(jnp.float32),
        lax.psum_scatter(
            by_owner(part_k).astype(jnp.bfloat16), "blk", scatter_dimension=0, tiled=True
        ).astype(jnp.float32),
        lax.psum_scatter(
            by_owner(part_v).astype(jnp.bfloat16), "blk", scatter_dimension=0, tiled=True
        ).astype(jnp.float32),
        lax.psum_scatter(
            part_o.astype(jnp.bfloat16), "blk", scatter_dimension=0, tiled=True
        ).astype(jnp.float32),
        lax.psum_scatter(
            by_owner(d_gain_one).astype(jnp.bfloat16), "blk", scatter_dimension=0, tiled=True
        ).astype(jnp.float32),
        lax.psum_scatter(
            by_owner(d_gain_q).astype(jnp.bfloat16), "blk", scatter_dimension=0, tiled=True
        ).astype(jnp.float32),
        lax.psum_scatter(
            by_owner(d_gain_k).astype(jnp.bfloat16), "blk", scatter_dimension=0, tiled=True
        ).astype(jnp.float32),
        lax.psum_scatter(
            by_owner(d_gain_two).astype(jnp.bfloat16), "blk", scatter_dimension=0, tiled=True
        ).astype(jnp.float32),
    )

    def widened(part):
        return lax.dynamic_update_slice_in_dim(
            jnp.zeros((part.shape[0], model_width), jnp.float32), part, group_index * head_cols, 1
        )

    col_sums = (
        lax.psum_scatter(
            widened(blk_sums[0]).astype(jnp.bfloat16), "ulysses", scatter_dimension=0, tiled=True
        ).astype(jnp.float32),
        lax.psum_scatter(
            widened(blk_sums[1]).astype(jnp.bfloat16), "ulysses", scatter_dimension=0, tiled=True
        ).astype(jnp.float32),
        lax.psum_scatter(
            widened(blk_sums[2]).astype(jnp.bfloat16), "ulysses", scatter_dimension=0, tiled=True
        ).astype(jnp.float32),
        lax.psum_scatter(
            blk_sums[4].astype(jnp.bfloat16), "ulysses", scatter_dimension=0, tiled=True
        ).astype(jnp.float32),
        lax.psum_scatter(
            blk_sums[5].astype(jnp.bfloat16), "ulysses", scatter_dimension=0, tiled=True
        ).astype(jnp.float32),
        lax.psum_scatter(
            blk_sums[6].astype(jnp.bfloat16), "ulysses", scatter_dimension=0, tiled=True
        ).astype(jnp.float32),
        lax.psum_scatter(
            blk_sums[7].astype(jnp.bfloat16), "ulysses", scatter_dimension=0, tiled=True
        ).astype(jnp.float32),
    )
    result_grads = (
        col_sums[0],
        col_sums[1],
        col_sums[2],
        blk_sums[3],
        col_sums[3],
        col_sums[4],
        col_sums[5],
        col_sums[6],
    )
    return (
        output,
        d_inputs,
        result_grads[4],
        result_grads[0],
        result_grads[1],
        result_grads[2],
        result_grads[3],
        result_grads[5],
        result_grads[6],
        result_grads[7],
        d_expert_gate,
        d_expert_up,
        d_expert_down,
    )


MESH = pl.DeviceIdType.MESH
P1 = 96

def place():
    u = lax.axis_index("ulysses"); z = lax.axis_index("z"); c = lax.axis_index("core")
    return u, z, c

def ag_kernel(cut, x_ref, o_ref, local_sem, s_sem, zr, xr, yr, d1r, d2r, bs, br, bzr):
    u, z, c = place()
    Z = 4
    R = x_ref.shape[0]
    ux, uy = u ^ 1, u ^ 2
    xn, yn, up, dn = (ux, z, c), (uy, z, c), (u, z + 1, c), (u, z - 1, c)
    has_up, has_dn = z < Z - 1, z > 0
    bar = pltpu.get_barrier_semaphore()
    for n in (xn, yn):
        pl.semaphore_signal(bar, inc=1, device_id=n, device_id_type=MESH)
    @pl.when(has_up)
    def _():
        pl.semaphore_signal(bar, inc=1, device_id=up, device_id_type=MESH)
    @pl.when(has_dn)
    def _():
        pl.semaphore_signal(bar, inc=1, device_id=dn, device_id_type=MESH)
    pl.semaphore_wait(bar, 2 + has_up.astype(jnp.int32) + has_dn.astype(jnp.int32))
    sends = []
    def copy(src, dst, ss, rs, dev):
        return pltpu.make_async_remote_copy(src_ref=src, dst_ref=dst, send_sem=ss, recv_sem=rs, device_id=dev, device_id_type=MESH)
    def go(cond, make):
        idx = len(sends)
        def mk():
            return make(s_sem.at[idx])
        sends.append((cond, mk))
        if cond is None:
            mk().start()
        else:
            pl.when(cond)(lambda: mk().start())
    def both(a, b):
        if a is None: return b
        if b is None: return a
        return jnp.logical_and(a, b)
    def wait(cond, ref, sem):
        def w():
            pltpu.make_async_copy(ref, ref, sem).wait()
        if cond is None: w()
        else: pl.when(cond)(w)
    own = pltpu.make_async_copy(x_ref, o_ref.at[u, z], local_sem)
    own.start()
    A = slice(0, cut)
    h = cut // 2
    def oa(uu, zz, lo=0, n=cut):
        return o_ref.at[uu, zz, pl.ds(lo, n), :]
    def spread(s, zz, cond):
        src = (lambda: x_ref.at[pl.ds(0, cut), :]) if s == 0 else (lambda: oa(u, zz))
        go(cond, lambda sm: copy(src(), oa(u, zz), sm, xr.at[zz], xn))
        go(cond, lambda sm: copy(src(), oa(u, zz), sm, yr.at[zz], yn))
    def cross(zz, cond):
        wait(cond, oa(ux, zz), xr.at[zz])
        go(cond, lambda sm: copy(oa(ux, zz, 0, h), oa(ux, zz, 0, h), sm, d1r.at[zz], yn))
        wait(cond, oa(uy, zz), yr.at[zz])
        go(cond, lambda sm: copy(oa(uy, zz, h, h), oa(uy, zz, h, h), sm, d2r.at[zz], xn))
    rb = R - cut
    hb = rb // 2
    def ob(uu, zz, lo=0, n=None):
        return o_ref.at[uu, zz, pl.ds(cut + lo, rb if n is None else n), :]
    go(has_up, lambda sm: copy(x_ref.at[pl.ds(0, cut), :], oa(u, z), sm, zr.at[z], up))
    go(has_dn, lambda sm: copy(x_ref.at[pl.ds(0, cut), :], oa(u, z), sm, zr.at[z], dn))
    if rb:
        go(None, lambda sm: copy(x_ref.at[pl.ds(cut, rb), :], ob(u, z), sm, br.at[0], xn))
        go(None, lambda sm: copy(x_ref.at[pl.ds(cut, rb), :], ob(u, z), sm, br.at[1], yn))
    spread(0, z, None)
    if rb:
        wait(None, ob(ux, z), br.at[0])
        go(None, lambda sm: copy(ob(ux, z, 0, hb), ob(ux, z, 0, hb), sm, br.at[2], yn))
        wait(None, ob(uy, z), br.at[1])
        go(None, lambda sm: copy(ob(uy, z, hb, hb), ob(uy, z, hb, hb), sm, br.at[3], xn))
    own.wait()
    def quad(zz):
        return o_ref.at[:, zz, pl.ds(cut, rb), :]
    def zs(s):
        zl, zh = z - s, z + s
        cl, ch = zl >= 0, zh < Z
        zlc, zhc = jnp.maximum(zl, 0), jnp.minimum(zh, Z - 1)
        return (zlc, cl, has_up, up), (zhc, ch, has_dn, dn)
    prev = [(z, None)]
    for s in range(1, Z):
        cur = []
        for (zz, cond, fwd, dev) in zs(s):
            wait(cond, oa(u, zz), zr.at[zz])
            go(both(cond, fwd), lambda sm, zz=zz, dev=dev: copy(oa(u, zz), oa(u, zz), sm, zr.at[zz], dev))
            spread(s, zz, cond)
            cur.append((zz, cond))
        if rb and s == 1:
            wait(None, ob(u ^ 3, z, 0, hb), br.at[2])
            wait(None, ob(u ^ 3, z, hb, hb), br.at[3])
            go(has_up, lambda sm: copy(quad(z), quad(z), sm, bzr.at[z], up))
            go(has_dn, lambda sm: copy(quad(z), quad(z), sm, bzr.at[z], dn))
        elif rb:
            for (zz, cond, fwd, dev) in zs(s - 1):
                wait(cond, quad(zz), bzr.at[zz])
                go(both(cond, fwd), lambda sm, zz=zz, dev=dev: copy(quad(zz), quad(zz), sm, bzr.at[zz], dev))
        for zz, cond in prev:
            cross(zz, cond)
        prev = cur
    if rb:
        for (zz, cond, fwd, dev) in zs(Z - 1):
            wait(cond, quad(zz), bzr.at[zz])
    for zz, cond in prev:
        cross(zz, cond)
    for zz in range(Z):
        wait(None, oa(u ^ 3, zz, 0, h), d1r.at[zz])
        wait(None, oa(u ^ 3, zz, h, h), d2r.at[zz])
    for cond, mk in sends:
        if cond is None: mk().wait_send()
        else: pl.when(cond)(lambda mk=mk: mk().wait_send())

def ag16(x, cid, cut=P1, space=pl.ANY):
    R, D = x.shape
    DMA = pltpu.SemaphoreType.DMA
    return pl.pallas_call(
        functools.partial(ag_kernel, cut),
        out_shape=jax.ShapeDtypeStruct((4, 4, R, D), x.dtype),
        in_specs=[pl.BlockSpec(memory_space=space)],
        out_specs=pl.BlockSpec(memory_space=space),
        scratch_shapes=[DMA, DMA((64,)), DMA((4,)), DMA((4,)), DMA((4,)), DMA((4,)), DMA((4,)), DMA((4,)), DMA((4,)), DMA((4,))],
        compiler_params=pltpu.CompilerParams(collective_id=cid, has_side_effects=True, vmem_limit_bytes=48 * 2**20),
        name="gather_rows",
    )(x)
F32 = jnp.float32
BF = jnp.bfloat16


class Net:
    def __init__(self, sems):
        self.sems, self.sends = sems, []
        self.u, self.z, self.c = place()
        u, z, c = self.u, self.z, self.c
        self.ux, self.uy, self.ud = u ^ 1, u ^ 2, u ^ 3
        self.xn, self.yn, self.up, self.dn = (u ^ 1, z, c), (u ^ 2, z, c), (u, z + 1, c), (u, z - 1, c)
        self.has_up, self.has_dn = z < 3, z > 0
        self.at = [z == i for i in range(4)]

    def barrier(self, more=()):
        bar = pltpu.get_barrier_semaphore()
        for n in (self.xn, self.yn) + tuple(more):
            pl.semaphore_signal(bar, inc=1, device_id=n, device_id_type=MESH)
        for cond, n in ((self.has_up, self.up), (self.has_dn, self.dn)):
            pl.when(cond)(lambda n=n: pl.semaphore_signal(bar, inc=1, device_id=n, device_id_type=MESH))
        pl.semaphore_wait(bar, 2 + len(more) + self.has_up.astype(jnp.int32) + self.has_dn.astype(jnp.int32))

    def go(self, cond, src, dst, rsem, dev):
        idx = len(self.sends)

        def mk():
            return pltpu.make_async_remote_copy(
                src_ref=src(), dst_ref=dst(), send_sem=self.sems.at[idx], recv_sem=rsem(),
                device_id=dev, device_id_type=MESH)

        self.sends.append((cond, mk))
        if cond is None:
            mk().start()
        else:
            pl.when(cond)(lambda: mk().start())

    def wait(self, cond, ref, sem):
        def w():
            pltpu.make_async_copy(ref(), ref(), sem).wait()

        if cond is None:
            w()
        else:
            pl.when(cond)(w)

    def finish(self):
        for cond, mk in self.sends:
            if cond is None:
                mk().wait_send()
            else:
                pl.when(cond)(lambda mk=mk: mk().wait_send())


def strips(rows, body, step=16):
    def it(i, _):
        body(pl.ds(pl.multiple_of(i * step, step), step))
        return 0

    lax.fori_loop(0, rows // step, it, 0)


def wide(v):
    return v.astype(F32)


class Scatter:
    def __init__(self, net, cut, P, bufs):
        self.net, self.cut, self.P = net, cut, P
        (self.mid1, self.mid2, self.fx, self.fy, self.be, self.ab, self.bbe, self.bab, self.bm,
         self.m1s, self.m2s, self.fxs, self.fys, self.bes, self.abs_, self.bbes, self.babs, self.bms) = bufs
        self.R = P.shape[2]
        self.h = cut // 2
        self.rb = self.R - cut
        self.hb = self.rb // 2

    def mid_send(self, zd):
        net, P, h = self.net, self.P, self.h
        net.go(None, lambda: P.at[net.ud, zd, pl.ds(0, h), :], lambda: self.mid1.at[zd], lambda: self.m1s.at[zd], net.xn)
        net.go(None, lambda: P.at[net.ud, zd, pl.ds(h, h), :], lambda: self.mid2.at[zd], lambda: self.m2s.at[zd], net.yn)

    def bfirst(self, zd):
        net, P, cut, rb = self.net, self.P, self.cut, self.rb
        if rb and zd > 0:
            net.go(net.at[0], lambda: P.at[:, zd, pl.ds(cut, rb), :], lambda: self.bbe.at[zd], lambda: self.bbes.at[zd], net.up)
        if rb and zd < 3:
            net.go(net.at[3], lambda: P.at[:, zd, pl.ds(cut, rb), :], lambda: self.bab.at[zd], lambda: self.babs.at[zd], net.dn)

    def direct(self, zd):
        net, P, h = self.net, self.P, self.h
        net.go(None, lambda: P.at[net.ux, zd, pl.ds(0, h), :], lambda: self.fx.at[zd, pl.ds(0, h), :], lambda: self.fxs.at[zd, 0], net.xn)
        net.go(None, lambda: P.at[net.uy, zd, pl.ds(h, h), :], lambda: self.fy.at[zd, pl.ds(h, h), :], lambda: self.fys.at[zd, 1], net.yn)

    def first(self, zd):
        self.mid_send(zd)
        self.bfirst(zd)
        self.direct(zd)

    def mids(self, zd):
        net, P, h, mid1, mid2 = self.net, self.P, self.h, self.mid1, self.mid2

        def add1(sl):
            mid1[zd, sl, :] = (wide(mid1[zd, sl, :]) + wide(P[net.uy, zd, sl, :])).astype(BF)

        def add2(sl):
            mid2[zd, sl, :] = (wide(mid2[zd, sl, :]) + wide(P[net.ux, zd, pl.ds(h + sl.start, 16), :])).astype(BF)

        net.wait(None, lambda: mid1.at[zd], self.m1s.at[zd])
        strips(h, add1)
        net.go(None, lambda: mid1.at[zd], lambda: self.fy.at[zd, pl.ds(0, h), :], lambda: self.fys.at[zd, 0], net.yn)
        net.wait(None, lambda: mid2.at[zd], self.m2s.at[zd])
        strips(h, add2)
        net.go(None, lambda: mid2.at[zd], lambda: self.fx.at[zd, pl.ds(h, h), :], lambda: self.fxs.at[zd, 1], net.xn)

    def route(self, zd, zz):
        if zz < zd:
            return True, self.net.up
        return False, self.net.dn

    def bhop(self, zd, zz):
        net, P, cut, rb = self.net, self.P, self.cut, self.rb
        if not rb:
            return
        upward, dev = self.route(zd, zz)
        buf, sems = (self.bbe, self.bbes) if upward else (self.bab, self.babs)
        here = net.at[zz]
        net.wait(here, lambda: buf.at[zd], sems.at[zd])

        def add():
            for q in range(4):
                def one(sl, q=q):
                    buf[zd, q, sl, :] = (wide(buf[zd, q, sl, :]) + wide(P[q, zd, pl.ds(cut + sl.start, 16), :])).astype(BF)
                strips(rb, one)

        pl.when(here)(add)
        net.go(here, lambda: buf.at[zd], lambda: buf.at[zd], lambda: sems.at[zd], dev)

    def square(self, zd, cond):
        net, h = self.net, self.h
        for half in (0, 1):
            net.wait(cond, lambda: self.fx.at[zd, pl.ds(half * h, h), :], self.fxs.at[zd, half])
            net.wait(cond, lambda: self.fy.at[zd, pl.ds(half * h, h), :], self.fys.at[zd, half])

    def local(self, zd, sl):
        return wide(self.P[self.net.u, zd, sl, :]) + wide(self.fx[zd, sl, :]) + wide(self.fy[zd, sl, :])

    def hop(self, zd, zz):
        net = self.net
        upward, dev = self.route(zd, zz)
        buf, sems = (self.be, self.bes) if upward else (self.ab, self.abs_)
        here = net.at[zz]
        self.square(zd, here)
        if zz in (0, 3):
            def begin(sl):
                self.fx[zd, sl, :] = self.local(zd, sl).astype(BF)

            pl.when(here)(lambda: strips(self.cut, begin))
            net.go(here, lambda: self.fx.at[zd], lambda: buf.at[zd], lambda: sems.at[zd], dev)
        else:
            def plus(sl):
                buf[zd, sl, :] = (self.local(zd, sl) + wide(buf[zd, sl, :])).astype(BF)

            net.wait(here, lambda: buf.at[zd], sems.at[zd])
            pl.when(here)(lambda: strips(self.cut, plus))
            net.go(here, lambda: buf.at[zd], lambda: buf.at[zd], lambda: sems.at[zd], dev)

    def bquad(self):
        net, P, cut, rb, hb, bm, bms = self.net, self.P, self.cut, self.rb, self.hb, self.bm, self.bms
        if not rb:
            return
        z = net.z
        net.wait(net.has_dn, lambda: self.bbe.at[z], self.bbes.at[z])
        net.wait(net.has_up, lambda: self.bab.at[z], self.babs.at[z])
        for q in range(4):
            def fold(sl, q=q):
                s = wide(P[q, z, pl.ds(cut + sl.start, 16), :])
                s = s + jnp.where(net.has_dn, wide(self.bbe[z, q, sl, :]), 0.0)
                s = s + jnp.where(net.has_up, wide(self.bab[z, q, sl, :]), 0.0)
                bm[q, sl, :] = s.astype(BF)
            strips(rb, fold)
        net.go(None, lambda: bm.at[net.ud, pl.ds(0, hb), :], lambda: bm.at[4, pl.ds(0, hb), :], lambda: bms.at[0], net.xn)
        net.go(None, lambda: bm.at[net.ud, pl.ds(hb, hb), :], lambda: bm.at[5, pl.ds(0, hb), :], lambda: bms.at[1], net.yn)
        net.go(None, lambda: bm.at[net.ux, pl.ds(0, hb), :], lambda: bm.at[6, pl.ds(0, hb), :], lambda: bms.at[2], net.xn)
        net.go(None, lambda: bm.at[net.uy, pl.ds(hb, hb), :], lambda: bm.at[7, pl.ds(hb, hb), :], lambda: bms.at[3], net.yn)

    def bquad2(self):
        net, rb, hb, bm, bms = self.net, self.rb, self.hb, self.bm, self.bms
        if not rb:
            return

        def add4(sl):
            bm[4, sl, :] = (wide(bm[4, sl, :]) + wide(bm[net.uy, sl, :])).astype(BF)

        def add5(sl):
            bm[5, sl, :] = (wide(bm[5, sl, :]) + wide(bm[net.ux, pl.ds(hb + sl.start, 16), :])).astype(BF)

        net.wait(None, lambda: bm.at[4, pl.ds(0, hb), :], bms.at[0])
        strips(hb, add4)
        net.go(None, lambda: bm.at[4, pl.ds(0, hb), :], lambda: bm.at[7, pl.ds(0, hb), :], lambda: bms.at[4], net.yn)
        net.wait(None, lambda: bm.at[5, pl.ds(0, hb), :], bms.at[1])
        strips(hb, add5)
        net.go(None, lambda: bm.at[5, pl.ds(0, hb), :], lambda: bm.at[6, pl.ds(hb, hb), :], lambda: bms.at[5], net.xn)

    def last(self, store):
        net, cut, rb, hb, bm, bms = self.net, self.cut, self.rb, self.hb, self.bm, self.bms
        z = net.z
        self.square(z, None)

        def own(sl):
            s = self.local(z, sl)
            s = s + jnp.where(net.has_dn, wide(self.be[z, sl, :]), 0.0)
            s = s + jnp.where(net.has_up, wide(self.ab[z, sl, :]), 0.0)
            store(sl, s)

        net.wait(net.has_dn, lambda: self.be.at[z], self.bes.at[z])
        net.wait(net.has_up, lambda: self.ab.at[z], self.abs_.at[z])
        strips(cut, own)
        if rb:
            net.wait(None, lambda: bm.at[6, pl.ds(0, hb), :], bms.at[2])
            net.wait(None, lambda: bm.at[6, pl.ds(hb, hb), :], bms.at[5])
            net.wait(None, lambda: bm.at[7, pl.ds(0, hb), :], bms.at[4])
            net.wait(None, lambda: bm.at[7, pl.ds(hb, hb), :], bms.at[3])
            strips(rb, lambda sl: store(
                pl.ds(cut + sl.start, 16), wide(bm[net.u, sl, :]) + wide(bm[6, sl, :]) + wide(bm[7, sl, :])))


def steps_of(sc, text):
    names = {"m": sc.mid_send, "f": sc.bfirst, "d": sc.direct, "M": sc.mids, "h": sc.hop, "b": sc.bhop, "Q": sc.bquad, "q": sc.bquad2}
    return [functools.partial(names[word[0]], *[int(digit) for digit in word[1:]]) for word in text.split()]


def run_steps(steps):
    for one in steps:
        one()


def rs_scratch(cut, R, D):
    h, rb = cut // 2, R - cut
    V = lambda *s: pltpu.VMEM(s, BF)
    S = pltpu.SemaphoreType.DMA
    return [V(4, h, D), V(4, h, D), V(4, cut, D), V(4, cut, D), V(4, cut, D), V(4, cut, D),
            V(4, 4, max(rb, 16), D), V(4, 4, max(rb, 16), D), V(8, max(rb, 16), D),
            S((4,)), S((4,)), S((4, 2)), S((4, 2)), S((4,)), S((4,)), S((4,)), S((4,)), S((6,))]


def rs_kernel(cut, P, o_ref, ssem, *scr):
    net = Net(ssem)
    net.barrier()
    sc = Scatter(net, cut, P, scr)

    def store(sl, v):
        o_ref[sl, :] = v.astype(o_ref.dtype)

    for zd in (3, 0, 2, 1):
        sc.first(zd)
    for zd in (3, 0, 2, 1):
        sc.mids(zd)
    sc.hop(3, 0); sc.hop(0, 3); sc.bhop(3, 1); sc.bhop(0, 2)
    sc.hop(2, 0); sc.hop(1, 3); sc.bhop(2, 1); sc.bhop(1, 2)
    sc.hop(3, 1); sc.hop(0, 2); sc.bhop(3, 2); sc.bhop(0, 1)
    sc.hop(1, 0); sc.hop(2, 3); sc.bquad()
    sc.hop(2, 1); sc.hop(1, 2)
    sc.hop(3, 2); sc.hop(0, 1); sc.bquad2()
    sc.last(store)
    net.finish()


def rs16(p, cid, cut=96, dtype=F32):
    _, _, R, D = p.shape
    DMA = pltpu.SemaphoreType.DMA
    return pl.pallas_call(
        functools.partial(rs_kernel, cut),
        out_shape=jax.ShapeDtypeStruct((R, D), dtype),
        in_specs=[pl.BlockSpec(memory_space=pltpu.VMEM)],
        out_specs=pl.BlockSpec(memory_space=pltpu.VMEM),
        scratch_shapes=[DMA((96,))] + rs_scratch(cut, R, D),
        compiler_params=pltpu.CompilerParams(collective_id=cid, has_side_effects=True, vmem_limit_bytes=56 * 2**20),
        name="scatter_rows",
    )(p)


class Gather:
    def __init__(self, net, rows, cut, at, plane, sems):
        self.net, self.rows, self.cut, self.ref, self.plane = net, rows, cut, at, plane
        self.zr, self.xr, self.yr, self.d1, self.d2, self.br, self.bz = sems
        self.h, self.rb = cut // 2, rows - cut
        self.hb = self.rb // 2
        z = net.z
        self.near = []
        for s in range(4):
            zl, zh = z - s, z + s
            self.near.append((
                (jnp.maximum(zl, 0), zl >= 0, jnp.logical_and(zl >= 0, net.has_up), net.up),
                (jnp.minimum(zh, 3), zh < 4, jnp.logical_and(zh < 4, net.has_dn), net.dn)))

    def same(self, cond, uu, zz, lo, n, sem, dev):
        ref = lambda: self.ref(uu, zz, lo, n)
        self.net.go(cond, ref, ref, sem, dev)

    def outward(self, zz, cond):
        net, cut = self.net, self.cut
        self.same(cond, net.u, zz, 0, cut, lambda: self.xr.at[zz], net.xn)
        self.same(cond, net.u, zz, 0, cut, lambda: self.yr.at[zz], net.yn)

    def begin(self):
        net, cut, rb, z = self.net, self.cut, self.rb, self.net.z
        self.same(net.has_up, net.u, z, 0, cut, lambda: self.zr.at[z], net.up)
        self.same(net.has_dn, net.u, z, 0, cut, lambda: self.zr.at[z], net.dn)
        if rb:
            self.same(None, net.u, z, cut, rb, lambda: self.br.at[0], net.xn)
            self.same(None, net.u, z, cut, rb, lambda: self.br.at[1], net.yn)
        self.outward(z, None)

    def begin2(self):
        net, cut, rb, hb, z = self.net, self.cut, self.rb, self.hb, self.net.z
        if rb:
            net.wait(None, lambda: self.ref(net.ux, z, cut, rb), self.br.at[0])
            self.same(None, net.ux, z, cut, hb, lambda: self.br.at[2], net.yn)
            net.wait(None, lambda: self.ref(net.uy, z, cut, rb), self.br.at[1])
            self.same(None, net.uy, z, cut + hb, hb, lambda: self.br.at[3], net.xn)

    def along(self, s):
        net = self.net
        for zz, cond, fwd, dev in self.near[s]:
            net.wait(cond, lambda zz=zz: self.ref(net.u, zz, 0, self.cut), self.zr.at[zz])
            self.same(fwd, net.u, zz, 0, self.cut, lambda zz=zz: self.zr.at[zz], dev)
            self.outward(zz, cond)

    def quads(self, s):
        net, cut, rb, hb, z = self.net, self.cut, self.rb, self.hb, self.net.z
        if not rb:
            return
        if s == 0:
            net.wait(None, lambda: self.ref(net.ud, z, cut, hb), self.br.at[2])
            net.wait(None, lambda: self.ref(net.ud, z, cut + hb, hb), self.br.at[3])
            whole = lambda: self.plane(z, cut, rb)
            net.go(net.has_up, whole, whole, lambda: self.bz.at[z], net.up)
            net.go(net.has_dn, whole, whole, lambda: self.bz.at[z], net.dn)
            return
        for zz, cond, fwd, dev in self.near[s]:
            whole = lambda zz=zz: self.plane(zz, cut, rb)
            net.wait(cond, whole, self.bz.at[zz])
            net.go(fwd, whole, whole, lambda zz=zz: self.bz.at[zz], dev)

    def planes(self, s):
        if s == 0:
            return ((self.net.z, None),)
        return tuple((zz, cond) for zz, cond, _f, _d in self.near[s])

    def cross(self, s):
        net, h, cut = self.net, self.h, self.cut
        for zz, cond in self.planes(s):
            net.wait(cond, lambda zz=zz: self.ref(net.ux, zz, 0, cut), self.xr.at[zz])
            self.same(cond, net.ux, zz, 0, h, lambda zz=zz: self.d1.at[zz], net.yn)
            net.wait(cond, lambda zz=zz: self.ref(net.uy, zz, 0, cut), self.yr.at[zz])
            self.same(cond, net.uy, zz, h, h, lambda zz=zz: self.d2.at[zz], net.xn)

    def settle(self, s):
        net, h = self.net, self.h
        for zz, cond in self.planes(s):
            net.wait(cond, lambda zz=zz: self.ref(net.ud, zz, 0, h), self.d1.at[zz])
            net.wait(cond, lambda zz=zz: self.ref(net.ud, zz, h, h), self.d2.at[zz])


def ag_sems():
    S = pltpu.SemaphoreType.DMA
    return [S((4,)) for _ in range(7)]


def greet(net, chips=16):
    bar = pltpu.get_barrier_semaphore()

    def hello(j, _):
        t = lax.rem(net.u * 4 + net.z + j, chips)
        pl.semaphore_signal(bar, inc=1, device_id=(t // 4, lax.rem(t, 4), net.c), device_id_type=MESH)
        return 0

    lax.fori_loop(1, chips, hello, 0)
    pl.semaphore_signal(bar, inc=1, device_id=(net.u, net.z, 1 - net.c), device_id_type=MESH)
    pl.semaphore_wait(bar, chips)


def each_chip(net, body, chips=16):
    def one(j, _):
        t = lax.rem(net.u * 4 + net.z + j, chips)
        body(t, (t // 4, lax.rem(t, 4), net.c))
        return 0

    lax.fori_loop(1, chips, one, 0)


def remote(src, dst, ssem, rsem, dev):
    return pltpu.make_async_remote_copy(
        src_ref=src, dst_ref=dst, send_sem=ssem, recv_sem=rsem, device_id=dev, device_id_type=MESH)


def landed(ref, sem):
    pltpu.make_async_copy(ref, ref, sem).wait()


def segment_rows(segments, k_seg, reach):
    k_seg[:, 0:reach] = jnp.full((1, reach), -1.0, F32)
    k_seg[:, reach:] = segments[...]


def rope_at(near, far, i):
    cf, sf = far[0, pl.ds(i, 1), :], far[1, pl.ds(i, 1), :]
    cn, sn = near[0], near[1]
    return cf * cn - sf * sn, sf * cn + cf * sn


def row_sums(v):
    return jnp.sum(v.T, axis=0, keepdims=True)


def column(row):
    return jnp.broadcast_to(row, (row.shape[1], row.shape[1])).T


def share_sums(net, sums, sums_all, out, lsem, ssem, rsem):
    me = net.u * 4 + net.z
    own = pltpu.make_async_copy(sums, sums_all.at[me], lsem)
    own.start()
    each_chip(net, lambda t, dev: remote(sums, sums_all.at[me], ssem, rsem, dev).start())
    own.wait()
    part = sums_all.at[pl.ds(0, 15)]
    landed(part, rsem)
    total = sums_all[0]
    for i in range(1, 16):
        total = total + sums_all[i]
    out[...] = total
    landed(part, ssem)


def greet_all(net, count=32):
    bar = pltpu.get_barrier_semaphore()
    me = net.u * 8 + net.z * 2 + net.c

    def hello(j, _):
        t = lax.rem(me + j, count)
        pl.semaphore_signal(bar, inc=1, device_id=(t // 8, lax.rem(t, 8) // 2, lax.rem(t, 2)), device_id_type=MESH)
        return 0

    lax.fori_loop(1, count, hello, 0)
    pl.semaphore_wait(bar, count - 1)


def qkv_kernel(cut, x_ref, wq, wk, wv, block, cot, n1_o, lin_o, wf_o, tot, sw, C, X, lin, wf, nb, gain, sums, sums_all, lsem, nsem, msem, ssem, csem, *gs):
    net = Net(ssem)
    u, z, c = net.u, net.z, net.c
    me = u * 4 + z
    rows, width = X.shape[2], X.shape[3]
    partner = (u, z, 1 - c)
    own = pltpu.make_async_copy(x_ref, X.at[u, z], lsem.at[0])
    own.start()

    def piece(t, i):
        return ((wq, wk, wv)[i].at[:, pl.ds(pl.multiple_of(t * 128, 128), 128)], wf.at[me, c, :, pl.ds(i * 128, 128)])

    own_w = [pltpu.make_async_copy(*piece(me, i), lsem.at[1]) for i in range(3)]
    for one in own_w:
        one.start()
    own_c = pltpu.make_async_copy(cot, C.at[u, z], lsem.at[3])
    own_c.start()
    dev_me = me * 2 + c
    greet_all(net)
    own.wait()
    ga = Gather(net, rows, cut, lambda uu, zz, lo, n: X.at[uu, zz, pl.ds(lo, n), :],
                lambda zz, lo, n: X.at[:, zz, pl.ds(lo, n), :], gs[:7])
    netc = Net(csem)
    gc = Gather(netc, rows, cut, lambda uu, zz, lo, n: C.at[uu, zz, pl.ds(lo, n), :],
                lambda zz, lo, n: C.at[:, zz, pl.ds(lo, n), :], gs[7:])
    ga.begin()

    def tell(j, _):
        t = lax.rem(dev_me + j, 32)
        remote(block.at[t // 2], sw.at[dev_me], msem.at[6], msem.at[7], (t // 8, lax.rem(t, 8) // 2, lax.rem(t, 2))).start()
        return 0

    lax.fori_loop(1, 32, tell, 0)
    sw[dev_me] = block[me]

    def columns(t, dev):
        for i in range(3):
            remote(*piece(t, i), msem.at[0], msem.at[1], dev).start()

    each_chip(net, columns)

    def plane(zz):
        def chunk(uu, _):
            slot = lax.rem(uu, 2)
            k = uu * 4 + zz

            def norm(i, _):
                sl = pl.ds(pl.multiple_of(i * 16, 16), 16)
                v = X[uu, zz, sl, :].astype(F32)
                r = lax.rsqrt(jnp.mean(v * v, axis=1, keepdims=True) + EPS)
                nb[slot, sl, :] = (v * r * gain[...]).astype(BF)
                return 0

            def stored(s):
                return pltpu.make_async_copy(nb.at[s], n1_o.at[k], nsem.at[s])

            pl.when(uu >= 2)(lambda: stored(slot).wait())
            lax.fori_loop(0, rows // 16, norm, 0)
            stored(slot).start()
            got = dot(nb[slot], wf[...].reshape(width, wf.shape[-1]), ((1,), (0,)))
            lin[k] = got
            q, kk = got[:, :128], got[:, 128:256]
            sums[pl.ds(k, 1), :] = row_sums(q * q)
            sums[pl.ds(16 + k, 1), :] = row_sums(kk * kk)
            return 0

        lax.fori_loop(0, 4, chunk, 0)
        for s in (0, 1):
            pltpu.make_async_copy(nb.at[s], n1_o.at[0], nsem.at[s]).wait()

    def compute(s):
        for zz, cond in ga.planes(s):
            if cond is None:
                plane(zz)
            else:
                pl.when(cond)(lambda zz=zz: plane(zz))

    ga.begin2()
    ga.along(1)
    ga.quads(0)
    ga.cross(0)
    landed(wf.at[0, 0], lsem.at[1])
    landed(wf.at[pl.ds(0, 15), 0], msem.at[1])
    to_partner = remote(wf.at[:, c], wf.at[:, c], msem.at[2], msem.at[3], partner)
    to_partner.start()
    own_c.wait()
    ga.along(2)
    ga.quads(1)
    ga.cross(1)
    gc.begin()
    landed(sw.at[pl.ds(0, 31)], msem.at[7])
    for e in range(16):
        gain[:, e * 128 : (e + 1) * 128] = sw[2 * e, 2:3, :] + sw[2 * e + 1, 2:3, :]
    ga.settle(0)
    landed(wf.at[:, 1 - c], msem.at[3])
    keep_w = pltpu.make_async_copy(wf, wf_o, lsem.at[0])
    keep_w.start()
    compute(0)
    gc.begin2()
    ga.along(3)
    ga.quads(2)
    ga.cross(2)
    ga.settle(1)
    gc.along(1)
    gc.quads(0)
    gc.cross(0)
    compute(1)
    ga.quads(3)
    ga.cross(3)
    ga.settle(2)
    gc.along(2)
    gc.quads(1)
    gc.cross(1)
    compute(2)
    ga.settle(3)
    gc.along(3)
    gc.quads(2)
    gc.cross(2)
    compute(3)
    keep = pltpu.make_async_copy(lin, lin_o, lsem.at[1])
    keep.start()
    landed(wf.at[pl.ds(0, 15), 0], msem.at[0])
    landed(wf.at[:, c], msem.at[2])
    share_sums(net, sums, sums_all, tot, lsem.at[2], msem.at[4], msem.at[5])
    gc.quads(3)
    gc.cross(3)
    for s in range(4):
        gc.settle(s)
    landed(sw.at[pl.ds(0, 31)], msem.at[6])
    keep_w.wait()
    keep.wait()
    net.finish()
    netc.finish()


def run_qkv(x, wq, wk, wv, block, cot, cid, cut=96):
    R, D = x.shape
    N = 384
    DMA = pltpu.SemaphoreType.DMA
    S = jax.ShapeDtypeStruct
    V = lambda *s: pltpu.VMEM(s, BF)
    VF = lambda *s: pltpu.VMEM(s, F32)
    A = pl.BlockSpec(memory_space=pl.ANY)
    M = pl.BlockSpec(memory_space=pltpu.VMEM)
    return pl.pallas_call(
        functools.partial(qkv_kernel, cut),
        out_shape=(S((16, R, D), BF), S((16, R, N), F32), S((16, 2, R // 2, N), BF), S((32, 128), F32),
                   S((32, 8, 128), F32), S((4, 4) + cot.shape, BF)),
        in_specs=[A, A, A, A, M, A],
        out_specs=(A, A, A, M, M, A),
        scratch_shapes=[V(4, 4, R, D), VF(16, R, N), V(16, 2, R // 2, N), V(2, R, D), VF(1, D), VF(32, 128), VF(16, 32, 128),
                        DMA((4,)), DMA((2,)), DMA((8,)), DMA((64,)), DMA((64,))] + ag_sems() + ag_sems(),
        compiler_params=pltpu.CompilerParams(collective_id=cid, has_side_effects=True, vmem_limit_bytes=63 * 2**20),
        name="project",
    )(x, wq, wk, wv, block, cot)


def group_of(t):
    g = t // 2
    return jnp.where(g == 0, 3, jnp.where(g == 1, 0, jnp.where(g == 2, 2, 1)))


def expert_kernel(cut, n2, cot_a, cot_b, share_rows, gate, up, down, d_n2, p_out, n2_o, other, dg_o, du_o, dd_o,
                  X, C, GU, W, A, hid, pb, fs, share, lsem, wsem, wrs, psem, tsem, osem, ors, fsem, sa, sr, *scr):
    ga_sems, rs_bufs = scr[:7], scr[7:]
    na, nr = Net(sa), Net(sr)
    u, z, c = na.u, na.z, na.c
    partner = (u, z, 1 - c)
    rows, width = X.shape[2], X.shape[3]
    ff = W.shape[0]
    half, half_ff = gate.shape[0], down.shape[0]
    tokens = 16 * rows
    tile = 256
    span = 512
    side = width // 2
    first = [pltpu.make_async_copy(n2, X.at[u, z], lsem.at[0]),
             pltpu.make_async_copy(cot_a, C.at[:, :, :, pl.ds(0, side)], lsem.at[1]),
             pltpu.make_async_copy(cot_b, C.at[:, :, :, pl.ds(side, side)], lsem.at[5])]

    def weights():
        mine = pl.ds(pl.multiple_of(c * half, half), half)
        mine_ff = pl.ds(pl.multiple_of(c * half_ff, half_ff), half_ff)
        return ((gate, GU.at[mine, pl.ds(0, ff)]), (up, GU.at[mine, pl.ds(ff, ff)]), (down, W.at[mine_ff, :]))

    own_w = [pltpu.make_async_copy(a, b, lsem.at[2 + i]) for i, (a, b) in enumerate(weights())]
    for one in first + own_w:
        one.start()
    for k in range(16):
        share[k // 4, k % 4] = column(share_rows[k : k + 1, :])[:, 0:1]
    na.barrier((partner,))
    first[0].wait()

    def gather(net, buf, sems):
        return Gather(net, rows, cut, lambda uu, zz, lo, n: buf.at[uu, zz, pl.ds(lo, n), :],
                      lambda zz, lo, n: buf.at[:, zz, pl.ds(lo, n), :], sems)

    ga = gather(na, X, ga_sems)
    ga.begin()
    sent_w = [remote(a, b, wsem.at[i], wrs.at[i], partner) for i, (a, b) in enumerate(weights())]
    for one in sent_w:
        one.start()

    def forward(zz):
        pltpu.make_async_copy(X.at[:, zz], n2_o.at[:, zz], psem.at[1]).start()

        def scale(i, _):
            sl = pl.ds(pl.multiple_of(i * 16, 16), 16)
            C[:, zz, sl, :] = (share[:, zz, sl, :] * C[:, zz, sl, :].astype(F32)).astype(BF)
            return 0

        lax.fori_loop(0, rows // 16, scale, 0)

        def inner(n, _):
            gcols = pl.ds(pl.multiple_of(n * span, span), span)
            ucols = pl.ds(pl.multiple_of(ff + n * span, span), span)
            xv = X[:, zz].reshape(4 * rows, width)
            g = dot(xv, GU[:, gcols], ((1,), (0,)))
            uu = dot(xv, GU[:, ucols], ((1,), (0,)))
            s = jax.nn.sigmoid(g)
            gs = g * s
            hid[:, zz, :, gcols] = (gs * uu).astype(BF).reshape(4, rows, span)
            dh = dot(C[:, zz].reshape(4 * rows, width), W[gcols, :], ((1,), (1,)))
            A[:, zz, :, gcols] = (dh * uu * s * (1.0 + g * (1.0 - s))).astype(BF).reshape(4, rows, span)
            A[:, zz, :, ucols] = (dh * gs).astype(BF).reshape(4, rows, span)
            return 0

        lax.fori_loop(0, ff // span, inner, 0)
        weight = share[:, zz]

        def flushed(n):
            cols = pl.ds(pl.multiple_of(n * span, span), span)
            slot = lax.rem(n, 2)
            return pltpu.make_async_copy(pb.at[slot], p_out.at[:, zz, :, cols], osem.at[slot])

        def outer(n, _):
            cols = pl.ds(pl.multiple_of(n * span, span), span)
            made = dot(hid[:, zz].reshape(4 * rows, ff), W[:, cols], ((1,), (0,)))
            made = made.astype(BF).astype(F32).reshape(4, rows, span)
            pl.when(n >= 2)(lambda: flushed(n - 2).wait())
            pb[lax.rem(n, 2)] = (weight * made).astype(BF)
            flushed(n).start()
            return 0

        count = width // span
        lax.fori_loop(0, count, outer, 0)
        flushed(count - 2).wait()
        flushed(count - 1).wait()

    def planes(s):
        if s == 0:
            forward(z)
            return

        def one(d, _):
            zz = jnp.where(d == 0, z - s, z + s)
            pl.when(jnp.logical_and(zz >= 0, zz < 4))(lambda: forward(zz))
            return 0

        lax.fori_loop(0, 2, one, 0)

    ga.begin2()
    ga.along(1)
    ga.quads(0)
    ga.cross(0)
    ga.along(2)
    ga.quads(1)
    ga.cross(1)
    ga.settle(0)
    for one in own_w:
        one.wait()
    for one in sent_w:
        one.wait_recv()
    first[1].wait()
    first[2].wait()
    planes(0)
    ga.along(3)
    ga.quads(2)
    ga.cross(2)
    ga.settle(1)
    planes(1)
    ga.quads(3)
    ga.cross(3)
    ga.settle(2)
    planes(2)
    ga.settle(3)
    planes(3)
    na.finish()
    for one in sent_w:
        one.wait_send()
    landed(X, psem.at[1])
    sc = Scatter(nr, cut, X, rs_bufs)

    def backward(t):
        zd = group_of(t)
        base = lax.rem(t, 2) * (width // 2)

        def outer(n, _):
            cols = pl.ds(pl.multiple_of(base + n * span, span), span)
            back = dot(A[:, zd].reshape(4 * rows, 2 * ff), GU[cols, :], ((1,), (1,)))
            X[:, zd, :, cols] = back.astype(BF).reshape(4, rows, span)
            return 0

        lax.fori_loop(0, width // 2 // span, outer, 0)

    def acts(steps, t):
        for at, todo in steps.items():
            def act(todo=todo):
                for one in todo:
                    one()
            pl.when(t == at)(act)

    def at_turns(table):
        return {t: steps_of(sc, words) for t, words in table.items()}

    steps = at_turns({1: "m3 f3 d3", 3: "m0 f0 d0", 5: "m2 f2 d2 M3", 6: "b31", 7: "m1 f1 d1 M0 b02"})

    def turn(t, _):
        backward(t)
        acts(steps, t)
        return 0

    lax.fori_loop(0, 8, turn, 0)

    GU4 = GU.reshape(4, 4, rows, width)
    left = W.at[pl.ds(0, tile), :]

    def tile_load(k, which):
        slot = lax.rem(k, 2)
        cols = pl.ds(pl.multiple_of((which * 4 + k) * tile, tile), tile)
        return pltpu.make_async_copy(
            n2_o.at[:, :, :, cols], GU4.at[:, :, :, pl.ds(pl.multiple_of(slot * tile, tile), tile)], tsem.at[slot])

    def left_tokens(k):
        cols = pl.ds(pl.multiple_of(lax.rem(k, 2) * tile, tile), tile)

        def one(b, _):
            sl = pl.ds(pl.multiple_of(b * tile, tile), tile)
            left[:, sl] = GU[sl, cols].T
            return 0

        lax.fori_loop(0, tokens // tile, one, 0)

    def left_hidden(k, which):
        cols = pl.ds(pl.multiple_of((which * 2 + k) * tile, tile), tile)
        flat = hid.reshape(tokens, ff)

        def one(b, _):
            sl = pl.ds(pl.multiple_of(b * tile, tile), tile)
            left[:, sl] = flat[sl, cols].T
            return 0

        lax.fori_loop(0, tokens // tile, one, 0)

    def products(right, store):
        flat = right.reshape(tokens, width)

        def one(n, _):
            cols = pl.ds(pl.multiple_of(n * 512, 512), 512)
            store(cols, n, dot(left[...], flat[:, cols], ((1,), (0,))))
            return 0

        lax.fori_loop(0, width // 512, one, 0)

    def sent(k):
        slot = W.at[pl.ds(pl.multiple_of(tile + lax.rem(k, 2) * tile, tile), tile), :]
        return slot, remote(slot, other.at[k], osem.at[k], ors.at[k], partner)

    tile_load(0, 1 - c).start()

    def other_tile(k, _):
        slot, copy = sent(k)

        @pl.when(k >= 2)
        def _():
            sent(k - 2)[1].wait_send()

        def store(cols, n, v):
            slot[:, cols] = v.astype(BF)

        @pl.when(k < 4)
        def _():
            pl.when(k < 3)(lambda: tile_load(k + 1, 1 - c).start())
            tile_load(k, 1 - c).wait()
            left_tokens(k)
            products(A, store)

        @pl.when(k >= 4)
        def _():
            left_hidden(k - 4, 1 - c)
            products(C, store)

        copy.start()
        acts(at_turns({0: "M2", 1: "h30 b32 b21", 2: "M1 h03 b01", 3: "h31 b12", 4: "h02 h20", 5: "h32 h23"}), k)
        return 0

    lax.fori_loop(0, 6, other_tile, 0)

    def store_out(sl, v):
        d_n2[sl, :] = v

    tile_load(0, c).start()
    got = W.at[pl.ds(3 * tile, tile), :]

    def flush(k, h):
        i = pl.ds(pl.multiple_of(lax.rem(k, 4) * tile, tile), tile)

        def go(dst):
            pltpu.make_async_copy(fs.at[h], dst, fsem.at[h]).start()

        pl.when(k < 4)(lambda: go((dg_o, du_o)[h].at[i, :]))
        pl.when(k >= 4)(lambda: go(dd_o.at[i, pl.ds(h * 1024, 1024)]))

    def own_tile(k, _):
        fetch = pltpu.make_async_copy(other.at[k], got, lsem.at[0])
        landed(other.at[k], ors.at[k])
        fetch.start()

        def finish(right):
            flat = right.reshape(tokens, width)
            fetch.wait()
            for h in (0, 1):
                pl.when(k > 0)(lambda: landed(fs.at[h], fsem.at[h]))
                for n in (0, 1):
                    cols = pl.ds(h * 1024 + n * 512, 512)
                    fs[h, :, n * 512 : (n + 1) * 512] = dot(left[...], flat[:, cols], ((1,), (0,))) + wide(got[:, cols])
                flush(k, h)

        @pl.when(k < 4)
        def _():
            pl.when(k < 3)(lambda: tile_load(k + 1, c).start())
            tile_load(k, c).wait()
            left_tokens(k)
            finish(A)

        @pl.when(k >= 4)
        def _():
            left_hidden(k - 4, c)
            finish(C)

        acts(at_turns({0: "h01 h10", 1: "Q h21", 2: "h13", 4: "h12", 5: "q"}), k)
        return 0

    lax.fori_loop(0, 6, own_tile, 0)
    sc.last(store_out)
    for h in (0, 1):
        landed(fs.at[h], fsem.at[h])
    for k in (4, 5):
        sent(k)[1].wait_send()
    nr.finish()


def run_expert(n2, cot_a, cot_b, share, gate, up, down, cid, cut=96):
    R, D = n2.shape
    half, ff = gate.shape
    DMA = pltpu.SemaphoreType.DMA
    S = jax.ShapeDtypeStruct
    V = lambda *s: pltpu.VMEM(s, BF)
    A = pl.BlockSpec(memory_space=pl.ANY)
    M = pl.BlockSpec(memory_space=pltpu.VMEM)
    return pl.pallas_call(
        functools.partial(expert_kernel, cut),
        out_shape=(S((R, D), F32), S((4, 4, R, D), BF), S((4, 4, R, D), BF), S((6, 256, D), BF),
                   S((half, ff), F32), S((half, ff), F32), S(down.shape, F32)),
        in_specs=[A, A, A, M, A, A, A],
        out_specs=(M,) + (A,) * 6,
        scratch_shapes=[V(4, 4, R, D), V(4, 4, R, D), V(D, 2 * ff), V(ff, D), V(4, 4, R, 2 * ff), V(4, 4, R, ff),
                        V(2, 4, R, 512), pltpu.VMEM((2, 256, 1024), F32), pltpu.VMEM((4, 4, R, 1), F32),
                        DMA((6,)), DMA((3,)), DMA((3,)), DMA((2,)), DMA((2,)), DMA((6,)), DMA((6,)), DMA((2,)),
                        DMA((64,)), DMA((96,))] + ag_sems() + rs_scratch(cut, R, D),
        compiler_params=pltpu.CompilerParams(collective_id=cid, has_side_effects=True, vmem_limit_bytes=63 * 2**20),
        name="expert",
    )(n2, cot_a, cot_b, share, gate, up, down)


def finish_kernel(cut, d_lin, wf, n1, att, x_in, d_res, gain, d_gain_two, d_gains,
                  d_wo, d_inputs, d_wq, d_wk, d_wv, gains_o,
                  P, PO, PG, PT, wsum, nt, left, keep, give, got, send, recv, d_n1, d_gain, gb, gr,
                  lsem, tsem, msem, s1, s2, *bufs):
    net, net2 = Net(s1), Net(s2)
    u, z, c = net.u, net.z, net.c
    me = u * 4 + z
    rows, width = P.shape[2], P.shape[3]
    lanes = d_lin.shape[2]
    tokens = 16 * rows
    tile = 256
    partner = (u, z, 1 - c)
    half = len(bufs) // 2
    sc1, sc2 = Scatter(net, cut, P, bufs[:half]), Scatter(net2, cut, PO, bufs[half:])

    def tile_load(k):
        slot = lax.rem(k, 2)
        return pltpu.make_async_copy(n1.at[:, :, pl.ds(pl.multiple_of(k * tile, tile), tile)], nt.at[slot], tsem.at[slot])

    tile_load(0).start()
    greet_all(net)

    def one(words):
        run_steps(steps_of(sc1, words))

    def two(words):
        run_steps(steps_of(sc2, words))

    def group(zd):
        def one(n, _):
            cols = pl.ds(pl.multiple_of(n * 512, 512), 512)
            w = wf.reshape(width, lanes)
            for q in range(4):
                P[q, zd, :, cols] = dot(d_lin[q * 4 + zd], w[cols, :], ((1,), (1,))).astype(BF)
            return 0

        lax.fori_loop(0, width // 512, one, 0)

    for zd in (3, 0, 2, 1):
        group(zd)
        one(f"m{zd}" + (f" f{zd}" if zd in (3, 0) else ""))

    side = width // 2
    own_cols = pl.ds(pl.multiple_of(c * side, side), side)
    give_cols = pl.ds(pl.multiple_of((1 - c) * side, side), side)

    def outer(e, _):
        turned_att = att[e].T
        PG[e // 4, lax.rem(e, 4)] = dot(turned_att, d_res[:, give_cols].astype(BF), ((1,), (0,))).astype(BF)
        PO[e // 4, lax.rem(e, 4)] = dot(turned_att, d_res[:, own_cols].astype(BF), ((1,), (0,))).astype(BF)
        return 0

    lax.fori_loop(0, 16, outer, 0)
    halves = remote(PG, PT, msem.at[6], msem.at[7], partner)
    halves.start()

    def join():
        landed(PT, msem.at[7])

        def add(e, _):
            def strip(sl):
                at = (e // 4, lax.rem(e, 4), sl, slice(None))
                PO[at] = (wide(PO[at]) + wide(PT[at])).astype(BF)

            strips(rows, strip)
            return 0

        lax.fori_loop(0, 16, add, 0)

    def store1(sl, v):
        d_n1[sl, :] = v

    def store2(sl, v):
        wsum[sl, :] = v


    def grads(k):
        if k < 7:
            tile_load(k + 1).start()
        tile_load(k).wait()
        slot = k % 2
        flat = nt.at[slot].reshape(tokens, tile)

        def turn(b, _):
            sl = pl.ds(pl.multiple_of(b * tile, tile), tile)
            left[:, sl] = flat[sl, :].T
            return 0

        lax.fori_loop(0, tokens // tile, turn, 0)
        made = dot(left[...], d_lin[...].reshape(tokens, lanes), ((1,), (0,)))
        for i in range(2):
            first, second = made[i * 128 : i * 128 + 64], made[i * 128 + 64 : (i + 1) * 128]
            keep[2 * k + i] = jnp.where(c == 0, first, second)
            give[2 * k + i] = jnp.where(c == 0, second, first).astype(BF)

    one("d3 d0")
    grads(0)
    grads(1)
    one("f2 f1 d2 d1")
    join()
    two("m3 m0 m2 m1 f3 f0")
    grads(2)
    grads(3)
    one("M3 M0 M2 M1")
    two("d3 d0 d2 d1 f2 f1")
    grads(4)
    grads(5)
    one("b31 b02")
    grads(6)
    grads(7)
    across = remote(give, got, msem.at[0], msem.at[1], partner)
    across.start()
    two("M3 M0 M2 M1")
    one("b21 b12 b32 b01 h30 h03")
    landed(got, msem.at[1])

    def total(e, _):
        send[e] = (keep[e] + wide(got[e])).astype(BF)
        return 0

    lax.fori_loop(0, 16, total, 0)
    each_chip(net, lambda t, dev: remote(send.at[t], recv.at[me], msem.at[2], msem.at[3], dev).start())
    recv[me] = send[me]
    two("b31 b02 b21 b12 b32 b01")
    one("h31 h02 h20 h13 Q")
    two("h30 h03 h20 h13 Q")
    one("h32 h01 h10 h23")
    two("h31 h02 h10 h23")
    one("h21 h12 q")
    sc1.last(store1)
    d_gain[...] = jnp.zeros_like(d_gain)

    def norm_back(i, _):
        sl = pl.ds(pl.multiple_of(i * 16, 16), 16)
        v, d = wide(x_in[sl, :]), d_n1[sl, :]
        r = lax.rsqrt(jnp.mean(v * v, axis=1, keepdims=True) + EPS)
        scaled = d * gain[...]
        inner = jnp.mean(scaled * v, axis=1, keepdims=True)
        d_inputs[sl, :] = d_res[sl, :] + r * scaled - v * (r * r * r * inner)
        d_gain[...] += jnp.sum(d * v * r, axis=0, keepdims=True)
        return 0

    lax.fori_loop(0, rows // 16, norm_back, 0)
    gb[...] = jnp.zeros_like(gb)
    gb[me, 2:4, :] = d_gains[0:2, :]
    for e in range(16):
        gb[e, 0:1, :] = d_gain[:, e * 128 : (e + 1) * 128]
        gb[e, 1:2, :] = d_gain_two[:, e * 128 : (e + 1) * 128]
    dev_me = me * 2 + c

    def tell(j, _):
        t = lax.rem(dev_me + j, 32)
        remote(gb.at[t // 2], gr.at[dev_me], msem.at[4], msem.at[5], (t // 8, lax.rem(t, 8) // 2, lax.rem(t, 2))).start()
        return 0

    lax.fori_loop(1, 32, tell, 0)
    gr[dev_me] = gb[me]
    two("h32 h01 h21 h12 q")
    landed(recv.at[pl.ds(0, 15)], msem.at[3])
    for e in range(16):
        piece = wide(recv[e])
        for i, out in enumerate((d_wq, d_wk, d_wv)):
            out[:, e * 128 : (e + 1) * 128] = piece[:, i * 128 : (i + 1) * 128]
    landed(gr.at[pl.ds(0, 31)], msem.at[5])
    sums = gr[0]
    for i in range(1, 32):
        sums = sums + gr[i]
    gains_o[...] = jnp.where(c == 0, sums[:, :64], sums[:, 64:])
    sc2.last(store2)
    d_wo[:, own_cols] = wsum[pl.ds(pl.multiple_of(c * 64, 64), 64), :]
    theirs = remote(wsum.at[pl.ds(pl.multiple_of((1 - c) * 64, 64), 64), :], d_wo.at[:, own_cols], msem.at[8], msem.at[9], partner)
    theirs.start()
    landed(PG, msem.at[6])
    landed(give, msem.at[0])
    landed(recv.at[pl.ds(0, 15)], msem.at[2])
    landed(gr.at[pl.ds(0, 31)], msem.at[4])
    theirs.wait_send()
    landed(d_wo.at[:, give_cols], msem.at[9])
    net.finish()
    net2.finish()


def run_finish(d_lin, wf, n1, att, x_in, d_res, gain, d_gain_two, d_gains, cid, cut=96):
    R, D = x_in.shape
    N = d_lin.shape[2]
    DMA = pltpu.SemaphoreType.DMA
    S = jax.ShapeDtypeStruct
    V = lambda *s: pltpu.VMEM(s, BF)
    VF = lambda *s: pltpu.VMEM(s, F32)
    A = pl.BlockSpec(memory_space=pl.ANY)
    M = pl.BlockSpec(memory_space=pltpu.VMEM)
    own = S((R // 2, D), F32)
    return pl.pallas_call(
        functools.partial(finish_kernel, cut),
        out_shape=(own, S((R, D), F32), own, own, own, S((8, 64), F32)),
        in_specs=[M, M, A] + [M] * 6,
        out_specs=(M,) * 6,
        scratch_shapes=[V(4, 4, R, D), V(4, 4, R, D // 2), V(4, 4, R, D // 2), V(4, 4, R, D // 2), VF(R, D // 2), V(2, 16, R, 256), V(256, 16 * R), VF(16, 64, N), V(16, 64, N),
                        V(16, 64, N), V(16, 64, N), V(16, 64, N), VF(R, D), VF(1, D), VF(16, 8, 128), VF(32, 8, 128),
                        DMA((1,)), DMA((2,)), DMA((10,)), DMA((64,)), DMA((64,))] + rs_scratch(cut, R, D) + rs_scratch(cut, R, D // 2),
        compiler_params=pltpu.CompilerParams(collective_id=cid, has_side_effects=True, vmem_limit_bytes=63 * 2**20),
        name="finish",
    )(d_lin, wf, n1, att, x_in, d_res, gain, d_gain_two, d_gains)

def band_scores(q, k, q_seg, k_seg, scale, reach):
    scores = dot(q, k, ((1,), (1,))) * scale
    q_at = lax.broadcasted_iota(jnp.int32, scores.shape, 0)
    k_at = lax.broadcasted_iota(jnp.int32, scores.shape, 1)
    return scores, (k_seg == q_seg) & (k_at <= q_at + reach)


def turned(v, cosine, sine):
    return v * cosine + pltpu.roll(v, 64, axis=1) * sine


def turned_back(v, cosine, sine):
    return v * cosine - pltpu.roll(v, 64, axis=1) * sine


def attend_kernel(scale, pads, cut, lin_h, tot, near, far, gq, gk, q_seg, segments, w_own, x_in, gain, cot,
                  wo_o, q_rot_o, kv_o, o_o, lse, att_o, residual_o, n2, C,
                  lin, k_seg, q_rot, kv, o_ref, att, residual, wo, lsem, msem, psem, ksem, ssem, csem, *gs):
    net = Net(ssem)
    u, z, c = net.u, net.z, net.c
    me = u * 4 + z
    rows = x_in.shape[0]
    width = x_in.shape[1]
    reach = pads * 2 * rows
    partner = (u, z, 1 - c)
    own = pltpu.make_async_copy(w_own, wo.at[u, z, c], lsem.at[0])
    own.start()
    load = pltpu.make_async_copy(lin_h, lin, ksem.at[0])
    load.start()
    own_c = pltpu.make_async_copy(cot, C.at[u, z], lsem.at[2])
    own_c.start()
    greet(net)
    own.wait()
    ga = Gather(net, rows // 2, rows // 2, lambda uu, zz, lo, n: wo.at[uu, zz, c, pl.ds(lo, n), :], None, gs[:7])
    netc = Net(csem)
    gc = Gather(netc, rows, cut, lambda uu, zz, lo, n: C.at[uu, zz, pl.ds(lo, n), :],
                lambda zz, lo, n: C.at[:, zz, pl.ds(lo, n), :], gs[7:])

    def halves(s):
        ga.settle(s)
        for zz, cond in ga.planes(s):
            ref = lambda zz=zz: wo.at[:, zz, c]
            net.go(cond, ref, ref, lambda zz=zz: psem.at[zz], partner)

    ga.begin()
    segment_rows(segments, k_seg, reach)
    load.wait()
    for i in range(pads):
        kv[:, i] = jnp.zeros(kv.shape[:1] + kv.shape[2:], BF)

    def ready(i, _):
        both = lin[i]
        rq = lax.rsqrt(column(tot[pl.ds(i, 1), :]) / width + EPS)
        rk = lax.rsqrt(column(tot[pl.ds(16 + i, 1), :]) / width + EPS)
        cs, sn = rope_at(near, far, i)
        q_rot[i] = turned(both[:, :128] * rq * gq[...], cs, sn).astype(BF)
        kv[0, pads + i, c] = turned(both[:, 128:256] * rk * gk[...], cs, sn).astype(BF)
        kv[1, pads + i, c] = both[:, 256:].astype(BF)
        return 0

    lax.fori_loop(0, 16, ready, 0)
    mine = kv.at[:, pl.ds(pads, 16), c]
    to_partner = remote(mine, mine, msem.at[0], msem.at[1], partner)
    to_partner.start()
    ga.along(1)
    ga.cross(0)
    own_c.wait()
    gc.begin()
    landed(kv.at[:, pl.ds(pads, 16), 1 - c], msem.at[1])

    def block(j, _):
        i = lax.rem(me + 1 + j, 16)
        first = 2 * i + c
        band = pl.ds(pl.multiple_of(first * rows, rows), rows + reach)
        kf, vf = kv.at[0].reshape((pads + 16) * 2 * rows, 128), kv.at[1].reshape((pads + 16) * 2 * rows, 128)
        scores, allowed = band_scores(q_rot[i], kf[band, :], column(q_seg[pl.ds(i, 1), :])[:, 0:1], k_seg[:, band], scale, reach)
        scores = jnp.where(allowed, scores, NEG)
        top = jnp.max(scores, axis=1, keepdims=True)
        weights = jnp.where(allowed, jnp.exp(scores - top), 0.0)
        total = jnp.sum(weights, axis=1, keepdims=True)
        probs = (weights / total).astype(BF)
        o_ref[i] = dot(probs, vf[band, :], ((1,), (0,))).astype(BF)
        lse[i] = top + jnp.log(total)

        @pl.when(j < 15)
        def _():
            remote(o_ref.at[i], att.at[me], msem.at[2], msem.at[3], (i // 4, lax.rem(i, 4), c)).start()

        return 0

    lax.fori_loop(0, 5, block, 0)
    ga.along(2)
    ga.cross(1)
    halves(0)
    gc.begin2()
    lax.fori_loop(5, 10, block, 0)
    ga.along(3)
    ga.cross(2)
    halves(1)
    gc.along(1)
    gc.quads(0)
    gc.cross(0)
    lax.fori_loop(10, 16, block, 0)
    ga.cross(3)
    halves(2)
    gc.along(2)
    gc.quads(1)
    gc.cross(1)
    halves(3)
    att[me] = o_ref[me]
    part = att.at[pl.ds(0, 15)]
    landed(part, msem.at[3])
    for zz in range(4):
        landed(wo.at[:, zz, 1 - c], psem.at[zz])
    keep = [pltpu.make_async_copy(a, o, ksem.at[j]) for j, (a, o) in enumerate(
        ((wo, wo_o), (q_rot, q_rot_o), (kv, kv_o), (o_ref, o_o), (att, att_o)))]
    for one in keep:
        one.start()
    tile = 256

    def out(n, _):
        cols = pl.ds(pl.multiple_of(n * tile, tile), tile)
        acc = x_in[:, cols].astype(F32)
        for e in range(0, 16, 2):
            pair = jnp.concatenate([att[e], att[e + 1]], axis=1)
            acc = acc + dot(pair, wo[e // 4, pl.ds(e % 4, 2), :, :, cols].reshape(256, tile), ((1,), (0,)))
        residual[:, cols] = acc
        return 0

    lax.fori_loop(0, width // tile, out, 0)
    keep.append(pltpu.make_async_copy(residual, residual_o, ksem.at[5]))
    keep[5].start()
    gc.along(3)
    gc.quads(2)
    gc.cross(2)

    def norm(i, _):
        sl = pl.ds(pl.multiple_of(i * 16, 16), 16)
        v = residual[sl, :]
        r = lax.rsqrt(jnp.mean(v * v, axis=1, keepdims=True) + EPS)
        n2[sl, :] = (v * r * gain[...]).astype(BF)
        return 0

    lax.fori_loop(0, rows // 16, norm, 0)
    landed(mine, msem.at[0])
    landed(part, msem.at[2])
    gc.quads(3)
    gc.cross(3)
    for s in range(4):
        gc.settle(s)
    for one in keep:
        one.wait()
    net.finish()
    netc.finish()


def run_attend(scale, pads, lin, tot, near, far, gq, gk, q_seg, segments, w_own, x_in, gain, cot, cid, cut=96):
    R, D = x_in.shape
    DMA = pltpu.SemaphoreType.DMA
    S = jax.ShapeDtypeStruct
    A = pl.BlockSpec(memory_space=pl.ANY)
    M = pl.BlockSpec(memory_space=pltpu.VMEM)
    V = pltpu.VMEM
    wo = (4, 4, 2, R // 2, D)
    return pl.pallas_call(
        functools.partial(attend_kernel, scale, pads, cut),
        out_shape=(S(wo, BF), S((16, R, 128), BF), S((2, pads + 16, 2, R, 128), BF), S((16, R, 128), BF),
                   S((16, R, 1), F32), S((16, R, 128), BF), S((R, D), F32), S((R, D), BF), S((4, 4) + cot.shape, BF)),
        in_specs=[A] + [M] * 7 + [A, M, M, A],
        out_specs=(A, A, A, A, M, A, A, M, A),
        scratch_shapes=[V((16, R, 384), F32), V((1, (pads + 16) * 2 * R), F32), V((16, R, 128), BF),
                        V((2, pads + 16, 2, R, 128), BF), V((16, R, 128), BF), V((16, R, 128), BF), V((R, D), F32),
                        V(wo, BF), DMA((3,)), DMA((4,)), DMA((4,)), DMA((6,)), DMA((64,)), DMA((64,))] + ag_sems() + ag_sems(),
        compiler_params=pltpu.CompilerParams(collective_id=cid, has_side_effects=True, vmem_limit_bytes=63 * 2**20),
        name="attend",
    )(lin, tot, near, far, gq, gk, q_seg, segments, w_own, x_in, gain, cot)


def attend_back_kernel(scale, pads, cut, d_n2, cot, gain, wo_h, p_out, residual, q_rot, kv, q_seg, segments, lse, o_ref, lin, tot, near, far, gq, gk,
                       d_lin, d_gains, output, d_residual, d_gain, d_res, k_seg, P, wo, d_mine, d_out, d_q, d_k, d_v, other, got, d_un, sums, sums_all, inner,
                       lsem, msem, ssem, *bufs):
    net = Net(ssem)
    sc = Scatter(net, cut, P, bufs)
    u, z, c = net.u, net.z, net.c
    me = u * 4 + z
    rows, width = d_n2.shape
    reach = pads * 2 * rows
    partner = (u, z, 1 - c)
    load = pltpu.make_async_copy(wo_h, wo, lsem.at[0])
    load.start()
    load_p = pltpu.make_async_copy(p_out, P, lsem.at[1])
    load_p.start()
    greet(net)

    def go(words):
        run_steps(steps_of(sc, words))

    load_p.wait()
    go("m3 m0 m2 m1")
    d_gain[...] = jnp.zeros_like(d_gain)

    def norm_back(i, _):
        sl = pl.ds(pl.multiple_of(i * 16, 16), 16)
        v, d = residual[sl, :], d_n2[sl, :]
        r = lax.rsqrt(jnp.mean(v * v, axis=1, keepdims=True) + EPS)
        scaled = d * gain[...]
        mean = jnp.mean(scaled * v, axis=1, keepdims=True)
        total = wide(cot[sl, :]) + r * scaled - v * (r * r * r * mean)
        d_residual[sl, :] = total
        d_res[sl, :] = total.astype(BF)
        d_gain[...] += jnp.sum(d * v * r, axis=0, keepdims=True)
        return 0

    lax.fori_loop(0, rows // 16, norm_back, 0)
    segment_rows(segments, k_seg, reach)
    load.wait()

    def send(j, _):
        pair = lax.rem(me // 2 + 1 + j, 8)
        both = dot(d_res[...], wo[pair // 2, pl.ds(lax.rem(pair, 2) * 2, 2)].reshape(256, width), ((1,), (1,))).astype(BF)
        for i in (0, 1):
            e = pair * 2 + i
            d_mine[e] = both[:, i * 128 : (i + 1) * 128]

            @pl.when(e != me)
            def _():
                remote(d_mine.at[e], d_out.at[me], msem.at[0], msem.at[1], (e // 4, lax.rem(e, 4), c)).start()

        return 0

    lax.fori_loop(0, 8, send, 0)
    d_out[me] = d_mine[me]
    d_k[...] = jnp.zeros_like(d_k)
    d_v[...] = jnp.zeros_like(d_v)
    landed(d_out.at[pl.ds(0, 15)], msem.at[1])
    count = (pads + 16) * 2 * rows

    def block(i, _):
        band = pl.ds(pl.multiple_of((2 * i + c) * rows, rows), rows + reach)
        kf, vf = kv.at[0].reshape(count, 128), kv.at[1].reshape(count, 128)
        q, k, dd = q_rot[i], kf[band, :], d_out[i]
        scores, allowed = band_scores(q, k, column(q_seg[pl.ds(i, 1), :])[:, 0:1], k_seg[:, band], scale, reach)
        probs = jnp.where(allowed, jnp.exp(scores - lse[i]), 0.0)
        d_probs = dot(dd, vf[band, :], ((1,), (1,)))
        delta = jnp.sum(dd.astype(F32) * o_ref[i].astype(F32), axis=1, keepdims=True)
        d_scores = (probs * (d_probs - delta)).astype(BF)
        d_q[i] = (dot(d_scores, k, ((1,), (0,))) * scale).astype(BF)
        d_k[band, :] += dot(d_scores, q, ((0,), (0,))) * scale
        d_v[band, :] += dot(probs.astype(BF), dd, ((0,), (0,)))
        return 0

    def store(sl, v):
        output[sl, :] = residual[sl, :] + v

    go("f3 f0 d3 d0")
    done = 0
    for upto, words in ((3, "M3 M0 M2 M1 d2 d1"), (6, "f2 f1"), (11, "b31 b02"), (16, "")):
        lax.fori_loop(done, upto, block, 0)
        go(words)
        done = upto

    def pack(i, _):
        at = pl.ds(pl.multiple_of(((pads + i) * 2 + 1 - c) * rows, rows), rows)
        other[0, i] = d_k[at, :].astype(BF)
        other[1, i] = d_v[at, :].astype(BF)
        return 0

    lax.fori_loop(0, 16, pack, 0)
    remote(other, got, msem.at[2], msem.at[3], partner).start()
    go("h30 h03")
    landed(got, msem.at[3])
    d_gains[...] = jnp.zeros_like(d_gains)

    def undo(i, _):
        at = pl.ds(pl.multiple_of(((pads + i) * 2 + c) * rows, rows), rows)
        cs, sn = rope_at(near, far, i)
        both = lin[i]
        rq = lax.rsqrt(column(tot[pl.ds(i, 1), :]) / width + EPS)
        rk = lax.rsqrt(column(tot[pl.ds(16 + i, 1), :]) / width + EPS)
        dk = (d_k[at, :] + wide(got[0, i])).astype(BF).astype(F32)
        d_lin[i, :, 256:] = (d_v[at, :] + wide(got[1, i])).astype(BF)
        uq = turned_back(wide(d_q[i]), cs, sn)
        uk = turned_back(dk, cs, sn)
        q, k = both[:, :128], both[:, 128:256]
        d_gains[0:1, :] += jnp.sum(uq * q * rq, axis=0, keepdims=True)
        d_gains[1:2, :] += jnp.sum(uk * k * rk, axis=0, keepdims=True)
        uq, uk = uq * gq[...], uk * gk[...]
        d_un[0, i] = uq
        d_un[1, i] = uk
        sums[pl.ds(i, 1), :] = row_sums(uq * q)
        sums[pl.ds(16 + i, 1), :] = row_sums(uk * k)
        return 0

    lax.fori_loop(0, 16, undo, 0)
    go("b21 b12 b32 b01")
    share_sums(net, sums, sums_all, inner, lsem.at[1], msem.at[4], msem.at[5])

    def finish(i, _):
        both = lin[i]
        for s in (0, 1):
            r = lax.rsqrt(column(tot[pl.ds(16 * s + i, 1), :]) / width + EPS)
            mean = column(inner[pl.ds(16 * s + i, 1), :]) / width
            own = both[:, 128 * s : 128 * (s + 1)]
            d_lin[i, :, 128 * s : 128 * (s + 1)] = (r * d_un[s, i] - own * (r * r * r * mean)).astype(BF)
        return 0

    lax.fori_loop(0, 16, finish, 0)
    go("h31 h02 h20 h13 Q h32 h01 h10 h23 h21 h12 q")
    sc.last(store)
    landed(d_out.at[pl.ds(0, 15)], msem.at[0])
    landed(other, msem.at[2])
    net.finish()


def run_attend_back(scale, pads, d_n2, cot, gain, wo, p_out, residual, q_rot, kv, q_seg, segments, lse, o, lin, tot, near, far, gq, gk, cid, cut=96):
    R, D = d_n2.shape
    DMA = pltpu.SemaphoreType.DMA
    S = jax.ShapeDtypeStruct
    A = pl.BlockSpec(memory_space=pl.ANY)
    M = pl.BlockSpec(memory_space=pltpu.VMEM)
    V = pltpu.VMEM
    span = (pads + 16) * 2 * R
    return pl.pallas_call(
        functools.partial(attend_back_kernel, scale, pads, cut),
        out_shape=(S((16, R, 384), BF), S((8, 128), F32), S((R, D), F32), S((R, D), F32), S((1, D), F32)),
        in_specs=[M, M, M, A, A] + [M] * 13,
        out_specs=(M,) * 5,
        scratch_shapes=[V((R, D), BF), V((1, span), F32), V((4, 4, R, D), BF), V(wo.shape, BF), V((16, R, 128), BF), V((16, R, 128), BF), V((16, R, 128), BF),
                        V((span, 128), F32), V((span, 128), F32), V((2, 16, R, 128), BF), V((2, 16, R, 128), BF),
                        V((2, 16, R, 128), F32), V((32, 128), F32), V((16, 32, 128), F32), V((32, 128), F32),
                        DMA((2,)), DMA((10,)), DMA((64,))] + rs_scratch(cut, R, D),
        compiler_params=pltpu.CompilerParams(collective_id=cid, has_side_effects=True, vmem_limit_bytes=63 * 2**20),
        name="attend_back",
    )(d_n2, cot, gain, wo, p_out, residual, q_rot, kv, q_seg, segments, lse, o, lin, tot, near, far, gq, gk)
def dot(a, b, dims):
    return lax.dot_general(a, b, (dims, ((), ())), preferred_element_type=jnp.float32)


def local_chip(
    inputs, cotangent, segments, expert_ids, gate_weights, fill_order, norm1_gain, w_query, w_key,
    w_value, w_output, query_gain, key_gain, norm2_gain, expert_gate, expert_up, expert_down,
):
    chips = 16
    devices = 2 * chips
    rows, width = inputs.shape
    u, z, core = place()
    chip = u * 4 + z
    device = chip * 2 + core
    topk = expert_ids.shape[1]
    experts_n = chips
    capacity = 9 * rows * devices * topk // (8 * experts_n)
    one_hot = expert_ids[:, :, None] == jnp.arange(experts_n, dtype=jnp.int32)[None, None, :]
    chosen = jnp.any(one_hot, axis=1)
    weight = jnp.sum(jnp.where(one_hot, gate_weights[:, :, None], 0.0), axis=1)
    earlier = (fill_order[None, :] < fill_order[:, None]).astype(jnp.bfloat16)
    rank = dot(earlier, chosen.astype(jnp.bfloat16), ((1,), (0,)))
    rank = jnp.where(chosen, rank, -1.0)
    gains = jnp.stack([norm1_gain, query_gain, key_gain, norm2_gain]).astype(F32)
    blank = jnp.zeros_like(gains)
    gains = jnp.where(core == 0, jnp.concatenate([gains, blank], axis=1), jnp.concatenate([blank, gains], axis=1))
    gains = jnp.broadcast_to(gains[None], (chips, 4, 128))
    block = jnp.concatenate(
        [weight.T[:, None, :], rank.T[:, None, :], gains, jnp.zeros((chips, 2, 128), F32)], axis=1)
    side = width // 2
    n1_rows, lin, w_qkv, squares, swapped, cot_a = run_qkv(
        inputs, w_query, w_key, w_value, block, cotangent[:, :side], 2)
    gains = jnp.sum(swapped.reshape(chips, 2, 8, 128), axis=1)
    gain_one, gain_two = gains[:, 2].reshape(1, width), gains[:, 5].reshape(1, width)
    gq, gk = (lax.dynamic_slice_in_dim(gains[:, i], chip, 1, 0) for i in (3, 4))
    rank_all = swapped[:, 1, :]
    taken = rank_all >= 0.0
    counts = jnp.sum(taken.astype(F32), axis=1)
    before = jnp.cumsum(counts) - counts
    kept = taken & (before[:, None] + rank_all < float(capacity))
    share = jnp.where(kept, swapped[:, 0, :], 0.0).reshape(chips, 2, rows)
    share = lax.dynamic_index_in_dim(share, core, 1, keepdims=False)


    half_dim = HEAD_DIM // 2
    inv_freq = jnp.exp(jnp.arange(half_dim, dtype=F32) * (-2.0 * math.log(ROPE_BASE) / HEAD_DIM))
    inv_freq = jnp.concatenate([inv_freq, inv_freq])[None, :]
    sign = jnp.where(jnp.arange(HEAD_DIM) < half_dim, -1.0, 1.0)[None, :]
    within = jnp.arange(rows, dtype=F32)[:, None] * inv_freq
    starts = ((jnp.arange(chips, dtype=jnp.int32) * 2 + core) * rows).astype(F32)[:, None] * inv_freq
    near = jnp.stack([jnp.cos(within), sign * jnp.sin(within)])
    far = jnp.stack([jnp.cos(starts), sign * jnp.sin(starts)])
    pads = chips // 4
    marks = segments.astype(F32)
    q_seg = lax.dynamic_index_in_dim(marks.reshape(chips, 2, rows), core, 1, keepdims=False)
    marks = marks.reshape(1, -1)
    scale = 1.0 / math.sqrt(HEAD_DIM)
    tokens = chips * rows
    w_o, q_rot, kv, head_out, log_total, attended, residual, normed_two, cot_b = run_attend(
        scale, pads, lin, squares, near, far, gq, gk, q_seg, marks, w_output, inputs, gain_two, cotangent[:, side:], 4)

    d_normed_two, mixed, _n2, _other, d_expert_gate, d_expert_up, d_expert_down = run_expert(
        normed_two, cot_a, cot_b, share, expert_gate, expert_up, expert_down, 6)
    d_lin, d_qk_gains, output, d_residual, d_gain_two = run_attend_back(
        scale, pads, d_normed_two, cotangent, gain_two, w_o, mixed, residual, q_rot, kv, q_seg, marks, log_total, head_out,
        lin, squares, near, far, gq, gk, 7)
    d_w_output, d_inputs, d_w_query, d_w_key, d_w_value, d_gains = run_finish(
        d_lin, w_qkv, n1_rows, attended, inputs, d_residual, gain_one, d_gain_two, d_qk_gains, 8)
    return (
        output,
        d_inputs,
        d_gains[0],
        d_w_query,
        d_w_key,
        d_w_value,
        d_w_output,
        d_gains[2],
        d_gains[3],
        d_gains[1],
        d_expert_gate,
        d_expert_up,
        d_expert_down,
    )
def whole(mesh, step, rows):
    return jax.shard_map(
        step,
        mesh=mesh,
        in_specs=(
            P(rows, None),
            P(rows, None),
            P(),
            P(rows, None),
            P(rows, None),
            P(rows),
            P(rows),
            P(rows, None),
            P(rows, None),
            P(rows, None),
            P(rows, None),
            P(rows),
            P(rows),
            P(rows),
            P(rows, None),
            P(rows, None),
            P(rows, None),
        ),
        out_specs=(
            P(rows, None),
            P(rows, None),
            P(rows),
            P(rows, None),
            P(rows, None),
            P(rows, None),
            P(rows, None),
            P(rows),
            P(rows),
            P(rows),
            P(rows, None),
            P(rows, None),
            P(rows, None),
        ),
        check_vma=False,
    )


def solution(mesh):
    groups, blk_size = mesh.shape["ulysses"], mesh.shape["blk"]

    def step(*args):
        if groups != 4 or blk_size != 8 or args[7].shape[1] // HEAD_DIM != groups * blk_size // 2:
            return whole(mesh, local, ("ulysses", "blk"))(*args)
        chips = Mesh(mesh.devices.reshape(groups, blk_size // 2, 2), ("ulysses", "z", "core"))
        return whole(chips, local_chip, ("ulysses", "z", "core"))(*args)

    return step
```

```python
import functools
import math

import jax
import jax.numpy as jnp
from jax import lax
from jax.experimental import pallas as pl
from jax.experimental.pallas import tpu as pltpu
from jax.sharding import Mesh
from jax.sharding import PartitionSpec as P

HEAD_DIM = 128


EPS = 1e-05
ROPE_BASE = 10000.0
NEG = -1e30


def as_sent(value):

    def short(part):
        return part.astype(jnp.bfloat16) if part.dtype == jnp.float32 else part

    return jax.tree.map(short, value)


def passed_along(block, axis, distance):
    devices = range(lax.axis_size(axis))
    route = [((i - distance) % len(devices), i) for i in devices]
    return lax.ppermute(block, axis, route)


def prefix(value, axis, join, neutral):
    count, mine = (lax.axis_size(axis), lax.axis_index(axis))
    pieces = lax.all_gather(value, axis)
    subtotal = jnp.full_like(value, 0) + jnp.asarray(neutral, value.dtype)

    def hop(position, subtotal):
        longer = join(subtotal, pieces[position])
        return jnp.where(position < mine, longer, subtotal)

    return lax.fori_loop(0, count - 1, hop, subtotal)


def partner_2(block, axis, bit):
    count = lax.axis_size(axis)
    route = []
    for low in range(count):
        high = low | 1 << bit
        if high != low and high < count:
            route += [(low, high), (high, low)]
    return lax.ppermute(block, axis, route)


def norm_rows(values, gain_vec):
    return values * lax.rsqrt(jnp.mean(values * values, axis=-1, keepdims=True) + EPS) * gain_vec


def rotate(values, positions):
    half_dim = HEAD_DIM // 2
    heads_here = values.shape[1] // HEAD_DIM
    inv_freq = jnp.exp(
        jnp.arange(half_dim, dtype=jnp.float32) * (-2.0 * math.log(ROPE_BASE) / HEAD_DIM)
    )
    angles = positions.astype(jnp.float32)[:, None] * inv_freq[None, :]
    cosine = jnp.cos(angles)[:, None, :]
    sin_t = jnp.sin(angles)[:, None, :]
    shaped = values.reshape(values.shape[0], heads_here, HEAD_DIM)
    lower_half = shaped[..., :half_dim]
    upper_half = shaped[..., half_dim:]
    turned = jnp.concatenate(
        [lower_half * cosine - upper_half * sin_t, upper_half * cosine + lower_half * sin_t],
        axis=-1,
    )
    return turned.reshape(values.shape)


def attn_inputs(q_lin, k_lin, gain_q, gain_k, positions):
    return (
        rotate(norm_rows(q_lin, gain_q), positions),
        rotate(norm_rows(k_lin, gain_k), positions),
    )


def banded(shaped, fill_value):
    earlier = jnp.concatenate([jnp.full_like(shaped[:1], fill_value), shaped[:-1]], axis=0)
    return jnp.concatenate([earlier, shaped], axis=1)


def unbanded(band, local_rows):
    earlier = band[:, :local_rows]
    own_part = band[:, local_rows:]
    moved_up = jnp.concatenate([earlier[1:], jnp.zeros_like(earlier[:1])], axis=0)
    return own_part + moved_up


def add_counts(earlier, later):
    return earlier + later


def expert_move(buffer):
    return lax.all_to_all(buffer, ("ulysses", "blk"), split_axis=0, concat_axis=0, tiled=True)


def to_head_layout(values):
    return jax.tree.map(
        lambda part, own: part.astype(own.dtype),
        lax.all_to_all(as_sent(values), "ulysses", split_axis=1, concat_axis=0, tiled=True),
        values,
    )


def to_token_layout(values):
    return jax.tree.map(
        lambda part, own: part.astype(own.dtype),
        lax.all_to_all(as_sent(values), "ulysses", split_axis=0, concat_axis=1, tiled=True),
        values,
    )


def local(
    inputs,
    cotangent,
    segments,
    expert_ids,
    gate_weights,
    fill_order,
    norm1_gain,
    w_query,
    w_key,
    w_value,
    w_output,
    query_gain,
    key_gain,
    norm2_gain,
    expert_gate,
    expert_up,
    expert_down,
):
    blk_size = lax.axis_size("blk")
    groups = lax.axis_size("ulysses")
    devices = blk_size * groups
    local_rows = inputs.shape[0]
    model_width = inputs.shape[1]
    blk_index = lax.axis_index("blk")
    group_index = lax.axis_index("ulysses")
    device_index = group_index * blk_size + blk_index
    positions = device_index * local_rows + jnp.arange(local_rows, dtype=jnp.int32)
    heads_dev = model_width // groups // HEAD_DIM
    score_scale = 1.0 / math.sqrt(HEAD_DIM)
    layer_in = inputs.astype(jnp.float32)
    dense = (w_query, w_key, w_value, w_output, norm1_gain, query_gain, key_gain, norm2_gain)
    gathered = (
        lax.all_gather(dense[0], ("ulysses", "blk"), axis=0, tiled=True),
        lax.all_gather(dense[1], ("ulysses", "blk"), axis=0, tiled=True),
        lax.all_gather(dense[2], ("ulysses", "blk"), axis=0, tiled=True),
        lax.all_gather(dense[3], ("ulysses", "blk"), axis=0, tiled=True),
        lax.all_gather(dense[4], ("ulysses", "blk"), axis=0, tiled=True),
        lax.all_gather(dense[5], ("ulysses", "blk"), axis=0, tiled=True),
        lax.all_gather(dense[6], ("ulysses", "blk"), axis=0, tiled=True),
        lax.all_gather(dense[7], ("ulysses", "blk"), axis=0, tiled=True),
    )
    w_q, w_k, w_v, w_o = (gathered[0], gathered[1], gathered[2], gathered[3])
    gain_one = gathered[4].astype(jnp.float32)
    gain_q = gathered[5].astype(jnp.float32)
    gain_k = gathered[6].astype(jnp.float32)
    gain_two = gathered[7].astype(jnp.float32)
    normed_one = norm_rows(layer_in, gain_one).astype(jnp.bfloat16)
    q_lin = jnp.dot(normed_one, w_q, preferred_element_type=jnp.float32)
    k_lin = jnp.dot(normed_one, w_k, preferred_element_type=jnp.float32)
    v_lin = jnp.dot(normed_one, w_v, preferred_element_type=jnp.float32)
    (q_rot, k_rot), pre_back = jax.vjp(
        lambda q_in, k_in, gq_in, gk_in: attn_inputs(q_in, k_in, gq_in, gk_in, positions),
        q_lin,
        k_lin,
        gain_q,
        gain_k,
    )
    q_heads, k_heads, v_heads = to_head_layout(
        (q_rot.astype(jnp.bfloat16), k_rot.astype(jnp.bfloat16), v_lin.astype(jnp.bfloat16))
    )
    group_ids = jnp.arange(groups, dtype=jnp.int32)[:, None]
    row_ids = jnp.arange(local_rows, dtype=jnp.int32)[None, :]
    q_pos = (group_ids * blk_size + blk_index) * local_rows + row_ids
    q_seg = segments[q_pos]
    four_shape = (groups, local_rows, heads_dev, HEAD_DIM)
    q_four = q_heads.reshape(four_shape)

    def score_block(k_now, source):
        k_pos = (group_ids * blk_size + source) * local_rows + row_ids
        k_seg = banded(segments[k_pos], -1)
        k_pos = banded(k_pos, 0)
        k_band = banded(k_now.reshape(four_shape), 0)
        raw_scores = (
            jnp.einsum("gqhd,gkhd->gqhk", q_four, k_band, preferred_element_type=jnp.float32)
            * score_scale
        )
        allowed = (k_seg[:, None, :] == q_seg[:, :, None]) & (
            k_pos[:, None, :] <= q_pos[:, :, None]
        )
        return (raw_scores, allowed[:, :, None, :], k_band)

    def forward_step(flash_state, kv_stack, step_id):
        run_max, run_sum, run_out = flash_state
        source = jnp.mod(blk_index - step_id, blk_size)
        raw_scores, allowed, k_band = score_block(kv_stack[0], source)
        raw_scores = jnp.where(allowed, raw_scores, NEG)
        new_max = jnp.maximum(run_max, jnp.max(raw_scores, axis=-1))
        shrink = jnp.exp(run_max - new_max)
        weights = jnp.where(allowed, jnp.exp(raw_scores - new_max[..., None]), 0.0)
        run_sum = run_sum * shrink + jnp.sum(weights, axis=-1)
        v_band = banded(kv_stack[1].reshape(four_shape), 0)
        run_out = run_out * shrink[..., None] + jnp.einsum(
            "gqhk,gkhd->gqhd",
            weights.astype(jnp.bfloat16),
            v_band,
            preferred_element_type=jnp.float32,
        )
        return (new_max, run_sum, run_out)

    start_state = (
        jnp.full((groups, local_rows, heads_dev), NEG, jnp.float32),
        jnp.zeros((groups, local_rows, heads_dev), jnp.float32),
        jnp.zeros(four_shape, jnp.float32),
    )
    kv_home = jnp.stack([k_heads, v_heads])
    first_state = forward_step(start_state, kv_home, 0)

    def forward_turn(step_id, loop_state):
        flash_state, kv_stack = loop_state
        moved = passed_along(kv_stack, "blk", 1)
        return (forward_step(flash_state, moved, step_id), moved)

    final_state, unused_kv = lax.fori_loop(1, blk_size, forward_turn, (first_state, kv_home))
    run_max, run_sum, run_out = final_state
    o_four = (run_out / run_sum[..., None]).astype(jnp.bfloat16)
    log_total = run_max + jnp.log(run_sum)
    o_heads = o_four.reshape(groups * local_rows, heads_dev * HEAD_DIM)
    attended = to_token_layout(o_heads)
    residual = layer_in + jnp.dot(attended, w_o, preferred_element_type=jnp.float32)
    normed_two_f, norm_two_back = jax.vjp(norm_rows, residual, gain_two)
    normed_two = normed_two_f.astype(jnp.bfloat16)
    experts_n = devices // 2
    topk = expert_ids.shape[1]
    per_source = 2 * local_rows * topk // experts_n
    half_slots = per_source // 2
    capacity = 9 * local_rows * devices * topk // (8 * experts_n)
    slots_all = experts_n * per_source
    tokens_local = jnp.arange(local_rows, dtype=jnp.int32)
    chosen = jnp.sum(
        (expert_ids[:, :, None] == jnp.arange(experts_n, dtype=jnp.int32)[None, None, :]).astype(
            jnp.int32
        ),
        axis=1,
    )
    by_fill = jnp.zeros((local_rows,), jnp.int32).at[fill_order].set(tokens_local)
    sorted_rows = chosen[by_fill]
    before = jnp.cumsum(sorted_rows, axis=0) - sorted_rows
    rank_all = before[fill_order]
    pair_rank = jnp.take_along_axis(rank_all, expert_ids, axis=1)
    counts = jnp.sum(chosen, axis=0)
    offsets = prefix(counts, ("ulysses", "blk"), add_counts, jnp.zeros_like(counts))
    kept_pair = offsets[expert_ids] + pair_rank < capacity
    pair_slot = expert_ids * per_source + pair_rank
    pair_index = tokens_local[:, None] * topk + jnp.arange(topk, dtype=jnp.int32)[None, :]
    slot_pair = (
        jnp.zeros((slots_all,), jnp.int32).at[pair_slot.reshape(-1)].set(pair_index.reshape(-1))
    )
    slot_live = (
        jnp.zeros((slots_all,), jnp.bool_).at[pair_slot.reshape(-1)].set(kept_pair.reshape(-1))
    )
    slot_token = slot_pair // topk
    send_rows = jnp.where(slot_live[:, None], normed_two[slot_token], jnp.zeros((), jnp.bfloat16))
    received = expert_move(send_rows.reshape(devices, half_slots, model_width)).reshape(
        devices * half_slots, model_width
    )
    parity = jnp.mod(blk_index, 2)
    partner = partner_2((expert_gate, expert_up, expert_down), "blk", 0)

    def joined(own_half, other_half):
        lower_part = jnp.where(parity == 0, own_half, other_half)
        upper_part = jnp.where(parity == 0, other_half, own_half)
        return jnp.concatenate([lower_part, upper_part], axis=0)

    gate_full = joined(expert_gate, partner[0])
    up_full = joined(expert_up, partner[1])
    down_full = joined(expert_down, partner[2])
    gate_pre = jnp.dot(received, gate_full, preferred_element_type=jnp.float32)
    up_pre = jnp.dot(received, up_full, preferred_element_type=jnp.float32)
    hidden = (jax.nn.silu(gate_pre) * up_pre).astype(jnp.bfloat16)
    produced = jnp.dot(hidden, down_full, preferred_element_type=jnp.float32).astype(jnp.bfloat16)
    returned = expert_move(produced.reshape(devices, half_slots, model_width)).reshape(
        slots_all, model_width
    )
    pair_share = jnp.where(kept_pair, gate_weights, 0.0)
    mixed = jnp.einsum("tk,tkd->td", pair_share, returned[pair_slot].astype(jnp.float32))
    output = residual + mixed
    grad_out = cotangent.astype(jnp.float32)
    slot_share = jnp.where(slot_live, gate_weights.reshape(-1)[slot_pair], 0.0)
    grad_send = (slot_share[:, None] * grad_out[slot_token]).astype(jnp.bfloat16)
    grad_rows = expert_move(grad_send.reshape(devices, half_slots, model_width)).reshape(
        devices * half_slots, model_width
    )
    d_down_full = jnp.einsum("rf,rd->fd", hidden, grad_rows, preferred_element_type=jnp.float32)
    d_hidden = jnp.einsum("rd,fd->rf", grad_rows, down_full, preferred_element_type=jnp.float32)
    sigma = jax.nn.sigmoid(gate_pre)
    d_gate_pre = (d_hidden * up_pre * sigma * (1.0 + gate_pre * (1.0 - sigma))).astype(jnp.bfloat16)
    d_up_pre = (d_hidden * gate_pre * sigma).astype(jnp.bfloat16)
    d_gate_full = jnp.einsum("rd,rf->df", received, d_gate_pre, preferred_element_type=jnp.float32)
    d_up_full = jnp.einsum("rd,rf->df", received, d_up_pre, preferred_element_type=jnp.float32)
    d_pair_rows = (
        jnp.einsum("rf,df->rd", d_gate_pre, gate_full, preferred_element_type=jnp.float32)
        + jnp.einsum("rf,df->rd", d_up_pre, up_full, preferred_element_type=jnp.float32)
    ).astype(jnp.bfloat16)
    back_rows = expert_move(d_pair_rows.reshape(devices, half_slots, model_width)).reshape(
        slots_all, model_width
    )
    d_normed_two = jnp.sum(
        jnp.where(kept_pair[:, :, None], back_rows[pair_slot].astype(jnp.float32), 0.0), axis=1
    )
    half_rows = expert_gate.shape[0]
    half_hidden = expert_down.shape[0]

    def halves(full_grad, size):
        own_half = lax.dynamic_slice_in_dim(full_grad, parity * size, size, 0)
        other_half = lax.dynamic_slice_in_dim(full_grad, (1 - parity) * size, size, 0)
        return (own_half, other_half)

    gate_own, gate_other = halves(d_gate_full, half_rows)
    up_own, up_other = halves(d_up_full, half_rows)
    down_own, down_other = halves(d_down_full, half_hidden)
    partner_grads = (
        partner_2(gate_other.astype(jnp.bfloat16), "blk", 0).astype(gate_other.dtype),
        partner_2(up_other.astype(jnp.bfloat16), "blk", 0).astype(up_other.dtype),
        partner_2(down_other.astype(jnp.bfloat16), "blk", 0).astype(down_other.dtype),
    )
    d_expert_gate = gate_own + partner_grads[0]
    d_expert_up = up_own + partner_grads[1]
    d_expert_down = down_own + partner_grads[2]
    d_resid_norm, d_gain_two = norm_two_back(d_normed_two)
    d_residual = grad_out + d_resid_norm
    d_res_low = d_residual.astype(jnp.bfloat16)
    d_attended = jnp.einsum("te,de->td", d_res_low, w_o, preferred_element_type=jnp.float32).astype(
        jnp.bfloat16
    )
    d_o_heads = to_head_layout(d_attended)
    d_o_four = d_o_heads.reshape(four_shape)
    row_delta = jnp.sum(d_o_four.astype(jnp.float32) * o_four.astype(jnp.float32), axis=-1)

    def back_turn(step_id, loop_state):
        moving, dq_acc = loop_state
        source = jnp.mod(blk_index - step_id, blk_size)
        k_now = moving[0].astype(jnp.bfloat16)
        v_now = moving[1].astype(jnp.bfloat16)
        raw_scores, allowed, k_band = score_block(k_now, source)
        prob_rows = jnp.where(allowed, jnp.exp(raw_scores - log_total[..., None]), 0.0)
        v_band = banded(v_now.reshape(four_shape), 0)
        d_probs = jnp.einsum(
            "gqhd,gkhd->gqhk", d_o_four, v_band, preferred_element_type=jnp.float32
        )
        d_scores = (prob_rows * (d_probs - row_delta[..., None])).astype(jnp.bfloat16)
        dv_band = jnp.einsum(
            "gqhk,gqhd->gkhd",
            prob_rows.astype(jnp.bfloat16),
            d_o_four,
            preferred_element_type=jnp.float32,
        )
        dk_band = (
            jnp.einsum("gqhk,gqhd->gkhd", d_scores, q_four, preferred_element_type=jnp.float32)
            * score_scale
        )
        dq_acc = (
            dq_acc
            + jnp.einsum("gqhk,gkhd->gqhd", d_scores, k_band, preferred_element_type=jnp.float32)
            * score_scale
        )
        flat_shape = moving[2].shape
        dk_new = moving[2] + unbanded(dk_band, local_rows).reshape(flat_shape)
        dv_new = moving[3] + unbanded(dv_band, local_rows).reshape(flat_shape)
        moving = passed_along(
            jnp.stack([moving[0], moving[1], dk_new, dv_new]).astype(jnp.bfloat16), "blk", 1
        ).astype(jnp.float32)
        return (moving, dq_acc)

    zero_rows = jnp.zeros(k_heads.shape, jnp.float32)
    start_moving = jnp.stack(
        [k_heads.astype(jnp.float32), v_heads.astype(jnp.float32), zero_rows, zero_rows]
    )
    moving, dq_acc = lax.fori_loop(
        0, blk_size, back_turn, (start_moving, jnp.zeros(four_shape, jnp.float32))
    )
    d_q_send = dq_acc.astype(jnp.bfloat16).reshape(k_heads.shape)
    d_k_send = moving[2].astype(jnp.bfloat16)
    d_v_send = moving[3].astype(jnp.bfloat16)
    d_q_rot, d_k_rot, d_v_lin = to_token_layout((d_q_send, d_k_send, d_v_send))
    d_q_lin, d_k_lin, d_gain_q, d_gain_k = pre_back(
        (d_q_rot.astype(jnp.float32), d_k_rot.astype(jnp.float32))
    )
    d_q_low = d_q_lin.astype(jnp.bfloat16)
    d_k_low = d_k_lin.astype(jnp.bfloat16)
    d_normed_one = jnp.einsum("te,de->td", d_q_low, w_q, preferred_element_type=jnp.float32)
    d_normed_one = d_normed_one + jnp.einsum(
        "te,de->td", d_k_low, w_k, preferred_element_type=jnp.float32
    )
    d_normed_one = d_normed_one + jnp.einsum(
        "te,de->td", d_v_lin, w_v, preferred_element_type=jnp.float32
    )
    unused_norm, norm_one_back = jax.vjp(norm_rows, layer_in, gain_one)
    d_layer_in, d_gain_one = norm_one_back(d_normed_one)
    d_inputs = d_residual + d_layer_in
    d_qk_heads = to_head_layout((d_q_low, d_k_low))
    rows_all = (
        lax.all_gather(normed_one, "ulysses", axis=0, tiled=True),
        lax.all_gather(d_res_low, "ulysses", axis=0, tiled=True),
    )
    head_cols = model_width // groups
    piece_rows = model_width // devices

    def by_owner(part):
        rest = part.shape[1:]
        shaped = part.reshape((groups, blk_size, piece_rows) + rest)
        return jnp.swapaxes(shaped, 0, 1).reshape((model_width,) + rest)

    part_q = jnp.einsum("td,te->de", rows_all[0], d_qk_heads[0], preferred_element_type=jnp.float32)
    part_k = jnp.einsum("td,te->de", rows_all[0], d_qk_heads[1], preferred_element_type=jnp.float32)
    part_v = jnp.einsum("td,te->de", rows_all[0], d_v_send, preferred_element_type=jnp.float32)
    part_o = jnp.einsum("te,td->ed", o_heads, rows_all[1], preferred_element_type=jnp.float32)
    blk_sums = (
        lax.psum_scatter(
            by_owner(part_q).astype(jnp.bfloat16), "blk", scatter_dimension=0, tiled=True
        ).astype(jnp.float32),
        lax.psum_scatter(
            by_owner(part_k).astype(jnp.bfloat16), "blk", scatter_dimension=0, tiled=True
        ).astype(jnp.float32),
        lax.psum_scatter(
            by_owner(part_v).astype(jnp.bfloat16), "blk", scatter_dimension=0, tiled=True
        ).astype(jnp.float32),
        lax.psum_scatter(
            part_o.astype(jnp.bfloat16), "blk", scatter_dimension=0, tiled=True
        ).astype(jnp.float32),
        lax.psum_scatter(
            by_owner(d_gain_one).astype(jnp.bfloat16), "blk", scatter_dimension=0, tiled=True
        ).astype(jnp.float32),
        lax.psum_scatter(
            by_owner(d_gain_q).astype(jnp.bfloat16), "blk", scatter_dimension=0, tiled=True
        ).astype(jnp.float32),
        lax.psum_scatter(
            by_owner(d_gain_k).astype(jnp.bfloat16), "blk", scatter_dimension=0, tiled=True
        ).astype(jnp.float32),
        lax.psum_scatter(
            by_owner(d_gain_two).astype(jnp.bfloat16), "blk", scatter_dimension=0, tiled=True
        ).astype(jnp.float32),
    )

    def widened(part):
        return lax.dynamic_update_slice_in_dim(
            jnp.zeros((part.shape[0], model_width), jnp.float32), part, group_index * head_cols, 1
        )

    col_sums = (
        lax.psum_scatter(
            widened(blk_sums[0]).astype(jnp.bfloat16), "ulysses", scatter_dimension=0, tiled=True
        ).astype(jnp.float32),
        lax.psum_scatter(
            widened(blk_sums[1]).astype(jnp.bfloat16), "ulysses", scatter_dimension=0, tiled=True
        ).astype(jnp.float32),
        lax.psum_scatter(
            widened(blk_sums[2]).astype(jnp.bfloat16), "ulysses", scatter_dimension=0, tiled=True
        ).astype(jnp.float32),
        lax.psum_scatter(
            blk_sums[4].astype(jnp.bfloat16), "ulysses", scatter_dimension=0, tiled=True
        ).astype(jnp.float32),
        lax.psum_scatter(
            blk_sums[5].astype(jnp.bfloat16), "ulysses", scatter_dimension=0, tiled=True
        ).astype(jnp.float32),
        lax.psum_scatter(
            blk_sums[6].astype(jnp.bfloat16), "ulysses", scatter_dimension=0, tiled=True
        ).astype(jnp.float32),
        lax.psum_scatter(
            blk_sums[7].astype(jnp.bfloat16), "ulysses", scatter_dimension=0, tiled=True
        ).astype(jnp.float32),
    )
    result_grads = (
        col_sums[0],
        col_sums[1],
        col_sums[2],
        blk_sums[3],
        col_sums[3],
        col_sums[4],
        col_sums[5],
        col_sums[6],
    )
    return (
        output,
        d_inputs,
        result_grads[4],
        result_grads[0],
        result_grads[1],
        result_grads[2],
        result_grads[3],
        result_grads[5],
        result_grads[6],
        result_grads[7],
        d_expert_gate,
        d_expert_up,
        d_expert_down,
    )


MESH = pl.DeviceIdType.MESH
P1 = 96

def place():
    u = lax.axis_index("ulysses"); z = lax.axis_index("z"); c = lax.axis_index("core")
    return u, z, c

def ag_kernel(cut, x_ref, o_ref, local_sem, s_sem, zr, xr, yr, d1r, d2r, bs, br, bzr):
    u, z, c = place()
    Z = 4
    R = x_ref.shape[0]
    ux, uy = u ^ 1, u ^ 2
    xn, yn, up, dn = (ux, z, c), (uy, z, c), (u, z + 1, c), (u, z - 1, c)
    has_up, has_dn = z < Z - 1, z > 0
    bar = pltpu.get_barrier_semaphore()
    for n in (xn, yn):
        pl.semaphore_signal(bar, inc=1, device_id=n, device_id_type=MESH)
    @pl.when(has_up)
    def _():
        pl.semaphore_signal(bar, inc=1, device_id=up, device_id_type=MESH)
    @pl.when(has_dn)
    def _():
        pl.semaphore_signal(bar, inc=1, device_id=dn, device_id_type=MESH)
    pl.semaphore_wait(bar, 2 + has_up.astype(jnp.int32) + has_dn.astype(jnp.int32))
    sends = []
    def copy(src, dst, ss, rs, dev):
        return pltpu.make_async_remote_copy(src_ref=src, dst_ref=dst, send_sem=ss, recv_sem=rs, device_id=dev, device_id_type=MESH)
    def go(cond, make):
        idx = len(sends)
        def mk():
            return make(s_sem.at[idx])
        sends.append((cond, mk))
        if cond is None:
            mk().start()
        else:
            pl.when(cond)(lambda: mk().start())
    def both(a, b):
        if a is None: return b
        if b is None: return a
        return jnp.logical_and(a, b)
    def wait(cond, ref, sem):
        def w():
            pltpu.make_async_copy(ref, ref, sem).wait()
        if cond is None: w()
        else: pl.when(cond)(w)
    own = pltpu.make_async_copy(x_ref, o_ref.at[u, z], local_sem)
    own.start()
    A = slice(0, cut)
    h = cut // 2
    def oa(uu, zz, lo=0, n=cut):
        return o_ref.at[uu, zz, pl.ds(lo, n), :]
    def spread(s, zz, cond):
        src = (lambda: x_ref.at[pl.ds(0, cut), :]) if s == 0 else (lambda: oa(u, zz))
        go(cond, lambda sm: copy(src(), oa(u, zz), sm, xr.at[zz], xn))
        go(cond, lambda sm: copy(src(), oa(u, zz), sm, yr.at[zz], yn))
    def cross(zz, cond):
        wait(cond, oa(ux, zz), xr.at[zz])
        go(cond, lambda sm: copy(oa(ux, zz, 0, h), oa(ux, zz, 0, h), sm, d1r.at[zz], yn))
        wait(cond, oa(uy, zz), yr.at[zz])
        go(cond, lambda sm: copy(oa(uy, zz, h, h), oa(uy, zz, h, h), sm, d2r.at[zz], xn))
    rb = R - cut
    hb = rb // 2
    def ob(uu, zz, lo=0, n=None):
        return o_ref.at[uu, zz, pl.ds(cut + lo, rb if n is None else n), :]
    go(has_up, lambda sm: copy(x_ref.at[pl.ds(0, cut), :], oa(u, z), sm, zr.at[z], up))
    go(has_dn, lambda sm: copy(x_ref.at[pl.ds(0, cut), :], oa(u, z), sm, zr.at[z], dn))
    if rb:
        go(None, lambda sm: copy(x_ref.at[pl.ds(cut, rb), :], ob(u, z), sm, br.at[0], xn))
        go(None, lambda sm: copy(x_ref.at[pl.ds(cut, rb), :], ob(u, z), sm, br.at[1], yn))
    spread(0, z, None)
    if rb:
        wait(None, ob(ux, z), br.at[0])
        go(None, lambda sm: copy(ob(ux, z, 0, hb), ob(ux, z, 0, hb), sm, br.at[2], yn))
        wait(None, ob(uy, z), br.at[1])
        go(None, lambda sm: copy(ob(uy, z, hb, hb), ob(uy, z, hb, hb), sm, br.at[3], xn))
    own.wait()
    def quad(zz):
        return o_ref.at[:, zz, pl.ds(cut, rb), :]
    def zs(s):
        zl, zh = z - s, z + s
        cl, ch = zl >= 0, zh < Z
        zlc, zhc = jnp.maximum(zl, 0), jnp.minimum(zh, Z - 1)
        return (zlc, cl, has_up, up), (zhc, ch, has_dn, dn)
    prev = [(z, None)]
    for s in range(1, Z):
        cur = []
        for (zz, cond, fwd, dev) in zs(s):
            wait(cond, oa(u, zz), zr.at[zz])
            go(both(cond, fwd), lambda sm, zz=zz, dev=dev: copy(oa(u, zz), oa(u, zz), sm, zr.at[zz], dev))
            spread(s, zz, cond)
            cur.append((zz, cond))
        if rb and s == 1:
            wait(None, ob(u ^ 3, z, 0, hb), br.at[2])
            wait(None, ob(u ^ 3, z, hb, hb), br.at[3])
            go(has_up, lambda sm: copy(quad(z), quad(z), sm, bzr.at[z], up))
            go(has_dn, lambda sm: copy(quad(z), quad(z), sm, bzr.at[z], dn))
        elif rb:
            for (zz, cond, fwd, dev) in zs(s - 1):
                wait(cond, quad(zz), bzr.at[zz])
                go(both(cond, fwd), lambda sm, zz=zz, dev=dev: copy(quad(zz), quad(zz), sm, bzr.at[zz], dev))
        for zz, cond in prev:
            cross(zz, cond)
        prev = cur
    if rb:
        for (zz, cond, fwd, dev) in zs(Z - 1):
            wait(cond, quad(zz), bzr.at[zz])
    for zz, cond in prev:
        cross(zz, cond)
    for zz in range(Z):
        wait(None, oa(u ^ 3, zz, 0, h), d1r.at[zz])
        wait(None, oa(u ^ 3, zz, h, h), d2r.at[zz])
    for cond, mk in sends:
        if cond is None: mk().wait_send()
        else: pl.when(cond)(lambda mk=mk: mk().wait_send())

def ag16(x, cid, cut=P1, space=pl.ANY):
    R, D = x.shape
    DMA = pltpu.SemaphoreType.DMA
    return pl.pallas_call(
        functools.partial(ag_kernel, cut),
        out_shape=jax.ShapeDtypeStruct((4, 4, R, D), x.dtype),
        in_specs=[pl.BlockSpec(memory_space=space)],
        out_specs=pl.BlockSpec(memory_space=space),
        scratch_shapes=[DMA, DMA((64,)), DMA((4,)), DMA((4,)), DMA((4,)), DMA((4,)), DMA((4,)), DMA((4,)), DMA((4,)), DMA((4,))],
        compiler_params=pltpu.CompilerParams(collective_id=cid, has_side_effects=True, vmem_limit_bytes=48 * 2**20),
        name="gather_rows",
    )(x)
F32 = jnp.float32
BF = jnp.bfloat16


class Net:
    def __init__(self, sems):
        self.sems, self.sends = sems, []
        self.u, self.z, self.c = place()
        u, z, c = self.u, self.z, self.c
        self.ux, self.uy, self.ud = u ^ 1, u ^ 2, u ^ 3
        self.xn, self.yn, self.up, self.dn = (u ^ 1, z, c), (u ^ 2, z, c), (u, z + 1, c), (u, z - 1, c)
        self.has_up, self.has_dn = z < 3, z > 0
        self.at = [z == i for i in range(4)]

    def barrier(self, more=()):
        bar = pltpu.get_barrier_semaphore()
        for n in (self.xn, self.yn) + tuple(more):
            pl.semaphore_signal(bar, inc=1, device_id=n, device_id_type=MESH)
        for cond, n in ((self.has_up, self.up), (self.has_dn, self.dn)):
            pl.when(cond)(lambda n=n: pl.semaphore_signal(bar, inc=1, device_id=n, device_id_type=MESH))
        pl.semaphore_wait(bar, 2 + len(more) + self.has_up.astype(jnp.int32) + self.has_dn.astype(jnp.int32))

    def go(self, cond, src, dst, rsem, dev):
        idx = len(self.sends)

        def mk():
            return pltpu.make_async_remote_copy(
                src_ref=src(), dst_ref=dst(), send_sem=self.sems.at[idx], recv_sem=rsem(),
                device_id=dev, device_id_type=MESH)

        self.sends.append((cond, mk))
        if cond is None:
            mk().start()
        else:
            pl.when(cond)(lambda: mk().start())

    def wait(self, cond, ref, sem):
        def w():
            pltpu.make_async_copy(ref(), ref(), sem).wait()

        if cond is None:
            w()
        else:
            pl.when(cond)(w)

    def finish(self):
        for cond, mk in self.sends:
            if cond is None:
                mk().wait_send()
            else:
                pl.when(cond)(lambda mk=mk: mk().wait_send())


def strips(rows, body, step=16):
    def it(i, _):
        body(pl.ds(pl.multiple_of(i * step, step), step))
        return 0

    lax.fori_loop(0, rows // step, it, 0)


def wide(v):
    return v.astype(F32)


class Scatter:
    def __init__(self, net, cut, P, bufs):
        self.net, self.cut, self.P = net, cut, P
        (self.mid1, self.mid2, self.fx, self.fy, self.be, self.ab, self.bbe, self.bab, self.bm,
         self.m1s, self.m2s, self.fxs, self.fys, self.bes, self.abs_, self.bbes, self.babs, self.bms) = bufs
        self.R = P.shape[2]
        self.h = cut // 2
        self.rb = self.R - cut
        self.hb = self.rb // 2

    def mid_send(self, zd):
        net, P, h = self.net, self.P, self.h
        net.go(None, lambda: P.at[net.ud, zd, pl.ds(0, h), :], lambda: self.mid1.at[zd], lambda: self.m1s.at[zd], net.xn)
        net.go(None, lambda: P.at[net.ud, zd, pl.ds(h, h), :], lambda: self.mid2.at[zd], lambda: self.m2s.at[zd], net.yn)

    def bfirst(self, zd):
        net, P, cut, rb = self.net, self.P, self.cut, self.rb
        if rb and zd > 0:
            net.go(net.at[0], lambda: P.at[:, zd, pl.ds(cut, rb), :], lambda: self.bbe.at[zd], lambda: self.bbes.at[zd], net.up)
        if rb and zd < 3:
            net.go(net.at[3], lambda: P.at[:, zd, pl.ds(cut, rb), :], lambda: self.bab.at[zd], lambda: self.babs.at[zd], net.dn)

    def direct(self, zd):
        net, P, h = self.net, self.P, self.h
        net.go(None, lambda: P.at[net.ux, zd, pl.ds(0, h), :], lambda: self.fx.at[zd, pl.ds(0, h), :], lambda: self.fxs.at[zd, 0], net.xn)
        net.go(None, lambda: P.at[net.uy, zd, pl.ds(h, h), :], lambda: self.fy.at[zd, pl.ds(h, h), :], lambda: self.fys.at[zd, 1], net.yn)

    def first(self, zd):
        self.mid_send(zd)
        self.bfirst(zd)
        self.direct(zd)

    def mids(self, zd):
        net, P, h, mid1, mid2 = self.net, self.P, self.h, self.mid1, self.mid2

        def add1(sl):
            mid1[zd, sl, :] = (wide(mid1[zd, sl, :]) + wide(P[net.uy, zd, sl, :])).astype(BF)

        def add2(sl):
            mid2[zd, sl, :] = (wide(mid2[zd, sl, :]) + wide(P[net.ux, zd, pl.ds(h + sl.start, 16), :])).astype(BF)

        net.wait(None, lambda: mid1.at[zd], self.m1s.at[zd])
        strips(h, add1)
        net.go(None, lambda: mid1.at[zd], lambda: self.fy.at[zd, pl.ds(0, h), :], lambda: self.fys.at[zd, 0], net.yn)
        net.wait(None, lambda: mid2.at[zd], self.m2s.at[zd])
        strips(h, add2)
        net.go(None, lambda: mid2.at[zd], lambda: self.fx.at[zd, pl.ds(h, h), :], lambda: self.fxs.at[zd, 1], net.xn)

    def route(self, zd, zz):
        if zz < zd:
            return True, self.net.up
        return False, self.net.dn

    def bhop(self, zd, zz):
        net, P, cut, rb = self.net, self.P, self.cut, self.rb
        if not rb:
            return
        upward, dev = self.route(zd, zz)
        buf, sems = (self.bbe, self.bbes) if upward else (self.bab, self.babs)
        here = net.at[zz]
        net.wait(here, lambda: buf.at[zd], sems.at[zd])

        def add():
            for q in range(4):
                def one(sl, q=q):
                    buf[zd, q, sl, :] = (wide(buf[zd, q, sl, :]) + wide(P[q, zd, pl.ds(cut + sl.start, 16), :])).astype(BF)
                strips(rb, one)

        pl.when(here)(add)
        net.go(here, lambda: buf.at[zd], lambda: buf.at[zd], lambda: sems.at[zd], dev)

    def square(self, zd, cond):
        net, h = self.net, self.h
        for half in (0, 1):
            net.wait(cond, lambda: self.fx.at[zd, pl.ds(half * h, h), :], self.fxs.at[zd, half])
            net.wait(cond, lambda: self.fy.at[zd, pl.ds(half * h, h), :], self.fys.at[zd, half])

    def local(self, zd, sl):
        return wide(self.P[self.net.u, zd, sl, :]) + wide(self.fx[zd, sl, :]) + wide(self.fy[zd, sl, :])

    def hop(self, zd, zz):
        net = self.net
        upward, dev = self.route(zd, zz)
        buf, sems = (self.be, self.bes) if upward else (self.ab, self.abs_)
        here = net.at[zz]
        self.square(zd, here)
        if zz in (0, 3):
            def begin(sl):
                self.fx[zd, sl, :] = self.local(zd, sl).astype(BF)

            pl.when(here)(lambda: strips(self.cut, begin))
            net.go(here, lambda: self.fx.at[zd], lambda: buf.at[zd], lambda: sems.at[zd], dev)
        else:
            def plus(sl):
                buf[zd, sl, :] = (self.local(zd, sl) + wide(buf[zd, sl, :])).astype(BF)

            net.wait(here, lambda: buf.at[zd], sems.at[zd])
            pl.when(here)(lambda: strips(self.cut, plus))
            net.go(here, lambda: buf.at[zd], lambda: buf.at[zd], lambda: sems.at[zd], dev)

    def bquad(self):
        net, P, cut, rb, hb, bm, bms = self.net, self.P, self.cut, self.rb, self.hb, self.bm, self.bms
        if not rb:
            return
        z = net.z
        net.wait(net.has_dn, lambda: self.bbe.at[z], self.bbes.at[z])
        net.wait(net.has_up, lambda: self.bab.at[z], self.babs.at[z])
        for q in range(4):
            def fold(sl, q=q):
                s = wide(P[q, z, pl.ds(cut + sl.start, 16), :])
                s = s + jnp.where(net.has_dn, wide(self.bbe[z, q, sl, :]), 0.0)
                s = s + jnp.where(net.has_up, wide(self.bab[z, q, sl, :]), 0.0)
                bm[q, sl, :] = s.astype(BF)
            strips(rb, fold)
        net.go(None, lambda: bm.at[net.ud, pl.ds(0, hb), :], lambda: bm.at[4, pl.ds(0, hb), :], lambda: bms.at[0], net.xn)
        net.go(None, lambda: bm.at[net.ud, pl.ds(hb, hb), :], lambda: bm.at[5, pl.ds(0, hb), :], lambda: bms.at[1], net.yn)
        net.go(None, lambda: bm.at[net.ux, pl.ds(0, hb), :], lambda: bm.at[6, pl.ds(0, hb), :], lambda: bms.at[2], net.xn)
        net.go(None, lambda: bm.at[net.uy, pl.ds(hb, hb), :], lambda: bm.at[7, pl.ds(hb, hb), :], lambda: bms.at[3], net.yn)

    def bquad2(self):
        net, rb, hb, bm, bms = self.net, self.rb, self.hb, self.bm, self.bms
        if not rb:
            return

        def add4(sl):
            bm[4, sl, :] = (wide(bm[4, sl, :]) + wide(bm[net.uy, sl, :])).astype(BF)

        def add5(sl):
            bm[5, sl, :] = (wide(bm[5, sl, :]) + wide(bm[net.ux, pl.ds(hb + sl.start, 16), :])).astype(BF)

        net.wait(None, lambda: bm.at[4, pl.ds(0, hb), :], bms.at[0])
        strips(hb, add4)
        net.go(None, lambda: bm.at[4, pl.ds(0, hb), :], lambda: bm.at[7, pl.ds(0, hb), :], lambda: bms.at[4], net.yn)
        net.wait(None, lambda: bm.at[5, pl.ds(0, hb), :], bms.at[1])
        strips(hb, add5)
        net.go(None, lambda: bm.at[5, pl.ds(0, hb), :], lambda: bm.at[6, pl.ds(hb, hb), :], lambda: bms.at[5], net.xn)

    def last(self, store):
        net, cut, rb, hb, bm, bms = self.net, self.cut, self.rb, self.hb, self.bm, self.bms
        z = net.z
        self.square(z, None)

        def own(sl):
            s = self.local(z, sl)
            s = s + jnp.where(net.has_dn, wide(self.be[z, sl, :]), 0.0)
            s = s + jnp.where(net.has_up, wide(self.ab[z, sl, :]), 0.0)
            store(sl, s)

        net.wait(net.has_dn, lambda: self.be.at[z], self.bes.at[z])
        net.wait(net.has_up, lambda: self.ab.at[z], self.abs_.at[z])
        strips(cut, own)
        if rb:
            net.wait(None, lambda: bm.at[6, pl.ds(0, hb), :], bms.at[2])
            net.wait(None, lambda: bm.at[6, pl.ds(hb, hb), :], bms.at[5])
            net.wait(None, lambda: bm.at[7, pl.ds(0, hb), :], bms.at[4])
            net.wait(None, lambda: bm.at[7, pl.ds(hb, hb), :], bms.at[3])
            strips(rb, lambda sl: store(
                pl.ds(cut + sl.start, 16), wide(bm[net.u, sl, :]) + wide(bm[6, sl, :]) + wide(bm[7, sl, :])))


def steps_of(sc, text):
    names = {"m": sc.mid_send, "f": sc.bfirst, "d": sc.direct, "M": sc.mids, "h": sc.hop, "b": sc.bhop, "Q": sc.bquad, "q": sc.bquad2}
    return [functools.partial(names[word[0]], *[int(digit) for digit in word[1:]]) for word in text.split()]


def run_steps(steps):
    for one in steps:
        one()


def rs_scratch(cut, R, D):
    h, rb = cut // 2, R - cut
    V = lambda *s: pltpu.VMEM(s, BF)
    S = pltpu.SemaphoreType.DMA
    return [V(4, h, D), V(4, h, D), V(4, cut, D), V(4, cut, D), V(4, cut, D), V(4, cut, D),
            V(4, 4, max(rb, 16), D), V(4, 4, max(rb, 16), D), V(8, max(rb, 16), D),
            S((4,)), S((4,)), S((4, 2)), S((4, 2)), S((4,)), S((4,)), S((4,)), S((4,)), S((6,))]


def rs_kernel(cut, P, o_ref, ssem, *scr):
    net = Net(ssem)
    net.barrier()
    sc = Scatter(net, cut, P, scr)

    def store(sl, v):
        o_ref[sl, :] = v.astype(o_ref.dtype)

    for zd in (3, 0, 2, 1):
        sc.first(zd)
    for zd in (3, 0, 2, 1):
        sc.mids(zd)
    sc.hop(3, 0); sc.hop(0, 3); sc.bhop(3, 1); sc.bhop(0, 2)
    sc.hop(2, 0); sc.hop(1, 3); sc.bhop(2, 1); sc.bhop(1, 2)
    sc.hop(3, 1); sc.hop(0, 2); sc.bhop(3, 2); sc.bhop(0, 1)
    sc.hop(1, 0); sc.hop(2, 3); sc.bquad()
    sc.hop(2, 1); sc.hop(1, 2)
    sc.hop(3, 2); sc.hop(0, 1); sc.bquad2()
    sc.last(store)
    net.finish()


def rs16(p, cid, cut=96, dtype=F32):
    _, _, R, D = p.shape
    DMA = pltpu.SemaphoreType.DMA
    return pl.pallas_call(
        functools.partial(rs_kernel, cut),
        out_shape=jax.ShapeDtypeStruct((R, D), dtype),
        in_specs=[pl.BlockSpec(memory_space=pltpu.VMEM)],
        out_specs=pl.BlockSpec(memory_space=pltpu.VMEM),
        scratch_shapes=[DMA((96,))] + rs_scratch(cut, R, D),
        compiler_params=pltpu.CompilerParams(collective_id=cid, has_side_effects=True, vmem_limit_bytes=56 * 2**20),
        name="scatter_rows",
    )(p)


class Gather:
    def __init__(self, net, rows, cut, at, plane, sems):
        self.net, self.rows, self.cut, self.ref, self.plane = net, rows, cut, at, plane
        self.zr, self.xr, self.yr, self.d1, self.d2, self.br, self.bz = sems
        self.h, self.rb = cut // 2, rows - cut
        self.hb = self.rb // 2
        z = net.z
        self.near = []
        for s in range(4):
            zl, zh = z - s, z + s
            self.near.append((
                (jnp.maximum(zl, 0), zl >= 0, jnp.logical_and(zl >= 0, net.has_up), net.up),
                (jnp.minimum(zh, 3), zh < 4, jnp.logical_and(zh < 4, net.has_dn), net.dn)))

    def same(self, cond, uu, zz, lo, n, sem, dev):
        ref = lambda: self.ref(uu, zz, lo, n)
        self.net.go(cond, ref, ref, sem, dev)

    def outward(self, zz, cond):
        net, cut = self.net, self.cut
        self.same(cond, net.u, zz, 0, cut, lambda: self.xr.at[zz], net.xn)
        self.same(cond, net.u, zz, 0, cut, lambda: self.yr.at[zz], net.yn)

    def begin(self):
        net, cut, rb, z = self.net, self.cut, self.rb, self.net.z
        self.same(net.has_up, net.u, z, 0, cut, lambda: self.zr.at[z], net.up)
        self.same(net.has_dn, net.u, z, 0, cut, lambda: self.zr.at[z], net.dn)
        if rb:
            self.same(None, net.u, z, cut, rb, lambda: self.br.at[0], net.xn)
            self.same(None, net.u, z, cut, rb, lambda: self.br.at[1], net.yn)
        self.outward(z, None)

    def begin2(self):
        net, cut, rb, hb, z = self.net, self.cut, self.rb, self.hb, self.net.z
        if rb:
            net.wait(None, lambda: self.ref(net.ux, z, cut, rb), self.br.at[0])
            self.same(None, net.ux, z, cut, hb, lambda: self.br.at[2], net.yn)
            net.wait(None, lambda: self.ref(net.uy, z, cut, rb), self.br.at[1])
            self.same(None, net.uy, z, cut + hb, hb, lambda: self.br.at[3], net.xn)

    def along(self, s):
        net = self.net
        for zz, cond, fwd, dev in self.near[s]:
            net.wait(cond, lambda zz=zz: self.ref(net.u, zz, 0, self.cut), self.zr.at[zz])
            self.same(fwd, net.u, zz, 0, self.cut, lambda zz=zz: self.zr.at[zz], dev)
            self.outward(zz, cond)

    def quads(self, s):
        net, cut, rb, hb, z = self.net, self.cut, self.rb, self.hb, self.net.z
        if not rb:
            return
        if s == 0:
            net.wait(None, lambda: self.ref(net.ud, z, cut, hb), self.br.at[2])
            net.wait(None, lambda: self.ref(net.ud, z, cut + hb, hb), self.br.at[3])
            whole = lambda: self.plane(z, cut, rb)
            net.go(net.has_up, whole, whole, lambda: self.bz.at[z], net.up)
            net.go(net.has_dn, whole, whole, lambda: self.bz.at[z], net.dn)
            return
        for zz, cond, fwd, dev in self.near[s]:
            whole = lambda zz=zz: self.plane(zz, cut, rb)
            net.wait(cond, whole, self.bz.at[zz])
            net.go(fwd, whole, whole, lambda zz=zz: self.bz.at[zz], dev)

    def planes(self, s):
        if s == 0:
            return ((self.net.z, None),)
        return tuple((zz, cond) for zz, cond, _f, _d in self.near[s])

    def cross(self, s):
        net, h, cut = self.net, self.h, self.cut
        for zz, cond in self.planes(s):
            net.wait(cond, lambda zz=zz: self.ref(net.ux, zz, 0, cut), self.xr.at[zz])
            self.same(cond, net.ux, zz, 0, h, lambda zz=zz: self.d1.at[zz], net.yn)
            net.wait(cond, lambda zz=zz: self.ref(net.uy, zz, 0, cut), self.yr.at[zz])
            self.same(cond, net.uy, zz, h, h, lambda zz=zz: self.d2.at[zz], net.xn)

    def settle(self, s):
        net, h = self.net, self.h
        for zz, cond in self.planes(s):
            net.wait(cond, lambda zz=zz: self.ref(net.ud, zz, 0, h), self.d1.at[zz])
            net.wait(cond, lambda zz=zz: self.ref(net.ud, zz, h, h), self.d2.at[zz])


def ag_sems():
    S = pltpu.SemaphoreType.DMA
    return [S((4,)) for _ in range(7)]


def greet(net, chips=16):
    bar = pltpu.get_barrier_semaphore()

    def hello(j, _):
        t = lax.rem(net.u * 4 + net.z + j, chips)
        pl.semaphore_signal(bar, inc=1, device_id=(t // 4, lax.rem(t, 4), net.c), device_id_type=MESH)
        return 0

    lax.fori_loop(1, chips, hello, 0)
    pl.semaphore_signal(bar, inc=1, device_id=(net.u, net.z, 1 - net.c), device_id_type=MESH)
    pl.semaphore_wait(bar, chips)


def each_chip(net, body, chips=16):
    def one(j, _):
        t = lax.rem(net.u * 4 + net.z + j, chips)
        body(t, (t // 4, lax.rem(t, 4), net.c))
        return 0

    lax.fori_loop(1, chips, one, 0)


def remote(src, dst, ssem, rsem, dev):
    return pltpu.make_async_remote_copy(
        src_ref=src, dst_ref=dst, send_sem=ssem, recv_sem=rsem, device_id=dev, device_id_type=MESH)


def landed(ref, sem):
    pltpu.make_async_copy(ref, ref, sem).wait()


def segment_rows(segments, k_seg, reach):
    k_seg[:, 0:reach] = jnp.full((1, reach), -1.0, F32)
    k_seg[:, reach:] = segments[...]


def rope_at(near, far, i):
    cf, sf = far[0, pl.ds(i, 1), :], far[1, pl.ds(i, 1), :]
    cn, sn = near[0], near[1]
    return cf * cn - sf * sn, sf * cn + cf * sn


def row_sums(v):
    return jnp.sum(v.T, axis=0, keepdims=True)


def column(row):
    return jnp.broadcast_to(row, (row.shape[1], row.shape[1])).T


def share_sums(net, sums, sums_all, out, lsem, ssem, rsem):
    me = net.u * 4 + net.z
    own = pltpu.make_async_copy(sums, sums_all.at[me], lsem)
    own.start()
    each_chip(net, lambda t, dev: remote(sums, sums_all.at[me], ssem, rsem, dev).start())
    own.wait()
    part = sums_all.at[pl.ds(0, 15)]
    landed(part, rsem)
    total = sums_all[0]
    for i in range(1, 16):
        total = total + sums_all[i]
    out[...] = total
    landed(part, ssem)


def greet_all(net, count=32):
    bar = pltpu.get_barrier_semaphore()
    me = net.u * 8 + net.z * 2 + net.c

    def hello(j, _):
        t = lax.rem(me + j, count)
        pl.semaphore_signal(bar, inc=1, device_id=(t // 8, lax.rem(t, 8) // 2, lax.rem(t, 2)), device_id_type=MESH)
        return 0

    lax.fori_loop(1, count, hello, 0)
    pl.semaphore_wait(bar, count - 1)


def weight_tiles(partner, plan, load, turn, right, left, ob, gt, fs, other, osem, ors, fsem, gsem, out):
    side = fs.shape[2]

    def sent(k):
        return remote(ob(k), other.at[k], osem.at[k], ors.at[k], partner)

    def tile_at(i):
        kind, k = plan[i]
        if load is not None and i + 1 < len(plan):
            load(i + 1).start()
        if kind == "o":
            if k >= 2:
                sent(k - 2).wait_send()
        else:
            landed(other.at[k], ors.at[k])
            fetch = pltpu.make_async_copy(other.at[k], gt, gsem)
            fetch.start()
        if load is not None:
            load(i).wait()
        turn(i)
        if kind == "w":
            fetch.wait()
        for h in (0, 1):
            if kind == "w" and k > 0:
                landed(fs.at[h], fsem.at[h])
            for n in (0, 1):
                made = dot(left[...], right(h, n), ((1,), (0,)))
                cols = slice(h * side + n * 512, h * side + (n + 1) * 512)
                if kind == "o":
                    ob(k)[:, cols] = made.astype(BF)
                else:
                    fs[h, :, n * 512 : (n + 1) * 512] = made + wide(gt[:, cols])
            if kind == "w":
                pltpu.make_async_copy(fs.at[h], out(k, h), fsem.at[h]).start()
        if kind == "o":
            sent(k).start()

    def finish():
        count = len(plan) // 2
        for k in (count - 2, count - 1):
            sent(k).wait_send()
        for h in (0, 1):
            landed(fs.at[h], fsem.at[h])

    return tile_at, finish


def turned_into(left, flat, cols, tile=256):
    def one(b, _):
        sl = pl.ds(pl.multiple_of(b * tile, tile), tile)
        left[:, sl] = flat[sl, cols].T
        return 0

    lax.fori_loop(0, flat.shape[0] // tile, one, 0)


def qkv_kernel(cut, x_ref, wq, wk, wv, block, cot, n1_o, lin_o, wf_o, tot, sw, C, X, lin, wf, nb, gain, sums, sums_all, lsem, nsem, msem, ssem, csem, *gs):
    net = Net(ssem)
    u, z, c = net.u, net.z, net.c
    me = u * 4 + z
    rows, width = X.shape[2], X.shape[3]
    partner = (u, z, 1 - c)
    own = pltpu.make_async_copy(x_ref, X.at[u, z], lsem.at[0])
    own.start()

    def piece(t, i):
        return ((wq, wk, wv)[i].at[:, pl.ds(pl.multiple_of(t * 128, 128), 128)], wf.at[me, c, :, pl.ds(i * 128, 128)])

    own_w = [pltpu.make_async_copy(*piece(me, i), lsem.at[1]) for i in range(3)]
    for one in own_w:
        one.start()
    own_c = pltpu.make_async_copy(cot, C.at[u, z], lsem.at[3])
    own_c.start()
    dev_me = me * 2 + c
    greet_all(net)
    own.wait()
    ga = Gather(net, rows, cut, lambda uu, zz, lo, n: X.at[uu, zz, pl.ds(lo, n), :],
                lambda zz, lo, n: X.at[:, zz, pl.ds(lo, n), :], gs[:7])
    netc = Net(csem)
    gc = Gather(netc, rows, cut, lambda uu, zz, lo, n: C.at[uu, zz, pl.ds(lo, n), :],
                lambda zz, lo, n: C.at[:, zz, pl.ds(lo, n), :], gs[7:])
    ga.begin()

    def tell(j, _):
        t = lax.rem(dev_me + j, 32)
        remote(block.at[t // 2], sw.at[dev_me], msem.at[6], msem.at[7], (t // 8, lax.rem(t, 8) // 2, lax.rem(t, 2))).start()
        return 0

    lax.fori_loop(1, 32, tell, 0)
    sw[dev_me] = block[me]

    def columns(t, dev):
        for i in range(3):
            remote(*piece(t, i), msem.at[0], msem.at[1], dev).start()

    each_chip(net, columns)

    def plane(zz):
        def chunk(uu, _):
            slot = lax.rem(uu, 2)
            k = uu * 4 + zz

            def norm(i, _):
                sl = pl.ds(pl.multiple_of(i * 16, 16), 16)
                v = X[uu, zz, sl, :].astype(F32)
                r = lax.rsqrt(jnp.mean(v * v, axis=1, keepdims=True) + EPS)
                nb[slot, sl, :] = (v * r * gain[...]).astype(BF)
                return 0

            def stored(s):
                return pltpu.make_async_copy(nb.at[s], n1_o.at[k], nsem.at[s])

            pl.when(uu >= 2)(lambda: stored(slot).wait())
            lax.fori_loop(0, rows // 16, norm, 0)
            stored(slot).start()
            got = dot(nb[slot], wf[...].reshape(width, wf.shape[-1]), ((1,), (0,)))
            lin[k] = got
            q, kk = got[:, :128], got[:, 128:256]
            sums[pl.ds(k, 1), :] = row_sums(q * q)
            sums[pl.ds(16 + k, 1), :] = row_sums(kk * kk)
            return 0

        lax.fori_loop(0, 4, chunk, 0)
        for s in (0, 1):
            pltpu.make_async_copy(nb.at[s], n1_o.at[0], nsem.at[s]).wait()

    def compute(s):
        for zz, cond in ga.planes(s):
            if cond is None:
                plane(zz)
            else:
                pl.when(cond)(lambda zz=zz: plane(zz))

    ga.begin2()
    ga.along(1)
    ga.quads(0)
    ga.cross(0)
    landed(wf.at[0, 0], lsem.at[1])
    landed(wf.at[pl.ds(0, 15), 0], msem.at[1])
    to_partner = remote(wf.at[:, c], wf.at[:, c], msem.at[2], msem.at[3], partner)
    to_partner.start()
    own_c.wait()
    ga.along(2)
    ga.quads(1)
    ga.cross(1)
    gc.begin()
    landed(sw.at[pl.ds(0, 31)], msem.at[7])
    for e in range(16):
        gain[:, e * 128 : (e + 1) * 128] = sw[2 * e, 2:3, :] + sw[2 * e + 1, 2:3, :]
    ga.settle(0)
    landed(wf.at[:, 1 - c], msem.at[3])
    keep_w = pltpu.make_async_copy(wf, wf_o, lsem.at[0])
    keep_w.start()
    compute(0)
    gc.begin2()
    ga.along(3)
    ga.quads(2)
    ga.cross(2)
    ga.settle(1)
    gc.along(1)
    gc.quads(0)
    gc.cross(0)
    compute(1)
    ga.quads(3)
    ga.cross(3)
    ga.settle(2)
    gc.along(2)
    gc.quads(1)
    gc.cross(1)
    compute(2)
    ga.settle(3)
    gc.along(3)
    gc.quads(2)
    gc.cross(2)
    compute(3)
    keep = pltpu.make_async_copy(lin, lin_o, lsem.at[1])
    keep.start()
    landed(wf.at[pl.ds(0, 15), 0], msem.at[0])
    landed(wf.at[:, c], msem.at[2])
    share_sums(net, sums, sums_all, tot, lsem.at[2], msem.at[4], msem.at[5])
    gc.quads(3)
    gc.cross(3)
    for s in range(4):
        gc.settle(s)
    landed(sw.at[pl.ds(0, 31)], msem.at[6])
    keep_w.wait()
    keep.wait()
    net.finish()
    netc.finish()


def run_qkv(x, wq, wk, wv, block, cot, cid, cut=96):
    R, D = x.shape
    N = 384
    DMA = pltpu.SemaphoreType.DMA
    S = jax.ShapeDtypeStruct
    V = lambda *s: pltpu.VMEM(s, BF)
    VF = lambda *s: pltpu.VMEM(s, F32)
    A = pl.BlockSpec(memory_space=pl.ANY)
    M = pl.BlockSpec(memory_space=pltpu.VMEM)
    return pl.pallas_call(
        functools.partial(qkv_kernel, cut),
        out_shape=(S((16, R, D), BF), S((16, R, N), F32), S((16, 2, R // 2, N), BF), S((32, 128), F32),
                   S((32, 8, 128), F32), S((4, 4) + cot.shape, BF)),
        in_specs=[A, A, A, A, M, A],
        out_specs=(A, A, A, M, M, A),
        scratch_shapes=[V(4, 4, R, D), VF(16, R, N), V(16, 2, R // 2, N), V(2, R, D), VF(1, D), VF(32, 128), VF(16, 32, 128),
                        DMA((4,)), DMA((2,)), DMA((8,)), DMA((64,)), DMA((64,))] + ag_sems() + ag_sems(),
        compiler_params=pltpu.CompilerParams(collective_id=cid, has_side_effects=True, vmem_limit_bytes=63 * 2**20),
        name="project",
    )(x, wq, wk, wv, block, cot)


def group_of(t):
    g = t // 2
    return jnp.where(g == 0, 3, jnp.where(g == 1, 0, jnp.where(g == 2, 2, 1)))


def expert_kernel(cut, n2, cot_a, cot_b, share_rows, gate, up, down, d_n2, p_out, n2_o, a_o, other, dd_o,
                  X, C, GU, W, A, hid, pb, fs, share, lsem, wsem, wrs, psem, osem, tsem, ors, fsem, sa, sr, *scr):
    ga_sems, rs_bufs = scr[:7], scr[7:]
    na, nr = Net(sa), Net(sr)
    u, z, c = na.u, na.z, na.c
    partner = (u, z, 1 - c)
    rows, width = X.shape[2], X.shape[3]
    ff = W.shape[0]
    half, half_ff = gate.shape[0], down.shape[0]
    tokens = 16 * rows
    tile = 256
    span = 512
    side = width // 2
    first = [pltpu.make_async_copy(n2, X.at[u, z], lsem.at[0]),
             pltpu.make_async_copy(cot_a, C.at[:, :, :, pl.ds(0, side)], lsem.at[1]),
             pltpu.make_async_copy(cot_b, C.at[:, :, :, pl.ds(side, side)], lsem.at[5])]

    def weights():
        mine = pl.ds(pl.multiple_of(c * half, half), half)
        mine_ff = pl.ds(pl.multiple_of(c * half_ff, half_ff), half_ff)
        return ((gate, GU.at[mine, pl.ds(0, ff)]), (up, GU.at[mine, pl.ds(ff, ff)]), (down, W.at[mine_ff, :]))

    own_w = [pltpu.make_async_copy(a, b, lsem.at[2 + i]) for i, (a, b) in enumerate(weights())]
    for one in first + own_w:
        one.start()
    for k in range(16):
        share[k // 4, k % 4] = column(share_rows[k : k + 1, :])[:, 0:1]
    na.barrier((partner,))
    first[0].wait()

    def gather(net, buf, sems):
        return Gather(net, rows, cut, lambda uu, zz, lo, n: buf.at[uu, zz, pl.ds(lo, n), :],
                      lambda zz, lo, n: buf.at[:, zz, pl.ds(lo, n), :], sems)

    ga = gather(na, X, ga_sems)
    ga.begin()
    sent_w = [remote(a, b, wsem.at[i], wrs.at[i], partner) for i, (a, b) in enumerate(weights())]
    for one in sent_w:
        one.start()

    def forward(zz):
        pltpu.make_async_copy(X.at[:, zz], n2_o.at[:, zz], psem.at[1]).start()

        def scale(i, _):
            sl = pl.ds(pl.multiple_of(i * 16, 16), 16)
            C[:, zz, sl, :] = (share[:, zz, sl, :] * C[:, zz, sl, :].astype(F32)).astype(BF)
            return 0

        lax.fori_loop(0, rows // 16, scale, 0)

        def inner(n, _):
            gcols = pl.ds(pl.multiple_of(n * span, span), span)
            ucols = pl.ds(pl.multiple_of(ff + n * span, span), span)
            xv = X[:, zz].reshape(4 * rows, width)
            g = dot(xv, GU[:, gcols], ((1,), (0,)))
            uu = dot(xv, GU[:, ucols], ((1,), (0,)))
            s = jax.nn.sigmoid(g)
            gs = g * s
            hid[:, zz, :, gcols] = (gs * uu).astype(BF).reshape(4, rows, span)
            dh = dot(C[:, zz].reshape(4 * rows, width), W[gcols, :], ((1,), (1,)))
            A[:, zz, :, gcols] = (dh * uu * s * (1.0 + g * (1.0 - s))).astype(BF).reshape(4, rows, span)
            A[:, zz, :, ucols] = (dh * gs).astype(BF).reshape(4, rows, span)
            return 0

        lax.fori_loop(0, ff // span, inner, 0)
        pltpu.make_async_copy(A.at[:, zz], a_o.at[:, zz], psem.at[2]).start()
        weight = share[:, zz]

        def flushed(n):
            cols = pl.ds(pl.multiple_of(n * span, span), span)
            slot = lax.rem(n, 2)
            return pltpu.make_async_copy(pb.at[slot], p_out.at[:, zz, :, cols], osem.at[slot])

        def outer(n, _):
            cols = pl.ds(pl.multiple_of(n * span, span), span)
            made = dot(hid[:, zz].reshape(4 * rows, ff), W[:, cols], ((1,), (0,)))
            made = made.astype(BF).astype(F32).reshape(4, rows, span)
            pl.when(n >= 2)(lambda: flushed(n - 2).wait())
            pb[lax.rem(n, 2)] = (weight * made).astype(BF)
            flushed(n).start()
            return 0

        count = width // span
        lax.fori_loop(0, count, outer, 0)
        flushed(count - 2).wait()
        flushed(count - 1).wait()

    def planes(s):
        if s == 0:
            forward(z)
            return

        def one(d, _):
            zz = jnp.where(d == 0, z - s, z + s)
            pl.when(jnp.logical_and(zz >= 0, zz < 4))(lambda: forward(zz))
            return 0

        lax.fori_loop(0, 2, one, 0)

    ga.begin2()
    ga.along(1)
    ga.quads(0)
    ga.cross(0)
    ga.along(2)
    ga.quads(1)
    ga.cross(1)
    ga.settle(0)
    for one in own_w:
        one.wait()
    for one in sent_w:
        one.wait_recv()
    first[1].wait()
    first[2].wait()
    planes(0)
    ga.along(3)
    ga.quads(2)
    ga.cross(2)
    ga.settle(1)
    planes(1)
    ga.quads(3)
    ga.cross(3)
    ga.settle(2)
    planes(2)
    ga.settle(3)
    planes(3)
    na.finish()
    for one in sent_w:
        one.wait_send()
    landed(X, psem.at[1])
    sc = Scatter(nr, cut, X, rs_bufs)

    def backward(t):
        zd = group_of(t)
        base = lax.rem(t, 2) * (width // 2)

        def outer(n, _):
            cols = pl.ds(pl.multiple_of(base + n * span, span), span)
            back = dot(A[:, zd].reshape(4 * rows, 2 * ff), GU[cols, :], ((1,), (1,)))
            X[:, zd, :, cols] = back.astype(BF).reshape(4, rows, span)
            return 0

        lax.fori_loop(0, width // 2 // span, outer, 0)

    def acts(steps, t):
        for at, todo in steps.items():
            def act(todo=todo):
                for one in todo:
                    one()
            pl.when(t == at)(act)

    def at_turns(table):
        return {t: steps_of(sc, words) for t, words in table.items()}

    steps = at_turns({1: "m3 f3 d3", 3: "m0 f0 d0", 4: "M3", 5: "m2 f2 d2 b31", 6: "M0", 7: "m1 f1 d1 b02 b32"})

    def turn(t, _):
        backward(t)
        acts(steps, t)
        return 0

    lax.fori_loop(0, 8, turn, 0)

    left = W.at[pl.ds(0, tile), :]

    def left_hidden(i):
        kind, k = plan[i]
        which = 1 - c if kind == "o" else c
        turned_into(left, hid.reshape(tokens, ff), pl.ds(pl.multiple_of((which * 2 + k) * tile, tile), tile))

    plan = [("o", 0), ("o", 1), ("w", 0), ("w", 1)]
    made = C.reshape(tokens, width)
    dw, dw_end = weight_tiles(
        partner, plan, None, left_hidden, lambda h, n: made[:, h * side + n * 512 : h * side + (n + 1) * 512], left,
        lambda k: W.at[pl.ds((1 + k % 2) * tile, tile), :], W.at[pl.ds(3 * tile, tile), :], fs, other, tsem, ors, fsem,
        lsem.at[0], lambda k, h: dd_o.at[pl.ds(k * tile, tile), pl.ds(h * side, side)])

    def go(words):
        run_steps(steps_of(sc, words))

    dw(0)
    go("M2 b21")
    dw(1)
    go("h30 M1 b01 b12 h03")
    dw(2)
    go("h31 h02 h20 h23")
    dw(3)
    go("h32 h01 h10 h13 Q h21 h12 q")

    def store_out(sl, v):
        d_n2[sl, :] = v

    sc.last(store_out)
    landed(A, psem.at[2])
    dw_end()
    nr.finish()


def run_expert(n2, cot_a, cot_b, share, gate, up, down, cid, cut=96):
    R, D = n2.shape
    half, ff = gate.shape
    DMA = pltpu.SemaphoreType.DMA
    S = jax.ShapeDtypeStruct
    V = lambda *s: pltpu.VMEM(s, BF)
    A = pl.BlockSpec(memory_space=pl.ANY)
    M = pl.BlockSpec(memory_space=pltpu.VMEM)
    return pl.pallas_call(
        functools.partial(expert_kernel, cut),
        out_shape=(S((R, D), F32), S((4, 4, R, D), BF), S((4, 4, R, D), BF), S((4, 4, R, 2 * ff), BF),
                   S((2, 256, D), BF), S(down.shape, F32)),
        in_specs=[A, A, A, M, A, A, A],
        out_specs=(M,) + (A,) * 5,
        scratch_shapes=[V(4, 4, R, D), V(4, 4, R, D), V(D, 2 * ff), V(ff, D), V(4, 4, R, 2 * ff), V(4, 4, R, ff),
                        V(2, 4, R, 512), pltpu.VMEM((2, 256, D // 2), F32), pltpu.VMEM((4, 4, R, 1), F32),
                        DMA((6,)), DMA((3,)), DMA((3,)), DMA((3,)), DMA((2,)), DMA((2,)), DMA((2,)), DMA((2,)),
                        DMA((64,)), DMA((96,))] + ag_sems() + rs_scratch(cut, R, D),
        compiler_params=pltpu.CompilerParams(collective_id=cid, has_side_effects=True, vmem_limit_bytes=63 * 2**20),
        name="expert",
    )(n2, cot_a, cot_b, share, gate, up, down)


def finish_kernel(cut, d_lin, wf, n1, att, x_in, d_res, gain, d_gain_two, d_gains,
                  d_wo, d_inputs, d_wq, d_wk, d_wv, gains_o,
                  P, PO, PG, PT, wsum, nt, left, keep, give, got, send, recv, d_n1, d_gain, gb, gr,
                  lsem, tsem, msem, s1, s2, *bufs):
    net, net2 = Net(s1), Net(s2)
    u, z, c = net.u, net.z, net.c
    me = u * 4 + z
    rows, width = P.shape[2], P.shape[3]
    lanes = d_lin.shape[2]
    tokens = 16 * rows
    tile = 256
    partner = (u, z, 1 - c)
    half = len(bufs) // 2
    sc1, sc2 = Scatter(net, cut, P, bufs[:half]), Scatter(net2, cut, PO, bufs[half:])

    def tile_load(k):
        slot = lax.rem(k, 2)
        return pltpu.make_async_copy(n1.at[:, :, pl.ds(pl.multiple_of(k * tile, tile), tile)], nt.at[slot], tsem.at[slot])

    tile_load(0).start()
    greet_all(net)

    def one(words):
        run_steps(steps_of(sc1, words))

    def two(words):
        run_steps(steps_of(sc2, words))

    def group(zd):
        def one(n, _):
            cols = pl.ds(pl.multiple_of(n * 512, 512), 512)
            w = wf.reshape(width, lanes)
            for q in range(4):
                P[q, zd, :, cols] = dot(d_lin[q * 4 + zd], w[cols, :], ((1,), (1,))).astype(BF)
            return 0

        lax.fori_loop(0, width // 512, one, 0)

    for zd in (3, 0, 2, 1):
        group(zd)
        one(f"m{zd}" + (f" f{zd}" if zd in (3, 0) else ""))

    side = width // 2
    own_cols = pl.ds(pl.multiple_of(c * side, side), side)
    give_cols = pl.ds(pl.multiple_of((1 - c) * side, side), side)

    def outer(e, _):
        turned_att = att[e].T
        PG[e // 4, lax.rem(e, 4)] = dot(turned_att, d_res[:, give_cols].astype(BF), ((1,), (0,))).astype(BF)
        PO[e // 4, lax.rem(e, 4)] = dot(turned_att, d_res[:, own_cols].astype(BF), ((1,), (0,))).astype(BF)
        return 0

    lax.fori_loop(0, 16, outer, 0)
    halves = remote(PG, PT, msem.at[6], msem.at[7], partner)
    halves.start()

    def join():
        landed(PT, msem.at[7])

        def add(e, _):
            def strip(sl):
                at = (e // 4, lax.rem(e, 4), sl, slice(None))
                PO[at] = (wide(PO[at]) + wide(PT[at])).astype(BF)

            strips(rows, strip)
            return 0

        lax.fori_loop(0, 16, add, 0)

    def store1(sl, v):
        d_n1[sl, :] = v

    def store2(sl, v):
        wsum[sl, :] = v


    def grads(k):
        if k < 7:
            tile_load(k + 1).start()
        tile_load(k).wait()
        slot = k % 2
        flat = nt.at[slot].reshape(tokens, tile)

        def turn(b, _):
            sl = pl.ds(pl.multiple_of(b * tile, tile), tile)
            left[:, sl] = flat[sl, :].T
            return 0

        lax.fori_loop(0, tokens // tile, turn, 0)
        made = dot(left[...], d_lin[...].reshape(tokens, lanes), ((1,), (0,)))
        for i in range(2):
            first, second = made[i * 128 : i * 128 + 64], made[i * 128 + 64 : (i + 1) * 128]
            keep[2 * k + i] = jnp.where(c == 0, first, second)
            give[2 * k + i] = jnp.where(c == 0, second, first).astype(BF)

    one("f2 f1")
    join()
    two("m3 m0 m2 m1 f3 f0")
    one("d3 d0")
    grads(0)
    one("M3 M0")
    one("d2 d1")
    grads(1)
    one("M2 M1")
    two("d3 d0 d2 d1 f2 f1")
    grads(2)
    one("b31 b02")
    two("M3 M0 M2 M1")
    grads(3)
    one("h30 h03 b21 b12")
    grads(4)
    grads(5)
    one("b32 b01")
    grads(6)
    grads(7)
    across = remote(give, got, msem.at[0], msem.at[1], partner)
    across.start()
    landed(got, msem.at[1])

    def total(e, _):
        send[e] = (keep[e] + wide(got[e])).astype(BF)
        return 0

    lax.fori_loop(0, 16, total, 0)
    each_chip(net, lambda t, dev: remote(send.at[t], recv.at[me], msem.at[2], msem.at[3], dev).start())
    recv[me] = send[me]
    two("b31 b02 b21 b12 b32 b01")
    one("h31 h02 h20 h13 Q")
    two("h30 h03 h20 h13 Q")
    one("h32 h01 h10 h23")
    two("h31 h02 h10 h23")
    one("h21 h12 q")
    sc1.last(store1)
    d_gain[...] = jnp.zeros_like(d_gain)

    def norm_back(i, _):
        sl = pl.ds(pl.multiple_of(i * 16, 16), 16)
        v, d = wide(x_in[sl, :]), d_n1[sl, :]
        r = lax.rsqrt(jnp.mean(v * v, axis=1, keepdims=True) + EPS)
        scaled = d * gain[...]
        inner = jnp.mean(scaled * v, axis=1, keepdims=True)
        d_inputs[sl, :] = d_res[sl, :] + r * scaled - v * (r * r * r * inner)
        d_gain[...] += jnp.sum(d * v * r, axis=0, keepdims=True)
        return 0

    lax.fori_loop(0, rows // 16, norm_back, 0)
    gb[...] = jnp.zeros_like(gb)
    gb[me, 2:4, :] = d_gains[0:2, :]
    for e in range(16):
        gb[e, 0:1, :] = d_gain[:, e * 128 : (e + 1) * 128]
        gb[e, 1:2, :] = d_gain_two[:, e * 128 : (e + 1) * 128]
    dev_me = me * 2 + c

    def tell(j, _):
        t = lax.rem(dev_me + j, 32)
        remote(gb.at[t // 2], gr.at[dev_me], msem.at[4], msem.at[5], (t // 8, lax.rem(t, 8) // 2, lax.rem(t, 2))).start()
        return 0

    lax.fori_loop(1, 32, tell, 0)
    gr[dev_me] = gb[me]
    two("h32 h01 h21 h12 q")
    landed(recv.at[pl.ds(0, 15)], msem.at[3])
    for e in range(16):
        piece = wide(recv[e])
        for i, out in enumerate((d_wq, d_wk, d_wv)):
            out[:, e * 128 : (e + 1) * 128] = piece[:, i * 128 : (i + 1) * 128]
    landed(gr.at[pl.ds(0, 31)], msem.at[5])
    sums = gr[0]
    for i in range(1, 32):
        sums = sums + gr[i]
    gains_o[...] = jnp.where(c == 0, sums[:, :64], sums[:, 64:])
    sc2.last(store2)
    d_wo[:, own_cols] = wsum[pl.ds(pl.multiple_of(c * 64, 64), 64), :]
    theirs = remote(wsum.at[pl.ds(pl.multiple_of((1 - c) * 64, 64), 64), :], d_wo.at[:, own_cols], msem.at[8], msem.at[9], partner)
    theirs.start()
    landed(PG, msem.at[6])
    landed(give, msem.at[0])
    landed(recv.at[pl.ds(0, 15)], msem.at[2])
    landed(gr.at[pl.ds(0, 31)], msem.at[4])
    theirs.wait_send()
    landed(d_wo.at[:, give_cols], msem.at[9])
    net.finish()
    net2.finish()


def run_finish(d_lin, wf, n1, att, x_in, d_res, gain, d_gain_two, d_gains, cid, cut=96):
    R, D = x_in.shape
    N = d_lin.shape[2]
    DMA = pltpu.SemaphoreType.DMA
    S = jax.ShapeDtypeStruct
    V = lambda *s: pltpu.VMEM(s, BF)
    VF = lambda *s: pltpu.VMEM(s, F32)
    A = pl.BlockSpec(memory_space=pl.ANY)
    M = pl.BlockSpec(memory_space=pltpu.VMEM)
    own = S((R // 2, D), F32)
    return pl.pallas_call(
        functools.partial(finish_kernel, cut),
        out_shape=(own, S((R, D), F32), own, own, own, S((8, 64), F32)),
        in_specs=[M, M, A] + [M] * 6,
        out_specs=(M,) * 6,
        scratch_shapes=[V(4, 4, R, D), V(4, 4, R, D // 2), V(4, 4, R, D // 2), V(4, 4, R, D // 2), VF(R, D // 2), V(2, 16, R, 256), V(256, 16 * R), VF(16, 64, N), V(16, 64, N),
                        V(16, 64, N), V(16, 64, N), V(16, 64, N), VF(R, D), VF(1, D), VF(16, 8, 128), VF(32, 8, 128),
                        DMA((1,)), DMA((2,)), DMA((10,)), DMA((64,)), DMA((64,))] + rs_scratch(cut, R, D) + rs_scratch(cut, R, D // 2),
        compiler_params=pltpu.CompilerParams(collective_id=cid, has_side_effects=True, vmem_limit_bytes=63 * 2**20),
        name="finish",
    )(d_lin, wf, n1, att, x_in, d_res, gain, d_gain_two, d_gains)

def band_scores(q, k, q_seg, k_seg, scale, reach):
    scores = dot(q, k, ((1,), (1,))) * scale
    q_at = lax.broadcasted_iota(jnp.int32, scores.shape, 0)
    k_at = lax.broadcasted_iota(jnp.int32, scores.shape, 1)
    return scores, (k_seg == q_seg) & (k_at <= q_at + reach)


def turned(v, cosine, sine):
    return v * cosine + pltpu.roll(v, 64, axis=1) * sine


def turned_back(v, cosine, sine):
    return v * cosine - pltpu.roll(v, 64, axis=1) * sine


def attend_kernel(scale, pads, cut, lin_h, tot, near, far, gq, gk, q_seg, segments, w_own, x_in, gain, cot,
                  wo_o, q_rot_o, kv_o, o_o, lse, att_o, residual_o, n2, C,
                  lin, k_seg, q_rot, kv, o_ref, att, residual, wo, lsem, msem, psem, ksem, ssem, csem, *gs):
    net = Net(ssem)
    u, z, c = net.u, net.z, net.c
    me = u * 4 + z
    rows = x_in.shape[0]
    width = x_in.shape[1]
    reach = pads * 2 * rows
    partner = (u, z, 1 - c)
    own = pltpu.make_async_copy(w_own, wo.at[u, z, c], lsem.at[0])
    own.start()
    load = pltpu.make_async_copy(lin_h, lin, ksem.at[0])
    load.start()
    own_c = pltpu.make_async_copy(cot, C.at[u, z], lsem.at[2])
    own_c.start()
    greet(net)
    own.wait()
    ga = Gather(net, rows // 2, rows // 2, lambda uu, zz, lo, n: wo.at[uu, zz, c, pl.ds(lo, n), :], None, gs[:7])
    netc = Net(csem)
    gc = Gather(netc, rows, cut, lambda uu, zz, lo, n: C.at[uu, zz, pl.ds(lo, n), :],
                lambda zz, lo, n: C.at[:, zz, pl.ds(lo, n), :], gs[7:])

    def halves(s):
        ga.settle(s)
        for zz, cond in ga.planes(s):
            ref = lambda zz=zz: wo.at[:, zz, c]
            net.go(cond, ref, ref, lambda zz=zz: psem.at[zz], partner)

    ga.begin()
    segment_rows(segments, k_seg, reach)
    load.wait()
    for i in range(pads):
        kv[:, i] = jnp.zeros(kv.shape[:1] + kv.shape[2:], BF)

    def ready(i, _):
        both = lin[i]
        rq = lax.rsqrt(column(tot[pl.ds(i, 1), :]) / width + EPS)
        rk = lax.rsqrt(column(tot[pl.ds(16 + i, 1), :]) / width + EPS)
        cs, sn = rope_at(near, far, i)
        q_rot[i] = turned(both[:, :128] * rq * gq[...], cs, sn).astype(BF)
        kv[0, pads + i, c] = turned(both[:, 128:256] * rk * gk[...], cs, sn).astype(BF)
        kv[1, pads + i, c] = both[:, 256:].astype(BF)
        return 0

    lax.fori_loop(0, 16, ready, 0)
    mine = kv.at[:, pl.ds(pads, 16), c]
    to_partner = remote(mine, mine, msem.at[0], msem.at[1], partner)
    to_partner.start()
    ga.along(1)
    ga.cross(0)
    own_c.wait()
    gc.begin()
    landed(kv.at[:, pl.ds(pads, 16), 1 - c], msem.at[1])

    def block(j, _):
        i = lax.rem(me + 1 + j, 16)
        first = 2 * i + c
        band = pl.ds(pl.multiple_of(first * rows, rows), rows + reach)
        kf, vf = kv.at[0].reshape((pads + 16) * 2 * rows, 128), kv.at[1].reshape((pads + 16) * 2 * rows, 128)
        scores, allowed = band_scores(q_rot[i], kf[band, :], column(q_seg[pl.ds(i, 1), :])[:, 0:1], k_seg[:, band], scale, reach)
        scores = jnp.where(allowed, scores, NEG)
        top = jnp.max(scores, axis=1, keepdims=True)
        weights = jnp.where(allowed, jnp.exp(scores - top), 0.0)
        total = jnp.sum(weights, axis=1, keepdims=True)
        probs = (weights / total).astype(BF)
        o_ref[i] = dot(probs, vf[band, :], ((1,), (0,))).astype(BF)
        lse[i] = top + jnp.log(total)

        @pl.when(j < 15)
        def _():
            remote(o_ref.at[i], att.at[me], msem.at[2], msem.at[3], (i // 4, lax.rem(i, 4), c)).start()

        return 0

    lax.fori_loop(0, 5, block, 0)
    ga.along(2)
    ga.cross(1)
    halves(0)
    gc.begin2()
    lax.fori_loop(5, 10, block, 0)
    ga.along(3)
    ga.cross(2)
    halves(1)
    gc.along(1)
    gc.quads(0)
    gc.cross(0)
    lax.fori_loop(10, 16, block, 0)
    ga.cross(3)
    halves(2)
    gc.along(2)
    gc.quads(1)
    gc.cross(1)
    halves(3)
    att[me] = o_ref[me]
    part = att.at[pl.ds(0, 15)]
    landed(part, msem.at[3])
    for zz in range(4):
        landed(wo.at[:, zz, 1 - c], psem.at[zz])
    keep = [pltpu.make_async_copy(a, o, ksem.at[j]) for j, (a, o) in enumerate(
        ((wo, wo_o), (q_rot, q_rot_o), (kv, kv_o), (o_ref, o_o), (att, att_o)))]
    for one in keep:
        one.start()
    tile = 256

    def out(n, _):
        cols = pl.ds(pl.multiple_of(n * tile, tile), tile)
        acc = x_in[:, cols].astype(F32)
        for e in range(0, 16, 2):
            pair = jnp.concatenate([att[e], att[e + 1]], axis=1)
            acc = acc + dot(pair, wo[e // 4, pl.ds(e % 4, 2), :, :, cols].reshape(256, tile), ((1,), (0,)))
        residual[:, cols] = acc
        return 0

    lax.fori_loop(0, width // tile, out, 0)
    keep.append(pltpu.make_async_copy(residual, residual_o, ksem.at[5]))
    keep[5].start()
    gc.along(3)
    gc.quads(2)
    gc.cross(2)

    def norm(i, _):
        sl = pl.ds(pl.multiple_of(i * 16, 16), 16)
        v = residual[sl, :]
        r = lax.rsqrt(jnp.mean(v * v, axis=1, keepdims=True) + EPS)
        n2[sl, :] = (v * r * gain[...]).astype(BF)
        return 0

    lax.fori_loop(0, rows // 16, norm, 0)
    landed(mine, msem.at[0])
    landed(part, msem.at[2])
    gc.quads(3)
    gc.cross(3)
    for s in range(4):
        gc.settle(s)
    for one in keep:
        one.wait()
    net.finish()
    netc.finish()


def run_attend(scale, pads, lin, tot, near, far, gq, gk, q_seg, segments, w_own, x_in, gain, cot, cid, cut=96):
    R, D = x_in.shape
    DMA = pltpu.SemaphoreType.DMA
    S = jax.ShapeDtypeStruct
    A = pl.BlockSpec(memory_space=pl.ANY)
    M = pl.BlockSpec(memory_space=pltpu.VMEM)
    V = pltpu.VMEM
    wo = (4, 4, 2, R // 2, D)
    return pl.pallas_call(
        functools.partial(attend_kernel, scale, pads, cut),
        out_shape=(S(wo, BF), S((16, R, 128), BF), S((2, pads + 16, 2, R, 128), BF), S((16, R, 128), BF),
                   S((16, R, 1), F32), S((16, R, 128), BF), S((R, D), F32), S((R, D), BF), S((4, 4) + cot.shape, BF)),
        in_specs=[A] + [M] * 7 + [A, M, M, A],
        out_specs=(A, A, A, A, M, A, A, M, A),
        scratch_shapes=[V((16, R, 384), F32), V((1, (pads + 16) * 2 * R), F32), V((16, R, 128), BF),
                        V((2, pads + 16, 2, R, 128), BF), V((16, R, 128), BF), V((16, R, 128), BF), V((R, D), F32),
                        V(wo, BF), DMA((3,)), DMA((4,)), DMA((4,)), DMA((6,)), DMA((64,)), DMA((64,))] + ag_sems() + ag_sems(),
        compiler_params=pltpu.CompilerParams(collective_id=cid, has_side_effects=True, vmem_limit_bytes=63 * 2**20),
        name="attend",
    )(lin, tot, near, far, gq, gk, q_seg, segments, w_own, x_in, gain, cot)


def attend_back_kernel(scale, pads, cut, d_n2, cot, gain, wo_h, p_out, residual, q_rot, kv, q_seg, segments, lse, o_ref, lin, tot, near, far, gq, gk, n2, a_h,
                       d_lin, d_gains, output, d_residual, d_gain, other_w, dg_o, du_o,
                       nt, left, ob, gt, fs, tsem, osem, ors, fsem, gsem, d_res, k_seg, P, wo, d_mine, d_out, d_q, d_k, d_v, other, got, d_un, sums, sums_all, inner,
                       lsem, msem, ssem, *bufs):
    net = Net(ssem)
    sc = Scatter(net, cut, P, bufs)
    u, z, c = net.u, net.z, net.c
    me = u * 4 + z
    rows, width = d_n2.shape
    reach = pads * 2 * rows
    partner = (u, z, 1 - c)
    load = pltpu.make_async_copy(wo_h, wo, lsem.at[0])
    load.start()
    load_p = pltpu.make_async_copy(p_out, P, lsem.at[1])
    load_p.start()
    greet(net)

    def go(words):
        run_steps(steps_of(sc, words))

    load_p.wait()
    go("m3 m0 m2 m1")
    d_gain[...] = jnp.zeros_like(d_gain)

    def norm_back(i, _):
        sl = pl.ds(pl.multiple_of(i * 16, 16), 16)
        v, d = residual[sl, :], d_n2[sl, :]
        r = lax.rsqrt(jnp.mean(v * v, axis=1, keepdims=True) + EPS)
        scaled = d * gain[...]
        mean = jnp.mean(scaled * v, axis=1, keepdims=True)
        total = wide(cot[sl, :]) + r * scaled - v * (r * r * r * mean)
        d_residual[sl, :] = total
        d_res[sl, :] = total.astype(BF)
        d_gain[...] += jnp.sum(d * v * r, axis=0, keepdims=True)
        return 0

    lax.fori_loop(0, rows // 16, norm_back, 0)
    segment_rows(segments, k_seg, reach)
    load.wait()

    def send(j, _):
        pair = lax.rem(me // 2 + 1 + j, 8)
        both = dot(d_res[...], wo[pair // 2, pl.ds(lax.rem(pair, 2) * 2, 2)].reshape(256, width), ((1,), (1,))).astype(BF)
        for i in (0, 1):
            e = pair * 2 + i
            d_mine[e] = both[:, i * 128 : (i + 1) * 128]

            @pl.when(e != me)
            def _():
                remote(d_mine.at[e], d_out.at[me], msem.at[0], msem.at[1], (e // 4, lax.rem(e, 4), c)).start()

        return 0

    lax.fori_loop(0, 8, send, 0)
    d_out[me] = d_mine[me]
    A = wo.reshape(16, rows, width)
    load_a = pltpu.make_async_copy(a_h, A, lsem.at[0])
    load_a.start()
    plan = [("o", 0), ("o", 1), ("o", 2), ("o", 3), ("w", 0), ("w", 1), ("w", 2), ("w", 3)]
    tile = 256

    def left_load(i):
        kind, k = plan[i]
        which = 1 - c if kind == "o" else c
        cols = pl.ds(pl.multiple_of((which * 4 + k) * tile, tile), tile)
        return pltpu.make_async_copy(n2.at[:, :, cols], nt.at[i % 2], tsem.at[i % 2])

    def left_turn(i):
        turned_into(left, nt.at[i % 2].reshape(16 * rows, tile), slice(None))

    left_load(0).start()
    made = A.reshape(16 * rows, width)
    dw, dw_end = weight_tiles(
        partner, plan, left_load, left_turn, lambda h, n: made[:, h * 1024 + n * 512 : h * 1024 + (n + 1) * 512], left,
        lambda k: ob.at[k % 2], gt, fs, other_w, osem, ors, fsem, gsem.at[0],
        lambda k, h: (dg_o, du_o)[h].at[pl.ds(k * tile, tile), :])
    d_k[...] = jnp.zeros_like(d_k)
    d_v[...] = jnp.zeros_like(d_v)
    landed(d_out.at[pl.ds(0, 15)], msem.at[1])
    count = (pads + 16) * 2 * rows

    def block(i, _):
        band = pl.ds(pl.multiple_of((2 * i + c) * rows, rows), rows + reach)
        kf, vf = kv.at[0].reshape(count, 128), kv.at[1].reshape(count, 128)
        q, k, dd = q_rot[i], kf[band, :], d_out[i]
        scores, allowed = band_scores(q, k, column(q_seg[pl.ds(i, 1), :])[:, 0:1], k_seg[:, band], scale, reach)
        probs = jnp.where(allowed, jnp.exp(scores - lse[i]), 0.0)
        d_probs = dot(dd, vf[band, :], ((1,), (1,)))
        delta = jnp.sum(dd.astype(F32) * o_ref[i].astype(F32), axis=1, keepdims=True)
        d_scores = (probs * (d_probs - delta)).astype(BF)
        d_q[i] = (dot(d_scores, k, ((1,), (0,))) * scale).astype(BF)
        d_k[band, :] += dot(d_scores, q, ((0,), (0,))) * scale
        d_v[band, :] += dot(probs.astype(BF), dd, ((0,), (0,)))
        return 0

    def store(sl, v):
        output[sl, :] = residual[sl, :] + v

    go("f3 f0 d3 d0")
    done = 0
    for upto, words in ((3, "M3 M0 M2 M1 d2 d1"), (6, "f2 f1"), (11, "b31 b02"), (16, "")):
        lax.fori_loop(done, upto, block, 0)
        go(words)
        done = upto

    def pack(i, _):
        at = pl.ds(pl.multiple_of(((pads + i) * 2 + 1 - c) * rows, rows), rows)
        other[0, i] = d_k[at, :].astype(BF)
        other[1, i] = d_v[at, :].astype(BF)
        return 0

    lax.fori_loop(0, 16, pack, 0)
    remote(other, got, msem.at[2], msem.at[3], partner).start()
    go("h30 h03")
    landed(got, msem.at[3])
    d_gains[...] = jnp.zeros_like(d_gains)

    def undo(i, _):
        at = pl.ds(pl.multiple_of(((pads + i) * 2 + c) * rows, rows), rows)
        cs, sn = rope_at(near, far, i)
        both = lin[i]
        rq = lax.rsqrt(column(tot[pl.ds(i, 1), :]) / width + EPS)
        rk = lax.rsqrt(column(tot[pl.ds(16 + i, 1), :]) / width + EPS)
        dk = (d_k[at, :] + wide(got[0, i])).astype(BF).astype(F32)
        d_lin[i, :, 256:] = (d_v[at, :] + wide(got[1, i])).astype(BF)
        uq = turned_back(wide(d_q[i]), cs, sn)
        uk = turned_back(dk, cs, sn)
        q, k = both[:, :128], both[:, 128:256]
        d_gains[0:1, :] += jnp.sum(uq * q * rq, axis=0, keepdims=True)
        d_gains[1:2, :] += jnp.sum(uk * k * rk, axis=0, keepdims=True)
        uq, uk = uq * gq[...], uk * gk[...]
        d_un[0, i] = uq
        d_un[1, i] = uk
        sums[pl.ds(i, 1), :] = row_sums(uq * q)
        sums[pl.ds(16 + i, 1), :] = row_sums(uk * k)
        return 0

    lax.fori_loop(0, 16, undo, 0)
    go("b21 b12 b32 b01")
    share_sums(net, sums, sums_all, inner, lsem.at[1], msem.at[4], msem.at[5])

    def finish(i, _):
        both = lin[i]
        for s in (0, 1):
            r = lax.rsqrt(column(tot[pl.ds(16 * s + i, 1), :]) / width + EPS)
            mean = column(inner[pl.ds(16 * s + i, 1), :]) / width
            own = both[:, 128 * s : 128 * (s + 1)]
            d_lin[i, :, 128 * s : 128 * (s + 1)] = (r * d_un[s, i] - own * (r * r * r * mean)).astype(BF)
        return 0

    lax.fori_loop(0, 16, finish, 0)
    load_a.wait()
    go("h31 h02")
    dw(0)
    dw(1)
    go("h20 h13 Q")
    dw(2)
    go("h32 h01")
    dw(3)
    dw(4)
    go("h10 h23")
    dw(5)
    go("h21 h12 q")
    dw(6)
    dw(7)
    sc.last(store)
    dw_end()
    landed(d_out.at[pl.ds(0, 15)], msem.at[0])
    landed(other, msem.at[2])
    net.finish()


def run_attend_back(scale, pads, d_n2, cot, gain, wo, p_out, residual, q_rot, kv, q_seg, segments, lse, o, lin, tot, near, far, gq, gk, n2, a_h, half, cid, cut=96):
    R, D = d_n2.shape
    DMA = pltpu.SemaphoreType.DMA
    S = jax.ShapeDtypeStruct
    A = pl.BlockSpec(memory_space=pl.ANY)
    M = pl.BlockSpec(memory_space=pltpu.VMEM)
    V = pltpu.VMEM
    span = (pads + 16) * 2 * R
    return pl.pallas_call(
        functools.partial(attend_back_kernel, scale, pads, cut),
        out_shape=(S((16, R, 384), BF), S((8, 128), F32), S((R, D), F32), S((R, D), F32), S((1, D), F32),
                   S((4, 256, D), BF), S(half, F32), S(half, F32)),
        in_specs=[M, M, M, A, A] + [M] * 13 + [A, A],
        out_specs=(M,) * 5 + (A,) * 3,
        scratch_shapes=[V((2, 16, R, 256), BF), V((256, 16 * R), BF), V((2, 256, D), BF), V((256, D), BF), V((2, 256, 1024), F32),
                        DMA((2,)), DMA((4,)), DMA((4,)), DMA((2,)), DMA((1,)), V((R, D), BF), V((1, span), F32), V((4, 4, R, D), BF), V(wo.shape, BF), V((16, R, 128), BF), V((16, R, 128), BF), V((16, R, 128), BF),
                        V((span, 128), F32), V((span, 128), F32), V((2, 16, R, 128), BF), V((2, 16, R, 128), BF),
                        V((2, 16, R, 128), F32), V((32, 128), F32), V((16, 32, 128), F32), V((32, 128), F32),
                        DMA((2,)), DMA((10,)), DMA((64,))] + rs_scratch(cut, R, D),
        compiler_params=pltpu.CompilerParams(collective_id=cid, has_side_effects=True, vmem_limit_bytes=63 * 2**20),
        name="attend_back",
    )(d_n2, cot, gain, wo, p_out, residual, q_rot, kv, q_seg, segments, lse, o, lin, tot, near, far, gq, gk, n2, a_h)
def dot(a, b, dims):
    return lax.dot_general(a, b, (dims, ((), ())), preferred_element_type=jnp.float32)


def local_chip(
    inputs, cotangent, segments, expert_ids, gate_weights, fill_order, norm1_gain, w_query, w_key,
    w_value, w_output, query_gain, key_gain, norm2_gain, expert_gate, expert_up, expert_down,
):
    chips = 16
    devices = 2 * chips
    rows, width = inputs.shape
    u, z, core = place()
    chip = u * 4 + z
    device = chip * 2 + core
    topk = expert_ids.shape[1]
    experts_n = chips
    capacity = 9 * rows * devices * topk // (8 * experts_n)
    one_hot = expert_ids[:, :, None] == jnp.arange(experts_n, dtype=jnp.int32)[None, None, :]
    chosen = jnp.any(one_hot, axis=1)
    weight = jnp.sum(jnp.where(one_hot, gate_weights[:, :, None], 0.0), axis=1)
    earlier = (fill_order[None, :] < fill_order[:, None]).astype(jnp.bfloat16)
    rank = dot(earlier, chosen.astype(jnp.bfloat16), ((1,), (0,)))
    rank = jnp.where(chosen, rank, -1.0)
    gains = jnp.stack([norm1_gain, query_gain, key_gain, norm2_gain]).astype(F32)
    blank = jnp.zeros_like(gains)
    gains = jnp.where(core == 0, jnp.concatenate([gains, blank], axis=1), jnp.concatenate([blank, gains], axis=1))
    gains = jnp.broadcast_to(gains[None], (chips, 4, 128))
    block = jnp.concatenate(
        [weight.T[:, None, :], rank.T[:, None, :], gains, jnp.zeros((chips, 2, 128), F32)], axis=1)
    side = width // 2
    n1_rows, lin, w_qkv, squares, swapped, cot_a = run_qkv(
        inputs, w_query, w_key, w_value, block, cotangent[:, :side], 2)
    gains = jnp.sum(swapped.reshape(chips, 2, 8, 128), axis=1)
    gain_one, gain_two = gains[:, 2].reshape(1, width), gains[:, 5].reshape(1, width)
    gq, gk = (lax.dynamic_slice_in_dim(gains[:, i], chip, 1, 0) for i in (3, 4))
    rank_all = swapped[:, 1, :]
    taken = rank_all >= 0.0
    counts = jnp.sum(taken.astype(F32), axis=1)
    before = jnp.cumsum(counts) - counts
    kept = taken & (before[:, None] + rank_all < float(capacity))
    share = jnp.where(kept, swapped[:, 0, :], 0.0).reshape(chips, 2, rows)
    share = lax.dynamic_index_in_dim(share, core, 1, keepdims=False)


    half_dim = HEAD_DIM // 2
    inv_freq = jnp.exp(jnp.arange(half_dim, dtype=F32) * (-2.0 * math.log(ROPE_BASE) / HEAD_DIM))
    inv_freq = jnp.concatenate([inv_freq, inv_freq])[None, :]
    sign = jnp.where(jnp.arange(HEAD_DIM) < half_dim, -1.0, 1.0)[None, :]
    within = jnp.arange(rows, dtype=F32)[:, None] * inv_freq
    starts = ((jnp.arange(chips, dtype=jnp.int32) * 2 + core) * rows).astype(F32)[:, None] * inv_freq
    near = jnp.stack([jnp.cos(within), sign * jnp.sin(within)])
    far = jnp.stack([jnp.cos(starts), sign * jnp.sin(starts)])
    pads = chips // 4
    marks = segments.astype(F32)
    q_seg = lax.dynamic_index_in_dim(marks.reshape(chips, 2, rows), core, 1, keepdims=False)
    marks = marks.reshape(1, -1)
    scale = 1.0 / math.sqrt(HEAD_DIM)
    tokens = chips * rows
    w_o, q_rot, kv, head_out, log_total, attended, residual, normed_two, cot_b = run_attend(
        scale, pads, lin, squares, near, far, gq, gk, q_seg, marks, w_output, inputs, gain_two, cotangent[:, side:], 4)

    d_normed_two, mixed, n2_rows, d_pre, _other, d_expert_down = run_expert(
        normed_two, cot_a, cot_b, share, expert_gate, expert_up, expert_down, 6)
    d_lin, d_qk_gains, output, d_residual, d_gain_two, _other, d_expert_gate, d_expert_up = run_attend_back(
        scale, pads, d_normed_two, cotangent, gain_two, w_o, mixed, residual, q_rot, kv, q_seg, marks, log_total, head_out,
        lin, squares, near, far, gq, gk, n2_rows.reshape(chips, rows, width), d_pre.reshape(chips, rows, -1), expert_gate.shape, 7)
    d_w_output, d_inputs, d_w_query, d_w_key, d_w_value, d_gains = run_finish(
        d_lin, w_qkv, n1_rows, attended, inputs, d_residual, gain_one, d_gain_two, d_qk_gains, 8)
    return (
        output,
        d_inputs,
        d_gains[0],
        d_w_query,
        d_w_key,
        d_w_value,
        d_w_output,
        d_gains[2],
        d_gains[3],
        d_gains[1],
        d_expert_gate,
        d_expert_up,
        d_expert_down,
    )
def whole(mesh, step, rows):
    return jax.shard_map(
        step,
        mesh=mesh,
        in_specs=(
            P(rows, None),
            P(rows, None),
            P(),
            P(rows, None),
            P(rows, None),
            P(rows),
            P(rows),
            P(rows, None),
            P(rows, None),
            P(rows, None),
            P(rows, None),
            P(rows),
            P(rows),
            P(rows),
            P(rows, None),
            P(rows, None),
            P(rows, None),
        ),
        out_specs=(
            P(rows, None),
            P(rows, None),
            P(rows),
            P(rows, None),
            P(rows, None),
            P(rows, None),
            P(rows, None),
            P(rows),
            P(rows),
            P(rows),
            P(rows, None),
            P(rows, None),
            P(rows, None),
        ),
        check_vma=False,
    )


def solution(mesh):
    groups, blk_size = mesh.shape["ulysses"], mesh.shape["blk"]

    def step(*args):
        if groups != 4 or blk_size != 8 or args[7].shape[1] // HEAD_DIM != groups * blk_size // 2:
            return whole(mesh, local, ("ulysses", "blk"))(*args)
        chips = Mesh(mesh.devices.reshape(groups, blk_size // 2, 2), ("ulysses", "z", "core"))
        return whole(chips, local_chip, ("ulysses", "z", "core"))(*args)

    return step
```

```python
import functools
import math

import jax
import jax.numpy as jnp
from jax import lax
from jax.experimental import pallas as pl
from jax.experimental.pallas import tpu as pltpu
from jax.sharding import Mesh
from jax.sharding import PartitionSpec as P

HEAD_DIM = 128


EPS = 1e-05
ROPE_BASE = 10000.0
NEG = -1e30


def as_sent(value):

    def short(part):
        return part.astype(jnp.bfloat16) if part.dtype == jnp.float32 else part

    return jax.tree.map(short, value)


def passed_along(block, axis, distance):
    devices = range(lax.axis_size(axis))
    route = [((i - distance) % len(devices), i) for i in devices]
    return lax.ppermute(block, axis, route)


def prefix(value, axis, join, neutral):
    count, mine = (lax.axis_size(axis), lax.axis_index(axis))
    pieces = lax.all_gather(value, axis)
    subtotal = jnp.full_like(value, 0) + jnp.asarray(neutral, value.dtype)

    def hop(position, subtotal):
        longer = join(subtotal, pieces[position])
        return jnp.where(position < mine, longer, subtotal)

    return lax.fori_loop(0, count - 1, hop, subtotal)


def partner_2(block, axis, bit):
    count = lax.axis_size(axis)
    route = []
    for low in range(count):
        high = low | 1 << bit
        if high != low and high < count:
            route += [(low, high), (high, low)]
    return lax.ppermute(block, axis, route)


def norm_rows(values, gain_vec):
    return values * lax.rsqrt(jnp.mean(values * values, axis=-1, keepdims=True) + EPS) * gain_vec


def rotate(values, positions):
    half_dim = HEAD_DIM // 2
    heads_here = values.shape[1] // HEAD_DIM
    inv_freq = jnp.exp(
        jnp.arange(half_dim, dtype=jnp.float32) * (-2.0 * math.log(ROPE_BASE) / HEAD_DIM)
    )
    angles = positions.astype(jnp.float32)[:, None] * inv_freq[None, :]
    cosine = jnp.cos(angles)[:, None, :]
    sin_t = jnp.sin(angles)[:, None, :]
    shaped = values.reshape(values.shape[0], heads_here, HEAD_DIM)
    lower_half = shaped[..., :half_dim]
    upper_half = shaped[..., half_dim:]
    turned = jnp.concatenate(
        [lower_half * cosine - upper_half * sin_t, upper_half * cosine + lower_half * sin_t],
        axis=-1,
    )
    return turned.reshape(values.shape)


def attn_inputs(q_lin, k_lin, gain_q, gain_k, positions):
    return (
        rotate(norm_rows(q_lin, gain_q), positions),
        rotate(norm_rows(k_lin, gain_k), positions),
    )


def banded(shaped, fill_value):
    earlier = jnp.concatenate([jnp.full_like(shaped[:1], fill_value), shaped[:-1]], axis=0)
    return jnp.concatenate([earlier, shaped], axis=1)


def unbanded(band, local_rows):
    earlier = band[:, :local_rows]
    own_part = band[:, local_rows:]
    moved_up = jnp.concatenate([earlier[1:], jnp.zeros_like(earlier[:1])], axis=0)
    return own_part + moved_up


def add_counts(earlier, later):
    return earlier + later


def expert_move(buffer):
    return lax.all_to_all(buffer, ("ulysses", "blk"), split_axis=0, concat_axis=0, tiled=True)


def to_head_layout(values):
    return jax.tree.map(
        lambda part, own: part.astype(own.dtype),
        lax.all_to_all(as_sent(values), "ulysses", split_axis=1, concat_axis=0, tiled=True),
        values,
    )


def to_token_layout(values):
    return jax.tree.map(
        lambda part, own: part.astype(own.dtype),
        lax.all_to_all(as_sent(values), "ulysses", split_axis=0, concat_axis=1, tiled=True),
        values,
    )


def local(
    inputs,
    cotangent,
    segments,
    expert_ids,
    gate_weights,
    fill_order,
    norm1_gain,
    w_query,
    w_key,
    w_value,
    w_output,
    query_gain,
    key_gain,
    norm2_gain,
    expert_gate,
    expert_up,
    expert_down,
):
    blk_size = lax.axis_size("blk")
    groups = lax.axis_size("ulysses")
    devices = blk_size * groups
    local_rows = inputs.shape[0]
    model_width = inputs.shape[1]
    blk_index = lax.axis_index("blk")
    group_index = lax.axis_index("ulysses")
    device_index = group_index * blk_size + blk_index
    positions = device_index * local_rows + jnp.arange(local_rows, dtype=jnp.int32)
    heads_dev = model_width // groups // HEAD_DIM
    score_scale = 1.0 / math.sqrt(HEAD_DIM)
    layer_in = inputs.astype(jnp.float32)
    dense = (w_query, w_key, w_value, w_output, norm1_gain, query_gain, key_gain, norm2_gain)
    gathered = (
        lax.all_gather(dense[0], ("ulysses", "blk"), axis=0, tiled=True),
        lax.all_gather(dense[1], ("ulysses", "blk"), axis=0, tiled=True),
        lax.all_gather(dense[2], ("ulysses", "blk"), axis=0, tiled=True),
        lax.all_gather(dense[3], ("ulysses", "blk"), axis=0, tiled=True),
        lax.all_gather(dense[4], ("ulysses", "blk"), axis=0, tiled=True),
        lax.all_gather(dense[5], ("ulysses", "blk"), axis=0, tiled=True),
        lax.all_gather(dense[6], ("ulysses", "blk"), axis=0, tiled=True),
        lax.all_gather(dense[7], ("ulysses", "blk"), axis=0, tiled=True),
    )
    w_q, w_k, w_v, w_o = (gathered[0], gathered[1], gathered[2], gathered[3])
    gain_one = gathered[4].astype(jnp.float32)
    gain_q = gathered[5].astype(jnp.float32)
    gain_k = gathered[6].astype(jnp.float32)
    gain_two = gathered[7].astype(jnp.float32)
    normed_one = norm_rows(layer_in, gain_one).astype(jnp.bfloat16)
    q_lin = jnp.dot(normed_one, w_q, preferred_element_type=jnp.float32)
    k_lin = jnp.dot(normed_one, w_k, preferred_element_type=jnp.float32)
    v_lin = jnp.dot(normed_one, w_v, preferred_element_type=jnp.float32)
    (q_rot, k_rot), pre_back = jax.vjp(
        lambda q_in, k_in, gq_in, gk_in: attn_inputs(q_in, k_in, gq_in, gk_in, positions),
        q_lin,
        k_lin,
        gain_q,
        gain_k,
    )
    q_heads, k_heads, v_heads = to_head_layout(
        (q_rot.astype(jnp.bfloat16), k_rot.astype(jnp.bfloat16), v_lin.astype(jnp.bfloat16))
    )
    group_ids = jnp.arange(groups, dtype=jnp.int32)[:, None]
    row_ids = jnp.arange(local_rows, dtype=jnp.int32)[None, :]
    q_pos = (group_ids * blk_size + blk_index) * local_rows + row_ids
    q_seg = segments[q_pos]
    four_shape = (groups, local_rows, heads_dev, HEAD_DIM)
    q_four = q_heads.reshape(four_shape)

    def score_block(k_now, source):
        k_pos = (group_ids * blk_size + source) * local_rows + row_ids
        k_seg = banded(segments[k_pos], -1)
        k_pos = banded(k_pos, 0)
        k_band = banded(k_now.reshape(four_shape), 0)
        raw_scores = (
            jnp.einsum("gqhd,gkhd->gqhk", q_four, k_band, preferred_element_type=jnp.float32)
            * score_scale
        )
        allowed = (k_seg[:, None, :] == q_seg[:, :, None]) & (
            k_pos[:, None, :] <= q_pos[:, :, None]
        )
        return (raw_scores, allowed[:, :, None, :], k_band)

    def forward_step(flash_state, kv_stack, step_id):
        run_max, run_sum, run_out = flash_state
        source = jnp.mod(blk_index - step_id, blk_size)
        raw_scores, allowed, k_band = score_block(kv_stack[0], source)
        raw_scores = jnp.where(allowed, raw_scores, NEG)
        new_max = jnp.maximum(run_max, jnp.max(raw_scores, axis=-1))
        shrink = jnp.exp(run_max - new_max)
        weights = jnp.where(allowed, jnp.exp(raw_scores - new_max[..., None]), 0.0)
        run_sum = run_sum * shrink + jnp.sum(weights, axis=-1)
        v_band = banded(kv_stack[1].reshape(four_shape), 0)
        run_out = run_out * shrink[..., None] + jnp.einsum(
            "gqhk,gkhd->gqhd",
            weights.astype(jnp.bfloat16),
            v_band,
            preferred_element_type=jnp.float32,
        )
        return (new_max, run_sum, run_out)

    start_state = (
        jnp.full((groups, local_rows, heads_dev), NEG, jnp.float32),
        jnp.zeros((groups, local_rows, heads_dev), jnp.float32),
        jnp.zeros(four_shape, jnp.float32),
    )
    kv_home = jnp.stack([k_heads, v_heads])
    first_state = forward_step(start_state, kv_home, 0)

    def forward_turn(step_id, loop_state):
        flash_state, kv_stack = loop_state
        moved = passed_along(kv_stack, "blk", 1)
        return (forward_step(flash_state, moved, step_id), moved)

    final_state, unused_kv = lax.fori_loop(1, blk_size, forward_turn, (first_state, kv_home))
    run_max, run_sum, run_out = final_state
    o_four = (run_out / run_sum[..., None]).astype(jnp.bfloat16)
    log_total = run_max + jnp.log(run_sum)
    o_heads = o_four.reshape(groups * local_rows, heads_dev * HEAD_DIM)
    attended = to_token_layout(o_heads)
    residual = layer_in + jnp.dot(attended, w_o, preferred_element_type=jnp.float32)
    normed_two_f, norm_two_back = jax.vjp(norm_rows, residual, gain_two)
    normed_two = normed_two_f.astype(jnp.bfloat16)
    experts_n = devices // 2
    topk = expert_ids.shape[1]
    per_source = 2 * local_rows * topk // experts_n
    half_slots = per_source // 2
    capacity = 9 * local_rows * devices * topk // (8 * experts_n)
    slots_all = experts_n * per_source
    tokens_local = jnp.arange(local_rows, dtype=jnp.int32)
    chosen = jnp.sum(
        (expert_ids[:, :, None] == jnp.arange(experts_n, dtype=jnp.int32)[None, None, :]).astype(
            jnp.int32
        ),
        axis=1,
    )
    by_fill = jnp.zeros((local_rows,), jnp.int32).at[fill_order].set(tokens_local)
    sorted_rows = chosen[by_fill]
    before = jnp.cumsum(sorted_rows, axis=0) - sorted_rows
    rank_all = before[fill_order]
    pair_rank = jnp.take_along_axis(rank_all, expert_ids, axis=1)
    counts = jnp.sum(chosen, axis=0)
    offsets = prefix(counts, ("ulysses", "blk"), add_counts, jnp.zeros_like(counts))
    kept_pair = offsets[expert_ids] + pair_rank < capacity
    pair_slot = expert_ids * per_source + pair_rank
    pair_index = tokens_local[:, None] * topk + jnp.arange(topk, dtype=jnp.int32)[None, :]
    slot_pair = (
        jnp.zeros((slots_all,), jnp.int32).at[pair_slot.reshape(-1)].set(pair_index.reshape(-1))
    )
    slot_live = (
        jnp.zeros((slots_all,), jnp.bool_).at[pair_slot.reshape(-1)].set(kept_pair.reshape(-1))
    )
    slot_token = slot_pair // topk
    send_rows = jnp.where(slot_live[:, None], normed_two[slot_token], jnp.zeros((), jnp.bfloat16))
    received = expert_move(send_rows.reshape(devices, half_slots, model_width)).reshape(
        devices * half_slots, model_width
    )
    parity = jnp.mod(blk_index, 2)
    partner = partner_2((expert_gate, expert_up, expert_down), "blk", 0)

    def joined(own_half, other_half):
        lower_part = jnp.where(parity == 0, own_half, other_half)
        upper_part = jnp.where(parity == 0, other_half, own_half)
        return jnp.concatenate([lower_part, upper_part], axis=0)

    gate_full = joined(expert_gate, partner[0])
    up_full = joined(expert_up, partner[1])
    down_full = joined(expert_down, partner[2])
    gate_pre = jnp.dot(received, gate_full, preferred_element_type=jnp.float32)
    up_pre = jnp.dot(received, up_full, preferred_element_type=jnp.float32)
    hidden = (jax.nn.silu(gate_pre) * up_pre).astype(jnp.bfloat16)
    produced = jnp.dot(hidden, down_full, preferred_element_type=jnp.float32).astype(jnp.bfloat16)
    returned = expert_move(produced.reshape(devices, half_slots, model_width)).reshape(
        slots_all, model_width
    )
    pair_share = jnp.where(kept_pair, gate_weights, 0.0)
    mixed = jnp.einsum("tk,tkd->td", pair_share, returned[pair_slot].astype(jnp.float32))
    output = residual + mixed
    grad_out = cotangent.astype(jnp.float32)
    slot_share = jnp.where(slot_live, gate_weights.reshape(-1)[slot_pair], 0.0)
    grad_send = (slot_share[:, None] * grad_out[slot_token]).astype(jnp.bfloat16)
    grad_rows = expert_move(grad_send.reshape(devices, half_slots, model_width)).reshape(
        devices * half_slots, model_width
    )
    d_down_full = jnp.einsum("rf,rd->fd", hidden, grad_rows, preferred_element_type=jnp.float32)
    d_hidden = jnp.einsum("rd,fd->rf", grad_rows, down_full, preferred_element_type=jnp.float32)
    sigma = jax.nn.sigmoid(gate_pre)
    d_gate_pre = (d_hidden * up_pre * sigma * (1.0 + gate_pre * (1.0 - sigma))).astype(jnp.bfloat16)
    d_up_pre = (d_hidden * gate_pre * sigma).astype(jnp.bfloat16)
    d_gate_full = jnp.einsum("rd,rf->df", received, d_gate_pre, preferred_element_type=jnp.float32)
    d_up_full = jnp.einsum("rd,rf->df", received, d_up_pre, preferred_element_type=jnp.float32)
    d_pair_rows = (
        jnp.einsum("rf,df->rd", d_gate_pre, gate_full, preferred_element_type=jnp.float32)
        + jnp.einsum("rf,df->rd", d_up_pre, up_full, preferred_element_type=jnp.float32)
    ).astype(jnp.bfloat16)
    back_rows = expert_move(d_pair_rows.reshape(devices, half_slots, model_width)).reshape(
        slots_all, model_width
    )
    d_normed_two = jnp.sum(
        jnp.where(kept_pair[:, :, None], back_rows[pair_slot].astype(jnp.float32), 0.0), axis=1
    )
    half_rows = expert_gate.shape[0]
    half_hidden = expert_down.shape[0]

    def halves(full_grad, size):
        own_half = lax.dynamic_slice_in_dim(full_grad, parity * size, size, 0)
        other_half = lax.dynamic_slice_in_dim(full_grad, (1 - parity) * size, size, 0)
        return (own_half, other_half)

    gate_own, gate_other = halves(d_gate_full, half_rows)
    up_own, up_other = halves(d_up_full, half_rows)
    down_own, down_other = halves(d_down_full, half_hidden)
    partner_grads = (
        partner_2(gate_other.astype(jnp.bfloat16), "blk", 0).astype(gate_other.dtype),
        partner_2(up_other.astype(jnp.bfloat16), "blk", 0).astype(up_other.dtype),
        partner_2(down_other.astype(jnp.bfloat16), "blk", 0).astype(down_other.dtype),
    )
    d_expert_gate = gate_own + partner_grads[0]
    d_expert_up = up_own + partner_grads[1]
    d_expert_down = down_own + partner_grads[2]
    d_resid_norm, d_gain_two = norm_two_back(d_normed_two)
    d_residual = grad_out + d_resid_norm
    d_res_low = d_residual.astype(jnp.bfloat16)
    d_attended = jnp.einsum("te,de->td", d_res_low, w_o, preferred_element_type=jnp.float32).astype(
        jnp.bfloat16
    )
    d_o_heads = to_head_layout(d_attended)
    d_o_four = d_o_heads.reshape(four_shape)
    row_delta = jnp.sum(d_o_four.astype(jnp.float32) * o_four.astype(jnp.float32), axis=-1)

    def back_turn(step_id, loop_state):
        moving, dq_acc = loop_state
        source = jnp.mod(blk_index - step_id, blk_size)
        k_now = moving[0].astype(jnp.bfloat16)
        v_now = moving[1].astype(jnp.bfloat16)
        raw_scores, allowed, k_band = score_block(k_now, source)
        prob_rows = jnp.where(allowed, jnp.exp(raw_scores - log_total[..., None]), 0.0)
        v_band = banded(v_now.reshape(four_shape), 0)
        d_probs = jnp.einsum(
            "gqhd,gkhd->gqhk", d_o_four, v_band, preferred_element_type=jnp.float32
        )
        d_scores = (prob_rows * (d_probs - row_delta[..., None])).astype(jnp.bfloat16)
        dv_band = jnp.einsum(
            "gqhk,gqhd->gkhd",
            prob_rows.astype(jnp.bfloat16),
            d_o_four,
            preferred_element_type=jnp.float32,
        )
        dk_band = (
            jnp.einsum("gqhk,gqhd->gkhd", d_scores, q_four, preferred_element_type=jnp.float32)
            * score_scale
        )
        dq_acc = (
            dq_acc
            + jnp.einsum("gqhk,gkhd->gqhd", d_scores, k_band, preferred_element_type=jnp.float32)
            * score_scale
        )
        flat_shape = moving[2].shape
        dk_new = moving[2] + unbanded(dk_band, local_rows).reshape(flat_shape)
        dv_new = moving[3] + unbanded(dv_band, local_rows).reshape(flat_shape)
        moving = passed_along(
            jnp.stack([moving[0], moving[1], dk_new, dv_new]).astype(jnp.bfloat16), "blk", 1
        ).astype(jnp.float32)
        return (moving, dq_acc)

    zero_rows = jnp.zeros(k_heads.shape, jnp.float32)
    start_moving = jnp.stack(
        [k_heads.astype(jnp.float32), v_heads.astype(jnp.float32), zero_rows, zero_rows]
    )
    moving, dq_acc = lax.fori_loop(
        0, blk_size, back_turn, (start_moving, jnp.zeros(four_shape, jnp.float32))
    )
    d_q_send = dq_acc.astype(jnp.bfloat16).reshape(k_heads.shape)
    d_k_send = moving[2].astype(jnp.bfloat16)
    d_v_send = moving[3].astype(jnp.bfloat16)
    d_q_rot, d_k_rot, d_v_lin = to_token_layout((d_q_send, d_k_send, d_v_send))
    d_q_lin, d_k_lin, d_gain_q, d_gain_k = pre_back(
        (d_q_rot.astype(jnp.float32), d_k_rot.astype(jnp.float32))
    )
    d_q_low = d_q_lin.astype(jnp.bfloat16)
    d_k_low = d_k_lin.astype(jnp.bfloat16)
    d_normed_one = jnp.einsum("te,de->td", d_q_low, w_q, preferred_element_type=jnp.float32)
    d_normed_one = d_normed_one + jnp.einsum(
        "te,de->td", d_k_low, w_k, preferred_element_type=jnp.float32
    )
    d_normed_one = d_normed_one + jnp.einsum(
        "te,de->td", d_v_lin, w_v, preferred_element_type=jnp.float32
    )
    unused_norm, norm_one_back = jax.vjp(norm_rows, layer_in, gain_one)
    d_layer_in, d_gain_one = norm_one_back(d_normed_one)
    d_inputs = d_residual + d_layer_in
    d_qk_heads = to_head_layout((d_q_low, d_k_low))
    rows_all = (
        lax.all_gather(normed_one, "ulysses", axis=0, tiled=True),
        lax.all_gather(d_res_low, "ulysses", axis=0, tiled=True),
    )
    head_cols = model_width // groups
    piece_rows = model_width // devices

    def by_owner(part):
        rest = part.shape[1:]
        shaped = part.reshape((groups, blk_size, piece_rows) + rest)
        return jnp.swapaxes(shaped, 0, 1).reshape((model_width,) + rest)

    part_q = jnp.einsum("td,te->de", rows_all[0], d_qk_heads[0], preferred_element_type=jnp.float32)
    part_k = jnp.einsum("td,te->de", rows_all[0], d_qk_heads[1], preferred_element_type=jnp.float32)
    part_v = jnp.einsum("td,te->de", rows_all[0], d_v_send, preferred_element_type=jnp.float32)
    part_o = jnp.einsum("te,td->ed", o_heads, rows_all[1], preferred_element_type=jnp.float32)
    blk_sums = (
        lax.psum_scatter(
            by_owner(part_q).astype(jnp.bfloat16), "blk", scatter_dimension=0, tiled=True
        ).astype(jnp.float32),
        lax.psum_scatter(
            by_owner(part_k).astype(jnp.bfloat16), "blk", scatter_dimension=0, tiled=True
        ).astype(jnp.float32),
        lax.psum_scatter(
            by_owner(part_v).astype(jnp.bfloat16), "blk", scatter_dimension=0, tiled=True
        ).astype(jnp.float32),
        lax.psum_scatter(
            part_o.astype(jnp.bfloat16), "blk", scatter_dimension=0, tiled=True
        ).astype(jnp.float32),
        lax.psum_scatter(
            by_owner(d_gain_one).astype(jnp.bfloat16), "blk", scatter_dimension=0, tiled=True
        ).astype(jnp.float32),
        lax.psum_scatter(
            by_owner(d_gain_q).astype(jnp.bfloat16), "blk", scatter_dimension=0, tiled=True
        ).astype(jnp.float32),
        lax.psum_scatter(
            by_owner(d_gain_k).astype(jnp.bfloat16), "blk", scatter_dimension=0, tiled=True
        ).astype(jnp.float32),
        lax.psum_scatter(
            by_owner(d_gain_two).astype(jnp.bfloat16), "blk", scatter_dimension=0, tiled=True
        ).astype(jnp.float32),
    )

    def widened(part):
        return lax.dynamic_update_slice_in_dim(
            jnp.zeros((part.shape[0], model_width), jnp.float32), part, group_index * head_cols, 1
        )

    col_sums = (
        lax.psum_scatter(
            widened(blk_sums[0]).astype(jnp.bfloat16), "ulysses", scatter_dimension=0, tiled=True
        ).astype(jnp.float32),
        lax.psum_scatter(
            widened(blk_sums[1]).astype(jnp.bfloat16), "ulysses", scatter_dimension=0, tiled=True
        ).astype(jnp.float32),
        lax.psum_scatter(
            widened(blk_sums[2]).astype(jnp.bfloat16), "ulysses", scatter_dimension=0, tiled=True
        ).astype(jnp.float32),
        lax.psum_scatter(
            blk_sums[4].astype(jnp.bfloat16), "ulysses", scatter_dimension=0, tiled=True
        ).astype(jnp.float32),
        lax.psum_scatter(
            blk_sums[5].astype(jnp.bfloat16), "ulysses", scatter_dimension=0, tiled=True
        ).astype(jnp.float32),
        lax.psum_scatter(
            blk_sums[6].astype(jnp.bfloat16), "ulysses", scatter_dimension=0, tiled=True
        ).astype(jnp.float32),
        lax.psum_scatter(
            blk_sums[7].astype(jnp.bfloat16), "ulysses", scatter_dimension=0, tiled=True
        ).astype(jnp.float32),
    )
    result_grads = (
        col_sums[0],
        col_sums[1],
        col_sums[2],
        blk_sums[3],
        col_sums[3],
        col_sums[4],
        col_sums[5],
        col_sums[6],
    )
    return (
        output,
        d_inputs,
        result_grads[4],
        result_grads[0],
        result_grads[1],
        result_grads[2],
        result_grads[3],
        result_grads[5],
        result_grads[6],
        result_grads[7],
        d_expert_gate,
        d_expert_up,
        d_expert_down,
    )


MESH = pl.DeviceIdType.MESH
P1 = 96

def place():
    u = lax.axis_index("ulysses"); z = lax.axis_index("z"); c = lax.axis_index("core")
    return u, z, c

def ag_kernel(cut, x_ref, o_ref, local_sem, s_sem, zr, xr, yr, d1r, d2r, bs, br, bzr):
    u, z, c = place()
    Z = 4
    R = x_ref.shape[0]
    ux, uy = u ^ 1, u ^ 2
    xn, yn, up, dn = (ux, z, c), (uy, z, c), (u, z + 1, c), (u, z - 1, c)
    has_up, has_dn = z < Z - 1, z > 0
    bar = pltpu.get_barrier_semaphore()
    for n in (xn, yn):
        pl.semaphore_signal(bar, inc=1, device_id=n, device_id_type=MESH)
    @pl.when(has_up)
    def _():
        pl.semaphore_signal(bar, inc=1, device_id=up, device_id_type=MESH)
    @pl.when(has_dn)
    def _():
        pl.semaphore_signal(bar, inc=1, device_id=dn, device_id_type=MESH)
    pl.semaphore_wait(bar, 2 + has_up.astype(jnp.int32) + has_dn.astype(jnp.int32))
    sends = []
    def copy(src, dst, ss, rs, dev):
        return pltpu.make_async_remote_copy(src_ref=src, dst_ref=dst, send_sem=ss, recv_sem=rs, device_id=dev, device_id_type=MESH)
    def go(cond, make):
        idx = len(sends)
        def mk():
            return make(s_sem.at[idx])
        sends.append((cond, mk))
        if cond is None:
            mk().start()
        else:
            pl.when(cond)(lambda: mk().start())
    def both(a, b):
        if a is None: return b
        if b is None: return a
        return jnp.logical_and(a, b)
    def wait(cond, ref, sem):
        def w():
            pltpu.make_async_copy(ref, ref, sem).wait()
        if cond is None: w()
        else: pl.when(cond)(w)
    own = pltpu.make_async_copy(x_ref, o_ref.at[u, z], local_sem)
    own.start()
    A = slice(0, cut)
    h = cut // 2
    def oa(uu, zz, lo=0, n=cut):
        return o_ref.at[uu, zz, pl.ds(lo, n), :]
    def spread(s, zz, cond):
        src = (lambda: x_ref.at[pl.ds(0, cut), :]) if s == 0 else (lambda: oa(u, zz))
        go(cond, lambda sm: copy(src(), oa(u, zz), sm, xr.at[zz], xn))
        go(cond, lambda sm: copy(src(), oa(u, zz), sm, yr.at[zz], yn))
    def cross(zz, cond):
        wait(cond, oa(ux, zz), xr.at[zz])
        go(cond, lambda sm: copy(oa(ux, zz, 0, h), oa(ux, zz, 0, h), sm, d1r.at[zz], yn))
        wait(cond, oa(uy, zz), yr.at[zz])
        go(cond, lambda sm: copy(oa(uy, zz, h, h), oa(uy, zz, h, h), sm, d2r.at[zz], xn))
    rb = R - cut
    hb = rb // 2
    def ob(uu, zz, lo=0, n=None):
        return o_ref.at[uu, zz, pl.ds(cut + lo, rb if n is None else n), :]
    go(has_up, lambda sm: copy(x_ref.at[pl.ds(0, cut), :], oa(u, z), sm, zr.at[z], up))
    go(has_dn, lambda sm: copy(x_ref.at[pl.ds(0, cut), :], oa(u, z), sm, zr.at[z], dn))
    if rb:
        go(None, lambda sm: copy(x_ref.at[pl.ds(cut, rb), :], ob(u, z), sm, br.at[0], xn))
        go(None, lambda sm: copy(x_ref.at[pl.ds(cut, rb), :], ob(u, z), sm, br.at[1], yn))
    spread(0, z, None)
    if rb:
        wait(None, ob(ux, z), br.at[0])
        go(None, lambda sm: copy(ob(ux, z, 0, hb), ob(ux, z, 0, hb), sm, br.at[2], yn))
        wait(None, ob(uy, z), br.at[1])
        go(None, lambda sm: copy(ob(uy, z, hb, hb), ob(uy, z, hb, hb), sm, br.at[3], xn))
    own.wait()
    def quad(zz):
        return o_ref.at[:, zz, pl.ds(cut, rb), :]
    def zs(s):
        zl, zh = z - s, z + s
        cl, ch = zl >= 0, zh < Z
        zlc, zhc = jnp.maximum(zl, 0), jnp.minimum(zh, Z - 1)
        return (zlc, cl, has_up, up), (zhc, ch, has_dn, dn)
    prev = [(z, None)]
    for s in range(1, Z):
        cur = []
        for (zz, cond, fwd, dev) in zs(s):
            wait(cond, oa(u, zz), zr.at[zz])
            go(both(cond, fwd), lambda sm, zz=zz, dev=dev: copy(oa(u, zz), oa(u, zz), sm, zr.at[zz], dev))
            spread(s, zz, cond)
            cur.append((zz, cond))
        if rb and s == 1:
            wait(None, ob(u ^ 3, z, 0, hb), br.at[2])
            wait(None, ob(u ^ 3, z, hb, hb), br.at[3])
            go(has_up, lambda sm: copy(quad(z), quad(z), sm, bzr.at[z], up))
            go(has_dn, lambda sm: copy(quad(z), quad(z), sm, bzr.at[z], dn))
        elif rb:
            for (zz, cond, fwd, dev) in zs(s - 1):
                wait(cond, quad(zz), bzr.at[zz])
                go(both(cond, fwd), lambda sm, zz=zz, dev=dev: copy(quad(zz), quad(zz), sm, bzr.at[zz], dev))
        for zz, cond in prev:
            cross(zz, cond)
        prev = cur
    if rb:
        for (zz, cond, fwd, dev) in zs(Z - 1):
            wait(cond, quad(zz), bzr.at[zz])
    for zz, cond in prev:
        cross(zz, cond)
    for zz in range(Z):
        wait(None, oa(u ^ 3, zz, 0, h), d1r.at[zz])
        wait(None, oa(u ^ 3, zz, h, h), d2r.at[zz])
    for cond, mk in sends:
        if cond is None: mk().wait_send()
        else: pl.when(cond)(lambda mk=mk: mk().wait_send())

def ag16(x, cid, cut=P1, space=pl.ANY):
    R, D = x.shape
    DMA = pltpu.SemaphoreType.DMA
    return pl.pallas_call(
        functools.partial(ag_kernel, cut),
        out_shape=jax.ShapeDtypeStruct((4, 4, R, D), x.dtype),
        in_specs=[pl.BlockSpec(memory_space=space)],
        out_specs=pl.BlockSpec(memory_space=space),
        scratch_shapes=[DMA, DMA((64,)), DMA((4,)), DMA((4,)), DMA((4,)), DMA((4,)), DMA((4,)), DMA((4,)), DMA((4,)), DMA((4,))],
        compiler_params=pltpu.CompilerParams(collective_id=cid, has_side_effects=True, vmem_limit_bytes=48 * 2**20),
        name="gather_rows",
    )(x)
F32 = jnp.float32
BF = jnp.bfloat16


class Net:
    def __init__(self, sems):
        self.sems, self.sends = sems, []
        self.u, self.z, self.c = place()
        u, z, c = self.u, self.z, self.c
        self.ux, self.uy, self.ud = u ^ 1, u ^ 2, u ^ 3
        self.xn, self.yn, self.up, self.dn = (u ^ 1, z, c), (u ^ 2, z, c), (u, z + 1, c), (u, z - 1, c)
        self.has_up, self.has_dn = z < 3, z > 0
        self.at = [z == i for i in range(4)]

    def barrier(self, more=()):
        bar = pltpu.get_barrier_semaphore()
        for n in (self.xn, self.yn) + tuple(more):
            pl.semaphore_signal(bar, inc=1, device_id=n, device_id_type=MESH)
        for cond, n in ((self.has_up, self.up), (self.has_dn, self.dn)):
            pl.when(cond)(lambda n=n: pl.semaphore_signal(bar, inc=1, device_id=n, device_id_type=MESH))
        pl.semaphore_wait(bar, 2 + len(more) + self.has_up.astype(jnp.int32) + self.has_dn.astype(jnp.int32))

    def go(self, cond, src, dst, rsem, dev):
        idx = len(self.sends)

        def mk():
            return pltpu.make_async_remote_copy(
                src_ref=src(), dst_ref=dst(), send_sem=self.sems.at[idx], recv_sem=rsem(),
                device_id=dev, device_id_type=MESH)

        self.sends.append((cond, mk))
        if cond is None:
            mk().start()
        else:
            pl.when(cond)(lambda: mk().start())

    def wait(self, cond, ref, sem):
        def w():
            pltpu.make_async_copy(ref(), ref(), sem).wait()

        if cond is None:
            w()
        else:
            pl.when(cond)(w)

    def finish(self):
        for cond, mk in self.sends:
            if cond is None:
                mk().wait_send()
            else:
                pl.when(cond)(lambda mk=mk: mk().wait_send())


def strips(rows, body, step=16):
    def it(i, _):
        body(pl.ds(pl.multiple_of(i * step, step), step))
        return 0

    lax.fori_loop(0, rows // step, it, 0)


def wide(v):
    return v.astype(F32)


class Scatter:
    def __init__(self, net, cut, P, bufs):
        self.net, self.cut, self.P = net, cut, P
        (self.mid1, self.mid2, self.fx, self.fy, self.be, self.ab, self.bbe, self.bab, self.bm,
         self.m1s, self.m2s, self.fxs, self.fys, self.bes, self.abs_, self.bbes, self.babs, self.bms) = bufs
        self.R = P.shape[2]
        self.h = cut // 2
        self.rb = self.R - cut
        self.hb = self.rb // 2

    def mid_send(self, zd):
        net, P, h = self.net, self.P, self.h
        net.go(None, lambda: P.at[net.ud, zd, pl.ds(0, h), :], lambda: self.mid1.at[zd], lambda: self.m1s.at[zd], net.xn)
        net.go(None, lambda: P.at[net.ud, zd, pl.ds(h, h), :], lambda: self.mid2.at[zd], lambda: self.m2s.at[zd], net.yn)

    def bfirst(self, zd):
        net, P, cut, rb = self.net, self.P, self.cut, self.rb
        if rb and zd > 0:
            net.go(net.at[0], lambda: P.at[:, zd, pl.ds(cut, rb), :], lambda: self.bbe.at[zd], lambda: self.bbes.at[zd], net.up)
        if rb and zd < 3:
            net.go(net.at[3], lambda: P.at[:, zd, pl.ds(cut, rb), :], lambda: self.bab.at[zd], lambda: self.babs.at[zd], net.dn)

    def direct(self, zd):
        net, P, h = self.net, self.P, self.h
        net.go(None, lambda: P.at[net.ux, zd, pl.ds(0, h), :], lambda: self.fx.at[zd, pl.ds(0, h), :], lambda: self.fxs.at[zd, 0], net.xn)
        net.go(None, lambda: P.at[net.uy, zd, pl.ds(h, h), :], lambda: self.fy.at[zd, pl.ds(h, h), :], lambda: self.fys.at[zd, 1], net.yn)

    def first(self, zd):
        self.mid_send(zd)
        self.bfirst(zd)
        self.direct(zd)

    def mids(self, zd):
        net, P, h, mid1, mid2 = self.net, self.P, self.h, self.mid1, self.mid2

        def add1(sl):
            mid1[zd, sl, :] = (wide(mid1[zd, sl, :]) + wide(P[net.uy, zd, sl, :])).astype(BF)

        def add2(sl):
            mid2[zd, sl, :] = (wide(mid2[zd, sl, :]) + wide(P[net.ux, zd, pl.ds(h + sl.start, 16), :])).astype(BF)

        net.wait(None, lambda: mid1.at[zd], self.m1s.at[zd])
        strips(h, add1)
        net.go(None, lambda: mid1.at[zd], lambda: self.fy.at[zd, pl.ds(0, h), :], lambda: self.fys.at[zd, 0], net.yn)
        net.wait(None, lambda: mid2.at[zd], self.m2s.at[zd])
        strips(h, add2)
        net.go(None, lambda: mid2.at[zd], lambda: self.fx.at[zd, pl.ds(h, h), :], lambda: self.fxs.at[zd, 1], net.xn)

    def route(self, zd, zz):
        if zz < zd:
            return True, self.net.up
        return False, self.net.dn

    def bhop(self, zd, zz):
        net, P, cut, rb = self.net, self.P, self.cut, self.rb
        if not rb:
            return
        upward, dev = self.route(zd, zz)
        buf, sems = (self.bbe, self.bbes) if upward else (self.bab, self.babs)
        here = net.at[zz]
        net.wait(here, lambda: buf.at[zd], sems.at[zd])

        def add():
            for q in range(4):
                def one(sl, q=q):
                    buf[zd, q, sl, :] = (wide(buf[zd, q, sl, :]) + wide(P[q, zd, pl.ds(cut + sl.start, 16), :])).astype(BF)
                strips(rb, one)

        pl.when(here)(add)
        net.go(here, lambda: buf.at[zd], lambda: buf.at[zd], lambda: sems.at[zd], dev)

    def square(self, zd, cond):
        net, h = self.net, self.h
        for half in (0, 1):
            net.wait(cond, lambda: self.fx.at[zd, pl.ds(half * h, h), :], self.fxs.at[zd, half])
            net.wait(cond, lambda: self.fy.at[zd, pl.ds(half * h, h), :], self.fys.at[zd, half])

    def local(self, zd, sl):
        return wide(self.P[self.net.u, zd, sl, :]) + wide(self.fx[zd, sl, :]) + wide(self.fy[zd, sl, :])

    def hop(self, zd, zz):
        net = self.net
        upward, dev = self.route(zd, zz)
        buf, sems = (self.be, self.bes) if upward else (self.ab, self.abs_)
        here = net.at[zz]
        self.square(zd, here)
        if zz in (0, 3):
            def begin(sl):
                self.fx[zd, sl, :] = self.local(zd, sl).astype(BF)

            pl.when(here)(lambda: strips(self.cut, begin))
            net.go(here, lambda: self.fx.at[zd], lambda: buf.at[zd], lambda: sems.at[zd], dev)
        else:
            def plus(sl):
                buf[zd, sl, :] = (self.local(zd, sl) + wide(buf[zd, sl, :])).astype(BF)

            net.wait(here, lambda: buf.at[zd], sems.at[zd])
            pl.when(here)(lambda: strips(self.cut, plus))
            net.go(here, lambda: buf.at[zd], lambda: buf.at[zd], lambda: sems.at[zd], dev)

    def bquad(self):
        net, P, cut, rb, hb, bm, bms = self.net, self.P, self.cut, self.rb, self.hb, self.bm, self.bms
        if not rb:
            return
        z = net.z
        net.wait(net.has_dn, lambda: self.bbe.at[z], self.bbes.at[z])
        net.wait(net.has_up, lambda: self.bab.at[z], self.babs.at[z])
        for q in range(4):
            def fold(sl, q=q):
                s = wide(P[q, z, pl.ds(cut + sl.start, 16), :])
                s = s + jnp.where(net.has_dn, wide(self.bbe[z, q, sl, :]), 0.0)
                s = s + jnp.where(net.has_up, wide(self.bab[z, q, sl, :]), 0.0)
                bm[q, sl, :] = s.astype(BF)
            strips(rb, fold)
        net.go(None, lambda: bm.at[net.ud, pl.ds(0, hb), :], lambda: bm.at[4, pl.ds(0, hb), :], lambda: bms.at[0], net.xn)
        net.go(None, lambda: bm.at[net.ud, pl.ds(hb, hb), :], lambda: bm.at[5, pl.ds(0, hb), :], lambda: bms.at[1], net.yn)
        net.go(None, lambda: bm.at[net.ux, pl.ds(0, hb), :], lambda: bm.at[6, pl.ds(0, hb), :], lambda: bms.at[2], net.xn)
        net.go(None, lambda: bm.at[net.uy, pl.ds(hb, hb), :], lambda: bm.at[7, pl.ds(hb, hb), :], lambda: bms.at[3], net.yn)

    def bquad2(self):
        net, rb, hb, bm, bms = self.net, self.rb, self.hb, self.bm, self.bms
        if not rb:
            return

        def add4(sl):
            bm[4, sl, :] = (wide(bm[4, sl, :]) + wide(bm[net.uy, sl, :])).astype(BF)

        def add5(sl):
            bm[5, sl, :] = (wide(bm[5, sl, :]) + wide(bm[net.ux, pl.ds(hb + sl.start, 16), :])).astype(BF)

        net.wait(None, lambda: bm.at[4, pl.ds(0, hb), :], bms.at[0])
        strips(hb, add4)
        net.go(None, lambda: bm.at[4, pl.ds(0, hb), :], lambda: bm.at[7, pl.ds(0, hb), :], lambda: bms.at[4], net.yn)
        net.wait(None, lambda: bm.at[5, pl.ds(0, hb), :], bms.at[1])
        strips(hb, add5)
        net.go(None, lambda: bm.at[5, pl.ds(0, hb), :], lambda: bm.at[6, pl.ds(hb, hb), :], lambda: bms.at[5], net.xn)

    def last(self, store):
        net, cut, rb, hb, bm, bms = self.net, self.cut, self.rb, self.hb, self.bm, self.bms
        z = net.z
        self.square(z, None)

        def own(sl):
            s = self.local(z, sl)
            s = s + jnp.where(net.has_dn, wide(self.be[z, sl, :]), 0.0)
            s = s + jnp.where(net.has_up, wide(self.ab[z, sl, :]), 0.0)
            store(sl, s)

        net.wait(net.has_dn, lambda: self.be.at[z], self.bes.at[z])
        net.wait(net.has_up, lambda: self.ab.at[z], self.abs_.at[z])
        strips(cut, own)
        if rb:
            net.wait(None, lambda: bm.at[6, pl.ds(0, hb), :], bms.at[2])
            net.wait(None, lambda: bm.at[6, pl.ds(hb, hb), :], bms.at[5])
            net.wait(None, lambda: bm.at[7, pl.ds(0, hb), :], bms.at[4])
            net.wait(None, lambda: bm.at[7, pl.ds(hb, hb), :], bms.at[3])
            strips(rb, lambda sl: store(
                pl.ds(cut + sl.start, 16), wide(bm[net.u, sl, :]) + wide(bm[6, sl, :]) + wide(bm[7, sl, :])))


def steps_of(sc, text):
    names = {"m": sc.mid_send, "f": sc.bfirst, "d": sc.direct, "M": sc.mids, "h": sc.hop, "b": sc.bhop, "Q": sc.bquad, "q": sc.bquad2}
    return [functools.partial(names[word[0]], *[int(digit) for digit in word[1:]]) for word in text.split()]


def run_steps(steps):
    for one in steps:
        one()


def rs_scratch(cut, R, D):
    h, rb = cut // 2, R - cut
    V = lambda *s: pltpu.VMEM(s, BF)
    S = pltpu.SemaphoreType.DMA
    return [V(4, h, D), V(4, h, D), V(4, cut, D), V(4, cut, D), V(4, cut, D), V(4, cut, D),
            V(4, 4, max(rb, 16), D), V(4, 4, max(rb, 16), D), V(8, max(rb, 16), D),
            S((4,)), S((4,)), S((4, 2)), S((4, 2)), S((4,)), S((4,)), S((4,)), S((4,)), S((6,))]


def rs_kernel(cut, P, o_ref, ssem, *scr):
    net = Net(ssem)
    net.barrier()
    sc = Scatter(net, cut, P, scr)

    def store(sl, v):
        o_ref[sl, :] = v.astype(o_ref.dtype)

    for zd in (3, 0, 2, 1):
        sc.first(zd)
    for zd in (3, 0, 2, 1):
        sc.mids(zd)
    sc.hop(3, 0); sc.hop(0, 3); sc.bhop(3, 1); sc.bhop(0, 2)
    sc.hop(2, 0); sc.hop(1, 3); sc.bhop(2, 1); sc.bhop(1, 2)
    sc.hop(3, 1); sc.hop(0, 2); sc.bhop(3, 2); sc.bhop(0, 1)
    sc.hop(1, 0); sc.hop(2, 3); sc.bquad()
    sc.hop(2, 1); sc.hop(1, 2)
    sc.hop(3, 2); sc.hop(0, 1); sc.bquad2()
    sc.last(store)
    net.finish()


def rs16(p, cid, cut=96, dtype=F32):
    _, _, R, D = p.shape
    DMA = pltpu.SemaphoreType.DMA
    return pl.pallas_call(
        functools.partial(rs_kernel, cut),
        out_shape=jax.ShapeDtypeStruct((R, D), dtype),
        in_specs=[pl.BlockSpec(memory_space=pltpu.VMEM)],
        out_specs=pl.BlockSpec(memory_space=pltpu.VMEM),
        scratch_shapes=[DMA((96,))] + rs_scratch(cut, R, D),
        compiler_params=pltpu.CompilerParams(collective_id=cid, has_side_effects=True, vmem_limit_bytes=56 * 2**20),
        name="scatter_rows",
    )(p)


class Gather:
    def __init__(self, net, rows, cut, at, plane, sems):
        self.net, self.rows, self.cut, self.ref, self.plane = net, rows, cut, at, plane
        self.zr, self.xr, self.yr, self.d1, self.d2, self.br, self.bz = sems
        self.h, self.rb = cut // 2, rows - cut
        self.hb = self.rb // 2
        z = net.z
        self.near = []
        for s in range(4):
            zl, zh = z - s, z + s
            self.near.append((
                (jnp.maximum(zl, 0), zl >= 0, jnp.logical_and(zl >= 0, net.has_up), net.up),
                (jnp.minimum(zh, 3), zh < 4, jnp.logical_and(zh < 4, net.has_dn), net.dn)))

    def same(self, cond, uu, zz, lo, n, sem, dev):
        ref = lambda: self.ref(uu, zz, lo, n)
        self.net.go(cond, ref, ref, sem, dev)

    def outward(self, zz, cond):
        net, cut = self.net, self.cut
        self.same(cond, net.u, zz, 0, cut, lambda: self.xr.at[zz], net.xn)
        self.same(cond, net.u, zz, 0, cut, lambda: self.yr.at[zz], net.yn)

    def begin(self):
        net, cut, rb, z = self.net, self.cut, self.rb, self.net.z
        self.same(net.has_up, net.u, z, 0, cut, lambda: self.zr.at[z], net.up)
        self.same(net.has_dn, net.u, z, 0, cut, lambda: self.zr.at[z], net.dn)
        if rb:
            self.same(None, net.u, z, cut, rb, lambda: self.br.at[0], net.xn)
            self.same(None, net.u, z, cut, rb, lambda: self.br.at[1], net.yn)
        self.outward(z, None)

    def begin2(self):
        net, cut, rb, hb, z = self.net, self.cut, self.rb, self.hb, self.net.z
        if rb:
            net.wait(None, lambda: self.ref(net.ux, z, cut, rb), self.br.at[0])
            self.same(None, net.ux, z, cut, hb, lambda: self.br.at[2], net.yn)
            net.wait(None, lambda: self.ref(net.uy, z, cut, rb), self.br.at[1])
            self.same(None, net.uy, z, cut + hb, hb, lambda: self.br.at[3], net.xn)

    def along(self, s):
        net = self.net
        for zz, cond, fwd, dev in self.near[s]:
            net.wait(cond, lambda zz=zz: self.ref(net.u, zz, 0, self.cut), self.zr.at[zz])
            self.same(fwd, net.u, zz, 0, self.cut, lambda zz=zz: self.zr.at[zz], dev)
            self.outward(zz, cond)

    def quads(self, s):
        net, cut, rb, hb, z = self.net, self.cut, self.rb, self.hb, self.net.z
        if not rb:
            return
        if s == 0:
            net.wait(None, lambda: self.ref(net.ud, z, cut, hb), self.br.at[2])
            net.wait(None, lambda: self.ref(net.ud, z, cut + hb, hb), self.br.at[3])
            whole = lambda: self.plane(z, cut, rb)
            net.go(net.has_up, whole, whole, lambda: self.bz.at[z], net.up)
            net.go(net.has_dn, whole, whole, lambda: self.bz.at[z], net.dn)
            return
        for zz, cond, fwd, dev in self.near[s]:
            whole = lambda zz=zz: self.plane(zz, cut, rb)
            net.wait(cond, whole, self.bz.at[zz])
            net.go(fwd, whole, whole, lambda zz=zz: self.bz.at[zz], dev)

    def planes(self, s):
        if s == 0:
            return ((self.net.z, None),)
        return tuple((zz, cond) for zz, cond, _f, _d in self.near[s])

    def cross(self, s):
        net, h, cut = self.net, self.h, self.cut
        for zz, cond in self.planes(s):
            net.wait(cond, lambda zz=zz: self.ref(net.ux, zz, 0, cut), self.xr.at[zz])
            self.same(cond, net.ux, zz, 0, h, lambda zz=zz: self.d1.at[zz], net.yn)
            net.wait(cond, lambda zz=zz: self.ref(net.uy, zz, 0, cut), self.yr.at[zz])
            self.same(cond, net.uy, zz, h, h, lambda zz=zz: self.d2.at[zz], net.xn)

    def settle(self, s):
        net, h = self.net, self.h
        for zz, cond in self.planes(s):
            net.wait(cond, lambda zz=zz: self.ref(net.ud, zz, 0, h), self.d1.at[zz])
            net.wait(cond, lambda zz=zz: self.ref(net.ud, zz, h, h), self.d2.at[zz])


def ag_sems():
    S = pltpu.SemaphoreType.DMA
    return [S((4,)) for _ in range(7)]


def greet(net, chips=16):
    bar = pltpu.get_barrier_semaphore()

    def hello(j, _):
        t = lax.rem(net.u * 4 + net.z + j, chips)
        pl.semaphore_signal(bar, inc=1, device_id=(t // 4, lax.rem(t, 4), net.c), device_id_type=MESH)
        return 0

    lax.fori_loop(1, chips, hello, 0)
    pl.semaphore_signal(bar, inc=1, device_id=(net.u, net.z, 1 - net.c), device_id_type=MESH)
    pl.semaphore_wait(bar, chips)


def each_chip(net, body, chips=16):
    def one(j, _):
        t = lax.rem(net.u * 4 + net.z + j, chips)
        body(t, (t // 4, lax.rem(t, 4), net.c))
        return 0

    lax.fori_loop(1, chips, one, 0)


def remote(src, dst, ssem, rsem, dev):
    return pltpu.make_async_remote_copy(
        src_ref=src, dst_ref=dst, send_sem=ssem, recv_sem=rsem, device_id=dev, device_id_type=MESH)


def landed(ref, sem):
    pltpu.make_async_copy(ref, ref, sem).wait()


def segment_rows(segments, k_seg, reach):
    k_seg[:, 0:reach] = jnp.full((1, reach), -1.0, F32)
    k_seg[:, reach:] = segments[...]


def rope_at(near, far, i):
    cf, sf = far[0, pl.ds(i, 1), :], far[1, pl.ds(i, 1), :]
    cn, sn = near[0], near[1]
    return cf * cn - sf * sn, sf * cn + cf * sn


def row_sums(v):
    return jnp.sum(v.T, axis=0, keepdims=True)


def column(row):
    return jnp.broadcast_to(row, (row.shape[1], row.shape[1])).T


def share_sums(net, sums, sums_all, out, lsem, ssem, rsem, meanwhile=None):
    me = net.u * 4 + net.z
    own = pltpu.make_async_copy(sums, sums_all.at[me], lsem)
    own.start()
    each_chip(net, lambda t, dev: remote(sums, sums_all.at[me], ssem, rsem, dev).start())
    own.wait()
    if meanwhile is not None:
        meanwhile()
    part = sums_all.at[pl.ds(0, 15)]
    landed(part, rsem)
    total = sums_all[0]
    for i in range(1, 16):
        total = total + sums_all[i]
    out[...] = total
    landed(part, ssem)


def greet_all(net, count=32):
    bar = pltpu.get_barrier_semaphore()
    me = net.u * 8 + net.z * 2 + net.c

    def hello(j, _):
        t = lax.rem(me + j, count)
        pl.semaphore_signal(bar, inc=1, device_id=(t // 8, lax.rem(t, 8) // 2, lax.rem(t, 2)), device_id_type=MESH)
        return 0

    lax.fori_loop(1, count, hello, 0)
    pl.semaphore_wait(bar, count - 1)


def weight_tiles(partner, plan, load, turn, right, left, ob, gt, fs, other, osem, ors, fsem, gsem, out):
    side = fs.shape[2]

    def sent(k):
        return remote(ob(k), other.at[k], osem.at[k], ors.at[k], partner)

    def tile_at(i):
        kind, k = plan[i]
        if load is not None and i + 1 < len(plan):
            load(i + 1).start()
        if kind == "o":
            if k >= 2:
                sent(k - 2).wait_send()
        else:
            landed(other.at[k], ors.at[k])
            fetch = pltpu.make_async_copy(other.at[k], gt, gsem)
            fetch.start()
        if load is not None:
            load(i).wait()
        turn(i)
        if kind == "w":
            fetch.wait()
        for h in (0, 1):
            if kind == "w" and k > 0:
                landed(fs.at[h], fsem.at[h])
            for n in (0, 1):
                made = dot(left[...], right(h, n), ((1,), (0,)))
                cols = slice(h * side + n * 512, h * side + (n + 1) * 512)
                if kind == "o":
                    ob(k)[:, cols] = made.astype(BF)
                else:
                    fs[h, :, n * 512 : (n + 1) * 512] = made + wide(gt[:, cols])
            if kind == "w":
                pltpu.make_async_copy(fs.at[h], out(k, h), fsem.at[h]).start()
        if kind == "o":
            sent(k).start()

    def finish():
        count = len(plan) // 2
        for k in (count - 2, count - 1):
            sent(k).wait_send()
        for h in (0, 1):
            landed(fs.at[h], fsem.at[h])

    return tile_at, finish


def turned_into(left, flat, cols, tile=256):
    def one(b, _):
        sl = pl.ds(pl.multiple_of(b * tile, tile), tile)
        left[:, sl] = flat[sl, cols].T
        return 0

    lax.fori_loop(0, flat.shape[0] // tile, one, 0)


def qkv_kernel(cut, x_ref, wq, wk, wv, block, cot, n1_o, lin_o, wf_o, tot, sw, C, X, lin, wf, nb, gain, sums, sums_all, lsem, nsem, msem, ssem, csem, *gs):
    net = Net(ssem)
    u, z, c = net.u, net.z, net.c
    me = u * 4 + z
    rows, width = X.shape[2], X.shape[3]
    partner = (u, z, 1 - c)
    own = pltpu.make_async_copy(x_ref, X.at[u, z], lsem.at[0])
    own.start()

    def piece(t, i):
        return ((wq, wk, wv)[i].at[:, pl.ds(pl.multiple_of(t * 128, 128), 128)], wf.at[me, c, :, pl.ds(i * 128, 128)])

    own_w = [pltpu.make_async_copy(*piece(me, i), lsem.at[1]) for i in range(3)]
    for one in own_w:
        one.start()
    own_c = pltpu.make_async_copy(cot, C.at[u, z], lsem.at[3])
    own_c.start()
    dev_me = me * 2 + c
    greet_all(net)
    own.wait()
    ga = Gather(net, rows, cut, lambda uu, zz, lo, n: X.at[uu, zz, pl.ds(lo, n), :],
                lambda zz, lo, n: X.at[:, zz, pl.ds(lo, n), :], gs[:7])
    netc = Net(csem)
    gc = Gather(netc, rows, cut, lambda uu, zz, lo, n: C.at[uu, zz, pl.ds(lo, n), :],
                lambda zz, lo, n: C.at[:, zz, pl.ds(lo, n), :], gs[7:])
    ga.begin()

    def tell(j, _):
        t = lax.rem(dev_me + j, 32)
        remote(block.at[t // 2], sw.at[dev_me], msem.at[6], msem.at[7], (t // 8, lax.rem(t, 8) // 2, lax.rem(t, 2))).start()
        return 0

    lax.fori_loop(1, 32, tell, 0)
    sw[dev_me] = block[me]

    def columns(t, dev):
        for i in range(3):
            remote(*piece(t, i), msem.at[0], msem.at[1], dev).start()

    each_chip(net, columns)

    def plane(zz):
        def chunk(uu, _):
            slot = lax.rem(uu, 2)
            k = uu * 4 + zz

            def norm(i, _):
                sl = pl.ds(pl.multiple_of(i * 16, 16), 16)
                v = X[uu, zz, sl, :].astype(F32)
                r = lax.rsqrt(jnp.mean(v * v, axis=1, keepdims=True) + EPS)
                nb[slot, sl, :] = (v * r * gain[...]).astype(BF)
                return 0

            def stored(s):
                return pltpu.make_async_copy(nb.at[s], n1_o.at[k], nsem.at[s])

            pl.when(uu >= 2)(lambda: stored(slot).wait())
            lax.fori_loop(0, rows // 16, norm, 0)
            stored(slot).start()
            got = dot(nb[slot], wf[...].reshape(width, wf.shape[-1]), ((1,), (0,)))
            lin[k] = got
            q, kk = got[:, :128], got[:, 128:256]
            sums[pl.ds(k, 1), :] = row_sums(q * q)
            sums[pl.ds(16 + k, 1), :] = row_sums(kk * kk)
            return 0

        lax.fori_loop(0, 4, chunk, 0)
        for s in (0, 1):
            pltpu.make_async_copy(nb.at[s], n1_o.at[0], nsem.at[s]).wait()

    def compute(s):
        for zz, cond in ga.planes(s):
            if cond is None:
                plane(zz)
            else:
                pl.when(cond)(lambda zz=zz: plane(zz))

    ga.begin2()
    ga.along(1)
    ga.quads(0)
    ga.cross(0)
    landed(wf.at[0, 0], lsem.at[1])
    landed(wf.at[pl.ds(0, 15), 0], msem.at[1])
    to_partner = remote(wf.at[:, c], wf.at[:, c], msem.at[2], msem.at[3], partner)
    to_partner.start()
    own_c.wait()
    ga.along(2)
    ga.quads(1)
    ga.cross(1)
    gc.begin()
    landed(sw.at[pl.ds(0, 31)], msem.at[7])
    for e in range(16):
        gain[:, e * 128 : (e + 1) * 128] = sw[2 * e, 2:3, :] + sw[2 * e + 1, 2:3, :]
    ga.settle(0)
    landed(wf.at[:, 1 - c], msem.at[3])
    keep_w = pltpu.make_async_copy(wf, wf_o, lsem.at[0])
    keep_w.start()
    compute(0)
    gc.begin2()
    ga.along(3)
    ga.quads(2)
    ga.cross(2)
    ga.settle(1)
    gc.along(1)
    gc.quads(0)
    gc.cross(0)
    compute(1)
    ga.quads(3)
    ga.cross(3)
    ga.settle(2)
    gc.along(2)
    gc.quads(1)
    gc.cross(1)
    compute(2)
    ga.settle(3)
    gc.along(3)
    gc.quads(2)
    gc.cross(2)
    compute(3)
    keep = pltpu.make_async_copy(lin, lin_o, lsem.at[1])
    keep.start()
    landed(wf.at[pl.ds(0, 15), 0], msem.at[0])
    landed(wf.at[:, c], msem.at[2])

    def rest():
        gc.quads(3)
        gc.cross(3)

    share_sums(net, sums, sums_all, tot, lsem.at[2], msem.at[4], msem.at[5], rest)
    for s in range(4):
        gc.settle(s)
    landed(sw.at[pl.ds(0, 31)], msem.at[6])
    keep_w.wait()
    keep.wait()
    net.finish()
    netc.finish()


def run_qkv(x, wq, wk, wv, block, cot, cid, cut=96):
    R, D = x.shape
    N = 384
    DMA = pltpu.SemaphoreType.DMA
    S = jax.ShapeDtypeStruct
    V = lambda *s: pltpu.VMEM(s, BF)
    VF = lambda *s: pltpu.VMEM(s, F32)
    A = pl.BlockSpec(memory_space=pl.ANY)
    M = pl.BlockSpec(memory_space=pltpu.VMEM)
    return pl.pallas_call(
        functools.partial(qkv_kernel, cut),
        out_shape=(S((16, R, D), BF), S((16, R, N), F32), S((16, 2, R // 2, N), BF), S((32, 128), F32),
                   S((32, 8, 128), F32), S((4, 4) + cot.shape, BF)),
        in_specs=[A, A, A, A, M, A],
        out_specs=(A, A, A, M, M, A),
        scratch_shapes=[V(4, 4, R, D), VF(16, R, N), V(16, 2, R // 2, N), V(2, R, D), VF(1, D), VF(32, 128), VF(16, 32, 128),
                        DMA((4,)), DMA((2,)), DMA((8,)), DMA((64,)), DMA((64,))] + ag_sems() + ag_sems(),
        compiler_params=pltpu.CompilerParams(collective_id=cid, has_side_effects=True, vmem_limit_bytes=63 * 2**20),
        name="project",
    )(x, wq, wk, wv, block, cot)


def group_of(t):
    g = t // 2
    return jnp.where(g == 0, 3, jnp.where(g == 1, 0, jnp.where(g == 2, 2, 1)))


def expert_kernel(cut, n2, cot_a, cot_b, share_rows, gate, up, down, d_n2, p_out, n2_o, a_o, other, dd_o,
                  X, C, GU, W, A, hid, pb, fs, share, lsem, wsem, wrs, psem, osem, tsem, ors, fsem, sa, sr, *scr):
    ga_sems, rs_bufs = scr[:7], scr[7:]
    na, nr = Net(sa), Net(sr)
    u, z, c = na.u, na.z, na.c
    partner = (u, z, 1 - c)
    rows, width = X.shape[2], X.shape[3]
    ff = W.shape[0]
    half, half_ff = gate.shape[0], down.shape[0]
    tokens = 16 * rows
    tile = 256
    span = 512
    side = width // 2
    first = [pltpu.make_async_copy(n2, X.at[u, z], lsem.at[0]),
             pltpu.make_async_copy(cot_a, C.at[:, :, :, pl.ds(0, side)], lsem.at[1]),
             pltpu.make_async_copy(cot_b, C.at[:, :, :, pl.ds(side, side)], lsem.at[5])]

    def weights():
        mine = pl.ds(pl.multiple_of(c * half, half), half)
        mine_ff = pl.ds(pl.multiple_of(c * half_ff, half_ff), half_ff)
        return ((gate, GU.at[mine, pl.ds(0, ff)]), (up, GU.at[mine, pl.ds(ff, ff)]), (down, W.at[mine_ff, :]))

    own_w = [pltpu.make_async_copy(a, b, lsem.at[2 + i]) for i, (a, b) in enumerate(weights())]
    for one in first + own_w:
        one.start()
    na.barrier((partner,))
    first[0].wait()

    def gather(net, buf, sems):
        return Gather(net, rows, cut, lambda uu, zz, lo, n: buf.at[uu, zz, pl.ds(lo, n), :],
                      lambda zz, lo, n: buf.at[:, zz, pl.ds(lo, n), :], sems)

    ga = gather(na, X, ga_sems)
    ga.begin()
    sent_w = [remote(a, b, wsem.at[i], wrs.at[i], partner) for i, (a, b) in enumerate(weights())]
    for one in sent_w:
        one.start()
    for k in range(16):
        share[k // 4, k % 4] = column(share_rows[k : k + 1, :])[:, 0:1]

    def forward(zz):
        pltpu.make_async_copy(X.at[:, zz], n2_o.at[:, zz], psem.at[1]).start()

        def scale(i, _):
            sl = pl.ds(pl.multiple_of(i * 16, 16), 16)
            C[:, zz, sl, :] = (share[:, zz, sl, :] * C[:, zz, sl, :].astype(F32)).astype(BF)
            return 0

        lax.fori_loop(0, rows // 16, scale, 0)

        def inner(n, _):
            gcols = pl.ds(pl.multiple_of(n * span, span), span)
            ucols = pl.ds(pl.multiple_of(ff + n * span, span), span)
            xv = X[:, zz].reshape(4 * rows, width)
            g = dot(xv, GU[:, gcols], ((1,), (0,)))
            uu = dot(xv, GU[:, ucols], ((1,), (0,)))
            s = jax.nn.sigmoid(g)
            gs = g * s
            hid[:, zz, :, gcols] = (gs * uu).astype(BF).reshape(4, rows, span)
            dh = dot(C[:, zz].reshape(4 * rows, width), W[gcols, :], ((1,), (1,)))
            A[:, zz, :, gcols] = (dh * uu * s * (1.0 + g * (1.0 - s))).astype(BF).reshape(4, rows, span)
            A[:, zz, :, ucols] = (dh * gs).astype(BF).reshape(4, rows, span)
            return 0

        lax.fori_loop(0, ff // span, inner, 0)
        pltpu.make_async_copy(A.at[:, zz], a_o.at[:, zz], psem.at[2]).start()
        weight = share[:, zz]

        def flushed(n):
            cols = pl.ds(pl.multiple_of(n * span, span), span)
            slot = lax.rem(n, 2)
            return pltpu.make_async_copy(pb.at[slot], p_out.at[:, zz, :, cols], osem.at[slot])

        def outer(n, _):
            cols = pl.ds(pl.multiple_of(n * span, span), span)
            made = dot(hid[:, zz].reshape(4 * rows, ff), W[:, cols], ((1,), (0,)))
            made = made.astype(BF).astype(F32).reshape(4, rows, span)
            pl.when(n >= 2)(lambda: flushed(n - 2).wait())
            pb[lax.rem(n, 2)] = (weight * made).astype(BF)
            flushed(n).start()
            return 0

        count = width // span
        lax.fori_loop(0, count, outer, 0)
        flushed(count - 2).wait()
        flushed(count - 1).wait()

    def planes(s):
        if s == 0:
            forward(z)
            return

        def one(d, _):
            zz = jnp.where(d == 0, z - s, z + s)
            pl.when(jnp.logical_and(zz >= 0, zz < 4))(lambda: forward(zz))
            return 0

        lax.fori_loop(0, 2, one, 0)

    ga.begin2()
    ga.along(1)
    ga.quads(0)
    ga.cross(0)
    ga.along(2)
    ga.quads(1)
    ga.cross(1)
    ga.settle(0)
    for one in own_w:
        one.wait()
    for one in sent_w:
        one.wait_recv()
    first[1].wait()
    first[2].wait()
    planes(0)
    ga.along(3)
    ga.quads(2)
    ga.cross(2)
    ga.settle(1)
    planes(1)
    ga.quads(3)
    ga.cross(3)
    ga.settle(2)
    planes(2)
    ga.settle(3)
    planes(3)
    na.finish()
    for one in sent_w:
        one.wait_send()
    landed(X, psem.at[1])
    sc = Scatter(nr, cut, X, rs_bufs)

    def backward(t):
        zd = group_of(t)
        base = lax.rem(t, 2) * (width // 2)

        def outer(n, _):
            cols = pl.ds(pl.multiple_of(base + n * span, span), span)
            back = dot(A[:, zd].reshape(4 * rows, 2 * ff), GU[cols, :], ((1,), (1,)))
            X[:, zd, :, cols] = back.astype(BF).reshape(4, rows, span)
            return 0

        lax.fori_loop(0, width // 2 // span, outer, 0)

    def acts(steps, t):
        for at, todo in steps.items():
            def act(todo=todo):
                for one in todo:
                    one()
            pl.when(t == at)(act)

    def at_turns(table):
        return {t: steps_of(sc, words) for t, words in table.items()}

    steps = at_turns({1: "m3 f3 d3", 3: "m0 f0 d0", 4: "M3", 5: "m2 f2 d2 b31", 6: "M0", 7: "m1 f1 d1 b02 b32"})

    def turn(t, _):
        backward(t)
        acts(steps, t)
        return 0

    lax.fori_loop(0, 8, turn, 0)

    left = W.at[pl.ds(0, tile), :]

    def left_hidden(i):
        kind, k = plan[i]
        which = 1 - c if kind == "o" else c
        turned_into(left, hid.reshape(tokens, ff), pl.ds(pl.multiple_of((which * 2 + k) * tile, tile), tile))

    plan = [("o", 0), ("o", 1), ("w", 0), ("w", 1)]
    made = C.reshape(tokens, width)
    dw, dw_end = weight_tiles(
        partner, plan, None, left_hidden, lambda h, n: made[:, h * side + n * 512 : h * side + (n + 1) * 512], left,
        lambda k: W.at[pl.ds((1 + k % 2) * tile, tile), :], W.at[pl.ds(3 * tile, tile), :], fs, other, tsem, ors, fsem,
        lsem.at[0], lambda k, h: dd_o.at[pl.ds(k * tile, tile), pl.ds(h * side, side)])

    def go(words):
        run_steps(steps_of(sc, words))

    dw(0)
    go("M2 b21")
    dw(1)
    go("h30 M1 b01 b12 h03")
    dw(2)
    go("h31 h02 h20 h23")
    dw(3)
    go("h32 h01 h10 h13 Q h21 h12 q")

    def store_out(sl, v):
        d_n2[sl, :] = v

    sc.last(store_out)
    landed(A, psem.at[2])
    dw_end()
    nr.finish()


def run_expert(n2, cot_a, cot_b, share, gate, up, down, cid, cut=96):
    R, D = n2.shape
    half, ff = gate.shape
    DMA = pltpu.SemaphoreType.DMA
    S = jax.ShapeDtypeStruct
    V = lambda *s: pltpu.VMEM(s, BF)
    A = pl.BlockSpec(memory_space=pl.ANY)
    M = pl.BlockSpec(memory_space=pltpu.VMEM)
    return pl.pallas_call(
        functools.partial(expert_kernel, cut),
        out_shape=(S((R, D), F32), S((4, 4, R, D), BF), S((4, 4, R, D), BF), S((4, 4, R, 2 * ff), BF),
                   S((2, 256, D), BF), S(down.shape, F32)),
        in_specs=[A, A, A, M, A, A, A],
        out_specs=(M,) + (A,) * 5,
        scratch_shapes=[V(4, 4, R, D), V(4, 4, R, D), V(D, 2 * ff), V(ff, D), V(4, 4, R, 2 * ff), V(4, 4, R, ff),
                        V(2, 4, R, 512), pltpu.VMEM((2, 256, D // 2), F32), pltpu.VMEM((4, 4, R, 1), F32),
                        DMA((6,)), DMA((3,)), DMA((3,)), DMA((3,)), DMA((2,)), DMA((2,)), DMA((2,)), DMA((2,)),
                        DMA((64,)), DMA((96,))] + ag_sems() + rs_scratch(cut, R, D),
        compiler_params=pltpu.CompilerParams(collective_id=cid, has_side_effects=True, vmem_limit_bytes=63 * 2**20),
        name="expert",
    )(n2, cot_a, cot_b, share, gate, up, down)


def finish_kernel(cut, d_lin, wf, n1, att, x_in, d_res, gain, d_gain_two, d_gains,
                  d_wo, d_inputs, d_wq, d_wk, d_wv, gains_o,
                  P, PO, PG, PT, wsum, nt, left, keep, give, got, send, recv, d_n1, d_gain, gb, gr,
                  lsem, tsem, msem, s1, s2, *bufs):
    net, net2 = Net(s1), Net(s2)
    u, z, c = net.u, net.z, net.c
    me = u * 4 + z
    rows, width = P.shape[2], P.shape[3]
    lanes = d_lin.shape[2]
    tokens = 16 * rows
    tile = 256
    partner = (u, z, 1 - c)
    half = len(bufs) // 2
    sc1, sc2 = Scatter(net, cut, P, bufs[:half]), Scatter(net2, cut, PO, bufs[half:])

    def tile_load(k):
        slot = lax.rem(k, 2)
        return pltpu.make_async_copy(n1.at[:, :, pl.ds(pl.multiple_of(k * tile, tile), tile)], nt.at[slot], tsem.at[slot])

    tile_load(0).start()
    greet_all(net)

    def one(words):
        run_steps(steps_of(sc1, words))

    def two(words):
        run_steps(steps_of(sc2, words))

    def group(zd):
        def one(n, _):
            cols = pl.ds(pl.multiple_of(n * 512, 512), 512)
            w = wf.reshape(width, lanes)
            for q in range(4):
                P[q, zd, :, cols] = dot(d_lin[q * 4 + zd], w[cols, :], ((1,), (1,))).astype(BF)
            return 0

        lax.fori_loop(0, width // 512, one, 0)

    for zd in (3, 0, 2, 1):
        group(zd)
        one(f"m{zd}" + (f" f{zd}" if zd in (3, 0) else ""))

    side = width // 2
    own_cols = pl.ds(pl.multiple_of(c * side, side), side)
    give_cols = pl.ds(pl.multiple_of((1 - c) * side, side), side)

    def outer(e, _):
        turned_att = att[e].T
        PG[e // 4, lax.rem(e, 4)] = dot(turned_att, d_res[:, give_cols].astype(BF), ((1,), (0,))).astype(BF)
        PO[e // 4, lax.rem(e, 4)] = dot(turned_att, d_res[:, own_cols].astype(BF), ((1,), (0,))).astype(BF)
        return 0

    lax.fori_loop(0, 16, outer, 0)
    halves = remote(PG, PT, msem.at[6], msem.at[7], partner)
    halves.start()

    def join():
        landed(PT, msem.at[7])

        def add(e, _):
            def strip(sl):
                at = (e // 4, lax.rem(e, 4), sl, slice(None))
                PO[at] = (wide(PO[at]) + wide(PT[at])).astype(BF)

            strips(rows, strip)
            return 0

        lax.fori_loop(0, 16, add, 0)

    def store1(sl, v):
        d_n1[sl, :] = v

    def store2(sl, v):
        wsum[sl, :] = v


    def grads(k):
        if k < 7:
            tile_load(k + 1).start()
        tile_load(k).wait()
        slot = k % 2
        flat = nt.at[slot].reshape(tokens, tile)

        def turn(b, _):
            sl = pl.ds(pl.multiple_of(b * tile, tile), tile)
            left[:, sl] = flat[sl, :].T
            return 0

        lax.fori_loop(0, tokens // tile, turn, 0)
        made = dot(left[...], d_lin[...].reshape(tokens, lanes), ((1,), (0,)))
        for i in range(2):
            first, second = made[i * 128 : i * 128 + 64], made[i * 128 + 64 : (i + 1) * 128]
            keep[2 * k + i] = jnp.where(c == 0, first, second)
            give[2 * k + i] = jnp.where(c == 0, second, first).astype(BF)

    one("f2 f1")
    join()
    two("m3 m0 m2 m1 f3 f0")
    one("d3 d0")
    grads(0)
    one("M3 M0")
    one("d2 d1")
    grads(1)
    one("M2 M1")
    two("d3 d0 d2 d1 f2 f1")
    grads(2)
    one("b31 b02")
    two("M3 M0 M2 M1")
    grads(3)
    one("h30 h03 b21 b12")
    grads(4)
    grads(5)
    one("b32 b01")
    grads(6)
    grads(7)
    across = remote(give, got, msem.at[0], msem.at[1], partner)
    across.start()
    landed(got, msem.at[1])

    def total(e, _):
        send[e] = (keep[e] + wide(got[e])).astype(BF)
        return 0

    lax.fori_loop(0, 16, total, 0)
    each_chip(net, lambda t, dev: remote(send.at[t], recv.at[me], msem.at[2], msem.at[3], dev).start())
    recv[me] = send[me]
    two("b31 b02 b21 b12 b32 b01")
    one("h31 h02 h20 h13 Q")
    two("h30 h03 h20 h13 Q")
    one("h32 h01 h10 h23")
    two("h31 h02 h10 h23")
    one("h21 h12 q")
    sc1.last(store1)
    d_gain[...] = jnp.zeros_like(d_gain)

    def norm_back(i, _):
        sl = pl.ds(pl.multiple_of(i * 16, 16), 16)
        v, d = wide(x_in[sl, :]), d_n1[sl, :]
        r = lax.rsqrt(jnp.mean(v * v, axis=1, keepdims=True) + EPS)
        scaled = d * gain[...]
        inner = jnp.mean(scaled * v, axis=1, keepdims=True)
        d_inputs[sl, :] = d_res[sl, :] + r * scaled - v * (r * r * r * inner)
        d_gain[...] += jnp.sum(d * v * r, axis=0, keepdims=True)
        return 0

    lax.fori_loop(0, rows // 16, norm_back, 0)
    gb[...] = jnp.zeros_like(gb)
    gb[me, 2:4, :] = d_gains[0:2, :]
    for e in range(16):
        gb[e, 0:1, :] = d_gain[:, e * 128 : (e + 1) * 128]
        gb[e, 1:2, :] = d_gain_two[:, e * 128 : (e + 1) * 128]
    dev_me = me * 2 + c

    def tell(j, _):
        t = lax.rem(dev_me + j, 32)
        remote(gb.at[t // 2], gr.at[dev_me], msem.at[4], msem.at[5], (t // 8, lax.rem(t, 8) // 2, lax.rem(t, 2))).start()
        return 0

    lax.fori_loop(1, 32, tell, 0)
    gr[dev_me] = gb[me]
    two("h32 h01 h21 h12 q")
    landed(recv.at[pl.ds(0, 15)], msem.at[3])
    for e in range(16):
        piece = wide(recv[e])
        for i, out in enumerate((d_wq, d_wk, d_wv)):
            out[:, e * 128 : (e + 1) * 128] = piece[:, i * 128 : (i + 1) * 128]
    landed(gr.at[pl.ds(0, 31)], msem.at[5])
    sums = gr[0]
    for i in range(1, 32):
        sums = sums + gr[i]
    gains_o[...] = jnp.where(c == 0, sums[:, :64], sums[:, 64:])
    sc2.last(store2)
    d_wo[:, own_cols] = wsum[pl.ds(pl.multiple_of(c * 64, 64), 64), :]
    theirs = remote(wsum.at[pl.ds(pl.multiple_of((1 - c) * 64, 64), 64), :], d_wo.at[:, own_cols], msem.at[8], msem.at[9], partner)
    theirs.start()
    landed(PG, msem.at[6])
    landed(give, msem.at[0])
    landed(recv.at[pl.ds(0, 15)], msem.at[2])
    landed(gr.at[pl.ds(0, 31)], msem.at[4])
    theirs.wait_send()
    landed(d_wo.at[:, give_cols], msem.at[9])
    net.finish()
    net2.finish()


def run_finish(d_lin, wf, n1, att, x_in, d_res, gain, d_gain_two, d_gains, cid, cut=96):
    R, D = x_in.shape
    N = d_lin.shape[2]
    DMA = pltpu.SemaphoreType.DMA
    S = jax.ShapeDtypeStruct
    V = lambda *s: pltpu.VMEM(s, BF)
    VF = lambda *s: pltpu.VMEM(s, F32)
    A = pl.BlockSpec(memory_space=pl.ANY)
    M = pl.BlockSpec(memory_space=pltpu.VMEM)
    own = S((R // 2, D), F32)
    return pl.pallas_call(
        functools.partial(finish_kernel, cut),
        out_shape=(own, S((R, D), F32), own, own, own, S((8, 64), F32)),
        in_specs=[M, M, A] + [M] * 6,
        out_specs=(M,) * 6,
        scratch_shapes=[V(4, 4, R, D), V(4, 4, R, D // 2), V(4, 4, R, D // 2), V(4, 4, R, D // 2), VF(R, D // 2), V(2, 16, R, 256), V(256, 16 * R), VF(16, 64, N), V(16, 64, N),
                        V(16, 64, N), V(16, 64, N), V(16, 64, N), VF(R, D), VF(1, D), VF(16, 8, 128), VF(32, 8, 128),
                        DMA((1,)), DMA((2,)), DMA((10,)), DMA((64,)), DMA((64,))] + rs_scratch(cut, R, D) + rs_scratch(cut, R, D // 2),
        compiler_params=pltpu.CompilerParams(collective_id=cid, has_side_effects=True, vmem_limit_bytes=63 * 2**20),
        name="finish",
    )(d_lin, wf, n1, att, x_in, d_res, gain, d_gain_two, d_gains)

def band_scores(q, k, q_seg, k_seg, scale, reach):
    scores = dot(q, k, ((1,), (1,))) * scale
    q_at = lax.broadcasted_iota(jnp.int32, scores.shape, 0)
    k_at = lax.broadcasted_iota(jnp.int32, scores.shape, 1)
    return scores, (k_seg == q_seg) & (k_at <= q_at + reach)


def turned(v, cosine, sine):
    return v * cosine + pltpu.roll(v, 64, axis=1) * sine


def turned_back(v, cosine, sine):
    return v * cosine - pltpu.roll(v, 64, axis=1) * sine


def attend_kernel(scale, pads, cut, lin_h, tot, near, far, gq, gk, q_seg, segments, w_own, x_in, gain, cot,
                  wo_o, q_rot_o, kv_o, o_o, lse, att_o, residual_o, n2, C,
                  lin, k_seg, q_rot, kv, o_ref, att, residual, wo, lsem, msem, psem, ksem, ssem, csem, *gs):
    net = Net(ssem)
    u, z, c = net.u, net.z, net.c
    me = u * 4 + z
    rows = x_in.shape[0]
    width = x_in.shape[1]
    reach = pads * 2 * rows
    partner = (u, z, 1 - c)
    own = pltpu.make_async_copy(w_own, wo.at[u, z, c], lsem.at[0])
    own.start()
    load = pltpu.make_async_copy(lin_h, lin, ksem.at[0])
    load.start()
    own_c = pltpu.make_async_copy(cot, C.at[u, z], lsem.at[2])
    own_c.start()
    greet(net)
    own.wait()
    ga = Gather(net, rows, cut, lambda uu, zz, lo, n: wo.at[uu, zz, c, :, pl.ds(lo * 16, n * 16)],
                lambda zz, lo, n: wo.at[:, zz, c, :, pl.ds(lo * 16, n * 16)], gs[:7])
    netc = Net(csem)
    gc = Gather(netc, rows, cut, lambda uu, zz, lo, n: C.at[uu, zz, pl.ds(lo, n), :],
                lambda zz, lo, n: C.at[:, zz, pl.ds(lo, n), :], gs[7:])

    def halves(s):
        ga.settle(s)
        for zz, cond in ga.planes(s):
            ref = lambda zz=zz: wo.at[:, zz, c]
            net.go(cond, ref, ref, lambda zz=zz: psem.at[zz], partner)

    ga.begin()
    segment_rows(segments, k_seg, reach)
    load.wait()
    for i in range(pads):
        kv[:, i] = jnp.zeros(kv.shape[:1] + kv.shape[2:], BF)

    def ready(i, _):
        both = lin[i]
        rq = lax.rsqrt(column(tot[pl.ds(i, 1), :]) / width + EPS)
        rk = lax.rsqrt(column(tot[pl.ds(16 + i, 1), :]) / width + EPS)
        cs, sn = rope_at(near, far, i)
        q_rot[i] = turned(both[:, :128] * rq * gq[...], cs, sn).astype(BF)
        kv[0, pads + i, c] = turned(both[:, 128:256] * rk * gk[...], cs, sn).astype(BF)
        kv[1, pads + i, c] = both[:, 256:].astype(BF)
        return 0

    lax.fori_loop(0, 16, ready, 0)
    mine = kv.at[:, pl.ds(pads, 16), c]
    to_partner = remote(mine, mine, msem.at[0], msem.at[1], partner)
    to_partner.start()
    ga.begin2()
    ga.along(1)
    ga.quads(0)
    ga.cross(0)
    own_c.wait()
    gc.begin()
    landed(kv.at[:, pl.ds(pads, 16), 1 - c], msem.at[1])

    def block(j, _):
        i = lax.rem(me + 1 + j, 16)
        first = 2 * i + c
        band = pl.ds(pl.multiple_of(first * rows, rows), rows + reach)
        kf, vf = kv.at[0].reshape((pads + 16) * 2 * rows, 128), kv.at[1].reshape((pads + 16) * 2 * rows, 128)
        scores, allowed = band_scores(q_rot[i], kf[band, :], column(q_seg[pl.ds(i, 1), :])[:, 0:1], k_seg[:, band], scale, reach)
        scores = jnp.where(allowed, scores, NEG)
        top = jnp.max(scores, axis=1, keepdims=True)
        weights = jnp.where(allowed, jnp.exp(scores - top), 0.0)
        total = jnp.sum(weights, axis=1, keepdims=True)
        probs = (weights / total).astype(BF)
        o_ref[i] = dot(probs, vf[band, :], ((1,), (0,))).astype(BF)
        lse[i] = top + jnp.log(total)

        @pl.when(j < 15)
        def _():
            remote(o_ref.at[i], att.at[me], msem.at[2], msem.at[3], (i // 4, lax.rem(i, 4), c)).start()

        return 0

    lax.fori_loop(0, 5, block, 0)
    ga.along(2)
    ga.quads(1)
    ga.cross(1)
    halves(0)
    gc.begin2()
    lax.fori_loop(5, 10, block, 0)
    ga.along(3)
    ga.quads(2)
    ga.cross(2)
    halves(1)
    gc.along(1)
    gc.quads(0)
    gc.cross(0)
    lax.fori_loop(10, 16, block, 0)
    ga.quads(3)
    ga.cross(3)
    halves(2)
    gc.along(2)
    gc.quads(1)
    gc.cross(1)
    halves(3)
    att[me] = o_ref[me]
    part = att.at[pl.ds(0, 15)]
    landed(part, msem.at[3])
    for zz in range(4):
        landed(wo.at[:, zz, 1 - c], psem.at[zz])
    keep = [pltpu.make_async_copy(a, o, ksem.at[j]) for j, (a, o) in enumerate(
        ((wo, wo_o), (q_rot, q_rot_o), (kv, kv_o), (o_ref, o_o), (att, att_o)))]
    for one in keep:
        one.start()
    tile = 256

    def out(n, _):
        cols = pl.ds(pl.multiple_of(n * tile, tile), tile)
        acc = x_in[:, cols].astype(F32)
        for e in range(0, 16, 2):
            pair = jnp.concatenate([att[e], att[e + 1]], axis=1)
            acc = acc + dot(pair, wo[e // 4, pl.ds(e % 4, 2), :, :, cols].reshape(256, tile), ((1,), (0,)))
        residual[:, cols] = acc
        return 0

    lax.fori_loop(0, width // tile, out, 0)
    keep.append(pltpu.make_async_copy(residual, residual_o, ksem.at[5]))
    keep[5].start()
    gc.along(3)
    gc.quads(2)
    gc.cross(2)

    def norm(i, _):
        sl = pl.ds(pl.multiple_of(i * 16, 16), 16)
        v = residual[sl, :]
        r = lax.rsqrt(jnp.mean(v * v, axis=1, keepdims=True) + EPS)
        n2[sl, :] = (v * r * gain[...]).astype(BF)
        return 0

    lax.fori_loop(0, rows // 16, norm, 0)
    landed(mine, msem.at[0])
    landed(part, msem.at[2])
    gc.quads(3)
    gc.cross(3)
    for s in range(4):
        gc.settle(s)
    for one in keep:
        one.wait()
    net.finish()
    netc.finish()


def run_attend(scale, pads, lin, tot, near, far, gq, gk, q_seg, segments, w_own, x_in, gain, cot, cid, cut=96):
    R, D = x_in.shape
    DMA = pltpu.SemaphoreType.DMA
    S = jax.ShapeDtypeStruct
    A = pl.BlockSpec(memory_space=pl.ANY)
    M = pl.BlockSpec(memory_space=pltpu.VMEM)
    V = pltpu.VMEM
    wo = (4, 4, 2, R // 2, D)
    return pl.pallas_call(
        functools.partial(attend_kernel, scale, pads, cut),
        out_shape=(S(wo, BF), S((16, R, 128), BF), S((2, pads + 16, 2, R, 128), BF), S((16, R, 128), BF),
                   S((16, R, 1), F32), S((16, R, 128), BF), S((R, D), F32), S((R, D), BF), S((4, 4) + cot.shape, BF)),
        in_specs=[A] + [M] * 7 + [A, M, M, A],
        out_specs=(A, A, A, A, M, A, A, M, A),
        scratch_shapes=[V((16, R, 384), F32), V((1, (pads + 16) * 2 * R), F32), V((16, R, 128), BF),
                        V((2, pads + 16, 2, R, 128), BF), V((16, R, 128), BF), V((16, R, 128), BF), V((R, D), F32),
                        V(wo, BF), DMA((3,)), DMA((4,)), DMA((4,)), DMA((6,)), DMA((64,)), DMA((64,))] + ag_sems() + ag_sems(),
        compiler_params=pltpu.CompilerParams(collective_id=cid, has_side_effects=True, vmem_limit_bytes=63 * 2**20),
        name="attend",
    )(lin, tot, near, far, gq, gk, q_seg, segments, w_own, x_in, gain, cot)


def attend_back_kernel(scale, pads, cut, d_n2, cot, gain, wo_h, p_out, residual, q_rot, kv, q_seg, segments, lse, o_ref, lin, tot, near, far, gq, gk, n2, a_h,
                       d_lin, d_gains, output, d_residual, d_gain, other_w, dg_o, du_o,
                       nt, left, ob, gt, fs, tsem, osem, ors, fsem, gsem, d_res, k_seg, P, wo, d_mine, d_out, d_q, d_k, d_v, other, got, d_un, sums, sums_all, inner,
                       lsem, msem, ssem, *bufs):
    net = Net(ssem)
    sc = Scatter(net, cut, P, bufs)
    u, z, c = net.u, net.z, net.c
    me = u * 4 + z
    rows, width = d_n2.shape
    reach = pads * 2 * rows
    partner = (u, z, 1 - c)
    load = pltpu.make_async_copy(wo_h, wo, lsem.at[0])
    load.start()
    load_p = pltpu.make_async_copy(p_out, P, lsem.at[1])
    load_p.start()
    greet(net)

    def go(words):
        run_steps(steps_of(sc, words))

    load_p.wait()
    go("m3 m0 m2 m1")
    d_gain[...] = jnp.zeros_like(d_gain)

    def norm_back(i, _):
        sl = pl.ds(pl.multiple_of(i * 16, 16), 16)
        v, d = residual[sl, :], d_n2[sl, :]
        r = lax.rsqrt(jnp.mean(v * v, axis=1, keepdims=True) + EPS)
        scaled = d * gain[...]
        mean = jnp.mean(scaled * v, axis=1, keepdims=True)
        total = wide(cot[sl, :]) + r * scaled - v * (r * r * r * mean)
        d_residual[sl, :] = total
        d_res[sl, :] = total.astype(BF)
        d_gain[...] += jnp.sum(d * v * r, axis=0, keepdims=True)
        return 0

    lax.fori_loop(0, rows // 16, norm_back, 0)
    segment_rows(segments, k_seg, reach)
    load.wait()

    def send(j, _):
        pair = lax.rem(me // 2 + 1 + j, 8)
        both = dot(d_res[...], wo[pair // 2, pl.ds(lax.rem(pair, 2) * 2, 2)].reshape(256, width), ((1,), (1,))).astype(BF)
        for i in (0, 1):
            e = pair * 2 + i
            d_mine[e] = both[:, i * 128 : (i + 1) * 128]

            @pl.when(e != me)
            def _():
                remote(d_mine.at[e], d_out.at[me], msem.at[0], msem.at[1], (e // 4, lax.rem(e, 4), c)).start()

        return 0

    lax.fori_loop(0, 8, send, 0)
    d_out[me] = d_mine[me]
    A = wo.reshape(16, rows, width)
    load_a = pltpu.make_async_copy(a_h, A, lsem.at[0])
    load_a.start()
    plan = [("o", 0), ("o", 1), ("o", 2), ("o", 3), ("w", 0), ("w", 1), ("w", 2), ("w", 3)]
    tile = 256

    def left_load(i):
        kind, k = plan[i]
        which = 1 - c if kind == "o" else c
        cols = pl.ds(pl.multiple_of((which * 4 + k) * tile, tile), tile)
        return pltpu.make_async_copy(n2.at[:, :, cols], nt.at[i % 2], tsem.at[i % 2])

    def left_turn(i):
        turned_into(left, nt.at[i % 2].reshape(16 * rows, tile), slice(None))

    left_load(0).start()
    made = A.reshape(16 * rows, width)
    dw, dw_end = weight_tiles(
        partner, plan, left_load, left_turn, lambda h, n: made[:, h * 1024 + n * 512 : h * 1024 + (n + 1) * 512], left,
        lambda k: ob.at[k % 2], gt, fs, other_w, osem, ors, fsem, gsem.at[0],
        lambda k, h: (dg_o, du_o)[h].at[pl.ds(k * tile, tile), :])
    d_k[...] = jnp.zeros_like(d_k)
    d_v[...] = jnp.zeros_like(d_v)
    load_a.wait()
    dw(0)
    dw(1)
    landed(d_out.at[pl.ds(0, 15)], msem.at[1])
    count = (pads + 16) * 2 * rows

    def block(i, _):
        band = pl.ds(pl.multiple_of((2 * i + c) * rows, rows), rows + reach)
        kf, vf = kv.at[0].reshape(count, 128), kv.at[1].reshape(count, 128)
        q, k, dd = q_rot[i], kf[band, :], d_out[i]
        scores, allowed = band_scores(q, k, column(q_seg[pl.ds(i, 1), :])[:, 0:1], k_seg[:, band], scale, reach)
        probs = jnp.where(allowed, jnp.exp(scores - lse[i]), 0.0)
        d_probs = dot(dd, vf[band, :], ((1,), (1,)))
        delta = jnp.sum(dd.astype(F32) * o_ref[i].astype(F32), axis=1, keepdims=True)
        d_scores = (probs * (d_probs - delta)).astype(BF)
        d_q[i] = (dot(d_scores, k, ((1,), (0,))) * scale).astype(BF)
        d_k[band, :] += dot(d_scores, q, ((0,), (0,))) * scale
        d_v[band, :] += dot(probs.astype(BF), dd, ((0,), (0,)))
        return 0

    def store(sl, v):
        output[sl, :] = residual[sl, :] + v

    go("f3 f0 d3 d0")
    done = 0
    for upto, words in ((3, "M3 M0 M2 M1 d2 d1"), (6, "f2 f1"), (11, "b31 b02"), (16, "")):
        lax.fori_loop(done, upto, block, 0)
        go(words)
        done = upto

    def pack(i, _):
        at = pl.ds(pl.multiple_of(((pads + i) * 2 + 1 - c) * rows, rows), rows)
        other[0, i] = d_k[at, :].astype(BF)
        other[1, i] = d_v[at, :].astype(BF)
        return 0

    lax.fori_loop(0, 16, pack, 0)
    remote(other, got, msem.at[2], msem.at[3], partner).start()
    go("h30 h03")
    landed(got, msem.at[3])
    d_gains[...] = jnp.zeros_like(d_gains)

    def undo(i, _):
        at = pl.ds(pl.multiple_of(((pads + i) * 2 + c) * rows, rows), rows)
        cs, sn = rope_at(near, far, i)
        both = lin[i]
        rq = lax.rsqrt(column(tot[pl.ds(i, 1), :]) / width + EPS)
        rk = lax.rsqrt(column(tot[pl.ds(16 + i, 1), :]) / width + EPS)
        dk = (d_k[at, :] + wide(got[0, i])).astype(BF).astype(F32)
        d_lin[i, :, 256:] = (d_v[at, :] + wide(got[1, i])).astype(BF)
        uq = turned_back(wide(d_q[i]), cs, sn)
        uk = turned_back(dk, cs, sn)
        q, k = both[:, :128], both[:, 128:256]
        d_gains[0:1, :] += jnp.sum(uq * q * rq, axis=0, keepdims=True)
        d_gains[1:2, :] += jnp.sum(uk * k * rk, axis=0, keepdims=True)
        uq, uk = uq * gq[...], uk * gk[...]
        d_un[0, i] = uq
        d_un[1, i] = uk
        sums[pl.ds(i, 1), :] = row_sums(uq * q)
        sums[pl.ds(16 + i, 1), :] = row_sums(uk * k)
        return 0

    lax.fori_loop(0, 16, undo, 0)

    def meanwhile():
        go("b21 b12 b32 b01")
        dw(2)
        dw(3)

    share_sums(net, sums, sums_all, inner, lsem.at[1], msem.at[4], msem.at[5], meanwhile)

    def finish(i, _):
        both = lin[i]
        for s in (0, 1):
            r = lax.rsqrt(column(tot[pl.ds(16 * s + i, 1), :]) / width + EPS)
            mean = column(inner[pl.ds(16 * s + i, 1), :]) / width
            own = both[:, 128 * s : 128 * (s + 1)]
            d_lin[i, :, 128 * s : 128 * (s + 1)] = (r * d_un[s, i] - own * (r * r * r * mean)).astype(BF)
        return 0

    lax.fori_loop(0, 16, finish, 0)
    go("h31 h02")
    dw(4)
    go("h20 h13 Q")
    dw(5)
    go("h32 h01")
    dw(6)
    go("h10 h23")
    dw(7)
    go("h21 h12 q")
    sc.last(store)
    dw_end()
    landed(d_out.at[pl.ds(0, 15)], msem.at[0])
    landed(other, msem.at[2])
    net.finish()


def run_attend_back(scale, pads, d_n2, cot, gain, wo, p_out, residual, q_rot, kv, q_seg, segments, lse, o, lin, tot, near, far, gq, gk, n2, a_h, half, cid, cut=96):
    R, D = d_n2.shape
    DMA = pltpu.SemaphoreType.DMA
    S = jax.ShapeDtypeStruct
    A = pl.BlockSpec(memory_space=pl.ANY)
    M = pl.BlockSpec(memory_space=pltpu.VMEM)
    V = pltpu.VMEM
    span = (pads + 16) * 2 * R
    return pl.pallas_call(
        functools.partial(attend_back_kernel, scale, pads, cut),
        out_shape=(S((16, R, 384), BF), S((8, 128), F32), S((R, D), F32), S((R, D), F32), S((1, D), F32),
                   S((4, 256, D), BF), S(half, F32), S(half, F32)),
        in_specs=[M, M, M, A, A] + [M] * 13 + [A, A],
        out_specs=(M,) * 5 + (A,) * 3,
        scratch_shapes=[V((2, 16, R, 256), BF), V((256, 16 * R), BF), V((2, 256, D), BF), V((256, D), BF), V((2, 256, 1024), F32),
                        DMA((2,)), DMA((4,)), DMA((4,)), DMA((2,)), DMA((1,)), V((R, D), BF), V((1, span), F32), V((4, 4, R, D), BF), V(wo.shape, BF), V((16, R, 128), BF), V((16, R, 128), BF), V((16, R, 128), BF),
                        V((span, 128), F32), V((span, 128), F32), V((2, 16, R, 128), BF), V((2, 16, R, 128), BF),
                        V((2, 16, R, 128), F32), V((32, 128), F32), V((16, 32, 128), F32), V((32, 128), F32),
                        DMA((2,)), DMA((10,)), DMA((64,))] + rs_scratch(cut, R, D),
        compiler_params=pltpu.CompilerParams(collective_id=cid, has_side_effects=True, vmem_limit_bytes=63 * 2**20),
        name="attend_back",
    )(d_n2, cot, gain, wo, p_out, residual, q_rot, kv, q_seg, segments, lse, o, lin, tot, near, far, gq, gk, n2, a_h)
def dot(a, b, dims):
    return lax.dot_general(a, b, (dims, ((), ())), preferred_element_type=jnp.float32)


def local_chip(
    inputs, cotangent, segments, expert_ids, gate_weights, fill_order, norm1_gain, w_query, w_key,
    w_value, w_output, query_gain, key_gain, norm2_gain, expert_gate, expert_up, expert_down,
):
    chips = 16
    devices = 2 * chips
    rows, width = inputs.shape
    u, z, core = place()
    chip = u * 4 + z
    device = chip * 2 + core
    topk = expert_ids.shape[1]
    experts_n = chips
    capacity = 9 * rows * devices * topk // (8 * experts_n)
    one_hot = expert_ids[:, :, None] == jnp.arange(experts_n, dtype=jnp.int32)[None, None, :]
    chosen = jnp.any(one_hot, axis=1)
    weight = jnp.sum(jnp.where(one_hot, gate_weights[:, :, None], 0.0), axis=1)
    earlier = (fill_order[None, :] < fill_order[:, None]).astype(jnp.bfloat16)
    rank = dot(earlier, chosen.astype(jnp.bfloat16), ((1,), (0,)))
    rank = jnp.where(chosen, rank, -1.0)
    gains = jnp.stack([norm1_gain, query_gain, key_gain, norm2_gain]).astype(F32)
    blank = jnp.zeros_like(gains)
    gains = jnp.where(core == 0, jnp.concatenate([gains, blank], axis=1), jnp.concatenate([blank, gains], axis=1))
    gains = jnp.broadcast_to(gains[None], (chips, 4, 128))
    block = jnp.concatenate(
        [weight.T[:, None, :], rank.T[:, None, :], gains, jnp.zeros((chips, 2, 128), F32)], axis=1)
    side = width // 2
    n1_rows, lin, w_qkv, squares, swapped, cot_a = run_qkv(
        inputs, w_query, w_key, w_value, block, cotangent[:, :side], 2)
    gains = jnp.sum(swapped.reshape(chips, 2, 8, 128), axis=1)
    gain_one, gain_two = gains[:, 2].reshape(1, width), gains[:, 5].reshape(1, width)
    gq, gk = (lax.dynamic_slice_in_dim(gains[:, i], chip, 1, 0) for i in (3, 4))
    rank_all = swapped[:, 1, :]
    taken = rank_all >= 0.0
    counts = jnp.sum(taken.astype(F32), axis=1)
    before = jnp.cumsum(counts) - counts
    kept = taken & (before[:, None] + rank_all < float(capacity))
    share = jnp.where(kept, swapped[:, 0, :], 0.0).reshape(chips, 2, rows)
    share = lax.dynamic_index_in_dim(share, core, 1, keepdims=False)


    half_dim = HEAD_DIM // 2
    inv_freq = jnp.exp(jnp.arange(half_dim, dtype=F32) * (-2.0 * math.log(ROPE_BASE) / HEAD_DIM))
    inv_freq = jnp.concatenate([inv_freq, inv_freq])[None, :]
    sign = jnp.where(jnp.arange(HEAD_DIM) < half_dim, -1.0, 1.0)[None, :]
    within = jnp.arange(rows, dtype=F32)[:, None] * inv_freq
    starts = ((jnp.arange(chips, dtype=jnp.int32) * 2 + core) * rows).astype(F32)[:, None] * inv_freq
    near = jnp.stack([jnp.cos(within), sign * jnp.sin(within)])
    far = jnp.stack([jnp.cos(starts), sign * jnp.sin(starts)])
    pads = chips // 4
    marks = segments.astype(F32)
    q_seg = lax.dynamic_index_in_dim(marks.reshape(chips, 2, rows), core, 1, keepdims=False)
    marks = marks.reshape(1, -1)
    scale = 1.0 / math.sqrt(HEAD_DIM)
    tokens = chips * rows
    w_o, q_rot, kv, head_out, log_total, attended, residual, normed_two, cot_b = run_attend(
        scale, pads, lin, squares, near, far, gq, gk, q_seg, marks, w_output, inputs, gain_two, cotangent[:, side:], 4)

    d_normed_two, mixed, n2_rows, d_pre, _other, d_expert_down = run_expert(
        normed_two, cot_a, cot_b, share, expert_gate, expert_up, expert_down, 6)
    d_lin, d_qk_gains, output, d_residual, d_gain_two, _other, d_expert_gate, d_expert_up = run_attend_back(
        scale, pads, d_normed_two, cotangent, gain_two, w_o, mixed, residual, q_rot, kv, q_seg, marks, log_total, head_out,
        lin, squares, near, far, gq, gk, n2_rows.reshape(chips, rows, width), d_pre.reshape(chips, rows, -1), expert_gate.shape, 7)
    d_w_output, d_inputs, d_w_query, d_w_key, d_w_value, d_gains = run_finish(
        d_lin, w_qkv, n1_rows, attended, inputs, d_residual, gain_one, d_gain_two, d_qk_gains, 8)
    return (
        output,
        d_inputs,
        d_gains[0],
        d_w_query,
        d_w_key,
        d_w_value,
        d_w_output,
        d_gains[2],
        d_gains[3],
        d_gains[1],
        d_expert_gate,
        d_expert_up,
        d_expert_down,
    )
def whole(mesh, step, rows):
    return jax.shard_map(
        step,
        mesh=mesh,
        in_specs=(
            P(rows, None),
            P(rows, None),
            P(),
            P(rows, None),
            P(rows, None),
            P(rows),
            P(rows),
            P(rows, None),
            P(rows, None),
            P(rows, None),
            P(rows, None),
            P(rows),
            P(rows),
            P(rows),
            P(rows, None),
            P(rows, None),
            P(rows, None),
        ),
        out_specs=(
            P(rows, None),
            P(rows, None),
            P(rows),
            P(rows, None),
            P(rows, None),
            P(rows, None),
            P(rows, None),
            P(rows),
            P(rows),
            P(rows),
            P(rows, None),
            P(rows, None),
            P(rows, None),
        ),
        check_vma=False,
    )


def solution(mesh):
    groups, blk_size = mesh.shape["ulysses"], mesh.shape["blk"]

    def step(*args):
        if groups != 4 or blk_size != 8 or args[7].shape[1] // HEAD_DIM != groups * blk_size // 2:
            return whole(mesh, local, ("ulysses", "blk"))(*args)
        chips = Mesh(mesh.devices.reshape(groups, blk_size // 2, 2), ("ulysses", "z", "core"))
        return whole(chips, local_chip, ("ulysses", "z", "core"))(*args)

    return step
```

```python
import functools
import math

import jax
import jax.numpy as jnp
from jax import lax
from jax.experimental import pallas as pl
from jax.experimental.pallas import tpu as pltpu
from jax.sharding import Mesh
from jax.sharding import PartitionSpec as P

HEAD_DIM = 128


EPS = 1e-05
ROPE_BASE = 10000.0
NEG = -1e30


def as_sent(value):

    def short(part):
        return part.astype(jnp.bfloat16) if part.dtype == jnp.float32 else part

    return jax.tree.map(short, value)


def passed_along(block, axis, distance):
    devices = range(lax.axis_size(axis))
    route = [((i - distance) % len(devices), i) for i in devices]
    return lax.ppermute(block, axis, route)


def prefix(value, axis, join, neutral):
    count, mine = (lax.axis_size(axis), lax.axis_index(axis))
    pieces = lax.all_gather(value, axis)
    subtotal = jnp.full_like(value, 0) + jnp.asarray(neutral, value.dtype)

    def hop(position, subtotal):
        longer = join(subtotal, pieces[position])
        return jnp.where(position < mine, longer, subtotal)

    return lax.fori_loop(0, count - 1, hop, subtotal)


def partner_2(block, axis, bit):
    count = lax.axis_size(axis)
    route = []
    for low in range(count):
        high = low | 1 << bit
        if high != low and high < count:
            route += [(low, high), (high, low)]
    return lax.ppermute(block, axis, route)


def norm_rows(values, gain_vec):
    return values * lax.rsqrt(jnp.mean(values * values, axis=-1, keepdims=True) + EPS) * gain_vec


def rotate(values, positions):
    half_dim = HEAD_DIM // 2
    heads_here = values.shape[1] // HEAD_DIM
    inv_freq = jnp.exp(
        jnp.arange(half_dim, dtype=jnp.float32) * (-2.0 * math.log(ROPE_BASE) / HEAD_DIM)
    )
    angles = positions.astype(jnp.float32)[:, None] * inv_freq[None, :]
    cosine = jnp.cos(angles)[:, None, :]
    sin_t = jnp.sin(angles)[:, None, :]
    shaped = values.reshape(values.shape[0], heads_here, HEAD_DIM)
    lower_half = shaped[..., :half_dim]
    upper_half = shaped[..., half_dim:]
    turned = jnp.concatenate(
        [lower_half * cosine - upper_half * sin_t, upper_half * cosine + lower_half * sin_t],
        axis=-1,
    )
    return turned.reshape(values.shape)


def attn_inputs(q_lin, k_lin, gain_q, gain_k, positions):
    return (
        rotate(norm_rows(q_lin, gain_q), positions),
        rotate(norm_rows(k_lin, gain_k), positions),
    )


def banded(shaped, fill_value):
    earlier = jnp.concatenate([jnp.full_like(shaped[:1], fill_value), shaped[:-1]], axis=0)
    return jnp.concatenate([earlier, shaped], axis=1)


def unbanded(band, local_rows):
    earlier = band[:, :local_rows]
    own_part = band[:, local_rows:]
    moved_up = jnp.concatenate([earlier[1:], jnp.zeros_like(earlier[:1])], axis=0)
    return own_part + moved_up


def add_counts(earlier, later):
    return earlier + later


def expert_move(buffer):
    return lax.all_to_all(buffer, ("ulysses", "blk"), split_axis=0, concat_axis=0, tiled=True)


def to_head_layout(values):
    return jax.tree.map(
        lambda part, own: part.astype(own.dtype),
        lax.all_to_all(as_sent(values), "ulysses", split_axis=1, concat_axis=0, tiled=True),
        values,
    )


def to_token_layout(values):
    return jax.tree.map(
        lambda part, own: part.astype(own.dtype),
        lax.all_to_all(as_sent(values), "ulysses", split_axis=0, concat_axis=1, tiled=True),
        values,
    )


def local(
    inputs,
    cotangent,
    segments,
    expert_ids,
    gate_weights,
    fill_order,
    norm1_gain,
    w_query,
    w_key,
    w_value,
    w_output,
    query_gain,
    key_gain,
    norm2_gain,
    expert_gate,
    expert_up,
    expert_down,
):
    blk_size = lax.axis_size("blk")
    groups = lax.axis_size("ulysses")
    devices = blk_size * groups
    local_rows = inputs.shape[0]
    model_width = inputs.shape[1]
    blk_index = lax.axis_index("blk")
    group_index = lax.axis_index("ulysses")
    device_index = group_index * blk_size + blk_index
    positions = device_index * local_rows + jnp.arange(local_rows, dtype=jnp.int32)
    heads_dev = model_width // groups // HEAD_DIM
    score_scale = 1.0 / math.sqrt(HEAD_DIM)
    layer_in = inputs.astype(jnp.float32)
    dense = (w_query, w_key, w_value, w_output, norm1_gain, query_gain, key_gain, norm2_gain)
    gathered = (
        lax.all_gather(dense[0], ("ulysses", "blk"), axis=0, tiled=True),
        lax.all_gather(dense[1], ("ulysses", "blk"), axis=0, tiled=True),
        lax.all_gather(dense[2], ("ulysses", "blk"), axis=0, tiled=True),
        lax.all_gather(dense[3], ("ulysses", "blk"), axis=0, tiled=True),
        lax.all_gather(dense[4], ("ulysses", "blk"), axis=0, tiled=True),
        lax.all_gather(dense[5], ("ulysses", "blk"), axis=0, tiled=True),
        lax.all_gather(dense[6], ("ulysses", "blk"), axis=0, tiled=True),
        lax.all_gather(dense[7], ("ulysses", "blk"), axis=0, tiled=True),
    )
    w_q, w_k, w_v, w_o = (gathered[0], gathered[1], gathered[2], gathered[3])
    gain_one = gathered[4].astype(jnp.float32)
    gain_q = gathered[5].astype(jnp.float32)
    gain_k = gathered[6].astype(jnp.float32)
    gain_two = gathered[7].astype(jnp.float32)
    normed_one = norm_rows(layer_in, gain_one).astype(jnp.bfloat16)
    q_lin = jnp.dot(normed_one, w_q, preferred_element_type=jnp.float32)
    k_lin = jnp.dot(normed_one, w_k, preferred_element_type=jnp.float32)
    v_lin = jnp.dot(normed_one, w_v, preferred_element_type=jnp.float32)
    (q_rot, k_rot), pre_back = jax.vjp(
        lambda q_in, k_in, gq_in, gk_in: attn_inputs(q_in, k_in, gq_in, gk_in, positions),
        q_lin,
        k_lin,
        gain_q,
        gain_k,
    )
    q_heads, k_heads, v_heads = to_head_layout(
        (q_rot.astype(jnp.bfloat16), k_rot.astype(jnp.bfloat16), v_lin.astype(jnp.bfloat16))
    )
    group_ids = jnp.arange(groups, dtype=jnp.int32)[:, None]
    row_ids = jnp.arange(local_rows, dtype=jnp.int32)[None, :]
    q_pos = (group_ids * blk_size + blk_index) * local_rows + row_ids
    q_seg = segments[q_pos]
    four_shape = (groups, local_rows, heads_dev, HEAD_DIM)
    q_four = q_heads.reshape(four_shape)

    def score_block(k_now, source):
        k_pos = (group_ids * blk_size + source) * local_rows + row_ids
        k_seg = banded(segments[k_pos], -1)
        k_pos = banded(k_pos, 0)
        k_band = banded(k_now.reshape(four_shape), 0)
        raw_scores = (
            jnp.einsum("gqhd,gkhd->gqhk", q_four, k_band, preferred_element_type=jnp.float32)
            * score_scale
        )
        allowed = (k_seg[:, None, :] == q_seg[:, :, None]) & (
            k_pos[:, None, :] <= q_pos[:, :, None]
        )
        return (raw_scores, allowed[:, :, None, :], k_band)

    def forward_step(flash_state, kv_stack, step_id):
        run_max, run_sum, run_out = flash_state
        source = jnp.mod(blk_index - step_id, blk_size)
        raw_scores, allowed, k_band = score_block(kv_stack[0], source)
        raw_scores = jnp.where(allowed, raw_scores, NEG)
        new_max = jnp.maximum(run_max, jnp.max(raw_scores, axis=-1))
        shrink = jnp.exp(run_max - new_max)
        weights = jnp.where(allowed, jnp.exp(raw_scores - new_max[..., None]), 0.0)
        run_sum = run_sum * shrink + jnp.sum(weights, axis=-1)
        v_band = banded(kv_stack[1].reshape(four_shape), 0)
        run_out = run_out * shrink[..., None] + jnp.einsum(
            "gqhk,gkhd->gqhd",
            weights.astype(jnp.bfloat16),
            v_band,
            preferred_element_type=jnp.float32,
        )
        return (new_max, run_sum, run_out)

    start_state = (
        jnp.full((groups, local_rows, heads_dev), NEG, jnp.float32),
        jnp.zeros((groups, local_rows, heads_dev), jnp.float32),
        jnp.zeros(four_shape, jnp.float32),
    )
    kv_home = jnp.stack([k_heads, v_heads])
    first_state = forward_step(start_state, kv_home, 0)

    def forward_turn(step_id, loop_state):
        flash_state, kv_stack = loop_state
        moved = passed_along(kv_stack, "blk", 1)
        return (forward_step(flash_state, moved, step_id), moved)

    final_state, unused_kv = lax.fori_loop(1, blk_size, forward_turn, (first_state, kv_home))
    run_max, run_sum, run_out = final_state
    o_four = (run_out / run_sum[..., None]).astype(jnp.bfloat16)
    log_total = run_max + jnp.log(run_sum)
    o_heads = o_four.reshape(groups * local_rows, heads_dev * HEAD_DIM)
    attended = to_token_layout(o_heads)
    residual = layer_in + jnp.dot(attended, w_o, preferred_element_type=jnp.float32)
    normed_two_f, norm_two_back = jax.vjp(norm_rows, residual, gain_two)
    normed_two = normed_two_f.astype(jnp.bfloat16)
    experts_n = devices // 2
    topk = expert_ids.shape[1]
    per_source = 2 * local_rows * topk // experts_n
    half_slots = per_source // 2
    capacity = 9 * local_rows * devices * topk // (8 * experts_n)
    slots_all = experts_n * per_source
    tokens_local = jnp.arange(local_rows, dtype=jnp.int32)
    chosen = jnp.sum(
        (expert_ids[:, :, None] == jnp.arange(experts_n, dtype=jnp.int32)[None, None, :]).astype(
            jnp.int32
        ),
        axis=1,
    )
    by_fill = jnp.zeros((local_rows,), jnp.int32).at[fill_order].set(tokens_local)
    sorted_rows = chosen[by_fill]
    before = jnp.cumsum(sorted_rows, axis=0) - sorted_rows
    rank_all = before[fill_order]
    pair_rank = jnp.take_along_axis(rank_all, expert_ids, axis=1)
    counts = jnp.sum(chosen, axis=0)
    offsets = prefix(counts, ("ulysses", "blk"), add_counts, jnp.zeros_like(counts))
    kept_pair = offsets[expert_ids] + pair_rank < capacity
    pair_slot = expert_ids * per_source + pair_rank
    pair_index = tokens_local[:, None] * topk + jnp.arange(topk, dtype=jnp.int32)[None, :]
    slot_pair = (
        jnp.zeros((slots_all,), jnp.int32).at[pair_slot.reshape(-1)].set(pair_index.reshape(-1))
    )
    slot_live = (
        jnp.zeros((slots_all,), jnp.bool_).at[pair_slot.reshape(-1)].set(kept_pair.reshape(-1))
    )
    slot_token = slot_pair // topk
    send_rows = jnp.where(slot_live[:, None], normed_two[slot_token], jnp.zeros((), jnp.bfloat16))
    received = expert_move(send_rows.reshape(devices, half_slots, model_width)).reshape(
        devices * half_slots, model_width
    )
    parity = jnp.mod(blk_index, 2)
    partner = partner_2((expert_gate, expert_up, expert_down), "blk", 0)

    def joined(own_half, other_half):
        lower_part = jnp.where(parity == 0, own_half, other_half)
        upper_part = jnp.where(parity == 0, other_half, own_half)
        return jnp.concatenate([lower_part, upper_part], axis=0)

    gate_full = joined(expert_gate, partner[0])
    up_full = joined(expert_up, partner[1])
    down_full = joined(expert_down, partner[2])
    gate_pre = jnp.dot(received, gate_full, preferred_element_type=jnp.float32)
    up_pre = jnp.dot(received, up_full, preferred_element_type=jnp.float32)
    hidden = (jax.nn.silu(gate_pre) * up_pre).astype(jnp.bfloat16)
    produced = jnp.dot(hidden, down_full, preferred_element_type=jnp.float32).astype(jnp.bfloat16)
    returned = expert_move(produced.reshape(devices, half_slots, model_width)).reshape(
        slots_all, model_width
    )
    pair_share = jnp.where(kept_pair, gate_weights, 0.0)
    mixed = jnp.einsum("tk,tkd->td", pair_share, returned[pair_slot].astype(jnp.float32))
    output = residual + mixed
    grad_out = cotangent.astype(jnp.float32)
    slot_share = jnp.where(slot_live, gate_weights.reshape(-1)[slot_pair], 0.0)
    grad_send = (slot_share[:, None] * grad_out[slot_token]).astype(jnp.bfloat16)
    grad_rows = expert_move(grad_send.reshape(devices, half_slots, model_width)).reshape(
        devices * half_slots, model_width
    )
    d_down_full = jnp.einsum("rf,rd->fd", hidden, grad_rows, preferred_element_type=jnp.float32)
    d_hidden = jnp.einsum("rd,fd->rf", grad_rows, down_full, preferred_element_type=jnp.float32)
    sigma = jax.nn.sigmoid(gate_pre)
    d_gate_pre = (d_hidden * up_pre * sigma * (1.0 + gate_pre * (1.0 - sigma))).astype(jnp.bfloat16)
    d_up_pre = (d_hidden * gate_pre * sigma).astype(jnp.bfloat16)
    d_gate_full = jnp.einsum("rd,rf->df", received, d_gate_pre, preferred_element_type=jnp.float32)
    d_up_full = jnp.einsum("rd,rf->df", received, d_up_pre, preferred_element_type=jnp.float32)
    d_pair_rows = (
        jnp.einsum("rf,df->rd", d_gate_pre, gate_full, preferred_element_type=jnp.float32)
        + jnp.einsum("rf,df->rd", d_up_pre, up_full, preferred_element_type=jnp.float32)
    ).astype(jnp.bfloat16)
    back_rows = expert_move(d_pair_rows.reshape(devices, half_slots, model_width)).reshape(
        slots_all, model_width
    )
    d_normed_two = jnp.sum(
        jnp.where(kept_pair[:, :, None], back_rows[pair_slot].astype(jnp.float32), 0.0), axis=1
    )
    half_rows = expert_gate.shape[0]
    half_hidden = expert_down.shape[0]

    def halves(full_grad, size):
        own_half = lax.dynamic_slice_in_dim(full_grad, parity * size, size, 0)
        other_half = lax.dynamic_slice_in_dim(full_grad, (1 - parity) * size, size, 0)
        return (own_half, other_half)

    gate_own, gate_other = halves(d_gate_full, half_rows)
    up_own, up_other = halves(d_up_full, half_rows)
    down_own, down_other = halves(d_down_full, half_hidden)
    partner_grads = (
        partner_2(gate_other.astype(jnp.bfloat16), "blk", 0).astype(gate_other.dtype),
        partner_2(up_other.astype(jnp.bfloat16), "blk", 0).astype(up_other.dtype),
        partner_2(down_other.astype(jnp.bfloat16), "blk", 0).astype(down_other.dtype),
    )
    d_expert_gate = gate_own + partner_grads[0]
    d_expert_up = up_own + partner_grads[1]
    d_expert_down = down_own + partner_grads[2]
    d_resid_norm, d_gain_two = norm_two_back(d_normed_two)
    d_residual = grad_out + d_resid_norm
    d_res_low = d_residual.astype(jnp.bfloat16)
    d_attended = jnp.einsum("te,de->td", d_res_low, w_o, preferred_element_type=jnp.float32).astype(
        jnp.bfloat16
    )
    d_o_heads = to_head_layout(d_attended)
    d_o_four = d_o_heads.reshape(four_shape)
    row_delta = jnp.sum(d_o_four.astype(jnp.float32) * o_four.astype(jnp.float32), axis=-1)

    def back_turn(step_id, loop_state):
        moving, dq_acc = loop_state
        source = jnp.mod(blk_index - step_id, blk_size)
        k_now = moving[0].astype(jnp.bfloat16)
        v_now = moving[1].astype(jnp.bfloat16)
        raw_scores, allowed, k_band = score_block(k_now, source)
        prob_rows = jnp.where(allowed, jnp.exp(raw_scores - log_total[..., None]), 0.0)
        v_band = banded(v_now.reshape(four_shape), 0)
        d_probs = jnp.einsum(
            "gqhd,gkhd->gqhk", d_o_four, v_band, preferred_element_type=jnp.float32
        )
        d_scores = (prob_rows * (d_probs - row_delta[..., None])).astype(jnp.bfloat16)
        dv_band = jnp.einsum(
            "gqhk,gqhd->gkhd",
            prob_rows.astype(jnp.bfloat16),
            d_o_four,
            preferred_element_type=jnp.float32,
        )
        dk_band = (
            jnp.einsum("gqhk,gqhd->gkhd", d_scores, q_four, preferred_element_type=jnp.float32)
            * score_scale
        )
        dq_acc = (
            dq_acc
            + jnp.einsum("gqhk,gkhd->gqhd", d_scores, k_band, preferred_element_type=jnp.float32)
            * score_scale
        )
        flat_shape = moving[2].shape
        dk_new = moving[2] + unbanded(dk_band, local_rows).reshape(flat_shape)
        dv_new = moving[3] + unbanded(dv_band, local_rows).reshape(flat_shape)
        moving = passed_along(
            jnp.stack([moving[0], moving[1], dk_new, dv_new]).astype(jnp.bfloat16), "blk", 1
        ).astype(jnp.float32)
        return (moving, dq_acc)

    zero_rows = jnp.zeros(k_heads.shape, jnp.float32)
    start_moving = jnp.stack(
        [k_heads.astype(jnp.float32), v_heads.astype(jnp.float32), zero_rows, zero_rows]
    )
    moving, dq_acc = lax.fori_loop(
        0, blk_size, back_turn, (start_moving, jnp.zeros(four_shape, jnp.float32))
    )
    d_q_send = dq_acc.astype(jnp.bfloat16).reshape(k_heads.shape)
    d_k_send = moving[2].astype(jnp.bfloat16)
    d_v_send = moving[3].astype(jnp.bfloat16)
    d_q_rot, d_k_rot, d_v_lin = to_token_layout((d_q_send, d_k_send, d_v_send))
    d_q_lin, d_k_lin, d_gain_q, d_gain_k = pre_back(
        (d_q_rot.astype(jnp.float32), d_k_rot.astype(jnp.float32))
    )
    d_q_low = d_q_lin.astype(jnp.bfloat16)
    d_k_low = d_k_lin.astype(jnp.bfloat16)
    d_normed_one = jnp.einsum("te,de->td", d_q_low, w_q, preferred_element_type=jnp.float32)
    d_normed_one = d_normed_one + jnp.einsum(
        "te,de->td", d_k_low, w_k, preferred_element_type=jnp.float32
    )
    d_normed_one = d_normed_one + jnp.einsum(
        "te,de->td", d_v_lin, w_v, preferred_element_type=jnp.float32
    )
    unused_norm, norm_one_back = jax.vjp(norm_rows, layer_in, gain_one)
    d_layer_in, d_gain_one = norm_one_back(d_normed_one)
    d_inputs = d_residual + d_layer_in
    d_qk_heads = to_head_layout((d_q_low, d_k_low))
    rows_all = (
        lax.all_gather(normed_one, "ulysses", axis=0, tiled=True),
        lax.all_gather(d_res_low, "ulysses", axis=0, tiled=True),
    )
    head_cols = model_width // groups
    piece_rows = model_width // devices

    def by_owner(part):
        rest = part.shape[1:]
        shaped = part.reshape((groups, blk_size, piece_rows) + rest)
        return jnp.swapaxes(shaped, 0, 1).reshape((model_width,) + rest)

    part_q = jnp.einsum("td,te->de", rows_all[0], d_qk_heads[0], preferred_element_type=jnp.float32)
    part_k = jnp.einsum("td,te->de", rows_all[0], d_qk_heads[1], preferred_element_type=jnp.float32)
    part_v = jnp.einsum("td,te->de", rows_all[0], d_v_send, preferred_element_type=jnp.float32)
    part_o = jnp.einsum("te,td->ed", o_heads, rows_all[1], preferred_element_type=jnp.float32)
    blk_sums = (
        lax.psum_scatter(
            by_owner(part_q).astype(jnp.bfloat16), "blk", scatter_dimension=0, tiled=True
        ).astype(jnp.float32),
        lax.psum_scatter(
            by_owner(part_k).astype(jnp.bfloat16), "blk", scatter_dimension=0, tiled=True
        ).astype(jnp.float32),
        lax.psum_scatter(
            by_owner(part_v).astype(jnp.bfloat16), "blk", scatter_dimension=0, tiled=True
        ).astype(jnp.float32),
        lax.psum_scatter(
            part_o.astype(jnp.bfloat16), "blk", scatter_dimension=0, tiled=True
        ).astype(jnp.float32),
        lax.psum_scatter(
            by_owner(d_gain_one).astype(jnp.bfloat16), "blk", scatter_dimension=0, tiled=True
        ).astype(jnp.float32),
        lax.psum_scatter(
            by_owner(d_gain_q).astype(jnp.bfloat16), "blk", scatter_dimension=0, tiled=True
        ).astype(jnp.float32),
        lax.psum_scatter(
            by_owner(d_gain_k).astype(jnp.bfloat16), "blk", scatter_dimension=0, tiled=True
        ).astype(jnp.float32),
        lax.psum_scatter(
            by_owner(d_gain_two).astype(jnp.bfloat16), "blk", scatter_dimension=0, tiled=True
        ).astype(jnp.float32),
    )

    def widened(part):
        return lax.dynamic_update_slice_in_dim(
            jnp.zeros((part.shape[0], model_width), jnp.float32), part, group_index * head_cols, 1
        )

    col_sums = (
        lax.psum_scatter(
            widened(blk_sums[0]).astype(jnp.bfloat16), "ulysses", scatter_dimension=0, tiled=True
        ).astype(jnp.float32),
        lax.psum_scatter(
            widened(blk_sums[1]).astype(jnp.bfloat16), "ulysses", scatter_dimension=0, tiled=True
        ).astype(jnp.float32),
        lax.psum_scatter(
            widened(blk_sums[2]).astype(jnp.bfloat16), "ulysses", scatter_dimension=0, tiled=True
        ).astype(jnp.float32),
        lax.psum_scatter(
            blk_sums[4].astype(jnp.bfloat16), "ulysses", scatter_dimension=0, tiled=True
        ).astype(jnp.float32),
        lax.psum_scatter(
            blk_sums[5].astype(jnp.bfloat16), "ulysses", scatter_dimension=0, tiled=True
        ).astype(jnp.float32),
        lax.psum_scatter(
            blk_sums[6].astype(jnp.bfloat16), "ulysses", scatter_dimension=0, tiled=True
        ).astype(jnp.float32),
        lax.psum_scatter(
            blk_sums[7].astype(jnp.bfloat16), "ulysses", scatter_dimension=0, tiled=True
        ).astype(jnp.float32),
    )
    result_grads = (
        col_sums[0],
        col_sums[1],
        col_sums[2],
        blk_sums[3],
        col_sums[3],
        col_sums[4],
        col_sums[5],
        col_sums[6],
    )
    return (
        output,
        d_inputs,
        result_grads[4],
        result_grads[0],
        result_grads[1],
        result_grads[2],
        result_grads[3],
        result_grads[5],
        result_grads[6],
        result_grads[7],
        d_expert_gate,
        d_expert_up,
        d_expert_down,
    )


MESH = pl.DeviceIdType.MESH
P1 = 96

def place():
    u = lax.axis_index("ulysses"); z = lax.axis_index("z"); c = lax.axis_index("core")
    return u, z, c

def ag_kernel(cut, x_ref, o_ref, local_sem, s_sem, zr, xr, yr, d1r, d2r, bs, br, bzr):
    u, z, c = place()
    Z = 4
    R = x_ref.shape[0]
    ux, uy = u ^ 1, u ^ 2
    xn, yn, up, dn = (ux, z, c), (uy, z, c), (u, z + 1, c), (u, z - 1, c)
    has_up, has_dn = z < Z - 1, z > 0
    bar = pltpu.get_barrier_semaphore()
    for n in (xn, yn):
        pl.semaphore_signal(bar, inc=1, device_id=n, device_id_type=MESH)
    @pl.when(has_up)
    def _():
        pl.semaphore_signal(bar, inc=1, device_id=up, device_id_type=MESH)
    @pl.when(has_dn)
    def _():
        pl.semaphore_signal(bar, inc=1, device_id=dn, device_id_type=MESH)
    pl.semaphore_wait(bar, 2 + has_up.astype(jnp.int32) + has_dn.astype(jnp.int32))
    sends = []
    def copy(src, dst, ss, rs, dev):
        return pltpu.make_async_remote_copy(src_ref=src, dst_ref=dst, send_sem=ss, recv_sem=rs, device_id=dev, device_id_type=MESH)
    def go(cond, make):
        idx = len(sends)
        def mk():
            return make(s_sem.at[idx])
        sends.append((cond, mk))
        if cond is None:
            mk().start()
        else:
            pl.when(cond)(lambda: mk().start())
    def both(a, b):
        if a is None: return b
        if b is None: return a
        return jnp.logical_and(a, b)
    def wait(cond, ref, sem):
        def w():
            pltpu.make_async_copy(ref, ref, sem).wait()
        if cond is None: w()
        else: pl.when(cond)(w)
    own = pltpu.make_async_copy(x_ref, o_ref.at[u, z], local_sem)
    own.start()
    A = slice(0, cut)
    h = cut // 2
    def oa(uu, zz, lo=0, n=cut):
        return o_ref.at[uu, zz, pl.ds(lo, n), :]
    def spread(s, zz, cond):
        src = (lambda: x_ref.at[pl.ds(0, cut), :]) if s == 0 else (lambda: oa(u, zz))
        go(cond, lambda sm: copy(src(), oa(u, zz), sm, xr.at[zz], xn))
        go(cond, lambda sm: copy(src(), oa(u, zz), sm, yr.at[zz], yn))
    def cross(zz, cond):
        wait(cond, oa(ux, zz), xr.at[zz])
        go(cond, lambda sm: copy(oa(ux, zz, 0, h), oa(ux, zz, 0, h), sm, d1r.at[zz], yn))
        wait(cond, oa(uy, zz), yr.at[zz])
        go(cond, lambda sm: copy(oa(uy, zz, h, h), oa(uy, zz, h, h), sm, d2r.at[zz], xn))
    rb = R - cut
    hb = rb // 2
    def ob(uu, zz, lo=0, n=None):
        return o_ref.at[uu, zz, pl.ds(cut + lo, rb if n is None else n), :]
    go(has_up, lambda sm: copy(x_ref.at[pl.ds(0, cut), :], oa(u, z), sm, zr.at[z], up))
    go(has_dn, lambda sm: copy(x_ref.at[pl.ds(0, cut), :], oa(u, z), sm, zr.at[z], dn))
    if rb:
        go(None, lambda sm: copy(x_ref.at[pl.ds(cut, rb), :], ob(u, z), sm, br.at[0], xn))
        go(None, lambda sm: copy(x_ref.at[pl.ds(cut, rb), :], ob(u, z), sm, br.at[1], yn))
    spread(0, z, None)
    if rb:
        wait(None, ob(ux, z), br.at[0])
        go(None, lambda sm: copy(ob(ux, z, 0, hb), ob(ux, z, 0, hb), sm, br.at[2], yn))
        wait(None, ob(uy, z), br.at[1])
        go(None, lambda sm: copy(ob(uy, z, hb, hb), ob(uy, z, hb, hb), sm, br.at[3], xn))
    own.wait()
    def quad(zz):
        return o_ref.at[:, zz, pl.ds(cut, rb), :]
    def zs(s):
        zl, zh = z - s, z + s
        cl, ch = zl >= 0, zh < Z
        zlc, zhc = jnp.maximum(zl, 0), jnp.minimum(zh, Z - 1)
        return (zlc, cl, has_up, up), (zhc, ch, has_dn, dn)
    prev = [(z, None)]
    for s in range(1, Z):
        cur = []
        for (zz, cond, fwd, dev) in zs(s):
            wait(cond, oa(u, zz), zr.at[zz])
            go(both(cond, fwd), lambda sm, zz=zz, dev=dev: copy(oa(u, zz), oa(u, zz), sm, zr.at[zz], dev))
            spread(s, zz, cond)
            cur.append((zz, cond))
        if rb and s == 1:
            wait(None, ob(u ^ 3, z, 0, hb), br.at[2])
            wait(None, ob(u ^ 3, z, hb, hb), br.at[3])
            go(has_up, lambda sm: copy(quad(z), quad(z), sm, bzr.at[z], up))
            go(has_dn, lambda sm: copy(quad(z), quad(z), sm, bzr.at[z], dn))
        elif rb:
            for (zz, cond, fwd, dev) in zs(s - 1):
                wait(cond, quad(zz), bzr.at[zz])
                go(both(cond, fwd), lambda sm, zz=zz, dev=dev: copy(quad(zz), quad(zz), sm, bzr.at[zz], dev))
        for zz, cond in prev:
            cross(zz, cond)
        prev = cur
    if rb:
        for (zz, cond, fwd, dev) in zs(Z - 1):
            wait(cond, quad(zz), bzr.at[zz])
    for zz, cond in prev:
        cross(zz, cond)
    for zz in range(Z):
        wait(None, oa(u ^ 3, zz, 0, h), d1r.at[zz])
        wait(None, oa(u ^ 3, zz, h, h), d2r.at[zz])
    for cond, mk in sends:
        if cond is None: mk().wait_send()
        else: pl.when(cond)(lambda mk=mk: mk().wait_send())

def ag16(x, cid, cut=P1, space=pl.ANY):
    R, D = x.shape
    DMA = pltpu.SemaphoreType.DMA
    return pl.pallas_call(
        functools.partial(ag_kernel, cut),
        out_shape=jax.ShapeDtypeStruct((4, 4, R, D), x.dtype),
        in_specs=[pl.BlockSpec(memory_space=space)],
        out_specs=pl.BlockSpec(memory_space=space),
        scratch_shapes=[DMA, DMA((64,)), DMA((4,)), DMA((4,)), DMA((4,)), DMA((4,)), DMA((4,)), DMA((4,)), DMA((4,)), DMA((4,))],
        compiler_params=pltpu.CompilerParams(collective_id=cid, has_side_effects=True, vmem_limit_bytes=48 * 2**20),
        name="gather_rows",
    )(x)
F32 = jnp.float32
BF = jnp.bfloat16


class Net:
    def __init__(self, sems):
        self.sems, self.sends = sems, []
        self.u, self.z, self.c = place()
        u, z, c = self.u, self.z, self.c
        self.ux, self.uy, self.ud = u ^ 1, u ^ 2, u ^ 3
        self.xn, self.yn, self.up, self.dn = (u ^ 1, z, c), (u ^ 2, z, c), (u, z + 1, c), (u, z - 1, c)
        self.has_up, self.has_dn = z < 3, z > 0
        self.at = [z == i for i in range(4)]

    def barrier(self, more=()):
        bar = pltpu.get_barrier_semaphore()
        for n in (self.xn, self.yn) + tuple(more):
            pl.semaphore_signal(bar, inc=1, device_id=n, device_id_type=MESH)
        for cond, n in ((self.has_up, self.up), (self.has_dn, self.dn)):
            pl.when(cond)(lambda n=n: pl.semaphore_signal(bar, inc=1, device_id=n, device_id_type=MESH))
        pl.semaphore_wait(bar, 2 + len(more) + self.has_up.astype(jnp.int32) + self.has_dn.astype(jnp.int32))

    def go(self, cond, src, dst, rsem, dev):
        idx = len(self.sends)

        def mk():
            return pltpu.make_async_remote_copy(
                src_ref=src(), dst_ref=dst(), send_sem=self.sems.at[idx], recv_sem=rsem(),
                device_id=dev, device_id_type=MESH)

        self.sends.append((cond, mk))
        if cond is None:
            mk().start()
        else:
            pl.when(cond)(lambda: mk().start())

    def wait(self, cond, ref, sem):
        def w():
            pltpu.make_async_copy(ref(), ref(), sem).wait()

        if cond is None:
            w()
        else:
            pl.when(cond)(w)

    def finish(self):
        for cond, mk in self.sends:
            if cond is None:
                mk().wait_send()
            else:
                pl.when(cond)(lambda mk=mk: mk().wait_send())


def strips(rows, body, step=16):
    def it(i, _):
        body(pl.ds(pl.multiple_of(i * step, step), step))
        return 0

    lax.fori_loop(0, rows // step, it, 0)


def wide(v):
    return v.astype(F32)


class Scatter:
    def __init__(self, net, cut, P, bufs):
        self.net, self.cut, self.P = net, cut, P
        (self.mid1, self.mid2, self.fx, self.fy, self.be, self.ab, self.bbe, self.bab, self.bm,
         self.m1s, self.m2s, self.fxs, self.fys, self.bes, self.abs_, self.bbes, self.babs, self.bms) = bufs
        self.R = P.shape[2]
        self.h = cut // 2
        self.rb = self.R - cut
        self.hb = self.rb // 2

    def mid_send(self, zd):
        net, P, h = self.net, self.P, self.h
        net.go(None, lambda: P.at[net.ud, zd, pl.ds(0, h), :], lambda: self.mid1.at[zd], lambda: self.m1s.at[zd], net.xn)
        net.go(None, lambda: P.at[net.ud, zd, pl.ds(h, h), :], lambda: self.mid2.at[zd], lambda: self.m2s.at[zd], net.yn)

    def bfirst(self, zd):
        net, P, cut, rb = self.net, self.P, self.cut, self.rb
        if rb and zd > 0:
            net.go(net.at[0], lambda: P.at[:, zd, pl.ds(cut, rb), :], lambda: self.bbe.at[zd], lambda: self.bbes.at[zd], net.up)
        if rb and zd < 3:
            net.go(net.at[3], lambda: P.at[:, zd, pl.ds(cut, rb), :], lambda: self.bab.at[zd], lambda: self.babs.at[zd], net.dn)

    def direct(self, zd):
        net, P, h = self.net, self.P, self.h
        net.go(None, lambda: P.at[net.ux, zd, pl.ds(0, h), :], lambda: self.fx.at[zd, pl.ds(0, h), :], lambda: self.fxs.at[zd, 0], net.xn)
        net.go(None, lambda: P.at[net.uy, zd, pl.ds(h, h), :], lambda: self.fy.at[zd, pl.ds(h, h), :], lambda: self.fys.at[zd, 1], net.yn)

    def first(self, zd):
        self.mid_send(zd)
        self.bfirst(zd)
        self.direct(zd)

    def mids(self, zd):
        net, P, h, mid1, mid2 = self.net, self.P, self.h, self.mid1, self.mid2

        def add1(sl):
            mid1[zd, sl, :] = (wide(mid1[zd, sl, :]) + wide(P[net.uy, zd, sl, :])).astype(BF)

        def add2(sl):
            mid2[zd, sl, :] = (wide(mid2[zd, sl, :]) + wide(P[net.ux, zd, pl.ds(h + sl.start, 16), :])).astype(BF)

        net.wait(None, lambda: mid1.at[zd], self.m1s.at[zd])
        strips(h, add1)
        net.go(None, lambda: mid1.at[zd], lambda: self.fy.at[zd, pl.ds(0, h), :], lambda: self.fys.at[zd, 0], net.yn)
        net.wait(None, lambda: mid2.at[zd], self.m2s.at[zd])
        strips(h, add2)
        net.go(None, lambda: mid2.at[zd], lambda: self.fx.at[zd, pl.ds(h, h), :], lambda: self.fxs.at[zd, 1], net.xn)

    def route(self, zd, zz):
        if zz < zd:
            return True, self.net.up
        return False, self.net.dn

    def bhop(self, zd, zz):
        net, P, cut, rb = self.net, self.P, self.cut, self.rb
        if not rb:
            return
        upward, dev = self.route(zd, zz)
        buf, sems = (self.bbe, self.bbes) if upward else (self.bab, self.babs)
        here = net.at[zz]
        net.wait(here, lambda: buf.at[zd], sems.at[zd])

        def add():
            for q in range(4):
                def one(sl, q=q):
                    buf[zd, q, sl, :] = (wide(buf[zd, q, sl, :]) + wide(P[q, zd, pl.ds(cut + sl.start, 16), :])).astype(BF)
                strips(rb, one)

        pl.when(here)(add)
        net.go(here, lambda: buf.at[zd], lambda: buf.at[zd], lambda: sems.at[zd], dev)

    def square(self, zd, cond):
        net, h = self.net, self.h
        for half in (0, 1):
            net.wait(cond, lambda: self.fx.at[zd, pl.ds(half * h, h), :], self.fxs.at[zd, half])
            net.wait(cond, lambda: self.fy.at[zd, pl.ds(half * h, h), :], self.fys.at[zd, half])

    def local(self, zd, sl):
        return wide(self.P[self.net.u, zd, sl, :]) + wide(self.fx[zd, sl, :]) + wide(self.fy[zd, sl, :])

    def hop(self, zd, zz):
        net = self.net
        upward, dev = self.route(zd, zz)
        buf, sems = (self.be, self.bes) if upward else (self.ab, self.abs_)
        here = net.at[zz]
        self.square(zd, here)
        if zz in (0, 3):
            def begin(sl):
                self.fx[zd, sl, :] = self.local(zd, sl).astype(BF)

            pl.when(here)(lambda: strips(self.cut, begin))
            net.go(here, lambda: self.fx.at[zd], lambda: buf.at[zd], lambda: sems.at[zd], dev)
        else:
            def plus(sl):
                buf[zd, sl, :] = (self.local(zd, sl) + wide(buf[zd, sl, :])).astype(BF)

            net.wait(here, lambda: buf.at[zd], sems.at[zd])
            pl.when(here)(lambda: strips(self.cut, plus))
            net.go(here, lambda: buf.at[zd], lambda: buf.at[zd], lambda: sems.at[zd], dev)

    def bquad(self):
        net, P, cut, rb, hb, bm, bms = self.net, self.P, self.cut, self.rb, self.hb, self.bm, self.bms
        if not rb:
            return
        z = net.z
        net.wait(net.has_dn, lambda: self.bbe.at[z], self.bbes.at[z])
        net.wait(net.has_up, lambda: self.bab.at[z], self.babs.at[z])
        for q in range(4):
            def fold(sl, q=q):
                s = wide(P[q, z, pl.ds(cut + sl.start, 16), :])
                s = s + jnp.where(net.has_dn, wide(self.bbe[z, q, sl, :]), 0.0)
                s = s + jnp.where(net.has_up, wide(self.bab[z, q, sl, :]), 0.0)
                bm[q, sl, :] = s.astype(BF)
            strips(rb, fold)
        net.go(None, lambda: bm.at[net.ud, pl.ds(0, hb), :], lambda: bm.at[4, pl.ds(0, hb), :], lambda: bms.at[0], net.xn)
        net.go(None, lambda: bm.at[net.ud, pl.ds(hb, hb), :], lambda: bm.at[5, pl.ds(0, hb), :], lambda: bms.at[1], net.yn)
        net.go(None, lambda: bm.at[net.ux, pl.ds(0, hb), :], lambda: bm.at[6, pl.ds(0, hb), :], lambda: bms.at[2], net.xn)
        net.go(None, lambda: bm.at[net.uy, pl.ds(hb, hb), :], lambda: bm.at[7, pl.ds(hb, hb), :], lambda: bms.at[3], net.yn)

    def bquad2(self):
        net, rb, hb, bm, bms = self.net, self.rb, self.hb, self.bm, self.bms
        if not rb:
            return

        def add4(sl):
            bm[4, sl, :] = (wide(bm[4, sl, :]) + wide(bm[net.uy, sl, :])).astype(BF)

        def add5(sl):
            bm[5, sl, :] = (wide(bm[5, sl, :]) + wide(bm[net.ux, pl.ds(hb + sl.start, 16), :])).astype(BF)

        net.wait(None, lambda: bm.at[4, pl.ds(0, hb), :], bms.at[0])
        strips(hb, add4)
        net.go(None, lambda: bm.at[4, pl.ds(0, hb), :], lambda: bm.at[7, pl.ds(0, hb), :], lambda: bms.at[4], net.yn)
        net.wait(None, lambda: bm.at[5, pl.ds(0, hb), :], bms.at[1])
        strips(hb, add5)
        net.go(None, lambda: bm.at[5, pl.ds(0, hb), :], lambda: bm.at[6, pl.ds(hb, hb), :], lambda: bms.at[5], net.xn)

    def last(self, store):
        net, cut, rb, hb, bm, bms = self.net, self.cut, self.rb, self.hb, self.bm, self.bms
        z = net.z
        self.square(z, None)

        def own(sl):
            s = self.local(z, sl)
            s = s + jnp.where(net.has_dn, wide(self.be[z, sl, :]), 0.0)
            s = s + jnp.where(net.has_up, wide(self.ab[z, sl, :]), 0.0)
            store(sl, s)

        net.wait(net.has_dn, lambda: self.be.at[z], self.bes.at[z])
        net.wait(net.has_up, lambda: self.ab.at[z], self.abs_.at[z])
        strips(cut, own)
        if rb:
            net.wait(None, lambda: bm.at[6, pl.ds(0, hb), :], bms.at[2])
            net.wait(None, lambda: bm.at[6, pl.ds(hb, hb), :], bms.at[5])
            net.wait(None, lambda: bm.at[7, pl.ds(0, hb), :], bms.at[4])
            net.wait(None, lambda: bm.at[7, pl.ds(hb, hb), :], bms.at[3])
            strips(rb, lambda sl: store(
                pl.ds(cut + sl.start, 16), wide(bm[net.u, sl, :]) + wide(bm[6, sl, :]) + wide(bm[7, sl, :])))


def steps_of(sc, text):
    names = {"m": sc.mid_send, "f": sc.bfirst, "d": sc.direct, "M": sc.mids, "h": sc.hop, "b": sc.bhop, "Q": sc.bquad, "q": sc.bquad2}
    words = []
    for letter in text:
        if letter in names:
            words.append((letter, []))
        else:
            words[-1][1].append(int(letter))
    return [functools.partial(names[name], *digits) for name, digits in words]


def run_steps(steps):
    for one in steps:
        one()


def rs_scratch(cut, R, D):
    h, rb = cut // 2, R - cut
    V = lambda *s: pltpu.VMEM(s, BF)
    S = pltpu.SemaphoreType.DMA
    return [V(4, h, D), V(4, h, D), V(4, cut, D), V(4, cut, D), V(4, cut, D), V(4, cut, D),
            V(4, 4, max(rb, 16), D), V(4, 4, max(rb, 16), D), V(8, max(rb, 16), D),
            S((4,)), S((4,)), S((4, 2)), S((4, 2)), S((4,)), S((4,)), S((4,)), S((4,)), S((6,))]


def rs_kernel(cut, P, o_ref, ssem, *scr):
    net = Net(ssem)
    net.barrier()
    sc = Scatter(net, cut, P, scr)

    def store(sl, v):
        o_ref[sl, :] = v.astype(o_ref.dtype)

    for zd in (3, 0, 2, 1):
        sc.first(zd)
    for zd in (3, 0, 2, 1):
        sc.mids(zd)
    sc.hop(3, 0); sc.hop(0, 3); sc.bhop(3, 1); sc.bhop(0, 2)
    sc.hop(2, 0); sc.hop(1, 3); sc.bhop(2, 1); sc.bhop(1, 2)
    sc.hop(3, 1); sc.hop(0, 2); sc.bhop(3, 2); sc.bhop(0, 1)
    sc.hop(1, 0); sc.hop(2, 3); sc.bquad()
    sc.hop(2, 1); sc.hop(1, 2)
    sc.hop(3, 2); sc.hop(0, 1); sc.bquad2()
    sc.last(store)
    net.finish()


def rs16(p, cid, cut=96, dtype=F32):
    _, _, R, D = p.shape
    DMA = pltpu.SemaphoreType.DMA
    return pl.pallas_call(
        functools.partial(rs_kernel, cut),
        out_shape=jax.ShapeDtypeStruct((R, D), dtype),
        in_specs=[pl.BlockSpec(memory_space=pltpu.VMEM)],
        out_specs=pl.BlockSpec(memory_space=pltpu.VMEM),
        scratch_shapes=[DMA((96,))] + rs_scratch(cut, R, D),
        compiler_params=pltpu.CompilerParams(collective_id=cid, has_side_effects=True, vmem_limit_bytes=56 * 2**20),
        name="scatter_rows",
    )(p)


class Gather:
    def __init__(self, net, rows, cut, at, plane, sems):
        self.net, self.rows, self.cut, self.ref, self.plane = net, rows, cut, at, plane
        self.zr, self.xr, self.yr, self.d1, self.d2, self.br, self.bz = sems
        self.h, self.rb = cut // 2, rows - cut
        self.hb = self.rb // 2
        z = net.z
        self.near = []
        for s in range(4):
            zl, zh = z - s, z + s
            self.near.append((
                (jnp.maximum(zl, 0), zl >= 0, jnp.logical_and(zl >= 0, net.has_up), net.up),
                (jnp.minimum(zh, 3), zh < 4, jnp.logical_and(zh < 4, net.has_dn), net.dn)))

    def same(self, cond, uu, zz, lo, n, sem, dev):
        ref = lambda: self.ref(uu, zz, lo, n)
        self.net.go(cond, ref, ref, sem, dev)

    def outward(self, zz, cond):
        net, cut = self.net, self.cut
        self.same(cond, net.u, zz, 0, cut, lambda: self.xr.at[zz], net.xn)
        self.same(cond, net.u, zz, 0, cut, lambda: self.yr.at[zz], net.yn)

    def begin(self):
        net, cut, rb, z = self.net, self.cut, self.rb, self.net.z
        self.same(net.has_up, net.u, z, 0, cut, lambda: self.zr.at[z], net.up)
        self.same(net.has_dn, net.u, z, 0, cut, lambda: self.zr.at[z], net.dn)
        if rb:
            self.same(None, net.u, z, cut, rb, lambda: self.br.at[0], net.xn)
            self.same(None, net.u, z, cut, rb, lambda: self.br.at[1], net.yn)
        self.outward(z, None)

    def begin2(self):
        net, cut, rb, hb, z = self.net, self.cut, self.rb, self.hb, self.net.z
        if rb:
            net.wait(None, lambda: self.ref(net.ux, z, cut, rb), self.br.at[0])
            self.same(None, net.ux, z, cut, hb, lambda: self.br.at[2], net.yn)
            net.wait(None, lambda: self.ref(net.uy, z, cut, rb), self.br.at[1])
            self.same(None, net.uy, z, cut + hb, hb, lambda: self.br.at[3], net.xn)

    def along(self, s):
        net = self.net
        for zz, cond, fwd, dev in self.near[s]:
            net.wait(cond, lambda zz=zz: self.ref(net.u, zz, 0, self.cut), self.zr.at[zz])
            self.same(fwd, net.u, zz, 0, self.cut, lambda zz=zz: self.zr.at[zz], dev)
            self.outward(zz, cond)

    def quads(self, s):
        net, cut, rb, hb, z = self.net, self.cut, self.rb, self.hb, self.net.z
        if not rb:
            return
        if s == 0:
            net.wait(None, lambda: self.ref(net.ud, z, cut, hb), self.br.at[2])
            net.wait(None, lambda: self.ref(net.ud, z, cut + hb, hb), self.br.at[3])
            whole = lambda: self.plane(z, cut, rb)
            net.go(net.has_up, whole, whole, lambda: self.bz.at[z], net.up)
            net.go(net.has_dn, whole, whole, lambda: self.bz.at[z], net.dn)
            return
        for zz, cond, fwd, dev in self.near[s]:
            whole = lambda zz=zz: self.plane(zz, cut, rb)
            net.wait(cond, whole, self.bz.at[zz])
            net.go(fwd, whole, whole, lambda zz=zz: self.bz.at[zz], dev)

    def planes(self, s):
        if s == 0:
            return ((self.net.z, None),)
        return tuple((zz, cond) for zz, cond, _f, _d in self.near[s])

    def cross(self, s):
        net, h, cut = self.net, self.h, self.cut
        for zz, cond in self.planes(s):
            net.wait(cond, lambda zz=zz: self.ref(net.ux, zz, 0, cut), self.xr.at[zz])
            self.same(cond, net.ux, zz, 0, h, lambda zz=zz: self.d1.at[zz], net.yn)
            net.wait(cond, lambda zz=zz: self.ref(net.uy, zz, 0, cut), self.yr.at[zz])
            self.same(cond, net.uy, zz, h, h, lambda zz=zz: self.d2.at[zz], net.xn)

    def settle(self, s):
        net, h = self.net, self.h
        for zz, cond in self.planes(s):
            net.wait(cond, lambda zz=zz: self.ref(net.ud, zz, 0, h), self.d1.at[zz])
            net.wait(cond, lambda zz=zz: self.ref(net.ud, zz, h, h), self.d2.at[zz])


def ag_sems():
    S = pltpu.SemaphoreType.DMA
    return [S((4,)) for _ in range(7)]


def greet(net, chips=16):
    bar = pltpu.get_barrier_semaphore()

    def hello(j, _):
        t = lax.rem(net.u * 4 + net.z + j, chips)
        pl.semaphore_signal(bar, inc=1, device_id=(t // 4, lax.rem(t, 4), net.c), device_id_type=MESH)
        return 0

    lax.fori_loop(1, chips, hello, 0)
    pl.semaphore_signal(bar, inc=1, device_id=(net.u, net.z, 1 - net.c), device_id_type=MESH)
    pl.semaphore_wait(bar, chips)


def each_chip(net, body, chips=16):
    def one(j, _):
        t = lax.rem(net.u * 4 + net.z + j, chips)
        body(t, (t // 4, lax.rem(t, 4), net.c))
        return 0

    lax.fori_loop(1, chips, one, 0)


def remote(src, dst, ssem, rsem, dev):
    return pltpu.make_async_remote_copy(
        src_ref=src, dst_ref=dst, send_sem=ssem, recv_sem=rsem, device_id=dev, device_id_type=MESH)


def landed(ref, sem):
    pltpu.make_async_copy(ref, ref, sem).wait()


def segment_rows(segments, k_seg, reach):
    k_seg[:, 0:reach] = jnp.full((1, reach), -1.0, F32)
    k_seg[:, reach:] = segments[...]


def rope_at(near, far, i):
    cf, sf = far[0, pl.ds(i, 1), :], far[1, pl.ds(i, 1), :]
    cn, sn = near[0], near[1]
    return cf * cn - sf * sn, sf * cn + cf * sn


def row_sums(v):
    return jnp.sum(v.T, axis=0, keepdims=True)


def column(row):
    return jnp.broadcast_to(row, (row.shape[1], row.shape[1])).T


def share_sums(net, sums, sums_all, out, lsem, ssem, rsem, meanwhile=None):
    me = net.u * 4 + net.z
    own = pltpu.make_async_copy(sums, sums_all.at[me], lsem)
    own.start()
    each_chip(net, lambda t, dev: remote(sums, sums_all.at[me], ssem, rsem, dev).start())
    own.wait()
    if meanwhile is not None:
        meanwhile()
    part = sums_all.at[pl.ds(0, 15)]
    landed(part, rsem)
    total = sums_all[0]
    for i in range(1, 16):
        total = total + sums_all[i]
    out[...] = total
    landed(part, ssem)


def greet_all(net, count=32):
    bar = pltpu.get_barrier_semaphore()
    me = net.u * 8 + net.z * 2 + net.c

    def hello(j, _):
        t = lax.rem(me + j, count)
        pl.semaphore_signal(bar, inc=1, device_id=(t // 8, lax.rem(t, 8) // 2, lax.rem(t, 2)), device_id_type=MESH)
        return 0

    lax.fori_loop(1, count, hello, 0)
    pl.semaphore_wait(bar, count - 1)


def weight_tiles(partner, plan, load, turn, right, left, ob, gt, fs, other, osem, ors, fsem, gsem, out):
    side = fs.shape[2]

    def sent(k):
        return remote(ob(k), other.at[k], osem.at[k], ors.at[k], partner)

    def tile_at(i):
        kind, k = plan[i]
        if load is not None and i + 1 < len(plan):
            load(i + 1).start()
        if kind == "o":
            if k >= 2:
                sent(k - 2).wait_send()
        else:
            landed(other.at[k], ors.at[k])
            fetch = pltpu.make_async_copy(other.at[k], gt, gsem)
            fetch.start()
        if load is not None:
            load(i).wait()
        turn(i)
        if kind == "w":
            fetch.wait()
        for h in (0, 1):
            if kind == "w" and k > 0:
                landed(fs.at[h], fsem.at[h])
            for n in (0, 1):
                made = dot(left[...], right(h, n), ((1,), (0,)))
                cols = slice(h * side + n * 512, h * side + (n + 1) * 512)
                if kind == "o":
                    ob(k)[:, cols] = made.astype(BF)
                else:
                    fs[h, :, n * 512 : (n + 1) * 512] = made + wide(gt[:, cols])
            if kind == "w":
                pltpu.make_async_copy(fs.at[h], out(k, h), fsem.at[h]).start()
        if kind == "o":
            sent(k).start()

    def finish():
        count = len(plan) // 2
        for k in (count - 2, count - 1):
            sent(k).wait_send()
        for h in (0, 1):
            landed(fs.at[h], fsem.at[h])

    return tile_at, finish


def turned_into(left, flat, cols, tile=256):
    def one(b, _):
        sl = pl.ds(pl.multiple_of(b * tile, tile), tile)
        left[:, sl] = flat[sl, cols].T
        return 0

    lax.fori_loop(0, flat.shape[0] // tile, one, 0)


def qkv_kernel(cut, x_ref, wq, wk, wv, block, cot, n1_o, lin_o, wf_o, tot, sw, C, X, lin, wf, nb, gain, sums, sums_all, lsem, nsem, msem, ssem, csem, *gs):
    net = Net(ssem)
    u, z, c = net.u, net.z, net.c
    me = u * 4 + z
    rows, width = X.shape[2], X.shape[3]
    partner = (u, z, 1 - c)
    own = pltpu.make_async_copy(x_ref, X.at[u, z], lsem.at[0])
    own.start()

    def piece(t, i):
        return ((wq, wk, wv)[i].at[:, pl.ds(pl.multiple_of(t * 128, 128), 128)], wf.at[me, c, :, pl.ds(i * 128, 128)])

    own_w = [pltpu.make_async_copy(*piece(me, i), lsem.at[1]) for i in range(3)]
    for one in own_w:
        one.start()
    own_c = pltpu.make_async_copy(cot, C.at[u, z], lsem.at[3])
    own_c.start()
    dev_me = me * 2 + c
    greet_all(net)
    own.wait()
    ga = Gather(net, rows, cut, lambda uu, zz, lo, n: X.at[uu, zz, pl.ds(lo, n), :],
                lambda zz, lo, n: X.at[:, zz, pl.ds(lo, n), :], gs[:7])
    netc = Net(csem)
    gc = Gather(netc, rows, cut, lambda uu, zz, lo, n: C.at[uu, zz, pl.ds(lo, n), :],
                lambda zz, lo, n: C.at[:, zz, pl.ds(lo, n), :], gs[7:])
    ga.begin()

    def tell(j, _):
        t = lax.rem(dev_me + j, 32)
        remote(block.at[t // 2], sw.at[dev_me], msem.at[6], msem.at[7], (t // 8, lax.rem(t, 8) // 2, lax.rem(t, 2))).start()
        return 0

    lax.fori_loop(1, 32, tell, 0)
    sw[dev_me] = block[me]

    def columns(t, dev):
        for i in range(3):
            remote(*piece(t, i), msem.at[0], msem.at[1], dev).start()

    each_chip(net, columns)

    def plane(zz):
        def chunk(uu, _):
            slot = lax.rem(uu, 2)
            k = uu * 4 + zz

            def norm(i, _):
                sl = pl.ds(pl.multiple_of(i * 16, 16), 16)
                v = X[uu, zz, sl, :].astype(F32)
                r = lax.rsqrt(jnp.mean(v * v, axis=1, keepdims=True) + EPS)
                nb[slot, sl, :] = (v * r * gain[...]).astype(BF)
                return 0

            def stored(s):
                return pltpu.make_async_copy(nb.at[s], n1_o.at[k], nsem.at[s])

            pl.when(uu >= 2)(lambda: stored(slot).wait())
            lax.fori_loop(0, rows // 16, norm, 0)
            stored(slot).start()
            got = dot(nb[slot], wf[...].reshape(width, wf.shape[-1]), ((1,), (0,)))
            lin[k] = got
            q, kk = got[:, :128], got[:, 128:256]
            sums[pl.ds(k, 1), :] = row_sums(q * q)
            sums[pl.ds(16 + k, 1), :] = row_sums(kk * kk)
            return 0

        lax.fori_loop(0, 4, chunk, 0)
        for s in (0, 1):
            pltpu.make_async_copy(nb.at[s], n1_o.at[0], nsem.at[s]).wait()

    def compute(s):
        for zz, cond in ga.planes(s):
            if cond is None:
                plane(zz)
            else:
                pl.when(cond)(lambda zz=zz: plane(zz))

    ga.begin2()
    ga.along(1)
    ga.quads(0)
    ga.cross(0)
    landed(wf.at[0, 0], lsem.at[1])
    landed(wf.at[pl.ds(0, 15), 0], msem.at[1])
    to_partner = remote(wf.at[:, c], wf.at[:, c], msem.at[2], msem.at[3], partner)
    to_partner.start()
    own_c.wait()
    ga.along(2)
    ga.quads(1)
    ga.cross(1)
    gc.begin()
    landed(sw.at[pl.ds(0, 31)], msem.at[7])
    for e in range(16):
        gain[:, e * 128 : (e + 1) * 128] = sw[2 * e, 2:3, :] + sw[2 * e + 1, 2:3, :]
    ga.settle(0)
    landed(wf.at[:, 1 - c], msem.at[3])
    keep_w = pltpu.make_async_copy(wf, wf_o, lsem.at[0])
    keep_w.start()
    compute(0)
    gc.begin2()
    ga.along(3)
    ga.quads(2)
    ga.cross(2)
    ga.settle(1)
    gc.along(1)
    gc.quads(0)
    gc.cross(0)
    compute(1)
    ga.quads(3)
    ga.cross(3)
    ga.settle(2)
    gc.along(2)
    gc.quads(1)
    gc.cross(1)
    compute(2)
    ga.settle(3)
    gc.along(3)
    gc.quads(2)
    gc.cross(2)
    compute(3)
    keep = pltpu.make_async_copy(lin, lin_o, lsem.at[1])
    keep.start()
    landed(wf.at[pl.ds(0, 15), 0], msem.at[0])
    landed(wf.at[:, c], msem.at[2])

    def rest():
        gc.quads(3)
        gc.cross(3)

    share_sums(net, sums, sums_all, tot, lsem.at[2], msem.at[4], msem.at[5], rest)
    for s in range(4):
        gc.settle(s)
    landed(sw.at[pl.ds(0, 31)], msem.at[6])
    keep_w.wait()
    keep.wait()
    net.finish()
    netc.finish()


def run_qkv(x, wq, wk, wv, block, cot, cid, cut=96):
    R, D = x.shape
    N = 384
    DMA = pltpu.SemaphoreType.DMA
    S = jax.ShapeDtypeStruct
    V = lambda *s: pltpu.VMEM(s, BF)
    VF = lambda *s: pltpu.VMEM(s, F32)
    A = pl.BlockSpec(memory_space=pl.ANY)
    M = pl.BlockSpec(memory_space=pltpu.VMEM)
    return pl.pallas_call(
        functools.partial(qkv_kernel, cut),
        out_shape=(S((16, R, D), BF), S((16, R, N), F32), S((16, 2, R // 2, N), BF), S((32, 128), F32),
                   S((32, 8, 128), F32), S((4, 4) + cot.shape, BF)),
        in_specs=[A, A, A, A, M, A],
        out_specs=(A, A, A, M, M, A),
        scratch_shapes=[V(4, 4, R, D), VF(16, R, N), V(16, 2, R // 2, N), V(2, R, D), VF(1, D), VF(32, 128), VF(16, 32, 128),
                        DMA((4,)), DMA((2,)), DMA((8,)), DMA((64,)), DMA((64,))] + ag_sems() + ag_sems(),
        compiler_params=pltpu.CompilerParams(collective_id=cid, has_side_effects=True, vmem_limit_bytes=63 * 2**20),
        name="project",
    )(x, wq, wk, wv, block, cot)


def group_of(t):
    g = t // 2
    return jnp.where(g == 0, 3, jnp.where(g == 1, 0, jnp.where(g == 2, 2, 1)))


def expert_kernel(cut, n2, cot_a, cot_b, share_rows, gate, up, down, d_n2, p_out, n2_o, a_o, other, dd_o,
                  X, C, GU, W, A, hid, pb, fs, share, lsem, wsem, wrs, psem, osem, tsem, ors, fsem, sa, sr, *scr):
    ga_sems, rs_bufs = scr[:7], scr[7:]
    na, nr = Net(sa), Net(sr)
    u, z, c = na.u, na.z, na.c
    partner = (u, z, 1 - c)
    rows, width = X.shape[2], X.shape[3]
    ff = W.shape[0]
    half, half_ff = gate.shape[0], down.shape[0]
    tokens = 16 * rows
    tile = 256
    span = 512
    side = width // 2
    first = [pltpu.make_async_copy(n2, X.at[u, z], lsem.at[0]),
             pltpu.make_async_copy(cot_a, C.at[:, :, :, pl.ds(0, side)], lsem.at[1]),
             pltpu.make_async_copy(cot_b, C.at[:, :, :, pl.ds(side, side)], lsem.at[5])]

    def weights():
        mine = pl.ds(pl.multiple_of(c * half, half), half)
        mine_ff = pl.ds(pl.multiple_of(c * half_ff, half_ff), half_ff)
        return ((gate, GU.at[mine, pl.ds(0, ff)]), (up, GU.at[mine, pl.ds(ff, ff)]), (down, W.at[mine_ff, :]))

    own_w = [pltpu.make_async_copy(a, b, lsem.at[2 + i]) for i, (a, b) in enumerate(weights())]
    for one in first + own_w:
        one.start()
    na.barrier((partner,))
    first[0].wait()

    def gather(net, buf, sems):
        return Gather(net, rows, cut, lambda uu, zz, lo, n: buf.at[uu, zz, pl.ds(lo, n), :],
                      lambda zz, lo, n: buf.at[:, zz, pl.ds(lo, n), :], sems)

    ga = gather(na, X, ga_sems)
    ga.begin()
    sent_w = [remote(a, b, wsem.at[i], wrs.at[i], partner) for i, (a, b) in enumerate(weights())]
    for one in sent_w:
        one.start()
    for k in range(16):
        share[k // 4, k % 4] = column(share_rows[k : k + 1, :])[:, 0:1]

    def forward(zz):
        pltpu.make_async_copy(X.at[:, zz], n2_o.at[:, zz], psem.at[1]).start()

        def scale(i, _):
            sl = pl.ds(pl.multiple_of(i * 16, 16), 16)
            C[:, zz, sl, :] = (share[:, zz, sl, :] * C[:, zz, sl, :].astype(F32)).astype(BF)
            return 0

        lax.fori_loop(0, rows // 16, scale, 0)

        def inner(n, _):
            gcols = pl.ds(pl.multiple_of(n * span, span), span)
            ucols = pl.ds(pl.multiple_of(ff + n * span, span), span)
            xv = X[:, zz].reshape(4 * rows, width)
            g = dot(xv, GU[:, gcols], ((1,), (0,)))
            uu = dot(xv, GU[:, ucols], ((1,), (0,)))
            s = jax.nn.sigmoid(g)
            gs = g * s
            hid[:, zz, :, gcols] = (gs * uu).astype(BF).reshape(4, rows, span)
            dh = dot(C[:, zz].reshape(4 * rows, width), W[gcols, :], ((1,), (1,)))
            A[:, zz, :, gcols] = (dh * uu * s * (1.0 + g * (1.0 - s))).astype(BF).reshape(4, rows, span)
            A[:, zz, :, ucols] = (dh * gs).astype(BF).reshape(4, rows, span)
            return 0

        lax.fori_loop(0, ff // span, inner, 0)
        pltpu.make_async_copy(A.at[:, zz], a_o.at[:, zz], psem.at[2]).start()
        weight = share[:, zz]

        def flushed(n):
            cols = pl.ds(pl.multiple_of(n * span, span), span)
            slot = lax.rem(n, 2)
            return pltpu.make_async_copy(pb.at[slot], p_out.at[:, zz, :, cols], osem.at[slot])

        def outer(n, _):
            cols = pl.ds(pl.multiple_of(n * span, span), span)
            made = dot(hid[:, zz].reshape(4 * rows, ff), W[:, cols], ((1,), (0,)))
            made = made.astype(BF).astype(F32).reshape(4, rows, span)
            pl.when(n >= 2)(lambda: flushed(n - 2).wait())
            pb[lax.rem(n, 2)] = (weight * made).astype(BF)
            flushed(n).start()
            return 0

        count = width // span
        lax.fori_loop(0, count, outer, 0)
        flushed(count - 2).wait()
        flushed(count - 1).wait()

    def planes(s):
        if s == 0:
            forward(z)
            return

        def one(d, _):
            zz = jnp.where(d == 0, z - s, z + s)
            pl.when(jnp.logical_and(zz >= 0, zz < 4))(lambda: forward(zz))
            return 0

        lax.fori_loop(0, 2, one, 0)

    ga.begin2()
    ga.along(1)
    ga.quads(0)
    ga.cross(0)
    ga.along(2)
    ga.quads(1)
    ga.cross(1)
    ga.settle(0)
    for one in own_w:
        one.wait()
    for one in sent_w:
        one.wait_recv()
    first[1].wait()
    first[2].wait()
    planes(0)
    ga.along(3)
    ga.quads(2)
    ga.cross(2)
    ga.settle(1)
    planes(1)
    ga.quads(3)
    ga.cross(3)
    ga.settle(2)
    planes(2)
    ga.settle(3)
    planes(3)
    na.finish()
    for one in sent_w:
        one.wait_send()
    landed(X, psem.at[1])
    sc = Scatter(nr, cut, X, rs_bufs)

    def backward(t):
        zd = group_of(t)
        base = lax.rem(t, 2) * (width // 2)

        def outer(n, _):
            cols = pl.ds(pl.multiple_of(base + n * span, span), span)
            back = dot(A[:, zd].reshape(4 * rows, 2 * ff), GU[cols, :], ((1,), (1,)))
            X[:, zd, :, cols] = back.astype(BF).reshape(4, rows, span)
            return 0

        lax.fori_loop(0, width // 2 // span, outer, 0)

    def acts(steps, t):
        for at, todo in steps.items():
            def act(todo=todo):
                for one in todo:
                    one()
            pl.when(t == at)(act)

    def at_turns(table):
        return {t: steps_of(sc, words) for t, words in table.items()}

    steps = at_turns({1: "m3f3d3", 3: "m0f0d0", 4: "M3", 5: "m2f2d2b31", 6: "M0", 7: "m1f1d1b02b32"})

    def turn(t, _):
        backward(t)
        acts(steps, t)
        return 0

    lax.fori_loop(0, 8, turn, 0)

    left = W.at[pl.ds(0, tile), :]

    def left_hidden(i):
        kind, k = plan[i]
        which = 1 - c if kind == "o" else c
        turned_into(left, hid.reshape(tokens, ff), pl.ds(pl.multiple_of((which * 2 + k) * tile, tile), tile))

    plan = [("o", 0), ("o", 1), ("w", 0), ("w", 1)]
    made = C.reshape(tokens, width)
    dw, dw_end = weight_tiles(
        partner, plan, None, left_hidden, lambda h, n: made[:, h * side + n * 512 : h * side + (n + 1) * 512], left,
        lambda k: W.at[pl.ds((1 + k % 2) * tile, tile), :], W.at[pl.ds(3 * tile, tile), :], fs, other, tsem, ors, fsem,
        lsem.at[0], lambda k, h: dd_o.at[pl.ds(k * tile, tile), pl.ds(h * side, side)])

    def go(words):
        run_steps(steps_of(sc, words))

    dw(0)
    go("M2b21")
    dw(1)
    go("h30M1b01b12h03")
    dw(2)
    go("h31h02h20h23")
    dw(3)
    go("h32h01h10h13Qh21h12q")

    def store_out(sl, v):
        d_n2[sl, :] = v

    sc.last(store_out)
    landed(A, psem.at[2])
    dw_end()
    nr.finish()


def run_expert(n2, cot_a, cot_b, share, gate, up, down, cid, cut=96):
    R, D = n2.shape
    half, ff = gate.shape
    DMA = pltpu.SemaphoreType.DMA
    S = jax.ShapeDtypeStruct
    V = lambda *s: pltpu.VMEM(s, BF)
    A = pl.BlockSpec(memory_space=pl.ANY)
    M = pl.BlockSpec(memory_space=pltpu.VMEM)
    return pl.pallas_call(
        functools.partial(expert_kernel, cut),
        out_shape=(S((R, D), F32), S((4, 4, R, D), BF), S((4, 4, R, D), BF), S((4, 4, R, 2 * ff), BF),
                   S((2, 256, D), BF), S(down.shape, F32)),
        in_specs=[A, A, A, M, A, A, A],
        out_specs=(M,) + (A,) * 5,
        scratch_shapes=[V(4, 4, R, D), V(4, 4, R, D), V(D, 2 * ff), V(ff, D), V(4, 4, R, 2 * ff), V(4, 4, R, ff),
                        V(2, 4, R, 512), pltpu.VMEM((2, 256, D // 2), F32), pltpu.VMEM((4, 4, R, 1), F32),
                        DMA((6,)), DMA((3,)), DMA((3,)), DMA((3,)), DMA((2,)), DMA((2,)), DMA((2,)), DMA((2,)),
                        DMA((64,)), DMA((96,))] + ag_sems() + rs_scratch(cut, R, D),
        compiler_params=pltpu.CompilerParams(collective_id=cid, has_side_effects=True, vmem_limit_bytes=63 * 2**20),
        name="expert",
    )(n2, cot_a, cot_b, share, gate, up, down)


def finish_kernel(cut, d_lin, wf, n1, att, x_in, d_res, gain, d_gain_two, d_gains,
                  d_wo, d_inputs, d_wq, d_wk, d_wv, gains_o,
                  P, PO, PG, PT, wsum, nt, left, keep, give, got, send, recv, d_n1, d_gain, gb, gr,
                  lsem, tsem, msem, s1, s2, *bufs):
    net, net2 = Net(s1), Net(s2)
    u, z, c = net.u, net.z, net.c
    me = u * 4 + z
    rows, width = P.shape[2], P.shape[3]
    lanes = d_lin.shape[2]
    tokens = 16 * rows
    tile = 256
    partner = (u, z, 1 - c)
    half = len(bufs) // 2
    sc1, sc2 = Scatter(net, cut, P, bufs[:half]), Scatter(net2, cut, PO, bufs[half:])

    def tile_load(k):
        slot = lax.rem(k, 2)
        return pltpu.make_async_copy(n1.at[:, :, pl.ds(pl.multiple_of(k * tile, tile), tile)], nt.at[slot], tsem.at[slot])

    tile_load(0).start()
    greet_all(net)

    def one(words):
        run_steps(steps_of(sc1, words))

    def two(words):
        run_steps(steps_of(sc2, words))

    def group(zd):
        def one(n, _):
            cols = pl.ds(pl.multiple_of(n * 512, 512), 512)
            w = wf.reshape(width, lanes)
            for q in range(4):
                P[q, zd, :, cols] = dot(d_lin[q * 4 + zd], w[cols, :], ((1,), (1,))).astype(BF)
            return 0

        lax.fori_loop(0, width // 512, one, 0)

    for zd in (3, 0, 2, 1):
        group(zd)
        one(f"m{zd}" + (f"f{zd}" if zd in (3, 0) else ""))

    side = width // 2
    own_cols = pl.ds(pl.multiple_of(c * side, side), side)
    give_cols = pl.ds(pl.multiple_of((1 - c) * side, side), side)

    def outer(e, _):
        turned_att = att[e].T
        PG[e // 4, lax.rem(e, 4)] = dot(turned_att, d_res[:, give_cols].astype(BF), ((1,), (0,))).astype(BF)
        PO[e // 4, lax.rem(e, 4)] = dot(turned_att, d_res[:, own_cols].astype(BF), ((1,), (0,))).astype(BF)
        return 0

    lax.fori_loop(0, 16, outer, 0)
    halves = remote(PG, PT, msem.at[6], msem.at[7], partner)
    halves.start()

    def join():
        landed(PT, msem.at[7])

        def add(e, _):
            def strip(sl):
                at = (e // 4, lax.rem(e, 4), sl, slice(None))
                PO[at] = (wide(PO[at]) + wide(PT[at])).astype(BF)

            strips(rows, strip)
            return 0

        lax.fori_loop(0, 16, add, 0)

    def store1(sl, v):
        d_n1[sl, :] = v

    def store2(sl, v):
        wsum[sl, :] = v


    def grads(k):
        if k < 7:
            tile_load(k + 1).start()
        tile_load(k).wait()
        slot = k % 2
        flat = nt.at[slot].reshape(tokens, tile)

        def turn(b, _):
            sl = pl.ds(pl.multiple_of(b * tile, tile), tile)
            left[:, sl] = flat[sl, :].T
            return 0

        lax.fori_loop(0, tokens // tile, turn, 0)
        made = dot(left[...], d_lin[...].reshape(tokens, lanes), ((1,), (0,)))
        for i in range(2):
            first, second = made[i * 128 : i * 128 + 64], made[i * 128 + 64 : (i + 1) * 128]
            keep[2 * k + i] = jnp.where(c == 0, first, second)
            give[2 * k + i] = jnp.where(c == 0, second, first).astype(BF)

    one("f2f1")
    join()
    two("m3m0m2m1f3f0")
    one("d3d0")
    grads(0)
    one("M3M0")
    one("d2d1")
    grads(1)
    one("M2M1")
    two("d3d0d2d1f2f1")
    grads(2)
    one("b31b02")
    two("M3M0M2M1")
    grads(3)
    one("h30h03b21b12")
    grads(4)
    grads(5)
    one("b32b01")
    grads(6)
    grads(7)
    across = remote(give, got, msem.at[0], msem.at[1], partner)
    across.start()
    landed(got, msem.at[1])

    def total(e, _):
        send[e] = (keep[e] + wide(got[e])).astype(BF)
        return 0

    lax.fori_loop(0, 16, total, 0)
    each_chip(net, lambda t, dev: remote(send.at[t], recv.at[me], msem.at[2], msem.at[3], dev).start())
    recv[me] = send[me]
    two("b31b02b21b12b32b01")
    one("h31h02h20h13Q")
    two("h30h03h20h13Q")
    one("h32h01h10h23")
    two("h31h02h10h23")
    one("h21h12q")
    sc1.last(store1)
    d_gain[...] = jnp.zeros_like(d_gain)

    def norm_back(i, _):
        sl = pl.ds(pl.multiple_of(i * 16, 16), 16)
        v, d = wide(x_in[sl, :]), d_n1[sl, :]
        r = lax.rsqrt(jnp.mean(v * v, axis=1, keepdims=True) + EPS)
        scaled = d * gain[...]
        inner = jnp.mean(scaled * v, axis=1, keepdims=True)
        d_inputs[sl, :] = d_res[sl, :] + r * scaled - v * (r * r * r * inner)
        d_gain[...] += jnp.sum(d * v * r, axis=0, keepdims=True)
        return 0

    lax.fori_loop(0, rows // 16, norm_back, 0)
    gb[...] = jnp.zeros_like(gb)
    gb[me, 2:4, :] = d_gains[0:2, :]
    for e in range(16):
        gb[e, 0:1, :] = d_gain[:, e * 128 : (e + 1) * 128]
        gb[e, 1:2, :] = d_gain_two[:, e * 128 : (e + 1) * 128]
    dev_me = me * 2 + c

    def tell(j, _):
        t = lax.rem(dev_me + j, 32)
        remote(gb.at[t // 2], gr.at[dev_me], msem.at[4], msem.at[5], (t // 8, lax.rem(t, 8) // 2, lax.rem(t, 2))).start()
        return 0

    lax.fori_loop(1, 32, tell, 0)
    gr[dev_me] = gb[me]
    two("h32h01h21h12q")
    landed(recv.at[pl.ds(0, 15)], msem.at[3])
    for e in range(16):
        piece = wide(recv[e])
        for i, out in enumerate((d_wq, d_wk, d_wv)):
            out[:, e * 128 : (e + 1) * 128] = piece[:, i * 128 : (i + 1) * 128]
    landed(gr.at[pl.ds(0, 31)], msem.at[5])
    sums = gr[0]
    for i in range(1, 32):
        sums = sums + gr[i]
    gains_o[...] = jnp.where(c == 0, sums[:, :64], sums[:, 64:])
    sc2.last(store2)
    d_wo[:, own_cols] = wsum[pl.ds(pl.multiple_of(c * 64, 64), 64), :]
    theirs = remote(wsum.at[pl.ds(pl.multiple_of((1 - c) * 64, 64), 64), :], d_wo.at[:, own_cols], msem.at[8], msem.at[9], partner)
    theirs.start()
    landed(PG, msem.at[6])
    landed(give, msem.at[0])
    landed(recv.at[pl.ds(0, 15)], msem.at[2])
    landed(gr.at[pl.ds(0, 31)], msem.at[4])
    theirs.wait_send()
    landed(d_wo.at[:, give_cols], msem.at[9])
    net.finish()
    net2.finish()


def run_finish(d_lin, wf, n1, att, x_in, d_res, gain, d_gain_two, d_gains, cid, cut=96):
    R, D = x_in.shape
    N = d_lin.shape[2]
    DMA = pltpu.SemaphoreType.DMA
    S = jax.ShapeDtypeStruct
    V = lambda *s: pltpu.VMEM(s, BF)
    VF = lambda *s: pltpu.VMEM(s, F32)
    A = pl.BlockSpec(memory_space=pl.ANY)
    M = pl.BlockSpec(memory_space=pltpu.VMEM)
    own = S((R // 2, D), F32)
    return pl.pallas_call(
        functools.partial(finish_kernel, cut),
        out_shape=(own, S((R, D), F32), own, own, own, S((8, 64), F32)),
        in_specs=[M, M, A] + [M] * 6,
        out_specs=(M,) * 6,
        scratch_shapes=[V(4, 4, R, D), V(4, 4, R, D // 2), V(4, 4, R, D // 2), V(4, 4, R, D // 2), VF(R, D // 2), V(2, 16, R, 256), V(256, 16 * R), VF(16, 64, N), V(16, 64, N),
                        V(16, 64, N), V(16, 64, N), V(16, 64, N), VF(R, D), VF(1, D), VF(16, 8, 128), VF(32, 8, 128),
                        DMA((1,)), DMA((2,)), DMA((10,)), DMA((64,)), DMA((64,))] + rs_scratch(cut, R, D) + rs_scratch(cut, R, D // 2),
        compiler_params=pltpu.CompilerParams(collective_id=cid, has_side_effects=True, vmem_limit_bytes=63 * 2**20),
        name="finish",
    )(d_lin, wf, n1, att, x_in, d_res, gain, d_gain_two, d_gains)

def band_scores(q, k, q_seg, k_seg, scale, reach):
    scores = dot(q, k, ((1,), (1,))) * scale
    q_at = lax.broadcasted_iota(jnp.int32, scores.shape, 0)
    k_at = lax.broadcasted_iota(jnp.int32, scores.shape, 1)
    return scores, (k_seg == q_seg) & (k_at <= q_at + reach)


def turned(v, cosine, sine):
    return v * cosine + pltpu.roll(v, 64, axis=1) * sine


def turned_back(v, cosine, sine):
    return v * cosine - pltpu.roll(v, 64, axis=1) * sine


def attend_kernel(scale, pads, cut, lin_h, tot, near, far, gq, gk, q_seg, segments, w_own, x_in, gain, cot,
                  wo_o, q_rot_o, kv_o, o_o, lse, att_o, residual_o, n2, C,
                  lin, k_seg, q_rot, kv, o_ref, att, residual, wo, lsem, msem, psem, ksem, ssem, csem, *gs):
    net = Net(ssem)
    u, z, c = net.u, net.z, net.c
    me = u * 4 + z
    rows = x_in.shape[0]
    width = x_in.shape[1]
    reach = pads * 2 * rows
    partner = (u, z, 1 - c)
    own = pltpu.make_async_copy(w_own, wo.at[u, z, c], lsem.at[0])
    own.start()
    load = pltpu.make_async_copy(lin_h, lin, ksem.at[0])
    load.start()
    own_c = pltpu.make_async_copy(cot, C.at[u, z], lsem.at[2])
    own_c.start()
    greet(net)
    own.wait()
    ga = Gather(net, rows, cut, lambda uu, zz, lo, n: wo.at[uu, zz, c, :, pl.ds(lo * 16, n * 16)],
                lambda zz, lo, n: wo.at[:, zz, c, :, pl.ds(lo * 16, n * 16)], gs[:7])
    netc = Net(csem)
    gc = Gather(netc, rows, cut, lambda uu, zz, lo, n: C.at[uu, zz, pl.ds(lo, n), :],
                lambda zz, lo, n: C.at[:, zz, pl.ds(lo, n), :], gs[7:])

    def halves(s):
        ga.settle(s)
        for zz, cond in ga.planes(s):
            ref = lambda zz=zz: wo.at[:, zz, c]
            net.go(cond, ref, ref, lambda zz=zz: psem.at[zz], partner)

    ga.begin()
    segment_rows(segments, k_seg, reach)
    load.wait()
    for i in range(pads):
        kv[:, i] = jnp.zeros(kv.shape[:1] + kv.shape[2:], BF)

    def ready(i, _):
        both = lin[i]
        rq = lax.rsqrt(column(tot[pl.ds(i, 1), :]) / width + EPS)
        rk = lax.rsqrt(column(tot[pl.ds(16 + i, 1), :]) / width + EPS)
        cs, sn = rope_at(near, far, i)
        q_rot[i] = turned(both[:, :128] * rq * gq[...], cs, sn).astype(BF)
        kv[0, pads + i, c] = turned(both[:, 128:256] * rk * gk[...], cs, sn).astype(BF)
        kv[1, pads + i, c] = both[:, 256:].astype(BF)
        return 0

    lax.fori_loop(0, 16, ready, 0)
    mine = kv.at[:, pl.ds(pads, 16), c]
    to_partner = remote(mine, mine, msem.at[0], msem.at[1], partner)
    to_partner.start()
    ga.begin2()
    ga.along(1)
    ga.quads(0)
    ga.cross(0)
    own_c.wait()
    gc.begin()
    landed(kv.at[:, pl.ds(pads, 16), 1 - c], msem.at[1])

    def block(j, _):
        i = lax.rem(me + 1 + j, 16)
        first = 2 * i + c
        band = pl.ds(pl.multiple_of(first * rows, rows), rows + reach)
        kf, vf = kv.at[0].reshape((pads + 16) * 2 * rows, 128), kv.at[1].reshape((pads + 16) * 2 * rows, 128)
        scores, allowed = band_scores(q_rot[i], kf[band, :], column(q_seg[pl.ds(i, 1), :])[:, 0:1], k_seg[:, band], scale, reach)
        scores = jnp.where(allowed, scores, NEG)
        top = jnp.max(scores, axis=1, keepdims=True)
        weights = jnp.where(allowed, jnp.exp(scores - top), 0.0)
        total = jnp.sum(weights, axis=1, keepdims=True)
        probs = (weights / total).astype(BF)
        o_ref[i] = dot(probs, vf[band, :], ((1,), (0,))).astype(BF)
        lse[i] = top + jnp.log(total)

        @pl.when(j < 15)
        def _():
            remote(o_ref.at[i], att.at[me], msem.at[2], msem.at[3], (i // 4, lax.rem(i, 4), c)).start()

        return 0

    lax.fori_loop(0, 5, block, 0)
    ga.along(2)
    ga.quads(1)
    ga.cross(1)
    halves(0)
    gc.begin2()
    lax.fori_loop(5, 10, block, 0)
    ga.along(3)
    ga.quads(2)
    ga.cross(2)
    halves(1)
    gc.along(1)
    gc.quads(0)
    gc.cross(0)
    lax.fori_loop(10, 16, block, 0)
    ga.quads(3)
    ga.cross(3)
    halves(2)
    gc.along(2)
    gc.quads(1)
    gc.cross(1)
    halves(3)
    att[me] = o_ref[me]
    part = att.at[pl.ds(0, 15)]
    landed(part, msem.at[3])
    for zz in range(4):
        landed(wo.at[:, zz, 1 - c], psem.at[zz])
    keep = [pltpu.make_async_copy(a, o, ksem.at[j]) for j, (a, o) in enumerate(
        ((wo, wo_o), (q_rot, q_rot_o), (kv, kv_o), (o_ref, o_o), (att, att_o)))]
    for one in keep:
        one.start()
    tile = 256

    def out(n, _):
        cols = pl.ds(pl.multiple_of(n * tile, tile), tile)
        acc = x_in[:, cols].astype(F32)
        for e in range(0, 16, 2):
            pair = jnp.concatenate([att[e], att[e + 1]], axis=1)
            acc = acc + dot(pair, wo[e // 4, pl.ds(e % 4, 2), :, :, cols].reshape(256, tile), ((1,), (0,)))
        residual[:, cols] = acc
        return 0

    lax.fori_loop(0, width // tile, out, 0)
    keep.append(pltpu.make_async_copy(residual, residual_o, ksem.at[5]))
    keep[5].start()
    gc.along(3)
    gc.quads(2)
    gc.cross(2)

    def norm(i, _):
        sl = pl.ds(pl.multiple_of(i * 16, 16), 16)
        v = residual[sl, :]
        r = lax.rsqrt(jnp.mean(v * v, axis=1, keepdims=True) + EPS)
        n2[sl, :] = (v * r * gain[...]).astype(BF)
        return 0

    lax.fori_loop(0, rows // 16, norm, 0)
    landed(mine, msem.at[0])
    landed(part, msem.at[2])
    gc.quads(3)
    gc.cross(3)
    for s in range(4):
        gc.settle(s)
    for one in keep:
        one.wait()
    net.finish()
    netc.finish()


def run_attend(scale, pads, lin, tot, near, far, gq, gk, q_seg, segments, w_own, x_in, gain, cot, cid, cut=96):
    R, D = x_in.shape
    DMA = pltpu.SemaphoreType.DMA
    S = jax.ShapeDtypeStruct
    A = pl.BlockSpec(memory_space=pl.ANY)
    M = pl.BlockSpec(memory_space=pltpu.VMEM)
    V = pltpu.VMEM
    wo = (4, 4, 2, R // 2, D)
    return pl.pallas_call(
        functools.partial(attend_kernel, scale, pads, cut),
        out_shape=(S(wo, BF), S((16, R, 128), BF), S((2, pads + 16, 2, R, 128), BF), S((16, R, 128), BF),
                   S((16, R, 1), F32), S((16, R, 128), BF), S((R, D), F32), S((R, D), BF), S((4, 4) + cot.shape, BF)),
        in_specs=[A] + [M] * 7 + [A, M, M, A],
        out_specs=(A, A, A, A, M, A, A, M, A),
        scratch_shapes=[V((16, R, 384), F32), V((1, (pads + 16) * 2 * R), F32), V((16, R, 128), BF),
                        V((2, pads + 16, 2, R, 128), BF), V((16, R, 128), BF), V((16, R, 128), BF), V((R, D), F32),
                        V(wo, BF), DMA((3,)), DMA((4,)), DMA((4,)), DMA((6,)), DMA((64,)), DMA((64,))] + ag_sems() + ag_sems(),
        compiler_params=pltpu.CompilerParams(collective_id=cid, has_side_effects=True, vmem_limit_bytes=63 * 2**20),
        name="attend",
    )(lin, tot, near, far, gq, gk, q_seg, segments, w_own, x_in, gain, cot)


def attend_back_kernel(scale, pads, cut, d_n2, cot, gain, wo_h, p_out, residual, q_rot, kv, q_seg, segments, lse, o_ref, lin, tot, near, far, gq, gk, n2, a_h,
                       d_lin, d_gains, output, d_residual, d_gain, other_w, dg_o, du_o,
                       nt, left, ob, gt, fs, tsem, osem, ors, fsem, gsem, d_res, k_seg, P, wo, d_mine, d_out, d_q, d_k, d_v, other, got, d_un, sums, sums_all, inner,
                       lsem, msem, ssem, *bufs):
    net = Net(ssem)
    sc = Scatter(net, cut, P, bufs)
    u, z, c = net.u, net.z, net.c
    me = u * 4 + z
    rows, width = d_n2.shape
    reach = pads * 2 * rows
    partner = (u, z, 1 - c)
    load = pltpu.make_async_copy(wo_h, wo, lsem.at[0])
    load.start()
    load_p = pltpu.make_async_copy(p_out, P, lsem.at[1])
    load_p.start()
    greet(net)

    def go(words):
        run_steps(steps_of(sc, words))

    load_p.wait()
    go("m3m0m2m1")
    d_gain[...] = jnp.zeros_like(d_gain)

    def norm_back(i, _):
        sl = pl.ds(pl.multiple_of(i * 16, 16), 16)
        v, d = residual[sl, :], d_n2[sl, :]
        r = lax.rsqrt(jnp.mean(v * v, axis=1, keepdims=True) + EPS)
        scaled = d * gain[...]
        mean = jnp.mean(scaled * v, axis=1, keepdims=True)
        total = wide(cot[sl, :]) + r * scaled - v * (r * r * r * mean)
        d_residual[sl, :] = total
        d_res[sl, :] = total.astype(BF)
        d_gain[...] += jnp.sum(d * v * r, axis=0, keepdims=True)
        return 0

    lax.fori_loop(0, rows // 16, norm_back, 0)
    segment_rows(segments, k_seg, reach)
    load.wait()

    def send(j, _):
        pair = lax.rem(me // 2 + 1 + j, 8)
        both = dot(d_res[...], wo[pair // 2, pl.ds(lax.rem(pair, 2) * 2, 2)].reshape(256, width), ((1,), (1,))).astype(BF)
        for i in (0, 1):
            e = pair * 2 + i
            d_mine[e] = both[:, i * 128 : (i + 1) * 128]

            @pl.when(e != me)
            def _():
                remote(d_mine.at[e], d_out.at[me], msem.at[0], msem.at[1], (e // 4, lax.rem(e, 4), c)).start()

        return 0

    lax.fori_loop(0, 8, send, 0)
    d_out[me] = d_mine[me]
    A = wo.reshape(16, rows, width)
    load_a = pltpu.make_async_copy(a_h, A, lsem.at[0])
    load_a.start()
    plan = [("o", 0), ("o", 1), ("o", 2), ("o", 3), ("w", 0), ("w", 1), ("w", 2), ("w", 3)]
    tile = 256

    def left_load(i):
        kind, k = plan[i]
        which = 1 - c if kind == "o" else c
        cols = pl.ds(pl.multiple_of((which * 4 + k) * tile, tile), tile)
        return pltpu.make_async_copy(n2.at[:, :, cols], nt.at[i % 2], tsem.at[i % 2])

    def left_turn(i):
        turned_into(left, nt.at[i % 2].reshape(16 * rows, tile), slice(None))

    left_load(0).start()
    made = A.reshape(16 * rows, width)
    dw, dw_end = weight_tiles(
        partner, plan, left_load, left_turn, lambda h, n: made[:, h * 1024 + n * 512 : h * 1024 + (n + 1) * 512], left,
        lambda k: ob.at[k % 2], gt, fs, other_w, osem, ors, fsem, gsem.at[0],
        lambda k, h: (dg_o, du_o)[h].at[pl.ds(k * tile, tile), :])
    d_k[...] = jnp.zeros_like(d_k)
    d_v[...] = jnp.zeros_like(d_v)
    load_a.wait()
    dw(0)
    dw(1)
    landed(d_out.at[pl.ds(0, 15)], msem.at[1])
    count = (pads + 16) * 2 * rows

    def block(i, _):
        band = pl.ds(pl.multiple_of((2 * i + c) * rows, rows), rows + reach)
        kf, vf = kv.at[0].reshape(count, 128), kv.at[1].reshape(count, 128)
        q, k, dd = q_rot[i], kf[band, :], d_out[i]
        scores, allowed = band_scores(q, k, column(q_seg[pl.ds(i, 1), :])[:, 0:1], k_seg[:, band], scale, reach)
        probs = jnp.where(allowed, jnp.exp(scores - lse[i]), 0.0)
        d_probs = dot(dd, vf[band, :], ((1,), (1,)))
        delta = jnp.sum(dd.astype(F32) * o_ref[i].astype(F32), axis=1, keepdims=True)
        d_scores = (probs * (d_probs - delta)).astype(BF)
        d_q[i] = (dot(d_scores, k, ((1,), (0,))) * scale).astype(BF)
        d_k[band, :] += dot(d_scores, q, ((0,), (0,))) * scale
        d_v[band, :] += dot(probs.astype(BF), dd, ((0,), (0,)))
        return 0

    def store(sl, v):
        output[sl, :] = residual[sl, :] + v

    go("f3f0d3d0")
    done = 0
    for upto, words in ((3, "M3M0M2M1d2d1"), (6, "f2f1"), (11, "b31b02"), (16, "")):
        lax.fori_loop(done, upto, block, 0)
        go(words)
        done = upto

    def pack(i, _):
        at = pl.ds(pl.multiple_of(((pads + i) * 2 + 1 - c) * rows, rows), rows)
        other[0, i] = d_k[at, :].astype(BF)
        other[1, i] = d_v[at, :].astype(BF)
        return 0

    lax.fori_loop(0, 16, pack, 0)
    remote(other, got, msem.at[2], msem.at[3], partner).start()
    go("h30h03")
    landed(got, msem.at[3])
    d_gains[...] = jnp.zeros_like(d_gains)

    def undo(i, _):
        at = pl.ds(pl.multiple_of(((pads + i) * 2 + c) * rows, rows), rows)
        cs, sn = rope_at(near, far, i)
        both = lin[i]
        rq = lax.rsqrt(column(tot[pl.ds(i, 1), :]) / width + EPS)
        rk = lax.rsqrt(column(tot[pl.ds(16 + i, 1), :]) / width + EPS)
        dk = (d_k[at, :] + wide(got[0, i])).astype(BF).astype(F32)
        d_lin[i, :, 256:] = (d_v[at, :] + wide(got[1, i])).astype(BF)
        uq = turned_back(wide(d_q[i]), cs, sn)
        uk = turned_back(dk, cs, sn)
        q, k = both[:, :128], both[:, 128:256]
        d_gains[0:1, :] += jnp.sum(uq * q * rq, axis=0, keepdims=True)
        d_gains[1:2, :] += jnp.sum(uk * k * rk, axis=0, keepdims=True)
        uq, uk = uq * gq[...], uk * gk[...]
        d_un[0, i] = uq
        d_un[1, i] = uk
        sums[pl.ds(i, 1), :] = row_sums(uq * q)
        sums[pl.ds(16 + i, 1), :] = row_sums(uk * k)
        return 0

    lax.fori_loop(0, 16, undo, 0)

    def meanwhile():
        go("b21b12b32b01")
        dw(2)
        dw(3)

    share_sums(net, sums, sums_all, inner, lsem.at[1], msem.at[4], msem.at[5], meanwhile)

    def finish(i, _):
        both = lin[i]
        for s in (0, 1):
            r = lax.rsqrt(column(tot[pl.ds(16 * s + i, 1), :]) / width + EPS)
            mean = column(inner[pl.ds(16 * s + i, 1), :]) / width
            own = both[:, 128 * s : 128 * (s + 1)]
            d_lin[i, :, 128 * s : 128 * (s + 1)] = (r * d_un[s, i] - own * (r * r * r * mean)).astype(BF)
        return 0

    lax.fori_loop(0, 16, finish, 0)
    go("h31h02")
    dw(4)
    go("h20h13Q")
    dw(5)
    go("h32h01")
    dw(6)
    go("h10h23")
    dw(7)
    go("h21h12q")
    sc.last(store)
    dw_end()
    landed(d_out.at[pl.ds(0, 15)], msem.at[0])
    landed(other, msem.at[2])
    net.finish()


def run_attend_back(scale, pads, d_n2, cot, gain, wo, p_out, residual, q_rot, kv, q_seg, segments, lse, o, lin, tot, near, far, gq, gk, n2, a_h, half, cid, cut=96):
    R, D = d_n2.shape
    DMA = pltpu.SemaphoreType.DMA
    S = jax.ShapeDtypeStruct
    A = pl.BlockSpec(memory_space=pl.ANY)
    M = pl.BlockSpec(memory_space=pltpu.VMEM)
    V = pltpu.VMEM
    span = (pads + 16) * 2 * R
    return pl.pallas_call(
        functools.partial(attend_back_kernel, scale, pads, cut),
        out_shape=(S((16, R, 384), BF), S((8, 128), F32), S((R, D), F32), S((R, D), F32), S((1, D), F32),
                   S((4, 256, D), BF), S(half, F32), S(half, F32)),
        in_specs=[M, M, M, A, A] + [M] * 13 + [A, A],
        out_specs=(M,) * 5 + (A,) * 3,
        scratch_shapes=[V((2, 16, R, 256), BF), V((256, 16 * R), BF), V((2, 256, D), BF), V((256, D), BF), V((2, 256, 1024), F32),
                        DMA((2,)), DMA((4,)), DMA((4,)), DMA((2,)), DMA((1,)), V((R, D), BF), V((1, span), F32), V((4, 4, R, D), BF), V(wo.shape, BF), V((16, R, 128), BF), V((16, R, 128), BF), V((16, R, 128), BF),
                        V((span, 128), F32), V((span, 128), F32), V((2, 16, R, 128), BF), V((2, 16, R, 128), BF),
                        V((2, 16, R, 128), F32), V((32, 128), F32), V((16, 32, 128), F32), V((32, 128), F32),
                        DMA((2,)), DMA((10,)), DMA((64,))] + rs_scratch(cut, R, D),
        compiler_params=pltpu.CompilerParams(collective_id=cid, has_side_effects=True, vmem_limit_bytes=63 * 2**20),
        name="attend_back",
    )(d_n2, cot, gain, wo, p_out, residual, q_rot, kv, q_seg, segments, lse, o, lin, tot, near, far, gq, gk, n2, a_h)
def dot(a, b, dims):
    return lax.dot_general(a, b, (dims, ((), ())), preferred_element_type=jnp.float32)


def local_chip(
    inputs, cotangent, segments, expert_ids, gate_weights, fill_order, norm1_gain, w_query, w_key,
    w_value, w_output, query_gain, key_gain, norm2_gain, expert_gate, expert_up, expert_down,
):
    chips = 16
    devices = 2 * chips
    rows, width = inputs.shape
    u, z, core = place()
    chip = u * 4 + z
    device = chip * 2 + core
    topk = expert_ids.shape[1]
    experts_n = chips
    capacity = 9 * rows * devices * topk // (8 * experts_n)
    one_hot = expert_ids[:, :, None] == jnp.arange(experts_n, dtype=jnp.int32)[None, None, :]
    chosen = jnp.any(one_hot, axis=1)
    weight = jnp.sum(jnp.where(one_hot, gate_weights[:, :, None], 0.0), axis=1)
    earlier = (fill_order[None, :] < fill_order[:, None]).astype(jnp.bfloat16)
    rank = dot(earlier, chosen.astype(jnp.bfloat16), ((1,), (0,)))
    rank = jnp.where(chosen, rank, -1.0)
    gains = jnp.stack([norm1_gain, query_gain, key_gain, norm2_gain]).astype(F32)
    blank = jnp.zeros_like(gains)
    gains = jnp.where(core == 0, jnp.concatenate([gains, blank], axis=1), jnp.concatenate([blank, gains], axis=1))
    gains = jnp.broadcast_to(gains[None], (chips, 4, 128))
    block = jnp.concatenate(
        [weight.T[:, None, :], rank.T[:, None, :], gains, jnp.zeros((chips, 2, 128), F32)], axis=1)
    side = width // 2
    n1_rows, lin, w_qkv, squares, swapped, cot_a = run_qkv(
        inputs, w_query, w_key, w_value, block, cotangent[:, :side], 2)
    gains = jnp.sum(swapped.reshape(chips, 2, 8, 128), axis=1)
    gain_one, gain_two = gains[:, 2].reshape(1, width), gains[:, 5].reshape(1, width)
    gq, gk = (lax.dynamic_slice_in_dim(gains[:, i], chip, 1, 0) for i in (3, 4))
    rank_all = swapped[:, 1, :]
    taken = rank_all >= 0.0
    counts = jnp.sum(taken.astype(F32), axis=1)
    before = jnp.cumsum(counts) - counts
    kept = taken & (before[:, None] + rank_all < float(capacity))
    share = jnp.where(kept, swapped[:, 0, :], 0.0).reshape(chips, 2, rows)
    share = lax.dynamic_index_in_dim(share, core, 1, keepdims=False)


    half_dim = HEAD_DIM // 2
    inv_freq = jnp.exp(jnp.arange(half_dim, dtype=F32) * (-2.0 * math.log(ROPE_BASE) / HEAD_DIM))
    inv_freq = jnp.concatenate([inv_freq, inv_freq])[None, :]
    sign = jnp.where(jnp.arange(HEAD_DIM) < half_dim, -1.0, 1.0)[None, :]
    within = jnp.arange(rows, dtype=F32)[:, None] * inv_freq
    starts = ((jnp.arange(chips, dtype=jnp.int32) * 2 + core) * rows).astype(F32)[:, None] * inv_freq
    near = jnp.stack([jnp.cos(within), sign * jnp.sin(within)])
    far = jnp.stack([jnp.cos(starts), sign * jnp.sin(starts)])
    pads = chips // 4
    marks = segments.astype(F32)
    q_seg = lax.dynamic_index_in_dim(marks.reshape(chips, 2, rows), core, 1, keepdims=False)
    marks = marks.reshape(1, -1)
    scale = 1.0 / math.sqrt(HEAD_DIM)
    tokens = chips * rows
    w_o, q_rot, kv, head_out, log_total, attended, residual, normed_two, cot_b = run_attend(
        scale, pads, lin, squares, near, far, gq, gk, q_seg, marks, w_output, inputs, gain_two, cotangent[:, side:], 4)

    d_normed_two, mixed, n2_rows, d_pre, _other, d_expert_down = run_expert(
        normed_two, cot_a, cot_b, share, expert_gate, expert_up, expert_down, 6)
    d_lin, d_qk_gains, output, d_residual, d_gain_two, _other, d_expert_gate, d_expert_up = run_attend_back(
        scale, pads, d_normed_two, cotangent, gain_two, w_o, mixed, residual, q_rot, kv, q_seg, marks, log_total, head_out,
        lin, squares, near, far, gq, gk, n2_rows.reshape(chips, rows, width), d_pre.reshape(chips, rows, -1), expert_gate.shape, 7)
    d_w_output, d_inputs, d_w_query, d_w_key, d_w_value, d_gains = run_finish(
        d_lin, w_qkv, n1_rows, attended, inputs, d_residual, gain_one, d_gain_two, d_qk_gains, 8)
    return (
        output,
        d_inputs,
        d_gains[0],
        d_w_query,
        d_w_key,
        d_w_value,
        d_w_output,
        d_gains[2],
        d_gains[3],
        d_gains[1],
        d_expert_gate,
        d_expert_up,
        d_expert_down,
    )
def whole(mesh, step, rows):
    return jax.shard_map(
        step,
        mesh=mesh,
        in_specs=(
            P(rows, None),
            P(rows, None),
            P(),
            P(rows, None),
            P(rows, None),
            P(rows),
            P(rows),
            P(rows, None),
            P(rows, None),
            P(rows, None),
            P(rows, None),
            P(rows),
            P(rows),
            P(rows),
            P(rows, None),
            P(rows, None),
            P(rows, None),
        ),
        out_specs=(
            P(rows, None),
            P(rows, None),
            P(rows),
            P(rows, None),
            P(rows, None),
            P(rows, None),
            P(rows, None),
            P(rows),
            P(rows),
            P(rows),
            P(rows, None),
            P(rows, None),
            P(rows, None),
        ),
        check_vma=False,
    )


def solution(mesh):
    groups, blk_size = mesh.shape["ulysses"], mesh.shape["blk"]

    def step(*args):
        if groups != 4 or blk_size != 8 or args[7].shape[1] // HEAD_DIM != groups * blk_size // 2:
            return whole(mesh, local, ("ulysses", "blk"))(*args)
        chips = Mesh(mesh.devices.reshape(groups, blk_size // 2, 2), ("ulysses", "z", "core"))
        return whole(chips, local_chip, ("ulysses", "z", "core"))(*args)

    return step
```
